32 devices in a mesh: dp: 4 (over y, x), tensor: 4 (over z), context: 2 (over core).
Axes of the slice: x: 2, y: 2, z: 4, core: 2. Of those that a mesh axis runs over, the one named last changes fastest.
Arguments:
- embedded: bfloat16 [8, 1024, 2048], P('dp', ('tensor', 'context')), may hold values from -6 to 6
- initial_state: bfloat16 [8, 1024, 2048], P('dp', ('tensor', 'context')), may hold values from -6 to 6
- cotangent: bfloat16 [8, 1024, 2048], P('dp', ('tensor', 'context')), may hold values from -6 to 6
- doc_ids: int32 [8, 1024], replicated, may hold values from 0 to 3, as said below
- recurrences: int32 [8], replicated, may hold values from 1 to 4, as said below
- adapter_weight: bfloat16 [4096, 2048], P(('dp', 'context')), may hold values from -0.09375 to 0.09375
- norm_gains: bfloat16 [2, 2048], P(None, ('dp', 'context')), may hold values from 0.5 to 1.5
- qkv_weight: bfloat16 [2048, 16, 384], P(('dp', 'context'), 'tensor'), may hold values from -0.125 to 0.125
- output_head_weight: bfloat16 [16, 128, 2048], P('tensor', None, ('dp', 'context')), may hold values from -0.75 to 0.75
- gate_up_weight: bfloat16 [2048, 2, 5632], P(('dp', 'context'), None, 'tensor'), may hold values from -0.125 to 0.125
- down_weight: bfloat16 [5632, 2048], P('tensor', ('dp', 'context')), may hold values from -0.078125 to 0.078125
Outputs:
- final_state: float32 [8, 1024, 2048], P('dp', ('tensor', 'context'))
- embed_grad: float32 [8, 1024, 2048], P('dp', ('tensor', 'context'))
- adapter_grad: float32 [4096, 2048], P(('dp', 'context'))
- gains_grad: float32 [2, 2048], P(None, ('dp', 'context'))
- qkv_grad: float32 [2048, 16, 384], P(('dp', 'context'), 'tensor')
- out_grad: float32 [16, 128, 2048], P('tensor', None, ('dp', 'context'))
- gate_up_grad: float32 [2048, 2, 5632], P(('dp', 'context'), None, 'tensor')
- down_grad: float32 [5632, 2048], P('tensor', ('dp', 'context'))
The draws below stay inside these ranges and needn't reach their ends.
Inputs may be any that keep to these rules, and one draw needn't show every extreme that they name: `doc_ids`: along a sequence the number never falls and rises by one at a time; at most 4 documents a sequence. In every draw some sequence takes exactly 4 recurrences and some exactly 1.
All inputs are finite; a program needn't handle non-finite values.
Results may differ from the reference program's by a relative error of at most 0.028.
Values may be sent and summed in bfloat16 or wider, within the bound.
A program may use at most 256 MiB of HBM per device.

```python
import math
import jax
import jax.numpy as jnp
from jax import lax

D = 2048
H = 16
HD = 128
FF = 5632
LEN = 1024
SEQ_DEV = 2
MAXR = 4
BACK = 1
DOCS = 4
SEQS = 8
N_TENSOR = 4
N_CONTEXT = 2


def draw_doc_ids(key, part):
    key = jax.random.fold_in(key, 11)
    cut_key, pick_key, start_key, final_random_key, tail_key = jax.random.split(key, 5)
    doc_stride = LEN // DOCS
    block_rows = LEN // (N_TENSOR * N_CONTEXT)
    offsets = jax.random.randint(cut_key, (SEQS, DOCS - 1), -(doc_stride // 2) + 1, doc_stride // 2)
    cut_points = (jnp.arange(1, DOCS, dtype=jnp.int32) * doc_stride)[None, :] + offsets
    positions = jnp.arange(LEN, dtype=jnp.int32)
    regular = jnp.sum((positions[None, :, None] >= cut_points[:, None, :]).astype(jnp.int32), axis=-1)
    groups = SEQS // SEQ_DEV
    picked = jax.random.randint(pick_key, (groups,), 0, SEQ_DEV)
    chosen = (jnp.arange(SEQ_DEV)[None, :] == picked[:, None]).reshape(SEQS)
    first_cut = jax.random.randint(start_key, (SEQS,), 1, block_rows)
    second_cut = jax.random.randint(final_random_key, (SEQS,), LEN - block_rows + 1, LEN - 1)
    third_cut = second_cut + 1 + jax.random.randint(tail_key, (SEQS,), 0, LEN - 1 - second_cut)
    spanning = (positions[None, :] >= first_cut[:, None]).astype(jnp.int32) + (positions[None, :] >= second_cut[:, None]).astype(jnp.int32) + (positions[None, :] >= third_cut[:, None]).astype(jnp.int32)
    return jnp.where(chosen[:, None], spanning, regular).astype(jnp.int32)


def draw_recurrences(key, part):
    key = jax.random.fold_in(key, 23)
    table_key, high_key, low_key = jax.random.split(key, 3)
    count_table = jnp.clip(jnp.array([BACK, BACK, 2, 2, 3, 3, 3, MAXR, MAXR], dtype=jnp.int32), BACK, MAXR)
    table_picks = jax.random.randint(table_key, (SEQS,), 0, 9)
    counts = count_table[table_picks]
    high_pos = jax.random.randint(high_key, (), 0, SEQS)
    low_pos = (high_pos + 1 + jax.random.randint(low_key, (), 0, SEQS - 1)) % SEQS
    index_row = jnp.arange(SEQS)
    counts = jnp.where(index_row == high_pos, MAXR, counts)
    counts = jnp.where(index_row == low_pos, BACK, counts)
    return counts.astype(jnp.int32)


def steps_of(key, shape, shards, smallest, top_value):
    def one(dim, parts):
        steps = jax.random.uniform(jax.random.fold_in(jax.random.fold_in(key, 6), dim), (parts,), jnp.float32, smallest / len(shards), top_value / len(shards))
        return jnp.repeat(jnp.exp(steps), shape[dim] // parts).reshape((-1,) + (1,) * (len(shape) - dim - 1))

    level = one(*shards[0])
    for cut in shards[1:]:
        level = level * one(*cut)
    return level


def normal_values(stream_key, extent, scale, limit, shards=(), held_as=jnp.bfloat16):
    values = scale * jax.random.normal(stream_key, extent, jnp.float32)
    if shards:
        values = values * steps_of(stream_key, extent, shards, -0.22, 0.18)
    return jnp.clip(values, -limit, limit).astype(held_as)


def setup_inputs(seed: int = 0) -> dict:
    key_of = jax.random.split(jax.random.key(seed), 12)
    return {
        "embedded": normal_values(key_of[0], (SEQS, LEN, D), 1.0, 6.0, ((0, 4), (1, 8))),
        "initial_state": normal_values(key_of[1], (SEQS, LEN, D), 1.0, 6.0, ((0, 4), (1, 8))),
        "cotangent": normal_values(key_of[2], (SEQS, LEN, D), 1.0, 6.0, ((0, 4), (1, 8))),
        "doc_ids": draw_doc_ids(jax.random.fold_in(key_of[11], 71), 0),
        "recurrences": draw_recurrences(jax.random.fold_in(key_of[11], 71), 0),
        "adapter_weight": normal_values(key_of[5], (2 * D, D), (2 * D) ** -0.5, 0.09375, ((0, 8),)),
        "norm_gains": jnp.clip(1.0 + 0.1 * jax.random.normal(key_of[6], (2, D), jnp.float32), 0.5, 1.5).astype(jnp.bfloat16),
        "qkv_weight": normal_values(key_of[7], (D, H, 3 * HD), D ** -0.5, 0.125, ((0, 8), (1, 4))),
        "output_head_weight": normal_values(key_of[8], (H, HD, D), (H * HD // 32) ** -0.5, 0.75, ((0, 4), (2, 8))),
        "gate_up_weight": normal_values(key_of[9], (D, 2, FF), D ** -0.5, 0.125, ((0, 8), (2, 4))),
        "down_weight": normal_values(key_of[10], (FF, D), FF ** -0.5, 0.078125, ((0, 4), (1, 8))),
    }


@jax.custom_vjp
def low(v):
    return lax.optimization_barrier(v.astype(jnp.bfloat16)).astype(jnp.float32)

@jax.custom_vjp
def low_back(v):
    return v

def low_keep(v):
    return (low(v), None)

def low_pass(kept, grad):
    return (grad,)

def back_keep(v):
    return (v, None)

def back_low(kept, grad):
    return (low(grad),)
low.defvjp(low_keep, low_pass)
low_back.defvjp(back_keep, back_low)
rope_base = 50000.0
norm_eps = 1e-06
masked_score = -1e+30
highest = lax.Precision.HIGHEST

def rope_angles(positions, head_dim):
    freq_index = jnp.arange(head_dim // 2, dtype=jnp.float32)
    inv_freq = 1.0 / rope_base ** (2.0 * freq_index / head_dim)
    angles = positions.astype(jnp.float32)[:, None] * inv_freq[None, :]
    return (jnp.cos(angles), jnp.sin(angles))

def rotate_fwd(values, cos_t, sin_t):
    half_dim = values.shape[-1] // 2
    first_half = values[..., :half_dim]
    second_half = values[..., half_dim:]
    return jnp.concatenate([first_half * cos_t - second_half * sin_t, second_half * cos_t + first_half * sin_t], axis=-1)

def rms_unit(rows):
    return rows * lax.rsqrt(lax.optimization_barrier(jnp.mean(rows * rows, axis=-1, keepdims=True)) + norm_eps)

def recurrence(latent, embed_row, doc_row, weights, cos_t, sin_t):
    adapter_w, gains_w, qkv_w, out_w, gate_up_w, down_w = weights
    joined = jnp.concatenate([low(latent), embed_row], axis=-1)
    adapted = low_back(jnp.dot(joined, adapter_w, precision=highest))
    normed_a = low(rms_unit(adapted) * gains_w[0])
    projected = low_back(jnp.einsum('ld,dhk->hlk', normed_a, qkv_w, precision=highest))
    query_rot = low(rotate_fwd(projected[..., :HD], cos_t, sin_t))
    key_rot = low(rotate_fwd(projected[..., HD:2 * HD], cos_t, sin_t))
    value_low = low(projected[..., 2 * HD:])
    positions = jnp.arange(LEN)
    allowed = (positions[None, :] <= positions[:, None]) & (doc_row[None, :] == doc_row[:, None])
    score_scale = 1.0 / math.sqrt(HD)

    def head_attend(packed):
        head_query, head_key, head_value = packed
        scores = low_back(jnp.dot(head_query, head_key.T, precision=highest) * score_scale)
        prob_vals = jax.nn.softmax(jnp.where(allowed, scores, masked_score), axis=-1)
        head_vals = jnp.dot(low(prob_vals), head_value, precision=highest)
        return low(low_back(head_vals))
    head_out = lax.map(jax.checkpoint(head_attend), (query_rot, key_rot, value_low))
    attn = low_back(jnp.einsum('hld,hdm->lm', head_out, out_w, precision=highest))
    mixed_rows = adapted + attn
    normed_b = low(rms_unit(mixed_rows) * gains_w[1])
    gate_up = low_back(jnp.einsum('ld,dgf->lgf', normed_b, gate_up_w, precision=highest))
    hidden_activations = low(jax.nn.silu(gate_up[:, 0]) * gate_up[:, 1])
    ffn_out = low_back(jnp.dot(hidden_activations, down_w, precision=highest))
    return mixed_rows + ffn_out

def reference(embedded, initial_state, cotangent, doc_ids, recurrences, adapter_weight, norm_gains, qkv_weight, output_head_weight, gate_up_weight, down_weight):
    weights = tuple((weight.astype(jnp.float32) for weight in (adapter_weight, norm_gains, qkv_weight, output_head_weight, gate_up_weight, down_weight)))
    embeds = embedded.astype(jnp.float32)
    cos_t, sin_t = rope_angles(jnp.arange(LEN), HD)

    def one_pass(latents, embeds_now, weights_now):

        def single(packed):
            return recurrence(packed[0], packed[1], packed[2], weights_now, cos_t, sin_t)
        return lax.map(jax.checkpoint(single), (latents, embeds_now, doc_ids))

    def prefix_round(step_index, latents):
        advanced = one_pass(latents, embeds, weights)
        return jnp.where((step_index < recurrences - BACK)[:, None, None], advanced, latents)
    detached = lax.fori_loop(0, MAXR - BACK, prefix_round, initial_state.astype(jnp.float32))

    def tail_pass(embeds_now, weights_now):
        latents = detached
        for round_index in range(BACK):
            latents = one_pass(latents, embeds_now, weights_now)
        return latents
    final_state, pullback = jax.vjp(tail_pass, embeds, weights)
    embed_grad, weight_grads = pullback(cotangent.astype(jnp.float32))
    return (final_state, embed_grad, weight_grads[0], weight_grads[1], weight_grads[2], weight_grads[3], weight_grads[4], weight_grads[5])
```

```python
from functools import partial
import math

import jax
import jax.numpy as jnp
from jax import lax
from jax.sharding import PartitionSpec as P

BACK = 1


rope_base = 50000.0
norm_eps = 1e-06
masked_score = -1e30


def rope_angles(positions, head_dim):
    freq_index = jnp.arange(head_dim // 2, dtype=jnp.float32)
    inv_freq = 1.0 / rope_base ** (2.0 * freq_index / head_dim)
    angles = positions.astype(jnp.float32)[:, None] * inv_freq[None, :]
    return (jnp.cos(angles), jnp.sin(angles))


def rotate_fwd(values, cos_t, sin_t):
    half_dim = values.shape[-1] // 2
    first_half = values[..., :half_dim]
    second_half = values[..., half_dim:]
    return jnp.concatenate(
        [first_half * cos_t - second_half * sin_t, second_half * cos_t + first_half * sin_t],
        axis=-1,
    )


def rotate_back(grad_vals, cos_t, sin_t):
    half_dim = grad_vals.shape[-1] // 2
    first_half = grad_vals[..., :half_dim]
    second_half = grad_vals[..., half_dim:]
    return jnp.concatenate(
        [first_half * cos_t + second_half * sin_t, second_half * cos_t - first_half * sin_t],
        axis=-1,
    )


def rms_parts(rows):
    factor = lax.rsqrt(jnp.mean(rows * rows, axis=-1, keepdims=True) + norm_eps)
    return (rows * factor, factor)


def score_block(query_blk, key_blk, doc_query, doc_key, query_pos, key_pos, score_scale):
    scores = (
        jnp.einsum("qhd,khd->hqk", query_blk, key_blk, preferred_element_type=jnp.float32)
        * score_scale
    )
    allowed = (key_pos[None, :] <= query_pos[:, None]) & (doc_query[:, None] == doc_key[None, :])
    return jnp.where(allowed[None], scores, masked_score)


def attend_block(packed, query_pos, key_pos, score_scale):
    query_blk, key_blk, value_blk, doc_query, doc_key = packed
    scores = score_block(query_blk, key_blk, doc_query, doc_key, query_pos, key_pos, score_scale)
    row_max = jnp.max(scores, axis=-1, keepdims=True)
    exp_vals = jnp.exp(scores - row_max)
    totals = jnp.sum(exp_vals, axis=-1, keepdims=True)
    prob_vals = exp_vals / totals
    head_vals = jnp.einsum(
        "hqk,khd->qhd",
        prob_vals.astype(jnp.bfloat16),
        value_blk,
        preferred_element_type=jnp.float32,
    )
    return (head_vals.astype(jnp.bfloat16), row_max + jnp.log(totals))


def attend_back(packed, query_pos, key_pos, score_scale):
    query_blk, key_blk, value_blk, grad_blk, lse_blk, doc_query, doc_key = packed
    scores = score_block(query_blk, key_blk, doc_query, doc_key, query_pos, key_pos, score_scale)
    prob_vals = jnp.exp(scores - lse_blk)
    grad_value = jnp.einsum(
        "hqk,qhd->khd", prob_vals.astype(jnp.bfloat16), grad_blk, preferred_element_type=jnp.float32
    )
    grad_prob = jnp.einsum("qhd,khd->hqk", grad_blk, value_blk, preferred_element_type=jnp.float32)
    row_dot = jnp.sum(prob_vals * grad_prob, axis=-1, keepdims=True)
    grad_score = (prob_vals * (grad_prob - row_dot)).astype(jnp.bfloat16)
    grad_query = (
        jnp.einsum("hqk,khd->qhd", grad_score, key_blk, preferred_element_type=jnp.float32)
        * score_scale
    )
    grad_key = (
        jnp.einsum("hqk,qhd->khd", grad_score, query_blk, preferred_element_type=jnp.float32)
        * score_scale
    )
    return (grad_query, grad_key, grad_value)


def shards(
    embedded,
    initial_state,
    cotangent,
    doc_ids,
    recurrences,
    adapter_weight,
    norm_gains,
    qkv_weight,
    output_head_weight,
    gate_up_weight,
    down_weight,
):
    n_dp = lax.axis_size("dp")
    n_tensor = lax.axis_size("tensor")
    n_context = lax.axis_size("context")
    dp_index = lax.axis_index("dp")
    t_index = lax.axis_index("tensor")
    ctx_index = lax.axis_index("context")
    seq_count, block_rows, model_width = embedded.shape
    seq_len = doc_ids.shape[1]
    half = n_tensor // seq_count
    group = t_index // half
    part = t_index % half
    heads_here = qkv_weight.shape[1]
    head_dim = qkv_weight.shape[2] // 3
    ff_here = down_weight.shape[0]
    score_scale = 1.0 / math.sqrt(head_dim)
    pair_swap = [(i, (i + half) % n_tensor) for i in range(n_tensor)]
    members = half * n_context
    groups = [
        [g * members + i for i in range(members)] for g in range(seq_count)
    ]

    def swap_in(rows):
        own = lax.dynamic_index_in_dim(rows, group, 0, keepdims=False)
        other = lax.dynamic_index_in_dim(rows, 1 - group, 0, keepdims=False)
        got = lax.ppermute(other, "tensor", pair_swap)
        first = jnp.where(group == 0, own, got)
        second = jnp.where(group == 0, got, own)
        return jnp.concatenate([first, second], axis=0)

    def swap_out(rows):
        first, second = rows[:block_rows], rows[block_rows:]
        own = jnp.where(group == 0, first, second)
        other = jnp.where(group == 0, second, first)
        got = lax.ppermute(other, "tensor", pair_swap)
        return jnp.stack(
            [jnp.where(group == 0, own, got), jnp.where(group == 0, got, own)], axis=0
        )

    def role_perm(flip):
        pairs = []
        for t in range(n_tensor):
            for c in range(n_context):
                g = (c + flip) % n_context
                dest = (g * half + t // n_context) * n_context + t % n_context
                pairs.append((t * n_context + c, dest))
        return pairs

    role_perms = [role_perm(0), role_perm(1)]

    def role_weight(block, axis):
        got = [lax.ppermute(block, ("tensor", "context"), perm) for perm in role_perms]
        low = jnp.where(group == 0, got[0], got[1])
        high = jnp.where(group == 0, got[1], got[0])
        both = jnp.concatenate([low, high], axis=axis)
        return lax.all_gather(both, "dp", axis=axis, tiled=True)

    def role_grad(grad, axis):
        piece = lax.psum_scatter(
            grad.astype(jnp.bfloat16), "dp", scatter_dimension=axis, tiled=True
        )
        low, high = jnp.split(piece, 2, axis=axis)
        give = [jnp.where(group == 0, low, high), jnp.where(group == 0, high, low)]
        back = [
            lax.ppermute(g, ("tensor", "context"), [(b, a) for a, b in perm])
            for g, perm in zip(give, role_perms)
        ]
        return back[0].astype(jnp.float32) + back[1].astype(jnp.float32)

    def gather_rows(rows):
        return lax.all_gather(
            rows, ("tensor", "context"), axis=0, tiled=True, axis_index_groups=groups
        )

    def sum_rows(partial_rows):
        return lax.psum_scatter(
            partial_rows.astype(jnp.bfloat16),
            ("tensor", "context"),
            scatter_dimension=0,
            tiled=True,
            axis_index_groups=groups,
        ).astype(jnp.float32)

    embed_rows = swap_in(embedded)
    state_rows = swap_in(initial_state)
    cot_rows = swap_in(cotangent)
    adapter_full = lax.all_gather(adapter_weight, ("dp", "context"), axis=0, tiled=True)
    gains_full = lax.all_gather(norm_gains, ("dp", "context"), axis=1, tiled=True)
    qkv_use = role_weight(qkv_weight, 0)
    out_use = role_weight(output_head_weight, 2)
    gate_up_use = role_weight(gate_up_weight, 0)
    down_use = role_weight(down_weight, 1)
    gains_f = gains_full.astype(jnp.float32)

    order = (
        jnp.arange(seq_len, dtype=jnp.int32)
        .reshape(seq_count, half, n_context, block_rows)
        .transpose(1, 2, 0, 3)
        .reshape(-1)
    )
    cos_t, sin_t = rope_angles(order, head_dim)
    cos_t = cos_t[:, None, :]
    sin_t = sin_t[:, None, :]
    own_seq = dp_index * seq_count + group
    docs = lax.dynamic_index_in_dim(doc_ids, own_seq, 0, keepdims=False)[order]
    steps_own = lax.dynamic_index_in_dim(recurrences, own_seq, 0, keepdims=False) - BACK
    embed_part = jnp.dot(
        embed_rows, adapter_full[model_width:], preferred_element_type=jnp.float32
    )

    def core_step(latent):
        low = latent.astype(jnp.bfloat16)
        adapted = (
            jnp.dot(low, adapter_full[:model_width], preferred_element_type=jnp.float32)
            + embed_part
        )
        unit_a, factor_a = rms_parts(adapted)
        normed_a = (unit_a * gains_f[0]).astype(jnp.bfloat16)
        feature_rows = gather_rows(normed_a)
        proj = jnp.einsum(
            "bx,xyf->byf", feature_rows, qkv_use, preferred_element_type=jnp.float32
        )
        query_rot = rotate_fwd(proj[..., :head_dim], cos_t, sin_t).astype(jnp.bfloat16)
        key_rot = rotate_fwd(proj[..., head_dim : 2 * head_dim], cos_t, sin_t).astype(
            jnp.bfloat16
        )
        value_rows = proj[..., 2 * head_dim :].astype(jnp.bfloat16)
        head_vals, lse_vals = attend_block(
            (query_rot, key_rot, value_rows, docs, docs), order, order, score_scale
        )
        attn_part = jnp.einsum(
            "qhd,hdm->qm", head_vals, out_use, preferred_element_type=jnp.float32
        )
        mixed_rows = adapted + sum_rows(attn_part)
        unit_b, factor_b = rms_parts(mixed_rows)
        normed_b = (unit_b * gains_f[1]).astype(jnp.bfloat16)
        ffn_input = gather_rows(normed_b)
        gate_up = jnp.einsum(
            "qd,dgf->qgf", ffn_input, gate_up_use, preferred_element_type=jnp.float32
        )
        gate_pre = gate_up[:, 0]
        up_pre = gate_up[:, 1]
        hidden = (jax.nn.silu(gate_pre) * up_pre).astype(jnp.bfloat16)
        ffn_part = jnp.dot(hidden, down_use, preferred_element_type=jnp.float32)
        result = mixed_rows + sum_rows(ffn_part)
        saved = (
            low,
            adapted,
            feature_rows,
            query_rot,
            key_rot,
            value_rows,
            head_vals,
            lse_vals,
            mixed_rows,
            ffn_input,
            gate_pre,
            up_pre,
            hidden,
        )
        return result, saved

    def advance(step_index, current):
        return jnp.where(step_index < steps_own, core_step(current)[0], current)

    detached = lax.fori_loop(
        0, jnp.max(recurrences) - BACK, advance, state_rows.astype(jnp.float32)
    )
    current, saved = core_step(detached)
    (
        latent_low,
        adapted,
        feature_rows,
        query_rot,
        key_rot,
        value_rows,
        head_vals,
        lse_vals,
        mixed_rows,
        ffn_input,
        gate_pre,
        up_pre,
        hidden,
    ) = saved
    grad_out = cot_rows.astype(jnp.float32)
    grad_ffn = gather_rows(cot_rows)
    down_g = jnp.einsum("qf,qd->fd", hidden, grad_ffn, preferred_element_type=jnp.float32)
    grad_hidden = jnp.einsum("qd,fd->qf", grad_ffn, down_use, preferred_element_type=jnp.float32)
    sig = jax.nn.sigmoid(gate_pre)
    grad_gate = grad_hidden * up_pre * sig * (1.0 + gate_pre * (1.0 - sig))
    grad_up = grad_hidden * jax.nn.silu(gate_pre)
    grad_pair = jnp.stack([grad_gate, grad_up], axis=1).astype(jnp.bfloat16)
    gate_up_g = jnp.einsum(
        "qd,qgf->dgf", ffn_input, grad_pair, preferred_element_type=jnp.float32
    )
    grad_normb = sum_rows(
        jnp.einsum("qgf,dgf->qd", grad_pair, gate_up_use, preferred_element_type=jnp.float32)
    )
    unit_b, factor_b = rms_parts(mixed_rows)
    weighted_b = grad_normb * gains_f[1]
    gain_b = jnp.sum(grad_normb * unit_b, axis=0)
    grad_mixed = grad_out + factor_b * (
        weighted_b - unit_b * jnp.mean(weighted_b * unit_b, axis=-1, keepdims=True)
    )
    grad_heads = gather_rows(grad_mixed.astype(jnp.bfloat16))
    out_g = jnp.einsum("qhd,qm->hdm", head_vals, grad_heads, preferred_element_type=jnp.float32)
    grad_head_vals = jnp.einsum(
        "qm,hdm->qhd", grad_heads, out_use, preferred_element_type=jnp.float32
    ).astype(jnp.bfloat16)
    grad_query, grad_key, grad_value = attend_back(
        (query_rot, key_rot, value_rows, grad_head_vals, lse_vals, docs, docs),
        order,
        order,
        score_scale,
    )
    grad_proj = jnp.concatenate(
        [
            rotate_back(grad_query, cos_t, sin_t),
            rotate_back(grad_key, cos_t, sin_t),
            grad_value,
        ],
        axis=-1,
    ).astype(jnp.bfloat16)
    qkv_g = jnp.einsum(
        "xq,xtu->qtu", feature_rows, grad_proj, preferred_element_type=jnp.float32
    )
    grad_norma = sum_rows(
        jnp.einsum("aew,iew->ai", grad_proj, qkv_use, preferred_element_type=jnp.float32)
    )
    unit_a, factor_a = rms_parts(adapted)
    weighted_a = grad_norma * gains_f[0]
    gain_a = jnp.sum(grad_norma * unit_a, axis=0)
    grad_adapted = grad_mixed + factor_a * (
        weighted_a - unit_a * jnp.mean(weighted_a * unit_a, axis=-1, keepdims=True)
    )
    adapted_low = grad_adapted.astype(jnp.bfloat16)
    joined = jnp.concatenate([latent_low, embed_rows], axis=-1)
    adapter_g = jnp.einsum("rk,rd->kd", joined, adapted_low, preferred_element_type=jnp.float32)
    embed_out = jnp.einsum(
        "srd,kd->srk",
        swap_out(adapted_low),
        adapter_full[model_width:],
        preferred_element_type=jnp.float32,
    )
    down_s = role_grad(down_g, 1)
    gate_up_s = role_grad(gate_up_g, 0)
    out_s = role_grad(out_g, 2)
    qkv_s = role_grad(qkv_g, 0)
    adapter_s = lax.psum_scatter(
        adapter_g.astype(jnp.bfloat16), ("dp", "context"), scatter_dimension=0, tiled=True
    )
    gains_s = lax.psum_scatter(
        jnp.stack([gain_a, gain_b]).astype(jnp.bfloat16),
        ("dp", "context"),
        scatter_dimension=1,
        tiled=True,
    )
    adapter_s = lax.psum(adapter_s, "tensor").astype(jnp.float32)
    gains_s = lax.psum(gains_s, "tensor").astype(jnp.float32)
    return (swap_out(current), embed_out, adapter_s, gains_s, qkv_s, out_s, gate_up_s, down_s)


def solution(mesh):
    placed = (
        P("dp", ("tensor", "context"), None),
        P("dp", ("tensor", "context"), None),
        P("dp", ("tensor", "context"), None),
        P(),
        P(),
        P(("dp", "context"), None),
        P(None, ("dp", "context")),
        P(("dp", "context"), "tensor", None),
        P("tensor", None, ("dp", "context")),
        P(("dp", "context"), None, "tensor"),
        P("tensor", ("dp", "context")),
    )
    return jax.shard_map(
        shards,
        mesh=mesh,
        in_specs=placed,
        out_specs=(
            P("dp", ("tensor", "context"), None),
            P("dp", ("tensor", "context"), None),
            P(("dp", "context"), None),
            P(None, ("dp", "context")),
            P(("dp", "context"), "tensor", None),
            P("tensor", None, ("dp", "context")),
            P(("dp", "context"), None, "tensor"),
            P("tensor", ("dp", "context")),
        ),
        check_vma=False,
    )
```

```python
from functools import partial
import math
from typing import NamedTuple

import jax
import jax.numpy as jnp
from jax import lax
from jax.experimental import pallas as pl
from jax.experimental.pallas import tpu as pltpu
from jax.sharding import PartitionSpec as P

BACK = 1


rope_base = 50000.0
norm_eps = 1e-06
masked_score = -1e30


def rope_angles(positions, head_dim):
    freq_index = jnp.arange(head_dim // 2, dtype=jnp.float32)
    inv_freq = 1.0 / rope_base ** (2.0 * freq_index / head_dim)
    angles = positions.astype(jnp.float32)[:, None] * inv_freq[None, :]
    return (jnp.cos(angles), jnp.sin(angles))


def rotate_fwd(values, cos_t, sin_t):
    half_dim = values.shape[-1] // 2
    first_half = values[..., :half_dim]
    second_half = values[..., half_dim:]
    return jnp.concatenate(
        [first_half * cos_t - second_half * sin_t, second_half * cos_t + first_half * sin_t],
        axis=-1,
    )


def rotate_back(grad_vals, cos_t, sin_t):
    half_dim = grad_vals.shape[-1] // 2
    first_half = grad_vals[..., :half_dim]
    second_half = grad_vals[..., half_dim:]
    return jnp.concatenate(
        [first_half * cos_t + second_half * sin_t, second_half * cos_t - first_half * sin_t],
        axis=-1,
    )


def rms_parts(rows):
    factor = lax.rsqrt(jnp.mean(rows * rows, axis=-1, keepdims=True) + norm_eps)
    return (rows * factor, factor)


def score_block(query_blk, key_blk, doc_query, doc_key, query_pos, key_pos, score_scale):
    scores = (
        jnp.einsum("qhd,khd->hqk", query_blk, key_blk, preferred_element_type=jnp.float32)
        * score_scale
    )
    allowed = (key_pos[None, :] <= query_pos[:, None]) & (doc_query[:, None] == doc_key[None, :])
    return jnp.where(allowed[None], scores, masked_score)


def attend_block(packed, query_pos, key_pos, score_scale):
    query_blk, key_blk, value_blk, doc_query, doc_key = packed
    scores = score_block(query_blk, key_blk, doc_query, doc_key, query_pos, key_pos, score_scale)
    row_max = jnp.max(scores, axis=-1, keepdims=True)
    exp_vals = jnp.exp(scores - row_max)
    totals = jnp.sum(exp_vals, axis=-1, keepdims=True)
    prob_vals = exp_vals / totals
    head_vals = jnp.einsum(
        "hqk,khd->qhd",
        prob_vals.astype(jnp.bfloat16),
        value_blk,
        preferred_element_type=jnp.float32,
    )
    return (head_vals.astype(jnp.bfloat16), row_max + jnp.log(totals))


def attend_back(packed, query_pos, key_pos, score_scale):
    query_blk, key_blk, value_blk, grad_blk, lse_blk, doc_query, doc_key = packed
    scores = score_block(query_blk, key_blk, doc_query, doc_key, query_pos, key_pos, score_scale)
    prob_vals = jnp.exp(scores - lse_blk)
    grad_value = jnp.einsum(
        "hqk,qhd->khd", prob_vals.astype(jnp.bfloat16), grad_blk, preferred_element_type=jnp.float32
    )
    grad_prob = jnp.einsum("qhd,khd->hqk", grad_blk, value_blk, preferred_element_type=jnp.float32)
    row_dot = jnp.sum(prob_vals * grad_prob, axis=-1, keepdims=True)
    grad_score = (prob_vals * (grad_prob - row_dot)).astype(jnp.bfloat16)
    grad_query = (
        jnp.einsum("hqk,khd->qhd", grad_score, key_blk, preferred_element_type=jnp.float32)
        * score_scale
    )
    grad_key = (
        jnp.einsum("hqk,qhd->khd", grad_score, query_blk, preferred_element_type=jnp.float32)
        * score_scale
    )
    return (grad_query, grad_key, grad_value)


MESH = pl.DeviceIdType.MESH
LOG2E = 1.4426950408889634
VMEM_BYTES = 62 << 20


class Sizes(NamedTuple):
    n_tensor: int
    n_context: int
    seqs: int
    half: int
    block: int
    tile: int
    rows: int
    seq_len: int
    width: int
    heads: int
    head_dim: int
    ff: int


def full_spec():
    return pl.BlockSpec(memory_space=pltpu.VMEM)


def any_spec():
    return pl.BlockSpec(memory_space=pl.ANY)


def nt_dot(a, b):
    return lax.dot_general(a, b, (((1,), (1,)), ((), ())), preferred_element_type=jnp.float32)


def tn_dot(a, b):
    return lax.dot_general(a, b, (((0,), (0,)), ((), ())), preferred_element_type=jnp.float32)


def nn_dot(a, b):
    return jnp.dot(a, b, preferred_element_type=jnp.float32)


class Place:
    def __init__(self, sz):
        t = lax.axis_index("tensor")
        self.sz = sz
        self.dp = lax.axis_index("dp")
        self.ctx = lax.axis_index("context")
        self.group = t // sz.half
        self.part = lax.rem(t, sz.half)

    def device(self, part, ctx):
        return (self.dp, self.group * self.sz.half + part, ctx)

    def ahead(self, q):
        return lax.rem(self.part + q, self.sz.half)

    def behind(self, q):
        return lax.rem(self.part + (self.sz.half - q), self.sz.half)

    def sibling(self):
        return self.device(self.part, 1 - self.ctx)

    def block(self, part, ctx, j):
        sz = self.sz
        first = ((part + j * sz.half) * sz.n_context + ctx) * sz.block
        return pl.ds(pl.multiple_of(first, sz.block), sz.block)

    def tile(self, q, j):
        sz = self.sz
        first = (self.ahead(q) + j * sz.half) * sz.tile
        return pl.ds(pl.multiple_of(first, sz.tile), sz.tile)

    def enter(self):
        barrier = pltpu.get_barrier_semaphore()
        pl.semaphore_signal(
            barrier, inc=1, device_id=self.sibling(), device_id_type=MESH
        )
        for q in range(1, self.sz.half):
            pl.semaphore_signal(
                barrier,
                inc=1,
                device_id=self.device(self.ahead(q), self.ctx),
                device_id_type=MESH,
            )
        pl.semaphore_wait(barrier, self.sz.half)


class Gather:
    @staticmethod
    def scratch(sz):
        kinds = 2 * sz.half - 1
        return [
            pltpu.SemaphoreType.DMA((kinds, sz.seqs)),
            pltpu.SemaphoreType.DMA((kinds, sz.seqs)),
        ]

    def __init__(self, place, ref, send, recv):
        self.place, self.ref, self.send, self.recv = place, ref, send, recv

    def copy(self, kind, j, rows):
        place, half = self.place, self.place.sz.half
        if 0 < kind < half:
            target = place.device(place.ahead(kind), place.ctx)
        else:
            target = place.sibling()
        return pltpu.make_async_remote_copy(
            src_ref=self.ref.at[rows],
            dst_ref=self.ref.at[rows],
            send_sem=self.send.at[kind, j],
            recv_sem=self.recv.at[kind, j],
            device_id=target,
            device_id_type=MESH,
        )

    def own(self, j):
        return self.place.block(self.place.part, self.place.ctx, j)

    def start(self, j):
        for q in range(1, self.place.sz.half):
            self.copy(q, j, self.own(j)).start()
        self.copy(0, j, self.own(j)).start()

    def wait_near(self, j):
        place = self.place
        self.copy(0, j, place.block(place.part, 1 - place.ctx, j)).wait_recv()

    def forward(self, q, j):
        place = self.place
        rows = place.block(place.behind(q), place.ctx, j)
        self.copy(q, j, rows).wait_recv()
        self.copy(place.sz.half - 1 + q, j, rows).start()

    def wait_far(self, q, j):
        place = self.place
        rows = place.block(place.behind(q), 1 - place.ctx, j)
        self.copy(place.sz.half - 1 + q, j, rows).wait_recv()

    def finish(self):
        place, half = self.place, self.place.sz.half
        for j in range(place.sz.seqs):
            for kind in range(half):
                self.copy(kind, j, self.own(j)).wait_send()
            for q in range(1, half):
                rows = place.block(place.behind(q), place.ctx, j)
                self.copy(half - 1 + q, j, rows).wait_send()


class Scatter:
    @staticmethod
    def scratch(sz):
        kinds = 2 * sz.half - 1
        near = (sz.half, sz.seqs, sz.block, sz.width)
        far = (max(sz.half - 1, 1), sz.seqs, sz.block, sz.width)
        return [
            pltpu.VMEM((sz.tile, sz.width), jnp.float32),
            pltpu.VMEM(near, jnp.float32),
            pltpu.VMEM(near, jnp.bfloat16),
            pltpu.VMEM(near, jnp.bfloat16),
            pltpu.VMEM(far, jnp.bfloat16),
            pltpu.VMEM(far, jnp.bfloat16),
            pltpu.SemaphoreType.DMA((kinds, sz.seqs)),
            pltpu.SemaphoreType.DMA((kinds, sz.seqs)),
        ]

    def __init__(self, place, part, mine, near_out, near_in, far_out, far_in, send, recv):
        self.place, self.part, self.mine = place, part, mine
        self.near_out, self.near_in = near_out, near_in
        self.far_out, self.far_in = far_out, far_in
        self.send, self.recv = send, recv

    def near(self, q, j):
        return pltpu.make_async_remote_copy(
            src_ref=self.near_out.at[q, j],
            dst_ref=self.near_in.at[q, j],
            send_sem=self.send.at[q, j],
            recv_sem=self.recv.at[q, j],
            device_id=self.place.sibling(),
            device_id_type=MESH,
        )

    def far(self, q, j):
        place = self.place
        return pltpu.make_async_remote_copy(
            src_ref=self.far_out.at[q - 1, j],
            dst_ref=self.far_in.at[q - 1, j],
            send_sem=self.send.at[place.sz.half - 1 + q, j],
            recv_sem=self.recv.at[place.sz.half - 1 + q, j],
            device_id=place.device(place.ahead(q), place.ctx),
            device_id_type=MESH,
        )

    def give(self, q, j):
        sz, ctx = self.place.sz, self.place.ctx
        mine = pl.ds(pl.multiple_of(ctx * sz.block, sz.block), sz.block)
        other = pl.ds(pl.multiple_of((1 - ctx) * sz.block, sz.block), sz.block)
        self.near_out[q, j] = self.part[other, :].astype(jnp.bfloat16)
        self.near(q, j).start()
        self.mine[q, j] = self.part[mine, :]

    def onward(self, q, j):
        self.near(q, j).wait_recv()
        self.far_out[q - 1, j] = (
            self.mine[q, j] + self.near_in[q, j].astype(jnp.float32)
        ).astype(jnp.bfloat16)
        self.far(q, j).start()

    def total(self, j):
        self.near(0, j).wait_recv()
        total = self.mine[0, j] + self.near_in[0, j].astype(jnp.float32)
        for q in range(1, self.place.sz.half):
            self.far(q, j).wait_recv()
            total = total + self.far_in[q - 1, j].astype(jnp.float32)
        return total

    def finish(self):
        half = self.place.sz.half
        for j in range(self.place.sz.seqs):
            for q in range(half):
                self.near(q, j).wait_send()
            for q in range(1, half):
                self.far(q, j).wait_send()


def column_loads(blocks_ref, vmem_ref, sem):
    count, _, columns = blocks_ref.shape
    return [
        pltpu.make_async_copy(
            blocks_ref.at[b], vmem_ref.at[:, pl.ds(b * columns, columns)], sem.at[b]
        )
        for b in range(count)
    ]


def split_loads(src_ref, vmem_ref, sem, count):
    columns = src_ref.shape[1] // count
    return [
        pltpu.make_async_copy(
            src_ref.at[:, pl.ds(n * columns, columns)],
            vmem_ref.at[:, pl.ds(n * columns, columns)],
            sem.at[n],
        )
        for n in range(count)
    ]


def rms_factor(rows):
    return lax.rsqrt(jnp.mean(rows * rows, axis=-1, keepdims=True) + norm_eps)


def turn(x, cos_t, sin_t):
    return x * cos_t + pltpu.roll(x, x.shape[-1] // 2, 1) * sin_t


def attn_kernel(sz, keep, *refs):
    (latent, embed, gains, cos_t, sin_t, begin, adapter_hbm, qkv_hbm, out_hbm) = refs[:9]
    refs = refs[9:]
    mixed = refs[0]
    refs = refs[1:]
    if keep:
        adapted_out, rows_out, q_out, k_out, v_out, head_out, lse_out = refs[:7]
        refs = refs[7:]
    (wa, wqkv, wout, adapted, rows_s, q_s, k_s, v_s, head_s, lse_s) = refs[:10]
    load_a, load_qkv, load_out, keep_sem = refs[10:14]
    gather_refs = refs[14:16]
    scatter_refs = refs[16:]

    place = Place(sz)
    a_loads = split_loads(adapter_hbm, wa, load_a, load_a.shape[0])
    qkv_load = pltpu.make_async_copy(qkv_hbm, wqkv, load_qkv)
    out_loads = column_loads(out_hbm, wout, load_out)
    for copy in a_loads:
        copy.start()
    qkv_load.start()
    for copy in out_loads:
        copy.start()
    place.enter()
    gather = Gather(place, rows_s, *gather_refs)
    scatter = Scatter(place, *scatter_refs)

    low = latent[...].astype(jnp.bfloat16)
    columns = sz.width // len(a_loads)
    square = None
    for n, copy in enumerate(a_loads):
        copy.wait()
        cols = pl.ds(n * columns, columns)
        chunk = nn_dot(low, wa[:, cols]) + embed[:, cols]
        adapted[:, cols] = chunk
        here = jnp.sum(chunk * chunk, axis=-1, keepdims=True)
        square = here if square is None else square + here
    factor = lax.rsqrt(square / sz.width + norm_eps)
    for j in range(sz.seqs):
        span = slice(j * sz.block, (j + 1) * sz.block)
        normed = (adapted[span, :] * factor[span]) * gains[0:1, :]
        rows_s[gather.own(j), :] = normed.astype(jnp.bfloat16)
        gather.start(j)

    qkv_load.wait()
    pair = min(2, sz.heads)
    d = sz.head_dim

    def project(q, j):
        rows = place.tile(q, j)
        x = rows_s[rows, :]
        cos_here, sin_here = cos_t[rows, :], sin_t[rows, :]
        for h0 in range(0, sz.heads, pair):
            proj = nn_dot(x, wqkv[:, 3 * d * h0 : 3 * d * (h0 + pair)])
            for h in range(pair):
                at = 3 * d * h
                q_s[h0 + h, rows, :] = turn(proj[:, at : at + d], cos_here, sin_here).astype(
                    jnp.bfloat16
                )
                k_s[h0 + h, rows, :] = turn(
                    proj[:, at + d : at + 2 * d], cos_here, sin_here
                ).astype(jnp.bfloat16)
                v_s[h0 + h, rows, :] = proj[:, at + 2 * d : at + 3 * d].astype(jnp.bfloat16)

    def attend(q, j):
        rows = place.tile(q, j)
        first = (place.ahead(q) + j * sz.half) * sz.tile
        length = (j + 1) * sz.half * sz.tile
        start = begin[:, pl.ds(pl.multiple_of(first, sz.tile), sz.tile)]
        key_at = lax.broadcasted_iota(jnp.int32, (length, sz.tile), 0)
        query_at = first + lax.broadcasted_iota(jnp.int32, (1, sz.tile), 1)
        allowed = (key_at >= start) & (key_at <= query_at)

        def head(h, carry):
            scores = nt_dot(k_s[h, 0:length, :], q_s[h, rows, :])
            scores = jnp.where(allowed, scores * (LOG2E / math.sqrt(d)), masked_score)
            top = jnp.max(scores, axis=0, keepdims=True)
            weight = jnp.exp2(scores - top)
            total = jnp.sum(weight, axis=0, keepdims=True)
            mixed_t = tn_dot(v_s[h, 0:length, :], weight.astype(jnp.bfloat16))
            result = jnp.transpose(mixed_t / total)
            head_s[rows, pl.ds(pl.multiple_of(h * d, d), d)] = result.astype(jnp.bfloat16)
            if keep:
                lse_s[h, :, rows] = top + jnp.log2(total)
            return carry

        lax.fori_loop(0, sz.heads, head, 0)

    def give(q, j):
        rows = place.tile(q, j)
        scatter.part[...] = nn_dot(head_s[rows, :], wout[...])
        scatter.give(q, j)

    copies = []

    def save(src, dst):
        copy = pltpu.make_async_copy(src, dst, keep_sem.at[len(copies)])
        copy.start()
        copies.append(copy)

    if keep:
        save(adapted, adapted_out)
    far = range(1, sz.half)
    for j in range(sz.seqs):
        gather.wait_near(j)
        project(0, j)
    for copy in out_loads:
        copy.wait()
    for j in range(sz.seqs):
        for q in far:
            gather.forward(q, j)
        for q in far:
            gather.wait_far(sz.half - q, j)
            project(q, j)
        for q in far:
            attend(q, j)
            give(q, j)
        attend(0, j)
        for q in far:
            scatter.onward(q, j)
        give(0, j)
    if keep:
        for src, dst in ((rows_s, rows_out), (q_s, q_out), (k_s, k_out), (v_s, v_out)):
            save(src, dst)
        save(head_s, head_out)
        save(lse_s, lse_out)
    gather.finish()
    for j in range(sz.seqs):
        span = slice(j * sz.block, (j + 1) * sz.block)
        mixed[span, :] = adapted[span, :] + scatter.total(j)
    scatter.finish()
    for copy in copies:
        copy.wait()


def run_attn(sz, keep, latent, embed_part, gains, cos_t, sin_t, begin, adapter, qkv, out):
    f32, bf16 = jnp.float32, jnp.bfloat16
    heads_shape = (sz.heads, sz.seq_len, sz.head_dim)
    shape = jax.ShapeDtypeStruct
    outs = [shape((sz.rows, sz.width), f32)]
    if keep:
        outs += [
            shape((sz.rows, sz.width), f32),
            shape((sz.seq_len, sz.width), bf16),
            shape(heads_shape, bf16),
            shape(heads_shape, bf16),
            shape(heads_shape, bf16),
            shape((sz.seq_len, sz.heads * sz.head_dim), bf16),
            shape((sz.heads, 1, sz.seq_len), f32),
        ]
    scratch = [
        pltpu.VMEM(adapter.shape, bf16),
        pltpu.VMEM(qkv.shape, bf16),
        pltpu.VMEM((sz.heads * sz.head_dim, sz.width), bf16),
        pltpu.VMEM((sz.rows, sz.width), f32),
        pltpu.VMEM((sz.seq_len, sz.width), bf16),
        pltpu.VMEM(heads_shape, bf16),
        pltpu.VMEM(heads_shape, bf16),
        pltpu.VMEM(heads_shape, bf16),
        pltpu.VMEM((sz.seq_len, sz.heads * sz.head_dim), bf16),
        pltpu.VMEM((sz.heads, 1, sz.seq_len), f32),
        pltpu.SemaphoreType.DMA((4,)),
        pltpu.SemaphoreType.DMA,
        pltpu.SemaphoreType.DMA((out.shape[0],)),
        pltpu.SemaphoreType.DMA((8,)),
    ]
    scratch += Gather.scratch(sz) + Scatter.scratch(sz)
    flops = 2 * sz.rows * sz.width * sz.width + 2 * sz.seq_len * sz.width * qkv.shape[1]
    return pl.pallas_call(
        partial(attn_kernel, sz, keep),
        out_shape=outs,
        in_specs=[full_spec()] * 6 + [any_spec()] * 3,
        out_specs=[full_spec()] + [any_spec()] * (len(outs) - 1),
        scratch_shapes=scratch,
        compiler_params=pltpu.CompilerParams(
            collective_id=2 if keep else 1, has_side_effects=True, vmem_limit_bytes=VMEM_BYTES
        ),
        cost_estimate=pl.CostEstimate(
            flops=flops, bytes_accessed=20 << 20, transcendentals=0
        ),
        name="attn_keep" if keep else "attn_round",
    )(latent, embed_part, gains, cos_t, sin_t, begin, adapter, qkv, out)


def ffn_kernel(sz, keep, *refs):
    (mixed, latent, active, gains, gate_hbm, up_hbm, down_hbm, result) = refs[:8]
    refs = refs[8:]
    if keep:
        rows_out, gate_out, up_out, hidden_out = refs[:4]
        refs = refs[4:]
    wg, wu, wd, rows_s = refs[:4]
    refs = refs[4:]
    if keep:
        gate_s, up_s, hidden_s = refs[:3]
        refs = refs[3:]
    load_gu, load_down, keep_sem = refs[:3]
    gather_refs = refs[3:5]
    scatter_refs = refs[5:]

    place = Place(sz)
    gate_load = pltpu.make_async_copy(gate_hbm, wg, load_gu.at[0])
    up_load = pltpu.make_async_copy(up_hbm, wu, load_gu.at[1])
    down_loads = column_loads(down_hbm, wd, load_down)
    gate_load.start()
    up_load.start()
    for copy in down_loads:
        copy.start()
    place.enter()
    gather = Gather(place, rows_s, *gather_refs)
    scatter = Scatter(place, *scatter_refs)
    for j in range(sz.seqs):
        span = slice(j * sz.block, (j + 1) * sz.block)
        rows = mixed[span, :]
        normed = (rows * rms_factor(rows)) * gains[1:2, :]
        rows_s[gather.own(j), :] = normed.astype(jnp.bfloat16)
        gather.start(j)
    gate_load.wait()
    up_load.wait()
    for copy in down_loads:
        copy.wait()

    copies = []

    def save(src, dst):
        copy = pltpu.make_async_copy(src, dst, keep_sem.at[len(copies)])
        copy.start()
        copies.append(copy)

    def work(q, j):
        rows = place.tile(q, j)
        x = rows_s[rows, :]
        gate = nn_dot(x, wg[...])
        up = nn_dot(x, wu[...])
        hidden = (gate / (1.0 + jnp.exp(-gate)) * up).astype(jnp.bfloat16)
        if keep:
            gate_s[rows, :] = gate.astype(jnp.bfloat16)
            up_s[rows, :] = up.astype(jnp.bfloat16)
            hidden_s[rows, :] = hidden
        scatter.part[...] = nn_dot(hidden, wd[...])
        scatter.give(q, j)

    far = range(1, sz.half)
    for j in range(sz.seqs):
        gather.wait_near(j)
        work(0, j)
    for j in range(sz.seqs):
        for q in far:
            gather.forward(q, j)
        for q in far:
            gather.wait_far(sz.half - q, j)
            work(q, j)
        for q in far:
            scatter.onward(q, j)
    if keep:
        save(rows_s, rows_out)
        save(gate_s, gate_out)
        save(up_s, up_out)
        save(hidden_s, hidden_out)
    gather.finish()
    for j in range(sz.seqs):
        span = slice(j * sz.block, (j + 1) * sz.block)
        total = mixed[span, :] + scatter.total(j)
        if not keep:
            total = jnp.where(active[...] > 0, total, latent[span, :])
        result[span, :] = total
    scatter.finish()
    for copy in copies:
        copy.wait()


def run_ffn(sz, keep, mixed, latent, active, gains, gate, up, down):
    f32, bf16 = jnp.float32, jnp.bfloat16
    shape = jax.ShapeDtypeStruct
    outs = [shape((sz.rows, sz.width), f32)]
    if keep:
        outs += [
            shape((sz.seq_len, sz.width), bf16),
            shape((sz.seq_len, sz.ff), bf16),
            shape((sz.seq_len, sz.ff), bf16),
            shape((sz.seq_len, sz.ff), bf16),
        ]
    scratch = [
        pltpu.VMEM(gate.shape, bf16),
        pltpu.VMEM(up.shape, bf16),
        pltpu.VMEM((sz.ff, sz.width), bf16),
        pltpu.VMEM((sz.seq_len, sz.width), bf16),
    ]
    if keep:
        scratch += [pltpu.VMEM((sz.seq_len, sz.ff), bf16)] * 3
    scratch += [
        pltpu.SemaphoreType.DMA((2,)),
        pltpu.SemaphoreType.DMA((down.shape[0],)),
        pltpu.SemaphoreType.DMA((4,)),
    ]
    scratch += Gather.scratch(sz) + Scatter.scratch(sz)
    return pl.pallas_call(
        partial(ffn_kernel, sz, keep),
        out_shape=outs,
        in_specs=[full_spec()] * 4 + [any_spec()] * 3,
        out_specs=[full_spec()] + [any_spec()] * (len(outs) - 1),
        scratch_shapes=scratch,
        compiler_params=pltpu.CompilerParams(
            collective_id=4 if keep else 3, has_side_effects=True, vmem_limit_bytes=VMEM_BYTES
        ),
        cost_estimate=pl.CostEstimate(
            flops=6 * sz.seq_len * sz.width * sz.ff, bytes_accessed=20 << 20, transcendentals=0
        ),
        name="ffn_keep" if keep else "ffn_round",
    )(mixed, latent, active, gains, gate, up, down)


def shards(
    embedded,
    initial_state,
    cotangent,
    doc_ids,
    recurrences,
    adapter_weight,
    norm_gains,
    qkv_weight,
    output_head_weight,
    gate_up_weight,
    down_weight,
):
    n_dp = lax.axis_size("dp")
    n_tensor = lax.axis_size("tensor")
    n_context = lax.axis_size("context")
    dp_index = lax.axis_index("dp")
    t_index = lax.axis_index("tensor")
    ctx_index = lax.axis_index("context")
    seq_count, block_rows, model_width = embedded.shape
    seq_len = doc_ids.shape[1]
    half = n_tensor // seq_count
    group = t_index // half
    part = t_index % half
    heads_here = qkv_weight.shape[1]
    head_dim = qkv_weight.shape[2] // 3
    ff_here = down_weight.shape[0]
    score_scale = 1.0 / math.sqrt(head_dim)
    pair_swap = [(i, (i + half) % n_tensor) for i in range(n_tensor)]
    members = half * n_context
    groups = [
        [g * members + i for i in range(members)] for g in range(seq_count)
    ]

    def swap_in(rows):
        own = lax.dynamic_index_in_dim(rows, group, 0, keepdims=False)
        other = lax.dynamic_index_in_dim(rows, 1 - group, 0, keepdims=False)
        got = lax.ppermute(other, "tensor", pair_swap)
        first = jnp.where(group == 0, own, got)
        second = jnp.where(group == 0, got, own)
        return jnp.concatenate([first, second], axis=0)

    def swap_out(rows):
        first, second = rows[:block_rows], rows[block_rows:]
        own = jnp.where(group == 0, first, second)
        other = jnp.where(group == 0, second, first)
        got = lax.ppermute(other, "tensor", pair_swap)
        return jnp.stack(
            [jnp.where(group == 0, own, got), jnp.where(group == 0, got, own)], axis=0
        )

    def role_perm(flip):
        pairs = []
        for t in range(n_tensor):
            for c in range(n_context):
                g = (c + flip) % n_context
                dest = (g * half + t // n_context) * n_context + t % n_context
                pairs.append((t * n_context + c, dest))
        return pairs

    role_perms = [role_perm(0), role_perm(1)]

    def role_weight(block, axis):
        got = [lax.ppermute(block, ("tensor", "context"), perm) for perm in role_perms]
        low = jnp.where(group == 0, got[0], got[1])
        high = jnp.where(group == 0, got[1], got[0])
        if axis == 0:
            both = jnp.concatenate([low, high], axis=0)
        else:
            both = jnp.stack([low, high], axis=0)
        return lax.all_gather(both, "dp", axis=0, tiled=True)

    def side_by_side(blocks):
        count, depth, columns = blocks.shape
        return blocks.transpose(1, 0, 2).reshape(depth, count * columns)

    def role_grad(grad, axis):
        piece = lax.psum_scatter(
            grad.astype(jnp.bfloat16), "dp", scatter_dimension=axis, tiled=True
        )
        low, high = jnp.split(piece, 2, axis=axis)
        give = [jnp.where(group == 0, low, high), jnp.where(group == 0, high, low)]
        back = [
            lax.ppermute(g, ("tensor", "context"), [(b, a) for a, b in perm])
            for g, perm in zip(give, role_perms)
        ]
        return back[0].astype(jnp.float32) + back[1].astype(jnp.float32)

    def gather_rows(rows):
        full = lax.all_gather(
            rows, ("tensor", "context"), axis=0, tiled=True, axis_index_groups=groups
        )
        split = full.reshape(half, n_context, seq_count, block_rows, model_width)
        return split.transpose(2, 0, 1, 3, 4).reshape(seq_len, model_width)

    def sum_rows(partial_rows):
        split = partial_rows.astype(jnp.bfloat16).reshape(
            seq_count, half, n_context, block_rows, model_width
        )
        return lax.psum_scatter(
            split.transpose(1, 2, 0, 3, 4).reshape(seq_len, model_width),
            ("tensor", "context"),
            scatter_dimension=0,
            tiled=True,
            axis_index_groups=groups,
        ).astype(jnp.float32)

    embed_rows = swap_in(embedded)
    state_rows = swap_in(initial_state)
    cot_rows = swap_in(cotangent)
    adapter_full = lax.all_gather(adapter_weight, ("dp", "context"), axis=0, tiled=True)
    gains_full = lax.all_gather(norm_gains, ("dp", "context"), axis=1, tiled=True)
    qkv_use = role_weight(qkv_weight.reshape(qkv_weight.shape[0], -1), 0)
    out_blocks = role_weight(output_head_weight.reshape(heads_here * head_dim, -1), 1)
    gate_use = role_weight(gate_up_weight[:, 0], 0)
    up_use = role_weight(gate_up_weight[:, 1], 0)
    down_blocks = role_weight(down_weight, 1)
    out_use = side_by_side(out_blocks)
    down_use = side_by_side(down_blocks)
    if out_blocks.shape[2] % 128:
        out_blocks = out_use[None]
        down_blocks = down_use[None]
    gains_f = gains_full.astype(jnp.float32)

    order = jnp.arange(seq_len, dtype=jnp.int32)
    cos_t, sin_t = rope_angles(order, head_dim)
    cos_full = jnp.concatenate([cos_t, cos_t], axis=1)
    sin_full = jnp.concatenate([-sin_t, sin_t], axis=1)
    cos_t = cos_t[:, None, :]
    sin_t = sin_t[:, None, :]
    own_seq = dp_index * seq_count + group
    docs = lax.dynamic_index_in_dim(doc_ids, own_seq, 0, keepdims=False)
    begin = jnp.sum((docs[None, :] < docs[:, None]).astype(jnp.int32), axis=1)[None, :]
    steps_own = lax.dynamic_index_in_dim(recurrences, own_seq, 0, keepdims=False) - BACK
    embed_part = jnp.dot(
        embed_rows, adapter_full[model_width:], preferred_element_type=jnp.float32
    )

    sz = Sizes(
        n_tensor,
        n_context,
        seq_count,
        half,
        block_rows,
        n_context * block_rows,
        seq_count * block_rows,
        seq_len,
        model_width,
        heads_here,
        head_dim,
        ff_here,
    )
    adapter_top = adapter_full[:model_width]

    def advance(step_index, current):
        (mixed,) = run_attn(
            sz, False, current, embed_part, gains_f, cos_full, sin_full, begin,
            adapter_top, qkv_use, out_blocks,
        )
        active = jnp.broadcast_to((step_index < steps_own).astype(jnp.float32), (1, model_width))
        (result,) = run_ffn(
            sz, False, mixed, current, active, gains_f, gate_use, up_use, down_blocks
        )
        return result

    detached = lax.fori_loop(
        0, jnp.max(recurrences) - BACK, advance, state_rows.astype(jnp.float32)
    )
    (mixed_rows, adapted, feature_rows, query_hm, key_hm, value_hm, head_flat, lse) = run_attn(
        sz, True, detached, embed_part, gains_f, cos_full, sin_full, begin,
        adapter_top, qkv_use, out_blocks,
    )
    (current, ffn_input, gate_pre, up_pre, hidden) = run_ffn(
        sz, True, mixed_rows, detached, gains_f[:1], gains_f, gate_use, up_use, down_blocks
    )
    latent_low = detached.astype(jnp.bfloat16)
    query_rot = query_hm.transpose(1, 0, 2)
    key_rot = key_hm.transpose(1, 0, 2)
    value_rows = value_hm.transpose(1, 0, 2)
    head_vals = head_flat.reshape(seq_len, heads_here, head_dim)
    lse_vals = lse.transpose(0, 2, 1) * math.log(2.0)
    gate_pre = gate_pre.astype(jnp.float32)
    up_pre = up_pre.astype(jnp.float32)
    gate_up_use = jnp.stack([gate_use, up_use], axis=1)
    out_use = out_use.reshape(heads_here, head_dim, model_width)
    qkv_use = qkv_use.reshape(model_width, heads_here, 3 * head_dim)
    grad_out = cot_rows.astype(jnp.float32)
    grad_ffn = gather_rows(cot_rows)
    down_g = jnp.einsum("qf,qd->fd", hidden, grad_ffn, preferred_element_type=jnp.float32)
    grad_hidden = jnp.einsum("qd,fd->qf", grad_ffn, down_use, preferred_element_type=jnp.float32)
    sig = jax.nn.sigmoid(gate_pre)
    grad_gate = grad_hidden * up_pre * sig * (1.0 + gate_pre * (1.0 - sig))
    grad_up = grad_hidden * jax.nn.silu(gate_pre)
    grad_pair = jnp.stack([grad_gate, grad_up], axis=1).astype(jnp.bfloat16)
    gate_up_g = jnp.einsum(
        "qd,qgf->dgf", ffn_input, grad_pair, preferred_element_type=jnp.float32
    )
    grad_normb = sum_rows(
        jnp.einsum("qgf,dgf->qd", grad_pair, gate_up_use, preferred_element_type=jnp.float32)
    )
    unit_b, factor_b = rms_parts(mixed_rows)
    weighted_b = grad_normb * gains_f[1]
    gain_b = jnp.sum(grad_normb * unit_b, axis=0)
    grad_mixed = grad_out + factor_b * (
        weighted_b - unit_b * jnp.mean(weighted_b * unit_b, axis=-1, keepdims=True)
    )
    grad_heads = gather_rows(grad_mixed.astype(jnp.bfloat16))
    out_g = jnp.einsum("qhd,qm->hdm", head_vals, grad_heads, preferred_element_type=jnp.float32)
    grad_head_vals = jnp.einsum(
        "qm,hdm->qhd", grad_heads, out_use, preferred_element_type=jnp.float32
    ).astype(jnp.bfloat16)
    grad_query, grad_key, grad_value = attend_back(
        (query_rot, key_rot, value_rows, grad_head_vals, lse_vals, docs, docs),
        order,
        order,
        score_scale,
    )
    grad_proj = jnp.concatenate(
        [
            rotate_back(grad_query, cos_t, sin_t),
            rotate_back(grad_key, cos_t, sin_t),
            grad_value,
        ],
        axis=-1,
    ).astype(jnp.bfloat16)
    qkv_g = jnp.einsum(
        "xq,xtu->qtu", feature_rows, grad_proj, preferred_element_type=jnp.float32
    )
    grad_norma = sum_rows(
        jnp.einsum("aew,iew->ai", grad_proj, qkv_use, preferred_element_type=jnp.float32)
    )
    unit_a, factor_a = rms_parts(adapted)
    weighted_a = grad_norma * gains_f[0]
    gain_a = jnp.sum(grad_norma * unit_a, axis=0)
    grad_adapted = grad_mixed + factor_a * (
        weighted_a - unit_a * jnp.mean(weighted_a * unit_a, axis=-1, keepdims=True)
    )
    adapted_low = grad_adapted.astype(jnp.bfloat16)
    joined = jnp.concatenate([latent_low, embed_rows], axis=-1)
    adapter_g = jnp.einsum("rk,rd->kd", joined, adapted_low, preferred_element_type=jnp.float32)
    embed_out = jnp.einsum(
        "srd,kd->srk",
        swap_out(adapted_low),
        adapter_full[model_width:],
        preferred_element_type=jnp.float32,
    )
    down_s = role_grad(down_g, 1)
    gate_up_s = role_grad(gate_up_g, 0)
    out_s = role_grad(out_g, 2)
    qkv_s = role_grad(qkv_g, 0)
    adapter_s = lax.psum_scatter(
        adapter_g.astype(jnp.bfloat16), ("dp", "context"), scatter_dimension=0, tiled=True
    )
    gains_s = lax.psum_scatter(
        jnp.stack([gain_a, gain_b]).astype(jnp.bfloat16),
        ("dp", "context"),
        scatter_dimension=1,
        tiled=True,
    )
    adapter_s = lax.psum(adapter_s, "tensor").astype(jnp.float32)
    gains_s = lax.psum(gains_s, "tensor").astype(jnp.float32)
    return (swap_out(current), embed_out, adapter_s, gains_s, qkv_s, out_s, gate_up_s, down_s)


def solution(mesh):
    placed = (
        P("dp", ("tensor", "context"), None),
        P("dp", ("tensor", "context"), None),
        P("dp", ("tensor", "context"), None),
        P(),
        P(),
        P(("dp", "context"), None),
        P(None, ("dp", "context")),
        P(("dp", "context"), "tensor", None),
        P("tensor", None, ("dp", "context")),
        P(("dp", "context"), None, "tensor"),
        P("tensor", ("dp", "context")),
    )
    return jax.shard_map(
        shards,
        mesh=mesh,
        in_specs=placed,
        out_specs=(
            P("dp", ("tensor", "context"), None),
            P("dp", ("tensor", "context"), None),
            P(("dp", "context"), None),
            P(None, ("dp", "context")),
            P(("dp", "context"), "tensor", None),
            P("tensor", None, ("dp", "context")),
            P(("dp", "context"), None, "tensor"),
            P("tensor", ("dp", "context")),
        ),
        check_vma=False,
    )
```

```python
from functools import partial
import math
from typing import NamedTuple

import jax
import jax.numpy as jnp
from jax import lax
from jax.experimental import pallas as pl
from jax.experimental.pallas import tpu as pltpu
from jax.sharding import PartitionSpec as P

BACK = 1


rope_base = 50000.0
norm_eps = 1e-06
masked_score = -1e30


def rope_angles(positions, head_dim):
    freq_index = jnp.arange(head_dim // 2, dtype=jnp.float32)
    inv_freq = 1.0 / rope_base ** (2.0 * freq_index / head_dim)
    angles = positions.astype(jnp.float32)[:, None] * inv_freq[None, :]
    return (jnp.cos(angles), jnp.sin(angles))


def rotate_fwd(values, cos_t, sin_t):
    half_dim = values.shape[-1] // 2
    first_half = values[..., :half_dim]
    second_half = values[..., half_dim:]
    return jnp.concatenate(
        [first_half * cos_t - second_half * sin_t, second_half * cos_t + first_half * sin_t],
        axis=-1,
    )


def rotate_back(grad_vals, cos_t, sin_t):
    half_dim = grad_vals.shape[-1] // 2
    first_half = grad_vals[..., :half_dim]
    second_half = grad_vals[..., half_dim:]
    return jnp.concatenate(
        [first_half * cos_t + second_half * sin_t, second_half * cos_t - first_half * sin_t],
        axis=-1,
    )


def rms_parts(rows):
    factor = lax.rsqrt(jnp.mean(rows * rows, axis=-1, keepdims=True) + norm_eps)
    return (rows * factor, factor)


def score_block(query_blk, key_blk, doc_query, doc_key, query_pos, key_pos, score_scale):
    scores = (
        jnp.einsum("qhd,khd->hqk", query_blk, key_blk, preferred_element_type=jnp.float32)
        * score_scale
    )
    allowed = (key_pos[None, :] <= query_pos[:, None]) & (doc_query[:, None] == doc_key[None, :])
    return jnp.where(allowed[None], scores, masked_score)


def attend_block(packed, query_pos, key_pos, score_scale):
    query_blk, key_blk, value_blk, doc_query, doc_key = packed
    scores = score_block(query_blk, key_blk, doc_query, doc_key, query_pos, key_pos, score_scale)
    row_max = jnp.max(scores, axis=-1, keepdims=True)
    exp_vals = jnp.exp(scores - row_max)
    totals = jnp.sum(exp_vals, axis=-1, keepdims=True)
    prob_vals = exp_vals / totals
    head_vals = jnp.einsum(
        "hqk,khd->qhd",
        prob_vals.astype(jnp.bfloat16),
        value_blk,
        preferred_element_type=jnp.float32,
    )
    return (head_vals.astype(jnp.bfloat16), row_max + jnp.log(totals))


def attend_back(packed, query_pos, key_pos, score_scale):
    query_blk, key_blk, value_blk, grad_blk, lse_blk, doc_query, doc_key = packed
    scores = score_block(query_blk, key_blk, doc_query, doc_key, query_pos, key_pos, score_scale)
    prob_vals = jnp.exp(scores - lse_blk)
    grad_value = jnp.einsum(
        "hqk,qhd->khd", prob_vals.astype(jnp.bfloat16), grad_blk, preferred_element_type=jnp.float32
    )
    grad_prob = jnp.einsum("qhd,khd->hqk", grad_blk, value_blk, preferred_element_type=jnp.float32)
    row_dot = jnp.sum(prob_vals * grad_prob, axis=-1, keepdims=True)
    grad_score = (prob_vals * (grad_prob - row_dot)).astype(jnp.bfloat16)
    grad_query = (
        jnp.einsum("hqk,khd->qhd", grad_score, key_blk, preferred_element_type=jnp.float32)
        * score_scale
    )
    grad_key = (
        jnp.einsum("hqk,qhd->khd", grad_score, query_blk, preferred_element_type=jnp.float32)
        * score_scale
    )
    return (grad_query, grad_key, grad_value)


MESH = pl.DeviceIdType.MESH
LOG2E = 1.4426950408889634
VMEM_BYTES = 62 << 20


class Sizes(NamedTuple):
    n_tensor: int
    n_context: int
    seqs: int
    half: int
    block: int
    tile: int
    rows: int
    seq_len: int
    width: int
    heads: int
    head_dim: int
    ff: int


def full_spec():
    return pl.BlockSpec(memory_space=pltpu.VMEM)


def any_spec():
    return pl.BlockSpec(memory_space=pl.ANY)


def nt_dot(a, b):
    return lax.dot_general(a, b, (((1,), (1,)), ((), ())), preferred_element_type=jnp.float32)


def tn_dot(a, b):
    return lax.dot_general(a, b, (((0,), (0,)), ((), ())), preferred_element_type=jnp.float32)


def nn_dot(a, b):
    return jnp.dot(a, b, preferred_element_type=jnp.float32)


class Place:
    def __init__(self, sz):
        t = lax.axis_index("tensor")
        self.sz = sz
        self.dp = lax.axis_index("dp")
        self.ctx = lax.axis_index("context")
        self.group = t // sz.half
        self.part = lax.rem(t, sz.half)

    def device(self, part, ctx):
        return (self.dp, self.group * self.sz.half + part, ctx)

    def ahead(self, q):
        return lax.rem(self.part + q, self.sz.half)

    def behind(self, q):
        return lax.rem(self.part + (self.sz.half - q), self.sz.half)

    def sibling(self):
        return self.device(self.part, 1 - self.ctx)

    def block(self, part, ctx, j):
        sz = self.sz
        first = ((part + j * sz.half) * sz.n_context + ctx) * sz.block
        return pl.ds(pl.multiple_of(first, sz.block), sz.block)

    def tile(self, q, j):
        sz = self.sz
        first = (self.ahead(q) + j * sz.half) * sz.tile
        return pl.ds(pl.multiple_of(first, sz.tile), sz.tile)

    def enter(self):
        barrier = pltpu.get_barrier_semaphore()
        pl.semaphore_signal(
            barrier, inc=1, device_id=self.sibling(), device_id_type=MESH
        )
        for q in range(1, self.sz.half):
            pl.semaphore_signal(
                barrier,
                inc=1,
                device_id=self.device(self.ahead(q), self.ctx),
                device_id_type=MESH,
            )
        pl.semaphore_wait(barrier, self.sz.half)


class Gather:
    @staticmethod
    def scratch(sz):
        kinds = 2 * sz.half - 1
        return [
            pltpu.SemaphoreType.DMA((kinds, sz.seqs)),
            pltpu.SemaphoreType.DMA((kinds, sz.seqs)),
        ]

    def __init__(self, place, ref, send, recv):
        self.place, self.ref, self.send, self.recv = place, ref, send, recv

    def copy(self, kind, j, rows):
        place, half = self.place, self.place.sz.half
        if 0 < kind < half:
            target = place.device(place.ahead(kind), place.ctx)
        else:
            target = place.sibling()
        return pltpu.make_async_remote_copy(
            src_ref=self.ref.at[rows],
            dst_ref=self.ref.at[rows],
            send_sem=self.send.at[kind, j],
            recv_sem=self.recv.at[kind, j],
            device_id=target,
            device_id_type=MESH,
        )

    def own(self, j):
        return self.place.block(self.place.part, self.place.ctx, j)

    def start(self, j):
        for q in range(1, self.place.sz.half):
            self.copy(q, j, self.own(j)).start()
        self.copy(0, j, self.own(j)).start()

    def wait_near(self, j):
        place = self.place
        self.copy(0, j, place.block(place.part, 1 - place.ctx, j)).wait_recv()

    def forward(self, q, j):
        place = self.place
        rows = place.block(place.behind(q), place.ctx, j)
        self.copy(q, j, rows).wait_recv()
        self.copy(place.sz.half - 1 + q, j, rows).start()

    def wait_far(self, q, j):
        place = self.place
        rows = place.block(place.behind(q), 1 - place.ctx, j)
        self.copy(place.sz.half - 1 + q, j, rows).wait_recv()

    def finish(self):
        place, half = self.place, self.place.sz.half
        for j in range(place.sz.seqs):
            for kind in range(half):
                self.copy(kind, j, self.own(j)).wait_send()
            for q in range(1, half):
                rows = place.block(place.behind(q), place.ctx, j)
                self.copy(half - 1 + q, j, rows).wait_send()


class Scatter:
    @staticmethod
    def scratch(sz):
        kinds = 2 * sz.half - 1
        near = (sz.half, sz.seqs, sz.block, sz.width)
        far = (max(sz.half - 1, 1), sz.seqs, sz.block, sz.width)
        return [
            pltpu.VMEM((sz.tile, sz.width), jnp.float32),
            pltpu.VMEM(near, jnp.float32),
            pltpu.VMEM(near, jnp.bfloat16),
            pltpu.VMEM(near, jnp.bfloat16),
            pltpu.VMEM(far, jnp.bfloat16),
            pltpu.VMEM(far, jnp.bfloat16),
            pltpu.SemaphoreType.DMA((kinds, sz.seqs)),
            pltpu.SemaphoreType.DMA((kinds, sz.seqs)),
        ]

    def __init__(self, place, part, mine, near_out, near_in, far_out, far_in, send, recv):
        self.place, self.part, self.mine = place, part, mine
        self.near_out, self.near_in = near_out, near_in
        self.far_out, self.far_in = far_out, far_in
        self.send, self.recv = send, recv

    def near(self, q, j):
        return pltpu.make_async_remote_copy(
            src_ref=self.near_out.at[q, j],
            dst_ref=self.near_in.at[q, j],
            send_sem=self.send.at[q, j],
            recv_sem=self.recv.at[q, j],
            device_id=self.place.sibling(),
            device_id_type=MESH,
        )

    def far(self, q, j):
        place = self.place
        return pltpu.make_async_remote_copy(
            src_ref=self.far_out.at[q - 1, j],
            dst_ref=self.far_in.at[q - 1, j],
            send_sem=self.send.at[place.sz.half - 1 + q, j],
            recv_sem=self.recv.at[place.sz.half - 1 + q, j],
            device_id=place.device(place.ahead(q), place.ctx),
            device_id_type=MESH,
        )

    def give(self, q, j):
        sz, ctx = self.place.sz, self.place.ctx
        mine = pl.ds(pl.multiple_of(ctx * sz.block, sz.block), sz.block)
        other = pl.ds(pl.multiple_of((1 - ctx) * sz.block, sz.block), sz.block)
        self.near_out[q, j] = self.part[other, :].astype(jnp.bfloat16)
        self.near(q, j).start()
        self.mine[q, j] = self.part[mine, :]

    def onward(self, q, j):
        self.near(q, j).wait_recv()
        self.far_out[q - 1, j] = (
            self.mine[q, j] + self.near_in[q, j].astype(jnp.float32)
        ).astype(jnp.bfloat16)
        self.far(q, j).start()

    def total(self, j):
        self.near(0, j).wait_recv()
        total = self.mine[0, j] + self.near_in[0, j].astype(jnp.float32)
        for q in range(1, self.place.sz.half):
            self.far(q, j).wait_recv()
            total = total + self.far_in[q - 1, j].astype(jnp.float32)
        return total

    def finish(self):
        half = self.place.sz.half
        for j in range(self.place.sz.seqs):
            for q in range(half):
                self.near(q, j).wait_send()
            for q in range(1, half):
                self.far(q, j).wait_send()


def column_loads(blocks_ref, vmem_ref, sem):
    count, _, columns = blocks_ref.shape
    return [
        pltpu.make_async_copy(
            blocks_ref.at[b], vmem_ref.at[:, pl.ds(b * columns, columns)], sem.at[b]
        )
        for b in range(count)
    ]


def adapter_loads(blocks_ref, vmem_ref, sem):
    count, tops = sem.shape
    depth, columns = vmem_ref.shape[0] // tops, vmem_ref.shape[1] // count
    return [
        [
            pltpu.make_async_copy(
                blocks_ref.at[b, pl.ds(0, depth), pl.ds(n * columns, columns)],
                vmem_ref.at[pl.ds(b * depth, depth), pl.ds(n * columns, columns)],
                sem.at[n, b],
            )
            for b in range(tops)
        ]
        for n in range(count)
    ]


def rms_factor(rows):
    return lax.rsqrt(jnp.mean(rows * rows, axis=-1, keepdims=True) + norm_eps)


def turn(x, cos_t, sin_t):
    return x * cos_t + pltpu.roll(x, x.shape[-1] // 2, 1) * sin_t


def attn_kernel(sz, keep, *refs):
    (latent, embed, gains, cos_t, sin_t, begin, adapter_hbm, qkv_hbm, out_hbm) = refs[:9]
    refs = refs[9:]
    mixed = refs[0]
    refs = refs[1:]
    if keep:
        adapted_out, rows_out, q_out, k_out, v_out, head_out, lse_out = refs[:7]
        refs = refs[7:]
    (wa, wqkv, wout, adapted, rows_s, q_s, k_s, v_s, head_s, lse_s) = refs[:10]
    load_a, load_qkv, load_out, keep_sem = refs[10:14]
    gather_refs = refs[14:16]
    scatter_refs = refs[16:]

    place = Place(sz)
    a_loads = adapter_loads(adapter_hbm, wa, load_a)
    qkv_load = pltpu.make_async_copy(qkv_hbm, wqkv, load_qkv)
    out_loads = column_loads(out_hbm, wout, load_out)
    for group in a_loads:
        for copy in group:
            copy.start()
    qkv_load.start()
    for copy in out_loads:
        copy.start()
    place.enter()
    gather = Gather(place, rows_s, *gather_refs)
    scatter = Scatter(place, *scatter_refs)

    low = latent[...].astype(jnp.bfloat16)
    columns = sz.width // len(a_loads)
    square = None
    for n, group in enumerate(a_loads):
        for copy in group:
            copy.wait()
        cols = pl.ds(n * columns, columns)
        chunk = nn_dot(low, wa[:, cols]) + embed[:, cols]
        adapted[:, cols] = chunk
        here = jnp.sum(chunk * chunk, axis=-1, keepdims=True)
        square = here if square is None else square + here
    factor = lax.rsqrt(square / sz.width + norm_eps)
    for j in range(sz.seqs):
        span = slice(j * sz.block, (j + 1) * sz.block)
        normed = (adapted[span, :] * factor[span]) * gains[0:1, :]
        rows_s[gather.own(j), :] = normed.astype(jnp.bfloat16)
        gather.start(j)

    qkv_load.wait()
    pair = min(2, sz.heads)
    d = sz.head_dim

    def project(q, j):
        rows = place.tile(q, j)
        x = rows_s[rows, :]
        cos_here, sin_here = cos_t[rows, :], sin_t[rows, :]
        for h0 in range(0, sz.heads, pair):
            proj = nn_dot(x, wqkv[:, 3 * d * h0 : 3 * d * (h0 + pair)])
            for h in range(pair):
                at = 3 * d * h
                q_s[h0 + h, rows, :] = turn(proj[:, at : at + d], cos_here, sin_here).astype(
                    jnp.bfloat16
                )
                k_s[h0 + h, rows, :] = turn(
                    proj[:, at + d : at + 2 * d], cos_here, sin_here
                ).astype(jnp.bfloat16)
                v_s[h0 + h, rows, :] = proj[:, at + 2 * d : at + 3 * d].astype(jnp.bfloat16)

    def attend(q, j):
        rows = place.tile(q, j)
        first = (place.ahead(q) + j * sz.half) * sz.tile
        length = (j + 1) * sz.half * sz.tile
        start = begin[:, pl.ds(pl.multiple_of(first, sz.tile), sz.tile)]
        key_at = lax.broadcasted_iota(jnp.int32, (length, sz.tile), 0)
        query_at = first + lax.broadcasted_iota(jnp.int32, (1, sz.tile), 1)
        allowed = (key_at >= start) & (key_at <= query_at)

        def head(h, carry):
            scores = nt_dot(k_s[h, 0:length, :], q_s[h, rows, :])
            scores = jnp.where(allowed, scores * (LOG2E / math.sqrt(d)), masked_score)
            top = jnp.max(scores, axis=0, keepdims=True)
            weight = jnp.exp2(scores - top)
            total = jnp.sum(weight, axis=0, keepdims=True)
            mixed_t = tn_dot(v_s[h, 0:length, :], weight.astype(jnp.bfloat16))
            result = jnp.transpose(mixed_t / total)
            head_s[rows, pl.ds(pl.multiple_of(h * d, d), d)] = result.astype(jnp.bfloat16)
            if keep:
                lse_s[h, :, rows] = top + jnp.log2(total)
            return carry

        lax.fori_loop(0, sz.heads, head, 0)

    def give(q, j):
        rows = place.tile(q, j)
        scatter.part[...] = nn_dot(head_s[rows, :], wout[...])
        scatter.give(q, j)

    copies = []

    def save(src, dst):
        copy = pltpu.make_async_copy(src, dst, keep_sem.at[len(copies)])
        copy.start()
        copies.append(copy)

    if keep:
        save(adapted, adapted_out)
    far = range(1, sz.half)
    for j in range(sz.seqs):
        gather.wait_near(j)
        project(0, j)
    for copy in out_loads:
        copy.wait()
    for j in range(sz.seqs):
        for q in far:
            gather.forward(q, j)
        for q in far:
            gather.wait_far(sz.half - q, j)
            project(q, j)
        for q in far:
            attend(q, j)
            give(q, j)
        attend(0, j)
        for q in far:
            scatter.onward(q, j)
        give(0, j)
    if keep:
        for src, dst in ((rows_s, rows_out), (q_s, q_out), (k_s, k_out), (v_s, v_out)):
            save(src, dst)
        save(head_s, head_out)
        save(lse_s, lse_out)
    gather.finish()
    for j in range(sz.seqs):
        span = slice(j * sz.block, (j + 1) * sz.block)
        mixed[span, :] = adapted[span, :] + scatter.total(j)
    scatter.finish()
    for copy in copies:
        copy.wait()


def run_attn(sz, keep, latent, embed_part, gains, cos_t, sin_t, begin, adapter, qkv, out):
    f32, bf16 = jnp.float32, jnp.bfloat16
    heads_shape = (sz.heads, sz.seq_len, sz.head_dim)
    shape = jax.ShapeDtypeStruct
    outs = [shape((sz.rows, sz.width), f32)]
    if keep:
        outs += [
            shape((sz.rows, sz.width), f32),
            shape((sz.seq_len, sz.width), bf16),
            shape(heads_shape, bf16),
            shape(heads_shape, bf16),
            shape(heads_shape, bf16),
            shape((sz.seq_len, sz.heads * sz.head_dim), bf16),
            shape((sz.heads, 1, sz.seq_len), f32),
        ]
    scratch = [
        pltpu.VMEM((sz.width, sz.width), bf16),
        pltpu.VMEM(qkv.shape, bf16),
        pltpu.VMEM((sz.heads * sz.head_dim, sz.width), bf16),
        pltpu.VMEM((sz.rows, sz.width), f32),
        pltpu.VMEM((sz.seq_len, sz.width), bf16),
        pltpu.VMEM(heads_shape, bf16),
        pltpu.VMEM(heads_shape, bf16),
        pltpu.VMEM(heads_shape, bf16),
        pltpu.VMEM((sz.seq_len, sz.heads * sz.head_dim), bf16),
        pltpu.VMEM((sz.heads, 1, sz.seq_len), f32),
        pltpu.SemaphoreType.DMA((4, adapter.shape[0] // 2)),
        pltpu.SemaphoreType.DMA,
        pltpu.SemaphoreType.DMA((out.shape[0],)),
        pltpu.SemaphoreType.DMA((8,)),
    ]
    scratch += Gather.scratch(sz) + Scatter.scratch(sz)
    flops = 2 * sz.rows * sz.width * sz.width + 2 * sz.seq_len * sz.width * qkv.shape[1]
    return pl.pallas_call(
        partial(attn_kernel, sz, keep),
        out_shape=outs,
        in_specs=[full_spec()] * 6 + [any_spec()] * 3,
        out_specs=[full_spec()] + [any_spec()] * (len(outs) - 1),
        scratch_shapes=scratch,
        compiler_params=pltpu.CompilerParams(
            collective_id=2 if keep else 1, has_side_effects=True, vmem_limit_bytes=VMEM_BYTES
        ),
        cost_estimate=pl.CostEstimate(
            flops=flops, bytes_accessed=20 << 20, transcendentals=0
        ),
        name="attn_keep" if keep else "attn_round",
    )(latent, embed_part, gains, cos_t, sin_t, begin, adapter, qkv, out)


def ffn_kernel(sz, keep, *refs):
    (mixed, latent, active, gains, gate_hbm, up_hbm, down_hbm, result) = refs[:8]
    refs = refs[8:]
    if keep:
        rows_out, gate_out, up_out, hidden_out = refs[:4]
        refs = refs[4:]
    wg, wu, wd, rows_s = refs[:4]
    refs = refs[4:]
    if keep:
        gate_s, up_s, hidden_s = refs[:3]
        refs = refs[3:]
    load_gu, load_down, keep_sem = refs[:3]
    gather_refs = refs[3:5]
    scatter_refs = refs[5:]

    place = Place(sz)
    gate_load = pltpu.make_async_copy(gate_hbm, wg, load_gu.at[0])
    up_load = pltpu.make_async_copy(up_hbm, wu, load_gu.at[1])
    down_loads = column_loads(down_hbm, wd, load_down)
    gate_load.start()
    up_load.start()
    for copy in down_loads:
        copy.start()
    place.enter()
    gather = Gather(place, rows_s, *gather_refs)
    scatter = Scatter(place, *scatter_refs)
    for j in range(sz.seqs):
        span = slice(j * sz.block, (j + 1) * sz.block)
        rows = mixed[span, :]
        normed = (rows * rms_factor(rows)) * gains[1:2, :]
        rows_s[gather.own(j), :] = normed.astype(jnp.bfloat16)
        gather.start(j)
    gate_load.wait()
    up_load.wait()
    for copy in down_loads:
        copy.wait()

    copies = []

    def save(src, dst):
        copy = pltpu.make_async_copy(src, dst, keep_sem.at[len(copies)])
        copy.start()
        copies.append(copy)

    def work(q, j):
        rows = place.tile(q, j)
        x = rows_s[rows, :]
        gate = nn_dot(x, wg[...])
        up = nn_dot(x, wu[...])
        hidden = (gate / (1.0 + jnp.exp(-gate)) * up).astype(jnp.bfloat16)
        if keep:
            gate_s[rows, :] = gate.astype(jnp.bfloat16)
            up_s[rows, :] = up.astype(jnp.bfloat16)
            hidden_s[rows, :] = hidden
        scatter.part[...] = nn_dot(hidden, wd[...])
        scatter.give(q, j)

    far = range(1, sz.half)
    for j in range(sz.seqs):
        gather.wait_near(j)
        work(0, j)
    for j in range(sz.seqs):
        for q in far:
            gather.forward(q, j)
        for q in far:
            gather.wait_far(sz.half - q, j)
            work(q, j)
        for q in far:
            scatter.onward(q, j)
    if keep:
        save(rows_s, rows_out)
        save(gate_s, gate_out)
        save(up_s, up_out)
        save(hidden_s, hidden_out)
    gather.finish()
    for j in range(sz.seqs):
        span = slice(j * sz.block, (j + 1) * sz.block)
        total = mixed[span, :] + scatter.total(j)
        if not keep:
            total = jnp.where(active[...] > 0, total, latent[span, :])
        result[span, :] = total
    scatter.finish()
    for copy in copies:
        copy.wait()


def run_ffn(sz, keep, mixed, latent, active, gains, gate, up, down):
    f32, bf16 = jnp.float32, jnp.bfloat16
    shape = jax.ShapeDtypeStruct
    outs = [shape((sz.rows, sz.width), f32)]
    if keep:
        outs += [
            shape((sz.seq_len, sz.width), bf16),
            shape((sz.seq_len, sz.ff), bf16),
            shape((sz.seq_len, sz.ff), bf16),
            shape((sz.seq_len, sz.ff), bf16),
        ]
    scratch = [
        pltpu.VMEM(gate.shape, bf16),
        pltpu.VMEM(up.shape, bf16),
        pltpu.VMEM((sz.ff, sz.width), bf16),
        pltpu.VMEM((sz.seq_len, sz.width), bf16),
    ]
    if keep:
        scratch += [pltpu.VMEM((sz.seq_len, sz.ff), bf16)] * 3
    scratch += [
        pltpu.SemaphoreType.DMA((2,)),
        pltpu.SemaphoreType.DMA((down.shape[0],)),
        pltpu.SemaphoreType.DMA((4,)),
    ]
    scratch += Gather.scratch(sz) + Scatter.scratch(sz)
    return pl.pallas_call(
        partial(ffn_kernel, sz, keep),
        out_shape=outs,
        in_specs=[full_spec()] * 4 + [any_spec()] * 3,
        out_specs=[full_spec()] + [any_spec()] * (len(outs) - 1),
        scratch_shapes=scratch,
        compiler_params=pltpu.CompilerParams(
            collective_id=4 if keep else 3, has_side_effects=True, vmem_limit_bytes=VMEM_BYTES
        ),
        cost_estimate=pl.CostEstimate(
            flops=6 * sz.seq_len * sz.width * sz.ff, bytes_accessed=20 << 20, transcendentals=0
        ),
        name="ffn_keep" if keep else "ffn_round",
    )(mixed, latent, active, gains, gate, up, down)


class Ring:
    def __init__(self, place, n_dp):
        self.place, self.count = place, n_dp
        self.at = self.swap(place.dp)

    def swap(self, i):
        if self.count != 4:
            return i
        x, y = lax.rem(i, 2), i // 2
        return 2 * y + x + y - 2 * x * y

    def index(self, offset):
        return self.swap(lax.rem(self.at + offset + 2 * self.count, self.count))

    def device(self, offset):
        return (self.index(offset), lax.axis_index("tensor"), self.place.ctx)


def weights_kernel(sz, n_dp, *refs):
    count = 5
    adapter_in, blocks_in = refs[0], refs[1 : 1 + count]
    adapter_out, blocks_out = refs[1 + count], refs[2 + count : 2 + 2 * count]
    (move_send, move_recv, ring_send, ring_recv, a_send, a_recv, x_send, x_recv, own_sem) = refs[
        2 + 2 * count :
    ]
    place = Place(sz)
    ring = Ring(place, n_dp)
    t = lax.axis_index("tensor")
    ctx, part, half, n_c = place.ctx, place.part, sz.half, sz.n_context
    role = part * n_c + ctx
    at_home = role == t
    steps = n_dp - 1
    sub = adapter_in.shape[0] // half
    ahead = 1 - 2 * ctx

    def holder(g):
        return (place.dp, g * half + t // n_c, lax.rem(t, n_c))

    barrier = pltpu.get_barrier_semaphore()

    def greet(device):
        pl.semaphore_signal(barrier, inc=1, device_id=device, device_id_type=MESH)

    greet(ring.device(1))
    greet(ring.device(n_dp - 1))
    greet(place.sibling())
    for q in range(1, half):
        greet(place.device(place.ahead(q), ctx))
    for c in range(n_c):
        pl.when(jnp.logical_not(at_home & (ctx == c)))(
            lambda c=c: greet((place.dp, role, c))
        )
    waits = 2 + half + sz.seqs - jnp.where(at_home, 1, 0)
    pl.semaphore_wait(barrier, waits)

    def move(w, g):
        slot = place.dp * n_c + ctx
        return pltpu.make_async_remote_copy(
            src_ref=blocks_in[w],
            dst_ref=blocks_out[w].at[slot],
            send_sem=move_send.at[w, g],
            recv_sem=move_recv.at[w, ctx],
            device_id=holder(g),
            device_id_type=MESH,
        )

    def stay(w):
        return pltpu.make_async_copy(
            blocks_in[w], blocks_out[w].at[place.dp * n_c + ctx], own_sem.at[w]
        )

    def moved(w, c):
        slot = place.dp * n_c + c
        arrival = pltpu.make_async_remote_copy(
            src_ref=blocks_in[w],
            dst_ref=blocks_out[w].at[slot],
            send_sem=move_send.at[w, 0],
            recv_sem=move_recv.at[w, c],
            device_id=place.sibling(),
            device_id_type=MESH,
        )
        here = at_home & (ctx == c)
        pl.when(here)(lambda: stay(w).wait())
        pl.when(jnp.logical_not(here))(lambda: arrival.wait_recv())

    def adapter_rows(offset, c, p):
        return adapter_out.at[
            ring.index(offset) * n_c + c, pl.ds(pl.multiple_of(p * sub, sub), sub)
        ]

    own_rows = adapter_in.at[pl.ds(pl.multiple_of(part * sub, sub), sub)]

    def around(s):
        rows = adapter_rows(-ahead * s, ctx, part)
        return pltpu.make_async_remote_copy(
            src_ref=own_rows if s == 0 else rows,
            dst_ref=rows,
            send_sem=a_send.at[s],
            recv_sem=a_recv.at[s],
            device_id=ring.device(ahead),
            device_id_type=MESH,
        )

    def across(kind, s):
        offset = -ahead * s
        if kind < half:
            dst = adapter_rows(offset, ctx, part)
            src = own_rows if s == 0 else dst
        else:
            src = dst = adapter_rows(offset, ctx, place.behind(kind - half + 1))
        target = place.device(place.ahead(kind), ctx) if 0 < kind < half else place.sibling()
        return pltpu.make_async_remote_copy(
            src_ref=src,
            dst_ref=dst,
            send_sem=x_send.at[kind, s],
            recv_sem=x_recv.at[kind, s],
            device_id=target,
            device_id_type=MESH,
        )

    def crossed(kind, s):
        if kind == 0:
            rows = adapter_rows(ahead * s, 1 - ctx, part)
        elif kind < half:
            rows = adapter_rows(-ahead * s, ctx, place.behind(kind))
        else:
            rows = adapter_rows(ahead * s, 1 - ctx, place.behind(kind - half + 1))
        return pltpu.make_async_remote_copy(
            src_ref=rows,
            dst_ref=rows,
            send_sem=x_send.at[kind, s],
            recv_sem=x_recv.at[kind, s],
            device_id=place.sibling(),
            device_id_type=MESH,
        )

    def hop(w, way, s):
        offset = -s if way == 0 else s
        rows = blocks_out[w].at[ring.index(offset) * n_c + way]
        return pltpu.make_async_remote_copy(
            src_ref=rows,
            dst_ref=rows,
            send_sem=ring_send.at[w, way, s],
            recv_sem=ring_recv.at[w, way, s],
            device_id=ring.device(1 if way == 0 else n_dp - 1),
            device_id_type=MESH,
        )

    def hopped(w, way, s):
        offset = -(s + 1) if way == 0 else s + 1
        rows = blocks_out[w].at[ring.index(offset) * n_c + way]
        return pltpu.make_async_remote_copy(
            src_ref=rows,
            dst_ref=rows,
            send_sem=ring_send.at[w, way, s],
            recv_sem=ring_recv.at[w, way, s],
            device_id=ring.device(1),
            device_id_type=MESH,
        )

    around(0).start()
    own = pltpu.make_async_copy(own_rows, adapter_rows(0, ctx, part), own_sem.at[count])
    own.start()
    for w in range(count):
        for g in range(sz.seqs):
            here = at_home & (place.group == g)
            pl.when(jnp.logical_not(here))(lambda w=w, g=g: move(w, g).start())
        pl.when(at_home)(lambda w=w: stay(w).start())
    for kind in range(half):
        across(kind, 0).start()

    def adapter_step(s):
        if s < steps:
            arrival = pltpu.make_async_remote_copy(
                src_ref=own_rows,
                dst_ref=adapter_rows(-ahead * (s + 1), ctx, part),
                send_sem=a_send.at[s],
                recv_sem=a_recv.at[s],
                device_id=ring.device(1),
                device_id_type=MESH,
            )
            arrival.wait_recv()
            if s + 1 < steps:
                around(s + 1).start()
            for kind in range(half):
                across(kind, s + 1).start()

    def adapter_pass(s):
        for q in range(1, half):
            crossed(q, s).wait_recv()
            across(half - 1 + q, s).start()

    todo = []
    for k in range(count + steps):
        for s in range(min(k, steps - 1), -1, -1):
            w = k - s
            if w < count:
                todo.append((w, s))
    done = 0
    for w, s in todo:
        for way in range(n_c):
            if s == 0:
                moved(w, way)
            else:
                hopped(w, way, s - 1).wait_recv()
            hop(w, way, s).start()
        if done < steps:
            adapter_step(done)
        done += 1
    for s in range(done, steps):
        adapter_step(s)
    for s in range(n_dp):
        adapter_pass(s)
    for w in range(count):
        for way in range(n_c):
            hopped(w, way, steps - 1).wait_recv()
    for s in range(n_dp):
        crossed(0, s).wait_recv()
        for q in range(1, half):
            crossed(half - 1 + q, s).wait_recv()
    own.wait()
    for w in range(count):
        for g in range(sz.seqs):
            here = at_home & (place.group == g)
            pl.when(jnp.logical_not(here))(lambda w=w, g=g: move(w, g).wait_send())
        for way in range(n_c):
            for s in range(steps):
                hop(w, way, s).wait_send()
    for s in range(steps):
        around(s).wait_send()
    for s in range(n_dp):
        for kind in range(2 * half - 1):
            across(kind, s).wait_send()


def run_weights(sz, n_dp, adapter, blocks):
    bf16 = jnp.bfloat16
    slots = n_dp * sz.n_context
    outs = [jax.ShapeDtypeStruct((slots,) + a.shape, bf16) for a in [adapter] + blocks]
    count, steps, dma = len(blocks), n_dp - 1, pltpu.SemaphoreType.DMA
    kinds = 2 * sz.half - 1
    return pl.pallas_call(
        partial(weights_kernel, sz, n_dp),
        out_shape=outs,
        in_specs=[any_spec()] * (1 + count),
        out_specs=[any_spec()] * (1 + count),
        scratch_shapes=[
            dma((count, sz.seqs)),
            dma((count, sz.n_context)),
            dma((count, sz.n_context, steps)),
            dma((count, sz.n_context, steps)),
            dma((steps,)),
            dma((steps,)),
            dma((kinds, n_dp)),
            dma((kinds, n_dp)),
            dma((count + 1,)),
        ],
        compiler_params=pltpu.CompilerParams(collective_id=5, has_side_effects=True),
        name="weights",
    )(adapter, *blocks)


def shards(
    embedded,
    initial_state,
    cotangent,
    doc_ids,
    recurrences,
    adapter_weight,
    norm_gains,
    qkv_weight,
    output_head_weight,
    gate_up_weight,
    down_weight,
):
    n_dp = lax.axis_size("dp")
    n_tensor = lax.axis_size("tensor")
    n_context = lax.axis_size("context")
    dp_index = lax.axis_index("dp")
    t_index = lax.axis_index("tensor")
    ctx_index = lax.axis_index("context")
    seq_count, block_rows, model_width = embedded.shape
    seq_len = doc_ids.shape[1]
    half = n_tensor // seq_count
    group = t_index // half
    part = t_index % half
    heads_here = qkv_weight.shape[1]
    head_dim = qkv_weight.shape[2] // 3
    ff_here = down_weight.shape[0]
    score_scale = 1.0 / math.sqrt(head_dim)
    pair_swap = [(i, (i + half) % n_tensor) for i in range(n_tensor)]
    members = half * n_context
    groups = [
        [g * members + i for i in range(members)] for g in range(seq_count)
    ]

    def swap_in(rows):
        own = lax.dynamic_index_in_dim(rows, group, 0, keepdims=False)
        other = lax.dynamic_index_in_dim(rows, 1 - group, 0, keepdims=False)
        got = lax.ppermute(other, "tensor", pair_swap)
        first = jnp.where(group == 0, own, got)
        second = jnp.where(group == 0, got, own)
        return jnp.concatenate([first, second], axis=0)

    def swap_out(rows):
        first, second = rows[:block_rows], rows[block_rows:]
        own = jnp.where(group == 0, first, second)
        other = jnp.where(group == 0, second, first)
        got = lax.ppermute(other, "tensor", pair_swap)
        return jnp.stack(
            [jnp.where(group == 0, own, got), jnp.where(group == 0, got, own)], axis=0
        )

    def role_perm(flip):
        pairs = []
        for t in range(n_tensor):
            for c in range(n_context):
                g = (c + flip) % n_context
                dest = (g * half + t // n_context) * n_context + t % n_context
                pairs.append((t * n_context + c, dest))
        return pairs

    role_perms = [role_perm(0), role_perm(1)]

    def side_by_side(blocks):
        count, depth, columns = blocks.shape
        return blocks.transpose(1, 0, 2).reshape(depth, count * columns)

    def role_grad(grad, axis):
        piece = lax.psum_scatter(
            grad.astype(jnp.bfloat16), "dp", scatter_dimension=axis, tiled=True
        )
        low, high = jnp.split(piece, 2, axis=axis)
        give = [jnp.where(group == 0, low, high), jnp.where(group == 0, high, low)]
        back = [
            lax.ppermute(g, ("tensor", "context"), [(b, a) for a, b in perm])
            for g, perm in zip(give, role_perms)
        ]
        return back[0].astype(jnp.float32) + back[1].astype(jnp.float32)

    def gather_rows(rows):
        full = lax.all_gather(
            rows, ("tensor", "context"), axis=0, tiled=True, axis_index_groups=groups
        )
        split = full.reshape(half, n_context, seq_count, block_rows, model_width)
        return split.transpose(2, 0, 1, 3, 4).reshape(seq_len, model_width)

    def sum_rows(partial_rows):
        split = partial_rows.astype(jnp.bfloat16).reshape(
            seq_count, half, n_context, block_rows, model_width
        )
        return lax.psum_scatter(
            split.transpose(1, 2, 0, 3, 4).reshape(seq_len, model_width),
            ("tensor", "context"),
            scatter_dimension=0,
            tiled=True,
            axis_index_groups=groups,
        ).astype(jnp.float32)

    embed_rows = swap_in(embedded)
    state_rows = swap_in(initial_state)
    cot_rows = swap_in(cotangent)
    sz = Sizes(
        n_tensor,
        n_context,
        seq_count,
        half,
        block_rows,
        n_context * block_rows,
        seq_count * block_rows,
        seq_len,
        model_width,
        heads_here,
        head_dim,
        ff_here,
    )
    adapter_block = adapter_weight.shape[0]
    gain_columns = norm_gains.shape[1]
    unit = 16 * half
    padded = -(-(adapter_block + 2) // unit) * unit
    adapter_rows = jnp.concatenate(
        [
            adapter_weight,
            jnp.pad(
                norm_gains,
                ((0, padded - adapter_block - 2), (0, model_width - gain_columns)),
            ),
        ],
        axis=0,
    )
    adapter_all, qkv_use, out_blocks, gate_use, up_use, down_blocks = run_weights(
        sz,
        n_dp,
        adapter_rows,
        [
            qkv_weight.reshape(qkv_weight.shape[0], -1),
            output_head_weight.reshape(heads_here * head_dim, -1),
            gate_up_weight[:, 0],
            gate_up_weight[:, 1],
            down_weight,
        ],
    )
    qkv_use = qkv_use.reshape(model_width, -1)
    gate_use = gate_use.reshape(model_width, -1)
    up_use = up_use.reshape(model_width, -1)
    gains_full = (
        adapter_all[:, adapter_block : adapter_block + 2, :gain_columns]
        .transpose(1, 0, 2)
        .reshape(2, model_width)
    )
    adapter_low = adapter_all[adapter_all.shape[0] // 2 :, :adapter_block].reshape(
        model_width, model_width
    )
    out_use = side_by_side(out_blocks)
    down_use = side_by_side(down_blocks)
    if out_blocks.shape[2] % 128:
        out_blocks = out_use[None]
        down_blocks = down_use[None]
    gains_f = gains_full.astype(jnp.float32)

    order = jnp.arange(seq_len, dtype=jnp.int32)
    cos_t, sin_t = rope_angles(order, head_dim)
    cos_full = jnp.concatenate([cos_t, cos_t], axis=1)
    sin_full = jnp.concatenate([-sin_t, sin_t], axis=1)
    cos_t = cos_t[:, None, :]
    sin_t = sin_t[:, None, :]
    own_seq = dp_index * seq_count + group
    docs = lax.dynamic_index_in_dim(doc_ids, own_seq, 0, keepdims=False)
    begin = jnp.sum((docs[None, :] < docs[:, None]).astype(jnp.int32), axis=1)[None, :]
    steps_own = lax.dynamic_index_in_dim(recurrences, own_seq, 0, keepdims=False) - BACK
    embed_part = jnp.dot(
        embed_rows, adapter_low, preferred_element_type=jnp.float32
    )

    def advance(step_index, current):
        (mixed,) = run_attn(
            sz, False, current, embed_part, gains_f, cos_full, sin_full, begin,
            adapter_all, qkv_use, out_blocks,
        )
        active = jnp.broadcast_to((step_index < steps_own).astype(jnp.float32), (1, model_width))
        (result,) = run_ffn(
            sz, False, mixed, current, active, gains_f, gate_use, up_use, down_blocks
        )
        return result

    detached = lax.fori_loop(
        0, jnp.max(recurrences) - BACK, advance, state_rows.astype(jnp.float32)
    )
    (mixed_rows, adapted, feature_rows, query_hm, key_hm, value_hm, head_flat, lse) = run_attn(
        sz, True, detached, embed_part, gains_f, cos_full, sin_full, begin,
        adapter_all, qkv_use, out_blocks,
    )
    (current, ffn_input, gate_pre, up_pre, hidden) = run_ffn(
        sz, True, mixed_rows, detached, gains_f[:1], gains_f, gate_use, up_use, down_blocks
    )
    latent_low = detached.astype(jnp.bfloat16)
    query_rot = query_hm.transpose(1, 0, 2)
    key_rot = key_hm.transpose(1, 0, 2)
    value_rows = value_hm.transpose(1, 0, 2)
    head_vals = head_flat.reshape(seq_len, heads_here, head_dim)
    lse_vals = lse.transpose(0, 2, 1) * math.log(2.0)
    gate_pre = gate_pre.astype(jnp.float32)
    up_pre = up_pre.astype(jnp.float32)
    gate_up_use = jnp.stack([gate_use, up_use], axis=1)
    out_use = out_use.reshape(heads_here, head_dim, model_width)
    qkv_use = qkv_use.reshape(model_width, heads_here, 3 * head_dim)
    grad_out = cot_rows.astype(jnp.float32)
    grad_ffn = gather_rows(cot_rows)
    down_g = jnp.einsum("qf,qd->fd", hidden, grad_ffn, preferred_element_type=jnp.float32)
    grad_hidden = jnp.einsum("qd,fd->qf", grad_ffn, down_use, preferred_element_type=jnp.float32)
    sig = jax.nn.sigmoid(gate_pre)
    grad_gate = grad_hidden * up_pre * sig * (1.0 + gate_pre * (1.0 - sig))
    grad_up = grad_hidden * jax.nn.silu(gate_pre)
    grad_pair = jnp.stack([grad_gate, grad_up], axis=1).astype(jnp.bfloat16)
    gate_up_g = jnp.einsum(
        "qd,qgf->dgf", ffn_input, grad_pair, preferred_element_type=jnp.float32
    )
    grad_normb = sum_rows(
        jnp.einsum("qgf,dgf->qd", grad_pair, gate_up_use, preferred_element_type=jnp.float32)
    )
    unit_b, factor_b = rms_parts(mixed_rows)
    weighted_b = grad_normb * gains_f[1]
    gain_b = jnp.sum(grad_normb * unit_b, axis=0)
    grad_mixed = grad_out + factor_b * (
        weighted_b - unit_b * jnp.mean(weighted_b * unit_b, axis=-1, keepdims=True)
    )
    grad_heads = gather_rows(grad_mixed.astype(jnp.bfloat16))
    out_g = jnp.einsum("qhd,qm->hdm", head_vals, grad_heads, preferred_element_type=jnp.float32)
    grad_head_vals = jnp.einsum(
        "qm,hdm->qhd", grad_heads, out_use, preferred_element_type=jnp.float32
    ).astype(jnp.bfloat16)
    grad_query, grad_key, grad_value = attend_back(
        (query_rot, key_rot, value_rows, grad_head_vals, lse_vals, docs, docs),
        order,
        order,
        score_scale,
    )
    grad_proj = jnp.concatenate(
        [
            rotate_back(grad_query, cos_t, sin_t),
            rotate_back(grad_key, cos_t, sin_t),
            grad_value,
        ],
        axis=-1,
    ).astype(jnp.bfloat16)
    qkv_g = jnp.einsum(
        "xq,xtu->qtu", feature_rows, grad_proj, preferred_element_type=jnp.float32
    )
    grad_norma = sum_rows(
        jnp.einsum("aew,iew->ai", grad_proj, qkv_use, preferred_element_type=jnp.float32)
    )
    unit_a, factor_a = rms_parts(adapted)
    weighted_a = grad_norma * gains_f[0]
    gain_a = jnp.sum(grad_norma * unit_a, axis=0)
    grad_adapted = grad_mixed + factor_a * (
        weighted_a - unit_a * jnp.mean(weighted_a * unit_a, axis=-1, keepdims=True)
    )
    adapted_low = grad_adapted.astype(jnp.bfloat16)
    joined = jnp.concatenate([latent_low, embed_rows], axis=-1)
    adapter_g = jnp.einsum("rk,rd->kd", joined, adapted_low, preferred_element_type=jnp.float32)
    embed_out = jnp.einsum(
        "srd,kd->srk",
        swap_out(adapted_low),
        adapter_low,
        preferred_element_type=jnp.float32,
    )
    down_s = role_grad(down_g, 1)
    gate_up_s = role_grad(gate_up_g, 0)
    out_s = role_grad(out_g, 2)
    qkv_s = role_grad(qkv_g, 0)
    adapter_s = lax.psum_scatter(
        adapter_g.astype(jnp.bfloat16), ("dp", "context"), scatter_dimension=0, tiled=True
    )
    gains_s = lax.psum_scatter(
        jnp.stack([gain_a, gain_b]).astype(jnp.bfloat16),
        ("dp", "context"),
        scatter_dimension=1,
        tiled=True,
    )
    adapter_s = lax.psum(adapter_s, "tensor").astype(jnp.float32)
    gains_s = lax.psum(gains_s, "tensor").astype(jnp.float32)
    return (swap_out(current), embed_out, adapter_s, gains_s, qkv_s, out_s, gate_up_s, down_s)


def solution(mesh):
    placed = (
        P("dp", ("tensor", "context"), None),
        P("dp", ("tensor", "context"), None),
        P("dp", ("tensor", "context"), None),
        P(),
        P(),
        P(("dp", "context"), None),
        P(None, ("dp", "context")),
        P(("dp", "context"), "tensor", None),
        P("tensor", None, ("dp", "context")),
        P(("dp", "context"), None, "tensor"),
        P("tensor", ("dp", "context")),
    )
    return jax.shard_map(
        shards,
        mesh=mesh,
        in_specs=placed,
        out_specs=(
            P("dp", ("tensor", "context"), None),
            P("dp", ("tensor", "context"), None),
            P(("dp", "context"), None),
            P(None, ("dp", "context")),
            P(("dp", "context"), "tensor", None),
            P("tensor", None, ("dp", "context")),
            P(("dp", "context"), None, "tensor"),
            P("tensor", ("dp", "context")),
        ),
        check_vma=False,
    )
```

```python
from functools import partial
import math
from typing import NamedTuple

import jax
import jax.numpy as jnp
from jax import lax
from jax.experimental import pallas as pl
from jax.experimental.pallas import tpu as pltpu
from jax.sharding import PartitionSpec as P

BACK = 1


rope_base = 50000.0
norm_eps = 1e-06
masked_score = -1e30


def rope_angles(positions, head_dim):
    freq_index = jnp.arange(head_dim // 2, dtype=jnp.float32)
    inv_freq = 1.0 / rope_base ** (2.0 * freq_index / head_dim)
    angles = positions.astype(jnp.float32)[:, None] * inv_freq[None, :]
    return (jnp.cos(angles), jnp.sin(angles))


MESH = pl.DeviceIdType.MESH
LOG2E = 1.4426950408889634
VMEM_BYTES = 62 << 20


class Sizes(NamedTuple):
    n_tensor: int
    n_context: int
    seqs: int
    half: int
    block: int
    tile: int
    rows: int
    seq_len: int
    width: int
    heads: int
    head_dim: int
    ff: int


def full_spec():
    return pl.BlockSpec(memory_space=pltpu.VMEM)


def any_spec():
    return pl.BlockSpec(memory_space=pl.ANY)


def nt_dot(a, b):
    return lax.dot_general(a, b, (((1,), (1,)), ((), ())), preferred_element_type=jnp.float32)


def tn_dot(a, b):
    return lax.dot_general(a, b, (((0,), (0,)), ((), ())), preferred_element_type=jnp.float32)


def nn_dot(a, b):
    return jnp.dot(a, b, preferred_element_type=jnp.float32)


class Place:
    def __init__(self, sz):
        t = lax.axis_index("tensor")
        self.sz = sz
        self.dp = lax.axis_index("dp")
        self.ctx = lax.axis_index("context")
        self.group = t // sz.half
        self.part = lax.rem(t, sz.half)

    def device(self, part, ctx):
        return (self.dp, self.group * self.sz.half + part, ctx)

    def ahead(self, q):
        return lax.rem(self.part + q, self.sz.half)

    def behind(self, q):
        return lax.rem(self.part + (self.sz.half - q), self.sz.half)

    def sibling(self):
        return self.device(self.part, 1 - self.ctx)

    def block(self, part, ctx, j):
        sz = self.sz
        first = ((part + j * sz.half) * sz.n_context + ctx) * sz.block
        return pl.ds(pl.multiple_of(first, sz.block), sz.block)

    def tile(self, q, j):
        sz = self.sz
        first = (self.ahead(q) + j * sz.half) * sz.tile
        return pl.ds(pl.multiple_of(first, sz.tile), sz.tile)

    def enter(self):
        barrier = pltpu.get_barrier_semaphore()
        pl.semaphore_signal(
            barrier, inc=1, device_id=self.sibling(), device_id_type=MESH
        )
        for q in range(1, self.sz.half):
            pl.semaphore_signal(
                barrier,
                inc=1,
                device_id=self.device(self.ahead(q), self.ctx),
                device_id_type=MESH,
            )
        pl.semaphore_wait(barrier, self.sz.half)


class Gather:
    @staticmethod
    def scratch(sz):
        kinds = 2 * sz.half - 1
        return [
            pltpu.SemaphoreType.DMA((kinds, sz.seqs)),
            pltpu.SemaphoreType.DMA((kinds, sz.seqs)),
        ]

    def __init__(self, place, ref, send, recv):
        self.place, self.ref, self.send, self.recv = place, ref, send, recv

    def copy(self, kind, j, rows):
        place, half = self.place, self.place.sz.half
        if 0 < kind < half:
            target = place.device(place.ahead(kind), place.ctx)
        else:
            target = place.sibling()
        return pltpu.make_async_remote_copy(
            src_ref=self.ref.at[rows],
            dst_ref=self.ref.at[rows],
            send_sem=self.send.at[kind, j],
            recv_sem=self.recv.at[kind, j],
            device_id=target,
            device_id_type=MESH,
        )

    def own(self, j):
        return self.place.block(self.place.part, self.place.ctx, j)

    def start(self, j):
        for q in range(1, self.place.sz.half):
            self.copy(q, j, self.own(j)).start()
        self.copy(0, j, self.own(j)).start()

    def wait_near(self, j):
        place = self.place
        self.copy(0, j, place.block(place.part, 1 - place.ctx, j)).wait_recv()

    def forward(self, q, j):
        place = self.place
        rows = place.block(place.behind(q), place.ctx, j)
        self.copy(q, j, rows).wait_recv()
        self.copy(place.sz.half - 1 + q, j, rows).start()

    def wait_far(self, q, j):
        place = self.place
        rows = place.block(place.behind(q), 1 - place.ctx, j)
        self.copy(place.sz.half - 1 + q, j, rows).wait_recv()

    def finish(self):
        place, half = self.place, self.place.sz.half
        for j in range(place.sz.seqs):
            for kind in range(half):
                self.copy(kind, j, self.own(j)).wait_send()
            for q in range(1, half):
                rows = place.block(place.behind(q), place.ctx, j)
                self.copy(half - 1 + q, j, rows).wait_send()


class Scatter:
    @staticmethod
    def scratch(sz):
        kinds = 2 * sz.half - 1
        near = (sz.half, sz.seqs, sz.block, sz.width)
        far = (max(sz.half - 1, 1), sz.seqs, sz.block, sz.width)
        return [
            pltpu.VMEM((sz.tile, sz.width), jnp.float32),
            pltpu.VMEM(near, jnp.float32),
            pltpu.VMEM(near, jnp.bfloat16),
            pltpu.VMEM(near, jnp.bfloat16),
            pltpu.VMEM(far, jnp.bfloat16),
            pltpu.VMEM(far, jnp.bfloat16),
            pltpu.SemaphoreType.DMA((kinds, sz.seqs)),
            pltpu.SemaphoreType.DMA((kinds, sz.seqs)),
        ]

    def __init__(self, place, part, mine, near_out, near_in, far_out, far_in, send, recv):
        self.place, self.part, self.mine = place, part, mine
        self.near_out, self.near_in = near_out, near_in
        self.far_out, self.far_in = far_out, far_in
        self.send, self.recv = send, recv

    def near(self, q, j):
        return pltpu.make_async_remote_copy(
            src_ref=self.near_out.at[q, j],
            dst_ref=self.near_in.at[q, j],
            send_sem=self.send.at[q, j],
            recv_sem=self.recv.at[q, j],
            device_id=self.place.sibling(),
            device_id_type=MESH,
        )

    def far(self, q, j):
        place = self.place
        return pltpu.make_async_remote_copy(
            src_ref=self.far_out.at[q - 1, j],
            dst_ref=self.far_in.at[q - 1, j],
            send_sem=self.send.at[place.sz.half - 1 + q, j],
            recv_sem=self.recv.at[place.sz.half - 1 + q, j],
            device_id=place.device(place.ahead(q), place.ctx),
            device_id_type=MESH,
        )

    def give(self, q, j):
        sz, ctx = self.place.sz, self.place.ctx
        mine = pl.ds(pl.multiple_of(ctx * sz.block, sz.block), sz.block)
        other = pl.ds(pl.multiple_of((1 - ctx) * sz.block, sz.block), sz.block)
        self.near_out[q, j] = self.part[other, :].astype(jnp.bfloat16)
        self.near(q, j).start()
        self.mine[q, j] = self.part[mine, :]

    def onward(self, q, j):
        self.near(q, j).wait_recv()
        self.far_out[q - 1, j] = (
            self.mine[q, j] + self.near_in[q, j].astype(jnp.float32)
        ).astype(jnp.bfloat16)
        self.far(q, j).start()

    def total(self, j):
        self.near(0, j).wait_recv()
        total = self.mine[0, j] + self.near_in[0, j].astype(jnp.float32)
        for q in range(1, self.place.sz.half):
            self.far(q, j).wait_recv()
            total = total + self.far_in[q - 1, j].astype(jnp.float32)
        return total

    def finish(self):
        half = self.place.sz.half
        for j in range(self.place.sz.seqs):
            for q in range(half):
                self.near(q, j).wait_send()
            for q in range(1, half):
                self.far(q, j).wait_send()


def column_loads(blocks_ref, vmem_ref, sem):
    count, _, columns = blocks_ref.shape
    return [
        pltpu.make_async_copy(
            blocks_ref.at[b], vmem_ref.at[:, pl.ds(b * columns, columns)], sem.at[b]
        )
        for b in range(count)
    ]


def adapter_loads(blocks_ref, vmem_ref, sem):
    count, tops = sem.shape
    depth, columns = vmem_ref.shape[0] // tops, vmem_ref.shape[1] // count
    return [
        [
            pltpu.make_async_copy(
                blocks_ref.at[b, pl.ds(0, depth), pl.ds(n * columns, columns)],
                vmem_ref.at[pl.ds(b * depth, depth), pl.ds(n * columns, columns)],
                sem.at[n, b],
            )
            for b in range(tops)
        ]
        for n in range(count)
    ]


def rms_factor(rows):
    return lax.rsqrt(jnp.mean(rows * rows, axis=-1, keepdims=True) + norm_eps)


def turn(x, cos_t, sin_t):
    return x * cos_t + pltpu.roll(x, x.shape[-1] // 2, 1) * sin_t


def attn_kernel(sz, keep, *refs):
    (latent, embed, gains, cos_t, sin_t, begin, adapter_hbm, qkv_hbm, out_hbm) = refs[:9]
    refs = refs[9:]
    mixed = refs[0]
    refs = refs[1:]
    if keep:
        adapted_out, rows_out, q_out, k_out, v_out, head_out, lse_out = refs[:7]
        refs = refs[7:]
    (wa, wqkv, wout, adapted, rows_s, q_s, k_s, v_s, head_s, lse_s) = refs[:10]
    load_a, load_qkv, load_out, keep_sem = refs[10:14]
    gather_refs = refs[14:16]
    scatter_refs = refs[16:]

    place = Place(sz)
    a_loads = adapter_loads(adapter_hbm, wa, load_a)
    qkv_load = pltpu.make_async_copy(qkv_hbm, wqkv, load_qkv)
    out_loads = column_loads(out_hbm, wout, load_out)
    for group in a_loads:
        for copy in group:
            copy.start()
    qkv_load.start()
    for copy in out_loads:
        copy.start()
    place.enter()
    gather = Gather(place, rows_s, *gather_refs)
    scatter = Scatter(place, *scatter_refs)

    low = latent[...].astype(jnp.bfloat16)
    columns = sz.width // len(a_loads)
    square = None
    for n, group in enumerate(a_loads):
        for copy in group:
            copy.wait()
        cols = pl.ds(n * columns, columns)
        chunk = nn_dot(low, wa[:, cols]) + embed[:, cols]
        adapted[:, cols] = chunk
        here = jnp.sum(chunk * chunk, axis=-1, keepdims=True)
        square = here if square is None else square + here
    factor = lax.rsqrt(square / sz.width + norm_eps)
    for j in range(sz.seqs):
        span = slice(j * sz.block, (j + 1) * sz.block)
        normed = (adapted[span, :] * factor[span]) * gains[0:1, :]
        rows_s[gather.own(j), :] = normed.astype(jnp.bfloat16)
        gather.start(j)

    qkv_load.wait()
    pair = min(2, sz.heads)
    d = sz.head_dim

    def project(q, j):
        rows = place.tile(q, j)
        x = rows_s[rows, :]
        cos_here, sin_here = cos_t[rows, :], sin_t[rows, :]
        for h0 in range(0, sz.heads, pair):
            proj = nn_dot(x, wqkv[:, 3 * d * h0 : 3 * d * (h0 + pair)])
            for h in range(pair):
                at = 3 * d * h
                q_s[h0 + h, rows, :] = turn(proj[:, at : at + d], cos_here, sin_here).astype(
                    jnp.bfloat16
                )
                k_s[h0 + h, rows, :] = turn(
                    proj[:, at + d : at + 2 * d], cos_here, sin_here
                ).astype(jnp.bfloat16)
                v_s[h0 + h, rows, :] = proj[:, at + 2 * d : at + 3 * d].astype(jnp.bfloat16)

    def attend(q, j):
        rows = place.tile(q, j)
        first = (place.ahead(q) + j * sz.half) * sz.tile
        length = (j + 1) * sz.half * sz.tile
        start = begin[:, pl.ds(pl.multiple_of(first, sz.tile), sz.tile)]
        key_at = lax.broadcasted_iota(jnp.int32, (length, sz.tile), 0)
        query_at = first + lax.broadcasted_iota(jnp.int32, (1, sz.tile), 1)
        allowed = (key_at >= start) & (key_at <= query_at)

        def head(h, carry):
            scores = nt_dot(k_s[h, 0:length, :], q_s[h, rows, :])
            scores = jnp.where(allowed, scores * (LOG2E / math.sqrt(d)), masked_score)
            top = jnp.max(scores, axis=0, keepdims=True)
            weight = jnp.exp2(scores - top)
            total = jnp.sum(weight, axis=0, keepdims=True)
            mixed_t = tn_dot(v_s[h, 0:length, :], weight.astype(jnp.bfloat16))
            result = jnp.transpose(mixed_t / total)
            head_s[rows, pl.ds(pl.multiple_of(h * d, d), d)] = result.astype(jnp.bfloat16)
            if keep:
                lse_s[h, :, rows] = top + jnp.log2(total)
            return carry

        lax.fori_loop(0, sz.heads, head, 0)

    def give(q, j):
        rows = place.tile(q, j)
        scatter.part[...] = nn_dot(head_s[rows, :], wout[...])
        scatter.give(q, j)

    copies = []

    def save(src, dst):
        copy = pltpu.make_async_copy(src, dst, keep_sem.at[len(copies)])
        copy.start()
        copies.append(copy)

    if keep:
        save(adapted, adapted_out)
    far = range(1, sz.half)
    for j in range(sz.seqs):
        gather.wait_near(j)
        project(0, j)
    for copy in out_loads:
        copy.wait()
    for j in range(sz.seqs):
        for q in far:
            gather.forward(q, j)
        for q in far:
            gather.wait_far(sz.half - q, j)
            project(q, j)
        for q in far:
            attend(q, j)
            give(q, j)
        attend(0, j)
        for q in far:
            scatter.onward(q, j)
        give(0, j)
    if keep:
        for src, dst in ((rows_s, rows_out), (q_s, q_out), (k_s, k_out), (v_s, v_out)):
            save(src, dst)
        save(head_s, head_out)
        save(lse_s, lse_out)
    gather.finish()
    for j in range(sz.seqs):
        span = slice(j * sz.block, (j + 1) * sz.block)
        mixed[span, :] = adapted[span, :] + scatter.total(j)
    scatter.finish()
    for copy in copies:
        copy.wait()


def run_attn(sz, keep, latent, embed_part, gains, cos_t, sin_t, begin, adapter, qkv, out):
    f32, bf16 = jnp.float32, jnp.bfloat16
    heads_shape = (sz.heads, sz.seq_len, sz.head_dim)
    shape = jax.ShapeDtypeStruct
    outs = [shape((sz.rows, sz.width), f32)]
    if keep:
        outs += [
            shape((sz.rows, sz.width), f32),
            shape((sz.seq_len, sz.width), bf16),
            shape(heads_shape, bf16),
            shape(heads_shape, bf16),
            shape(heads_shape, bf16),
            shape((sz.seq_len, sz.heads * sz.head_dim), bf16),
            shape((sz.heads, 1, sz.seq_len), f32),
        ]
    scratch = [
        pltpu.VMEM((sz.width, sz.width), bf16),
        pltpu.VMEM(qkv.shape, bf16),
        pltpu.VMEM((sz.heads * sz.head_dim, sz.width), bf16),
        pltpu.VMEM((sz.rows, sz.width), f32),
        pltpu.VMEM((sz.seq_len, sz.width), bf16),
        pltpu.VMEM(heads_shape, bf16),
        pltpu.VMEM(heads_shape, bf16),
        pltpu.VMEM(heads_shape, bf16),
        pltpu.VMEM((sz.seq_len, sz.heads * sz.head_dim), bf16),
        pltpu.VMEM((sz.heads, 1, sz.seq_len), f32),
        pltpu.SemaphoreType.DMA((4, adapter.shape[0] // 2)),
        pltpu.SemaphoreType.DMA,
        pltpu.SemaphoreType.DMA((out.shape[0],)),
        pltpu.SemaphoreType.DMA((8,)),
    ]
    scratch += Gather.scratch(sz) + Scatter.scratch(sz)
    flops = 2 * sz.rows * sz.width * sz.width + 2 * sz.seq_len * sz.width * qkv.shape[1]
    return pl.pallas_call(
        partial(attn_kernel, sz, keep),
        out_shape=outs,
        in_specs=[full_spec()] * 6 + [any_spec()] * 3,
        out_specs=[full_spec()] + [any_spec()] * (len(outs) - 1),
        scratch_shapes=scratch,
        compiler_params=pltpu.CompilerParams(
            collective_id=2 if keep else 1, has_side_effects=True, vmem_limit_bytes=VMEM_BYTES
        ),
        cost_estimate=pl.CostEstimate(
            flops=flops, bytes_accessed=20 << 20, transcendentals=0
        ),
        name="attn_keep" if keep else "attn_round",
    )(latent, embed_part, gains, cos_t, sin_t, begin, adapter, qkv, out)


def ffn_kernel(sz, keep, *refs):
    (mixed, latent, active, gains, gate_hbm, up_hbm, down_hbm, result) = refs[:8]
    refs = refs[8:]
    if keep:
        rows_out, gate_out, up_out, hidden_out = refs[:4]
        refs = refs[4:]
    wg, wu, wd, rows_s = refs[:4]
    refs = refs[4:]
    if keep:
        gate_s, up_s, hidden_s = refs[:3]
        refs = refs[3:]
    load_gu, load_down, keep_sem = refs[:3]
    gather_refs = refs[3:5]
    scatter_refs = refs[5:]

    place = Place(sz)
    gate_load = pltpu.make_async_copy(gate_hbm, wg, load_gu.at[0])
    up_load = pltpu.make_async_copy(up_hbm, wu, load_gu.at[1])
    down_loads = column_loads(down_hbm, wd, load_down)
    gate_load.start()
    up_load.start()
    for copy in down_loads:
        copy.start()
    place.enter()
    gather = Gather(place, rows_s, *gather_refs)
    scatter = Scatter(place, *scatter_refs)
    for j in range(sz.seqs):
        span = slice(j * sz.block, (j + 1) * sz.block)
        rows = mixed[span, :]
        normed = (rows * rms_factor(rows)) * gains[1:2, :]
        rows_s[gather.own(j), :] = normed.astype(jnp.bfloat16)
        gather.start(j)
    gate_load.wait()
    up_load.wait()
    for copy in down_loads:
        copy.wait()

    copies = []

    def save(src, dst):
        copy = pltpu.make_async_copy(src, dst, keep_sem.at[len(copies)])
        copy.start()
        copies.append(copy)

    def work(q, j):
        rows = place.tile(q, j)
        x = rows_s[rows, :]
        gate = nn_dot(x, wg[...])
        up = nn_dot(x, wu[...])
        hidden = (gate / (1.0 + jnp.exp(-gate)) * up).astype(jnp.bfloat16)
        if keep:
            gate_s[rows, :] = gate.astype(jnp.bfloat16)
            up_s[rows, :] = up.astype(jnp.bfloat16)
            hidden_s[rows, :] = hidden
        scatter.part[...] = nn_dot(hidden, wd[...])
        scatter.give(q, j)

    far = range(1, sz.half)
    for j in range(sz.seqs):
        gather.wait_near(j)
        work(0, j)
    for j in range(sz.seqs):
        for q in far:
            gather.forward(q, j)
        for q in far:
            gather.wait_far(sz.half - q, j)
            work(q, j)
        for q in far:
            scatter.onward(q, j)
    if keep:
        save(rows_s, rows_out)
        save(gate_s, gate_out)
        save(up_s, up_out)
        save(hidden_s, hidden_out)
    gather.finish()
    for j in range(sz.seqs):
        span = slice(j * sz.block, (j + 1) * sz.block)
        total = mixed[span, :] + scatter.total(j)
        if not keep:
            total = jnp.where(active[...] > 0, total, latent[span, :])
        result[span, :] = total
    scatter.finish()
    for copy in copies:
        copy.wait()


def run_ffn(sz, keep, mixed, latent, active, gains, gate, up, down):
    f32, bf16 = jnp.float32, jnp.bfloat16
    shape = jax.ShapeDtypeStruct
    outs = [shape((sz.rows, sz.width), f32)]
    if keep:
        outs += [
            shape((sz.seq_len, sz.width), bf16),
            shape((sz.seq_len, sz.ff), bf16),
            shape((sz.seq_len, sz.ff), bf16),
            shape((sz.seq_len, sz.ff), bf16),
        ]
    scratch = [
        pltpu.VMEM(gate.shape, bf16),
        pltpu.VMEM(up.shape, bf16),
        pltpu.VMEM((sz.ff, sz.width), bf16),
        pltpu.VMEM((sz.seq_len, sz.width), bf16),
    ]
    if keep:
        scratch += [pltpu.VMEM((sz.seq_len, sz.ff), bf16)] * 3
    scratch += [
        pltpu.SemaphoreType.DMA((2,)),
        pltpu.SemaphoreType.DMA((down.shape[0],)),
        pltpu.SemaphoreType.DMA((4,)),
    ]
    scratch += Gather.scratch(sz) + Scatter.scratch(sz)
    return pl.pallas_call(
        partial(ffn_kernel, sz, keep),
        out_shape=outs,
        in_specs=[full_spec()] * 4 + [any_spec()] * 3,
        out_specs=[full_spec()] + [any_spec()] * (len(outs) - 1),
        scratch_shapes=scratch,
        compiler_params=pltpu.CompilerParams(
            collective_id=4 if keep else 3, has_side_effects=True, vmem_limit_bytes=VMEM_BYTES
        ),
        cost_estimate=pl.CostEstimate(
            flops=6 * sz.seq_len * sz.width * sz.ff, bytes_accessed=20 << 20, transcendentals=0
        ),
        name="ffn_keep" if keep else "ffn_round",
    )(mixed, latent, active, gains, gate, up, down)


class Ring:
    def __init__(self, place, n_dp):
        self.place, self.count = place, n_dp
        self.at = self.swap(place.dp)

    def swap(self, i):
        if self.count != 4:
            return i
        x, y = lax.rem(i, 2), i // 2
        return 2 * y + x + y - 2 * x * y

    def index(self, offset):
        return self.swap(lax.rem(self.at + offset + 2 * self.count, self.count))

    def device(self, offset):
        return (self.index(offset), lax.axis_index("tensor"), self.place.ctx)


def weights_kernel(sz, n_dp, *refs):
    count = 5
    adapter_in, blocks_in = refs[0], refs[1 : 1 + count]
    adapter_out, blocks_out = refs[1 + count], refs[2 + count : 2 + 2 * count]
    (move_send, move_recv, ring_send, ring_recv, a_send, a_recv, x_send, x_recv, own_sem) = refs[
        2 + 2 * count :
    ]
    place = Place(sz)
    ring = Ring(place, n_dp)
    t = lax.axis_index("tensor")
    ctx, part, half, n_c = place.ctx, place.part, sz.half, sz.n_context
    role = part * n_c + ctx
    at_home = role == t
    steps = n_dp - 1
    sub = adapter_in.shape[0] // half
    ahead = 1 - 2 * ctx

    def holder(g):
        return (place.dp, g * half + t // n_c, lax.rem(t, n_c))

    barrier = pltpu.get_barrier_semaphore()

    def greet(device):
        pl.semaphore_signal(barrier, inc=1, device_id=device, device_id_type=MESH)

    greet(ring.device(1))
    greet(ring.device(n_dp - 1))
    greet(place.sibling())
    for q in range(1, half):
        greet(place.device(place.ahead(q), ctx))
    for c in range(n_c):
        pl.when(jnp.logical_not(at_home & (ctx == c)))(
            lambda c=c: greet((place.dp, role, c))
        )
    waits = 2 + half + sz.seqs - jnp.where(at_home, 1, 0)
    pl.semaphore_wait(barrier, waits)

    def move(w, g):
        slot = place.dp * n_c + ctx
        return pltpu.make_async_remote_copy(
            src_ref=blocks_in[w],
            dst_ref=blocks_out[w].at[slot],
            send_sem=move_send.at[w, g],
            recv_sem=move_recv.at[w, ctx],
            device_id=holder(g),
            device_id_type=MESH,
        )

    def stay(w):
        return pltpu.make_async_copy(
            blocks_in[w], blocks_out[w].at[place.dp * n_c + ctx], own_sem.at[w]
        )

    def moved(w, c):
        slot = place.dp * n_c + c
        arrival = pltpu.make_async_remote_copy(
            src_ref=blocks_in[w],
            dst_ref=blocks_out[w].at[slot],
            send_sem=move_send.at[w, 0],
            recv_sem=move_recv.at[w, c],
            device_id=place.sibling(),
            device_id_type=MESH,
        )
        here = at_home & (ctx == c)
        pl.when(here)(lambda: stay(w).wait())
        pl.when(jnp.logical_not(here))(lambda: arrival.wait_recv())

    def adapter_rows(offset, c, p):
        return adapter_out.at[
            ring.index(offset) * n_c + c, pl.ds(pl.multiple_of(p * sub, sub), sub)
        ]

    own_rows = adapter_in.at[pl.ds(pl.multiple_of(part * sub, sub), sub)]

    def around(s):
        rows = adapter_rows(-ahead * s, ctx, part)
        return pltpu.make_async_remote_copy(
            src_ref=own_rows if s == 0 else rows,
            dst_ref=rows,
            send_sem=a_send.at[s],
            recv_sem=a_recv.at[s],
            device_id=ring.device(ahead),
            device_id_type=MESH,
        )

    def across(kind, s):
        offset = -ahead * s
        if kind < half:
            dst = adapter_rows(offset, ctx, part)
            src = own_rows if s == 0 else dst
        else:
            src = dst = adapter_rows(offset, ctx, place.behind(kind - half + 1))
        target = place.device(place.ahead(kind), ctx) if 0 < kind < half else place.sibling()
        return pltpu.make_async_remote_copy(
            src_ref=src,
            dst_ref=dst,
            send_sem=x_send.at[kind, s],
            recv_sem=x_recv.at[kind, s],
            device_id=target,
            device_id_type=MESH,
        )

    def crossed(kind, s):
        if kind == 0:
            rows = adapter_rows(ahead * s, 1 - ctx, part)
        elif kind < half:
            rows = adapter_rows(-ahead * s, ctx, place.behind(kind))
        else:
            rows = adapter_rows(ahead * s, 1 - ctx, place.behind(kind - half + 1))
        return pltpu.make_async_remote_copy(
            src_ref=rows,
            dst_ref=rows,
            send_sem=x_send.at[kind, s],
            recv_sem=x_recv.at[kind, s],
            device_id=place.sibling(),
            device_id_type=MESH,
        )

    def hop(w, way, s):
        offset = -s if way == 0 else s
        rows = blocks_out[w].at[ring.index(offset) * n_c + way]
        return pltpu.make_async_remote_copy(
            src_ref=rows,
            dst_ref=rows,
            send_sem=ring_send.at[w, way, s],
            recv_sem=ring_recv.at[w, way, s],
            device_id=ring.device(1 if way == 0 else n_dp - 1),
            device_id_type=MESH,
        )

    def hopped(w, way, s):
        offset = -(s + 1) if way == 0 else s + 1
        rows = blocks_out[w].at[ring.index(offset) * n_c + way]
        return pltpu.make_async_remote_copy(
            src_ref=rows,
            dst_ref=rows,
            send_sem=ring_send.at[w, way, s],
            recv_sem=ring_recv.at[w, way, s],
            device_id=ring.device(1),
            device_id_type=MESH,
        )

    around(0).start()
    own = pltpu.make_async_copy(own_rows, adapter_rows(0, ctx, part), own_sem.at[count])
    own.start()
    for w in range(count):
        for g in range(sz.seqs):
            here = at_home & (place.group == g)
            pl.when(jnp.logical_not(here))(lambda w=w, g=g: move(w, g).start())
        pl.when(at_home)(lambda w=w: stay(w).start())
    for kind in range(half):
        across(kind, 0).start()

    def adapter_step(s):
        if s < steps:
            arrival = pltpu.make_async_remote_copy(
                src_ref=own_rows,
                dst_ref=adapter_rows(-ahead * (s + 1), ctx, part),
                send_sem=a_send.at[s],
                recv_sem=a_recv.at[s],
                device_id=ring.device(1),
                device_id_type=MESH,
            )
            arrival.wait_recv()
            if s + 1 < steps:
                around(s + 1).start()
            for kind in range(half):
                across(kind, s + 1).start()

    def adapter_pass(s):
        for q in range(1, half):
            crossed(q, s).wait_recv()
            across(half - 1 + q, s).start()

    todo = []
    for k in range(count + steps):
        for s in range(min(k, steps - 1), -1, -1):
            w = k - s
            if w < count:
                todo.append((w, s))
    done = 0
    for w, s in todo:
        for way in range(n_c):
            if s == 0:
                moved(w, way)
            else:
                hopped(w, way, s - 1).wait_recv()
            hop(w, way, s).start()
        if done < steps:
            adapter_step(done)
        done += 1
    for s in range(done, steps):
        adapter_step(s)
    for s in range(n_dp):
        adapter_pass(s)
    for w in range(count):
        for way in range(n_c):
            hopped(w, way, steps - 1).wait_recv()
    for s in range(n_dp):
        crossed(0, s).wait_recv()
        for q in range(1, half):
            crossed(half - 1 + q, s).wait_recv()
    own.wait()
    for w in range(count):
        for g in range(sz.seqs):
            here = at_home & (place.group == g)
            pl.when(jnp.logical_not(here))(lambda w=w, g=g: move(w, g).wait_send())
        for way in range(n_c):
            for s in range(steps):
                hop(w, way, s).wait_send()
    for s in range(steps):
        around(s).wait_send()
    for s in range(n_dp):
        for kind in range(2 * half - 1):
            across(kind, s).wait_send()


def run_weights(sz, n_dp, adapter, blocks):
    bf16 = jnp.bfloat16
    slots = n_dp * sz.n_context
    outs = [jax.ShapeDtypeStruct((slots,) + a.shape, bf16) for a in [adapter] + blocks]
    count, steps, dma = len(blocks), n_dp - 1, pltpu.SemaphoreType.DMA
    kinds = 2 * sz.half - 1
    return pl.pallas_call(
        partial(weights_kernel, sz, n_dp),
        out_shape=outs,
        in_specs=[any_spec()] * (1 + count),
        out_specs=[any_spec()] * (1 + count),
        scratch_shapes=[
            dma((count, sz.seqs)),
            dma((count, sz.n_context)),
            dma((count, sz.n_context, steps)),
            dma((count, sz.n_context, steps)),
            dma((steps,)),
            dma((steps,)),
            dma((kinds, n_dp)),
            dma((kinds, n_dp)),
            dma((count + 1,)),
        ],
        compiler_params=pltpu.CompilerParams(collective_id=5, has_side_effects=True),
        name="weights",
    )(adapter, *blocks)


def norm_back(grad, rows, factor, gain):
    unit = rows * factor
    weighted = grad * gain
    inner = jnp.mean(weighted * unit, axis=-1, keepdims=True)
    return factor * (weighted - unit * inner), jnp.sum(grad * unit, axis=0, keepdims=True)


def ffn_back_kernel(sz, *refs):
    (cot, mixed, gains, rows_hbm, gate_hbm, up_hbm, wg_hbm, wu_hbm, down_hbm) = refs[:9]
    (grad_mixed, gain_grad, dgate_out, dup_out) = refs[9:13]
    (rows_s, gate_s, up_s, wg, wu, wd, load, load_down, keep_sem) = refs[13:22]
    scatter_refs = refs[22:]
    place = Place(sz)
    pairs = ((rows_hbm, rows_s), (gate_hbm, gate_s), (up_hbm, up_s), (wg_hbm, wg), (wu_hbm, wu))
    loads = [
        pltpu.make_async_copy(src, dst, load.at[i]) for i, (src, dst) in enumerate(pairs)
    ]
    down_loads = column_loads(down_hbm, wd, load_down)
    loads[0].start()
    for copy in down_loads + loads[1:]:
        copy.start()
    place.enter()
    scatter = Scatter(place, *scatter_refs)
    for copy in [loads[0]] + down_loads + loads[1:]:
        copy.wait()

    def work(q, j):
        rows = place.tile(q, j)
        dh = nt_dot(rows_s[rows, :], wd[...])
        gate = gate_s[rows, :].astype(jnp.float32)
        up = up_s[rows, :].astype(jnp.float32)
        sig = 1.0 / (1.0 + jnp.exp(-gate))
        dgate = (dh * up * sig * (1.0 + gate * (1.0 - sig))).astype(jnp.bfloat16)
        dup = (dh * gate * sig).astype(jnp.bfloat16)
        gate_s[rows, :] = dgate
        up_s[rows, :] = dup
        scatter.part[...] = nt_dot(dgate, wg[...]) + nt_dot(dup, wu[...])
        scatter.give(q, j)

    far = range(1, sz.half)
    for j in range(sz.seqs):
        for q in far:
            work(q, j)
        if j:
            for q in far:
                scatter.onward(q, j - 1)
    work(0, 0)
    for q in far:
        scatter.onward(q, sz.seqs - 1)
    for j in range(1, sz.seqs):
        work(0, j)
    copies = [
        pltpu.make_async_copy(gate_s, dgate_out, keep_sem.at[0]),
        pltpu.make_async_copy(up_s, dup_out, keep_sem.at[1]),
    ]
    for copy in copies:
        copy.start()
    gain_total = None
    for j in range(sz.seqs):
        span = slice(j * sz.block, (j + 1) * sz.block)
        rows = mixed[span, :]
        grad, gain_here = norm_back(scatter.total(j), rows, rms_factor(rows), gains[1:2, :])
        grad_mixed[span, :] = cot[span, :].astype(jnp.float32) + grad
        gain_total = gain_here if gain_total is None else gain_total + gain_here
    gain_grad[...] = gain_total
    scatter.finish()
    for copy in copies:
        copy.wait()


def run_ffn_back(sz, cot, mixed, gains, rows, gate, up, wg, wu, down):
    f32, bf16, shape = jnp.float32, jnp.bfloat16, jax.ShapeDtypeStruct
    dma = pltpu.SemaphoreType.DMA
    return pl.pallas_call(
        partial(ffn_back_kernel, sz),
        out_shape=[
            shape((sz.rows, sz.width), f32),
            shape((1, sz.width), f32),
            shape((sz.seq_len, sz.ff), bf16),
            shape((sz.seq_len, sz.ff), bf16),
        ],
        in_specs=[full_spec()] * 3 + [any_spec()] * 6,
        out_specs=[full_spec()] * 2 + [any_spec()] * 2,
        scratch_shapes=[
            pltpu.VMEM((sz.seq_len, sz.width), bf16),
            pltpu.VMEM((sz.seq_len, sz.ff), bf16),
            pltpu.VMEM((sz.seq_len, sz.ff), bf16),
            pltpu.VMEM(wg.shape, bf16),
            pltpu.VMEM(wu.shape, bf16),
            pltpu.VMEM((sz.ff, sz.width), bf16),
            dma((5,)),
            dma((down.shape[0],)),
            dma((2,)),
        ]
        + Scatter.scratch(sz),
        compiler_params=pltpu.CompilerParams(
            collective_id=6, has_side_effects=True, vmem_limit_bytes=VMEM_BYTES
        ),
        cost_estimate=pl.CostEstimate(
            flops=6 * sz.seq_len * sz.width * sz.ff, bytes_accessed=40 << 20, transcendentals=0
        ),
        name="ffn_back",
    )(cot, mixed, gains, rows, gate, up, wg, wu, down)


def attn_back_kernel(sz, *refs):
    (grad_mixed, adapted, gains, cos_t, sin_t, begin) = refs[:6]
    (q_hbm, k_hbm, v_hbm, lse_hbm, out_hbm, qkv_hbm) = refs[6:12]
    (grad_low, gain_grad, rows_out, proj_out) = refs[12:16]
    (rows_s, q_s, k_s, v_s, lse_s, do_s, dk_s, dv_s, proj_s, wout, wqkv) = refs[16:27]
    (load, load_out, keep_sem) = refs[27:30]
    gather_refs = refs[30:32]
    scatter_refs = refs[32:]
    place = Place(sz)
    pairs = ((q_hbm, q_s), (k_hbm, k_s), (v_hbm, v_s), (lse_hbm, lse_s), (qkv_hbm, wqkv))
    loads = [
        pltpu.make_async_copy(src, dst, load.at[i]) for i, (src, dst) in enumerate(pairs)
    ]
    out_loads = column_loads(out_hbm, wout, load_out)
    for copy in out_loads + loads:
        copy.start()
    place.enter()
    gather = Gather(place, rows_s, *gather_refs)
    scatter = Scatter(place, *scatter_refs)
    for j in range(sz.seqs):
        span = slice(j * sz.block, (j + 1) * sz.block)
        rows_s[gather.own(j), :] = grad_mixed[span, :].astype(jnp.bfloat16)
        gather.start(j)
    for copy in out_loads:
        copy.wait()
    d = sz.head_dim

    def heads_grad(q, j):
        rows = place.tile(q, j)
        dhead = nt_dot(rows_s[rows, :], wout[...]).astype(jnp.bfloat16)
        for h in range(sz.heads):
            do_s[h, rows, :] = dhead[:, h * d : (h + 1) * d]

    far = range(1, sz.half)
    for j in range(sz.seqs):
        gather.wait_near(j)
        heads_grad(0, j)
    for copy in loads:
        copy.wait()
    for j in range(sz.seqs):
        for q in far:
            gather.forward(q, j)
        for q in far:
            gather.wait_far(sz.half - q, j)
            heads_grad(q, j)
    copies = [pltpu.make_async_copy(rows_s, rows_out, keep_sem.at[0])]
    copies[0].start()

    tiles = sz.n_tensor
    scale = 1.0 / math.sqrt(d)

    def head(h, carry):
        for i in reversed(range(tiles)):
            rows = slice(i * sz.tile, (i + 1) * sz.tile)
            length = (i + 1) * sz.tile
            keys, values = k_s[h, 0:length, :], v_s[h, 0:length, :]
            query, grad = q_s[h, rows, :], do_s[h, rows, :]
            start = begin[:, rows]
            key_at = lax.broadcasted_iota(jnp.int32, (length, sz.tile), 0)
            query_at = i * sz.tile + lax.broadcasted_iota(jnp.int32, (1, sz.tile), 1)
            allowed = (key_at >= start) & (key_at <= query_at)
            scores = nt_dot(keys, query)
            scores = jnp.where(allowed, scores * (LOG2E * scale), masked_score)
            probs = jnp.exp2(scores - lse_s[h, :, rows])
            dprobs = nt_dot(values, grad)
            inner = jnp.sum(probs * dprobs, axis=0, keepdims=True)
            dscores = (probs * (dprobs - inner)).astype(jnp.bfloat16)
            dv = nn_dot(probs.astype(jnp.bfloat16), grad)
            dk = nn_dot(dscores, query)
            if i == tiles - 1:
                dv_s[...] = dv
                dk_s[...] = dk
            else:
                dv_s[0:length, :] += dv
                dk_s[0:length, :] += dk
            dq = jnp.transpose(tn_dot(keys, dscores)) * scale
            cos_here, sin_here = cos_t[rows, :], sin_t[rows, :]
            proj_s[rows, pl.ds(pl.multiple_of(h * 3 * d, d), d)] = turn(
                dq, cos_here, -sin_here
            ).astype(jnp.bfloat16)
        dk = turn(dk_s[...] * scale, cos_t[...], -sin_t[...])
        proj_s[:, pl.ds(pl.multiple_of(h * 3 * d + d, d), d)] = dk.astype(jnp.bfloat16)
        proj_s[:, pl.ds(pl.multiple_of(h * 3 * d + 2 * d, d), d)] = dv_s[...].astype(jnp.bfloat16)
        return carry

    lax.fori_loop(0, sz.heads, head, 0)
    copies.append(pltpu.make_async_copy(proj_s, proj_out, keep_sem.at[1]))
    copies[1].start()

    def give(q, j):
        scatter.part[...] = nt_dot(proj_s[place.tile(q, j), :], wqkv[...])
        scatter.give(q, j)

    for j in range(sz.seqs):
        for q in far:
            give(q, j)
        if j:
            for q in far:
                scatter.onward(q, j - 1)
    give(0, 0)
    for q in far:
        scatter.onward(q, sz.seqs - 1)
    for j in range(1, sz.seqs):
        give(0, j)
    gather.finish()
    gain_total = None
    for j in range(sz.seqs):
        span = slice(j * sz.block, (j + 1) * sz.block)
        rows = adapted[span, :]
        grad, gain_here = norm_back(scatter.total(j), rows, rms_factor(rows), gains[0:1, :])
        grad_low[span, :] = (grad_mixed[span, :] + grad).astype(jnp.bfloat16)
        gain_total = gain_here if gain_total is None else gain_total + gain_here
    gain_grad[...] = gain_total
    scatter.finish()
    for copy in copies:
        copy.wait()


def run_attn_back(sz, grad_mixed, adapted, gains, cos_t, sin_t, begin, q, k, v, lse, out, qkv):
    f32, bf16, shape = jnp.float32, jnp.bfloat16, jax.ShapeDtypeStruct
    dma = pltpu.SemaphoreType.DMA
    heads_shape = (sz.heads, sz.seq_len, sz.head_dim)
    return pl.pallas_call(
        partial(attn_back_kernel, sz),
        out_shape=[
            shape((sz.rows, sz.width), bf16),
            shape((1, sz.width), f32),
            shape((sz.seq_len, sz.width), bf16),
            shape((sz.seq_len, qkv.shape[1]), bf16),
        ],
        in_specs=[full_spec()] * 6 + [any_spec()] * 6,
        out_specs=[full_spec()] * 2 + [any_spec()] * 2,
        scratch_shapes=[
            pltpu.VMEM((sz.seq_len, sz.width), bf16),
            pltpu.VMEM(heads_shape, bf16),
            pltpu.VMEM(heads_shape, bf16),
            pltpu.VMEM(heads_shape, bf16),
            pltpu.VMEM((sz.heads, 1, sz.seq_len), f32),
            pltpu.VMEM(heads_shape, bf16),
            pltpu.VMEM((sz.seq_len, sz.head_dim), f32),
            pltpu.VMEM((sz.seq_len, sz.head_dim), f32),
            pltpu.VMEM((sz.seq_len, qkv.shape[1]), bf16),
            pltpu.VMEM((sz.heads * sz.head_dim, sz.width), bf16),
            pltpu.VMEM(qkv.shape, bf16),
            dma((5,)),
            dma((out.shape[0],)),
            dma((2,)),
        ]
        + Gather.scratch(sz)
        + Scatter.scratch(sz),
        compiler_params=pltpu.CompilerParams(
            collective_id=7, has_side_effects=True, vmem_limit_bytes=VMEM_BYTES
        ),
        cost_estimate=pl.CostEstimate(
            flops=4 * sz.seq_len * sz.width * qkv.shape[1], bytes_accessed=30 << 20, transcendentals=0
        ),
        name="attn_back",
    )(grad_mixed, adapted, gains, cos_t, sin_t, begin, q, k, v, lse, out, qkv)


def grads_kernel(sz, n_dp, count, *refs):
    xs, ys, outs = refs[:count], refs[count : 2 * count], refs[2 * count : 3 * count]
    refs = refs[3 * count :]
    y_s, first, held, landed = (refs[i * count : (i + 1) * count] for i in range(4))
    (x_s, load_y, load_x, ring_send, ring_recv, move_send, move_recv, own_sem) = refs[4 * count :]
    place = Place(sz)
    ring = Ring(place, n_dp)
    t = lax.axis_index("tensor")
    ctx, part, half, n_c = place.ctx, place.part, sz.half, sz.n_context
    role = part * n_c + ctx
    at_home = role == t
    depth = x_s.shape[3]

    y_loads = [pltpu.make_async_copy(ys[w], y_s[w], load_y.at[w]) for w in range(count)]
    for copy in y_loads:
        copy.start()

    tasks = []
    for k in range(count + n_dp):
        for s in range(min(k, n_dp - 1), -1, -1):
            if k - s < count:
                tasks.append((k - s, s))

    def slot(way, s):
        return ring.index(-(s + 1) if way == 0 else s + 1) * n_c + way

    def x_load(k, way):
        w, s = tasks[k]
        if xs[w].shape[0] == 1:
            at = pl.multiple_of(slot(way, s) * depth, depth)
            src = xs[w].at[0, :, pl.ds(at, depth)]
        else:
            src = xs[w].at[slot(way, s)]
        return pltpu.make_async_copy(src, x_s.at[k % 2, way], load_x.at[k % 2, way])

    for way in range(n_c):
        x_load(0, way).start()

    barrier = pltpu.get_barrier_semaphore()

    def greet(device):
        pl.semaphore_signal(barrier, inc=1, device_id=device, device_id_type=MESH)

    def holder(g):
        return (place.dp, g * half + t // n_c, lax.rem(t, n_c))

    greet(ring.device(1))
    greet(ring.device(n_dp - 1))
    for g in range(sz.seqs):
        pl.when(jnp.logical_not(at_home & (place.group == g)))(lambda g=g: greet(holder(g)))
    pl.semaphore_wait(barrier, 2 + n_c - jnp.where(at_home, 1, 0))

    def source(w, way, s):
        return first[w].at[way] if s == 0 else held[w].at[way, s - 1]

    def hop(w, way, s):
        return pltpu.make_async_remote_copy(
            src_ref=source(w, way, s),
            dst_ref=held[w].at[way, s],
            send_sem=ring_send.at[w, way, s],
            recv_sem=ring_recv.at[w, way, s],
            device_id=ring.device(1 if way == 0 else n_dp - 1),
            device_id_type=MESH,
        )

    def deliver(w, way):
        return pltpu.make_async_remote_copy(
            src_ref=source(w, way, n_dp - 1),
            dst_ref=landed[w].at[place.group],
            send_sem=move_send.at[w, way],
            recv_sem=move_recv.at[w, place.group],
            device_id=(place.dp, role, way),
            device_id_type=MESH,
        )

    def stay(w, way):
        return pltpu.make_async_copy(
            source(w, way, n_dp - 1), landed[w].at[place.group], own_sem.at[w]
        )

    def arrived(w, g):
        arrival = pltpu.make_async_remote_copy(
            src_ref=landed[w].at[g],
            dst_ref=landed[w].at[g],
            send_sem=move_send.at[w, 0],
            recv_sem=move_recv.at[w, g],
            device_id=(place.dp, t, 1 - ctx),
            device_id_type=MESH,
        )
        here = at_home & (place.group == g)
        pl.when(here)(lambda: stay(w, 0).wait())
        pl.when(jnp.logical_not(here))(lambda: arrival.wait_recv())

    waited = set()
    for k, (w, s) in enumerate(tasks):
        if k + 1 < len(tasks):
            for way in range(n_c):
                x_load(k + 1, way).start()
        if w not in waited:
            y_loads[w].wait()
            waited.add(w)
        for way in range(n_c):
            x_load(k, way).wait()
            value = tn_dot(x_s[k % 2, way], y_s[w][...])
            if s:
                hop(w, way, s - 1).wait_recv()
                value = value + held[w][way, s - 1].astype(jnp.float32)
            ref = source(w, way, s)
            ref[...] = value.astype(jnp.bfloat16)
            if s < n_dp - 1:
                hop(w, way, s).start()
            else:
                here = at_home & (ctx == way)
                pl.when(here)(lambda w=w, way=way: stay(w, way).start())
                pl.when(jnp.logical_not(here))(lambda w=w, way=way: deliver(w, way).start())
    for w in range(count):
        for g in range(sz.seqs):
            arrived(w, g)
        total = landed[w][0].astype(jnp.float32)
        for g in range(1, sz.seqs):
            total = total + landed[w][g].astype(jnp.float32)
        outs[w][...] = total
    for w in range(count):
        for way in range(n_c):
            for s in range(n_dp - 1):
                hop(w, way, s).wait_send()
            here = at_home & (ctx == way)
            pl.when(jnp.logical_not(here))(lambda w=w, way=way: deliver(w, way).wait_send())


def run_grads(sz, n_dp, xs, ys):
    bf16, count, dma = jnp.bfloat16, len(xs), pltpu.SemaphoreType.DMA
    slots = n_dp * sz.n_context
    depth = sz.width // slots
    if depth % 128:
        xs = [x.reshape(sz.seq_len, slots, depth).transpose(1, 0, 2) for x in xs]
    else:
        xs = [x[None] for x in xs]
    wide = [y.shape[1] for y in ys]
    ways, steps = sz.n_context, n_dp - 1
    return pl.pallas_call(
        partial(grads_kernel, sz, n_dp, count),
        out_shape=[jax.ShapeDtypeStruct((depth, n), jnp.float32) for n in wide],
        in_specs=[any_spec()] * (2 * count),
        out_specs=[full_spec()] * count,
        scratch_shapes=[pltpu.VMEM((sz.seq_len, n), bf16) for n in wide]
        + [pltpu.VMEM((ways, depth, n), bf16) for n in wide]
        + [pltpu.VMEM((ways, steps, depth, n), bf16) for n in wide]
        + [pltpu.VMEM((sz.seqs, depth, n), bf16) for n in wide]
        + [
            pltpu.VMEM((2, ways, sz.seq_len, depth), bf16),
            dma((count,)),
            dma((2, ways)),
            dma((count, ways, steps)),
            dma((count, ways, steps)),
            dma((count, ways)),
            dma((count, sz.seqs)),
            dma((count,)),
        ],
        compiler_params=pltpu.CompilerParams(
            collective_id=8, has_side_effects=True, vmem_limit_bytes=VMEM_BYTES
        ),
        cost_estimate=pl.CostEstimate(
            flops=2 * sz.seq_len * sz.width * sum(wide), bytes_accessed=60 << 20, transcendentals=0
        ),
        name="grads",
    )(*xs, *ys)


def shards(
    embedded,
    initial_state,
    cotangent,
    doc_ids,
    recurrences,
    adapter_weight,
    norm_gains,
    qkv_weight,
    output_head_weight,
    gate_up_weight,
    down_weight,
):
    n_dp = lax.axis_size("dp")
    n_tensor = lax.axis_size("tensor")
    n_context = lax.axis_size("context")
    dp_index = lax.axis_index("dp")
    t_index = lax.axis_index("tensor")
    ctx_index = lax.axis_index("context")
    seq_count, block_rows, model_width = embedded.shape
    seq_len = doc_ids.shape[1]
    half = n_tensor // seq_count
    group = t_index // half
    part = t_index % half
    heads_here = qkv_weight.shape[1]
    head_dim = qkv_weight.shape[2] // 3
    ff_here = down_weight.shape[0]
    pair_swap = [(i, (i + half) % n_tensor) for i in range(n_tensor)]
    members = half * n_context
    groups = [
        [g * members + i for i in range(members)] for g in range(seq_count)
    ]

    def swap_in(rows):
        own = lax.dynamic_index_in_dim(rows, group, 0, keepdims=False)
        other = lax.dynamic_index_in_dim(rows, 1 - group, 0, keepdims=False)
        got = lax.ppermute(other, "tensor", pair_swap)
        first = jnp.where(group == 0, own, got)
        second = jnp.where(group == 0, got, own)
        return jnp.concatenate([first, second], axis=0)

    def swap_out(rows):
        first, second = rows[:block_rows], rows[block_rows:]
        own = jnp.where(group == 0, first, second)
        other = jnp.where(group == 0, second, first)
        got = lax.ppermute(other, "tensor", pair_swap)
        return jnp.stack(
            [jnp.where(group == 0, own, got), jnp.where(group == 0, got, own)], axis=0
        )

    def side_by_side(blocks):
        count, depth, columns = blocks.shape
        return blocks.transpose(1, 0, 2).reshape(depth, count * columns)

    def role_grad(grad, axis):
        piece = lax.psum_scatter(
            grad.astype(jnp.bfloat16), "dp", scatter_dimension=axis, tiled=True
        )
        low, high = jnp.split(piece, 2, axis=axis)
        give = [jnp.where(group == 0, low, high), jnp.where(group == 0, high, low)]
        back = [
            lax.ppermute(g, ("tensor", "context"), [(b, a) for a, b in perm])
            for g, perm in zip(give, role_perms)
        ]
        return back[0].astype(jnp.float32) + back[1].astype(jnp.float32)

    def gather_rows(rows):
        full = lax.all_gather(
            rows, ("tensor", "context"), axis=0, tiled=True, axis_index_groups=groups
        )
        split = full.reshape(half, n_context, seq_count, block_rows, model_width)
        return split.transpose(2, 0, 1, 3, 4).reshape(seq_len, model_width)

    embed_rows = swap_in(embedded)
    state_rows = swap_in(initial_state)
    cot_rows = swap_in(cotangent)
    sz = Sizes(
        n_tensor,
        n_context,
        seq_count,
        half,
        block_rows,
        n_context * block_rows,
        seq_count * block_rows,
        seq_len,
        model_width,
        heads_here,
        head_dim,
        ff_here,
    )
    adapter_block = adapter_weight.shape[0]
    gain_columns = norm_gains.shape[1]
    unit = 16 * half
    padded = -(-(adapter_block + 2) // unit) * unit
    adapter_rows = jnp.concatenate(
        [
            adapter_weight,
            jnp.pad(
                norm_gains,
                ((0, padded - adapter_block - 2), (0, model_width - gain_columns)),
            ),
        ],
        axis=0,
    )
    adapter_all, qkv_use, out_blocks, gate_use, up_use, down_blocks = run_weights(
        sz,
        n_dp,
        adapter_rows,
        [
            qkv_weight.reshape(qkv_weight.shape[0], -1),
            output_head_weight.reshape(heads_here * head_dim, -1),
            gate_up_weight[:, 0],
            gate_up_weight[:, 1],
            down_weight,
        ],
    )
    qkv_use = qkv_use.reshape(model_width, -1)
    gate_use = gate_use.reshape(model_width, -1)
    up_use = up_use.reshape(model_width, -1)
    gains_full = (
        adapter_all[:, adapter_block : adapter_block + 2, :gain_columns]
        .transpose(1, 0, 2)
        .reshape(2, model_width)
    )
    adapter_low = adapter_all[adapter_all.shape[0] // 2 :, :adapter_block].reshape(
        model_width, model_width
    )
    if out_blocks.shape[2] % 128:
        out_blocks = side_by_side(out_blocks)[None]
        down_blocks = side_by_side(down_blocks)[None]
    gains_f = gains_full.astype(jnp.float32)

    order = jnp.arange(seq_len, dtype=jnp.int32)
    cos_t, sin_t = rope_angles(order, head_dim)
    cos_full = jnp.concatenate([cos_t, cos_t], axis=1)
    sin_full = jnp.concatenate([-sin_t, sin_t], axis=1)
    own_seq = dp_index * seq_count + group
    docs = lax.dynamic_index_in_dim(doc_ids, own_seq, 0, keepdims=False)
    begin = jnp.sum((docs[None, :] < docs[:, None]).astype(jnp.int32), axis=1)[None, :]
    steps_own = lax.dynamic_index_in_dim(recurrences, own_seq, 0, keepdims=False) - BACK
    embed_part = jnp.dot(
        embed_rows, adapter_low, preferred_element_type=jnp.float32
    )

    def advance(step_index, current):
        (mixed,) = run_attn(
            sz, False, current, embed_part, gains_f, cos_full, sin_full, begin,
            adapter_all, qkv_use, out_blocks,
        )
        active = jnp.broadcast_to((step_index < steps_own).astype(jnp.float32), (1, model_width))
        (result,) = run_ffn(
            sz, False, mixed, current, active, gains_f, gate_use, up_use, down_blocks
        )
        return result

    detached = lax.fori_loop(
        0, jnp.max(recurrences) - BACK, advance, state_rows.astype(jnp.float32)
    )
    (mixed_rows, adapted, feature_rows, query_hm, key_hm, value_hm, head_flat, lse) = run_attn(
        sz, True, detached, embed_part, gains_f, cos_full, sin_full, begin,
        adapter_all, qkv_use, out_blocks,
    )
    (current, ffn_input, gate_pre, up_pre, hidden) = run_ffn(
        sz, True, mixed_rows, detached, gains_f[:1], gains_f, gate_use, up_use, down_blocks
    )
    latent_low = detached.astype(jnp.bfloat16)
    grad_ffn = gather_rows(cot_rows)
    grad_mixed, gain_b, grad_gate, grad_up = run_ffn_back(
        sz, cot_rows, mixed_rows, gains_f, grad_ffn, gate_pre, up_pre, gate_use, up_use, down_blocks
    )
    adapted_low, gain_a, grad_rows, grad_proj = run_attn_back(
        sz, grad_mixed, adapted, gains_f, cos_full, sin_full, begin,
        query_hm, key_hm, value_hm, lse, out_blocks, qkv_use,
    )
    down_t, gate_s, up_s, qkv_s, out_t = run_grads(
        sz,
        n_dp,
        [grad_ffn, ffn_input, ffn_input, feature_rows, grad_rows],
        [hidden, grad_gate, grad_up, grad_proj, head_flat],
    )
    down_s = down_t.T
    out_s = out_t.T.reshape(heads_here, head_dim, -1)
    qkv_s = qkv_s.reshape(-1, heads_here, 3 * head_dim)
    gate_up_s = jnp.stack([gate_s, up_s], axis=1)
    joined = jnp.concatenate([latent_low, embed_rows], axis=-1)
    adapter_g = jnp.einsum("rk,rd->kd", joined, adapted_low, preferred_element_type=jnp.float32)
    embed_out = jnp.einsum(
        "srd,kd->srk",
        swap_out(adapted_low),
        adapter_low,
        preferred_element_type=jnp.float32,
    )
    adapter_s = lax.psum_scatter(
        adapter_g.astype(jnp.bfloat16), ("dp", "context"), scatter_dimension=0, tiled=True
    )
    gains_s = lax.psum_scatter(
        jnp.concatenate([gain_a, gain_b]).astype(jnp.bfloat16),
        ("dp", "context"),
        scatter_dimension=1,
        tiled=True,
    )
    adapter_s = lax.psum(adapter_s, "tensor").astype(jnp.float32)
    gains_s = lax.psum(gains_s, "tensor").astype(jnp.float32)
    return (swap_out(current), embed_out, adapter_s, gains_s, qkv_s, out_s, gate_up_s, down_s)


def solution(mesh):
    placed = (
        P("dp", ("tensor", "context"), None),
        P("dp", ("tensor", "context"), None),
        P("dp", ("tensor", "context"), None),
        P(),
        P(),
        P(("dp", "context"), None),
        P(None, ("dp", "context")),
        P(("dp", "context"), "tensor", None),
        P("tensor", None, ("dp", "context")),
        P(("dp", "context"), None, "tensor"),
        P("tensor", ("dp", "context")),
    )
    return jax.shard_map(
        shards,
        mesh=mesh,
        in_specs=placed,
        out_specs=(
            P("dp", ("tensor", "context"), None),
            P("dp", ("tensor", "context"), None),
            P(("dp", "context"), None),
            P(None, ("dp", "context")),
            P(("dp", "context"), "tensor", None),
            P("tensor", None, ("dp", "context")),
            P(("dp", "context"), None, "tensor"),
            P("tensor", ("dp", "context")),
        ),
        check_vma=False,
    )
```

```python
from functools import partial
import math
from typing import NamedTuple

import jax
import jax.numpy as jnp
import numpy as np
from jax import lax
from jax.experimental import pallas as pl
from jax.experimental.pallas import tpu as pltpu
from jax.sharding import PartitionSpec as P

BACK = 1
MAXR = 4


rope_base = 50000.0
norm_eps = 1e-06
masked_score = -1e30


def rope_tables(seq_len, head_dim):
    freq_index = np.arange(head_dim // 2, dtype=np.float32)
    inv_freq = 1.0 / np.float32(rope_base) ** (np.float32(2.0) * freq_index / head_dim)
    angles = np.arange(seq_len, dtype=np.float32)[:, None] * inv_freq.astype(np.float32)[None, :]
    cos_t, sin_t = np.cos(angles), np.sin(angles)
    return (
        jnp.asarray(np.concatenate([cos_t, cos_t], axis=1), jnp.float32),
        jnp.asarray(np.concatenate([-sin_t, sin_t], axis=1), jnp.float32),
    )


MESH = pl.DeviceIdType.MESH
LOG2E = 1.4426950408889634
VMEM_BYTES = 62 << 20


class Sizes(NamedTuple):
    n_tensor: int
    n_context: int
    seqs: int
    half: int
    block: int
    tile: int
    rows: int
    seq_len: int
    width: int
    heads: int
    head_dim: int
    ff: int


def full_spec():
    return pl.BlockSpec(memory_space=pltpu.VMEM)


def any_spec():
    return pl.BlockSpec(memory_space=pl.ANY)


def nt_dot(a, b):
    return lax.dot_general(a, b, (((1,), (1,)), ((), ())), preferred_element_type=jnp.float32)


def tn_dot(a, b):
    return lax.dot_general(a, b, (((0,), (0,)), ((), ())), preferred_element_type=jnp.float32)


def nn_dot(a, b):
    return jnp.dot(a, b, preferred_element_type=jnp.float32)


class Place:
    def __init__(self, sz):
        t = lax.axis_index("tensor")
        self.sz = sz
        self.dp = lax.axis_index("dp")
        self.ctx = lax.axis_index("context")
        self.group = t // sz.half
        self.part = lax.rem(t, sz.half)

    def device(self, part, ctx):
        return (self.dp, self.group * self.sz.half + part, ctx)

    def ahead(self, q):
        return lax.rem(self.part + q, self.sz.half)

    def behind(self, q):
        return lax.rem(self.part + (self.sz.half - q), self.sz.half)

    def sibling(self):
        return self.device(self.part, 1 - self.ctx)

    def block(self, part, ctx, j):
        sz = self.sz
        first = ((part + j * sz.half) * sz.n_context + ctx) * sz.block
        return pl.ds(pl.multiple_of(first, sz.block), sz.block)

    def tile(self, q, j):
        sz = self.sz
        first = (self.ahead(q) + j * sz.half) * sz.tile
        return pl.ds(pl.multiple_of(first, sz.tile), sz.tile)

    def enter(self, others=(), more=0):
        barrier = pltpu.get_barrier_semaphore()
        for device in others:
            pl.semaphore_signal(barrier, inc=1, device_id=device, device_id_type=MESH)
        pl.semaphore_signal(
            barrier, inc=1, device_id=self.sibling(), device_id_type=MESH
        )
        for q in range(1, self.sz.half):
            pl.semaphore_signal(
                barrier,
                inc=1,
                device_id=self.device(self.ahead(q), self.ctx),
                device_id_type=MESH,
            )
        pl.semaphore_wait(barrier, self.sz.half + len(others) + more)


class Gather:
    @staticmethod
    def scratch(sz):
        kinds = 2 * sz.half - 1
        return [
            pltpu.SemaphoreType.DMA((kinds, sz.seqs)),
            pltpu.SemaphoreType.DMA((kinds, sz.seqs)),
        ]

    def __init__(self, place, ref, send, recv):
        self.place, self.ref, self.send, self.recv = place, ref, send, recv

    def copy(self, kind, j, rows):
        place, half = self.place, self.place.sz.half
        if 0 < kind < half:
            target = place.device(place.ahead(kind), place.ctx)
        else:
            target = place.sibling()
        return pltpu.make_async_remote_copy(
            src_ref=self.ref.at[rows],
            dst_ref=self.ref.at[rows],
            send_sem=self.send.at[kind, j],
            recv_sem=self.recv.at[kind, j],
            device_id=target,
            device_id_type=MESH,
        )

    def own(self, j):
        return self.place.block(self.place.part, self.place.ctx, j)

    def start(self, j):
        for q in range(1, self.place.sz.half):
            self.copy(q, j, self.own(j)).start()
        self.copy(0, j, self.own(j)).start()

    def wait_near(self, j):
        place = self.place
        self.copy(0, j, place.block(place.part, 1 - place.ctx, j)).wait_recv()

    def forward(self, q, j):
        place = self.place
        rows = place.block(place.behind(q), place.ctx, j)
        self.copy(q, j, rows).wait_recv()
        self.copy(place.sz.half - 1 + q, j, rows).start()

    def wait_far(self, q, j):
        place = self.place
        rows = place.block(place.behind(q), 1 - place.ctx, j)
        self.copy(place.sz.half - 1 + q, j, rows).wait_recv()

    def finish(self):
        place, half = self.place, self.place.sz.half
        for j in range(place.sz.seqs):
            for kind in range(half):
                self.copy(kind, j, self.own(j)).wait_send()
            for q in range(1, half):
                rows = place.block(place.behind(q), place.ctx, j)
                self.copy(half - 1 + q, j, rows).wait_send()


class Scatter:
    @staticmethod
    def scratch(sz):
        kinds = 2 * sz.half - 1
        near = (sz.half, sz.seqs, sz.block, sz.width)
        far = (max(sz.half - 1, 1), sz.seqs, sz.block, sz.width)
        return [
            pltpu.VMEM((sz.tile, sz.width), jnp.float32),
            pltpu.VMEM(near, jnp.bfloat16),
            pltpu.VMEM(near, jnp.bfloat16),
            pltpu.VMEM(near, jnp.bfloat16),
            pltpu.VMEM(far, jnp.bfloat16),
            pltpu.VMEM(far, jnp.bfloat16),
            pltpu.SemaphoreType.DMA((kinds, sz.seqs)),
            pltpu.SemaphoreType.DMA((kinds, sz.seqs)),
        ]

    def __init__(self, place, part, mine, near_out, near_in, far_out, far_in, send, recv):
        self.place, self.part, self.mine = place, part, mine
        self.near_out, self.near_in = near_out, near_in
        self.far_out, self.far_in = far_out, far_in
        self.send, self.recv = send, recv

    def near(self, q, j):
        return pltpu.make_async_remote_copy(
            src_ref=self.near_out.at[q, j],
            dst_ref=self.near_in.at[q, j],
            send_sem=self.send.at[q, j],
            recv_sem=self.recv.at[q, j],
            device_id=self.place.sibling(),
            device_id_type=MESH,
        )

    def far(self, q, j):
        place = self.place
        return pltpu.make_async_remote_copy(
            src_ref=self.far_out.at[q - 1, j],
            dst_ref=self.far_in.at[q - 1, j],
            send_sem=self.send.at[place.sz.half - 1 + q, j],
            recv_sem=self.recv.at[place.sz.half - 1 + q, j],
            device_id=place.device(place.ahead(q), place.ctx),
            device_id_type=MESH,
        )

    def give(self, q, j):
        sz, ctx = self.place.sz, self.place.ctx
        mine = pl.ds(pl.multiple_of(ctx * sz.block, sz.block), sz.block)
        other = pl.ds(pl.multiple_of((1 - ctx) * sz.block, sz.block), sz.block)
        self.near_out[q, j] = self.part[other, :].astype(jnp.bfloat16)
        self.near(q, j).start()
        self.mine[q, j] = self.part[mine, :].astype(jnp.bfloat16)

    def onward(self, q, j):
        self.near(q, j).wait_recv()
        self.far_out[q - 1, j] = (
            self.mine[q, j].astype(jnp.float32) + self.near_in[q, j].astype(jnp.float32)
        ).astype(jnp.bfloat16)
        self.far(q, j).start()

    def total(self, j):
        self.near(0, j).wait_recv()
        total = self.mine[0, j].astype(jnp.float32) + self.near_in[0, j].astype(jnp.float32)
        for q in range(1, self.place.sz.half):
            self.far(q, j).wait_recv()
            total = total + self.far_in[q - 1, j].astype(jnp.float32)
        return total

    def finish(self):
        half = self.place.sz.half
        for j in range(self.place.sz.seqs):
            for q in range(half):
                self.near(q, j).wait_send()
            for q in range(1, half):
                self.far(q, j).wait_send()


def column_loads(blocks_ref, vmem_ref, sem):
    count, _, columns = blocks_ref.shape
    return [
        pltpu.make_async_copy(
            blocks_ref.at[b], vmem_ref.at[:, pl.ds(b * columns, columns)], sem.at[b]
        )
        for b in range(count)
    ]


def adapter_loads(blocks_ref, vmem_ref, sem):
    count, tops = sem.shape
    depth, columns = vmem_ref.shape[0] // tops, vmem_ref.shape[1] // count
    return [
        [
            pltpu.make_async_copy(
                blocks_ref.at[b, pl.ds(0, depth), pl.ds(n * columns, columns)],
                vmem_ref.at[pl.ds(b * depth, depth), pl.ds(n * columns, columns)],
                sem.at[n, b],
            )
            for b in range(tops)
        ]
        for n in range(count)
    ]


def rms_factor(rows):
    return lax.rsqrt(jnp.mean(rows * rows, axis=-1, keepdims=True) + norm_eps)


def turn(x, cos_t, sin_t):
    return x * cos_t + pltpu.roll(x, x.shape[-1] // 2, 1) * sin_t


def attn_kernel(sz, n_dp, keep, *refs):
    (latent, embed, gains, cos_t, sin_t, begin, adapter_hbm, qkv_hbm, out_hbm) = refs[:9]
    refs = refs[9:]
    if keep:
        embed_hbm, refs = refs[0], refs[1:]
    mixed = refs[0]
    refs = refs[1:]
    if keep:
        adapted_out, rows_out, q_out, k_out, v_out, head_out, lse_out, joined_out = refs[:8]
        refs = refs[8:]
    (wa, wqkv, wout, adapted, rows_s, q_s, k_s, v_s, head_s, lse_s) = refs[:10]
    load_a, load_qkv, load_out, keep_sem = refs[10:14]
    gather_refs = refs[14:16]
    scatter_refs = refs[16:24]
    if keep:
        joined_s, load_embed, x_send, x_recv = refs[24:]

    place = Place(sz)
    a_loads = adapter_loads(adapter_hbm, wa, load_a)
    qkv_load = pltpu.make_async_copy(qkv_hbm, wqkv, load_qkv)
    out_loads = column_loads(out_hbm, wout, load_out)
    for group in a_loads:
        for copy in group:
            copy.start()
    qkv_load.start()
    for copy in out_loads:
        copy.start()
    others = []
    if keep:
        ring = Ring(place, n_dp)
        t = lax.axis_index("tensor")
        embed_load = pltpu.make_async_copy(
            embed_hbm, joined_s.at[:, pl.ds(sz.width, sz.width)], load_embed
        )
        embed_load.start()
        plane = [(o, c) for o in range(n_dp) for c in range(2) if (o, c) != (0, 0)]

        def member(o, c):
            return (ring.index(o), t, place.ctx if c == 0 else 1 - place.ctx)

        def columns_to(o, c):
            to = member(o, c)
            depth = joined_out.shape[2]
            first = pl.multiple_of((to[0] * sz.n_context + to[2]) * depth, depth)
            return pltpu.make_async_remote_copy(
                src_ref=joined_s.at[:, pl.ds(first, depth)],
                dst_ref=joined_out.at[place.dp * sz.n_context + place.ctx],
                send_sem=x_send.at[o, c],
                recv_sem=x_recv.at[o, c],
                device_id=to,
                device_id_type=MESH,
            )

        def columns_from(o, c):
            ref = joined_out.at[
                ring.index(-o) * sz.n_context + (place.ctx if c == 0 else 1 - place.ctx)
            ]
            return pltpu.make_async_remote_copy(
                src_ref=ref,
                dst_ref=ref,
                send_sem=x_send.at[o, c],
                recv_sem=x_recv.at[o, c],
                device_id=place.sibling(),
                device_id_type=MESH,
            )

        others = [member(o, c) for o, c in plane if o]
    place.enter(others)
    gather = Gather(place, rows_s, *gather_refs)
    scatter = Scatter(place, *scatter_refs)

    low = latent[...].astype(jnp.bfloat16)
    columns = sz.width // len(a_loads)
    square = None
    for n, group in enumerate(a_loads):
        for copy in group:
            copy.wait()
        cols = pl.ds(n * columns, columns)
        chunk = nn_dot(low, wa[:, cols]) + embed[:, cols]
        adapted[:, cols] = chunk
        here = jnp.sum(chunk * chunk, axis=-1, keepdims=True)
        square = here if square is None else square + here
    factor = lax.rsqrt(square / sz.width + norm_eps)
    for j in range(sz.seqs):
        span = slice(j * sz.block, (j + 1) * sz.block)
        normed = (adapted[span, :] * factor[span]) * gains[0:1, :]
        rows_s[gather.own(j), :] = normed.astype(jnp.bfloat16)
        gather.start(j)

    qkv_load.wait()
    pair = min(2, sz.heads)
    d = sz.head_dim

    def project(q, j):
        rows = place.tile(q, j)
        x = rows_s[rows, :]
        cos_here, sin_here = cos_t[rows, :], sin_t[rows, :]
        for h0 in range(0, sz.heads, pair):
            proj = nn_dot(x, wqkv[:, 3 * d * h0 : 3 * d * (h0 + pair)])
            for h in range(pair):
                at = 3 * d * h
                q_s[h0 + h, rows, :] = turn(proj[:, at : at + d], cos_here, sin_here).astype(
                    jnp.bfloat16
                )
                k_s[h0 + h, rows, :] = turn(
                    proj[:, at + d : at + 2 * d], cos_here, sin_here
                ).astype(jnp.bfloat16)
                v_s[h0 + h, rows, :] = proj[:, at + 2 * d : at + 3 * d].astype(jnp.bfloat16)

    def attend(q, j):
        rows = place.tile(q, j)
        first = (place.ahead(q) + j * sz.half) * sz.tile
        length = (j + 1) * sz.half * sz.tile
        start = begin[:, pl.ds(pl.multiple_of(first, sz.tile), sz.tile)]
        key_at = lax.broadcasted_iota(jnp.int32, (length, sz.tile), 0)
        query_at = first + lax.broadcasted_iota(jnp.int32, (1, sz.tile), 1)
        allowed = (key_at >= start) & (key_at <= query_at)

        def head(h, carry):
            scores = nt_dot(k_s[h, 0:length, :], q_s[h, rows, :])
            scores = jnp.where(allowed, scores * (LOG2E / math.sqrt(d)), masked_score)
            top = jnp.max(scores, axis=0, keepdims=True)
            weight = jnp.exp2(scores - top)
            total = jnp.sum(weight, axis=0, keepdims=True)
            mixed_t = tn_dot(v_s[h, 0:length, :], weight.astype(jnp.bfloat16))
            result = jnp.transpose(mixed_t / total)
            head_s[rows, pl.ds(pl.multiple_of(h * d, d), d)] = result.astype(jnp.bfloat16)
            if keep:
                lse_s[h, :, rows] = top + jnp.log2(total)
            return carry

        lax.fori_loop(0, sz.heads, head, 0)

    def give(q, j):
        rows = place.tile(q, j)
        scatter.part[...] = nn_dot(head_s[rows, :], wout[...])
        scatter.give(q, j)

    copies = []

    def save(src, dst):
        copy = pltpu.make_async_copy(src, dst, keep_sem.at[len(copies)])
        copy.start()
        copies.append(copy)

    if keep:
        save(adapted, adapted_out)
        joined_s[:, : sz.width] = low
        embed_load.wait()
        for o, c in plane:
            columns_to(o, c).start()
        mine = place.dp * sz.n_context + place.ctx
        depth = joined_out.shape[2]
        save(
            joined_s.at[:, pl.ds(pl.multiple_of(mine * depth, depth), depth)], joined_out.at[mine]
        )
    far = range(1, sz.half)
    for j in range(sz.seqs):
        gather.wait_near(j)
        project(0, j)
    for copy in out_loads:
        copy.wait()
    for j in range(sz.seqs):
        for q in far:
            gather.forward(q, j)
        for q in far:
            gather.wait_far(sz.half - q, j)
            project(q, j)
        for q in far:
            attend(q, j)
            give(q, j)
        attend(0, j)
        for q in far:
            scatter.onward(q, j)
        give(0, j)
    if keep:
        for src, dst in ((rows_s, rows_out), (q_s, q_out), (k_s, k_out), (v_s, v_out)):
            save(src, dst)
        save(head_s, head_out)
        save(lse_s, lse_out)
    gather.finish()
    for j in range(sz.seqs):
        span = slice(j * sz.block, (j + 1) * sz.block)
        mixed[span, :] = adapted[span, :] + scatter.total(j)
    scatter.finish()
    if keep:
        for o, c in plane:
            columns_from(o, c).wait_recv()
            columns_to(o, c).wait_send()
    for copy in copies:
        copy.wait()


def run_attn(
    sz, n_dp, keep, latent, embed_part, gains, cos_t, sin_t, begin, adapter, qkv, out, *embed
):
    f32, bf16 = jnp.float32, jnp.bfloat16
    heads_shape = (sz.heads, sz.seq_len, sz.head_dim)
    shape = jax.ShapeDtypeStruct
    outs = [shape((sz.rows, sz.width), f32)]
    if keep:
        outs += [
            shape((sz.rows, sz.width), f32),
            shape((sz.seq_len, sz.width), bf16),
            shape(heads_shape, bf16),
            shape(heads_shape, bf16),
            shape(heads_shape, bf16),
            shape((sz.seq_len, sz.heads * sz.head_dim), bf16),
            shape((sz.heads, 1, sz.seq_len), f32),
            shape((adapter.shape[0], sz.rows, 2 * sz.width // adapter.shape[0]), bf16),
        ]
    scratch = [
        pltpu.VMEM((sz.width, sz.width), bf16),
        pltpu.VMEM(qkv.shape, bf16),
        pltpu.VMEM((sz.heads * sz.head_dim, sz.width), bf16),
        pltpu.VMEM((sz.rows, sz.width), f32),
        pltpu.VMEM((sz.seq_len, sz.width), bf16),
        pltpu.VMEM(heads_shape, bf16),
        pltpu.VMEM(heads_shape, bf16),
        pltpu.VMEM(heads_shape, bf16),
        pltpu.VMEM((sz.seq_len, sz.heads * sz.head_dim), bf16),
        pltpu.VMEM((sz.heads, 1, sz.seq_len), f32),
        pltpu.SemaphoreType.DMA((4, adapter.shape[0] // 2)),
        pltpu.SemaphoreType.DMA,
        pltpu.SemaphoreType.DMA((out.shape[0],)),
        pltpu.SemaphoreType.DMA((8,)),
    ]
    scratch += Gather.scratch(sz) + Scatter.scratch(sz)
    if keep:
        scratch += [
            pltpu.VMEM((sz.rows, 2 * sz.width), bf16),
            pltpu.SemaphoreType.DMA,
            pltpu.SemaphoreType.DMA((n_dp, 2)),
            pltpu.SemaphoreType.DMA((n_dp, 2)),
        ]
    flops = 2 * sz.rows * sz.width * sz.width + 2 * sz.seq_len * sz.width * qkv.shape[1]
    return pl.pallas_call(
        partial(attn_kernel, sz, n_dp, keep),
        out_shape=outs,
        in_specs=[full_spec()] * 6 + [any_spec()] * (3 + len(embed)),
        out_specs=[full_spec()] + [any_spec()] * (len(outs) - 1),
        scratch_shapes=scratch,
        compiler_params=pltpu.CompilerParams(
            collective_id=2 if keep else 1, has_side_effects=True, vmem_limit_bytes=VMEM_BYTES
        ),
        cost_estimate=pl.CostEstimate(
            flops=flops, bytes_accessed=20 << 20, transcendentals=0
        ),
        name="attn_keep" if keep else "attn_round",
    )(latent, embed_part, gains, cos_t, sin_t, begin, adapter, qkv, out, *embed)


def ffn_kernel(sz, keep, *refs):
    (mixed, latent, active, gains, gate_hbm, up_hbm, down_hbm, result) = refs[:8]
    refs = refs[8:]
    if keep:
        rows_out, gate_out, up_out, hidden_out = refs[:4]
        refs = refs[4:]
    wg, wu, wd, rows_s = refs[:4]
    refs = refs[4:]
    if keep:
        gate_s, up_s, hidden_s = refs[:3]
        refs = refs[3:]
    load_gu, load_down, keep_sem = refs[:3]
    gather_refs = refs[3:5]
    scatter_refs = refs[5:]

    place = Place(sz)
    gate_load = pltpu.make_async_copy(gate_hbm, wg, load_gu.at[0])
    up_load = pltpu.make_async_copy(up_hbm, wu, load_gu.at[1])
    down_loads = column_loads(down_hbm, wd, load_down)
    gate_load.start()
    up_load.start()
    for copy in down_loads:
        copy.start()
    place.enter()
    gather = Gather(place, rows_s, *gather_refs)
    scatter = Scatter(place, *scatter_refs)
    for j in range(sz.seqs):
        span = slice(j * sz.block, (j + 1) * sz.block)
        rows = mixed[span, :]
        normed = (rows * rms_factor(rows)) * gains[1:2, :]
        rows_s[gather.own(j), :] = normed.astype(jnp.bfloat16)
        gather.start(j)
    gate_load.wait()
    up_load.wait()
    for copy in down_loads:
        copy.wait()

    copies = []

    def save(src, dst):
        copy = pltpu.make_async_copy(src, dst, keep_sem.at[len(copies)])
        copy.start()
        copies.append(copy)

    def work(q, j):
        rows = place.tile(q, j)
        x = rows_s[rows, :]
        gate = nn_dot(x, wg[...])
        up = nn_dot(x, wu[...])
        hidden = (gate / (1.0 + jnp.exp(-gate)) * up).astype(jnp.bfloat16)
        if keep:
            gate_s[rows, :] = gate.astype(jnp.bfloat16)
            up_s[rows, :] = up.astype(jnp.bfloat16)
            hidden_s[rows, :] = hidden
        scatter.part[...] = nn_dot(hidden, wd[...])
        scatter.give(q, j)

    far = range(1, sz.half)
    for j in range(sz.seqs):
        gather.wait_near(j)
        work(0, j)
    for j in range(sz.seqs):
        for q in far:
            gather.forward(q, j)
        for q in far:
            gather.wait_far(sz.half - q, j)
            work(q, j)
        for q in far:
            scatter.onward(q, j)
    if keep:
        save(rows_s, rows_out)
        save(gate_s, gate_out)
        save(up_s, up_out)
        save(hidden_s, hidden_out)
    gather.finish()
    for j in range(sz.seqs):
        span = slice(j * sz.block, (j + 1) * sz.block)
        total = mixed[span, :] + scatter.total(j)
        if not keep:
            total = jnp.where(active[...] > 0, total, latent[span, :])
        result[span, :] = total
    scatter.finish()
    for copy in copies:
        copy.wait()


def run_ffn(sz, keep, mixed, latent, active, gains, gate, up, down):
    f32, bf16 = jnp.float32, jnp.bfloat16
    shape = jax.ShapeDtypeStruct
    outs = [shape((sz.rows, sz.width), f32)]
    if keep:
        outs += [
            shape((sz.seq_len, sz.width), bf16),
            shape((sz.seq_len, sz.ff), bf16),
            shape((sz.seq_len, sz.ff), bf16),
            shape((sz.seq_len, sz.ff), bf16),
        ]
    scratch = [
        pltpu.VMEM(gate.shape, bf16),
        pltpu.VMEM(up.shape, bf16),
        pltpu.VMEM((sz.ff, sz.width), bf16),
        pltpu.VMEM((sz.seq_len, sz.width), bf16),
    ]
    if keep:
        scratch += [pltpu.VMEM((sz.seq_len, sz.ff), bf16)] * 3
    scratch += [
        pltpu.SemaphoreType.DMA((2,)),
        pltpu.SemaphoreType.DMA((down.shape[0],)),
        pltpu.SemaphoreType.DMA((4,)),
    ]
    scratch += Gather.scratch(sz) + Scatter.scratch(sz)
    return pl.pallas_call(
        partial(ffn_kernel, sz, keep),
        out_shape=outs,
        in_specs=[full_spec()] * 4 + [any_spec()] * 3,
        out_specs=[full_spec()] + [any_spec()] * (len(outs) - 1),
        scratch_shapes=scratch,
        compiler_params=pltpu.CompilerParams(
            collective_id=4 if keep else 3, has_side_effects=True, vmem_limit_bytes=VMEM_BYTES
        ),
        cost_estimate=pl.CostEstimate(
            flops=6 * sz.seq_len * sz.width * sz.ff, bytes_accessed=20 << 20, transcendentals=0
        ),
        name="ffn_keep" if keep else "ffn_round",
    )(mixed, latent, active, gains, gate, up, down)


def other_group(place):
    return (place.dp, (1 - place.group) * place.sz.half + place.part, place.ctx)


class Ring:
    def __init__(self, place, n_dp):
        self.place, self.count = place, n_dp
        self.at = self.swap(place.dp)

    def swap(self, i):
        if self.count != 4:
            return i
        x, y = lax.rem(i, 2), i // 2
        return 2 * y + x + y - 2 * x * y

    def index(self, offset):
        return self.swap(lax.rem(self.at + offset + 2 * self.count, self.count))

    def device(self, offset):
        return (self.index(offset), lax.axis_index("tensor"), self.place.ctx)


def weights_kernel(sz, n_dp, *refs):
    count = 5
    adapter_in, blocks_in = refs[0], refs[1 : 1 + count]
    rows_in, refs = refs[1 + count : 4 + count], refs[4 + count :]
    adapter_out, blocks_out = refs[0], refs[1 : 1 + count]
    embed_out, cot_out, cot_all, embed_part, state_out = refs[1 + count : 6 + count]
    refs = refs[6 + count :]
    (move_send, move_recv, ring_send, ring_recv, a_send, a_recv, x_send, x_recv, own_sem) = refs[:9]
    embed_s, state_s, weight_s, swap_send, swap_recv, keep_sem, weight_sem = refs[9:16]
    gather_refs = refs[16:]
    place = Place(sz)
    ring = Ring(place, n_dp)
    t = lax.axis_index("tensor")
    ctx, part, half, n_c = place.ctx, place.part, sz.half, sz.n_context
    role = part * n_c + ctx
    at_home = role == t
    steps = n_dp - 1
    sub = adapter_in.shape[0] // half
    ahead = 1 - 2 * ctx

    def holder(g):
        return (place.dp, g * half + t // n_c, lax.rem(t, n_c))

    barrier = pltpu.get_barrier_semaphore()

    def greet(device):
        pl.semaphore_signal(barrier, inc=1, device_id=device, device_id_type=MESH)

    greet(ring.device(1))
    greet(ring.device(n_dp - 1))
    greet(place.sibling())
    for q in range(1, half):
        greet(place.device(place.ahead(q), ctx))
    for c in range(n_c):
        pl.when(jnp.logical_not(at_home & (ctx == c)))(
            lambda c=c: greet((place.dp, role, c))
        )
    other = other_group(place)
    greet(other)
    waits = 3 + half + sz.seqs - jnp.where(at_home, 1, 0)
    pl.semaphore_wait(barrier, waits)

    own_at = pl.ds(pl.multiple_of(place.group * sz.block, sz.block), sz.block)
    other_at = pl.ds(pl.multiple_of((1 - place.group) * sz.block, sz.block), sz.block)
    rows_to = (embed_s, state_s, cot_out)

    def swap(i):
        return pltpu.make_async_remote_copy(
            src_ref=rows_in[i].at[1 - place.group],
            dst_ref=rows_to[i].at[own_at],
            send_sem=swap_send.at[i],
            recv_sem=swap_recv.at[i],
            device_id=other,
            device_id_type=MESH,
        )

    def swapped(i):
        ref = rows_to[i].at[other_at]
        return pltpu.make_async_remote_copy(
            src_ref=ref,
            dst_ref=ref,
            send_sem=swap_send.at[i],
            recv_sem=swap_recv.at[i],
            device_id=other,
            device_id_type=MESH,
        )

    def keep(i):
        return pltpu.make_async_copy(
            rows_in[i].at[place.group], rows_to[i].at[own_at], keep_sem.at[i]
        )

    for i in range(3):
        swap(i).start()
        keep(i).start()
    gather = Gather(place, cot_all, *gather_refs)

    def own_rows_of(j):
        return pltpu.make_async_copy(
            cot_out.at[pl.ds(j * sz.block, sz.block)], cot_all.at[gather.own(j)], keep_sem.at[3 + j]
        )

    def move(w, g):
        slot = place.dp * n_c + ctx
        return pltpu.make_async_remote_copy(
            src_ref=blocks_in[w],
            dst_ref=blocks_out[w].at[slot],
            send_sem=move_send.at[w, g],
            recv_sem=move_recv.at[w, ctx],
            device_id=holder(g),
            device_id_type=MESH,
        )

    def stay(w):
        return pltpu.make_async_copy(
            blocks_in[w], blocks_out[w].at[place.dp * n_c + ctx], own_sem.at[w]
        )

    def moved(w, c):
        slot = place.dp * n_c + c
        arrival = pltpu.make_async_remote_copy(
            src_ref=blocks_in[w],
            dst_ref=blocks_out[w].at[slot],
            send_sem=move_send.at[w, 0],
            recv_sem=move_recv.at[w, c],
            device_id=place.sibling(),
            device_id_type=MESH,
        )
        here = at_home & (ctx == c)
        pl.when(here)(lambda: stay(w).wait())
        pl.when(jnp.logical_not(here))(lambda: arrival.wait_recv())

    def adapter_rows(offset, c, p):
        return adapter_out.at[
            ring.index(offset) * n_c + c, pl.ds(pl.multiple_of(p * sub, sub), sub)
        ]

    own_rows = adapter_in.at[pl.ds(pl.multiple_of(part * sub, sub), sub)]

    def around(s):
        rows = adapter_rows(-ahead * s, ctx, part)
        return pltpu.make_async_remote_copy(
            src_ref=own_rows if s == 0 else rows,
            dst_ref=rows,
            send_sem=a_send.at[s],
            recv_sem=a_recv.at[s],
            device_id=ring.device(ahead),
            device_id_type=MESH,
        )

    def across(kind, s):
        offset = -ahead * s
        if kind < half:
            dst = adapter_rows(offset, ctx, part)
            src = own_rows if s == 0 else dst
        else:
            src = dst = adapter_rows(offset, ctx, place.behind(kind - half + 1))
        target = place.device(place.ahead(kind), ctx) if 0 < kind < half else place.sibling()
        return pltpu.make_async_remote_copy(
            src_ref=src,
            dst_ref=dst,
            send_sem=x_send.at[kind, s],
            recv_sem=x_recv.at[kind, s],
            device_id=target,
            device_id_type=MESH,
        )

    def crossed(kind, s):
        if kind == 0:
            rows = adapter_rows(ahead * s, 1 - ctx, part)
        elif kind < half:
            rows = adapter_rows(-ahead * s, ctx, place.behind(kind))
        else:
            rows = adapter_rows(ahead * s, 1 - ctx, place.behind(kind - half + 1))
        return pltpu.make_async_remote_copy(
            src_ref=rows,
            dst_ref=rows,
            send_sem=x_send.at[kind, s],
            recv_sem=x_recv.at[kind, s],
            device_id=place.sibling(),
            device_id_type=MESH,
        )

    def hop(w, way, s):
        offset = -s if way == 0 else s
        rows = blocks_out[w].at[ring.index(offset) * n_c + way]
        return pltpu.make_async_remote_copy(
            src_ref=rows,
            dst_ref=rows,
            send_sem=ring_send.at[w, way, s],
            recv_sem=ring_recv.at[w, way, s],
            device_id=ring.device(1 if way == 0 else n_dp - 1),
            device_id_type=MESH,
        )

    def hopped(w, way, s):
        offset = -(s + 1) if way == 0 else s + 1
        rows = blocks_out[w].at[ring.index(offset) * n_c + way]
        return pltpu.make_async_remote_copy(
            src_ref=rows,
            dst_ref=rows,
            send_sem=ring_send.at[w, way, s],
            recv_sem=ring_recv.at[w, way, s],
            device_id=ring.device(1),
            device_id_type=MESH,
        )

    around(0).start()
    own = pltpu.make_async_copy(own_rows, adapter_rows(0, ctx, part), own_sem.at[count])
    own.start()
    for w in range(count):
        for g in range(sz.seqs):
            here = at_home & (place.group == g)
            pl.when(jnp.logical_not(here))(lambda w=w, g=g: move(w, g).start())
        pl.when(at_home)(lambda w=w: stay(w).start())
    for kind in range(half):
        across(kind, 0).start()

    def adapter_step(s):
        if s < steps:
            arrival = pltpu.make_async_remote_copy(
                src_ref=own_rows,
                dst_ref=adapter_rows(-ahead * (s + 1), ctx, part),
                send_sem=a_send.at[s],
                recv_sem=a_recv.at[s],
                device_id=ring.device(1),
                device_id_type=MESH,
            )
            arrival.wait_recv()
            if s + 1 < steps:
                around(s + 1).start()
            for kind in range(half):
                across(kind, s + 1).start()

    def adapter_pass(s):
        for q in range(1, half):
            crossed(q, s).wait_recv()
            across(half - 1 + q, s).start()

    embed_save = pltpu.make_async_copy(embed_s, embed_out, keep_sem.at[3 + sz.seqs])
    todo = []
    for k in range(count + steps):
        for s in range(min(k, steps - 1), -1, -1):
            w = k - s
            if w < count:
                todo.append((w, s))
    done = 0
    for w, s in todo:
        for way in range(n_c):
            if s == 0:
                moved(w, way)
            else:
                hopped(w, way, s - 1).wait_recv()
            hop(w, way, s).start()
        if done < steps:
            adapter_step(done)
        if done == 5:
            for i in range(3):
                keep(i).wait()
                swapped(i).wait_recv()
            for j in range(sz.seqs):
                own_rows_of(j).start()
            embed_save.start()
            for j in range(sz.seqs):
                own_rows_of(j).wait()
                gather.start(j)
            state_out[...] = state_s[...].astype(jnp.float32)
        done += 1
    for s in range(done, steps):
        adapter_step(s)
    for s in range(n_dp):
        adapter_pass(s)
    for j in range(sz.seqs):
        gather.wait_near(j)
        for q in range(1, half):
            gather.forward(q, j)
    for s in range(n_dp):
        crossed(0, s).wait_recv()
        for q in range(1, half):
            crossed(half - 1 + q, s).wait_recv()
    own.wait()
    slots, depth = adapter_out.shape[0], weight_s.shape[1]
    loads = [
        pltpu.make_async_copy(
            adapter_out.at[slots // 2 + b, pl.ds(0, depth)], weight_s.at[b % 2], weight_sem.at[b % 2]
        )
        for b in range(slots // 2)
    ]
    loads[0].start()
    for b, copy in enumerate(loads):
        if b + 1 < len(loads):
            loads[b + 1].start()
        copy.wait()
        part_here = nn_dot(embed_s[:, b * depth : (b + 1) * depth], weight_s[b % 2])
        if b:
            embed_part[...] += part_here
        else:
            embed_part[...] = part_here
    for w in range(count):
        for way in range(n_c):
            hopped(w, way, steps - 1).wait_recv()
    for j in range(sz.seqs):
        for q in range(1, half):
            gather.wait_far(q, j)
    gather.finish()
    embed_save.wait()
    for i in range(3):
        swap(i).wait_send()
    for w in range(count):
        for g in range(sz.seqs):
            here = at_home & (place.group == g)
            pl.when(jnp.logical_not(here))(lambda w=w, g=g: move(w, g).wait_send())
        for way in range(n_c):
            for s in range(steps):
                hop(w, way, s).wait_send()
    for s in range(steps):
        around(s).wait_send()
    for s in range(n_dp):
        for kind in range(2 * half - 1):
            across(kind, s).wait_send()


def run_weights(sz, n_dp, adapter, adapter_block, blocks, rows):
    bf16, f32 = jnp.bfloat16, jnp.float32
    slots = n_dp * sz.n_context
    outs = [jax.ShapeDtypeStruct((slots,) + a.shape, bf16) for a in [adapter] + blocks]
    outs += [
        jax.ShapeDtypeStruct((sz.rows, sz.width), bf16),
        jax.ShapeDtypeStruct((sz.rows, sz.width), bf16),
        jax.ShapeDtypeStruct((sz.seq_len, sz.width), bf16),
        jax.ShapeDtypeStruct((sz.rows, sz.width), f32),
        jax.ShapeDtypeStruct((sz.rows, sz.width), f32),
    ]
    count, steps, dma = len(blocks), n_dp - 1, pltpu.SemaphoreType.DMA
    kinds = 2 * sz.half - 1
    return pl.pallas_call(
        partial(weights_kernel, sz, n_dp),
        out_shape=outs,
        in_specs=[any_spec()] * (4 + count),
        out_specs=[any_spec()] * (4 + count) + [full_spec()] * 2,
        scratch_shapes=[
            dma((count, sz.seqs)),
            dma((count, sz.n_context)),
            dma((count, sz.n_context, steps)),
            dma((count, sz.n_context, steps)),
            dma((steps,)),
            dma((steps,)),
            dma((kinds, n_dp)),
            dma((kinds, n_dp)),
            dma((count + 1,)),
            pltpu.VMEM((sz.rows, sz.width), bf16),
            pltpu.VMEM((sz.rows, sz.width), bf16),
            pltpu.VMEM((2, adapter_block, sz.width), bf16),
            dma((3,)),
            dma((3,)),
            dma((4 + sz.seqs,)),
            dma((2,)),
        ]
        + Gather.scratch(sz),
        compiler_params=pltpu.CompilerParams(
            collective_id=5, has_side_effects=True, vmem_limit_bytes=VMEM_BYTES
        ),
        name="weights",
    )(adapter, *blocks, *rows)


def norm_back(grad, rows, factor, gain):
    unit = rows * factor
    weighted = grad * gain
    inner = jnp.mean(weighted * unit, axis=-1, keepdims=True)
    return factor * (weighted - unit * inner), jnp.sum(grad * unit, axis=0, keepdims=True)


class GradRing:
    @staticmethod
    def scratch(sz, n_dp, wide):
        slots, ways, steps, dma = n_dp * sz.n_context, sz.n_context, n_dp - 1, pltpu.SemaphoreType.DMA
        depth, bf16, count = sz.width // slots, jnp.bfloat16, len(wide)
        return (
            [pltpu.VMEM((sz.seq_len, n), bf16) for n in wide]
            + [pltpu.VMEM((ways, depth, n), bf16) for n in wide]
            + [pltpu.VMEM((ways, steps, depth, n), bf16) for n in wide]
            + [
                pltpu.VMEM((2, ways, sz.seq_len, depth), bf16),
                dma((count,)),
                dma((2, ways)),
                dma((count, ways, steps)),
                dma((count, ways, steps)),
            ]
        )

    def __init__(self, sz, place, ring, xs, ys, refs):
        count = len(xs)
        self.sz, self.place, self.ring, self.xs, self.count = sz, place, ring, xs, count
        self.ys, self.first, self.held = (refs[i * count : (i + 1) * count] for i in range(3))
        self.x_s, self.load_y, self.load_x, self.send, self.recv = refs[3 * count :]
        self.y_loads = [
            pltpu.make_async_copy(ys[w], self.ys[w], self.load_y.at[w]) for w in range(count)
        ]
        self.tasks = [
            (k - s, s)
            for k in range(count + ring.count)
            for s in range(min(k, ring.count - 1), -1, -1)
            if k - s < count
        ]
        self.done, self.seen = 0, set()

    def start(self):
        for copy in self.y_loads:
            copy.start()
        for way in range(self.sz.n_context):
            self.x_load(0, way).start()

    def slot(self, way, s):
        return self.ring.index(-(s + 1) if way == 0 else s + 1) * self.sz.n_context + way

    def x_load(self, k, way):
        w, s = self.tasks[k]
        depth = self.x_s.shape[3]
        if self.xs[w].shape[0] == 1:
            at = pl.multiple_of(self.slot(way, s) * depth, depth)
            src = self.xs[w].at[0, :, pl.ds(at, depth)]
        else:
            src = self.xs[w].at[self.slot(way, s)]
        return pltpu.make_async_copy(src, self.x_s.at[k % 2, way], self.load_x.at[k % 2, way])

    def source(self, w, way, s):
        return self.first[w].at[way] if s == 0 else self.held[w].at[way, s - 1]

    def hop(self, w, way, s):
        return pltpu.make_async_remote_copy(
            src_ref=self.source(w, way, s),
            dst_ref=self.held[w].at[way, s],
            send_sem=self.send.at[w, way, s],
            recv_sem=self.recv.at[w, way, s],
            device_id=self.ring.device(1 if way == 0 else self.ring.count - 1),
            device_id_type=MESH,
        )

    def result(self, w, way):
        return self.source(w, way, self.ring.count - 1)

    def step(self):
        k = self.done
        self.done += 1
        w, s = self.tasks[k]
        ways = range(self.sz.n_context)
        if k + 1 < len(self.tasks):
            for way in ways:
                self.x_load(k + 1, way).start()
        if w not in self.seen:
            self.y_loads[w].wait()
            self.seen.add(w)
        for way in ways:
            self.x_load(k, way).wait()
            value = tn_dot(self.x_s[k % 2, way], self.ys[w][...])
            if s:
                self.hop(w, way, s - 1).wait_recv()
                value = value + self.held[w][way, s - 1].astype(jnp.float32)
            ref = self.source(w, way, s)
            ref[...] = value.astype(jnp.bfloat16)
            if s < self.ring.count - 1:
                self.hop(w, way, s).start()
        return w, s == self.ring.count - 1

    def left(self):
        return len(self.tasks) - self.done

    def finish(self):
        for w in range(self.count):
            for way in range(self.sz.n_context):
                for s in range(self.ring.count - 1):
                    self.hop(w, way, s).wait_send()


class Deliver:
    @staticmethod
    def scratch(sz, n_dp, wide):
        depth, count, dma = sz.width // (n_dp * sz.n_context), len(wide), pltpu.SemaphoreType.DMA
        return [pltpu.VMEM((sz.seqs, depth, n), jnp.bfloat16) for n in wide] + [
            dma((count, sz.n_context)),
            dma((count, sz.seqs)),
            dma((count,)),
        ]

    def __init__(self, sz, place, refs):
        self.sz, self.place = sz, place
        self.landed = refs[:-3]
        self.send, self.recv, self.own = refs[-3:]
        self.count = len(self.landed)
        self.t = lax.axis_index("tensor")
        self.role = place.part * sz.n_context + place.ctx
        self.at_home = self.role == self.t
        self.sources = [None] * self.count

    def greet(self):
        sz, place = self.sz, self.place
        barrier = pltpu.get_barrier_semaphore()
        for g in range(sz.seqs):
            holder = (place.dp, g * sz.half + self.t // sz.n_context, lax.rem(self.t, sz.n_context))
            pl.when(jnp.logical_not(self.at_home & (place.group == g)))(
                lambda holder=holder: pl.semaphore_signal(
                    barrier, inc=1, device_id=holder, device_id_type=MESH
                )
            )
        return sz.n_context - jnp.where(self.at_home, 1, 0)

    def remote(self, w, way):
        return pltpu.make_async_remote_copy(
            src_ref=self.sources[w][way],
            dst_ref=self.landed[w].at[self.place.group],
            send_sem=self.send.at[w, way],
            recv_sem=self.recv.at[w, self.place.group],
            device_id=(self.place.dp, self.role, way),
            device_id_type=MESH,
        )

    def local(self, w, way):
        return pltpu.make_async_copy(
            self.sources[w][way], self.landed[w].at[self.place.group], self.own.at[w]
        )

    def start(self, w, sources):
        self.sources[w] = sources
        for way in range(self.sz.n_context):
            here = self.at_home & (self.place.ctx == way)
            pl.when(here)(lambda way=way: self.local(w, way).start())
            pl.when(jnp.logical_not(here))(lambda way=way: self.remote(w, way).start())

    def total(self, w):
        place = self.place
        for g in range(self.sz.seqs):
            ref = self.landed[w].at[g]
            arrival = pltpu.make_async_remote_copy(
                src_ref=ref,
                dst_ref=ref,
                send_sem=self.send.at[w, 0],
                recv_sem=self.recv.at[w, g],
                device_id=(place.dp, self.t, 1 - place.ctx),
                device_id_type=MESH,
            )
            here = self.at_home & (place.group == g)
            pl.when(here)(lambda: self.local(w, 0).wait())
            pl.when(jnp.logical_not(here))(lambda arrival=arrival: arrival.wait_recv())
        total = self.landed[w][0].astype(jnp.float32)
        for g in range(1, self.sz.seqs):
            total = total + self.landed[w][g].astype(jnp.float32)
        return total

    def finish(self):
        for w in range(self.count):
            for way in range(self.sz.n_context):
                here = self.at_home & (self.place.ctx == way)
                pl.when(jnp.logical_not(here))(lambda w=w, way=way: self.remote(w, way).wait_send())


def slot_columns(sz, n_dp, x):
    slots = n_dp * sz.n_context
    depth = sz.width // slots
    if depth % 128:
        return x.reshape(sz.seq_len, slots, depth).transpose(1, 0, 2)
    return x[None]


def ffn_back_kernel(sz, n_dp, *refs):
    (cot, mixed, gains, state) = refs[:4]
    (rows_hbm, gate_hbm, up_hbm, wg_hbm, wu_hbm, down_hbm, x_hbm, hidden_hbm) = refs[4:12]
    (grad_mixed, gain_grad, state_out, dgate_out, dup_out, down_sum) = refs[12:18]
    (rows_s, gate_s, up_s, wg, wu, wd, load, load_down, keep_sem) = refs[18:27]
    (swap_out, swap_in, swap_sem) = refs[27:30]
    scatter_refs, ring_refs = refs[30:38], refs[38:]
    place = Place(sz)
    ring = Ring(place, n_dp)
    grads = GradRing(sz, place, ring, [x_hbm], [hidden_hbm], ring_refs)
    grads.start()
    pairs = ((rows_hbm, rows_s), (gate_hbm, gate_s), (up_hbm, up_s), (wg_hbm, wg), (wu_hbm, wu))
    loads = [
        pltpu.make_async_copy(src, dst, load.at[i]) for i, (src, dst) in enumerate(pairs)
    ]
    down_loads = column_loads(down_hbm, wd, load_down)
    loads[0].start()
    for copy in down_loads + loads[1:]:
        copy.start()
    other = (place.dp, (1 - place.group) * sz.half + place.part, place.ctx)
    place.enter([ring.device(1), ring.device(n_dp - 1), other])
    scatter = Scatter(place, *scatter_refs)
    grads.step()
    for copy in [loads[0]] + down_loads + loads[1:]:
        copy.wait()
    give_rows = pl.ds(pl.multiple_of((1 - place.group) * sz.block, sz.block), sz.block)
    keep_rows = pl.ds(pl.multiple_of(place.group * sz.block, sz.block), sz.block)
    swap = pltpu.make_async_remote_copy(
        src_ref=swap_out,
        dst_ref=swap_in,
        send_sem=swap_sem.at[0],
        recv_sem=swap_sem.at[1],
        device_id=other,
        device_id_type=MESH,
    )
    swap_out[...] = state[give_rows, :].astype(jnp.bfloat16)
    state_out[place.group] = state[keep_rows, :]

    def work(q, j):
        rows = place.tile(q, j)
        dh = nt_dot(rows_s[rows, :], wd[...])
        gate = gate_s[rows, :].astype(jnp.float32)
        up = up_s[rows, :].astype(jnp.float32)
        sig = 1.0 / (1.0 + jnp.exp(-gate))
        dgate = (dh * up * sig * (1.0 + gate * (1.0 - sig))).astype(jnp.bfloat16)
        dup = (dh * gate * sig).astype(jnp.bfloat16)
        gate_s[rows, :] = dgate
        up_s[rows, :] = dup
        scatter.part[...] = nt_dot(dgate, wg[...]) + nt_dot(dup, wu[...])
        scatter.give(q, j)

    far = range(1, sz.half)
    for j in range(sz.seqs):
        for q in far:
            work(q, j)
        if j:
            for q in far:
                scatter.onward(q, j - 1)
    work(0, 0)
    for q in far:
        scatter.onward(q, sz.seqs - 1)
    swap.start()
    grads.step()
    for j in range(1, sz.seqs):
        work(0, j)
    copies = [
        pltpu.make_async_copy(gate_s, dgate_out, keep_sem.at[0]),
        pltpu.make_async_copy(up_s, dup_out, keep_sem.at[1]),
    ]
    for copy in copies:
        copy.start()
    gain_total = None
    for j in range(sz.seqs):
        span = slice(j * sz.block, (j + 1) * sz.block)
        rows = mixed[span, :]
        grad, gain_here = norm_back(scatter.total(j), rows, rms_factor(rows), gains[1:2, :])
        grad_mixed[span, :] = cot[span, :].astype(jnp.float32) + grad
        gain_total = gain_here if gain_total is None else gain_total + gain_here
    gain_grad[...] = gain_total
    while grads.left() > 1:
        grads.step()
    swap.wait()
    state_out[1 - place.group] = swap_in[...].astype(jnp.float32)
    grads.step()
    for way in range(sz.n_context):
        copies.append(
            pltpu.make_async_copy(grads.result(0, way), down_sum.at[way], keep_sem.at[2 + way])
        )
        copies[-1].start()
    scatter.finish()
    grads.finish()
    for copy in copies:
        copy.wait()


def run_ffn_back(sz, n_dp, cot, mixed, gains, state, rows, gate, up, wg, wu, down, hidden):
    f32, bf16, shape = jnp.float32, jnp.bfloat16, jax.ShapeDtypeStruct
    dma = pltpu.SemaphoreType.DMA
    depth = sz.width // (n_dp * sz.n_context)
    return pl.pallas_call(
        partial(ffn_back_kernel, sz, n_dp),
        out_shape=[
            shape((sz.rows, sz.width), f32),
            shape((1, sz.width), f32),
            shape((sz.seqs, sz.block, sz.width), f32),
            shape((sz.seq_len, sz.ff), bf16),
            shape((sz.seq_len, sz.ff), bf16),
            shape((sz.n_context, depth, sz.ff), bf16),
        ],
        in_specs=[full_spec()] * 4 + [any_spec()] * 8,
        out_specs=[full_spec()] * 3 + [any_spec()] * 3,
        scratch_shapes=[
            pltpu.VMEM((sz.seq_len, sz.width), bf16),
            pltpu.VMEM((sz.seq_len, sz.ff), bf16),
            pltpu.VMEM((sz.seq_len, sz.ff), bf16),
            pltpu.VMEM(wg.shape, bf16),
            pltpu.VMEM(wu.shape, bf16),
            pltpu.VMEM((sz.ff, sz.width), bf16),
            dma((5,)),
            dma((down.shape[0],)),
            dma((2 + sz.n_context,)),
            pltpu.VMEM((sz.block, sz.width), bf16),
            pltpu.VMEM((sz.block, sz.width), bf16),
            dma((2,)),
        ]
        + Scatter.scratch(sz)
        + GradRing.scratch(sz, n_dp, [sz.ff]),
        compiler_params=pltpu.CompilerParams(
            collective_id=6, has_side_effects=True, vmem_limit_bytes=VMEM_BYTES
        ),
        cost_estimate=pl.CostEstimate(
            flops=8 * sz.seq_len * sz.width * sz.ff, bytes_accessed=40 << 20, transcendentals=0
        ),
        name="ffn_back",
    )(cot, mixed, gains, state, rows, gate, up, wg, wu, down, slot_columns(sz, n_dp, rows), hidden)


def attn_back_kernel(sz, n_dp, *refs):
    (grad_mixed, adapted, gains, cos_t, sin_t, begin, gain_b) = refs[:7]
    (q_hbm, k_hbm, v_hbm, lse_hbm, out_hbm, qkv_hbm, x_hbm, dgate_hbm, down_sum) = refs[7:16]
    (grad_low, down_grad, rows_out, proj_out, gate_sum) = refs[16:21]
    (rows_s, q_s, k_s, v_s, lse_s, do_s, dk_s, dv_s, proj_s, wout, wqkv) = refs[21:32]
    (load, load_out, keep_sem) = refs[32:35]
    gather_refs, scatter_refs = refs[35:37], refs[37:45]
    ring_refs, deliver_refs = refs[45:53], refs[53:]
    place = Place(sz)
    ring = Ring(place, n_dp)
    grads = GradRing(sz, place, ring, [x_hbm], [dgate_hbm], ring_refs)
    deliver = Deliver(sz, place, deliver_refs)
    grads.start()
    pairs = ((q_hbm, q_s), (k_hbm, k_s), (v_hbm, v_s), (lse_hbm, lse_s), (qkv_hbm, wqkv))
    loads = [
        pltpu.make_async_copy(src, dst, load.at[i]) for i, (src, dst) in enumerate(pairs)
    ]
    out_loads = column_loads(out_hbm, wout, load_out)
    for copy in out_loads + loads:
        copy.start()
    targets = deliver.greet()
    place.enter([ring.device(1), ring.device(n_dp - 1)], targets)
    gather = Gather(place, rows_s, *gather_refs)
    scatter = Scatter(place, *scatter_refs)
    for j in range(sz.seqs):
        span = slice(j * sz.block, (j + 1) * sz.block)
        rows_s[gather.own(j), :] = grad_mixed[span, :].astype(jnp.bfloat16)
        gather.start(j)
    grads.step()
    deliver.start(0, [down_sum.at[way] for way in range(sz.n_context)])
    for copy in out_loads:
        copy.wait()
    d = sz.head_dim

    def heads_grad(q, j):
        rows = place.tile(q, j)
        dhead = nt_dot(rows_s[rows, :], wout[...]).astype(jnp.bfloat16)
        for h in range(sz.heads):
            do_s[h, rows, :] = dhead[:, h * d : (h + 1) * d]

    far = range(1, sz.half)
    for j in range(sz.seqs):
        gather.wait_near(j)
        heads_grad(0, j)
    for copy in loads:
        copy.wait()
    for j in range(sz.seqs):
        for q in far:
            gather.forward(q, j)
        for q in far:
            gather.wait_far(sz.half - q, j)
            heads_grad(q, j)
    copies = [pltpu.make_async_copy(rows_s, rows_out, keep_sem.at[0])]
    copies[0].start()
    grads.step()

    tiles = sz.n_tensor
    scale = 1.0 / math.sqrt(d)

    def head(h, carry):
        for i in reversed(range(tiles)):
            rows = slice(i * sz.tile, (i + 1) * sz.tile)
            length = (i + 1) * sz.tile
            keys, values = k_s[h, 0:length, :], v_s[h, 0:length, :]
            query, grad = q_s[h, rows, :], do_s[h, rows, :]
            start = begin[:, rows]
            key_at = lax.broadcasted_iota(jnp.int32, (length, sz.tile), 0)
            query_at = i * sz.tile + lax.broadcasted_iota(jnp.int32, (1, sz.tile), 1)
            allowed = (key_at >= start) & (key_at <= query_at)
            scores = nt_dot(keys, query)
            scores = jnp.where(allowed, scores * (LOG2E * scale), masked_score)
            probs = jnp.exp2(scores - lse_s[h, :, rows])
            dprobs = nt_dot(values, grad)
            inner = jnp.sum(probs * dprobs, axis=0, keepdims=True)
            dscores = (probs * (dprobs - inner)).astype(jnp.bfloat16)
            dv = nn_dot(probs.astype(jnp.bfloat16), grad)
            dk = nn_dot(dscores, query)
            if i == tiles - 1:
                dv_s[...] = dv
                dk_s[...] = dk
            else:
                dv_s[0:length, :] += dv
                dk_s[0:length, :] += dk
            dq = jnp.transpose(tn_dot(keys, dscores)) * scale
            cos_here, sin_here = cos_t[rows, :], sin_t[rows, :]
            proj_s[rows, pl.ds(pl.multiple_of(h * 3 * d, d), d)] = turn(
                dq, cos_here, -sin_here
            ).astype(jnp.bfloat16)
        dk = turn(dk_s[...] * scale, cos_t[...], -sin_t[...])
        proj_s[:, pl.ds(pl.multiple_of(h * 3 * d + d, d), d)] = dk.astype(jnp.bfloat16)
        proj_s[:, pl.ds(pl.multiple_of(h * 3 * d + 2 * d, d), d)] = dv_s[...].astype(jnp.bfloat16)
        return carry

    lax.fori_loop(0, sz.heads // 2, head, 0)
    grads.step()
    lax.fori_loop(sz.heads // 2, sz.heads, head, 0)
    copies.append(pltpu.make_async_copy(proj_s, proj_out, keep_sem.at[1]))
    copies[1].start()

    def give(q, j):
        scatter.part[...] = nt_dot(proj_s[place.tile(q, j), :], wqkv[...])
        scatter.give(q, j)

    for j in range(sz.seqs):
        for q in far:
            give(q, j)
        if j:
            for q in far:
                scatter.onward(q, j - 1)
    give(0, 0)
    for q in far:
        scatter.onward(q, sz.seqs - 1)
    for j in range(1, sz.seqs):
        give(0, j)
    gather.finish()
    down_grad[...] = deliver.total(0)
    while grads.left():
        grads.step()
    for way in range(sz.n_context):
        copies.append(
            pltpu.make_async_copy(grads.result(0, way), gate_sum.at[way], keep_sem.at[2 + way])
        )
        copies[-1].start()
    gain_total = None
    for j in range(sz.seqs):
        span = slice(j * sz.block, (j + 1) * sz.block)
        rows = adapted[span, :]
        grad, gain_here = norm_back(scatter.total(j), rows, rms_factor(rows), gains[0:1, :])
        grad_low[span, :] = (grad_mixed[span, :] + grad).astype(jnp.bfloat16)
        gain_total = gain_here if gain_total is None else gain_total + gain_here
    extra = grad_low.shape[0] - sz.rows
    at_row = lax.broadcasted_iota(jnp.int32, (extra, sz.width), 0)
    shares = jnp.where(at_row == 0, gain_total, jnp.where(at_row == 1, gain_b[...], 0.0))
    grad_low[sz.rows :, :] = shares.astype(jnp.bfloat16)
    scatter.finish()
    grads.finish()
    deliver.finish()
    for copy in copies:
        copy.wait()


def run_attn_back(
    sz, n_dp, grad_mixed, adapted, gains, cos_t, sin_t, begin, gain_b, q, k, v, lse, out, qkv,
    x, dgate, down_sum,
):
    f32, bf16, shape = jnp.float32, jnp.bfloat16, jax.ShapeDtypeStruct
    dma = pltpu.SemaphoreType.DMA
    heads_shape = (sz.heads, sz.seq_len, sz.head_dim)
    return pl.pallas_call(
        partial(attn_back_kernel, sz, n_dp),
        out_shape=[
            shape((sz.rows + 16, sz.width), bf16),
            shape(down_sum.shape[1:], f32),
            shape((sz.seq_len, sz.width), bf16),
            shape((sz.seq_len, qkv.shape[1]), bf16),
            shape(down_sum.shape, bf16),
        ],
        in_specs=[full_spec()] * 7 + [any_spec()] * 9,
        out_specs=[full_spec()] * 2 + [any_spec()] * 3,
        scratch_shapes=[
            pltpu.VMEM((sz.seq_len, sz.width), bf16),
            pltpu.VMEM(heads_shape, bf16),
            pltpu.VMEM(heads_shape, bf16),
            pltpu.VMEM(heads_shape, bf16),
            pltpu.VMEM((sz.heads, 1, sz.seq_len), f32),
            pltpu.VMEM(heads_shape, bf16),
            pltpu.VMEM((sz.seq_len, sz.head_dim), f32),
            pltpu.VMEM((sz.seq_len, sz.head_dim), f32),
            pltpu.VMEM((sz.seq_len, qkv.shape[1]), bf16),
            pltpu.VMEM((sz.heads * sz.head_dim, sz.width), bf16),
            pltpu.VMEM(qkv.shape, bf16),
            dma((5,)),
            dma((out.shape[0],)),
            dma((2 + sz.n_context,)),
        ]
        + Gather.scratch(sz)
        + Scatter.scratch(sz)
        + GradRing.scratch(sz, n_dp, [sz.ff])
        + Deliver.scratch(sz, n_dp, [sz.ff]),
        compiler_params=pltpu.CompilerParams(
            collective_id=7, has_side_effects=True, vmem_limit_bytes=VMEM_BYTES
        ),
        cost_estimate=pl.CostEstimate(
            flops=4 * sz.seq_len * sz.width * qkv.shape[1], bytes_accessed=30 << 20, transcendentals=0
        ),
        name="attn_back",
    )(
        grad_mixed, adapted, gains, cos_t, sin_t, begin, gain_b, q, k, v, lse, out, qkv,
        slot_columns(sz, n_dp, x), dgate, down_sum,
    )


class PlaneRows:
    @staticmethod
    def scratch(n_dp):
        dma = pltpu.SemaphoreType.DMA
        return [dma((n_dp - 1,)), dma((n_dp - 1,)), dma((n_dp,)), dma((n_dp,))]

    def __init__(self, place, ring, own, landed, refs):
        self.place, self.ring, self.own, self.landed = place, ring, own, landed
        self.send, self.recv, self.near_send, self.near_recv = refs
        self.ahead = 1 - 2 * place.ctx

    def slot(self, offset, ctx):
        return self.landed.at[self.ring.index(offset) * self.place.sz.n_context + ctx]

    def source(self, s):
        return self.own if s == 0 else self.slot(-self.ahead * s, self.place.ctx)

    def hop(self, s):
        return pltpu.make_async_remote_copy(
            src_ref=self.source(s),
            dst_ref=self.slot(-self.ahead * s, self.place.ctx),
            send_sem=self.send.at[s],
            recv_sem=self.recv.at[s],
            device_id=self.ring.device(self.ahead),
            device_id_type=MESH,
        )

    def near(self, s):
        return pltpu.make_async_remote_copy(
            src_ref=self.source(s),
            dst_ref=self.slot(-self.ahead * s, self.place.ctx),
            send_sem=self.near_send.at[s],
            recv_sem=self.near_recv.at[s],
            device_id=self.place.sibling(),
            device_id_type=MESH,
        )

    def start(self):
        self.hop(0).start()
        self.near(0).start()

    def step(self, s):
        ref = self.slot(-self.ahead * (s + 1), self.place.ctx)
        pltpu.make_async_remote_copy(
            src_ref=ref,
            dst_ref=ref,
            send_sem=self.send.at[s],
            recv_sem=self.recv.at[s],
            device_id=self.place.sibling(),
            device_id_type=MESH,
        ).wait_recv()
        if s + 1 < self.ring.count - 1:
            self.hop(s + 1).start()
        self.near(s + 1).start()

    def wait_near(self, s):
        ref = self.slot(self.ahead * s, 1 - self.place.ctx)
        pltpu.make_async_remote_copy(
            src_ref=ref,
            dst_ref=ref,
            send_sem=self.near_send.at[s],
            recv_sem=self.near_recv.at[s],
            device_id=self.place.sibling(),
            device_id_type=MESH,
        ).wait_recv()

    def finish(self):
        for s in range(self.ring.count):
            if s < self.ring.count - 1:
                self.hop(s).wait_send()
            self.near(s).wait_send()


class LineSum:
    @staticmethod
    def scratch(sz, parts, chunk):
        dma, bf16 = pltpu.SemaphoreType.DMA, jnp.bfloat16
        far = pltpu.VMEM((max(sz.half - 1, 1), parts, chunk, sz.width), bf16)
        one = pltpu.VMEM((parts, chunk, sz.width), bf16)
        kinds = 2 * sz.half - 1
        return [far, far, one, one, one, far, dma((kinds, parts)), dma((kinds, parts))]

    def __init__(self, place, total, parts, refs):
        self.place, self.total, self.parts = place, total, parts
        (self.out, self.got, self.sum, self.cross, self.done, self.back, self.send, self.recv) = refs
        self.chunk = self.sum.shape[1]

    def rows(self, part, k):
        first = (part * self.parts + k) * self.chunk
        return pl.ds(pl.multiple_of(first, self.chunk), self.chunk)

    def copy(self, src, dst, kind, k, device):
        return pltpu.make_async_remote_copy(
            src_ref=src,
            dst_ref=dst,
            send_sem=self.send.at[kind, k],
            recv_sem=self.recv.at[kind, k],
            device_id=device,
            device_id_type=MESH,
        )

    def spread(self, q, k):
        place = self.place
        device = place.device(place.ahead(q), place.ctx)
        return self.copy(self.out.at[q - 1, k], self.got.at[q - 1, k], q, k, device)

    def swap(self, k):
        return self.copy(self.sum.at[k], self.cross.at[k], 0, k, other_group(self.place))

    def collect(self, q, k):
        place = self.place
        device = place.device(place.ahead(q), place.ctx)
        return self.copy(
            self.done.at[k], self.back.at[q - 1, k], place.sz.half - 1 + q, k, device
        )

    def start(self, k):
        for q in range(1, self.place.sz.half):
            rows = self.rows(self.place.ahead(q), k)
            self.out[q - 1, k] = self.total[rows, :].astype(jnp.bfloat16)
            self.spread(q, k).start()

    def cross_over(self, k):
        value = self.total[self.rows(self.place.part, k), :]
        for q in range(1, self.place.sz.half):
            self.spread(q, k).wait_recv()
            value = value + self.got[q - 1, k].astype(jnp.float32)
        self.sum[k] = value.astype(jnp.bfloat16)
        self.swap(k).start()

    def share(self, k):
        self.swap(k).wait_recv()
        value = self.sum[k].astype(jnp.float32) + self.cross[k].astype(jnp.float32)
        self.done[k] = value.astype(jnp.bfloat16)
        for q in range(1, self.place.sz.half):
            self.collect(q, k).start()
        self.total[self.rows(self.place.part, k), :] = self.done[k].astype(jnp.float32)

    def complete(self, k):
        for q in range(1, self.place.sz.half):
            self.collect(q, k).wait_recv()
            rows = self.rows(self.place.behind(q), k)
            self.total[rows, :] = self.back[q - 1, k].astype(jnp.float32)

    def finish(self):
        for k in range(self.parts):
            self.swap(k).wait_send()
            for q in range(1, self.place.sz.half):
                self.spread(q, k).wait_send()
                self.collect(q, k).wait_send()


SUM_PARTS = 2


def grads_kernel(sz, n_dp, count, *refs):
    n_in = 4 + 2 * count
    gate_sum, low, joined, adapter = refs[:4]
    xs, ys = refs[4 : 4 + count], refs[4 + count : n_in]
    outs = refs[n_in : n_in + 1 + count]
    embed_grad, adapter_out, gains_out, landed = refs[n_in + 1 + count : n_in + 5 + count]
    refs = refs[n_in + 5 + count :]

    def take(n):
        nonlocal refs
        head, refs = refs[:n], refs[n:]
        return head

    ring_refs, deliver_refs = take(3 * count + 5), take(count + 4)
    plane_refs, sum_refs = take(4), take(8)
    adapter_grad, d_s, j_s, weight_s, rows_s, swap_in = refs[:6]
    d_sem, j_sem, weight_sem, swap_sem, out_sem = refs[6:]
    place = Place(sz)
    ring = Ring(place, n_dp)
    grads = GradRing(sz, place, ring, xs, ys, ring_refs)
    deliver = Deliver(sz, place, deliver_refs)
    plane = PlaneRows(place, ring, low, landed, plane_refs)
    line = LineSum(place, adapter_grad, SUM_PARTS, sum_refs)
    other = other_group(place)
    grads.start()
    weight_load = [
        pltpu.make_async_copy(
            adapter.at[adapter.shape[0] // 2 + b, pl.ds(0, weight_s.shape[0])], weight_s, weight_sem
        )
        for b in range(adapter.shape[0] // 2)
    ]
    weight_load[0].start()
    place.enter([ring.device(1), ring.device(n_dp - 1), other], deliver.greet())
    plane.start()
    give_rows = pl.ds(pl.multiple_of((1 - place.group) * sz.block, sz.block), sz.block)
    keep_rows = pl.ds(pl.multiple_of(place.group * sz.block, sz.block), sz.block)
    swap = pltpu.make_async_remote_copy(
        src_ref=low.at[give_rows],
        dst_ref=swap_in,
        send_sem=swap_sem.at[0],
        recv_sem=swap_sem.at[1],
        device_id=other,
        device_id_type=MESH,
    )
    swap.start()
    deliver.start(0, [gate_sum.at[way] for way in range(sz.n_context)])

    def ring_step():
        if grads.left():
            w, complete = grads.step()
            if complete:
                deliver.start(1 + w, [grads.result(w, way) for way in range(sz.n_context)])

    depth = joined.shape[2]

    def batch(ctx):
        copies = []
        for d in range(n_dp):
            at = d * sz.n_context + ctx
            rows = pl.ds(d * sz.rows, sz.rows)
            copies.append(
                pltpu.make_async_copy(landed.at[at, pl.ds(0, sz.rows)], d_s.at[rows], d_sem.at[d, 0])
            )
            copies.append(pltpu.make_async_copy(joined.at[at], j_s.at[rows], j_sem.at[d]))
            copies.append(
                pltpu.make_async_copy(
                    landed.at[at, pl.ds(sz.rows, 16)],
                    d_s.at[pl.ds(n_dp * sz.rows + 16 * d, 16)],
                    d_sem.at[d, 1],
                )
            )
        return copies

    def product(ctx, first):
        copies = batch(ctx)
        for copy in copies:
            copy.start()
        for copy in copies:
            copy.wait()
        chunk = sz.width // 4
        for n in range(4):
            cols = slice(n * chunk, (n + 1) * chunk)
            value = tn_dot(j_s[...], d_s[: n_dp * sz.rows, cols])
            tail = d_s[n_dp * sz.rows : n_dp * sz.rows + 16, cols].astype(jnp.float32)
            for d in range(1, n_dp):
                at = n_dp * sz.rows + 16 * d
                tail = tail + d_s[at : at + 16, cols].astype(jnp.float32)
            if first:
                adapter_grad[:depth, cols] = value
                adapter_grad[depth : depth + 16, cols] = tail
            else:
                adapter_grad[:depth, cols] += value
                adapter_grad[depth : depth + 16, cols] += tail

    own = pltpu.make_async_copy(low, landed.at[place.dp * sz.n_context + place.ctx], d_sem.at[0, 0])
    own.start()
    rest = adapter_grad.shape[0] - depth - 16
    if rest:
        adapter_grad[depth + 16 :, :] = jnp.zeros((rest, sz.width), jnp.float32)
    for s in range(n_dp - 1):
        ring_step()
        plane.step(s)
    own.wait()
    product(place.ctx, True)
    for s in range(n_dp):
        plane.wait_near(s)
    product(1 - place.ctx, False)
    for k in range(SUM_PARTS):
        line.start(k)
    ring_step()
    swap.wait()
    rows_s[place.group] = low[keep_rows, :]
    rows_s[1 - place.group] = swap_in[...]
    rows = rows_s[...].reshape(sz.rows, sz.width)
    ring_step()
    for k in range(SUM_PARTS):
        line.cross_over(k)
    ring_step()
    for b, copy in enumerate(weight_load):
        copy.wait()
        part = nt_dot(rows, weight_s[...]).reshape(sz.seqs, sz.block, weight_s.shape[0])
        embed_grad[:, :, b * weight_s.shape[0] : (b + 1) * weight_s.shape[0]] = part
        if b + 1 < len(weight_load):
            weight_load[b + 1].start()
    ring_step()
    for k in range(SUM_PARTS):
        line.share(k)
        ring_step()
    while grads.left():
        ring_step()
    for k in range(SUM_PARTS):
        line.complete(k)
    saves = [
        pltpu.make_async_copy(adapter_grad.at[pl.ds(0, depth)], adapter_out, out_sem.at[0]),
        pltpu.make_async_copy(adapter_grad.at[pl.ds(depth, 16)], gains_out, out_sem.at[1]),
    ]
    for copy in saves:
        copy.start()
    for w in range(1 + count):
        outs[w][...] = deliver.total(w)
    for copy in saves:
        copy.wait()
    grads.finish()
    deliver.finish()
    plane.finish()
    line.finish()


def run_grads(sz, n_dp, gate_sum, low, joined, adapter, xs, ys):
    count, bf16, f32, dma = len(xs), jnp.bfloat16, jnp.float32, pltpu.SemaphoreType.DMA
    shape = jax.ShapeDtypeStruct
    depth = sz.width // (n_dp * sz.n_context)
    wide = [y.shape[1] for y in ys]
    all_wide = [gate_sum.shape[2]] + wide
    slots, columns = joined.shape[0], joined.shape[2]
    unit = 16 * sz.half * SUM_PARTS
    total_rows = -(-(columns + 16) // unit) * unit
    return pl.pallas_call(
        partial(grads_kernel, sz, n_dp, count),
        out_shape=[shape((depth, n), f32) for n in all_wide]
        + [
            shape((sz.seqs, sz.block, sz.width), f32),
            shape((columns, sz.width), f32),
            shape((16, sz.width), f32),
            shape((slots,) + low.shape, bf16),
        ],
        in_specs=[any_spec(), full_spec()] + [any_spec()] * (2 + 2 * count),
        out_specs=[full_spec()] * (2 + count) + [any_spec()] * 3,
        scratch_shapes=GradRing.scratch(sz, n_dp, wide)
        + Deliver.scratch(sz, n_dp, all_wide)
        + PlaneRows.scratch(n_dp)
        + LineSum.scratch(sz, SUM_PARTS, total_rows // (sz.half * SUM_PARTS))
        + [
            pltpu.VMEM((total_rows, sz.width), f32),
            pltpu.VMEM((n_dp * (sz.rows + 16), sz.width), bf16),
            pltpu.VMEM((n_dp * sz.rows, columns), bf16),
            pltpu.VMEM((columns, sz.width), bf16),
            pltpu.VMEM((sz.seqs, sz.block, sz.width), bf16),
            pltpu.VMEM((sz.block, sz.width), bf16),
            dma((n_dp, 2)),
            dma((n_dp,)),
            dma,
            dma((2,)),
            dma((2,)),
        ],
        compiler_params=pltpu.CompilerParams(
            collective_id=8, has_side_effects=True, vmem_limit_bytes=VMEM_BYTES
        ),
        cost_estimate=pl.CostEstimate(
            flops=2 * sz.seq_len * sz.width * sum(wide), bytes_accessed=60 << 20, transcendentals=0
        ),
        name="grads",
    )(gate_sum, low, joined, adapter, *[slot_columns(sz, n_dp, x) for x in xs], *ys)


def shards(
    embedded,
    initial_state,
    cotangent,
    doc_ids,
    recurrences,
    adapter_weight,
    norm_gains,
    qkv_weight,
    output_head_weight,
    gate_up_weight,
    down_weight,
):
    n_dp = lax.axis_size("dp")
    n_tensor = lax.axis_size("tensor")
    n_context = lax.axis_size("context")
    dp_index = lax.axis_index("dp")
    t_index = lax.axis_index("tensor")
    ctx_index = lax.axis_index("context")
    seq_count, block_rows, model_width = embedded.shape
    seq_len = doc_ids.shape[1]
    half = n_tensor // seq_count
    group = t_index // half
    part = t_index % half
    heads_here = qkv_weight.shape[1]
    head_dim = qkv_weight.shape[2] // 3
    ff_here = down_weight.shape[0]
    def side_by_side(blocks):
        count, depth, columns = blocks.shape
        return blocks.transpose(1, 0, 2).reshape(depth, count * columns)

    def role_grad(grad, axis):
        piece = lax.psum_scatter(
            grad.astype(jnp.bfloat16), "dp", scatter_dimension=axis, tiled=True
        )
        low, high = jnp.split(piece, 2, axis=axis)
        give = [jnp.where(group == 0, low, high), jnp.where(group == 0, high, low)]
        back = [
            lax.ppermute(g, ("tensor", "context"), [(b, a) for a, b in perm])
            for g, perm in zip(give, role_perms)
        ]
        return back[0].astype(jnp.float32) + back[1].astype(jnp.float32)

    def gather_rows(rows):
        full = lax.all_gather(
            rows, ("tensor", "context"), axis=0, tiled=True, axis_index_groups=groups
        )
        split = full.reshape(half, n_context, seq_count, block_rows, model_width)
        return split.transpose(2, 0, 1, 3, 4).reshape(seq_len, model_width)

    sz = Sizes(
        n_tensor,
        n_context,
        seq_count,
        half,
        block_rows,
        n_context * block_rows,
        seq_count * block_rows,
        seq_len,
        model_width,
        heads_here,
        head_dim,
        ff_here,
    )
    adapter_block = adapter_weight.shape[0]
    gain_columns = norm_gains.shape[1]
    unit = 16 * half
    padded = -(-(adapter_block + 2) // unit) * unit
    adapter_rows = jnp.concatenate(
        [
            adapter_weight,
            jnp.pad(
                norm_gains,
                ((0, padded - adapter_block - 2), (0, model_width - gain_columns)),
            ),
        ],
        axis=0,
    )
    (
        adapter_all,
        qkv_use,
        out_blocks,
        gate_use,
        up_use,
        down_blocks,
        embed_rows,
        cot_rows,
        grad_ffn,
        embed_part,
        current,
    ) = run_weights(
        sz,
        n_dp,
        adapter_rows,
        adapter_block,
        [
            qkv_weight.reshape(qkv_weight.shape[0], -1),
            output_head_weight.reshape(heads_here * head_dim, -1),
            gate_up_weight[:, 0],
            gate_up_weight[:, 1],
            down_weight,
        ],
        [embedded, initial_state, cotangent],
    )
    qkv_use = qkv_use.reshape(model_width, -1)
    gate_use = gate_use.reshape(model_width, -1)
    up_use = up_use.reshape(model_width, -1)
    gains_full = (
        adapter_all[:, adapter_block : adapter_block + 2, :gain_columns]
        .transpose(1, 0, 2)
        .reshape(2, model_width)
    )
    if out_blocks.shape[2] % 128:
        out_blocks = side_by_side(out_blocks)[None]
        down_blocks = side_by_side(down_blocks)[None]
    gains_f = gains_full.astype(jnp.float32)

    cos_full, sin_full = rope_tables(seq_len, head_dim)
    own_seq = dp_index * seq_count + group
    docs = lax.dynamic_index_in_dim(doc_ids, own_seq, 0, keepdims=False)
    begin = jnp.sum((docs[None, :] < docs[:, None]).astype(jnp.int32), axis=1)[None, :]
    steps_own = lax.dynamic_index_in_dim(recurrences, own_seq, 0, keepdims=False) - BACK
    for step_index in range(MAXR - BACK):
        (mixed,) = run_attn(
            sz, n_dp, False, current, embed_part, gains_f, cos_full, sin_full, begin,
            adapter_all, qkv_use, out_blocks,
        )
        active = jnp.broadcast_to((step_index < steps_own).astype(jnp.float32), (1, model_width))
        (current,) = run_ffn(
            sz, False, mixed, current, active, gains_f, gate_use, up_use, down_blocks
        )
    detached = current
    (mixed_rows, adapted, feature_rows, query_hm, key_hm, value_hm, head_flat, lse, joined) = run_attn(
        sz, n_dp, True, detached, embed_part, gains_f, cos_full, sin_full, begin,
        adapter_all, qkv_use, out_blocks, embed_rows,
    )
    (current, ffn_input, gate_pre, up_pre, hidden) = run_ffn(
        sz, True, mixed_rows, detached, gains_f[:1], gains_f, gate_use, up_use, down_blocks
    )
    grad_mixed, gain_b, state_out, grad_gate, grad_up, down_sum = run_ffn_back(
        sz, n_dp, cot_rows, mixed_rows, gains_f, current, grad_ffn, gate_pre, up_pre,
        gate_use, up_use, down_blocks, hidden,
    )
    grad_low, down_t, grad_rows, grad_proj, gate_sum = run_attn_back(
        sz, n_dp, grad_mixed, adapted, gains_f, cos_full, sin_full, begin, gain_b,
        query_hm, key_hm, value_hm, lse, out_blocks, qkv_use, ffn_input, grad_gate, down_sum,
    )
    gate_s, up_s, qkv_s, out_t, embed_out, adapter_s, gains_rows, _ = run_grads(
        sz,
        n_dp,
        gate_sum,
        grad_low,
        joined,
        adapter_all,
        [ffn_input, feature_rows, grad_rows],
        [grad_up, grad_proj, head_flat],
    )
    place_at = (dp_index * n_context + ctx_index) * gain_columns
    gains_s = lax.dynamic_slice_in_dim(gains_rows[:2], place_at, gain_columns, 1)
    down_s = down_t.T
    out_s = out_t.T.reshape(heads_here, head_dim, -1)
    qkv_s = qkv_s.reshape(-1, heads_here, 3 * head_dim)
    gate_up_s = jnp.stack([gate_s, up_s], axis=1)
    return (state_out, embed_out, adapter_s, gains_s, qkv_s, out_s, gate_up_s, down_s)


def solution(mesh):
    placed = (
        P("dp", ("tensor", "context"), None),
        P("dp", ("tensor", "context"), None),
        P("dp", ("tensor", "context"), None),
        P(),
        P(),
        P(("dp", "context"), None),
        P(None, ("dp", "context")),
        P(("dp", "context"), "tensor", None),
        P("tensor", None, ("dp", "context")),
        P(("dp", "context"), None, "tensor"),
        P("tensor", ("dp", "context")),
    )
    return jax.shard_map(
        shards,
        mesh=mesh,
        in_specs=placed,
        out_specs=(
            P("dp", ("tensor", "context"), None),
            P("dp", ("tensor", "context"), None),
            P(("dp", "context"), None),
            P(None, ("dp", "context")),
            P(("dp", "context"), "tensor", None),
            P("tensor", None, ("dp", "context")),
            P(("dp", "context"), None, "tensor"),
            P("tensor", ("dp", "context")),
        ),
        check_vma=False,
    )
```

```python
from functools import partial
import math
from typing import NamedTuple

import jax
import jax.numpy as jnp
import numpy as np
from jax import lax
from jax.experimental import pallas as pl
from jax.experimental.pallas import tpu as pltpu
from jax.sharding import PartitionSpec as P

BACK = 1
MAXR = 4


rope_base = 50000.0
norm_eps = 1e-06
masked_score = -1e30


def rope_tables(seq_len, head_dim):
    freq_index = np.arange(head_dim // 2, dtype=np.float32)
    inv_freq = 1.0 / np.float32(rope_base) ** (np.float32(2.0) * freq_index / head_dim)
    angles = np.arange(seq_len, dtype=np.float32)[:, None] * inv_freq.astype(np.float32)[None, :]
    cos_t, sin_t = np.cos(angles), np.sin(angles)
    return (
        jnp.asarray(np.concatenate([cos_t, cos_t], axis=1), jnp.float32),
        jnp.asarray(np.concatenate([-sin_t, sin_t], axis=1), jnp.float32),
    )


MESH = pl.DeviceIdType.MESH
LOG2E = 1.4426950408889634
VMEM_BYTES = 62 << 20


class Sizes(NamedTuple):
    n_tensor: int
    n_context: int
    seqs: int
    half: int
    block: int
    tile: int
    rows: int
    seq_len: int
    width: int
    heads: int
    head_dim: int
    ff: int


def full_spec():
    return pl.BlockSpec(memory_space=pltpu.VMEM)


def any_spec():
    return pl.BlockSpec(memory_space=pl.ANY)


def nt_dot(a, b):
    return lax.dot_general(a, b, (((1,), (1,)), ((), ())), preferred_element_type=jnp.float32)


def tn_dot(a, b):
    return lax.dot_general(a, b, (((0,), (0,)), ((), ())), preferred_element_type=jnp.float32)


def nn_dot(a, b):
    return jnp.dot(a, b, preferred_element_type=jnp.float32)


class Place:
    def __init__(self, sz):
        t = lax.axis_index("tensor")
        self.sz = sz
        self.dp = lax.axis_index("dp")
        self.ctx = lax.axis_index("context")
        self.group = t // sz.half
        self.part = lax.rem(t, sz.half)

    def device(self, part, ctx):
        return (self.dp, self.group * self.sz.half + part, ctx)

    def ahead(self, q):
        return lax.rem(self.part + q, self.sz.half)

    def behind(self, q):
        return lax.rem(self.part + (self.sz.half - q), self.sz.half)

    def sibling(self):
        return self.device(self.part, 1 - self.ctx)

    def block(self, part, ctx, j):
        sz = self.sz
        first = ((part + j * sz.half) * sz.n_context + ctx) * sz.block
        return pl.ds(pl.multiple_of(first, sz.block), sz.block)

    def tile(self, q, j):
        sz = self.sz
        first = (self.ahead(q) + j * sz.half) * sz.tile
        return pl.ds(pl.multiple_of(first, sz.tile), sz.tile)

    def enter(self, others=(), more=0):
        barrier = pltpu.get_barrier_semaphore()
        for device in others:
            pl.semaphore_signal(barrier, inc=1, device_id=device, device_id_type=MESH)
        pl.semaphore_signal(
            barrier, inc=1, device_id=self.sibling(), device_id_type=MESH
        )
        for q in range(1, self.sz.half):
            pl.semaphore_signal(
                barrier,
                inc=1,
                device_id=self.device(self.ahead(q), self.ctx),
                device_id_type=MESH,
            )
        pl.semaphore_wait(barrier, self.sz.half + len(others) + more)


class Gather:
    @staticmethod
    def scratch(sz):
        kinds = 2 * sz.half - 1
        return [
            pltpu.SemaphoreType.DMA((kinds, sz.seqs)),
            pltpu.SemaphoreType.DMA((kinds, sz.seqs)),
        ]

    def __init__(self, place, ref, send, recv):
        self.place, self.ref, self.send, self.recv = place, ref, send, recv

    def copy(self, kind, j, rows):
        place, half = self.place, self.place.sz.half
        if 0 < kind < half:
            target = place.device(place.ahead(kind), place.ctx)
        else:
            target = place.sibling()
        return pltpu.make_async_remote_copy(
            src_ref=self.ref.at[rows],
            dst_ref=self.ref.at[rows],
            send_sem=self.send.at[kind, j],
            recv_sem=self.recv.at[kind, j],
            device_id=target,
            device_id_type=MESH,
        )

    def own(self, j):
        return self.place.block(self.place.part, self.place.ctx, j)

    def start(self, j):
        for q in range(1, self.place.sz.half):
            self.copy(q, j, self.own(j)).start()
        self.copy(0, j, self.own(j)).start()

    def wait_near(self, j):
        place = self.place
        self.copy(0, j, place.block(place.part, 1 - place.ctx, j)).wait_recv()

    def forward(self, q, j):
        place = self.place
        rows = place.block(place.behind(q), place.ctx, j)
        self.copy(q, j, rows).wait_recv()
        self.copy(place.sz.half - 1 + q, j, rows).start()

    def wait_far(self, q, j):
        place = self.place
        rows = place.block(place.behind(q), 1 - place.ctx, j)
        self.copy(place.sz.half - 1 + q, j, rows).wait_recv()

    def passed_on(self, j):
        place, half = self.place, self.place.sz.half
        for q in range(1, half):
            rows = place.block(place.behind(q), place.ctx, j)
            self.copy(half - 1 + q, j, rows).wait_send()

    def finish(self, forwards=True):
        for j in range(self.place.sz.seqs):
            for kind in range(self.place.sz.half):
                self.copy(kind, j, self.own(j)).wait_send()
            if forwards:
                self.passed_on(j)


class Scatter:
    @staticmethod
    def scratch(sz):
        kinds = 2 * sz.half - 1
        near = (sz.half, sz.seqs, sz.block, sz.width)
        far = (max(sz.half - 1, 1), sz.seqs, sz.block, sz.width)
        return [
            pltpu.VMEM((sz.tile, sz.width), jnp.float32),
            pltpu.VMEM(near, jnp.bfloat16),
            pltpu.VMEM(near, jnp.bfloat16),
            pltpu.VMEM(near, jnp.bfloat16),
            pltpu.VMEM(far, jnp.bfloat16),
            pltpu.VMEM(far, jnp.bfloat16),
            pltpu.SemaphoreType.DMA((kinds, sz.seqs)),
            pltpu.SemaphoreType.DMA((kinds, sz.seqs)),
        ]

    def __init__(self, place, part, mine, near_out, near_in, far_out, far_in, send, recv):
        self.place, self.part, self.mine = place, part, mine
        self.near_out, self.near_in = near_out, near_in
        self.far_out, self.far_in = far_out, far_in
        self.send, self.recv = send, recv

    def near(self, q, j):
        return pltpu.make_async_remote_copy(
            src_ref=self.near_out.at[q, j],
            dst_ref=self.near_in.at[q, j],
            send_sem=self.send.at[q, j],
            recv_sem=self.recv.at[q, j],
            device_id=self.place.sibling(),
            device_id_type=MESH,
        )

    def far(self, q, j):
        place = self.place
        return pltpu.make_async_remote_copy(
            src_ref=self.far_out.at[q - 1, j],
            dst_ref=self.far_in.at[q - 1, j],
            send_sem=self.send.at[place.sz.half - 1 + q, j],
            recv_sem=self.recv.at[place.sz.half - 1 + q, j],
            device_id=place.device(place.ahead(q), place.ctx),
            device_id_type=MESH,
        )

    def give(self, q, j):
        sz, ctx = self.place.sz, self.place.ctx
        mine = pl.ds(pl.multiple_of(ctx * sz.block, sz.block), sz.block)
        other = pl.ds(pl.multiple_of((1 - ctx) * sz.block, sz.block), sz.block)
        self.near_out[q, j] = self.part[other, :].astype(jnp.bfloat16)
        self.near(q, j).start()
        self.mine[q, j] = self.part[mine, :].astype(jnp.bfloat16)

    def onward(self, q, j):
        self.near(q, j).wait_recv()
        self.far_out[q - 1, j] = (
            self.mine[q, j].astype(jnp.float32) + self.near_in[q, j].astype(jnp.float32)
        ).astype(jnp.bfloat16)
        self.far(q, j).start()

    def total(self, j):
        self.near(0, j).wait_recv()
        total = self.mine[0, j].astype(jnp.float32) + self.near_in[0, j].astype(jnp.float32)
        for q in range(1, self.place.sz.half):
            self.far(q, j).wait_recv()
            total = total + self.far_in[q - 1, j].astype(jnp.float32)
        return total

    def finish(self):
        half = self.place.sz.half
        for j in range(self.place.sz.seqs):
            for q in range(half):
                self.near(q, j).wait_send()
            for q in range(1, half):
                self.far(q, j).wait_send()


def column_loads(blocks_ref, vmem_ref, sem):
    count, _, columns = blocks_ref.shape
    return [
        pltpu.make_async_copy(
            blocks_ref.at[b], vmem_ref.at[:, pl.ds(b * columns, columns)], sem.at[b]
        )
        for b in range(count)
    ]


def adapter_loads(blocks_ref, vmem_ref, sem):
    count, tops = sem.shape
    depth, columns = vmem_ref.shape[0] // tops, vmem_ref.shape[1] // count
    return [
        [
            pltpu.make_async_copy(
                blocks_ref.at[b, pl.ds(0, depth), pl.ds(n * columns, columns)],
                vmem_ref.at[pl.ds(b * depth, depth), pl.ds(n * columns, columns)],
                sem.at[n, b],
            )
            for b in range(tops)
        ]
        for n in range(count)
    ]


def rms_factor(rows):
    return lax.rsqrt(jnp.mean(rows * rows, axis=-1, keepdims=True) + norm_eps)


def turn(x, cos_t, sin_t):
    return x * cos_t + pltpu.roll(x, x.shape[-1] // 2, 1) * sin_t


def attn_kernel(sz, n_dp, keep, *refs):
    (latent, embed, gains, cos_t, sin_t, begin, adapter_hbm, qkv_hbm, out_hbm) = refs[:9]
    refs = refs[9:]
    if keep:
        embed_hbm, refs = refs[0], refs[1:]
    mixed = refs[0]
    refs = refs[1:]
    if keep:
        adapted_out, rows_out, q_out, k_out, v_out, head_out, lse_out, joined_out = refs[:8]
        refs = refs[8:]
    (wa, wqkv, wout, adapted, rows_s, q_s, k_s, v_s, head_s, lse_s) = refs[:10]
    load_a, load_qkv, load_out, keep_sem = refs[10:14]
    gather_refs = refs[14:16]
    scatter_refs = refs[16:24]
    if keep:
        joined_s, load_embed, x_send, x_recv = refs[24:]

    place = Place(sz)
    a_loads = adapter_loads(adapter_hbm, wa, load_a)
    qkv_load = pltpu.make_async_copy(qkv_hbm, wqkv, load_qkv)
    out_loads = column_loads(out_hbm, wout, load_out)
    for group in a_loads:
        for copy in group:
            copy.start()
    qkv_load.start()
    for copy in out_loads:
        copy.start()
    others = []
    if keep:
        ring = Ring(place, n_dp)
        t = lax.axis_index("tensor")
        embed_load = pltpu.make_async_copy(
            embed_hbm, joined_s.at[:, pl.ds(sz.width, sz.width)], load_embed
        )
        embed_load.start()
        plane = [(o, c) for o in range(n_dp) for c in range(2) if (o, c) != (0, 0)]

        def member(o, c):
            return (ring.index(o), t, place.ctx if c == 0 else 1 - place.ctx)

        def columns_to(o, c):
            to = member(o, c)
            depth = joined_out.shape[2]
            first = pl.multiple_of((to[0] * sz.n_context + to[2]) * depth, depth)
            return pltpu.make_async_remote_copy(
                src_ref=joined_s.at[:, pl.ds(first, depth)],
                dst_ref=joined_out.at[place.dp * sz.n_context + place.ctx],
                send_sem=x_send.at[o, c],
                recv_sem=x_recv.at[o, c],
                device_id=to,
                device_id_type=MESH,
            )

        def columns_from(o, c):
            ref = joined_out.at[
                ring.index(-o) * sz.n_context + (place.ctx if c == 0 else 1 - place.ctx)
            ]
            return pltpu.make_async_remote_copy(
                src_ref=ref,
                dst_ref=ref,
                send_sem=x_send.at[o, c],
                recv_sem=x_recv.at[o, c],
                device_id=place.sibling(),
                device_id_type=MESH,
            )

        others = [member(o, c) for o, c in plane if o]
    place.enter(others)
    gather = Gather(place, rows_s, *gather_refs)
    scatter = Scatter(place, *scatter_refs)

    low = latent[...].astype(jnp.bfloat16)
    columns = sz.width // len(a_loads)
    square = None
    for n, group in enumerate(a_loads):
        for copy in group:
            copy.wait()
        cols = pl.ds(n * columns, columns)
        chunk = nn_dot(low, wa[:, cols]) + embed[:, cols]
        adapted[:, cols] = chunk
        here = jnp.sum(chunk * chunk, axis=-1, keepdims=True)
        square = here if square is None else square + here
    factor = lax.rsqrt(square / sz.width + norm_eps)
    for j in range(sz.seqs):
        span = slice(j * sz.block, (j + 1) * sz.block)
        normed = (adapted[span, :] * factor[span]) * gains[0:1, :]
        rows_s[gather.own(j), :] = normed.astype(jnp.bfloat16)
        gather.start(j)

    qkv_load.wait()
    pair = min(2, sz.heads)
    d = sz.head_dim

    def project(q, j):
        rows = place.tile(q, j)
        x = rows_s[rows, :]
        cos_here, sin_here = cos_t[rows, :], sin_t[rows, :]
        for h0 in range(0, sz.heads, pair):
            proj = nn_dot(x, wqkv[:, 3 * d * h0 : 3 * d * (h0 + pair)])
            for h in range(pair):
                at = 3 * d * h
                q_s[h0 + h, rows, :] = turn(proj[:, at : at + d], cos_here, sin_here).astype(
                    jnp.bfloat16
                )
                k_s[h0 + h, rows, :] = turn(
                    proj[:, at + d : at + 2 * d], cos_here, sin_here
                ).astype(jnp.bfloat16)
                v_s[h0 + h, rows, :] = proj[:, at + 2 * d : at + 3 * d].astype(jnp.bfloat16)

    def attend(q, j):
        rows = place.tile(q, j)
        first = (place.ahead(q) + j * sz.half) * sz.tile
        length = (j + 1) * sz.half * sz.tile
        start = begin[:, pl.ds(pl.multiple_of(first, sz.tile), sz.tile)]
        key_at = lax.broadcasted_iota(jnp.int32, (length, sz.tile), 0)
        query_at = first + lax.broadcasted_iota(jnp.int32, (1, sz.tile), 1)
        allowed = (key_at >= start) & (key_at <= query_at)

        def head(h, carry):
            scores = nt_dot(k_s[h, 0:length, :], q_s[h, rows, :])
            scores = jnp.where(allowed, scores * (LOG2E / math.sqrt(d)), masked_score)
            top = jnp.max(scores, axis=0, keepdims=True)
            weight = jnp.exp2(scores - top)
            total = jnp.sum(weight, axis=0, keepdims=True)
            mixed_t = tn_dot(v_s[h, 0:length, :], weight.astype(jnp.bfloat16))
            result = jnp.transpose(mixed_t / total)
            head_s[rows, pl.ds(pl.multiple_of(h * d, d), d)] = result.astype(jnp.bfloat16)
            if keep:
                lse_s[h, :, rows] = top + jnp.log2(total)
            return carry

        lax.fori_loop(0, sz.heads, head, 0)

    def give(q, j):
        rows = place.tile(q, j)
        scatter.part[...] = nn_dot(head_s[rows, :], wout[...])
        scatter.give(q, j)

    copies = []

    def save(src, dst):
        copy = pltpu.make_async_copy(src, dst, keep_sem.at[len(copies)])
        copy.start()
        copies.append(copy)

    if keep:
        save(adapted, adapted_out)
        joined_s[:, : sz.width] = low
        embed_load.wait()
        for o, c in plane:
            columns_to(o, c).start()
        mine = place.dp * sz.n_context + place.ctx
        depth = joined_out.shape[2]
        save(
            joined_s.at[:, pl.ds(pl.multiple_of(mine * depth, depth), depth)], joined_out.at[mine]
        )
    far = range(1, sz.half)
    for j in range(sz.seqs):
        gather.wait_near(j)
        project(0, j)
    for copy in out_loads:
        copy.wait()
    for j in range(sz.seqs):
        for q in far:
            gather.forward(q, j)
        for q in far:
            gather.wait_far(sz.half - q, j)
            project(q, j)
        for q in far:
            attend(q, j)
            give(q, j)
        attend(0, j)
        for q in far:
            scatter.onward(q, j)
        give(0, j)
    if keep:
        for src, dst in ((rows_s, rows_out), (q_s, q_out), (k_s, k_out), (v_s, v_out)):
            save(src, dst)
        save(head_s, head_out)
        save(lse_s, lse_out)
    gather.finish()
    for j in range(sz.seqs):
        span = slice(j * sz.block, (j + 1) * sz.block)
        mixed[span, :] = adapted[span, :] + scatter.total(j)
    scatter.finish()
    if keep:
        for o, c in plane:
            columns_from(o, c).wait_recv()
            columns_to(o, c).wait_send()
    for copy in copies:
        copy.wait()


def run_attn(
    sz, n_dp, keep, latent, embed_part, gains, cos_t, sin_t, begin, adapter, qkv, out, *embed
):
    f32, bf16 = jnp.float32, jnp.bfloat16
    heads_shape = (sz.heads, sz.seq_len, sz.head_dim)
    shape = jax.ShapeDtypeStruct
    outs = [shape((sz.rows, sz.width), f32)]
    if keep:
        outs += [
            shape((sz.rows, sz.width), f32),
            shape((sz.seq_len, sz.width), bf16),
            shape(heads_shape, bf16),
            shape(heads_shape, bf16),
            shape(heads_shape, bf16),
            shape((sz.seq_len, sz.heads * sz.head_dim), bf16),
            shape((sz.heads, 1, sz.seq_len), f32),
            shape((adapter.shape[0], sz.rows, 2 * sz.width // adapter.shape[0]), bf16),
        ]
    scratch = [
        pltpu.VMEM((sz.width, sz.width), bf16),
        pltpu.VMEM(qkv.shape, bf16),
        pltpu.VMEM((sz.heads * sz.head_dim, sz.width), bf16),
        pltpu.VMEM((sz.rows, sz.width), f32),
        pltpu.VMEM((sz.seq_len, sz.width), bf16),
        pltpu.VMEM(heads_shape, bf16),
        pltpu.VMEM(heads_shape, bf16),
        pltpu.VMEM(heads_shape, bf16),
        pltpu.VMEM((sz.seq_len, sz.heads * sz.head_dim), bf16),
        pltpu.VMEM((sz.heads, 1, sz.seq_len), f32),
        pltpu.SemaphoreType.DMA((4, adapter.shape[0] // 2)),
        pltpu.SemaphoreType.DMA,
        pltpu.SemaphoreType.DMA((out.shape[0],)),
        pltpu.SemaphoreType.DMA((8,)),
    ]
    scratch += Gather.scratch(sz) + Scatter.scratch(sz)
    if keep:
        scratch += [
            pltpu.VMEM((sz.rows, 2 * sz.width), bf16),
            pltpu.SemaphoreType.DMA,
            pltpu.SemaphoreType.DMA((n_dp, 2)),
            pltpu.SemaphoreType.DMA((n_dp, 2)),
        ]
    flops = 2 * sz.rows * sz.width * sz.width + 2 * sz.seq_len * sz.width * qkv.shape[1]
    return pl.pallas_call(
        partial(attn_kernel, sz, n_dp, keep),
        out_shape=outs,
        in_specs=[full_spec()] * 6 + [any_spec()] * (3 + len(embed)),
        out_specs=[full_spec()] + [any_spec()] * (len(outs) - 1),
        scratch_shapes=scratch,
        compiler_params=pltpu.CompilerParams(
            collective_id=2 if keep else 1, has_side_effects=True, vmem_limit_bytes=VMEM_BYTES
        ),
        cost_estimate=pl.CostEstimate(
            flops=flops, bytes_accessed=20 << 20, transcendentals=0
        ),
        name="attn_keep" if keep else "attn_round",
    )(latent, embed_part, gains, cos_t, sin_t, begin, adapter, qkv, out, *embed)


def ffn_kernel(sz, keep, *refs):
    (mixed, latent, active, gains, gate_hbm, up_hbm, down_hbm, result) = refs[:8]
    refs = refs[8:]
    if keep:
        rows_out, gate_out, up_out, hidden_out = refs[:4]
        refs = refs[4:]
    wg, wu, wd, rows_s = refs[:4]
    refs = refs[4:]
    if keep:
        gate_s, up_s, hidden_s = refs[:3]
        refs = refs[3:]
    load_gu, load_down, keep_sem = refs[:3]
    gather_refs = refs[3:5]
    scatter_refs = refs[5:]

    place = Place(sz)
    gate_load = pltpu.make_async_copy(gate_hbm, wg, load_gu.at[0])
    up_load = pltpu.make_async_copy(up_hbm, wu, load_gu.at[1])
    down_loads = column_loads(down_hbm, wd, load_down)
    gate_load.start()
    up_load.start()
    for copy in down_loads:
        copy.start()
    place.enter()
    gather = Gather(place, rows_s, *gather_refs)
    scatter = Scatter(place, *scatter_refs)
    for j in range(sz.seqs):
        span = slice(j * sz.block, (j + 1) * sz.block)
        rows = mixed[span, :]
        normed = (rows * rms_factor(rows)) * gains[1:2, :]
        rows_s[gather.own(j), :] = normed.astype(jnp.bfloat16)
        gather.start(j)
    gate_load.wait()
    up_load.wait()
    for copy in down_loads:
        copy.wait()

    copies = []

    def save(src, dst):
        copy = pltpu.make_async_copy(src, dst, keep_sem.at[len(copies)])
        copy.start()
        copies.append(copy)

    def work(q, j):
        rows = place.tile(q, j)
        x = rows_s[rows, :]
        gate = nn_dot(x, wg[...])
        up = nn_dot(x, wu[...])
        hidden = (gate / (1.0 + jnp.exp(-gate)) * up).astype(jnp.bfloat16)
        if keep:
            gate_s[rows, :] = gate.astype(jnp.bfloat16)
            up_s[rows, :] = up.astype(jnp.bfloat16)
            hidden_s[rows, :] = hidden
        scatter.part[...] = nn_dot(hidden, wd[...])
        scatter.give(q, j)

    far = range(1, sz.half)
    for j in range(sz.seqs):
        gather.wait_near(j)
        work(0, j)
    for j in range(sz.seqs):
        for q in far:
            gather.forward(q, j)
        for q in far:
            gather.wait_far(sz.half - q, j)
            work(q, j)
        for q in far:
            scatter.onward(q, j)
    if keep:
        save(rows_s, rows_out)
        save(gate_s, gate_out)
        save(up_s, up_out)
        save(hidden_s, hidden_out)
    gather.finish()
    for j in range(sz.seqs):
        span = slice(j * sz.block, (j + 1) * sz.block)
        total = mixed[span, :] + scatter.total(j)
        if not keep:
            total = jnp.where(active[...] > 0, total, latent[span, :])
        result[span, :] = total
    scatter.finish()
    for copy in copies:
        copy.wait()


def run_ffn(sz, keep, mixed, latent, active, gains, gate, up, down):
    f32, bf16 = jnp.float32, jnp.bfloat16
    shape = jax.ShapeDtypeStruct
    outs = [shape((sz.rows, sz.width), f32)]
    if keep:
        outs += [
            shape((sz.seq_len, sz.width), bf16),
            shape((sz.seq_len, sz.ff), bf16),
            shape((sz.seq_len, sz.ff), bf16),
            shape((sz.seq_len, sz.ff), bf16),
        ]
    scratch = [
        pltpu.VMEM(gate.shape, bf16),
        pltpu.VMEM(up.shape, bf16),
        pltpu.VMEM((sz.ff, sz.width), bf16),
        pltpu.VMEM((sz.seq_len, sz.width), bf16),
    ]
    if keep:
        scratch += [pltpu.VMEM((sz.seq_len, sz.ff), bf16)] * 3
    scratch += [
        pltpu.SemaphoreType.DMA((2,)),
        pltpu.SemaphoreType.DMA((down.shape[0],)),
        pltpu.SemaphoreType.DMA((4,)),
    ]
    scratch += Gather.scratch(sz) + Scatter.scratch(sz)
    return pl.pallas_call(
        partial(ffn_kernel, sz, keep),
        out_shape=outs,
        in_specs=[full_spec()] * 4 + [any_spec()] * 3,
        out_specs=[full_spec()] + [any_spec()] * (len(outs) - 1),
        scratch_shapes=scratch,
        compiler_params=pltpu.CompilerParams(
            collective_id=4 if keep else 3, has_side_effects=True, vmem_limit_bytes=VMEM_BYTES
        ),
        cost_estimate=pl.CostEstimate(
            flops=6 * sz.seq_len * sz.width * sz.ff, bytes_accessed=20 << 20, transcendentals=0
        ),
        name="ffn_keep" if keep else "ffn_round",
    )(mixed, latent, active, gains, gate, up, down)


def round_kernel(sz, *refs):
    (latent, active, gains, cos_t, sin_t, begin) = refs[:6]
    (embed_hbm, adapter_hbm, qkv_hbm, out_hbm, gate_hbm, up_hbm, down_hbm, result) = refs[6:14]
    (wa, wqkv, wout, wg, wu, mixed, rows_s, q_s, k_s, v_s, head_s) = refs[14:25]
    load_embed, load_a, load_qkv, load_out, load_gu, load_down = refs[25:31]
    gather_refs, again_refs, scatter_refs = refs[31:33], refs[33:35], refs[35:43]

    place = Place(sz)
    embed_load = pltpu.make_async_copy(embed_hbm, mixed, load_embed)
    a_loads = adapter_loads(adapter_hbm, wa, load_a)
    qkv_load = pltpu.make_async_copy(qkv_hbm, wqkv, load_qkv)
    out_loads = column_loads(out_hbm, wout, load_out)
    gate_load = pltpu.make_async_copy(gate_hbm, wg, load_gu.at[0])
    up_load = pltpu.make_async_copy(up_hbm, wu, load_gu.at[1])
    wd = wa.at[pl.ds(0, sz.ff)]
    down_loads = column_loads(down_hbm, wd, load_down)
    embed_load.start()
    for group in a_loads:
        for copy in group:
            copy.start()
    qkv_load.start()
    for copy in out_loads:
        copy.start()
    place.enter()
    gather = Gather(place, rows_s, *gather_refs)
    again = Gather(place, rows_s, *again_refs)
    scatter = Scatter(place, *scatter_refs)

    low = latent[...].astype(jnp.bfloat16)
    columns = sz.width // len(a_loads)
    square = None
    embed_load.wait()
    for n, group in enumerate(a_loads):
        for copy in group:
            copy.wait()
        cols = pl.ds(n * columns, columns)
        chunk = nn_dot(low, wa[:, cols]) + mixed[:, cols]
        mixed[:, cols] = chunk
        here = jnp.sum(chunk * chunk, axis=-1, keepdims=True)
        square = here if square is None else square + here
    factor = lax.rsqrt(square / sz.width + norm_eps)
    for j in range(sz.seqs):
        span = slice(j * sz.block, (j + 1) * sz.block)
        normed = (mixed[span, :] * factor[span]) * gains[0:1, :]
        rows_s[gather.own(j), :] = normed.astype(jnp.bfloat16)
        gather.start(j)
    gate_load.start()
    up_load.start()
    for copy in down_loads:
        copy.start()
    qkv_load.wait()
    pair = min(2, sz.heads)
    d = sz.head_dim

    def project(q, j):
        rows = place.tile(q, j)
        x = rows_s[rows, :]
        cos_here, sin_here = cos_t[rows, :], sin_t[rows, :]
        for h0 in range(0, sz.heads, pair):
            proj = nn_dot(x, wqkv[:, 3 * d * h0 : 3 * d * (h0 + pair)])
            for h in range(pair):
                at = 3 * d * h
                q_s[h0 + h, rows, :] = turn(proj[:, at : at + d], cos_here, sin_here).astype(
                    jnp.bfloat16
                )
                k_s[h0 + h, rows, :] = turn(
                    proj[:, at + d : at + 2 * d], cos_here, sin_here
                ).astype(jnp.bfloat16)
                v_s[h0 + h, rows, :] = proj[:, at + 2 * d : at + 3 * d].astype(jnp.bfloat16)

    def attend(q, j):
        rows = place.tile(q, j)
        first = (place.ahead(q) + j * sz.half) * sz.tile
        length = (j + 1) * sz.half * sz.tile
        start = begin[:, pl.ds(pl.multiple_of(first, sz.tile), sz.tile)]
        key_at = lax.broadcasted_iota(jnp.int32, (length, sz.tile), 0)
        query_at = first + lax.broadcasted_iota(jnp.int32, (1, sz.tile), 1)
        allowed = (key_at >= start) & (key_at <= query_at)

        def head(h, carry):
            scores = nt_dot(k_s[h, 0:length, :], q_s[h, rows, :])
            scores = jnp.where(allowed, scores * (LOG2E / math.sqrt(d)), masked_score)
            top = jnp.max(scores, axis=0, keepdims=True)
            weight = jnp.exp2(scores - top)
            total = jnp.sum(weight, axis=0, keepdims=True)
            mixed_t = tn_dot(v_s[h, 0:length, :], weight.astype(jnp.bfloat16))
            result = jnp.transpose(mixed_t / total)
            head_s[rows, pl.ds(pl.multiple_of(h * d, d), d)] = result.astype(jnp.bfloat16)
            return carry

        lax.fori_loop(0, sz.heads, head, 0)

    def give(q, j):
        rows = place.tile(q, j)
        scatter.part[...] = nn_dot(head_s[rows, :], wout[...])
        scatter.give(q, j)

    far = range(1, sz.half)
    for j in range(sz.seqs):
        gather.wait_near(j)
        project(0, j)
    for copy in out_loads:
        copy.wait()
    for j in range(sz.seqs):
        for q in far:
            gather.forward(q, j)
        for q in far:
            gather.wait_far(sz.half - q, j)
            project(q, j)
        for q in far:
            attend(q, j)
            give(q, j)
        attend(0, j)
        gather.passed_on(j)
        for q in far:
            scatter.onward(q, j)
        give(0, j)
    gather.finish(forwards=False)
    for j in range(sz.seqs):
        span = slice(j * sz.block, (j + 1) * sz.block)
        rows = mixed[span, :] + scatter.total(j)
        mixed[span, :] = rows
        normed = (rows * rms_factor(rows)) * gains[1:2, :]
        rows_s[again.own(j), :] = normed.astype(jnp.bfloat16)
        again.start(j)
    scatter.finish()
    gate_load.wait()
    up_load.wait()
    for copy in down_loads:
        copy.wait()

    def work(q, j):
        x = rows_s[place.tile(q, j), :]
        gate = nn_dot(x, wg[...])
        up = nn_dot(x, wu[...])
        hidden = (gate / (1.0 + jnp.exp(-gate)) * up).astype(jnp.bfloat16)
        scatter.part[...] = nn_dot(hidden, wd[...])
        scatter.give(q, j)

    for j in range(sz.seqs):
        again.wait_near(j)
        work(0, j)
    for j in range(sz.seqs):
        for q in far:
            again.forward(q, j)
        for q in far:
            again.wait_far(sz.half - q, j)
            work(q, j)
        for q in far:
            scatter.onward(q, j)
    again.finish()
    for j in range(sz.seqs):
        span = slice(j * sz.block, (j + 1) * sz.block)
        total = mixed[span, :] + scatter.total(j)
        result[span, :] = jnp.where(active[...] > 0, total, latent[span, :])
    scatter.finish()


def run_round(sz, latent, active, gains, cos_t, sin_t, begin, embed, adapter, qkv, out, gate, up, down):
    f32, bf16, dma = jnp.float32, jnp.bfloat16, pltpu.SemaphoreType.DMA
    heads_shape = (sz.heads, sz.seq_len, sz.head_dim)
    return pl.pallas_call(
        partial(round_kernel, sz),
        out_shape=jax.ShapeDtypeStruct((sz.rows, sz.width), f32),
        in_specs=[full_spec()] * 6 + [any_spec()] * 7,
        out_specs=full_spec(),
        scratch_shapes=[
            pltpu.VMEM((sz.width, sz.width), bf16),
            pltpu.VMEM(qkv.shape, bf16),
            pltpu.VMEM((sz.heads * sz.head_dim, sz.width), bf16),
            pltpu.VMEM(gate.shape, bf16),
            pltpu.VMEM(up.shape, bf16),
            pltpu.VMEM((sz.rows, sz.width), f32),
            pltpu.VMEM((sz.seq_len, sz.width), bf16),
            pltpu.VMEM(heads_shape, bf16),
            pltpu.VMEM(heads_shape, bf16),
            pltpu.VMEM(heads_shape, bf16),
            pltpu.VMEM((sz.seq_len, sz.heads * sz.head_dim), bf16),
            dma,
            dma((4, adapter.shape[0] // 2)),
            dma,
            dma((out.shape[0],)),
            dma((2,)),
            dma((down.shape[0],)),
        ]
        + Gather.scratch(sz)
        + Gather.scratch(sz)
        + Scatter.scratch(sz),
        compiler_params=pltpu.CompilerParams(
            collective_id=1, has_side_effects=True, vmem_limit_bytes=VMEM_BYTES
        ),
        cost_estimate=pl.CostEstimate(
            flops=8 * sz.seq_len * sz.width * sz.ff, bytes_accessed=40 << 20, transcendentals=0
        ),
        name="round",
    )(latent, active, gains, cos_t, sin_t, begin, embed, adapter, qkv, out, gate, up, down)


def other_group(place):
    return (place.dp, (1 - place.group) * place.sz.half + place.part, place.ctx)


class Ring:
    def __init__(self, place, n_dp):
        self.place, self.count = place, n_dp
        self.at = self.swap(place.dp)

    def swap(self, i):
        if self.count != 4:
            return i
        x, y = lax.rem(i, 2), i // 2
        return 2 * y + x + y - 2 * x * y

    def index(self, offset):
        return self.swap(lax.rem(self.at + offset + 2 * self.count, self.count))

    def device(self, offset):
        return (self.index(offset), lax.axis_index("tensor"), self.place.ctx)


def weights_kernel(sz, n_dp, *refs):
    count = 5
    adapter_in, blocks_in = refs[0], refs[1 : 1 + count]
    rows_in, refs = refs[1 + count : 4 + count], refs[4 + count :]
    adapter_out, blocks_out = refs[0], refs[1 : 1 + count]
    embed_out, cot_out, cot_all, embed_part, state_out = refs[1 + count : 6 + count]
    refs = refs[6 + count :]
    (move_send, move_recv, ring_send, ring_recv, a_send, a_recv, x_send, x_recv, own_sem) = refs[:9]
    embed_s, state_s, weight_s, swap_send, swap_recv, keep_sem, weight_sem = refs[9:16]
    gather_refs = refs[16:]
    place = Place(sz)
    ring = Ring(place, n_dp)
    t = lax.axis_index("tensor")
    ctx, part, half, n_c = place.ctx, place.part, sz.half, sz.n_context
    role = part * n_c + ctx
    at_home = role == t
    steps = n_dp - 1
    sub = adapter_in.shape[0] // half
    ahead = 1 - 2 * ctx

    def holder(g):
        return (place.dp, g * half + t // n_c, lax.rem(t, n_c))

    barrier = pltpu.get_barrier_semaphore()

    def greet(device):
        pl.semaphore_signal(barrier, inc=1, device_id=device, device_id_type=MESH)

    greet(ring.device(1))
    greet(ring.device(n_dp - 1))
    greet(place.sibling())
    for q in range(1, half):
        greet(place.device(place.ahead(q), ctx))
    for c in range(n_c):
        pl.when(jnp.logical_not(at_home & (ctx == c)))(
            lambda c=c: greet((place.dp, role, c))
        )
    other = other_group(place)
    greet(other)
    waits = 3 + half + sz.seqs - jnp.where(at_home, 1, 0)
    pl.semaphore_wait(barrier, waits)

    own_at = pl.ds(pl.multiple_of(place.group * sz.block, sz.block), sz.block)
    other_at = pl.ds(pl.multiple_of((1 - place.group) * sz.block, sz.block), sz.block)
    rows_to = (embed_s, state_s, cot_out)

    def swap(i):
        return pltpu.make_async_remote_copy(
            src_ref=rows_in[i].at[1 - place.group],
            dst_ref=rows_to[i].at[own_at],
            send_sem=swap_send.at[i],
            recv_sem=swap_recv.at[i],
            device_id=other,
            device_id_type=MESH,
        )

    def swapped(i):
        ref = rows_to[i].at[other_at]
        return pltpu.make_async_remote_copy(
            src_ref=ref,
            dst_ref=ref,
            send_sem=swap_send.at[i],
            recv_sem=swap_recv.at[i],
            device_id=other,
            device_id_type=MESH,
        )

    def keep(i):
        return pltpu.make_async_copy(
            rows_in[i].at[place.group], rows_to[i].at[own_at], keep_sem.at[i]
        )

    for i in range(3):
        keep(i).start()
    gather = Gather(place, cot_all, *gather_refs)

    def own_rows_of(j):
        return pltpu.make_async_copy(
            cot_out.at[pl.ds(j * sz.block, sz.block)], cot_all.at[gather.own(j)], keep_sem.at[3 + j]
        )

    def move(w, g):
        slot = place.dp * n_c + ctx
        return pltpu.make_async_remote_copy(
            src_ref=blocks_in[w],
            dst_ref=blocks_out[w].at[slot],
            send_sem=move_send.at[w, g],
            recv_sem=move_recv.at[w, ctx],
            device_id=holder(g),
            device_id_type=MESH,
        )

    def stay(w):
        return pltpu.make_async_copy(
            blocks_in[w], blocks_out[w].at[place.dp * n_c + ctx], own_sem.at[w]
        )

    def moved(w, c):
        slot = place.dp * n_c + c
        arrival = pltpu.make_async_remote_copy(
            src_ref=blocks_in[w],
            dst_ref=blocks_out[w].at[slot],
            send_sem=move_send.at[w, 0],
            recv_sem=move_recv.at[w, c],
            device_id=place.sibling(),
            device_id_type=MESH,
        )
        here = at_home & (ctx == c)
        pl.when(here)(lambda: stay(w).wait())
        pl.when(jnp.logical_not(here))(lambda: arrival.wait_recv())

    def adapter_rows(offset, c, p):
        return adapter_out.at[
            ring.index(offset) * n_c + c, pl.ds(pl.multiple_of(p * sub, sub), sub)
        ]

    own_rows = adapter_in.at[pl.ds(pl.multiple_of(part * sub, sub), sub)]

    def around(s):
        rows = adapter_rows(-ahead * s, ctx, part)
        return pltpu.make_async_remote_copy(
            src_ref=own_rows if s == 0 else rows,
            dst_ref=rows,
            send_sem=a_send.at[s],
            recv_sem=a_recv.at[s],
            device_id=ring.device(ahead),
            device_id_type=MESH,
        )

    def across(kind, s):
        offset = -ahead * s
        if kind < half:
            dst = adapter_rows(offset, ctx, part)
            src = own_rows if s == 0 else dst
        else:
            src = dst = adapter_rows(offset, ctx, place.behind(kind - half + 1))
        target = place.device(place.ahead(kind), ctx) if 0 < kind < half else place.sibling()
        return pltpu.make_async_remote_copy(
            src_ref=src,
            dst_ref=dst,
            send_sem=x_send.at[kind, s],
            recv_sem=x_recv.at[kind, s],
            device_id=target,
            device_id_type=MESH,
        )

    def crossed(kind, s):
        if kind == 0:
            rows = adapter_rows(ahead * s, 1 - ctx, part)
        elif kind < half:
            rows = adapter_rows(-ahead * s, ctx, place.behind(kind))
        else:
            rows = adapter_rows(ahead * s, 1 - ctx, place.behind(kind - half + 1))
        return pltpu.make_async_remote_copy(
            src_ref=rows,
            dst_ref=rows,
            send_sem=x_send.at[kind, s],
            recv_sem=x_recv.at[kind, s],
            device_id=place.sibling(),
            device_id_type=MESH,
        )

    def hop(w, way, s):
        offset = -s if way == 0 else s
        rows = blocks_out[w].at[ring.index(offset) * n_c + way]
        return pltpu.make_async_remote_copy(
            src_ref=rows,
            dst_ref=rows,
            send_sem=ring_send.at[w, way, s],
            recv_sem=ring_recv.at[w, way, s],
            device_id=ring.device(1 if way == 0 else n_dp - 1),
            device_id_type=MESH,
        )

    def hopped(w, way, s):
        offset = -(s + 1) if way == 0 else s + 1
        rows = blocks_out[w].at[ring.index(offset) * n_c + way]
        return pltpu.make_async_remote_copy(
            src_ref=rows,
            dst_ref=rows,
            send_sem=ring_send.at[w, way, s],
            recv_sem=ring_recv.at[w, way, s],
            device_id=ring.device(1),
            device_id_type=MESH,
        )

    around(0).start()
    own = pltpu.make_async_copy(own_rows, adapter_rows(0, ctx, part), own_sem.at[count])
    own.start()

    def start_move(w):
        for g in range(sz.seqs):
            here = at_home & (place.group == g)
            pl.when(jnp.logical_not(here))(lambda w=w, g=g: move(w, g).start())
        pl.when(at_home)(lambda w=w: stay(w).start())

    start_move(0)
    start_move(1)
    for kind in range(half):
        across(kind, 0).start()

    def adapter_step(s):
        if s < steps:
            arrival = pltpu.make_async_remote_copy(
                src_ref=own_rows,
                dst_ref=adapter_rows(-ahead * (s + 1), ctx, part),
                send_sem=a_send.at[s],
                recv_sem=a_recv.at[s],
                device_id=ring.device(1),
                device_id_type=MESH,
            )
            arrival.wait_recv()
            if s + 1 < steps:
                around(s + 1).start()
            for kind in range(half):
                across(kind, s + 1).start()

    def adapter_pass(s):
        for q in range(1, half):
            crossed(q, s).wait_recv()
            across(half - 1 + q, s).start()

    embed_save = pltpu.make_async_copy(embed_s, embed_out, keep_sem.at[3 + sz.seqs])
    todo = []
    for k in range(count + steps):
        for s in range(min(k, steps - 1), -1, -1):
            w = k - s
            if w < count:
                todo.append((w, s))
    done = 0
    for w, s in todo:
        for way in range(n_c):
            if s == 0:
                moved(w, way)
            else:
                hopped(w, way, s - 1).wait_recv()
            hop(w, way, s).start()
        if s == 0 and w + 2 < count:
            start_move(w + 2)
        if s == 0 and w == count - 2:
            for i in range(3):
                swap(i).start()
        if done < steps:
            adapter_step(done)
        if s == min(1, steps - 1) and w == count - 1:
            for i in range(3):
                keep(i).wait()
                swapped(i).wait_recv()
            for j in range(sz.seqs):
                own_rows_of(j).start()
            embed_save.start()
            for j in range(sz.seqs):
                own_rows_of(j).wait()
                gather.start(j)
            state_out[...] = state_s[...].astype(jnp.float32)
        done += 1
    for s in range(done, steps):
        adapter_step(s)
    for s in range(n_dp):
        adapter_pass(s)
    for j in range(sz.seqs):
        gather.wait_near(j)
        for q in range(1, half):
            gather.forward(q, j)
    for s in range(n_dp):
        crossed(0, s).wait_recv()
        for q in range(1, half):
            crossed(half - 1 + q, s).wait_recv()
    own.wait()
    slots, depth = adapter_out.shape[0], weight_s.shape[1]
    loads = [
        pltpu.make_async_copy(
            adapter_out.at[slots // 2 + b, pl.ds(0, depth)], weight_s.at[b % 2], weight_sem.at[b % 2]
        )
        for b in range(slots // 2)
    ]
    loads[0].start()
    for b, copy in enumerate(loads):
        if b + 1 < len(loads):
            loads[b + 1].start()
        copy.wait()
        part_here = nn_dot(embed_s[:, b * depth : (b + 1) * depth], weight_s[b % 2])
        if b:
            embed_part[...] += part_here
        else:
            embed_part[...] = part_here
    for w in range(count):
        for way in range(n_c):
            hopped(w, way, steps - 1).wait_recv()
    for j in range(sz.seqs):
        for q in range(1, half):
            gather.wait_far(q, j)
    gather.finish()
    embed_save.wait()
    for i in range(3):
        swap(i).wait_send()
    for w in range(count):
        for g in range(sz.seqs):
            here = at_home & (place.group == g)
            pl.when(jnp.logical_not(here))(lambda w=w, g=g: move(w, g).wait_send())
        for way in range(n_c):
            for s in range(steps):
                hop(w, way, s).wait_send()
    for s in range(steps):
        around(s).wait_send()
    for s in range(n_dp):
        for kind in range(2 * half - 1):
            across(kind, s).wait_send()


def run_weights(sz, n_dp, adapter, adapter_block, blocks, rows):
    bf16, f32 = jnp.bfloat16, jnp.float32
    slots = n_dp * sz.n_context
    outs = [jax.ShapeDtypeStruct((slots,) + a.shape, bf16) for a in [adapter] + blocks]
    outs += [
        jax.ShapeDtypeStruct((sz.rows, sz.width), bf16),
        jax.ShapeDtypeStruct((sz.rows, sz.width), bf16),
        jax.ShapeDtypeStruct((sz.seq_len, sz.width), bf16),
        jax.ShapeDtypeStruct((sz.rows, sz.width), f32),
        jax.ShapeDtypeStruct((sz.rows, sz.width), f32),
    ]
    count, steps, dma = len(blocks), n_dp - 1, pltpu.SemaphoreType.DMA
    kinds = 2 * sz.half - 1
    return pl.pallas_call(
        partial(weights_kernel, sz, n_dp),
        out_shape=outs,
        in_specs=[any_spec()] * (4 + count),
        out_specs=[any_spec()] * (4 + count) + [full_spec()] * 2,
        scratch_shapes=[
            dma((count, sz.seqs)),
            dma((count, sz.n_context)),
            dma((count, sz.n_context, steps)),
            dma((count, sz.n_context, steps)),
            dma((steps,)),
            dma((steps,)),
            dma((kinds, n_dp)),
            dma((kinds, n_dp)),
            dma((count + 1,)),
            pltpu.VMEM((sz.rows, sz.width), bf16),
            pltpu.VMEM((sz.rows, sz.width), bf16),
            pltpu.VMEM((2, adapter_block, sz.width), bf16),
            dma((3,)),
            dma((3,)),
            dma((4 + sz.seqs,)),
            dma((2,)),
        ]
        + Gather.scratch(sz),
        compiler_params=pltpu.CompilerParams(
            collective_id=5, has_side_effects=True, vmem_limit_bytes=VMEM_BYTES
        ),
        name="weights",
    )(adapter, *blocks, *rows)


def norm_back(grad, rows, factor, gain):
    unit = rows * factor
    weighted = grad * gain
    inner = jnp.mean(weighted * unit, axis=-1, keepdims=True)
    return factor * (weighted - unit * inner), jnp.sum(grad * unit, axis=0, keepdims=True)


class GradRing:
    @staticmethod
    def scratch(sz, n_dp, wide):
        slots, ways, steps, dma = n_dp * sz.n_context, sz.n_context, n_dp - 1, pltpu.SemaphoreType.DMA
        depth, bf16, count = sz.width // slots, jnp.bfloat16, len(wide)
        return (
            [pltpu.VMEM((sz.seq_len, n), bf16) for n in wide]
            + [pltpu.VMEM((ways, depth, n), bf16) for n in wide]
            + [pltpu.VMEM((ways, steps, depth, n), bf16) for n in wide]
            + [
                pltpu.VMEM((2, ways, sz.seq_len, depth), bf16),
                dma((count,)),
                dma((2, ways)),
                dma((count, ways, steps)),
                dma((count, ways, steps)),
            ]
        )

    def __init__(self, sz, place, ring, xs, ys, refs):
        count = len(xs)
        self.sz, self.place, self.ring, self.xs, self.count = sz, place, ring, xs, count
        self.ys, self.first, self.held = (refs[i * count : (i + 1) * count] for i in range(3))
        self.x_s, self.load_y, self.load_x, self.send, self.recv = refs[3 * count :]
        self.y_loads = [
            pltpu.make_async_copy(ys[w], self.ys[w], self.load_y.at[w]) for w in range(count)
        ]
        self.tasks = [
            (k - s, s)
            for k in range(count + ring.count)
            for s in range(min(k, ring.count - 1), -1, -1)
            if k - s < count
        ]
        self.done, self.seen = 0, set()

    def start(self):
        for copy in self.y_loads:
            copy.start()
        for way in range(self.sz.n_context):
            self.x_load(0, way).start()

    def slot(self, way, s):
        return self.ring.index(-(s + 1) if way == 0 else s + 1) * self.sz.n_context + way

    def x_load(self, k, way):
        w, s = self.tasks[k]
        depth = self.x_s.shape[3]
        if self.xs[w].shape[0] == 1:
            at = pl.multiple_of(self.slot(way, s) * depth, depth)
            src = self.xs[w].at[0, :, pl.ds(at, depth)]
        else:
            src = self.xs[w].at[self.slot(way, s)]
        return pltpu.make_async_copy(src, self.x_s.at[k % 2, way], self.load_x.at[k % 2, way])

    def source(self, w, way, s):
        return self.first[w].at[way] if s == 0 else self.held[w].at[way, s - 1]

    def hop(self, w, way, s):
        return pltpu.make_async_remote_copy(
            src_ref=self.source(w, way, s),
            dst_ref=self.held[w].at[way, s],
            send_sem=self.send.at[w, way, s],
            recv_sem=self.recv.at[w, way, s],
            device_id=self.ring.device(1 if way == 0 else self.ring.count - 1),
            device_id_type=MESH,
        )

    def result(self, w, way):
        return self.source(w, way, self.ring.count - 1)

    def step(self):
        k = self.done
        self.done += 1
        w, s = self.tasks[k]
        ways = range(self.sz.n_context)
        if k + 1 < len(self.tasks):
            for way in ways:
                self.x_load(k + 1, way).start()
        if w not in self.seen:
            self.y_loads[w].wait()
            self.seen.add(w)
        for way in ways:
            self.x_load(k, way).wait()
            value = tn_dot(self.x_s[k % 2, way], self.ys[w][...])
            if s:
                self.hop(w, way, s - 1).wait_recv()
                value = value + self.held[w][way, s - 1].astype(jnp.float32)
            ref = self.source(w, way, s)
            ref[...] = value.astype(jnp.bfloat16)
            if s < self.ring.count - 1:
                self.hop(w, way, s).start()
        return w, s == self.ring.count - 1

    def left(self):
        return len(self.tasks) - self.done

    def finish(self):
        for w in range(self.count):
            for way in range(self.sz.n_context):
                for s in range(self.ring.count - 1):
                    self.hop(w, way, s).wait_send()


class Deliver:
    @staticmethod
    def scratch(sz, n_dp, wide):
        depth, count, dma = sz.width // (n_dp * sz.n_context), len(wide), pltpu.SemaphoreType.DMA
        return [pltpu.VMEM((sz.seqs, depth, n), jnp.bfloat16) for n in wide] + [
            dma((count, sz.n_context)),
            dma((count, sz.seqs)),
            dma((count,)),
        ]

    def __init__(self, sz, place, refs):
        self.sz, self.place = sz, place
        self.landed = refs[:-3]
        self.send, self.recv, self.own = refs[-3:]
        self.count = len(self.landed)
        self.t = lax.axis_index("tensor")
        self.role = place.part * sz.n_context + place.ctx
        self.at_home = self.role == self.t
        self.sources = [None] * self.count

    def greet(self):
        sz, place = self.sz, self.place
        barrier = pltpu.get_barrier_semaphore()
        for g in range(sz.seqs):
            holder = (place.dp, g * sz.half + self.t // sz.n_context, lax.rem(self.t, sz.n_context))
            pl.when(jnp.logical_not(self.at_home & (place.group == g)))(
                lambda holder=holder: pl.semaphore_signal(
                    barrier, inc=1, device_id=holder, device_id_type=MESH
                )
            )
        return sz.n_context - jnp.where(self.at_home, 1, 0)

    def remote(self, w, way):
        return pltpu.make_async_remote_copy(
            src_ref=self.sources[w][way],
            dst_ref=self.landed[w].at[self.place.group],
            send_sem=self.send.at[w, way],
            recv_sem=self.recv.at[w, self.place.group],
            device_id=(self.place.dp, self.role, way),
            device_id_type=MESH,
        )

    def local(self, w, way):
        return pltpu.make_async_copy(
            self.sources[w][way], self.landed[w].at[self.place.group], self.own.at[w]
        )

    def start(self, w, sources):
        self.sources[w] = sources
        for way in range(self.sz.n_context):
            here = self.at_home & (self.place.ctx == way)
            pl.when(here)(lambda way=way: self.local(w, way).start())
            pl.when(jnp.logical_not(here))(lambda way=way: self.remote(w, way).start())

    def total(self, w):
        place = self.place
        for g in range(self.sz.seqs):
            ref = self.landed[w].at[g]
            arrival = pltpu.make_async_remote_copy(
                src_ref=ref,
                dst_ref=ref,
                send_sem=self.send.at[w, 0],
                recv_sem=self.recv.at[w, g],
                device_id=(place.dp, self.t, 1 - place.ctx),
                device_id_type=MESH,
            )
            here = self.at_home & (place.group == g)
            pl.when(here)(lambda: self.local(w, 0).wait())
            pl.when(jnp.logical_not(here))(lambda arrival=arrival: arrival.wait_recv())
        total = self.landed[w][0].astype(jnp.float32)
        for g in range(1, self.sz.seqs):
            total = total + self.landed[w][g].astype(jnp.float32)
        return total

    def finish(self):
        for w in range(self.count):
            for way in range(self.sz.n_context):
                here = self.at_home & (self.place.ctx == way)
                pl.when(jnp.logical_not(here))(lambda w=w, way=way: self.remote(w, way).wait_send())


def slot_columns(sz, n_dp, x):
    slots = n_dp * sz.n_context
    depth = sz.width // slots
    if depth % 128:
        return x.reshape(sz.seq_len, slots, depth).transpose(1, 0, 2)
    return x[None]


def ffn_back_kernel(sz, n_dp, *refs):
    (cot, mixed, gains, state) = refs[:4]
    (rows_hbm, gate_hbm, up_hbm, wg_hbm, wu_hbm, down_hbm, x_hbm, hidden_hbm) = refs[4:12]
    (grad_mixed, gain_grad, state_out, dgate_out, dup_out, down_sum) = refs[12:18]
    (rows_s, gate_s, up_s, wg, wu, wd, load, load_down, keep_sem) = refs[18:27]
    (swap_out, swap_in, swap_sem) = refs[27:30]
    scatter_refs, ring_refs = refs[30:38], refs[38:]
    place = Place(sz)
    ring = Ring(place, n_dp)
    grads = GradRing(sz, place, ring, [x_hbm], [hidden_hbm], ring_refs)
    grads.start()
    pairs = ((rows_hbm, rows_s), (gate_hbm, gate_s), (up_hbm, up_s), (wg_hbm, wg), (wu_hbm, wu))
    loads = [
        pltpu.make_async_copy(src, dst, load.at[i]) for i, (src, dst) in enumerate(pairs)
    ]
    down_loads = column_loads(down_hbm, wd, load_down)
    loads[0].start()
    for copy in down_loads + loads[1:]:
        copy.start()
    other = (place.dp, (1 - place.group) * sz.half + place.part, place.ctx)
    place.enter([ring.device(1), ring.device(n_dp - 1), other])
    scatter = Scatter(place, *scatter_refs)
    grads.step()
    for copy in [loads[0]] + down_loads + loads[1:]:
        copy.wait()
    give_rows = pl.ds(pl.multiple_of((1 - place.group) * sz.block, sz.block), sz.block)
    keep_rows = pl.ds(pl.multiple_of(place.group * sz.block, sz.block), sz.block)
    swap = pltpu.make_async_remote_copy(
        src_ref=swap_out,
        dst_ref=swap_in,
        send_sem=swap_sem.at[0],
        recv_sem=swap_sem.at[1],
        device_id=other,
        device_id_type=MESH,
    )
    swap_out[...] = state[give_rows, :].astype(jnp.bfloat16)
    state_out[place.group] = state[keep_rows, :]

    def work(q, j):
        rows = place.tile(q, j)
        dh = nt_dot(rows_s[rows, :], wd[...])
        gate = gate_s[rows, :].astype(jnp.float32)
        up = up_s[rows, :].astype(jnp.float32)
        sig = 1.0 / (1.0 + jnp.exp(-gate))
        dgate = (dh * up * sig * (1.0 + gate * (1.0 - sig))).astype(jnp.bfloat16)
        dup = (dh * gate * sig).astype(jnp.bfloat16)
        gate_s[rows, :] = dgate
        up_s[rows, :] = dup
        scatter.part[...] = nt_dot(dgate, wg[...]) + nt_dot(dup, wu[...])
        scatter.give(q, j)

    far = range(1, sz.half)
    for j in range(sz.seqs):
        for q in far:
            work(q, j)
        if j:
            for q in far:
                scatter.onward(q, j - 1)
    work(0, 0)
    for q in far:
        scatter.onward(q, sz.seqs - 1)
    swap.start()
    grads.step()
    for j in range(1, sz.seqs):
        work(0, j)
    copies = [
        pltpu.make_async_copy(gate_s, dgate_out, keep_sem.at[0]),
        pltpu.make_async_copy(up_s, dup_out, keep_sem.at[1]),
    ]
    for copy in copies:
        copy.start()
    gain_total = None
    for j in range(sz.seqs):
        span = slice(j * sz.block, (j + 1) * sz.block)
        rows = mixed[span, :]
        grad, gain_here = norm_back(scatter.total(j), rows, rms_factor(rows), gains[1:2, :])
        grad_mixed[span, :] = cot[span, :].astype(jnp.float32) + grad
        gain_total = gain_here if gain_total is None else gain_total + gain_here
    gain_grad[...] = gain_total
    while grads.left() > 1:
        grads.step()
    swap.wait()
    state_out[1 - place.group] = swap_in[...].astype(jnp.float32)
    grads.step()
    for way in range(sz.n_context):
        copies.append(
            pltpu.make_async_copy(grads.result(0, way), down_sum.at[way], keep_sem.at[2 + way])
        )
        copies[-1].start()
    scatter.finish()
    grads.finish()
    for copy in copies:
        copy.wait()


def run_ffn_back(sz, n_dp, cot, mixed, gains, state, rows, gate, up, wg, wu, down, hidden):
    f32, bf16, shape = jnp.float32, jnp.bfloat16, jax.ShapeDtypeStruct
    dma = pltpu.SemaphoreType.DMA
    depth = sz.width // (n_dp * sz.n_context)
    return pl.pallas_call(
        partial(ffn_back_kernel, sz, n_dp),
        out_shape=[
            shape((sz.rows, sz.width), f32),
            shape((1, sz.width), f32),
            shape((sz.seqs, sz.block, sz.width), f32),
            shape((sz.seq_len, sz.ff), bf16),
            shape((sz.seq_len, sz.ff), bf16),
            shape((sz.n_context, depth, sz.ff), bf16),
        ],
        in_specs=[full_spec()] * 4 + [any_spec()] * 8,
        out_specs=[full_spec()] * 3 + [any_spec()] * 3,
        scratch_shapes=[
            pltpu.VMEM((sz.seq_len, sz.width), bf16),
            pltpu.VMEM((sz.seq_len, sz.ff), bf16),
            pltpu.VMEM((sz.seq_len, sz.ff), bf16),
            pltpu.VMEM(wg.shape, bf16),
            pltpu.VMEM(wu.shape, bf16),
            pltpu.VMEM((sz.ff, sz.width), bf16),
            dma((5,)),
            dma((down.shape[0],)),
            dma((2 + sz.n_context,)),
            pltpu.VMEM((sz.block, sz.width), bf16),
            pltpu.VMEM((sz.block, sz.width), bf16),
            dma((2,)),
        ]
        + Scatter.scratch(sz)
        + GradRing.scratch(sz, n_dp, [sz.ff]),
        compiler_params=pltpu.CompilerParams(
            collective_id=6, has_side_effects=True, vmem_limit_bytes=VMEM_BYTES
        ),
        cost_estimate=pl.CostEstimate(
            flops=8 * sz.seq_len * sz.width * sz.ff, bytes_accessed=40 << 20, transcendentals=0
        ),
        name="ffn_back",
    )(cot, mixed, gains, state, rows, gate, up, wg, wu, down, slot_columns(sz, n_dp, rows), hidden)


def attn_back_kernel(sz, n_dp, *refs):
    (grad_mixed, adapted, gains, cos_t, sin_t, begin, gain_b) = refs[:7]
    (q_hbm, k_hbm, v_hbm, lse_hbm, out_hbm, qkv_hbm, x_hbm, dgate_hbm, down_sum) = refs[7:16]
    (grad_low, down_grad, rows_out, proj_out, gate_sum) = refs[16:21]
    (rows_s, q_s, k_s, v_s, lse_s, do_s, dk_s, dv_s, proj_s, wout, wqkv) = refs[21:32]
    (load, load_out, keep_sem) = refs[32:35]
    gather_refs, scatter_refs = refs[35:37], refs[37:45]
    ring_refs, deliver_refs = refs[45:53], refs[53:]
    place = Place(sz)
    ring = Ring(place, n_dp)
    grads = GradRing(sz, place, ring, [x_hbm], [dgate_hbm], ring_refs)
    deliver = Deliver(sz, place, deliver_refs)
    grads.start()
    pairs = ((q_hbm, q_s), (k_hbm, k_s), (v_hbm, v_s), (lse_hbm, lse_s), (qkv_hbm, wqkv))
    loads = [
        pltpu.make_async_copy(src, dst, load.at[i]) for i, (src, dst) in enumerate(pairs)
    ]
    out_loads = column_loads(out_hbm, wout, load_out)
    for copy in out_loads + loads:
        copy.start()
    targets = deliver.greet()
    place.enter([ring.device(1), ring.device(n_dp - 1)], targets)
    gather = Gather(place, rows_s, *gather_refs)
    scatter = Scatter(place, *scatter_refs)
    for j in range(sz.seqs):
        span = slice(j * sz.block, (j + 1) * sz.block)
        rows_s[gather.own(j), :] = grad_mixed[span, :].astype(jnp.bfloat16)
        gather.start(j)
    grads.step()
    deliver.start(0, [down_sum.at[way] for way in range(sz.n_context)])
    for copy in out_loads:
        copy.wait()
    d = sz.head_dim

    def heads_grad(q, j):
        rows = place.tile(q, j)
        dhead = nt_dot(rows_s[rows, :], wout[...]).astype(jnp.bfloat16)
        for h in range(sz.heads):
            do_s[h, rows, :] = dhead[:, h * d : (h + 1) * d]

    far = range(1, sz.half)
    for j in range(sz.seqs):
        gather.wait_near(j)
        heads_grad(0, j)
    for copy in loads:
        copy.wait()
    for j in range(sz.seqs):
        for q in far:
            gather.forward(q, j)
        for q in far:
            gather.wait_far(sz.half - q, j)
            heads_grad(q, j)
    copies = [pltpu.make_async_copy(rows_s, rows_out, keep_sem.at[0])]
    copies[0].start()
    grads.step()

    tiles = sz.n_tensor
    scale = 1.0 / math.sqrt(d)

    def head(h, carry):
        for i in reversed(range(tiles)):
            rows = slice(i * sz.tile, (i + 1) * sz.tile)
            length = (i + 1) * sz.tile
            keys, values = k_s[h, 0:length, :], v_s[h, 0:length, :]
            query, grad = q_s[h, rows, :], do_s[h, rows, :]
            start = begin[:, rows]
            key_at = lax.broadcasted_iota(jnp.int32, (length, sz.tile), 0)
            query_at = i * sz.tile + lax.broadcasted_iota(jnp.int32, (1, sz.tile), 1)
            allowed = (key_at >= start) & (key_at <= query_at)
            scores = nt_dot(keys, query)
            scores = jnp.where(allowed, scores * (LOG2E * scale), masked_score)
            probs = jnp.exp2(scores - lse_s[h, :, rows])
            dprobs = nt_dot(values, grad)
            inner = jnp.sum(probs * dprobs, axis=0, keepdims=True)
            dscores = (probs * (dprobs - inner)).astype(jnp.bfloat16)
            dv = nn_dot(probs.astype(jnp.bfloat16), grad)
            dk = nn_dot(dscores, query)
            if i == tiles - 1:
                dv_s[...] = dv
                dk_s[...] = dk
            else:
                dv_s[0:length, :] += dv
                dk_s[0:length, :] += dk
            dq = jnp.transpose(tn_dot(keys, dscores)) * scale
            cos_here, sin_here = cos_t[rows, :], sin_t[rows, :]
            proj_s[rows, pl.ds(pl.multiple_of(h * 3 * d, d), d)] = turn(
                dq, cos_here, -sin_here
            ).astype(jnp.bfloat16)
        dk = turn(dk_s[...] * scale, cos_t[...], -sin_t[...])
        proj_s[:, pl.ds(pl.multiple_of(h * 3 * d + d, d), d)] = dk.astype(jnp.bfloat16)
        proj_s[:, pl.ds(pl.multiple_of(h * 3 * d + 2 * d, d), d)] = dv_s[...].astype(jnp.bfloat16)
        return carry

    lax.fori_loop(0, sz.heads // 2, head, 0)
    grads.step()
    lax.fori_loop(sz.heads // 2, sz.heads, head, 0)
    copies.append(pltpu.make_async_copy(proj_s, proj_out, keep_sem.at[1]))
    copies[1].start()

    def give(q, j):
        scatter.part[...] = nt_dot(proj_s[place.tile(q, j), :], wqkv[...])
        scatter.give(q, j)

    for j in range(sz.seqs):
        for q in far:
            give(q, j)
        if j:
            for q in far:
                scatter.onward(q, j - 1)
    give(0, 0)
    for q in far:
        scatter.onward(q, sz.seqs - 1)
    for j in range(1, sz.seqs):
        give(0, j)
    gather.finish()
    down_grad[...] = deliver.total(0)
    while grads.left():
        grads.step()
    for way in range(sz.n_context):
        copies.append(
            pltpu.make_async_copy(grads.result(0, way), gate_sum.at[way], keep_sem.at[2 + way])
        )
        copies[-1].start()
    gain_total = None
    for j in range(sz.seqs):
        span = slice(j * sz.block, (j + 1) * sz.block)
        rows = adapted[span, :]
        grad, gain_here = norm_back(scatter.total(j), rows, rms_factor(rows), gains[0:1, :])
        grad_low[span, :] = (grad_mixed[span, :] + grad).astype(jnp.bfloat16)
        gain_total = gain_here if gain_total is None else gain_total + gain_here
    extra = grad_low.shape[0] - sz.rows
    at_row = lax.broadcasted_iota(jnp.int32, (extra, sz.width), 0)
    shares = jnp.where(at_row == 0, gain_total, jnp.where(at_row == 1, gain_b[...], 0.0))
    grad_low[sz.rows :, :] = shares.astype(jnp.bfloat16)
    scatter.finish()
    grads.finish()
    deliver.finish()
    for copy in copies:
        copy.wait()


def run_attn_back(
    sz, n_dp, grad_mixed, adapted, gains, cos_t, sin_t, begin, gain_b, q, k, v, lse, out, qkv,
    x, dgate, down_sum,
):
    f32, bf16, shape = jnp.float32, jnp.bfloat16, jax.ShapeDtypeStruct
    dma = pltpu.SemaphoreType.DMA
    heads_shape = (sz.heads, sz.seq_len, sz.head_dim)
    return pl.pallas_call(
        partial(attn_back_kernel, sz, n_dp),
        out_shape=[
            shape((sz.rows + 16, sz.width), bf16),
            shape(down_sum.shape[1:], f32),
            shape((sz.seq_len, sz.width), bf16),
            shape((sz.seq_len, qkv.shape[1]), bf16),
            shape(down_sum.shape, bf16),
        ],
        in_specs=[full_spec()] * 7 + [any_spec()] * 9,
        out_specs=[full_spec()] * 2 + [any_spec()] * 3,
        scratch_shapes=[
            pltpu.VMEM((sz.seq_len, sz.width), bf16),
            pltpu.VMEM(heads_shape, bf16),
            pltpu.VMEM(heads_shape, bf16),
            pltpu.VMEM(heads_shape, bf16),
            pltpu.VMEM((sz.heads, 1, sz.seq_len), f32),
            pltpu.VMEM(heads_shape, bf16),
            pltpu.VMEM((sz.seq_len, sz.head_dim), f32),
            pltpu.VMEM((sz.seq_len, sz.head_dim), f32),
            pltpu.VMEM((sz.seq_len, qkv.shape[1]), bf16),
            pltpu.VMEM((sz.heads * sz.head_dim, sz.width), bf16),
            pltpu.VMEM(qkv.shape, bf16),
            dma((5,)),
            dma((out.shape[0],)),
            dma((2 + sz.n_context,)),
        ]
        + Gather.scratch(sz)
        + Scatter.scratch(sz)
        + GradRing.scratch(sz, n_dp, [sz.ff])
        + Deliver.scratch(sz, n_dp, [sz.ff]),
        compiler_params=pltpu.CompilerParams(
            collective_id=7, has_side_effects=True, vmem_limit_bytes=VMEM_BYTES
        ),
        cost_estimate=pl.CostEstimate(
            flops=4 * sz.seq_len * sz.width * qkv.shape[1], bytes_accessed=30 << 20, transcendentals=0
        ),
        name="attn_back",
    )(
        grad_mixed, adapted, gains, cos_t, sin_t, begin, gain_b, q, k, v, lse, out, qkv,
        slot_columns(sz, n_dp, x), dgate, down_sum,
    )


class PlaneRows:
    @staticmethod
    def scratch(n_dp):
        dma = pltpu.SemaphoreType.DMA
        return [dma((n_dp - 1,)), dma((n_dp - 1,)), dma((n_dp,)), dma((n_dp,))]

    def __init__(self, place, ring, own, landed, refs):
        self.place, self.ring, self.own, self.landed = place, ring, own, landed
        self.send, self.recv, self.near_send, self.near_recv = refs
        self.ahead = 1 - 2 * place.ctx

    def slot(self, offset, ctx):
        return self.landed.at[self.ring.index(offset) * self.place.sz.n_context + ctx]

    def source(self, s):
        return self.own if s == 0 else self.slot(-self.ahead * s, self.place.ctx)

    def hop(self, s):
        return pltpu.make_async_remote_copy(
            src_ref=self.source(s),
            dst_ref=self.slot(-self.ahead * s, self.place.ctx),
            send_sem=self.send.at[s],
            recv_sem=self.recv.at[s],
            device_id=self.ring.device(self.ahead),
            device_id_type=MESH,
        )

    def near(self, s):
        return pltpu.make_async_remote_copy(
            src_ref=self.source(s),
            dst_ref=self.slot(-self.ahead * s, self.place.ctx),
            send_sem=self.near_send.at[s],
            recv_sem=self.near_recv.at[s],
            device_id=self.place.sibling(),
            device_id_type=MESH,
        )

    def start(self):
        self.hop(0).start()
        self.near(0).start()

    def step(self, s):
        ref = self.slot(-self.ahead * (s + 1), self.place.ctx)
        pltpu.make_async_remote_copy(
            src_ref=ref,
            dst_ref=ref,
            send_sem=self.send.at[s],
            recv_sem=self.recv.at[s],
            device_id=self.place.sibling(),
            device_id_type=MESH,
        ).wait_recv()
        if s + 1 < self.ring.count - 1:
            self.hop(s + 1).start()
        self.near(s + 1).start()

    def wait_near(self, s):
        ref = self.slot(self.ahead * s, 1 - self.place.ctx)
        pltpu.make_async_remote_copy(
            src_ref=ref,
            dst_ref=ref,
            send_sem=self.near_send.at[s],
            recv_sem=self.near_recv.at[s],
            device_id=self.place.sibling(),
            device_id_type=MESH,
        ).wait_recv()

    def finish(self):
        for s in range(self.ring.count):
            if s < self.ring.count - 1:
                self.hop(s).wait_send()
            self.near(s).wait_send()


class LineSum:
    @staticmethod
    def scratch(sz, parts, chunk):
        dma, bf16 = pltpu.SemaphoreType.DMA, jnp.bfloat16
        far = pltpu.VMEM((max(sz.half - 1, 1), parts, chunk, sz.width), bf16)
        one = pltpu.VMEM((parts, chunk, sz.width), bf16)
        kinds = 2 * sz.half - 1
        return [far, far, one, one, one, far, dma((kinds, parts)), dma((kinds, parts))]

    def __init__(self, place, total, parts, refs):
        self.place, self.total, self.parts = place, total, parts
        (self.out, self.got, self.sum, self.cross, self.done, self.back, self.send, self.recv) = refs
        self.chunk = self.sum.shape[1]

    def rows(self, part, k):
        first = (part * self.parts + k) * self.chunk
        return pl.ds(pl.multiple_of(first, self.chunk), self.chunk)

    def copy(self, src, dst, kind, k, device):
        return pltpu.make_async_remote_copy(
            src_ref=src,
            dst_ref=dst,
            send_sem=self.send.at[kind, k],
            recv_sem=self.recv.at[kind, k],
            device_id=device,
            device_id_type=MESH,
        )

    def spread(self, q, k):
        place = self.place
        device = place.device(place.ahead(q), place.ctx)
        return self.copy(self.out.at[q - 1, k], self.got.at[q - 1, k], q, k, device)

    def swap(self, k):
        return self.copy(self.sum.at[k], self.cross.at[k], 0, k, other_group(self.place))

    def collect(self, q, k):
        place = self.place
        device = place.device(place.ahead(q), place.ctx)
        return self.copy(
            self.done.at[k], self.back.at[q - 1, k], place.sz.half - 1 + q, k, device
        )

    def start(self, k):
        for q in range(1, self.place.sz.half):
            rows = self.rows(self.place.ahead(q), k)
            self.out[q - 1, k] = self.total[rows, :].astype(jnp.bfloat16)
            self.spread(q, k).start()

    def cross_over(self, k):
        value = self.total[self.rows(self.place.part, k), :]
        for q in range(1, self.place.sz.half):
            self.spread(q, k).wait_recv()
            value = value + self.got[q - 1, k].astype(jnp.float32)
        self.sum[k] = value.astype(jnp.bfloat16)
        self.swap(k).start()

    def share(self, k):
        self.swap(k).wait_recv()
        value = self.sum[k].astype(jnp.float32) + self.cross[k].astype(jnp.float32)
        self.done[k] = value.astype(jnp.bfloat16)
        for q in range(1, self.place.sz.half):
            self.collect(q, k).start()
        self.total[self.rows(self.place.part, k), :] = self.done[k].astype(jnp.float32)

    def complete(self, k):
        for q in range(1, self.place.sz.half):
            self.collect(q, k).wait_recv()
            rows = self.rows(self.place.behind(q), k)
            self.total[rows, :] = self.back[q - 1, k].astype(jnp.float32)

    def finish(self):
        for k in range(self.parts):
            self.swap(k).wait_send()
            for q in range(1, self.place.sz.half):
                self.spread(q, k).wait_send()
                self.collect(q, k).wait_send()


SUM_PARTS = 2


def grads_kernel(sz, n_dp, count, *refs):
    n_in = 4 + 2 * count
    gate_sum, low, joined, adapter = refs[:4]
    xs, ys = refs[4 : 4 + count], refs[4 + count : n_in]
    outs = refs[n_in : n_in + 1 + count]
    embed_grad, adapter_out, gains_out, landed = refs[n_in + 1 + count : n_in + 5 + count]
    refs = refs[n_in + 5 + count :]

    def take(n):
        nonlocal refs
        head, refs = refs[:n], refs[n:]
        return head

    ring_refs, deliver_refs = take(3 * count + 5), take(count + 4)
    plane_refs, sum_refs = take(4), take(8)
    adapter_grad, d_s, j_s, weight_s, rows_s, swap_in = refs[:6]
    d_sem, j_sem, weight_sem, swap_sem, out_sem = refs[6:]
    place = Place(sz)
    ring = Ring(place, n_dp)
    grads = GradRing(sz, place, ring, xs, ys, ring_refs)
    deliver = Deliver(sz, place, deliver_refs)
    plane = PlaneRows(place, ring, low, landed, plane_refs)
    line = LineSum(place, adapter_grad, SUM_PARTS, sum_refs)
    other = other_group(place)
    grads.start()
    weight_load = [
        pltpu.make_async_copy(
            adapter.at[adapter.shape[0] // 2 + b, pl.ds(0, weight_s.shape[0])], weight_s, weight_sem
        )
        for b in range(adapter.shape[0] // 2)
    ]
    weight_load[0].start()
    place.enter([ring.device(1), ring.device(n_dp - 1), other], deliver.greet())
    plane.start()
    give_rows = pl.ds(pl.multiple_of((1 - place.group) * sz.block, sz.block), sz.block)
    keep_rows = pl.ds(pl.multiple_of(place.group * sz.block, sz.block), sz.block)
    swap = pltpu.make_async_remote_copy(
        src_ref=low.at[give_rows],
        dst_ref=swap_in,
        send_sem=swap_sem.at[0],
        recv_sem=swap_sem.at[1],
        device_id=other,
        device_id_type=MESH,
    )
    swap.start()
    deliver.start(0, [gate_sum.at[way] for way in range(sz.n_context)])

    def ring_step():
        if grads.left():
            w, complete = grads.step()
            if complete:
                deliver.start(1 + w, [grads.result(w, way) for way in range(sz.n_context)])

    depth = joined.shape[2]

    def batch(ctx):
        copies = []
        for d in range(n_dp):
            at = d * sz.n_context + ctx
            rows = pl.ds(d * sz.rows, sz.rows)
            copies.append(
                pltpu.make_async_copy(landed.at[at, pl.ds(0, sz.rows)], d_s.at[rows], d_sem.at[d, 0])
            )
            copies.append(pltpu.make_async_copy(joined.at[at], j_s.at[rows], j_sem.at[d]))
            copies.append(
                pltpu.make_async_copy(
                    landed.at[at, pl.ds(sz.rows, 16)],
                    d_s.at[pl.ds(n_dp * sz.rows + 16 * d, 16)],
                    d_sem.at[d, 1],
                )
            )
        return copies

    def product(ctx, first):
        copies = batch(ctx)
        for copy in copies:
            copy.start()
        for copy in copies:
            copy.wait()
        chunk = sz.width // 4
        for n in range(4):
            cols = slice(n * chunk, (n + 1) * chunk)
            value = tn_dot(j_s[...], d_s[: n_dp * sz.rows, cols])
            tail = d_s[n_dp * sz.rows : n_dp * sz.rows + 16, cols].astype(jnp.float32)
            for d in range(1, n_dp):
                at = n_dp * sz.rows + 16 * d
                tail = tail + d_s[at : at + 16, cols].astype(jnp.float32)
            if first:
                adapter_grad[:depth, cols] = value
                adapter_grad[depth : depth + 16, cols] = tail
            else:
                adapter_grad[:depth, cols] += value
                adapter_grad[depth : depth + 16, cols] += tail

    own = pltpu.make_async_copy(low, landed.at[place.dp * sz.n_context + place.ctx], d_sem.at[0, 0])
    own.start()
    rest = adapter_grad.shape[0] - depth - 16
    if rest:
        adapter_grad[depth + 16 :, :] = jnp.zeros((rest, sz.width), jnp.float32)
    for s in range(n_dp - 1):
        ring_step()
        plane.step(s)
    own.wait()
    product(place.ctx, True)
    for s in range(n_dp):
        plane.wait_near(s)
    product(1 - place.ctx, False)
    for k in range(SUM_PARTS):
        line.start(k)
    ring_step()
    swap.wait()
    rows_s[place.group] = low[keep_rows, :]
    rows_s[1 - place.group] = swap_in[...]
    rows = rows_s[...].reshape(sz.rows, sz.width)
    ring_step()
    for k in range(SUM_PARTS):
        line.cross_over(k)
    ring_step()
    for b, copy in enumerate(weight_load):
        copy.wait()
        part = nt_dot(rows, weight_s[...]).reshape(sz.seqs, sz.block, weight_s.shape[0])
        embed_grad[:, :, b * weight_s.shape[0] : (b + 1) * weight_s.shape[0]] = part
        if b + 1 < len(weight_load):
            weight_load[b + 1].start()
    ring_step()
    for k in range(SUM_PARTS):
        line.share(k)
        ring_step()
    while grads.left():
        ring_step()
    for k in range(SUM_PARTS):
        line.complete(k)
    saves = [
        pltpu.make_async_copy(adapter_grad.at[pl.ds(0, depth)], adapter_out, out_sem.at[0]),
        pltpu.make_async_copy(adapter_grad.at[pl.ds(depth, 16)], gains_out, out_sem.at[1]),
    ]
    for copy in saves:
        copy.start()
    for w in range(1 + count):
        outs[w][...] = deliver.total(w)
    for copy in saves:
        copy.wait()
    grads.finish()
    deliver.finish()
    plane.finish()
    line.finish()


def run_grads(sz, n_dp, gate_sum, low, joined, adapter, xs, ys):
    count, bf16, f32, dma = len(xs), jnp.bfloat16, jnp.float32, pltpu.SemaphoreType.DMA
    shape = jax.ShapeDtypeStruct
    depth = sz.width // (n_dp * sz.n_context)
    wide = [y.shape[1] for y in ys]
    all_wide = [gate_sum.shape[2]] + wide
    slots, columns = joined.shape[0], joined.shape[2]
    unit = 16 * sz.half * SUM_PARTS
    total_rows = -(-(columns + 16) // unit) * unit
    return pl.pallas_call(
        partial(grads_kernel, sz, n_dp, count),
        out_shape=[shape((depth, n), f32) for n in all_wide]
        + [
            shape((sz.seqs, sz.block, sz.width), f32),
            shape((columns, sz.width), f32),
            shape((16, sz.width), f32),
            shape((slots,) + low.shape, bf16),
        ],
        in_specs=[any_spec(), full_spec()] + [any_spec()] * (2 + 2 * count),
        out_specs=[full_spec()] * (2 + count) + [any_spec()] * 3,
        scratch_shapes=GradRing.scratch(sz, n_dp, wide)
        + Deliver.scratch(sz, n_dp, all_wide)
        + PlaneRows.scratch(n_dp)
        + LineSum.scratch(sz, SUM_PARTS, total_rows // (sz.half * SUM_PARTS))
        + [
            pltpu.VMEM((total_rows, sz.width), f32),
            pltpu.VMEM((n_dp * (sz.rows + 16), sz.width), bf16),
            pltpu.VMEM((n_dp * sz.rows, columns), bf16),
            pltpu.VMEM((columns, sz.width), bf16),
            pltpu.VMEM((sz.seqs, sz.block, sz.width), bf16),
            pltpu.VMEM((sz.block, sz.width), bf16),
            dma((n_dp, 2)),
            dma((n_dp,)),
            dma,
            dma((2,)),
            dma((2,)),
        ],
        compiler_params=pltpu.CompilerParams(
            collective_id=8, has_side_effects=True, vmem_limit_bytes=VMEM_BYTES
        ),
        cost_estimate=pl.CostEstimate(
            flops=2 * sz.seq_len * sz.width * sum(wide), bytes_accessed=60 << 20, transcendentals=0
        ),
        name="grads",
    )(gate_sum, low, joined, adapter, *[slot_columns(sz, n_dp, x) for x in xs], *ys)


def shards(
    embedded,
    initial_state,
    cotangent,
    doc_ids,
    recurrences,
    adapter_weight,
    norm_gains,
    qkv_weight,
    output_head_weight,
    gate_up_weight,
    down_weight,
):
    n_dp = lax.axis_size("dp")
    n_tensor = lax.axis_size("tensor")
    n_context = lax.axis_size("context")
    dp_index = lax.axis_index("dp")
    t_index = lax.axis_index("tensor")
    ctx_index = lax.axis_index("context")
    seq_count, block_rows, model_width = embedded.shape
    seq_len = doc_ids.shape[1]
    half = n_tensor // seq_count
    group = t_index // half
    part = t_index % half
    heads_here = qkv_weight.shape[1]
    head_dim = qkv_weight.shape[2] // 3
    ff_here = down_weight.shape[0]
    def side_by_side(blocks):
        count, depth, columns = blocks.shape
        return blocks.transpose(1, 0, 2).reshape(depth, count * columns)

    def role_grad(grad, axis):
        piece = lax.psum_scatter(
            grad.astype(jnp.bfloat16), "dp", scatter_dimension=axis, tiled=True
        )
        low, high = jnp.split(piece, 2, axis=axis)
        give = [jnp.where(group == 0, low, high), jnp.where(group == 0, high, low)]
        back = [
            lax.ppermute(g, ("tensor", "context"), [(b, a) for a, b in perm])
            for g, perm in zip(give, role_perms)
        ]
        return back[0].astype(jnp.float32) + back[1].astype(jnp.float32)

    def gather_rows(rows):
        full = lax.all_gather(
            rows, ("tensor", "context"), axis=0, tiled=True, axis_index_groups=groups
        )
        split = full.reshape(half, n_context, seq_count, block_rows, model_width)
        return split.transpose(2, 0, 1, 3, 4).reshape(seq_len, model_width)

    sz = Sizes(
        n_tensor,
        n_context,
        seq_count,
        half,
        block_rows,
        n_context * block_rows,
        seq_count * block_rows,
        seq_len,
        model_width,
        heads_here,
        head_dim,
        ff_here,
    )
    adapter_block = adapter_weight.shape[0]
    gain_columns = norm_gains.shape[1]
    unit = 16 * half
    padded = -(-(adapter_block + 2) // unit) * unit
    adapter_rows = jnp.concatenate(
        [
            adapter_weight,
            jnp.pad(
                norm_gains,
                ((0, padded - adapter_block - 2), (0, model_width - gain_columns)),
            ),
        ],
        axis=0,
    )
    (
        adapter_all,
        out_blocks,
        qkv_use,
        gate_use,
        up_use,
        down_blocks,
        embed_rows,
        cot_rows,
        grad_ffn,
        embed_part,
        current,
    ) = run_weights(
        sz,
        n_dp,
        adapter_rows,
        adapter_block,
        [
            output_head_weight.reshape(heads_here * head_dim, -1),
            qkv_weight.reshape(qkv_weight.shape[0], -1),
            gate_up_weight[:, 0],
            gate_up_weight[:, 1],
            down_weight,
        ],
        [embedded, initial_state, cotangent],
    )
    qkv_use = qkv_use.reshape(model_width, -1)
    gate_use = gate_use.reshape(model_width, -1)
    up_use = up_use.reshape(model_width, -1)
    gains_full = (
        adapter_all[:, adapter_block : adapter_block + 2, :gain_columns]
        .transpose(1, 0, 2)
        .reshape(2, model_width)
    )
    if out_blocks.shape[2] % 128:
        out_blocks = side_by_side(out_blocks)[None]
        down_blocks = side_by_side(down_blocks)[None]
    gains_f = gains_full.astype(jnp.float32)

    cos_full, sin_full = rope_tables(seq_len, head_dim)
    own_seq = dp_index * seq_count + group
    docs = lax.dynamic_index_in_dim(doc_ids, own_seq, 0, keepdims=False)
    begin = jnp.sum((docs[None, :] < docs[:, None]).astype(jnp.int32), axis=1)[None, :]
    steps_own = lax.dynamic_index_in_dim(recurrences, own_seq, 0, keepdims=False) - BACK
    for step_index in range(MAXR - BACK):
        active = jnp.broadcast_to((step_index < steps_own).astype(jnp.float32), (1, model_width))
        current = run_round(
            sz, current, active, gains_f, cos_full, sin_full, begin, embed_part,
            adapter_all, qkv_use, out_blocks, gate_use, up_use, down_blocks,
        )
    detached = current
    (mixed_rows, adapted, feature_rows, query_hm, key_hm, value_hm, head_flat, lse, joined) = run_attn(
        sz, n_dp, True, detached, embed_part, gains_f, cos_full, sin_full, begin,
        adapter_all, qkv_use, out_blocks, embed_rows,
    )
    (current, ffn_input, gate_pre, up_pre, hidden) = run_ffn(
        sz, True, mixed_rows, detached, gains_f[:1], gains_f, gate_use, up_use, down_blocks
    )
    grad_mixed, gain_b, state_out, grad_gate, grad_up, down_sum = run_ffn_back(
        sz, n_dp, cot_rows, mixed_rows, gains_f, current, grad_ffn, gate_pre, up_pre,
        gate_use, up_use, down_blocks, hidden,
    )
    grad_low, down_t, grad_rows, grad_proj, gate_sum = run_attn_back(
        sz, n_dp, grad_mixed, adapted, gains_f, cos_full, sin_full, begin, gain_b,
        query_hm, key_hm, value_hm, lse, out_blocks, qkv_use, ffn_input, grad_gate, down_sum,
    )
    gate_s, up_s, qkv_s, out_t, embed_out, adapter_s, gains_rows, _ = run_grads(
        sz,
        n_dp,
        gate_sum,
        grad_low,
        joined,
        adapter_all,
        [ffn_input, feature_rows, grad_rows],
        [grad_up, grad_proj, head_flat],
    )
    place_at = (dp_index * n_context + ctx_index) * gain_columns
    gains_s = lax.dynamic_slice_in_dim(gains_rows[:2], place_at, gain_columns, 1)
    down_s = down_t.T
    out_s = out_t.T.reshape(heads_here, head_dim, -1)
    qkv_s = qkv_s.reshape(-1, heads_here, 3 * head_dim)
    gate_up_s = jnp.stack([gate_s, up_s], axis=1)
    return (state_out, embed_out, adapter_s, gains_s, qkv_s, out_s, gate_up_s, down_s)


def solution(mesh):
    placed = (
        P("dp", ("tensor", "context"), None),
        P("dp", ("tensor", "context"), None),
        P("dp", ("tensor", "context"), None),
        P(),
        P(),
        P(("dp", "context"), None),
        P(None, ("dp", "context")),
        P(("dp", "context"), "tensor", None),
        P("tensor", None, ("dp", "context")),
        P(("dp", "context"), None, "tensor"),
        P("tensor", ("dp", "context")),
    )
    return jax.shard_map(
        shards,
        mesh=mesh,
        in_specs=placed,
        out_specs=(
            P("dp", ("tensor", "context"), None),
            P("dp", ("tensor", "context"), None),
            P(("dp", "context"), None),
            P(None, ("dp", "context")),
            P(("dp", "context"), "tensor", None),
            P("tensor", None, ("dp", "context")),
            P(("dp", "context"), None, "tensor"),
            P("tensor", ("dp", "context")),
        ),
        check_vma=False,
    )
```

```python
from functools import partial
import math
from typing import NamedTuple

import jax
import jax.numpy as jnp
import numpy as np
from jax import lax
from jax.experimental import pallas as pl
from jax.experimental.pallas import tpu as pltpu
from jax.sharding import PartitionSpec as P

BACK = 1
MAXR = 4


rope_base = 50000.0
norm_eps = 1e-06
masked_score = -1e30


def rope_tables(seq_len, head_dim):
    freq_index = np.arange(head_dim // 2, dtype=np.float32)
    inv_freq = 1.0 / np.float32(rope_base) ** (np.float32(2.0) * freq_index / head_dim)
    angles = np.arange(seq_len, dtype=np.float32)[:, None] * inv_freq.astype(np.float32)[None, :]
    cos_t, sin_t = np.cos(angles), np.sin(angles)
    return (
        jnp.asarray(np.concatenate([cos_t, cos_t], axis=1), jnp.float32),
        jnp.asarray(np.concatenate([-sin_t, sin_t], axis=1), jnp.float32),
    )


MESH = pl.DeviceIdType.MESH
LOG2E = 1.4426950408889634
VMEM_BYTES = 62 << 20


class Sizes(NamedTuple):
    n_tensor: int
    n_context: int
    seqs: int
    half: int
    block: int
    tile: int
    rows: int
    seq_len: int
    width: int
    heads: int
    head_dim: int
    ff: int


def full_spec():
    return pl.BlockSpec(memory_space=pltpu.VMEM)


def any_spec():
    return pl.BlockSpec(memory_space=pl.ANY)


def nt_dot(a, b):
    return lax.dot_general(a, b, (((1,), (1,)), ((), ())), preferred_element_type=jnp.float32)


def tn_dot(a, b):
    return lax.dot_general(a, b, (((0,), (0,)), ((), ())), preferred_element_type=jnp.float32)


def nn_dot(a, b):
    return jnp.dot(a, b, preferred_element_type=jnp.float32)


class Place:
    def __init__(self, sz):
        t = lax.axis_index("tensor")
        self.sz = sz
        self.dp = lax.axis_index("dp")
        self.ctx = lax.axis_index("context")
        self.group = t // sz.half
        self.part = lax.rem(t, sz.half)

    def device(self, part, ctx):
        return (self.dp, self.group * self.sz.half + part, ctx)

    def ahead(self, q):
        return lax.rem(self.part + q, self.sz.half)

    def behind(self, q):
        return lax.rem(self.part + (self.sz.half - q), self.sz.half)

    def sibling(self):
        return self.device(self.part, 1 - self.ctx)

    def block(self, part, ctx, j):
        sz = self.sz
        first = ((part + j * sz.half) * sz.n_context + ctx) * sz.block
        return pl.ds(pl.multiple_of(first, sz.block), sz.block)

    def tile(self, q, j):
        sz = self.sz
        first = (self.ahead(q) + j * sz.half) * sz.tile
        return pl.ds(pl.multiple_of(first, sz.tile), sz.tile)

    def enter(self, others=(), more=0):
        barrier = pltpu.get_barrier_semaphore()
        for device in others:
            pl.semaphore_signal(barrier, inc=1, device_id=device, device_id_type=MESH)
        pl.semaphore_signal(
            barrier, inc=1, device_id=self.sibling(), device_id_type=MESH
        )
        for q in range(1, self.sz.half):
            pl.semaphore_signal(
                barrier,
                inc=1,
                device_id=self.device(self.ahead(q), self.ctx),
                device_id_type=MESH,
            )
        pl.semaphore_wait(barrier, self.sz.half + len(others) + more)


class Gather:
    @staticmethod
    def scratch(sz):
        kinds = 2 * sz.half - 1
        return [
            pltpu.SemaphoreType.DMA((kinds, sz.seqs)),
            pltpu.SemaphoreType.DMA((kinds, sz.seqs)),
        ]

    def __init__(self, place, ref, send, recv):
        self.place, self.ref, self.send, self.recv = place, ref, send, recv

    def copy(self, kind, j, rows):
        place, half = self.place, self.place.sz.half
        if 0 < kind < half:
            target = place.device(place.ahead(kind), place.ctx)
        else:
            target = place.sibling()
        return pltpu.make_async_remote_copy(
            src_ref=self.ref.at[rows],
            dst_ref=self.ref.at[rows],
            send_sem=self.send.at[kind, j],
            recv_sem=self.recv.at[kind, j],
            device_id=target,
            device_id_type=MESH,
        )

    def own(self, j):
        return self.place.block(self.place.part, self.place.ctx, j)

    def start(self, j):
        for q in range(1, self.place.sz.half):
            self.copy(q, j, self.own(j)).start()
        self.copy(0, j, self.own(j)).start()

    def wait_near(self, j):
        place = self.place
        self.copy(0, j, place.block(place.part, 1 - place.ctx, j)).wait_recv()

    def forward(self, q, j):
        place = self.place
        rows = place.block(place.behind(q), place.ctx, j)
        self.copy(q, j, rows).wait_recv()
        self.copy(place.sz.half - 1 + q, j, rows).start()

    def wait_far(self, q, j):
        place = self.place
        rows = place.block(place.behind(q), 1 - place.ctx, j)
        self.copy(place.sz.half - 1 + q, j, rows).wait_recv()

    def passed_on(self, j):
        place, half = self.place, self.place.sz.half
        for q in range(1, half):
            rows = place.block(place.behind(q), place.ctx, j)
            self.copy(half - 1 + q, j, rows).wait_send()

    def finish(self, forwards=True):
        for j in range(self.place.sz.seqs):
            for kind in range(self.place.sz.half):
                self.copy(kind, j, self.own(j)).wait_send()
            if forwards:
                self.passed_on(j)


class Scatter:
    @staticmethod
    def scratch(sz):
        kinds = 2 * sz.half - 1
        near = (sz.half, sz.seqs, sz.block, sz.width)
        far = (max(sz.half - 1, 1), sz.seqs, sz.block, sz.width)
        return [
            pltpu.VMEM((sz.tile, sz.width), jnp.float32),
            pltpu.VMEM(near, jnp.bfloat16),
            pltpu.VMEM(near, jnp.bfloat16),
            pltpu.VMEM(near, jnp.bfloat16),
            pltpu.VMEM(far, jnp.bfloat16),
            pltpu.VMEM(far, jnp.bfloat16),
            pltpu.SemaphoreType.DMA((kinds, sz.seqs)),
            pltpu.SemaphoreType.DMA((kinds, sz.seqs)),
        ]

    def __init__(self, place, part, mine, near_out, near_in, far_out, far_in, send, recv):
        self.place, self.part, self.mine = place, part, mine
        self.near_out, self.near_in = near_out, near_in
        self.far_out, self.far_in = far_out, far_in
        self.send, self.recv = send, recv

    def near(self, q, j):
        return pltpu.make_async_remote_copy(
            src_ref=self.near_out.at[q, j],
            dst_ref=self.near_in.at[q, j],
            send_sem=self.send.at[q, j],
            recv_sem=self.recv.at[q, j],
            device_id=self.place.sibling(),
            device_id_type=MESH,
        )

    def far(self, q, j):
        place = self.place
        return pltpu.make_async_remote_copy(
            src_ref=self.far_out.at[q - 1, j],
            dst_ref=self.far_in.at[q - 1, j],
            send_sem=self.send.at[place.sz.half - 1 + q, j],
            recv_sem=self.recv.at[place.sz.half - 1 + q, j],
            device_id=place.device(place.ahead(q), place.ctx),
            device_id_type=MESH,
        )

    def give(self, q, j):
        sz, ctx = self.place.sz, self.place.ctx
        mine = pl.ds(pl.multiple_of(ctx * sz.block, sz.block), sz.block)
        other = pl.ds(pl.multiple_of((1 - ctx) * sz.block, sz.block), sz.block)
        self.near_out[q, j] = self.part[other, :].astype(jnp.bfloat16)
        self.near(q, j).start()
        self.mine[q, j] = self.part[mine, :].astype(jnp.bfloat16)

    def onward(self, q, j):
        self.near(q, j).wait_recv()
        self.far_out[q - 1, j] = (
            self.mine[q, j].astype(jnp.float32) + self.near_in[q, j].astype(jnp.float32)
        ).astype(jnp.bfloat16)
        self.far(q, j).start()

    def total(self, j):
        self.near(0, j).wait_recv()
        total = self.mine[0, j].astype(jnp.float32) + self.near_in[0, j].astype(jnp.float32)
        for q in range(1, self.place.sz.half):
            self.far(q, j).wait_recv()
            total = total + self.far_in[q - 1, j].astype(jnp.float32)
        return total

    def finish(self):
        half = self.place.sz.half
        for j in range(self.place.sz.seqs):
            for q in range(half):
                self.near(q, j).wait_send()
            for q in range(1, half):
                self.far(q, j).wait_send()


def column_loads(blocks_ref, vmem_ref, sem):
    count, _, columns = blocks_ref.shape
    return [
        pltpu.make_async_copy(
            blocks_ref.at[b], vmem_ref.at[:, pl.ds(b * columns, columns)], sem.at[b]
        )
        for b in range(count)
    ]


def adapter_loads(blocks_ref, vmem_ref, sem):
    count, tops = sem.shape
    depth, columns = vmem_ref.shape[0] // tops, vmem_ref.shape[1] // count
    return [
        [
            pltpu.make_async_copy(
                blocks_ref.at[b, pl.ds(0, depth), pl.ds(n * columns, columns)],
                vmem_ref.at[pl.ds(b * depth, depth), pl.ds(n * columns, columns)],
                sem.at[n, b],
            )
            for b in range(tops)
        ]
        for n in range(count)
    ]


def rms_factor(rows):
    return lax.rsqrt(jnp.mean(rows * rows, axis=-1, keepdims=True) + norm_eps)


def turn(x, cos_t, sin_t):
    return x * cos_t + pltpu.roll(x, x.shape[-1] // 2, 1) * sin_t


def attn_kernel(sz, n_dp, keep, *refs):
    (latent, embed, gains, cos_t, sin_t, begin, adapter_hbm, qkv_hbm, out_hbm) = refs[:9]
    refs = refs[9:]
    if keep:
        embed_hbm, refs = refs[0], refs[1:]
    mixed = refs[0]
    refs = refs[1:]
    if keep:
        adapted_out, rows_out, q_out, k_out, v_out, head_out, lse_out, joined_out = refs[:8]
        refs = refs[8:]
    (wa, wqkv, wout, adapted, rows_s, q_s, k_s, v_s, head_s, lse_s) = refs[:10]
    load_a, load_qkv, load_out, keep_sem = refs[10:14]
    gather_refs = refs[14:16]
    scatter_refs = refs[16:24]
    if keep:
        joined_s, load_embed, x_send, x_recv = refs[24:]

    place = Place(sz)
    a_loads = adapter_loads(adapter_hbm, wa, load_a)
    qkv_load = pltpu.make_async_copy(qkv_hbm, wqkv, load_qkv)
    out_loads = column_loads(out_hbm, wout, load_out)
    for group in a_loads:
        for copy in group:
            copy.start()
    qkv_load.start()
    for copy in out_loads:
        copy.start()
    others = []
    if keep:
        ring = Ring(place, n_dp)
        t = lax.axis_index("tensor")
        embed_load = pltpu.make_async_copy(
            embed_hbm, joined_s.at[:, pl.ds(sz.width, sz.width)], load_embed
        )
        embed_load.start()
        plane = [(o, c) for o in range(n_dp) for c in range(2) if (o, c) != (0, 0)]

        def member(o, c):
            return (ring.index(o), t, place.ctx if c == 0 else 1 - place.ctx)

        def columns_to(o, c):
            to = member(o, c)
            depth = joined_out.shape[2]
            first = pl.multiple_of((to[0] * sz.n_context + to[2]) * depth, depth)
            return pltpu.make_async_remote_copy(
                src_ref=joined_s.at[:, pl.ds(first, depth)],
                dst_ref=joined_out.at[place.dp * sz.n_context + place.ctx],
                send_sem=x_send.at[o, c],
                recv_sem=x_recv.at[o, c],
                device_id=to,
                device_id_type=MESH,
            )

        def columns_from(o, c):
            ref = joined_out.at[
                ring.index(-o) * sz.n_context + (place.ctx if c == 0 else 1 - place.ctx)
            ]
            return pltpu.make_async_remote_copy(
                src_ref=ref,
                dst_ref=ref,
                send_sem=x_send.at[o, c],
                recv_sem=x_recv.at[o, c],
                device_id=place.sibling(),
                device_id_type=MESH,
            )

        others = [member(o, c) for o, c in plane if o]
    place.enter(others)
    gather = Gather(place, rows_s, *gather_refs)
    scatter = Scatter(place, *scatter_refs)

    low = latent[...].astype(jnp.bfloat16)
    columns = sz.width // len(a_loads)
    square = None
    for n, group in enumerate(a_loads):
        for copy in group:
            copy.wait()
        cols = pl.ds(n * columns, columns)
        chunk = nn_dot(low, wa[:, cols]) + embed[:, cols]
        adapted[:, cols] = chunk
        here = jnp.sum(chunk * chunk, axis=-1, keepdims=True)
        square = here if square is None else square + here
    factor = lax.rsqrt(square / sz.width + norm_eps)
    for j in range(sz.seqs):
        span = slice(j * sz.block, (j + 1) * sz.block)
        normed = (adapted[span, :] * factor[span]) * gains[0:1, :]
        rows_s[gather.own(j), :] = normed.astype(jnp.bfloat16)
        gather.start(j)

    qkv_load.wait()
    pair = min(2, sz.heads)
    d = sz.head_dim

    def project(q, j):
        rows = place.tile(q, j)
        x = rows_s[rows, :]
        cos_here, sin_here = cos_t[rows, :], sin_t[rows, :]
        for h0 in range(0, sz.heads, pair):
            proj = nn_dot(x, wqkv[:, 3 * d * h0 : 3 * d * (h0 + pair)])
            for h in range(pair):
                at = 3 * d * h
                q_s[h0 + h, rows, :] = turn(proj[:, at : at + d], cos_here, sin_here).astype(
                    jnp.bfloat16
                )
                k_s[h0 + h, rows, :] = turn(
                    proj[:, at + d : at + 2 * d], cos_here, sin_here
                ).astype(jnp.bfloat16)
                v_s[h0 + h, rows, :] = proj[:, at + 2 * d : at + 3 * d].astype(jnp.bfloat16)

    def attend(q, j):
        rows = place.tile(q, j)
        first = (place.ahead(q) + j * sz.half) * sz.tile
        length = (j + 1) * sz.half * sz.tile
        start = begin[:, pl.ds(pl.multiple_of(first, sz.tile), sz.tile)]
        key_at = lax.broadcasted_iota(jnp.int32, (length, sz.tile), 0)
        query_at = first + lax.broadcasted_iota(jnp.int32, (1, sz.tile), 1)
        allowed = (key_at >= start) & (key_at <= query_at)

        def head(h, carry):
            scores = nt_dot(k_s[h, 0:length, :], q_s[h, rows, :])
            scores = jnp.where(allowed, scores * (LOG2E / math.sqrt(d)), masked_score)
            top = jnp.max(scores, axis=0, keepdims=True)
            weight = jnp.exp2(scores - top)
            total = jnp.sum(weight, axis=0, keepdims=True)
            mixed_t = tn_dot(v_s[h, 0:length, :], weight.astype(jnp.bfloat16))
            result = jnp.transpose(mixed_t / total)
            head_s[rows, pl.ds(pl.multiple_of(h * d, d), d)] = result.astype(jnp.bfloat16)
            if keep:
                lse_s[h, :, rows] = top + jnp.log2(total)
            return carry

        lax.fori_loop(0, sz.heads, head, 0)

    def give(q, j):
        rows = place.tile(q, j)
        scatter.part[...] = nn_dot(head_s[rows, :], wout[...])
        scatter.give(q, j)

    copies = []

    def save(src, dst):
        copy = pltpu.make_async_copy(src, dst, keep_sem.at[len(copies)])
        copy.start()
        copies.append(copy)

    if keep:
        save(adapted, adapted_out)
        joined_s[:, : sz.width] = low
        embed_load.wait()
        for o, c in plane:
            columns_to(o, c).start()
        mine = place.dp * sz.n_context + place.ctx
        depth = joined_out.shape[2]
        save(
            joined_s.at[:, pl.ds(pl.multiple_of(mine * depth, depth), depth)], joined_out.at[mine]
        )
    far = range(1, sz.half)
    for j in range(sz.seqs):
        gather.wait_near(j)
        project(0, j)
    for copy in out_loads:
        copy.wait()
    for j in range(sz.seqs):
        for q in far:
            gather.forward(q, j)
        for q in far:
            gather.wait_far(sz.half - q, j)
            project(q, j)
        for q in far:
            attend(q, j)
            give(q, j)
        attend(0, j)
        for q in far:
            scatter.onward(q, j)
        give(0, j)
    if keep:
        for src, dst in ((rows_s, rows_out), (q_s, q_out), (k_s, k_out), (v_s, v_out)):
            save(src, dst)
        save(head_s, head_out)
        save(lse_s, lse_out)
    gather.finish()
    for j in range(sz.seqs):
        span = slice(j * sz.block, (j + 1) * sz.block)
        mixed[span, :] = adapted[span, :] + scatter.total(j)
    scatter.finish()
    if keep:
        for o, c in plane:
            columns_from(o, c).wait_recv()
            columns_to(o, c).wait_send()
    for copy in copies:
        copy.wait()


def run_attn(
    sz, n_dp, keep, latent, embed_part, gains, cos_t, sin_t, begin, adapter, qkv, out, *embed
):
    f32, bf16 = jnp.float32, jnp.bfloat16
    heads_shape = (sz.heads, sz.seq_len, sz.head_dim)
    shape = jax.ShapeDtypeStruct
    outs = [shape((sz.rows, sz.width), f32)]
    if keep:
        outs += [
            shape((sz.rows, sz.width), f32),
            shape((sz.seq_len, sz.width), bf16),
            shape(heads_shape, bf16),
            shape(heads_shape, bf16),
            shape(heads_shape, bf16),
            shape((sz.seq_len, sz.heads * sz.head_dim), bf16),
            shape((sz.heads, 1, sz.seq_len), f32),
            shape((adapter.shape[0], sz.rows, 2 * sz.width // adapter.shape[0]), bf16),
        ]
    scratch = [
        pltpu.VMEM((sz.width, sz.width), bf16),
        pltpu.VMEM(qkv.shape, bf16),
        pltpu.VMEM((sz.heads * sz.head_dim, sz.width), bf16),
        pltpu.VMEM((sz.rows, sz.width), f32),
        pltpu.VMEM((sz.seq_len, sz.width), bf16),
        pltpu.VMEM(heads_shape, bf16),
        pltpu.VMEM(heads_shape, bf16),
        pltpu.VMEM(heads_shape, bf16),
        pltpu.VMEM((sz.seq_len, sz.heads * sz.head_dim), bf16),
        pltpu.VMEM((sz.heads, 1, sz.seq_len), f32),
        pltpu.SemaphoreType.DMA((4, adapter.shape[0] // 2)),
        pltpu.SemaphoreType.DMA,
        pltpu.SemaphoreType.DMA((out.shape[0],)),
        pltpu.SemaphoreType.DMA((8,)),
    ]
    scratch += Gather.scratch(sz) + Scatter.scratch(sz)
    if keep:
        scratch += [
            pltpu.VMEM((sz.rows, 2 * sz.width), bf16),
            pltpu.SemaphoreType.DMA,
            pltpu.SemaphoreType.DMA((n_dp, 2)),
            pltpu.SemaphoreType.DMA((n_dp, 2)),
        ]
    flops = 2 * sz.rows * sz.width * sz.width + 2 * sz.seq_len * sz.width * qkv.shape[1]
    return pl.pallas_call(
        partial(attn_kernel, sz, n_dp, keep),
        out_shape=outs,
        in_specs=[full_spec()] * 6 + [any_spec()] * (3 + len(embed)),
        out_specs=[full_spec()] + [any_spec()] * (len(outs) - 1),
        scratch_shapes=scratch,
        compiler_params=pltpu.CompilerParams(
            collective_id=2 if keep else 1, has_side_effects=True, vmem_limit_bytes=VMEM_BYTES
        ),
        cost_estimate=pl.CostEstimate(
            flops=flops, bytes_accessed=20 << 20, transcendentals=0
        ),
        name="attn_keep" if keep else "attn_round",
    )(latent, embed_part, gains, cos_t, sin_t, begin, adapter, qkv, out, *embed)


def ffn_kernel(sz, keep, *refs):
    (mixed, latent, active, gains, gate_hbm, up_hbm, down_hbm, result) = refs[:8]
    refs = refs[8:]
    if keep:
        rows_out, gate_out, up_out, hidden_out = refs[:4]
        refs = refs[4:]
    wg, wu, wd, rows_s = refs[:4]
    refs = refs[4:]
    if keep:
        gate_s, up_s, hidden_s = refs[:3]
        refs = refs[3:]
    load_gu, load_down, keep_sem = refs[:3]
    gather_refs = refs[3:5]
    scatter_refs = refs[5:]

    place = Place(sz)
    gate_load = pltpu.make_async_copy(gate_hbm, wg, load_gu.at[0])
    up_load = pltpu.make_async_copy(up_hbm, wu, load_gu.at[1])
    down_loads = column_loads(down_hbm, wd, load_down)
    gate_load.start()
    up_load.start()
    for copy in down_loads:
        copy.start()
    place.enter()
    gather = Gather(place, rows_s, *gather_refs)
    scatter = Scatter(place, *scatter_refs)
    for j in range(sz.seqs):
        span = slice(j * sz.block, (j + 1) * sz.block)
        rows = mixed[span, :]
        normed = (rows * rms_factor(rows)) * gains[1:2, :]
        rows_s[gather.own(j), :] = normed.astype(jnp.bfloat16)
        gather.start(j)
    gate_load.wait()
    up_load.wait()
    for copy in down_loads:
        copy.wait()

    copies = []

    def save(src, dst):
        copy = pltpu.make_async_copy(src, dst, keep_sem.at[len(copies)])
        copy.start()
        copies.append(copy)

    def work(q, j):
        rows = place.tile(q, j)
        x = rows_s[rows, :]
        gate = nn_dot(x, wg[...])
        up = nn_dot(x, wu[...])
        hidden = (gate / (1.0 + jnp.exp(-gate)) * up).astype(jnp.bfloat16)
        if keep:
            gate_s[rows, :] = gate.astype(jnp.bfloat16)
            up_s[rows, :] = up.astype(jnp.bfloat16)
            hidden_s[rows, :] = hidden
        scatter.part[...] = nn_dot(hidden, wd[...])
        scatter.give(q, j)

    far = range(1, sz.half)
    for j in range(sz.seqs):
        gather.wait_near(j)
        work(0, j)
    for j in range(sz.seqs):
        for q in far:
            gather.forward(q, j)
        for q in far:
            gather.wait_far(sz.half - q, j)
            work(q, j)
        for q in far:
            scatter.onward(q, j)
    if keep:
        save(rows_s, rows_out)
        save(gate_s, gate_out)
        save(up_s, up_out)
        save(hidden_s, hidden_out)
    gather.finish()
    for j in range(sz.seqs):
        span = slice(j * sz.block, (j + 1) * sz.block)
        total = mixed[span, :] + scatter.total(j)
        if not keep:
            total = jnp.where(active[...] > 0, total, latent[span, :])
        result[span, :] = total
    scatter.finish()
    for copy in copies:
        copy.wait()


def run_ffn(sz, keep, mixed, latent, active, gains, gate, up, down):
    f32, bf16 = jnp.float32, jnp.bfloat16
    shape = jax.ShapeDtypeStruct
    outs = [shape((sz.rows, sz.width), f32)]
    if keep:
        outs += [
            shape((sz.seq_len, sz.width), bf16),
            shape((sz.seq_len, sz.ff), bf16),
            shape((sz.seq_len, sz.ff), bf16),
            shape((sz.seq_len, sz.ff), bf16),
        ]
    scratch = [
        pltpu.VMEM(gate.shape, bf16),
        pltpu.VMEM(up.shape, bf16),
        pltpu.VMEM((sz.ff, sz.width), bf16),
        pltpu.VMEM((sz.seq_len, sz.width), bf16),
    ]
    if keep:
        scratch += [pltpu.VMEM((sz.seq_len, sz.ff), bf16)] * 3
    scratch += [
        pltpu.SemaphoreType.DMA((2,)),
        pltpu.SemaphoreType.DMA((down.shape[0],)),
        pltpu.SemaphoreType.DMA((4,)),
    ]
    scratch += Gather.scratch(sz) + Scatter.scratch(sz)
    return pl.pallas_call(
        partial(ffn_kernel, sz, keep),
        out_shape=outs,
        in_specs=[full_spec()] * 4 + [any_spec()] * 3,
        out_specs=[full_spec()] + [any_spec()] * (len(outs) - 1),
        scratch_shapes=scratch,
        compiler_params=pltpu.CompilerParams(
            collective_id=4 if keep else 3, has_side_effects=True, vmem_limit_bytes=VMEM_BYTES
        ),
        cost_estimate=pl.CostEstimate(
            flops=6 * sz.seq_len * sz.width * sz.ff, bytes_accessed=20 << 20, transcendentals=0
        ),
        name="ffn_keep" if keep else "ffn_round",
    )(mixed, latent, active, gains, gate, up, down)


def round_kernel(sz, *refs):
    (latent, active, gains, cos_t, sin_t, begin) = refs[:6]
    (embed_hbm, adapter_hbm, qkv_hbm, out_hbm, gate_hbm, up_hbm, down_hbm, result) = refs[6:14]
    (wa, wqkv, wout, wg, wu, mixed, rows_s, q_s, k_s, v_s, head_s) = refs[14:25]
    load_embed, load_a, load_qkv, load_out, load_gu, load_down = refs[25:31]
    gather_refs, again_refs, scatter_refs = refs[31:33], refs[33:35], refs[35:43]

    place = Place(sz)
    embed_load = pltpu.make_async_copy(embed_hbm, mixed, load_embed)
    a_loads = adapter_loads(adapter_hbm, wa, load_a)
    qkv_load = pltpu.make_async_copy(qkv_hbm, wqkv, load_qkv)
    out_loads = column_loads(out_hbm, wout, load_out)
    gate_load = pltpu.make_async_copy(gate_hbm, wg, load_gu.at[0])
    up_load = pltpu.make_async_copy(up_hbm, wu, load_gu.at[1])
    wd = wa.at[pl.ds(0, sz.ff)]
    down_loads = column_loads(down_hbm, wd, load_down)
    embed_load.start()
    for group in a_loads:
        for copy in group:
            copy.start()
    qkv_load.start()
    for copy in out_loads:
        copy.start()
    place.enter()
    gather = Gather(place, rows_s, *gather_refs)
    again = Gather(place, rows_s, *again_refs)
    scatter = Scatter(place, *scatter_refs)

    low = latent[...].astype(jnp.bfloat16)
    columns = sz.width // len(a_loads)
    square = None
    embed_load.wait()
    for n, group in enumerate(a_loads):
        for copy in group:
            copy.wait()
        cols = pl.ds(n * columns, columns)
        chunk = nn_dot(low, wa[:, cols]) + mixed[:, cols]
        mixed[:, cols] = chunk
        here = jnp.sum(chunk * chunk, axis=-1, keepdims=True)
        square = here if square is None else square + here
    factor = lax.rsqrt(square / sz.width + norm_eps)
    for j in range(sz.seqs):
        span = slice(j * sz.block, (j + 1) * sz.block)
        normed = (mixed[span, :] * factor[span]) * gains[0:1, :]
        rows_s[gather.own(j), :] = normed.astype(jnp.bfloat16)
        gather.start(j)
    gate_load.start()
    up_load.start()
    for copy in down_loads:
        copy.start()
    qkv_load.wait()
    pair = min(2, sz.heads)
    d = sz.head_dim

    def project(q, j):
        rows = place.tile(q, j)
        x = rows_s[rows, :]
        cos_here, sin_here = cos_t[rows, :], sin_t[rows, :]
        for h0 in range(0, sz.heads, pair):
            proj = nn_dot(x, wqkv[:, 3 * d * h0 : 3 * d * (h0 + pair)])
            for h in range(pair):
                at = 3 * d * h
                q_s[h0 + h, rows, :] = turn(proj[:, at : at + d], cos_here, sin_here).astype(
                    jnp.bfloat16
                )
                k_s[h0 + h, rows, :] = turn(
                    proj[:, at + d : at + 2 * d], cos_here, sin_here
                ).astype(jnp.bfloat16)
                v_s[h0 + h, rows, :] = proj[:, at + 2 * d : at + 3 * d].astype(jnp.bfloat16)

    def attend(q, j):
        rows = place.tile(q, j)
        first = (place.ahead(q) + j * sz.half) * sz.tile
        length = (j + 1) * sz.half * sz.tile
        start = begin[:, pl.ds(pl.multiple_of(first, sz.tile), sz.tile)]
        key_at = lax.broadcasted_iota(jnp.int32, (length, sz.tile), 0)
        query_at = first + lax.broadcasted_iota(jnp.int32, (1, sz.tile), 1)
        allowed = (key_at >= start) & (key_at <= query_at)

        def head(h, carry):
            scores = nt_dot(k_s[h, 0:length, :], q_s[h, rows, :])
            scores = jnp.where(allowed, scores * (LOG2E / math.sqrt(d)), masked_score)
            top = jnp.max(scores, axis=0, keepdims=True)
            weight = jnp.exp2(scores - top)
            total = jnp.sum(weight, axis=0, keepdims=True)
            mixed_t = tn_dot(v_s[h, 0:length, :], weight.astype(jnp.bfloat16))
            result = jnp.transpose(mixed_t / total)
            head_s[rows, pl.ds(pl.multiple_of(h * d, d), d)] = result.astype(jnp.bfloat16)
            return carry

        lax.fori_loop(0, sz.heads, head, 0)

    def give(q, j):
        rows = place.tile(q, j)
        scatter.part[...] = nn_dot(head_s[rows, :], wout[...])
        scatter.give(q, j)

    far = range(1, sz.half)
    for j in range(sz.seqs):
        gather.wait_near(j)
        project(0, j)
    for copy in out_loads:
        copy.wait()
    for j in range(sz.seqs):
        for q in far:
            gather.forward(q, j)
        for q in far:
            gather.wait_far(sz.half - q, j)
            project(q, j)
        for q in far:
            attend(q, j)
            give(q, j)
        attend(0, j)
        gather.passed_on(j)
        for q in far:
            scatter.onward(q, j)
        give(0, j)
    gather.finish(forwards=False)
    for j in range(sz.seqs):
        span = slice(j * sz.block, (j + 1) * sz.block)
        rows = mixed[span, :] + scatter.total(j)
        mixed[span, :] = rows
        normed = (rows * rms_factor(rows)) * gains[1:2, :]
        rows_s[again.own(j), :] = normed.astype(jnp.bfloat16)
        again.start(j)
    scatter.finish()
    gate_load.wait()
    up_load.wait()
    for copy in down_loads:
        copy.wait()

    def work(q, j):
        x = rows_s[place.tile(q, j), :]
        gate = nn_dot(x, wg[...])
        up = nn_dot(x, wu[...])
        hidden = (gate / (1.0 + jnp.exp(-gate)) * up).astype(jnp.bfloat16)
        scatter.part[...] = nn_dot(hidden, wd[...])
        scatter.give(q, j)

    for j in range(sz.seqs):
        again.wait_near(j)
        work(0, j)
    for j in range(sz.seqs):
        for q in far:
            again.forward(q, j)
        for q in far:
            again.wait_far(sz.half - q, j)
            work(q, j)
        for q in far:
            scatter.onward(q, j)
    again.finish()
    for j in range(sz.seqs):
        span = slice(j * sz.block, (j + 1) * sz.block)
        total = mixed[span, :] + scatter.total(j)
        result[span, :] = jnp.where(active[...] > 0, total, latent[span, :])
    scatter.finish()


def run_round(sz, latent, active, gains, cos_t, sin_t, begin, embed, adapter, qkv, out, gate, up, down):
    f32, bf16, dma = jnp.float32, jnp.bfloat16, pltpu.SemaphoreType.DMA
    heads_shape = (sz.heads, sz.seq_len, sz.head_dim)
    return pl.pallas_call(
        partial(round_kernel, sz),
        out_shape=jax.ShapeDtypeStruct((sz.rows, sz.width), f32),
        in_specs=[full_spec()] * 6 + [any_spec()] * 7,
        out_specs=full_spec(),
        scratch_shapes=[
            pltpu.VMEM((sz.width, sz.width), bf16),
            pltpu.VMEM(qkv.shape, bf16),
            pltpu.VMEM((sz.heads * sz.head_dim, sz.width), bf16),
            pltpu.VMEM(gate.shape, bf16),
            pltpu.VMEM(up.shape, bf16),
            pltpu.VMEM((sz.rows, sz.width), f32),
            pltpu.VMEM((sz.seq_len, sz.width), bf16),
            pltpu.VMEM(heads_shape, bf16),
            pltpu.VMEM(heads_shape, bf16),
            pltpu.VMEM(heads_shape, bf16),
            pltpu.VMEM((sz.seq_len, sz.heads * sz.head_dim), bf16),
            dma,
            dma((4, adapter.shape[0] // 2)),
            dma,
            dma((out.shape[0],)),
            dma((2,)),
            dma((down.shape[0],)),
        ]
        + Gather.scratch(sz)
        + Gather.scratch(sz)
        + Scatter.scratch(sz),
        compiler_params=pltpu.CompilerParams(
            collective_id=1, has_side_effects=True, vmem_limit_bytes=VMEM_BYTES
        ),
        cost_estimate=pl.CostEstimate(
            flops=8 * sz.seq_len * sz.width * sz.ff, bytes_accessed=40 << 20, transcendentals=0
        ),
        name="round",
    )(latent, active, gains, cos_t, sin_t, begin, embed, adapter, qkv, out, gate, up, down)


def other_group(place):
    return (place.dp, (1 - place.group) * place.sz.half + place.part, place.ctx)


class Ring:
    def __init__(self, place, n_dp):
        self.place, self.count = place, n_dp
        self.at = self.swap(place.dp)

    def swap(self, i):
        if self.count != 4:
            return i
        x, y = lax.rem(i, 2), i // 2
        return 2 * y + x + y - 2 * x * y

    def index(self, offset):
        return self.swap(lax.rem(self.at + offset + 2 * self.count, self.count))

    def device(self, offset):
        return (self.index(offset), lax.axis_index("tensor"), self.place.ctx)


def weights_kernel(sz, n_dp, *refs):
    count = 5
    adapter_in, blocks_in = refs[0], refs[1 : 1 + count]
    rows_in, refs = refs[1 + count : 4 + count], refs[4 + count :]
    adapter_out, blocks_out = refs[0], refs[1 : 1 + count]
    embed_out, cot_out, cot_all, embed_part, state_out = refs[1 + count : 6 + count]
    refs = refs[6 + count :]
    (move_send, move_recv, ring_send, ring_recv, a_send, a_recv, x_send, x_recv, own_sem) = refs[:9]
    embed_s, state_s, weight_s, swap_send, swap_recv, keep_sem, weight_sem = refs[9:16]
    gather_refs = refs[16:]
    place = Place(sz)
    ring = Ring(place, n_dp)
    t = lax.axis_index("tensor")
    ctx, part, half, n_c = place.ctx, place.part, sz.half, sz.n_context
    role = part * n_c + ctx
    at_home = role == t
    steps = n_dp - 1
    sub = adapter_in.shape[0] // half
    ahead = 1 - 2 * ctx

    def holder(g):
        return (place.dp, g * half + t // n_c, lax.rem(t, n_c))

    barrier = pltpu.get_barrier_semaphore()

    def greet(device):
        pl.semaphore_signal(barrier, inc=1, device_id=device, device_id_type=MESH)

    greet(ring.device(1))
    greet(ring.device(n_dp - 1))
    greet(place.sibling())
    for q in range(1, half):
        greet(place.device(place.ahead(q), ctx))
    for c in range(n_c):
        pl.when(jnp.logical_not(at_home & (ctx == c)))(
            lambda c=c: greet((place.dp, role, c))
        )
    other = other_group(place)
    greet(other)
    waits = 3 + half + sz.seqs - jnp.where(at_home, 1, 0)
    pl.semaphore_wait(barrier, waits)

    own_at = pl.ds(pl.multiple_of(place.group * sz.block, sz.block), sz.block)
    other_at = pl.ds(pl.multiple_of((1 - place.group) * sz.block, sz.block), sz.block)
    rows_to = (embed_s, state_s, cot_out)

    def swap(i):
        return pltpu.make_async_remote_copy(
            src_ref=rows_in[i].at[1 - place.group],
            dst_ref=rows_to[i].at[own_at],
            send_sem=swap_send.at[i],
            recv_sem=swap_recv.at[i],
            device_id=other,
            device_id_type=MESH,
        )

    def swapped(i):
        ref = rows_to[i].at[other_at]
        return pltpu.make_async_remote_copy(
            src_ref=ref,
            dst_ref=ref,
            send_sem=swap_send.at[i],
            recv_sem=swap_recv.at[i],
            device_id=other,
            device_id_type=MESH,
        )

    def keep(i):
        return pltpu.make_async_copy(
            rows_in[i].at[place.group], rows_to[i].at[own_at], keep_sem.at[i]
        )

    for i in range(3):
        keep(i).start()
    gather = Gather(place, cot_all, *gather_refs)

    def own_rows_of(j):
        return pltpu.make_async_copy(
            cot_out.at[pl.ds(j * sz.block, sz.block)], cot_all.at[gather.own(j)], keep_sem.at[3 + j]
        )

    def move(w, g):
        slot = place.dp * n_c + ctx
        return pltpu.make_async_remote_copy(
            src_ref=blocks_in[w],
            dst_ref=blocks_out[w].at[slot],
            send_sem=move_send.at[w, g],
            recv_sem=move_recv.at[w, ctx],
            device_id=holder(g),
            device_id_type=MESH,
        )

    def stay(w):
        return pltpu.make_async_copy(
            blocks_in[w], blocks_out[w].at[place.dp * n_c + ctx], own_sem.at[w]
        )

    def moved(w, c):
        slot = place.dp * n_c + c
        arrival = pltpu.make_async_remote_copy(
            src_ref=blocks_in[w],
            dst_ref=blocks_out[w].at[slot],
            send_sem=move_send.at[w, 0],
            recv_sem=move_recv.at[w, c],
            device_id=place.sibling(),
            device_id_type=MESH,
        )
        here = at_home & (ctx == c)
        pl.when(here)(lambda: stay(w).wait())
        pl.when(jnp.logical_not(here))(lambda: arrival.wait_recv())

    def adapter_rows(offset, c, p):
        return adapter_out.at[
            ring.index(offset) * n_c + c, pl.ds(pl.multiple_of(p * sub, sub), sub)
        ]

    own_rows = adapter_in.at[pl.ds(pl.multiple_of(part * sub, sub), sub)]

    def around(s):
        rows = adapter_rows(-ahead * s, ctx, part)
        return pltpu.make_async_remote_copy(
            src_ref=own_rows if s == 0 else rows,
            dst_ref=rows,
            send_sem=a_send.at[s],
            recv_sem=a_recv.at[s],
            device_id=ring.device(ahead),
            device_id_type=MESH,
        )

    def across(kind, s):
        offset = -ahead * s
        if kind < half:
            dst = adapter_rows(offset, ctx, part)
            src = own_rows if s == 0 else dst
        else:
            src = dst = adapter_rows(offset, ctx, place.behind(kind - half + 1))
        target = place.device(place.ahead(kind), ctx) if 0 < kind < half else place.sibling()
        return pltpu.make_async_remote_copy(
            src_ref=src,
            dst_ref=dst,
            send_sem=x_send.at[kind, s],
            recv_sem=x_recv.at[kind, s],
            device_id=target,
            device_id_type=MESH,
        )

    def crossed(kind, s):
        if kind == 0:
            rows = adapter_rows(ahead * s, 1 - ctx, part)
        elif kind < half:
            rows = adapter_rows(-ahead * s, ctx, place.behind(kind))
        else:
            rows = adapter_rows(ahead * s, 1 - ctx, place.behind(kind - half + 1))
        return pltpu.make_async_remote_copy(
            src_ref=rows,
            dst_ref=rows,
            send_sem=x_send.at[kind, s],
            recv_sem=x_recv.at[kind, s],
            device_id=place.sibling(),
            device_id_type=MESH,
        )

    def hop(w, way, s):
        offset = -s if way == 0 else s
        rows = blocks_out[w].at[ring.index(offset) * n_c + way]
        return pltpu.make_async_remote_copy(
            src_ref=rows,
            dst_ref=rows,
            send_sem=ring_send.at[w, way, s],
            recv_sem=ring_recv.at[w, way, s],
            device_id=ring.device(1 if way == 0 else n_dp - 1),
            device_id_type=MESH,
        )

    def hopped(w, way, s):
        offset = -(s + 1) if way == 0 else s + 1
        rows = blocks_out[w].at[ring.index(offset) * n_c + way]
        return pltpu.make_async_remote_copy(
            src_ref=rows,
            dst_ref=rows,
            send_sem=ring_send.at[w, way, s],
            recv_sem=ring_recv.at[w, way, s],
            device_id=ring.device(1),
            device_id_type=MESH,
        )

    around(0).start()
    own = pltpu.make_async_copy(own_rows, adapter_rows(0, ctx, part), own_sem.at[count])
    own.start()

    def start_move(w):
        for g in range(sz.seqs):
            here = at_home & (place.group == g)
            pl.when(jnp.logical_not(here))(lambda w=w, g=g: move(w, g).start())
        pl.when(at_home)(lambda w=w: stay(w).start())

    start_move(0)
    start_move(1)
    for kind in range(half):
        across(kind, 0).start()

    def adapter_step(s):
        if s < steps:
            arrival = pltpu.make_async_remote_copy(
                src_ref=own_rows,
                dst_ref=adapter_rows(-ahead * (s + 1), ctx, part),
                send_sem=a_send.at[s],
                recv_sem=a_recv.at[s],
                device_id=ring.device(1),
                device_id_type=MESH,
            )
            arrival.wait_recv()
            if s + 1 < steps:
                around(s + 1).start()
            for kind in range(half):
                across(kind, s + 1).start()

    def adapter_pass(s):
        for q in range(1, half):
            crossed(q, s).wait_recv()
            across(half - 1 + q, s).start()

    embed_save = pltpu.make_async_copy(embed_s, embed_out, keep_sem.at[3 + sz.seqs])
    todo = []
    for k in range(count + steps):
        for s in range(min(k, steps - 1), -1, -1):
            w = k - s
            if w < count:
                todo.append((w, s))
    done = 0
    for w, s in todo:
        for way in range(n_c):
            if s == 0:
                moved(w, way)
            else:
                hopped(w, way, s - 1).wait_recv()
            hop(w, way, s).start()
        if s == 0 and w + 2 < count:
            start_move(w + 2)
        if s == 0 and w == count - 2:
            for i in range(3):
                swap(i).start()
        if done < steps:
            adapter_step(done)
        if s == min(1, steps - 1) and w == count - 1:
            for i in range(3):
                keep(i).wait()
                swapped(i).wait_recv()
            for j in range(sz.seqs):
                own_rows_of(j).start()
            embed_save.start()
            for j in range(sz.seqs):
                own_rows_of(j).wait()
                gather.start(j)
            state_out[...] = state_s[...].astype(jnp.float32)
        done += 1
    for s in range(done, steps):
        adapter_step(s)
    for s in range(n_dp):
        adapter_pass(s)
    for j in range(sz.seqs):
        gather.wait_near(j)
        for q in range(1, half):
            gather.forward(q, j)
    for s in range(n_dp):
        crossed(0, s).wait_recv()
        for q in range(1, half):
            crossed(half - 1 + q, s).wait_recv()
    own.wait()
    slots, depth = adapter_out.shape[0], weight_s.shape[1]
    loads = [
        pltpu.make_async_copy(
            adapter_out.at[slots // 2 + b, pl.ds(0, depth)], weight_s.at[b % 2], weight_sem.at[b % 2]
        )
        for b in range(slots // 2)
    ]
    loads[0].start()
    for b, copy in enumerate(loads):
        if b + 1 < len(loads):
            loads[b + 1].start()
        copy.wait()
        part_here = nn_dot(embed_s[:, b * depth : (b + 1) * depth], weight_s[b % 2])
        if b:
            embed_part[...] += part_here
        else:
            embed_part[...] = part_here
    for w in range(count):
        for way in range(n_c):
            hopped(w, way, steps - 1).wait_recv()
    for j in range(sz.seqs):
        for q in range(1, half):
            gather.wait_far(q, j)
    gather.finish()
    embed_save.wait()
    for i in range(3):
        swap(i).wait_send()
    for w in range(count):
        for g in range(sz.seqs):
            here = at_home & (place.group == g)
            pl.when(jnp.logical_not(here))(lambda w=w, g=g: move(w, g).wait_send())
        for way in range(n_c):
            for s in range(steps):
                hop(w, way, s).wait_send()
    for s in range(steps):
        around(s).wait_send()
    for s in range(n_dp):
        for kind in range(2 * half - 1):
            across(kind, s).wait_send()


def run_weights(sz, n_dp, adapter, adapter_block, blocks, rows):
    bf16, f32 = jnp.bfloat16, jnp.float32
    slots = n_dp * sz.n_context
    outs = [jax.ShapeDtypeStruct((slots,) + a.shape, bf16) for a in [adapter] + blocks]
    outs += [
        jax.ShapeDtypeStruct((sz.rows, sz.width), bf16),
        jax.ShapeDtypeStruct((sz.rows, sz.width), bf16),
        jax.ShapeDtypeStruct((sz.seq_len, sz.width), bf16),
        jax.ShapeDtypeStruct((sz.rows, sz.width), f32),
        jax.ShapeDtypeStruct((sz.rows, sz.width), f32),
    ]
    count, steps, dma = len(blocks), n_dp - 1, pltpu.SemaphoreType.DMA
    kinds = 2 * sz.half - 1
    return pl.pallas_call(
        partial(weights_kernel, sz, n_dp),
        out_shape=outs,
        in_specs=[any_spec()] * (4 + count),
        out_specs=[any_spec()] * (4 + count) + [full_spec()] * 2,
        scratch_shapes=[
            dma((count, sz.seqs)),
            dma((count, sz.n_context)),
            dma((count, sz.n_context, steps)),
            dma((count, sz.n_context, steps)),
            dma((steps,)),
            dma((steps,)),
            dma((kinds, n_dp)),
            dma((kinds, n_dp)),
            dma((count + 1,)),
            pltpu.VMEM((sz.rows, sz.width), bf16),
            pltpu.VMEM((sz.rows, sz.width), bf16),
            pltpu.VMEM((2, adapter_block, sz.width), bf16),
            dma((3,)),
            dma((3,)),
            dma((4 + sz.seqs,)),
            dma((2,)),
        ]
        + Gather.scratch(sz),
        compiler_params=pltpu.CompilerParams(
            collective_id=5, has_side_effects=True, vmem_limit_bytes=VMEM_BYTES
        ),
        name="weights",
    )(adapter, *blocks, *rows)


def norm_back(grad, rows, factor, gain):
    unit = rows * factor
    weighted = grad * gain
    inner = jnp.mean(weighted * unit, axis=-1, keepdims=True)
    return factor * (weighted - unit * inner), jnp.sum(grad * unit, axis=0, keepdims=True)


class GradRing:
    @staticmethod
    def scratch(sz, n_dp, tasks, wide, own_rows=None):
        slots, ways, dma = n_dp * sz.n_context, sz.n_context, pltpu.SemaphoreType.DMA
        depth, bf16, count, last = sz.width // slots, jnp.bfloat16, len(wide), n_dp - 1
        own_rows = [True] * count if own_rows is None else own_rows
        hops = [[s for w, s in tasks if w == i] for i in range(count)]
        return (
            [pltpu.VMEM((sz.seq_len, n), bf16) for n, own in zip(wide, own_rows) if own]
            + [pltpu.VMEM((ways, depth, n) if 0 in h else (ways, 16, 128), bf16) for n, h in zip(wide, hops)]
            + [pltpu.VMEM((ways, min(max(h) + 1, last), depth, n), bf16) for n, h in zip(wide, hops)]
            + [
                pltpu.VMEM((2, ways, sz.seq_len, depth), bf16),
                dma((count,)),
                dma((2, ways)),
                dma((count, ways, last)),
                dma((count, ways, last)),
                dma((ways,)),
            ]
        )

    @staticmethod
    def size(wide, own_rows=None):
        return 2 * len(wide) + (len(wide) if own_rows is None else sum(own_rows)) + 6

    @staticmethod
    def all_tasks(n_dp, count):
        return [
            (k - s, s)
            for k in range(count + n_dp)
            for s in range(min(k, n_dp - 1), -1, -1)
            if k - s < count
        ]

    def __init__(self, sz, place, ring, tasks, xs, ys, refs, rows=None, given=None):
        count, refs = len(xs), list(refs)
        self.sz, self.place, self.ring, self.xs, self.count = sz, place, ring, xs, count
        self.tasks = tasks
        self.ys = [refs.pop(0) if ys[w] is not None else rows[w] for w in range(count)]
        self.first, self.held = refs[:count], refs[count : 2 * count]
        self.x_s, self.load_y, self.load_x, self.send, self.recv, load_given = refs[2 * count :]
        self.y_loads = [
            pltpu.make_async_copy(ys[w], self.ys[w], self.load_y.at[w])
            for w in range(count)
            if ys[w] is not None
        ]
        self.unread = {w: self.y_loads[i] for i, w in enumerate(
            w for w in range(count) if ys[w] is not None
        )}
        self.given = []
        if given is not None:
            self.given = [
                pltpu.make_async_copy(
                    given.at[way], self.held[0].at[way, tasks[0][1] - 1], load_given.at[way]
                )
                for way in range(sz.n_context)
            ]
        self.done = 0

    def start(self):
        for copy in self.y_loads + self.given:
            copy.start()
        for way in range(self.sz.n_context):
            self.x_load(0, way).start()

    def slot(self, way, s):
        return self.ring.index(-(s + 1) if way == 0 else s + 1) * self.sz.n_context + way

    def x_load(self, k, way):
        w, s = self.tasks[k]
        depth = self.x_s.shape[3]
        if self.xs[w].shape[0] == 1:
            at = pl.multiple_of(self.slot(way, s) * depth, depth)
            src = self.xs[w].at[0, :, pl.ds(at, depth)]
        else:
            src = self.xs[w].at[self.slot(way, s)]
        return pltpu.make_async_copy(src, self.x_s.at[k % 2, way], self.load_x.at[k % 2, way])

    def source(self, w, way, s):
        return self.first[w].at[way] if s == 0 else self.held[w].at[way, s - 1]

    def hop(self, w, way, s):
        return pltpu.make_async_remote_copy(
            src_ref=self.source(w, way, s),
            dst_ref=self.held[w].at[way, s],
            send_sem=self.send.at[w, way, s],
            recv_sem=self.recv.at[w, way, s],
            device_id=self.ring.device(1 if way == 0 else self.ring.count - 1),
            device_id_type=MESH,
        )

    def result(self, w, way):
        return self.source(w, way, self.ring.count - 1)

    def step(self):
        k = self.done
        self.done += 1
        w, s = self.tasks[k]
        ways = range(self.sz.n_context)
        if k + 1 < len(self.tasks):
            for way in ways:
                self.x_load(k + 1, way).start()
        if w in self.unread:
            self.unread.pop(w).wait()
        for way in ways:
            self.x_load(k, way).wait()
            value = tn_dot(self.x_s[k % 2, way], self.ys[w][...])
            if k == 0 and self.given:
                self.given[way].wait()
            elif s:
                self.hop(w, way, s - 1).wait_recv()
            if s:
                value = value + self.held[w][way, s - 1].astype(jnp.float32)
            ref = self.source(w, way, s)
            ref[...] = value.astype(jnp.bfloat16)
            if s < self.ring.count - 1:
                self.hop(w, way, s).start()
        return w, s == self.ring.count - 1

    def left(self):
        return len(self.tasks) - self.done

    def finish(self):
        for w, s in self.tasks:
            if s < self.ring.count - 1:
                for way in range(self.sz.n_context):
                    self.hop(w, way, s).wait_send()


class Deliver:
    @staticmethod
    def scratch(sz, n_dp, wide):
        depth, count, dma = sz.width // (n_dp * sz.n_context), len(wide), pltpu.SemaphoreType.DMA
        return [pltpu.VMEM((sz.seqs, depth, n), jnp.bfloat16) for n in wide] + [
            dma((count, sz.n_context)),
            dma((count, sz.seqs)),
            dma((count,)),
        ]

    def __init__(self, sz, place, refs):
        self.sz, self.place = sz, place
        self.landed = refs[:-3]
        self.send, self.recv, self.own = refs[-3:]
        self.count = len(self.landed)
        self.t = lax.axis_index("tensor")
        self.role = place.part * sz.n_context + place.ctx
        self.at_home = self.role == self.t
        self.sources = [None] * self.count

    def greet(self):
        sz, place = self.sz, self.place
        barrier = pltpu.get_barrier_semaphore()
        for g in range(sz.seqs):
            holder = (place.dp, g * sz.half + self.t // sz.n_context, lax.rem(self.t, sz.n_context))
            pl.when(jnp.logical_not(self.at_home & (place.group == g)))(
                lambda holder=holder: pl.semaphore_signal(
                    barrier, inc=1, device_id=holder, device_id_type=MESH
                )
            )
        return sz.n_context - jnp.where(self.at_home, 1, 0)

    def remote(self, w, way):
        return pltpu.make_async_remote_copy(
            src_ref=self.sources[w][way],
            dst_ref=self.landed[w].at[self.place.group],
            send_sem=self.send.at[w, way],
            recv_sem=self.recv.at[w, self.place.group],
            device_id=(self.place.dp, self.role, way),
            device_id_type=MESH,
        )

    def local(self, w, way):
        return pltpu.make_async_copy(
            self.sources[w][way], self.landed[w].at[self.place.group], self.own.at[w]
        )

    def start(self, w, sources):
        self.sources[w] = sources
        for way in range(self.sz.n_context):
            here = self.at_home & (self.place.ctx == way)
            pl.when(here)(lambda way=way: self.local(w, way).start())
            pl.when(jnp.logical_not(here))(lambda way=way: self.remote(w, way).start())

    def total(self, w):
        place = self.place
        for g in range(self.sz.seqs):
            ref = self.landed[w].at[g]
            arrival = pltpu.make_async_remote_copy(
                src_ref=ref,
                dst_ref=ref,
                send_sem=self.send.at[w, 0],
                recv_sem=self.recv.at[w, g],
                device_id=(place.dp, self.t, 1 - place.ctx),
                device_id_type=MESH,
            )
            here = self.at_home & (place.group == g)
            pl.when(here)(lambda: self.local(w, 0).wait())
            pl.when(jnp.logical_not(here))(lambda arrival=arrival: arrival.wait_recv())
        total = self.landed[w][0].astype(jnp.float32)
        for g in range(1, self.sz.seqs):
            total = total + self.landed[w][g].astype(jnp.float32)
        return total

    def finish(self):
        for w in range(self.count):
            for way in range(self.sz.n_context):
                here = self.at_home & (self.place.ctx == way)
                pl.when(jnp.logical_not(here))(lambda w=w, way=way: self.remote(w, way).wait_send())


def slot_columns(sz, n_dp, x):
    slots = n_dp * sz.n_context
    depth = sz.width // slots
    if depth % 128:
        return x.reshape(sz.seq_len, slots, depth).transpose(1, 0, 2)
    return x[None]


def ffn_back_kernel(sz, n_dp, *refs):
    (cot, mixed, gains) = refs[:3]
    (rows_hbm, gate_hbm, up_hbm, wg_hbm, wu_hbm, down_hbm) = refs[3:9]
    (x_hbm, normed_hbm, hidden_hbm) = refs[9:12]
    (grad_mixed, gain_grad, dgate_out, dup_out, down_sum, gate_part) = refs[12:18]
    (rows_s, gate_s, up_s, wg, wu, wd, load, load_down, keep_sem) = refs[18:27]
    scatter_refs, ring_refs = refs[27:35], refs[35:]
    place = Place(sz)
    ring = Ring(place, n_dp)
    grads = GradRing(
        sz, place, ring, ffn_back_tasks(n_dp), [x_hbm, normed_hbm], [hidden_hbm, None], ring_refs,
        rows=[None, gate_s],
    )
    grads.start()
    pairs = ((rows_hbm, rows_s), (gate_hbm, gate_s), (up_hbm, up_s), (wg_hbm, wg), (wu_hbm, wu))
    loads = [
        pltpu.make_async_copy(src, dst, load.at[i]) for i, (src, dst) in enumerate(pairs)
    ]
    down_loads = column_loads(down_hbm, wd, load_down)
    loads[0].start()
    for copy in down_loads + loads[1:]:
        copy.start()
    place.enter([ring.device(1), ring.device(n_dp - 1)])
    scatter = Scatter(place, *scatter_refs)
    grads.step()
    for copy in [loads[0]] + down_loads + loads[1:]:
        copy.wait()

    def work(q, j):
        rows = place.tile(q, j)
        dh = nt_dot(rows_s[rows, :], wd[...])
        gate = gate_s[rows, :].astype(jnp.float32)
        up = up_s[rows, :].astype(jnp.float32)
        sig = 1.0 / (1.0 + jnp.exp(-gate))
        dgate = (dh * up * sig * (1.0 + gate * (1.0 - sig))).astype(jnp.bfloat16)
        dup = (dh * gate * sig).astype(jnp.bfloat16)
        gate_s[rows, :] = dgate
        up_s[rows, :] = dup
        scatter.part[...] = nt_dot(dgate, wg[...]) + nt_dot(dup, wu[...])
        scatter.give(q, j)

    far = range(1, sz.half)
    for j in range(sz.seqs):
        for q in far:
            work(q, j)
        if j:
            for q in far:
                scatter.onward(q, j - 1)
    work(0, 0)
    for q in far:
        scatter.onward(q, sz.seqs - 1)
    grads.step()
    for j in range(1, sz.seqs):
        work(0, j)
    grads.step()
    copies = [
        pltpu.make_async_copy(gate_s, dgate_out, keep_sem.at[0]),
        pltpu.make_async_copy(up_s, dup_out, keep_sem.at[1]),
    ]
    for copy in copies:
        copy.start()
    gain_total = None
    for j in range(sz.seqs):
        span = slice(j * sz.block, (j + 1) * sz.block)
        rows = mixed[span, :]
        grad, gain_here = norm_back(scatter.total(j), rows, rms_factor(rows), gains[1:2, :])
        grad_mixed[span, :] = cot[span, :].astype(jnp.float32) + grad
        gain_total = gain_here if gain_total is None else gain_total + gain_here
    gain_grad[...] = gain_total
    while grads.left():
        grads.step()
    for way in range(sz.n_context):
        grads.hop(1, way, 0).wait_recv()
        for i, (src, dst) in enumerate(
            ((grads.result(0, way), down_sum), (grads.held[1].at[way, 0], gate_part))
        ):
            copies.append(
                pltpu.make_async_copy(src, dst.at[way], keep_sem.at[2 + 2 * way + i])
            )
            copies[-1].start()
    scatter.finish()
    grads.finish()
    for copy in copies:
        copy.wait()


def ffn_back_tasks(n_dp):
    return [(0, 0), (0, 1), (1, 0)] + [(0, s) for s in range(2, n_dp)]


def run_ffn_back(sz, n_dp, cot, mixed, gains, rows, gate, up, wg, wu, down, normed, hidden):
    f32, bf16, shape = jnp.float32, jnp.bfloat16, jax.ShapeDtypeStruct
    dma = pltpu.SemaphoreType.DMA
    depth = sz.width // (n_dp * sz.n_context)
    return pl.pallas_call(
        partial(ffn_back_kernel, sz, n_dp),
        out_shape=[
            shape((sz.rows, sz.width), f32),
            shape((1, sz.width), f32),
            shape((sz.seq_len, sz.ff), bf16),
            shape((sz.seq_len, sz.ff), bf16),
            shape((sz.n_context, depth, sz.ff), bf16),
            shape((sz.n_context, depth, sz.ff), bf16),
        ],
        in_specs=[full_spec()] * 3 + [any_spec()] * 9,
        out_specs=[full_spec()] * 2 + [any_spec()] * 4,
        scratch_shapes=[
            pltpu.VMEM((sz.seq_len, sz.width), bf16),
            pltpu.VMEM((sz.seq_len, sz.ff), bf16),
            pltpu.VMEM((sz.seq_len, sz.ff), bf16),
            pltpu.VMEM(wg.shape, bf16),
            pltpu.VMEM(wu.shape, bf16),
            pltpu.VMEM((sz.ff, sz.width), bf16),
            dma((5,)),
            dma((down.shape[0],)),
            dma((2 + 2 * sz.n_context,)),
        ]
        + Scatter.scratch(sz)
        + GradRing.scratch(sz, n_dp, ffn_back_tasks(n_dp), [sz.ff, sz.ff], [True, False]),
        compiler_params=pltpu.CompilerParams(
            collective_id=6, has_side_effects=True, vmem_limit_bytes=VMEM_BYTES
        ),
        cost_estimate=pl.CostEstimate(
            flops=8 * sz.seq_len * sz.width * sz.ff, bytes_accessed=40 << 20, transcendentals=0
        ),
        name="ffn_back",
    )(
        cot, mixed, gains, rows, gate, up, wg, wu, down,
        slot_columns(sz, n_dp, rows), slot_columns(sz, n_dp, normed), hidden,
    )


def attn_back_kernel(sz, n_dp, *refs):
    (grad_mixed, adapted, gains, cos_t, sin_t, begin, gain_b, state) = refs[:8]
    (q_hbm, k_hbm, v_hbm, lse_hbm, out_hbm, qkv_hbm) = refs[8:14]
    (x_hbm, dgate_hbm, down_sum, gate_part) = refs[14:18]
    (grad_low, down_grad, gate_grad, state_out, rows_out, proj_out) = refs[18:24]
    (rows_s, q_s, k_s, v_s, lse_s, do_s, dk_s, dv_s, proj_s, wout, wqkv) = refs[24:35]
    (load, load_out, keep_sem, swap_out, swap_in, swap_sem) = refs[35:41]
    gather_refs, scatter_refs = refs[41:43], refs[43:51]
    ring_refs, deliver_refs = refs[51:60], refs[60:]
    place = Place(sz)
    ring = Ring(place, n_dp)
    tasks = [(0, s) for s in range(1, n_dp)]
    grads = GradRing(
        sz, place, ring, tasks, [x_hbm], [dgate_hbm], ring_refs, given=gate_part
    )
    deliver = Deliver(sz, place, deliver_refs)
    grads.start()
    pairs = ((q_hbm, q_s), (k_hbm, k_s), (v_hbm, v_s), (lse_hbm, lse_s), (qkv_hbm, wqkv))
    loads = [
        pltpu.make_async_copy(src, dst, load.at[i]) for i, (src, dst) in enumerate(pairs)
    ]
    out_loads = column_loads(out_hbm, wout, load_out)
    for copy in out_loads + loads:
        copy.start()
    targets = deliver.greet()
    other = other_group(place)
    place.enter([ring.device(1), ring.device(n_dp - 1), other], targets)
    gather = Gather(place, rows_s, *gather_refs)
    scatter = Scatter(place, *scatter_refs)
    for j in range(sz.seqs):
        span = slice(j * sz.block, (j + 1) * sz.block)
        rows_s[gather.own(j), :] = grad_mixed[span, :].astype(jnp.bfloat16)
        gather.start(j)
    grads.step()
    deliver.start(0, [down_sum.at[way] for way in range(sz.n_context)])
    give_rows = pl.ds(pl.multiple_of((1 - place.group) * sz.block, sz.block), sz.block)
    keep_rows = pl.ds(pl.multiple_of(place.group * sz.block, sz.block), sz.block)
    swap = pltpu.make_async_remote_copy(
        src_ref=swap_out,
        dst_ref=swap_in,
        send_sem=swap_sem.at[0],
        recv_sem=swap_sem.at[1],
        device_id=other,
        device_id_type=MESH,
    )
    swap_out[...] = state[give_rows, :].astype(jnp.bfloat16)
    state_out[place.group] = state[keep_rows, :]
    swap.start()
    for copy in out_loads:
        copy.wait()
    d = sz.head_dim

    def heads_grad(q, j):
        rows = place.tile(q, j)
        dhead = nt_dot(rows_s[rows, :], wout[...]).astype(jnp.bfloat16)
        for h in range(sz.heads):
            do_s[h, rows, :] = dhead[:, h * d : (h + 1) * d]

    far = range(1, sz.half)
    for j in range(sz.seqs):
        gather.wait_near(j)
        heads_grad(0, j)
    for copy in loads:
        copy.wait()
    for j in range(sz.seqs):
        if j == sz.seqs - 1:
            grads.step()
        for q in far:
            gather.forward(q, j)
        for q in far:
            gather.wait_far(sz.half - q, j)
            heads_grad(q, j)
    copies = [pltpu.make_async_copy(rows_s, rows_out, keep_sem.at[0])]
    copies[0].start()

    tiles = sz.n_tensor
    scale = 1.0 / math.sqrt(d)

    def head(h, carry):
        for i in reversed(range(tiles)):
            rows = slice(i * sz.tile, (i + 1) * sz.tile)
            length = (i + 1) * sz.tile
            keys, values = k_s[h, 0:length, :], v_s[h, 0:length, :]
            query, grad = q_s[h, rows, :], do_s[h, rows, :]
            start = begin[:, rows]
            key_at = lax.broadcasted_iota(jnp.int32, (length, sz.tile), 0)
            query_at = i * sz.tile + lax.broadcasted_iota(jnp.int32, (1, sz.tile), 1)
            allowed = (key_at >= start) & (key_at <= query_at)
            scores = nt_dot(keys, query)
            scores = jnp.where(allowed, scores * (LOG2E * scale), masked_score)
            probs = jnp.exp2(scores - lse_s[h, :, rows])
            dprobs = nt_dot(values, grad)
            inner = jnp.sum(probs * dprobs, axis=0, keepdims=True)
            dscores = (probs * (dprobs - inner)).astype(jnp.bfloat16)
            dv = nn_dot(probs.astype(jnp.bfloat16), grad)
            dk = nn_dot(dscores, query)
            if i == tiles - 1:
                dv_s[...] = dv
                dk_s[...] = dk
            else:
                dv_s[0:length, :] += dv
                dk_s[0:length, :] += dk
            dq = jnp.transpose(tn_dot(keys, dscores)) * scale
            cos_here, sin_here = cos_t[rows, :], sin_t[rows, :]
            proj_s[rows, pl.ds(pl.multiple_of(h * 3 * d, d), d)] = turn(
                dq, cos_here, -sin_here
            ).astype(jnp.bfloat16)
        dk = turn(dk_s[...] * scale, cos_t[...], -sin_t[...])
        proj_s[:, pl.ds(pl.multiple_of(h * 3 * d + d, d), d)] = dk.astype(jnp.bfloat16)
        proj_s[:, pl.ds(pl.multiple_of(h * 3 * d + 2 * d, d), d)] = dv_s[...].astype(jnp.bfloat16)
        return carry

    lax.fori_loop(0, sz.heads, head, 0)
    copies.append(pltpu.make_async_copy(proj_s, proj_out, keep_sem.at[1]))
    copies[1].start()

    def give(q, j):
        scatter.part[...] = nt_dot(proj_s[place.tile(q, j), :], wqkv[...])
        scatter.give(q, j)

    for j in range(sz.seqs):
        for q in far:
            give(q, j)
        if j:
            for q in far:
                scatter.onward(q, j - 1)
    give(0, 0)
    for q in far:
        scatter.onward(q, sz.seqs - 1)
    while grads.left():
        grads.step()
    deliver.start(1, [grads.result(0, way) for way in range(sz.n_context)])
    for j in range(1, sz.seqs):
        give(0, j)
    gather.finish()
    swap.wait()
    state_out[1 - place.group] = swap_in[...].astype(jnp.float32)
    down_grad[...] = deliver.total(0)
    gain_total = None
    for j in range(sz.seqs):
        span = slice(j * sz.block, (j + 1) * sz.block)
        rows = adapted[span, :]
        grad, gain_here = norm_back(scatter.total(j), rows, rms_factor(rows), gains[0:1, :])
        grad_low[span, :] = (grad_mixed[span, :] + grad).astype(jnp.bfloat16)
        gain_total = gain_here if gain_total is None else gain_total + gain_here
    extra = grad_low.shape[0] - sz.rows
    at_row = lax.broadcasted_iota(jnp.int32, (extra, sz.width), 0)
    shares = jnp.where(at_row == 0, gain_total, jnp.where(at_row == 1, gain_b[...], 0.0))
    grad_low[sz.rows :, :] = shares.astype(jnp.bfloat16)
    gate_grad[...] = deliver.total(1)
    scatter.finish()
    grads.finish()
    deliver.finish()
    for copy in copies:
        copy.wait()


def run_attn_back(
    sz, n_dp, grad_mixed, adapted, gains, cos_t, sin_t, begin, gain_b, state, q, k, v, lse, out,
    qkv, x, dgate, down_sum, gate_part,
):
    f32, bf16, shape = jnp.float32, jnp.bfloat16, jax.ShapeDtypeStruct
    dma = pltpu.SemaphoreType.DMA
    heads_shape = (sz.heads, sz.seq_len, sz.head_dim)
    return pl.pallas_call(
        partial(attn_back_kernel, sz, n_dp),
        out_shape=[
            shape((sz.rows + 16, sz.width), bf16),
            shape(down_sum.shape[1:], f32),
            shape(gate_part.shape[1:], f32),
            shape((sz.seqs, sz.block, sz.width), f32),
            shape((sz.seq_len, sz.width), bf16),
            shape((sz.seq_len, qkv.shape[1]), bf16),
        ],
        in_specs=[full_spec()] * 8 + [any_spec()] * 10,
        out_specs=[full_spec()] * 4 + [any_spec()] * 2,
        scratch_shapes=[
            pltpu.VMEM((sz.seq_len, sz.width), bf16),
            pltpu.VMEM(heads_shape, bf16),
            pltpu.VMEM(heads_shape, bf16),
            pltpu.VMEM(heads_shape, bf16),
            pltpu.VMEM((sz.heads, 1, sz.seq_len), f32),
            pltpu.VMEM(heads_shape, bf16),
            pltpu.VMEM((sz.seq_len, sz.head_dim), f32),
            pltpu.VMEM((sz.seq_len, sz.head_dim), f32),
            pltpu.VMEM((sz.seq_len, qkv.shape[1]), bf16),
            pltpu.VMEM((sz.heads * sz.head_dim, sz.width), bf16),
            pltpu.VMEM(qkv.shape, bf16),
            dma((5,)),
            dma((out.shape[0],)),
            dma((2,)),
            pltpu.VMEM((sz.block, sz.width), bf16),
            pltpu.VMEM((sz.block, sz.width), bf16),
            dma((2,)),
        ]
        + Gather.scratch(sz)
        + Scatter.scratch(sz)
        + GradRing.scratch(sz, n_dp, [(0, s) for s in range(1, n_dp)], [sz.ff])
        + Deliver.scratch(sz, n_dp, [sz.ff, sz.ff]),
        compiler_params=pltpu.CompilerParams(
            collective_id=7, has_side_effects=True, vmem_limit_bytes=VMEM_BYTES
        ),
        cost_estimate=pl.CostEstimate(
            flops=4 * sz.seq_len * sz.width * qkv.shape[1], bytes_accessed=30 << 20, transcendentals=0
        ),
        name="attn_back",
    )(
        grad_mixed, adapted, gains, cos_t, sin_t, begin, gain_b, state, q, k, v, lse, out, qkv,
        slot_columns(sz, n_dp, x), dgate, down_sum, gate_part,
    )


class PlaneRows:
    @staticmethod
    def scratch(n_dp):
        dma = pltpu.SemaphoreType.DMA
        return [dma((n_dp - 1,)), dma((n_dp - 1,)), dma((n_dp,)), dma((n_dp,))]

    def __init__(self, place, ring, own, landed, refs):
        self.place, self.ring, self.own, self.landed = place, ring, own, landed
        self.send, self.recv, self.near_send, self.near_recv = refs
        self.ahead = 1 - 2 * place.ctx

    def slot(self, offset, ctx):
        return self.landed.at[self.ring.index(offset) * self.place.sz.n_context + ctx]

    def source(self, s):
        return self.own if s == 0 else self.slot(-self.ahead * s, self.place.ctx)

    def hop(self, s):
        return pltpu.make_async_remote_copy(
            src_ref=self.source(s),
            dst_ref=self.slot(-self.ahead * s, self.place.ctx),
            send_sem=self.send.at[s],
            recv_sem=self.recv.at[s],
            device_id=self.ring.device(self.ahead),
            device_id_type=MESH,
        )

    def near(self, s):
        return pltpu.make_async_remote_copy(
            src_ref=self.source(s),
            dst_ref=self.slot(-self.ahead * s, self.place.ctx),
            send_sem=self.near_send.at[s],
            recv_sem=self.near_recv.at[s],
            device_id=self.place.sibling(),
            device_id_type=MESH,
        )

    def start(self):
        self.hop(0).start()
        self.near(0).start()

    def step(self, s):
        ref = self.slot(-self.ahead * (s + 1), self.place.ctx)
        pltpu.make_async_remote_copy(
            src_ref=ref,
            dst_ref=ref,
            send_sem=self.send.at[s],
            recv_sem=self.recv.at[s],
            device_id=self.place.sibling(),
            device_id_type=MESH,
        ).wait_recv()
        if s + 1 < self.ring.count - 1:
            self.hop(s + 1).start()
        self.near(s + 1).start()

    def wait_near(self, s):
        ref = self.slot(self.ahead * s, 1 - self.place.ctx)
        pltpu.make_async_remote_copy(
            src_ref=ref,
            dst_ref=ref,
            send_sem=self.near_send.at[s],
            recv_sem=self.near_recv.at[s],
            device_id=self.place.sibling(),
            device_id_type=MESH,
        ).wait_recv()

    def finish(self):
        for s in range(self.ring.count):
            if s < self.ring.count - 1:
                self.hop(s).wait_send()
            self.near(s).wait_send()


class LineSum:
    @staticmethod
    def scratch(sz, parts, chunk):
        dma, bf16 = pltpu.SemaphoreType.DMA, jnp.bfloat16
        far = pltpu.VMEM((max(sz.half - 1, 1), parts, chunk, sz.width), bf16)
        one = pltpu.VMEM((parts, chunk, sz.width), bf16)
        kinds = 2 * sz.half - 1
        return [far, far, one, one, one, far, dma((kinds, parts)), dma((kinds, parts))]

    def __init__(self, place, total, parts, refs):
        self.place, self.total, self.parts = place, total, parts
        (self.out, self.got, self.sum, self.cross, self.done, self.back, self.send, self.recv) = refs
        self.chunk = self.sum.shape[1]

    def rows(self, part, k):
        first = (part * self.parts + k) * self.chunk
        return pl.ds(pl.multiple_of(first, self.chunk), self.chunk)

    def copy(self, src, dst, kind, k, device):
        return pltpu.make_async_remote_copy(
            src_ref=src,
            dst_ref=dst,
            send_sem=self.send.at[kind, k],
            recv_sem=self.recv.at[kind, k],
            device_id=device,
            device_id_type=MESH,
        )

    def spread(self, q, k):
        place = self.place
        device = place.device(place.ahead(q), place.ctx)
        return self.copy(self.out.at[q - 1, k], self.got.at[q - 1, k], q, k, device)

    def swap(self, k):
        return self.copy(self.sum.at[k], self.cross.at[k], 0, k, other_group(self.place))

    def collect(self, q, k):
        place = self.place
        device = place.device(place.ahead(q), place.ctx)
        return self.copy(
            self.done.at[k], self.back.at[q - 1, k], place.sz.half - 1 + q, k, device
        )

    def start(self, k):
        for q in range(1, self.place.sz.half):
            rows = self.rows(self.place.ahead(q), k)
            self.out[q - 1, k] = self.total[rows, :].astype(jnp.bfloat16)
            self.spread(q, k).start()

    def cross_over(self, k):
        value = self.total[self.rows(self.place.part, k), :]
        for q in range(1, self.place.sz.half):
            self.spread(q, k).wait_recv()
            value = value + self.got[q - 1, k].astype(jnp.float32)
        self.sum[k] = value.astype(jnp.bfloat16)
        self.swap(k).start()

    def share(self, k):
        self.swap(k).wait_recv()
        value = self.sum[k].astype(jnp.float32) + self.cross[k].astype(jnp.float32)
        self.done[k] = value.astype(jnp.bfloat16)
        for q in range(1, self.place.sz.half):
            self.collect(q, k).start()
        self.total[self.rows(self.place.part, k), :] = self.done[k].astype(jnp.float32)

    def complete(self, k):
        for q in range(1, self.place.sz.half):
            self.collect(q, k).wait_recv()
            rows = self.rows(self.place.behind(q), k)
            self.total[rows, :] = self.back[q - 1, k].astype(jnp.float32)

    def finish(self):
        for k in range(self.parts):
            self.swap(k).wait_send()
            for q in range(1, self.place.sz.half):
                self.spread(q, k).wait_send()
                self.collect(q, k).wait_send()


SUM_PARTS = 2


def grads_kernel(sz, n_dp, count, *refs):
    n_in = 3 + 2 * count
    low, joined, adapter = refs[:3]
    xs, ys = refs[3 : 3 + count], refs[3 + count : n_in]
    outs = refs[n_in : n_in + count]
    embed_grad, adapter_out, gains_out, landed = refs[n_in + count : n_in + 4 + count]
    refs = refs[n_in + 4 + count :]

    def take(n):
        nonlocal refs
        head, refs = refs[:n], refs[n:]
        return head

    ring_refs, deliver_refs = take(3 * count + 6), take(count + 3)
    plane_refs, sum_refs = take(4), take(8)
    adapter_grad, d_s, j_s, weight_s, rows_s, swap_in = refs[:6]
    d_sem, j_sem, weight_sem, swap_sem, out_sem = refs[6:]
    place = Place(sz)
    ring = Ring(place, n_dp)
    tasks = GradRing.all_tasks(n_dp, count)
    grads = GradRing(sz, place, ring, tasks, xs, ys, ring_refs)
    deliver = Deliver(sz, place, deliver_refs)
    plane = PlaneRows(place, ring, low, landed, plane_refs)
    line = LineSum(place, adapter_grad, SUM_PARTS, sum_refs)
    other = other_group(place)
    grads.start()
    weight_load = [
        pltpu.make_async_copy(
            adapter.at[adapter.shape[0] // 2 + b, pl.ds(0, weight_s.shape[0])], weight_s, weight_sem
        )
        for b in range(adapter.shape[0] // 2)
    ]
    weight_load[0].start()
    place.enter([ring.device(1), ring.device(n_dp - 1), other], deliver.greet())
    plane.start()
    give_rows = pl.ds(pl.multiple_of((1 - place.group) * sz.block, sz.block), sz.block)
    keep_rows = pl.ds(pl.multiple_of(place.group * sz.block, sz.block), sz.block)
    swap = pltpu.make_async_remote_copy(
        src_ref=low.at[give_rows],
        dst_ref=swap_in,
        send_sem=swap_sem.at[0],
        recv_sem=swap_sem.at[1],
        device_id=other,
        device_id_type=MESH,
    )
    swap.start()

    def ring_step():
        if grads.left():
            w, complete = grads.step()
            if complete:
                deliver.start(w, [grads.result(w, way) for way in range(sz.n_context)])

    depth = joined.shape[2]

    def batch(ctx):
        copies = []
        for d in range(n_dp):
            at = d * sz.n_context + ctx
            rows = pl.ds(d * sz.rows, sz.rows)
            copies.append(
                pltpu.make_async_copy(landed.at[at, pl.ds(0, sz.rows)], d_s.at[rows], d_sem.at[d, 0])
            )
            copies.append(pltpu.make_async_copy(joined.at[at], j_s.at[rows], j_sem.at[d]))
            copies.append(
                pltpu.make_async_copy(
                    landed.at[at, pl.ds(sz.rows, 16)],
                    d_s.at[pl.ds(n_dp * sz.rows + 16 * d, 16)],
                    d_sem.at[d, 1],
                )
            )
        return copies

    def product(ctx, first):
        copies = batch(ctx)
        for copy in copies:
            copy.start()
        for copy in copies:
            copy.wait()
        chunk = sz.width // 4
        for n in range(4):
            cols = slice(n * chunk, (n + 1) * chunk)
            value = tn_dot(j_s[...], d_s[: n_dp * sz.rows, cols])
            tail = d_s[n_dp * sz.rows : n_dp * sz.rows + 16, cols].astype(jnp.float32)
            for d in range(1, n_dp):
                at = n_dp * sz.rows + 16 * d
                tail = tail + d_s[at : at + 16, cols].astype(jnp.float32)
            if first:
                adapter_grad[:depth, cols] = value
                adapter_grad[depth : depth + 16, cols] = tail
            else:
                adapter_grad[:depth, cols] += value
                adapter_grad[depth : depth + 16, cols] += tail

    own = pltpu.make_async_copy(low, landed.at[place.dp * sz.n_context + place.ctx], d_sem.at[0, 0])
    own.start()
    rest = adapter_grad.shape[0] - depth - 16
    if rest:
        adapter_grad[depth + 16 :, :] = jnp.zeros((rest, sz.width), jnp.float32)
    for s in range(n_dp - 1):
        if s == n_dp - 2:
            ring_step()
        plane.step(s)
    own.wait()
    product(place.ctx, True)
    for s in range(n_dp):
        plane.wait_near(s)
    product(1 - place.ctx, False)
    for k in range(SUM_PARTS):
        line.start(k)
    ring_step()
    ring_step()
    swap.wait()
    rows_s[place.group] = low[keep_rows, :]
    rows_s[1 - place.group] = swap_in[...]
    rows = rows_s[...].reshape(sz.rows, sz.width)
    ring_step()
    for k in range(SUM_PARTS):
        line.cross_over(k)
    ring_step()
    for b, copy in enumerate(weight_load):
        copy.wait()
        part = nt_dot(rows, weight_s[...]).reshape(sz.seqs, sz.block, weight_s.shape[0])
        embed_grad[:, :, b * weight_s.shape[0] : (b + 1) * weight_s.shape[0]] = part
        if b + 1 < len(weight_load):
            weight_load[b + 1].start()
    ring_step()
    for k in range(SUM_PARTS):
        line.share(k)
        ring_step()
    while grads.left():
        ring_step()
    for k in range(SUM_PARTS):
        line.complete(k)
    saves = [
        pltpu.make_async_copy(adapter_grad.at[pl.ds(0, depth)], adapter_out, out_sem.at[0]),
        pltpu.make_async_copy(adapter_grad.at[pl.ds(depth, 16)], gains_out, out_sem.at[1]),
    ]
    for copy in saves:
        copy.start()
    for w in range(count):
        outs[w][...] = deliver.total(w)
    for copy in saves:
        copy.wait()
    grads.finish()
    deliver.finish()
    plane.finish()
    line.finish()


def run_grads(sz, n_dp, low, joined, adapter, xs, ys):
    count, bf16, f32, dma = len(xs), jnp.bfloat16, jnp.float32, pltpu.SemaphoreType.DMA
    shape = jax.ShapeDtypeStruct
    depth = sz.width // (n_dp * sz.n_context)
    wide = [y.shape[1] for y in ys]
    slots, columns = joined.shape[0], joined.shape[2]
    unit = 16 * sz.half * SUM_PARTS
    total_rows = -(-(columns + 16) // unit) * unit
    return pl.pallas_call(
        partial(grads_kernel, sz, n_dp, count),
        out_shape=[shape((depth, n), f32) for n in wide]
        + [
            shape((sz.seqs, sz.block, sz.width), f32),
            shape((columns, sz.width), f32),
            shape((16, sz.width), f32),
            shape((slots,) + low.shape, bf16),
        ],
        in_specs=[full_spec()] + [any_spec()] * (2 + 2 * count),
        out_specs=[full_spec()] * (1 + count) + [any_spec()] * 3,
        scratch_shapes=GradRing.scratch(sz, n_dp, GradRing.all_tasks(n_dp, count), wide)
        + Deliver.scratch(sz, n_dp, wide)
        + PlaneRows.scratch(n_dp)
        + LineSum.scratch(sz, SUM_PARTS, total_rows // (sz.half * SUM_PARTS))
        + [
            pltpu.VMEM((total_rows, sz.width), f32),
            pltpu.VMEM((n_dp * (sz.rows + 16), sz.width), bf16),
            pltpu.VMEM((n_dp * sz.rows, columns), bf16),
            pltpu.VMEM((columns, sz.width), bf16),
            pltpu.VMEM((sz.seqs, sz.block, sz.width), bf16),
            pltpu.VMEM((sz.block, sz.width), bf16),
            dma((n_dp, 2)),
            dma((n_dp,)),
            dma,
            dma((2,)),
            dma((2,)),
        ],
        compiler_params=pltpu.CompilerParams(
            collective_id=8, has_side_effects=True, vmem_limit_bytes=VMEM_BYTES
        ),
        cost_estimate=pl.CostEstimate(
            flops=2 * sz.seq_len * sz.width * sum(wide), bytes_accessed=60 << 20, transcendentals=0
        ),
        name="grads",
    )(low, joined, adapter, *[slot_columns(sz, n_dp, x) for x in xs], *ys)


def shards(
    embedded,
    initial_state,
    cotangent,
    doc_ids,
    recurrences,
    adapter_weight,
    norm_gains,
    qkv_weight,
    output_head_weight,
    gate_up_weight,
    down_weight,
):
    n_dp = lax.axis_size("dp")
    n_tensor = lax.axis_size("tensor")
    n_context = lax.axis_size("context")
    dp_index = lax.axis_index("dp")
    t_index = lax.axis_index("tensor")
    ctx_index = lax.axis_index("context")
    seq_count, block_rows, model_width = embedded.shape
    seq_len = doc_ids.shape[1]
    half = n_tensor // seq_count
    group = t_index // half
    part = t_index % half
    heads_here = qkv_weight.shape[1]
    head_dim = qkv_weight.shape[2] // 3
    ff_here = down_weight.shape[0]
    def side_by_side(blocks):
        count, depth, columns = blocks.shape
        return blocks.transpose(1, 0, 2).reshape(depth, count * columns)

    def role_grad(grad, axis):
        piece = lax.psum_scatter(
            grad.astype(jnp.bfloat16), "dp", scatter_dimension=axis, tiled=True
        )
        low, high = jnp.split(piece, 2, axis=axis)
        give = [jnp.where(group == 0, low, high), jnp.where(group == 0, high, low)]
        back = [
            lax.ppermute(g, ("tensor", "context"), [(b, a) for a, b in perm])
            for g, perm in zip(give, role_perms)
        ]
        return back[0].astype(jnp.float32) + back[1].astype(jnp.float32)

    def gather_rows(rows):
        full = lax.all_gather(
            rows, ("tensor", "context"), axis=0, tiled=True, axis_index_groups=groups
        )
        split = full.reshape(half, n_context, seq_count, block_rows, model_width)
        return split.transpose(2, 0, 1, 3, 4).reshape(seq_len, model_width)

    sz = Sizes(
        n_tensor,
        n_context,
        seq_count,
        half,
        block_rows,
        n_context * block_rows,
        seq_count * block_rows,
        seq_len,
        model_width,
        heads_here,
        head_dim,
        ff_here,
    )
    adapter_block = adapter_weight.shape[0]
    gain_columns = norm_gains.shape[1]
    unit = 16 * half
    padded = -(-(adapter_block + 2) // unit) * unit
    adapter_rows = jnp.concatenate(
        [
            adapter_weight,
            jnp.pad(
                norm_gains,
                ((0, padded - adapter_block - 2), (0, model_width - gain_columns)),
            ),
        ],
        axis=0,
    )
    (
        adapter_all,
        out_blocks,
        qkv_use,
        gate_use,
        up_use,
        down_blocks,
        embed_rows,
        cot_rows,
        grad_ffn,
        embed_part,
        current,
    ) = run_weights(
        sz,
        n_dp,
        adapter_rows,
        adapter_block,
        [
            output_head_weight.reshape(heads_here * head_dim, -1),
            qkv_weight.reshape(qkv_weight.shape[0], -1),
            gate_up_weight[:, 0],
            gate_up_weight[:, 1],
            down_weight,
        ],
        [embedded, initial_state, cotangent],
    )
    qkv_use = qkv_use.reshape(model_width, -1)
    gate_use = gate_use.reshape(model_width, -1)
    up_use = up_use.reshape(model_width, -1)
    gains_full = (
        adapter_all[:, adapter_block : adapter_block + 2, :gain_columns]
        .transpose(1, 0, 2)
        .reshape(2, model_width)
    )
    if out_blocks.shape[2] % 128:
        out_blocks = side_by_side(out_blocks)[None]
        down_blocks = side_by_side(down_blocks)[None]
    gains_f = gains_full.astype(jnp.float32)

    cos_full, sin_full = rope_tables(seq_len, head_dim)
    own_seq = dp_index * seq_count + group
    docs = lax.dynamic_index_in_dim(doc_ids, own_seq, 0, keepdims=False)
    begin = jnp.sum((docs[None, :] < docs[:, None]).astype(jnp.int32), axis=1)[None, :]
    steps_own = lax.dynamic_index_in_dim(recurrences, own_seq, 0, keepdims=False) - BACK
    for step_index in range(MAXR - BACK):
        active = jnp.broadcast_to((step_index < steps_own).astype(jnp.float32), (1, model_width))
        current = run_round(
            sz, current, active, gains_f, cos_full, sin_full, begin, embed_part,
            adapter_all, qkv_use, out_blocks, gate_use, up_use, down_blocks,
        )
    detached = current
    (mixed_rows, adapted, feature_rows, query_hm, key_hm, value_hm, head_flat, lse, joined) = run_attn(
        sz, n_dp, True, detached, embed_part, gains_f, cos_full, sin_full, begin,
        adapter_all, qkv_use, out_blocks, embed_rows,
    )
    (current, ffn_input, gate_pre, up_pre, hidden) = run_ffn(
        sz, True, mixed_rows, detached, gains_f[:1], gains_f, gate_use, up_use, down_blocks
    )
    grad_mixed, gain_b, grad_gate, grad_up, down_sum, gate_part = run_ffn_back(
        sz, n_dp, cot_rows, mixed_rows, gains_f, grad_ffn, gate_pre, up_pre,
        gate_use, up_use, down_blocks, ffn_input, hidden,
    )
    grad_low, down_t, gate_s, state_out, grad_rows, grad_proj = run_attn_back(
        sz, n_dp, grad_mixed, adapted, gains_f, cos_full, sin_full, begin, gain_b, current,
        query_hm, key_hm, value_hm, lse, out_blocks, qkv_use, ffn_input, grad_gate, down_sum,
        gate_part,
    )
    qkv_s, up_s, out_t, embed_out, adapter_s, gains_rows, _ = run_grads(
        sz,
        n_dp,
        grad_low,
        joined,
        adapter_all,
        [feature_rows, ffn_input, grad_rows],
        [grad_proj, grad_up, head_flat],
    )
    place_at = (dp_index * n_context + ctx_index) * gain_columns
    gains_s = lax.dynamic_slice_in_dim(gains_rows[:2], place_at, gain_columns, 1)
    down_s = down_t.T
    out_s = out_t.T.reshape(heads_here, head_dim, -1)
    qkv_s = qkv_s.reshape(-1, heads_here, 3 * head_dim)
    gate_up_s = jnp.stack([gate_s, up_s], axis=1)
    return (state_out, embed_out, adapter_s, gains_s, qkv_s, out_s, gate_up_s, down_s)


def solution(mesh):
    placed = (
        P("dp", ("tensor", "context"), None),
        P("dp", ("tensor", "context"), None),
        P("dp", ("tensor", "context"), None),
        P(),
        P(),
        P(("dp", "context"), None),
        P(None, ("dp", "context")),
        P(("dp", "context"), "tensor", None),
        P("tensor", None, ("dp", "context")),
        P(("dp", "context"), None, "tensor"),
        P("tensor", ("dp", "context")),
    )
    return jax.shard_map(
        shards,
        mesh=mesh,
        in_specs=placed,
        out_specs=(
            P("dp", ("tensor", "context"), None),
            P("dp", ("tensor", "context"), None),
            P(("dp", "context"), None),
            P(None, ("dp", "context")),
            P(("dp", "context"), "tensor", None),
            P("tensor", None, ("dp", "context")),
            P(("dp", "context"), None, "tensor"),
            P("tensor", ("dp", "context")),
        ),
        check_vma=False,
    )
```

```python
from functools import partial
import math
from typing import NamedTuple

import jax
import jax.numpy as jnp
import numpy as np
from jax import lax
from jax.experimental import pallas as pl
from jax.experimental.pallas import tpu as pltpu
from jax.sharding import PartitionSpec as P

BACK = 1
MAXR = 4


rope_base = 50000.0
norm_eps = 1e-06
masked_score = -1e30


def rope_tables(seq_len, head_dim):
    freq_index = np.arange(head_dim // 2, dtype=np.float32)
    inv_freq = 1.0 / np.float32(rope_base) ** (np.float32(2.0) * freq_index / head_dim)
    angles = np.arange(seq_len, dtype=np.float32)[:, None] * inv_freq.astype(np.float32)[None, :]
    cos_t, sin_t = np.cos(angles), np.sin(angles)
    return (
        jnp.asarray(np.concatenate([cos_t, cos_t], axis=1), jnp.float32),
        jnp.asarray(np.concatenate([-sin_t, sin_t], axis=1), jnp.float32),
    )


MESH = pl.DeviceIdType.MESH
LOG2E = 1.4426950408889634
VMEM_BYTES = 62 << 20


class Sizes(NamedTuple):
    n_tensor: int
    n_context: int
    seqs: int
    half: int
    block: int
    tile: int
    rows: int
    seq_len: int
    width: int
    heads: int
    head_dim: int
    ff: int


def full_spec():
    return pl.BlockSpec(memory_space=pltpu.VMEM)


def any_spec():
    return pl.BlockSpec(memory_space=pl.ANY)


def nt_dot(a, b):
    return lax.dot_general(a, b, (((1,), (1,)), ((), ())), preferred_element_type=jnp.float32)


def tn_dot(a, b):
    return lax.dot_general(a, b, (((0,), (0,)), ((), ())), preferred_element_type=jnp.float32)


def nn_dot(a, b):
    return jnp.dot(a, b, preferred_element_type=jnp.float32)


class Place:
    def __init__(self, sz):
        t = lax.axis_index("tensor")
        self.sz = sz
        self.dp = lax.axis_index("dp")
        self.ctx = lax.axis_index("context")
        self.group = t // sz.half
        self.part = lax.rem(t, sz.half)

    def device(self, part, ctx):
        return (self.dp, self.group * self.sz.half + part, ctx)

    def ahead(self, q):
        return lax.rem(self.part + q, self.sz.half)

    def behind(self, q):
        return lax.rem(self.part + (self.sz.half - q), self.sz.half)

    def sibling(self):
        return self.device(self.part, 1 - self.ctx)

    def block(self, part, ctx, j):
        sz = self.sz
        first = ((part + j * sz.half) * sz.n_context + ctx) * sz.block
        return pl.ds(pl.multiple_of(first, sz.block), sz.block)

    def tile(self, q, j):
        sz = self.sz
        first = (self.ahead(q) + j * sz.half) * sz.tile
        return pl.ds(pl.multiple_of(first, sz.tile), sz.tile)

    def enter(self, others=(), more=0):
        barrier = pltpu.get_barrier_semaphore()
        for device in others:
            pl.semaphore_signal(barrier, inc=1, device_id=device, device_id_type=MESH)
        pl.semaphore_signal(
            barrier, inc=1, device_id=self.sibling(), device_id_type=MESH
        )
        for q in range(1, self.sz.half):
            pl.semaphore_signal(
                barrier,
                inc=1,
                device_id=self.device(self.ahead(q), self.ctx),
                device_id_type=MESH,
            )
        pl.semaphore_wait(barrier, self.sz.half + len(others) + more)


class Gather:
    @staticmethod
    def scratch(sz):
        kinds = 2 * sz.half - 1
        return [
            pltpu.SemaphoreType.DMA((kinds, sz.seqs)),
            pltpu.SemaphoreType.DMA((kinds, sz.seqs)),
        ]

    def __init__(self, place, ref, send, recv):
        self.place, self.ref, self.send, self.recv = place, ref, send, recv

    def copy(self, kind, j, rows):
        place, half = self.place, self.place.sz.half
        if 0 < kind < half:
            target = place.device(place.ahead(kind), place.ctx)
        else:
            target = place.sibling()
        return pltpu.make_async_remote_copy(
            src_ref=self.ref.at[rows],
            dst_ref=self.ref.at[rows],
            send_sem=self.send.at[kind, j],
            recv_sem=self.recv.at[kind, j],
            device_id=target,
            device_id_type=MESH,
        )

    def own(self, j):
        return self.place.block(self.place.part, self.place.ctx, j)

    def start(self, j):
        for q in range(1, self.place.sz.half):
            self.copy(q, j, self.own(j)).start()
        self.copy(0, j, self.own(j)).start()

    def wait_near(self, j):
        place = self.place
        self.copy(0, j, place.block(place.part, 1 - place.ctx, j)).wait_recv()

    def forward(self, q, j):
        place = self.place
        rows = place.block(place.behind(q), place.ctx, j)
        self.copy(q, j, rows).wait_recv()
        self.copy(place.sz.half - 1 + q, j, rows).start()

    def wait_far(self, q, j):
        place = self.place
        rows = place.block(place.behind(q), 1 - place.ctx, j)
        self.copy(place.sz.half - 1 + q, j, rows).wait_recv()

    def passed_on(self, j):
        place, half = self.place, self.place.sz.half
        for q in range(1, half):
            rows = place.block(place.behind(q), place.ctx, j)
            self.copy(half - 1 + q, j, rows).wait_send()

    def finish(self, forwards=True):
        for j in range(self.place.sz.seqs):
            for kind in range(self.place.sz.half):
                self.copy(kind, j, self.own(j)).wait_send()
            if forwards:
                self.passed_on(j)


class Scatter:
    @staticmethod
    def scratch(sz):
        kinds = 2 * sz.half - 1
        near = (sz.half, sz.seqs, sz.block, sz.width)
        far = (max(sz.half - 1, 1), sz.seqs, sz.block, sz.width)
        return [
            pltpu.VMEM((sz.tile, sz.width), jnp.float32),
            pltpu.VMEM(near, jnp.bfloat16),
            pltpu.VMEM(near, jnp.bfloat16),
            pltpu.VMEM(near, jnp.bfloat16),
            pltpu.VMEM(far, jnp.bfloat16),
            pltpu.VMEM(far, jnp.bfloat16),
            pltpu.SemaphoreType.DMA((kinds, sz.seqs)),
            pltpu.SemaphoreType.DMA((kinds, sz.seqs)),
        ]

    def __init__(self, place, part, mine, near_out, near_in, far_out, far_in, send, recv):
        self.place, self.part, self.mine = place, part, mine
        self.near_out, self.near_in = near_out, near_in
        self.far_out, self.far_in = far_out, far_in
        self.send, self.recv = send, recv

    def near(self, q, j):
        return pltpu.make_async_remote_copy(
            src_ref=self.near_out.at[q, j],
            dst_ref=self.near_in.at[q, j],
            send_sem=self.send.at[q, j],
            recv_sem=self.recv.at[q, j],
            device_id=self.place.sibling(),
            device_id_type=MESH,
        )

    def far(self, q, j):
        place = self.place
        return pltpu.make_async_remote_copy(
            src_ref=self.far_out.at[q - 1, j],
            dst_ref=self.far_in.at[q - 1, j],
            send_sem=self.send.at[place.sz.half - 1 + q, j],
            recv_sem=self.recv.at[place.sz.half - 1 + q, j],
            device_id=place.device(place.ahead(q), place.ctx),
            device_id_type=MESH,
        )

    def give(self, q, j):
        sz, ctx = self.place.sz, self.place.ctx
        mine = pl.ds(pl.multiple_of(ctx * sz.block, sz.block), sz.block)
        other = pl.ds(pl.multiple_of((1 - ctx) * sz.block, sz.block), sz.block)
        self.near_out[q, j] = self.part[other, :].astype(jnp.bfloat16)
        self.near(q, j).start()
        self.mine[q, j] = self.part[mine, :].astype(jnp.bfloat16)

    def onward(self, q, j):
        self.near(q, j).wait_recv()
        self.far_out[q - 1, j] = (
            self.mine[q, j].astype(jnp.float32) + self.near_in[q, j].astype(jnp.float32)
        ).astype(jnp.bfloat16)
        self.far(q, j).start()

    def total(self, j):
        self.near(0, j).wait_recv()
        total = self.mine[0, j].astype(jnp.float32) + self.near_in[0, j].astype(jnp.float32)
        for q in range(1, self.place.sz.half):
            self.far(q, j).wait_recv()
            total = total + self.far_in[q - 1, j].astype(jnp.float32)
        return total

    def finish(self):
        half = self.place.sz.half
        for j in range(self.place.sz.seqs):
            for q in range(half):
                self.near(q, j).wait_send()
            for q in range(1, half):
                self.far(q, j).wait_send()


def column_loads(blocks_ref, vmem_ref, sem):
    count, _, columns = blocks_ref.shape
    return [
        pltpu.make_async_copy(
            blocks_ref.at[b], vmem_ref.at[:, pl.ds(b * columns, columns)], sem.at[b]
        )
        for b in range(count)
    ]


def adapter_loads(blocks_ref, vmem_ref, sem):
    count, tops = sem.shape
    depth, columns = vmem_ref.shape[0] // tops, vmem_ref.shape[1] // count
    return [
        [
            pltpu.make_async_copy(
                blocks_ref.at[b, pl.ds(0, depth), pl.ds(n * columns, columns)],
                vmem_ref.at[pl.ds(b * depth, depth), pl.ds(n * columns, columns)],
                sem.at[n, b],
            )
            for b in range(tops)
        ]
        for n in range(count)
    ]


def rms_factor(rows):
    return lax.rsqrt(jnp.mean(rows * rows, axis=-1, keepdims=True) + norm_eps)


def turn(x, cos_t, sin_t):
    return x * cos_t + pltpu.roll(x, x.shape[-1] // 2, 1) * sin_t


def attn_kernel(sz, n_dp, keep, *refs):
    (latent, embed, gains, cos_t, sin_t, begin, adapter_hbm, qkv_hbm, out_hbm) = refs[:9]
    refs = refs[9:]
    if keep:
        embed_hbm, refs = refs[0], refs[1:]
    mixed = refs[0]
    refs = refs[1:]
    if keep:
        adapted_out, rows_out, q_out, k_out, v_out, head_out, lse_out, joined_out = refs[:8]
        refs = refs[8:]
    (wa, wqkv, wout, adapted, rows_s, q_s, k_s, v_s, head_s, lse_s) = refs[:10]
    load_a, load_qkv, load_out, keep_sem = refs[10:14]
    gather_refs = refs[14:16]
    scatter_refs = refs[16:24]
    if keep:
        joined_s, load_embed, x_send, x_recv = refs[24:]

    place = Place(sz)
    a_loads = adapter_loads(adapter_hbm, wa, load_a)
    qkv_load = pltpu.make_async_copy(qkv_hbm, wqkv, load_qkv)
    out_loads = column_loads(out_hbm, wout, load_out)
    for group in a_loads:
        for copy in group:
            copy.start()
    qkv_load.start()
    for copy in out_loads:
        copy.start()
    others = []
    if keep:
        ring = Ring(place, n_dp)
        t = lax.axis_index("tensor")
        embed_load = pltpu.make_async_copy(
            embed_hbm, joined_s.at[:, pl.ds(sz.width, sz.width)], load_embed
        )
        embed_load.start()
        plane = [(o, c) for o in range(n_dp) for c in range(2) if (o, c) != (0, 0)]

        def member(o, c):
            return (ring.index(o), t, place.ctx if c == 0 else 1 - place.ctx)

        def columns_to(o, c):
            to = member(o, c)
            depth = joined_out.shape[2]
            first = pl.multiple_of((to[0] * sz.n_context + to[2]) * depth, depth)
            return pltpu.make_async_remote_copy(
                src_ref=joined_s.at[:, pl.ds(first, depth)],
                dst_ref=joined_out.at[place.dp * sz.n_context + place.ctx],
                send_sem=x_send.at[o, c],
                recv_sem=x_recv.at[o, c],
                device_id=to,
                device_id_type=MESH,
            )

        def columns_from(o, c):
            ref = joined_out.at[
                ring.index(-o) * sz.n_context + (place.ctx if c == 0 else 1 - place.ctx)
            ]
            return pltpu.make_async_remote_copy(
                src_ref=ref,
                dst_ref=ref,
                send_sem=x_send.at[o, c],
                recv_sem=x_recv.at[o, c],
                device_id=place.sibling(),
                device_id_type=MESH,
            )

        others = [member(o, c) for o, c in plane if o]
    place.enter(others)
    gather = Gather(place, rows_s, *gather_refs)
    scatter = Scatter(place, *scatter_refs)

    low = latent[...].astype(jnp.bfloat16)
    columns = sz.width // len(a_loads)
    square = None
    for n, group in enumerate(a_loads):
        for copy in group:
            copy.wait()
        cols = pl.ds(n * columns, columns)
        chunk = nn_dot(low, wa[:, cols]) + embed[:, cols]
        adapted[:, cols] = chunk
        here = jnp.sum(chunk * chunk, axis=-1, keepdims=True)
        square = here if square is None else square + here
    factor = lax.rsqrt(square / sz.width + norm_eps)
    for j in range(sz.seqs):
        span = slice(j * sz.block, (j + 1) * sz.block)
        normed = (adapted[span, :] * factor[span]) * gains[0:1, :]
        rows_s[gather.own(j), :] = normed.astype(jnp.bfloat16)
        gather.start(j)

    qkv_load.wait()
    pair = min(2, sz.heads)
    d = sz.head_dim

    def project(q, j):
        rows = place.tile(q, j)
        x = rows_s[rows, :]
        cos_here, sin_here = cos_t[rows, :], sin_t[rows, :]
        for h0 in range(0, sz.heads, pair):
            proj = nn_dot(x, wqkv[:, 3 * d * h0 : 3 * d * (h0 + pair)])
            for h in range(pair):
                at = 3 * d * h
                q_s[h0 + h, rows, :] = turn(proj[:, at : at + d], cos_here, sin_here).astype(
                    jnp.bfloat16
                )
                k_s[h0 + h, rows, :] = turn(
                    proj[:, at + d : at + 2 * d], cos_here, sin_here
                ).astype(jnp.bfloat16)
                v_s[h0 + h, rows, :] = proj[:, at + 2 * d : at + 3 * d].astype(jnp.bfloat16)

    def attend(q, j):
        rows = place.tile(q, j)
        first = (place.ahead(q) + j * sz.half) * sz.tile
        length = (j + 1) * sz.half * sz.tile
        start = begin[:, pl.ds(pl.multiple_of(first, sz.tile), sz.tile)]
        key_at = lax.broadcasted_iota(jnp.int32, (length, sz.tile), 0)
        query_at = first + lax.broadcasted_iota(jnp.int32, (1, sz.tile), 1)
        allowed = (key_at >= start) & (key_at <= query_at)

        def head(h, carry):
            scores = nt_dot(k_s[h, 0:length, :], q_s[h, rows, :])
            scores = jnp.where(allowed, scores * (LOG2E / math.sqrt(d)), masked_score)
            top = jnp.max(scores, axis=0, keepdims=True)
            weight = jnp.exp2(scores - top)
            total = jnp.sum(weight, axis=0, keepdims=True)
            mixed_t = tn_dot(v_s[h, 0:length, :], weight.astype(jnp.bfloat16))
            result = jnp.transpose(mixed_t / total)
            head_s[rows, pl.ds(pl.multiple_of(h * d, d), d)] = result.astype(jnp.bfloat16)
            if keep:
                lse_s[h, :, rows] = top + jnp.log2(total)
            return carry

        lax.fori_loop(0, sz.heads, head, 0)

    def give(q, j):
        rows = place.tile(q, j)
        scatter.part[...] = nn_dot(head_s[rows, :], wout[...])
        scatter.give(q, j)

    copies = []

    def save(src, dst):
        copy = pltpu.make_async_copy(src, dst, keep_sem.at[len(copies)])
        copy.start()
        copies.append(copy)

    if keep:
        save(adapted, adapted_out)
        joined_s[:, : sz.width] = low
        embed_load.wait()
        for o, c in plane:
            columns_to(o, c).start()
        mine = place.dp * sz.n_context + place.ctx
        depth = joined_out.shape[2]
        save(
            joined_s.at[:, pl.ds(pl.multiple_of(mine * depth, depth), depth)], joined_out.at[mine]
        )
    far = range(1, sz.half)
    for j in range(sz.seqs):
        gather.wait_near(j)
        project(0, j)
    for copy in out_loads:
        copy.wait()
    for j in range(sz.seqs):
        for q in far:
            gather.forward(q, j)
        for q in far:
            gather.wait_far(sz.half - q, j)
            project(q, j)
        for q in far:
            attend(q, j)
            give(q, j)
        attend(0, j)
        for q in far:
            scatter.onward(q, j)
        give(0, j)
    if keep:
        for src, dst in ((rows_s, rows_out), (q_s, q_out), (k_s, k_out), (v_s, v_out)):
            save(src, dst)
        save(head_s, head_out)
        save(lse_s, lse_out)
    gather.finish()
    for j in range(sz.seqs):
        span = slice(j * sz.block, (j + 1) * sz.block)
        mixed[span, :] = adapted[span, :] + scatter.total(j)
    scatter.finish()
    if keep:
        for o, c in plane:
            columns_from(o, c).wait_recv()
            columns_to(o, c).wait_send()
    for copy in copies:
        copy.wait()


def run_attn(
    sz, n_dp, keep, latent, embed_part, gains, cos_t, sin_t, begin, adapter, qkv, out, *embed
):
    f32, bf16 = jnp.float32, jnp.bfloat16
    heads_shape = (sz.heads, sz.seq_len, sz.head_dim)
    shape = jax.ShapeDtypeStruct
    outs = [shape((sz.rows, sz.width), f32)]
    if keep:
        outs += [
            shape((sz.rows, sz.width), f32),
            shape((sz.seq_len, sz.width), bf16),
            shape(heads_shape, bf16),
            shape(heads_shape, bf16),
            shape(heads_shape, bf16),
            shape((sz.seq_len, sz.heads * sz.head_dim), bf16),
            shape((sz.heads, 1, sz.seq_len), f32),
            shape((adapter.shape[0], sz.rows, 2 * sz.width // adapter.shape[0]), bf16),
        ]
    scratch = [
        pltpu.VMEM((sz.width, sz.width), bf16),
        pltpu.VMEM(qkv.shape, bf16),
        pltpu.VMEM((sz.heads * sz.head_dim, sz.width), bf16),
        pltpu.VMEM((sz.rows, sz.width), f32),
        pltpu.VMEM((sz.seq_len, sz.width), bf16),
        pltpu.VMEM(heads_shape, bf16),
        pltpu.VMEM(heads_shape, bf16),
        pltpu.VMEM(heads_shape, bf16),
        pltpu.VMEM((sz.seq_len, sz.heads * sz.head_dim), bf16),
        pltpu.VMEM((sz.heads, 1, sz.seq_len), f32),
        pltpu.SemaphoreType.DMA((4, adapter.shape[0] // 2)),
        pltpu.SemaphoreType.DMA,
        pltpu.SemaphoreType.DMA((out.shape[0],)),
        pltpu.SemaphoreType.DMA((8,)),
    ]
    scratch += Gather.scratch(sz) + Scatter.scratch(sz)
    if keep:
        scratch += [
            pltpu.VMEM((sz.rows, 2 * sz.width), bf16),
            pltpu.SemaphoreType.DMA,
            pltpu.SemaphoreType.DMA((n_dp, 2)),
            pltpu.SemaphoreType.DMA((n_dp, 2)),
        ]
    flops = 2 * sz.rows * sz.width * sz.width + 2 * sz.seq_len * sz.width * qkv.shape[1]
    return pl.pallas_call(
        partial(attn_kernel, sz, n_dp, keep),
        out_shape=outs,
        in_specs=[full_spec()] * 6 + [any_spec()] * (3 + len(embed)),
        out_specs=[full_spec()] + [any_spec()] * (len(outs) - 1),
        scratch_shapes=scratch,
        compiler_params=pltpu.CompilerParams(
            collective_id=2 if keep else 1, has_side_effects=True, vmem_limit_bytes=VMEM_BYTES
        ),
        cost_estimate=pl.CostEstimate(
            flops=flops, bytes_accessed=20 << 20, transcendentals=0
        ),
        name="attn_keep" if keep else "attn_round",
    )(latent, embed_part, gains, cos_t, sin_t, begin, adapter, qkv, out, *embed)


def ffn_kernel(sz, keep, *refs):
    (mixed, latent, active, gains, gate_hbm, up_hbm, down_hbm, result) = refs[:8]
    refs = refs[8:]
    if keep:
        rows_out, gate_out, up_out, hidden_out = refs[:4]
        refs = refs[4:]
    wg, wu, wd, rows_s = refs[:4]
    refs = refs[4:]
    if keep:
        gate_s, up_s, hidden_s = refs[:3]
        refs = refs[3:]
    load_gu, load_down, keep_sem = refs[:3]
    gather_refs = refs[3:5]
    scatter_refs = refs[5:]

    place = Place(sz)
    gate_load = pltpu.make_async_copy(gate_hbm, wg, load_gu.at[0])
    up_load = pltpu.make_async_copy(up_hbm, wu, load_gu.at[1])
    down_loads = column_loads(down_hbm, wd, load_down)
    gate_load.start()
    up_load.start()
    for copy in down_loads:
        copy.start()
    place.enter()
    gather = Gather(place, rows_s, *gather_refs)
    scatter = Scatter(place, *scatter_refs)
    for j in range(sz.seqs):
        span = slice(j * sz.block, (j + 1) * sz.block)
        rows = mixed[span, :]
        normed = (rows * rms_factor(rows)) * gains[1:2, :]
        rows_s[gather.own(j), :] = normed.astype(jnp.bfloat16)
        gather.start(j)
    gate_load.wait()
    up_load.wait()
    for copy in down_loads:
        copy.wait()

    copies = []

    def save(src, dst):
        copy = pltpu.make_async_copy(src, dst, keep_sem.at[len(copies)])
        copy.start()
        copies.append(copy)

    def work(q, j):
        rows = place.tile(q, j)
        x = rows_s[rows, :]
        gate = nn_dot(x, wg[...])
        up = nn_dot(x, wu[...])
        hidden = (gate / (1.0 + jnp.exp(-gate)) * up).astype(jnp.bfloat16)
        if keep:
            gate_s[rows, :] = gate.astype(jnp.bfloat16)
            up_s[rows, :] = up.astype(jnp.bfloat16)
            hidden_s[rows, :] = hidden
        scatter.part[...] = nn_dot(hidden, wd[...])
        scatter.give(q, j)

    far = range(1, sz.half)
    for j in range(sz.seqs):
        gather.wait_near(j)
        work(0, j)
    for j in range(sz.seqs):
        for q in far:
            gather.forward(q, j)
        for q in far:
            gather.wait_far(sz.half - q, j)
            work(q, j)
        for q in far:
            scatter.onward(q, j)
    if keep:
        save(rows_s, rows_out)
        save(gate_s, gate_out)
        save(up_s, up_out)
        save(hidden_s, hidden_out)
    gather.finish()
    for j in range(sz.seqs):
        span = slice(j * sz.block, (j + 1) * sz.block)
        total = mixed[span, :] + scatter.total(j)
        if not keep:
            total = jnp.where(active[...] > 0, total, latent[span, :])
        result[span, :] = total
    scatter.finish()
    for copy in copies:
        copy.wait()


def run_ffn(sz, keep, mixed, latent, active, gains, gate, up, down):
    f32, bf16 = jnp.float32, jnp.bfloat16
    shape = jax.ShapeDtypeStruct
    outs = [shape((sz.rows, sz.width), f32)]
    if keep:
        outs += [
            shape((sz.seq_len, sz.width), bf16),
            shape((sz.seq_len, sz.ff), bf16),
            shape((sz.seq_len, sz.ff), bf16),
            shape((sz.seq_len, sz.ff), bf16),
        ]
    scratch = [
        pltpu.VMEM(gate.shape, bf16),
        pltpu.VMEM(up.shape, bf16),
        pltpu.VMEM((sz.ff, sz.width), bf16),
        pltpu.VMEM((sz.seq_len, sz.width), bf16),
    ]
    if keep:
        scratch += [pltpu.VMEM((sz.seq_len, sz.ff), bf16)] * 3
    scratch += [
        pltpu.SemaphoreType.DMA((2,)),
        pltpu.SemaphoreType.DMA((down.shape[0],)),
        pltpu.SemaphoreType.DMA((4,)),
    ]
    scratch += Gather.scratch(sz) + Scatter.scratch(sz)
    return pl.pallas_call(
        partial(ffn_kernel, sz, keep),
        out_shape=outs,
        in_specs=[full_spec()] * 4 + [any_spec()] * 3,
        out_specs=[full_spec()] + [any_spec()] * (len(outs) - 1),
        scratch_shapes=scratch,
        compiler_params=pltpu.CompilerParams(
            collective_id=4 if keep else 3, has_side_effects=True, vmem_limit_bytes=VMEM_BYTES
        ),
        cost_estimate=pl.CostEstimate(
            flops=6 * sz.seq_len * sz.width * sz.ff, bytes_accessed=20 << 20, transcendentals=0
        ),
        name="ffn_keep" if keep else "ffn_round",
    )(mixed, latent, active, gains, gate, up, down)


def round_kernel(sz, *refs):
    (latent, active, gains, cos_t, sin_t, begin) = refs[:6]
    (embed_hbm, adapter_hbm, qkv_hbm, out_hbm, gate_hbm, up_hbm, down_hbm, result) = refs[6:14]
    (wa, wqkv, wout, wg, wu, mixed, rows_s, q_s, k_s, v_s, head_s) = refs[14:25]
    load_embed, load_a, load_qkv, load_out, load_gu, load_down = refs[25:31]
    gather_refs, again_refs, scatter_refs = refs[31:33], refs[33:35], refs[35:43]

    place = Place(sz)
    embed_load = pltpu.make_async_copy(embed_hbm, mixed, load_embed)
    a_loads = adapter_loads(adapter_hbm, wa, load_a)
    qkv_load = pltpu.make_async_copy(qkv_hbm, wqkv, load_qkv)
    out_loads = column_loads(out_hbm, wout, load_out)
    gate_load = pltpu.make_async_copy(gate_hbm, wg, load_gu.at[0])
    up_load = pltpu.make_async_copy(up_hbm, wu, load_gu.at[1])
    wd = wa.at[pl.ds(0, sz.ff)]
    down_loads = column_loads(down_hbm, wd, load_down)
    embed_load.start()
    for group in a_loads:
        for copy in group:
            copy.start()
    qkv_load.start()
    for copy in out_loads:
        copy.start()
    place.enter()
    gather = Gather(place, rows_s, *gather_refs)
    again = Gather(place, rows_s, *again_refs)
    scatter = Scatter(place, *scatter_refs)

    low = latent[...].astype(jnp.bfloat16)
    columns = sz.width // len(a_loads)
    square = None
    embed_load.wait()
    for n, group in enumerate(a_loads):
        for copy in group:
            copy.wait()
        cols = pl.ds(n * columns, columns)
        chunk = nn_dot(low, wa[:, cols]) + mixed[:, cols]
        mixed[:, cols] = chunk
        here = jnp.sum(chunk * chunk, axis=-1, keepdims=True)
        square = here if square is None else square + here
    factor = lax.rsqrt(square / sz.width + norm_eps)
    for j in range(sz.seqs):
        span = slice(j * sz.block, (j + 1) * sz.block)
        normed = (mixed[span, :] * factor[span]) * gains[0:1, :]
        rows_s[gather.own(j), :] = normed.astype(jnp.bfloat16)
        gather.start(j)
    gate_load.start()
    up_load.start()
    for copy in down_loads:
        copy.start()
    qkv_load.wait()
    pair = min(2, sz.heads)
    d = sz.head_dim

    def project(q, j):
        rows = place.tile(q, j)
        x = rows_s[rows, :]
        cos_here, sin_here = cos_t[rows, :], sin_t[rows, :]
        for h0 in range(0, sz.heads, pair):
            proj = nn_dot(x, wqkv[:, 3 * d * h0 : 3 * d * (h0 + pair)])
            for h in range(pair):
                at = 3 * d * h
                q_s[h0 + h, rows, :] = turn(proj[:, at : at + d], cos_here, sin_here).astype(
                    jnp.bfloat16
                )
                k_s[h0 + h, rows, :] = turn(
                    proj[:, at + d : at + 2 * d], cos_here, sin_here
                ).astype(jnp.bfloat16)
                v_s[h0 + h, rows, :] = proj[:, at + 2 * d : at + 3 * d].astype(jnp.bfloat16)

    def attend(q, j):
        rows = place.tile(q, j)
        first = (place.ahead(q) + j * sz.half) * sz.tile
        length = (j + 1) * sz.half * sz.tile
        start = begin[:, pl.ds(pl.multiple_of(first, sz.tile), sz.tile)]
        key_at = lax.broadcasted_iota(jnp.int32, (length, sz.tile), 0)
        query_at = first + lax.broadcasted_iota(jnp.int32, (1, sz.tile), 1)
        allowed = (key_at >= start) & (key_at <= query_at)

        def head(h, carry):
            scores = nt_dot(k_s[h, 0:length, :], q_s[h, rows, :])
            scores = jnp.where(allowed, scores * (LOG2E / math.sqrt(d)), masked_score)
            top = jnp.max(scores, axis=0, keepdims=True)
            weight = jnp.exp2(scores - top)
            total = jnp.sum(weight, axis=0, keepdims=True)
            mixed_t = tn_dot(v_s[h, 0:length, :], weight.astype(jnp.bfloat16))
            result = jnp.transpose(mixed_t / total)
            head_s[rows, pl.ds(pl.multiple_of(h * d, d), d)] = result.astype(jnp.bfloat16)
            return carry

        lax.fori_loop(0, sz.heads, head, 0)

    def give(q, j):
        rows = place.tile(q, j)
        scatter.part[...] = nn_dot(head_s[rows, :], wout[...])
        scatter.give(q, j)

    far = range(1, sz.half)
    for j in range(sz.seqs):
        gather.wait_near(j)
        project(0, j)
    for copy in out_loads:
        copy.wait()
    for j in range(sz.seqs):
        for q in far:
            gather.forward(q, j)
        for q in far:
            gather.wait_far(sz.half - q, j)
            project(q, j)
        for q in far:
            attend(q, j)
            give(q, j)
        attend(0, j)
        gather.passed_on(j)
        for q in far:
            scatter.onward(q, j)
        give(0, j)
    gather.finish(forwards=False)
    for j in range(sz.seqs):
        span = slice(j * sz.block, (j + 1) * sz.block)
        rows = mixed[span, :] + scatter.total(j)
        mixed[span, :] = rows
        normed = (rows * rms_factor(rows)) * gains[1:2, :]
        rows_s[again.own(j), :] = normed.astype(jnp.bfloat16)
        again.start(j)
    scatter.finish()
    gate_load.wait()
    up_load.wait()
    for copy in down_loads:
        copy.wait()

    def work(q, j):
        x = rows_s[place.tile(q, j), :]
        gate = nn_dot(x, wg[...])
        up = nn_dot(x, wu[...])
        hidden = (gate / (1.0 + jnp.exp(-gate)) * up).astype(jnp.bfloat16)
        scatter.part[...] = nn_dot(hidden, wd[...])
        scatter.give(q, j)

    for j in range(sz.seqs):
        again.wait_near(j)
        work(0, j)
    for j in range(sz.seqs):
        for q in far:
            again.forward(q, j)
        for q in far:
            again.wait_far(sz.half - q, j)
            work(q, j)
        for q in far:
            scatter.onward(q, j)
    again.finish()
    for j in range(sz.seqs):
        span = slice(j * sz.block, (j + 1) * sz.block)
        total = mixed[span, :] + scatter.total(j)
        result[span, :] = jnp.where(active[...] > 0, total, latent[span, :])
    scatter.finish()


def run_round(sz, latent, active, gains, cos_t, sin_t, begin, embed, adapter, qkv, out, gate, up, down):
    f32, bf16, dma = jnp.float32, jnp.bfloat16, pltpu.SemaphoreType.DMA
    heads_shape = (sz.heads, sz.seq_len, sz.head_dim)
    return pl.pallas_call(
        partial(round_kernel, sz),
        out_shape=jax.ShapeDtypeStruct((sz.rows, sz.width), f32),
        in_specs=[full_spec()] * 6 + [any_spec()] * 7,
        out_specs=full_spec(),
        scratch_shapes=[
            pltpu.VMEM((sz.width, sz.width), bf16),
            pltpu.VMEM(qkv.shape, bf16),
            pltpu.VMEM((sz.heads * sz.head_dim, sz.width), bf16),
            pltpu.VMEM(gate.shape, bf16),
            pltpu.VMEM(up.shape, bf16),
            pltpu.VMEM((sz.rows, sz.width), f32),
            pltpu.VMEM((sz.seq_len, sz.width), bf16),
            pltpu.VMEM(heads_shape, bf16),
            pltpu.VMEM(heads_shape, bf16),
            pltpu.VMEM(heads_shape, bf16),
            pltpu.VMEM((sz.seq_len, sz.heads * sz.head_dim), bf16),
            dma,
            dma((4, adapter.shape[0] // 2)),
            dma,
            dma((out.shape[0],)),
            dma((2,)),
            dma((down.shape[0],)),
        ]
        + Gather.scratch(sz)
        + Gather.scratch(sz)
        + Scatter.scratch(sz),
        compiler_params=pltpu.CompilerParams(
            collective_id=1, has_side_effects=True, vmem_limit_bytes=VMEM_BYTES
        ),
        cost_estimate=pl.CostEstimate(
            flops=8 * sz.seq_len * sz.width * sz.ff, bytes_accessed=40 << 20, transcendentals=0
        ),
        name="round",
    )(latent, active, gains, cos_t, sin_t, begin, embed, adapter, qkv, out, gate, up, down)


def other_group(place):
    return (place.dp, (1 - place.group) * place.sz.half + place.part, place.ctx)


class Ring:
    def __init__(self, place, n_dp):
        self.place, self.count = place, n_dp
        self.at = self.swap(place.dp)

    def swap(self, i):
        if self.count != 4:
            return i
        x, y = lax.rem(i, 2), i // 2
        return 2 * y + x + y - 2 * x * y

    def index(self, offset):
        return self.swap(lax.rem(self.at + offset + 2 * self.count, self.count))

    def device(self, offset):
        return (self.index(offset), lax.axis_index("tensor"), self.place.ctx)


def weights_kernel(sz, n_dp, *refs):
    count = 5
    adapter_in, blocks_in = refs[0], refs[1 : 1 + count]
    rows_in, refs = refs[1 + count : 4 + count], refs[4 + count :]
    adapter_out, blocks_out = refs[0], refs[1 : 1 + count]
    embed_out, cot_out, cot_all, embed_part, state_out = refs[1 + count : 6 + count]
    refs = refs[6 + count :]
    (move_send, move_recv, ring_send, ring_recv, a_send, a_recv, x_send, x_recv, own_sem) = refs[:9]
    embed_s, state_s, weight_s, swap_send, swap_recv, keep_sem, weight_sem = refs[9:16]
    gather_refs = refs[16:]
    place = Place(sz)
    ring = Ring(place, n_dp)
    t = lax.axis_index("tensor")
    ctx, part, half, n_c = place.ctx, place.part, sz.half, sz.n_context
    role = part * n_c + ctx
    at_home = role == t
    steps = n_dp - 1
    sub = adapter_in.shape[0] // half
    ahead = 1 - 2 * ctx

    def holder(g):
        return (place.dp, g * half + t // n_c, lax.rem(t, n_c))

    barrier = pltpu.get_barrier_semaphore()

    def greet(device):
        pl.semaphore_signal(barrier, inc=1, device_id=device, device_id_type=MESH)

    greet(ring.device(1))
    greet(ring.device(n_dp - 1))
    greet(place.sibling())
    for q in range(1, half):
        greet(place.device(place.ahead(q), ctx))
    for c in range(n_c):
        pl.when(jnp.logical_not(at_home & (ctx == c)))(
            lambda c=c: greet((place.dp, role, c))
        )
    other = other_group(place)
    greet(other)
    waits = 3 + half + sz.seqs - jnp.where(at_home, 1, 0)
    pl.semaphore_wait(barrier, waits)

    own_at = pl.ds(pl.multiple_of(place.group * sz.block, sz.block), sz.block)
    other_at = pl.ds(pl.multiple_of((1 - place.group) * sz.block, sz.block), sz.block)
    rows_to = (embed_s, state_s, cot_out)

    def swap(i):
        return pltpu.make_async_remote_copy(
            src_ref=rows_in[i].at[1 - place.group],
            dst_ref=rows_to[i].at[own_at],
            send_sem=swap_send.at[i],
            recv_sem=swap_recv.at[i],
            device_id=other,
            device_id_type=MESH,
        )

    def swapped(i):
        ref = rows_to[i].at[other_at]
        return pltpu.make_async_remote_copy(
            src_ref=ref,
            dst_ref=ref,
            send_sem=swap_send.at[i],
            recv_sem=swap_recv.at[i],
            device_id=other,
            device_id_type=MESH,
        )

    def keep(i):
        return pltpu.make_async_copy(
            rows_in[i].at[place.group], rows_to[i].at[own_at], keep_sem.at[i]
        )

    for i in range(3):
        keep(i).start()
    gather = Gather(place, cot_all, *gather_refs)

    def own_rows_of(j):
        return pltpu.make_async_copy(
            cot_out.at[pl.ds(j * sz.block, sz.block)], cot_all.at[gather.own(j)], keep_sem.at[3 + j]
        )

    def move(w, g):
        slot = place.dp * n_c + ctx
        return pltpu.make_async_remote_copy(
            src_ref=blocks_in[w],
            dst_ref=blocks_out[w].at[slot],
            send_sem=move_send.at[w, g],
            recv_sem=move_recv.at[w, ctx],
            device_id=holder(g),
            device_id_type=MESH,
        )

    def stay(w):
        return pltpu.make_async_copy(
            blocks_in[w], blocks_out[w].at[place.dp * n_c + ctx], own_sem.at[w]
        )

    def moved(w, c):
        slot = place.dp * n_c + c
        arrival = pltpu.make_async_remote_copy(
            src_ref=blocks_in[w],
            dst_ref=blocks_out[w].at[slot],
            send_sem=move_send.at[w, 0],
            recv_sem=move_recv.at[w, c],
            device_id=place.sibling(),
            device_id_type=MESH,
        )
        here = at_home & (ctx == c)
        pl.when(here)(lambda: stay(w).wait())
        pl.when(jnp.logical_not(here))(lambda: arrival.wait_recv())

    def adapter_rows(offset, c, p):
        return adapter_out.at[
            ring.index(offset) * n_c + c, pl.ds(pl.multiple_of(p * sub, sub), sub)
        ]

    own_rows = adapter_in.at[pl.ds(pl.multiple_of(part * sub, sub), sub)]

    def around(s):
        rows = adapter_rows(-ahead * s, ctx, part)
        return pltpu.make_async_remote_copy(
            src_ref=own_rows if s == 0 else rows,
            dst_ref=rows,
            send_sem=a_send.at[s],
            recv_sem=a_recv.at[s],
            device_id=ring.device(ahead),
            device_id_type=MESH,
        )

    def across(kind, s):
        offset = -ahead * s
        if kind < half:
            dst = adapter_rows(offset, ctx, part)
            src = own_rows if s == 0 else dst
        else:
            src = dst = adapter_rows(offset, ctx, place.behind(kind - half + 1))
        target = place.device(place.ahead(kind), ctx) if 0 < kind < half else place.sibling()
        return pltpu.make_async_remote_copy(
            src_ref=src,
            dst_ref=dst,
            send_sem=x_send.at[kind, s],
            recv_sem=x_recv.at[kind, s],
            device_id=target,
            device_id_type=MESH,
        )

    def crossed(kind, s):
        if kind == 0:
            rows = adapter_rows(ahead * s, 1 - ctx, part)
        elif kind < half:
            rows = adapter_rows(-ahead * s, ctx, place.behind(kind))
        else:
            rows = adapter_rows(ahead * s, 1 - ctx, place.behind(kind - half + 1))
        return pltpu.make_async_remote_copy(
            src_ref=rows,
            dst_ref=rows,
            send_sem=x_send.at[kind, s],
            recv_sem=x_recv.at[kind, s],
            device_id=place.sibling(),
            device_id_type=MESH,
        )

    def hop(w, way, s):
        offset = -s if way == 0 else s
        rows = blocks_out[w].at[ring.index(offset) * n_c + way]
        return pltpu.make_async_remote_copy(
            src_ref=rows,
            dst_ref=rows,
            send_sem=ring_send.at[w, way, s],
            recv_sem=ring_recv.at[w, way, s],
            device_id=ring.device(1 if way == 0 else n_dp - 1),
            device_id_type=MESH,
        )

    def hopped(w, way, s):
        offset = -(s + 1) if way == 0 else s + 1
        rows = blocks_out[w].at[ring.index(offset) * n_c + way]
        return pltpu.make_async_remote_copy(
            src_ref=rows,
            dst_ref=rows,
            send_sem=ring_send.at[w, way, s],
            recv_sem=ring_recv.at[w, way, s],
            device_id=ring.device(1),
            device_id_type=MESH,
        )

    around(0).start()
    own = pltpu.make_async_copy(own_rows, adapter_rows(0, ctx, part), own_sem.at[count])
    own.start()

    def start_move(w):
        for g in range(sz.seqs):
            here = at_home & (place.group == g)
            pl.when(jnp.logical_not(here))(lambda w=w, g=g: move(w, g).start())
        pl.when(at_home)(lambda w=w: stay(w).start())

    start_move(0)
    start_move(1)
    for kind in range(half):
        across(kind, 0).start()

    def adapter_step(s):
        if s < steps:
            arrival = pltpu.make_async_remote_copy(
                src_ref=own_rows,
                dst_ref=adapter_rows(-ahead * (s + 1), ctx, part),
                send_sem=a_send.at[s],
                recv_sem=a_recv.at[s],
                device_id=ring.device(1),
                device_id_type=MESH,
            )
            arrival.wait_recv()
            if s + 1 < steps:
                around(s + 1).start()
            for kind in range(half):
                across(kind, s + 1).start()

    def adapter_pass(s):
        for q in range(1, half):
            crossed(q, s).wait_recv()
            across(half - 1 + q, s).start()

    embed_save = pltpu.make_async_copy(embed_s, embed_out, keep_sem.at[3 + sz.seqs])
    todo = []
    for k in range(count + steps):
        for s in range(min(k, steps - 1), -1, -1):
            w = k - s
            if w < count:
                todo.append((w, s))
    done = 0
    for w, s in todo:
        for way in range(n_c):
            if s == 0:
                moved(w, way)
            else:
                hopped(w, way, s - 1).wait_recv()
            hop(w, way, s).start()
        if s == 0 and w + 2 < count:
            start_move(w + 2)
        if s == 0 and w == count - 2:
            for i in range(3):
                swap(i).start()
        if done < steps:
            adapter_step(done)
        if s == min(1, steps - 1) and w == count - 1:
            for i in range(3):
                keep(i).wait()
                swapped(i).wait_recv()
            for j in range(sz.seqs):
                own_rows_of(j).start()
            embed_save.start()
            for j in range(sz.seqs):
                own_rows_of(j).wait()
                gather.start(j)
            state_out[...] = state_s[...].astype(jnp.float32)
        done += 1
    for s in range(done, steps):
        adapter_step(s)
    for s in range(n_dp):
        adapter_pass(s)
    for j in range(sz.seqs):
        gather.wait_near(j)
        for q in range(1, half):
            gather.forward(q, j)
    for s in range(n_dp):
        crossed(0, s).wait_recv()
        for q in range(1, half):
            crossed(half - 1 + q, s).wait_recv()
    own.wait()
    slots, depth = adapter_out.shape[0], weight_s.shape[1]
    loads = [
        pltpu.make_async_copy(
            adapter_out.at[slots // 2 + b, pl.ds(0, depth)], weight_s.at[b % 2], weight_sem.at[b % 2]
        )
        for b in range(slots // 2)
    ]
    loads[0].start()
    for b, copy in enumerate(loads):
        if b + 1 < len(loads):
            loads[b + 1].start()
        copy.wait()
        part_here = nn_dot(embed_s[:, b * depth : (b + 1) * depth], weight_s[b % 2])
        if b:
            embed_part[...] += part_here
        else:
            embed_part[...] = part_here
    for w in range(count):
        for way in range(n_c):
            hopped(w, way, steps - 1).wait_recv()
    for j in range(sz.seqs):
        for q in range(1, half):
            gather.wait_far(q, j)
    gather.finish()
    embed_save.wait()
    for i in range(3):
        swap(i).wait_send()
    for w in range(count):
        for g in range(sz.seqs):
            here = at_home & (place.group == g)
            pl.when(jnp.logical_not(here))(lambda w=w, g=g: move(w, g).wait_send())
        for way in range(n_c):
            for s in range(steps):
                hop(w, way, s).wait_send()
    for s in range(steps):
        around(s).wait_send()
    for s in range(n_dp):
        for kind in range(2 * half - 1):
            across(kind, s).wait_send()


def run_weights(sz, n_dp, adapter, adapter_block, blocks, rows):
    bf16, f32 = jnp.bfloat16, jnp.float32
    slots = n_dp * sz.n_context
    outs = [jax.ShapeDtypeStruct((slots,) + a.shape, bf16) for a in [adapter] + blocks]
    outs += [
        jax.ShapeDtypeStruct((sz.rows, sz.width), bf16),
        jax.ShapeDtypeStruct((sz.rows, sz.width), bf16),
        jax.ShapeDtypeStruct((sz.seq_len, sz.width), bf16),
        jax.ShapeDtypeStruct((sz.rows, sz.width), f32),
        jax.ShapeDtypeStruct((sz.rows, sz.width), f32),
    ]
    count, steps, dma = len(blocks), n_dp - 1, pltpu.SemaphoreType.DMA
    kinds = 2 * sz.half - 1
    return pl.pallas_call(
        partial(weights_kernel, sz, n_dp),
        out_shape=outs,
        in_specs=[any_spec()] * (4 + count),
        out_specs=[any_spec()] * (4 + count) + [full_spec()] * 2,
        scratch_shapes=[
            dma((count, sz.seqs)),
            dma((count, sz.n_context)),
            dma((count, sz.n_context, steps)),
            dma((count, sz.n_context, steps)),
            dma((steps,)),
            dma((steps,)),
            dma((kinds, n_dp)),
            dma((kinds, n_dp)),
            dma((count + 1,)),
            pltpu.VMEM((sz.rows, sz.width), bf16),
            pltpu.VMEM((sz.rows, sz.width), bf16),
            pltpu.VMEM((2, adapter_block, sz.width), bf16),
            dma((3,)),
            dma((3,)),
            dma((4 + sz.seqs,)),
            dma((2,)),
        ]
        + Gather.scratch(sz),
        compiler_params=pltpu.CompilerParams(
            collective_id=5, has_side_effects=True, vmem_limit_bytes=VMEM_BYTES
        ),
        name="weights",
    )(adapter, *blocks, *rows)


def norm_back(grad, rows, factor, gain):
    unit = rows * factor
    weighted = grad * gain
    inner = jnp.mean(weighted * unit, axis=-1, keepdims=True)
    return factor * (weighted - unit * inner), jnp.sum(grad * unit, axis=0, keepdims=True)


class GradRing:
    @staticmethod
    def scratch(sz, n_dp, tasks, wide, own_rows=None):
        slots, ways, dma = n_dp * sz.n_context, sz.n_context, pltpu.SemaphoreType.DMA
        depth, bf16, count, last = sz.width // slots, jnp.bfloat16, len(wide), n_dp - 1
        own_rows = [True] * count if own_rows is None else own_rows
        hops = [[s for w, s in tasks if w == i] for i in range(count)]
        return (
            [pltpu.VMEM((sz.seq_len, n), bf16) for n, own in zip(wide, own_rows) if own]
            + [pltpu.VMEM((ways, depth, n) if 0 in h else (ways, 16, 128), bf16) for n, h in zip(wide, hops)]
            + [pltpu.VMEM((ways, min(max(h) + 1, last), depth, n), bf16) for n, h in zip(wide, hops)]
            + [
                pltpu.VMEM((2, ways, sz.seq_len, depth), bf16),
                dma((count,)),
                dma((2, ways)),
                dma((count, ways, last)),
                dma((count, ways, last)),
                dma((ways,)),
            ]
        )

    @staticmethod
    def size(wide, own_rows=None):
        return 2 * len(wide) + (len(wide) if own_rows is None else sum(own_rows)) + 6

    @staticmethod
    def all_tasks(n_dp, count):
        return [
            (k - s, s)
            for k in range(count + n_dp)
            for s in range(min(k, n_dp - 1), -1, -1)
            if k - s < count
        ]

    def __init__(self, sz, place, ring, tasks, xs, ys, refs, rows=None, given=None):
        count, refs = len(xs), list(refs)
        self.sz, self.place, self.ring, self.xs, self.count = sz, place, ring, xs, count
        self.tasks = tasks
        self.ys = [refs.pop(0) if ys[w] is not None else rows[w] for w in range(count)]
        self.first, self.held = refs[:count], refs[count : 2 * count]
        self.x_s, self.load_y, self.load_x, self.send, self.recv, load_given = refs[2 * count :]
        self.y_loads = [
            pltpu.make_async_copy(ys[w], self.ys[w], self.load_y.at[w])
            for w in range(count)
            if ys[w] is not None
        ]
        self.unread = {w: self.y_loads[i] for i, w in enumerate(
            w for w in range(count) if ys[w] is not None
        )}
        self.given = []
        if given is not None:
            self.given = [
                pltpu.make_async_copy(
                    given.at[way], self.held[0].at[way, tasks[0][1] - 1], load_given.at[way]
                )
                for way in range(sz.n_context)
            ]
        self.done = 0

    def start(self):
        for copy in self.y_loads + self.given:
            copy.start()
        for way in range(self.sz.n_context):
            self.x_load(0, way).start()

    def slot(self, way, s):
        return self.ring.index(-(s + 1) if way == 0 else s + 1) * self.sz.n_context + way

    def x_load(self, k, way):
        w, s = self.tasks[k]
        depth = self.x_s.shape[3]
        if self.xs[w].shape[0] == 1:
            at = pl.multiple_of(self.slot(way, s) * depth, depth)
            src = self.xs[w].at[0, :, pl.ds(at, depth)]
        else:
            src = self.xs[w].at[self.slot(way, s)]
        return pltpu.make_async_copy(src, self.x_s.at[k % 2, way], self.load_x.at[k % 2, way])

    def source(self, w, way, s):
        return self.first[w].at[way] if s == 0 else self.held[w].at[way, s - 1]

    def hop(self, w, way, s):
        return pltpu.make_async_remote_copy(
            src_ref=self.source(w, way, s),
            dst_ref=self.held[w].at[way, s],
            send_sem=self.send.at[w, way, s],
            recv_sem=self.recv.at[w, way, s],
            device_id=self.ring.device(1 if way == 0 else self.ring.count - 1),
            device_id_type=MESH,
        )

    def result(self, w, way):
        return self.source(w, way, self.ring.count - 1)

    def step(self):
        k = self.done
        self.done += 1
        w, s = self.tasks[k]
        ways = range(self.sz.n_context)
        if k + 1 < len(self.tasks):
            for way in ways:
                self.x_load(k + 1, way).start()
        if w in self.unread:
            self.unread.pop(w).wait()
        for way in ways:
            self.x_load(k, way).wait()
            value = tn_dot(self.x_s[k % 2, way], self.ys[w][...])
            if k == 0 and self.given:
                self.given[way].wait()
            elif s:
                self.hop(w, way, s - 1).wait_recv()
            if s:
                value = value + self.held[w][way, s - 1].astype(jnp.float32)
            ref = self.source(w, way, s)
            ref[...] = value.astype(jnp.bfloat16)
            if s < self.ring.count - 1:
                self.hop(w, way, s).start()
        return w, s == self.ring.count - 1

    def left(self):
        return len(self.tasks) - self.done

    def finish(self):
        for w, s in self.tasks:
            if s < self.ring.count - 1:
                for way in range(self.sz.n_context):
                    self.hop(w, way, s).wait_send()


class Deliver:
    @staticmethod
    def scratch(sz, n_dp, wide):
        depth, count, dma = sz.width // (n_dp * sz.n_context), len(wide), pltpu.SemaphoreType.DMA
        return [pltpu.VMEM((sz.seqs, depth, n), jnp.bfloat16) for n in wide] + [
            dma((count, sz.n_context)),
            dma((count, sz.seqs)),
            dma((count,)),
        ]

    def __init__(self, sz, place, refs):
        self.sz, self.place = sz, place
        self.landed = refs[:-3]
        self.send, self.recv, self.own = refs[-3:]
        self.count = len(self.landed)
        self.t = lax.axis_index("tensor")
        self.role = place.part * sz.n_context + place.ctx
        self.at_home = self.role == self.t
        self.sources = [None] * self.count

    def greet(self):
        sz, place = self.sz, self.place
        barrier = pltpu.get_barrier_semaphore()
        for g in range(sz.seqs):
            holder = (place.dp, g * sz.half + self.t // sz.n_context, lax.rem(self.t, sz.n_context))
            pl.when(jnp.logical_not(self.at_home & (place.group == g)))(
                lambda holder=holder: pl.semaphore_signal(
                    barrier, inc=1, device_id=holder, device_id_type=MESH
                )
            )
        return sz.n_context - jnp.where(self.at_home, 1, 0)

    def remote(self, w, way):
        return pltpu.make_async_remote_copy(
            src_ref=self.sources[w][way],
            dst_ref=self.landed[w].at[self.place.group],
            send_sem=self.send.at[w, way],
            recv_sem=self.recv.at[w, self.place.group],
            device_id=(self.place.dp, self.role, way),
            device_id_type=MESH,
        )

    def local(self, w, way):
        return pltpu.make_async_copy(
            self.sources[w][way], self.landed[w].at[self.place.group], self.own.at[w]
        )

    def start(self, w, sources):
        self.sources[w] = sources
        for way in range(self.sz.n_context):
            here = self.at_home & (self.place.ctx == way)
            pl.when(here)(lambda way=way: self.local(w, way).start())
            pl.when(jnp.logical_not(here))(lambda way=way: self.remote(w, way).start())

    def total(self, w):
        place = self.place
        for g in range(self.sz.seqs):
            ref = self.landed[w].at[g]
            arrival = pltpu.make_async_remote_copy(
                src_ref=ref,
                dst_ref=ref,
                send_sem=self.send.at[w, 0],
                recv_sem=self.recv.at[w, g],
                device_id=(place.dp, self.t, 1 - place.ctx),
                device_id_type=MESH,
            )
            here = self.at_home & (place.group == g)
            pl.when(here)(lambda: self.local(w, 0).wait())
            pl.when(jnp.logical_not(here))(lambda arrival=arrival: arrival.wait_recv())
        total = self.landed[w][0].astype(jnp.float32)
        for g in range(1, self.sz.seqs):
            total = total + self.landed[w][g].astype(jnp.float32)
        return total

    def finish(self):
        for w in range(self.count):
            for way in range(self.sz.n_context):
                here = self.at_home & (self.place.ctx == way)
                pl.when(jnp.logical_not(here))(lambda w=w, way=way: self.remote(w, way).wait_send())


def slot_columns(sz, n_dp, x):
    slots = n_dp * sz.n_context
    depth = sz.width // slots
    if depth % 128:
        return x.reshape(sz.seq_len, slots, depth).transpose(1, 0, 2)
    return x[None]


def ffn_back_kernel(sz, n_dp, *refs):
    (cot, mixed, gains) = refs[:3]
    (rows_hbm, gate_hbm, up_hbm, wg_hbm, wu_hbm, down_hbm) = refs[3:9]
    (x_hbm, normed_hbm, hidden_hbm) = refs[9:12]
    (grad_mixed, gain_grad, dgate_out, dup_out, down_sum, gate_part) = refs[12:18]
    (rows_s, gate_s, up_s, wg, wu, wd, load, load_down, keep_sem) = refs[18:27]
    scatter_refs, ring_refs = refs[27:35], refs[35:]
    place = Place(sz)
    ring = Ring(place, n_dp)
    grads = GradRing(
        sz, place, ring, ffn_back_tasks(n_dp), [x_hbm, normed_hbm], [hidden_hbm, None], ring_refs,
        rows=[None, gate_s],
    )
    grads.start()
    pairs = ((rows_hbm, rows_s), (gate_hbm, gate_s), (up_hbm, up_s), (wg_hbm, wg), (wu_hbm, wu))
    loads = [
        pltpu.make_async_copy(src, dst, load.at[i]) for i, (src, dst) in enumerate(pairs)
    ]
    down_loads = column_loads(down_hbm, wd, load_down)
    place.enter([ring.device(1), ring.device(n_dp - 1)])
    scatter = Scatter(place, *scatter_refs)
    for copy in [loads[0]] + down_loads + loads[1:]:
        copy.start()
    grads.step()
    for copy in [loads[0]] + down_loads + loads[1:]:
        copy.wait()

    def work(q, j):
        rows = place.tile(q, j)
        dh = nt_dot(rows_s[rows, :], wd[...])
        gate = gate_s[rows, :].astype(jnp.float32)
        up = up_s[rows, :].astype(jnp.float32)
        sig = 1.0 / (1.0 + jnp.exp(-gate))
        dgate = (dh * up * sig * (1.0 + gate * (1.0 - sig))).astype(jnp.bfloat16)
        dup = (dh * gate * sig).astype(jnp.bfloat16)
        gate_s[rows, :] = dgate
        up_s[rows, :] = dup
        scatter.part[...] = nt_dot(dgate, wg[...]) + nt_dot(dup, wu[...])
        scatter.give(q, j)

    far = range(1, sz.half)
    for j in range(sz.seqs):
        for q in far:
            work(q, j)
        if j:
            for q in far:
                scatter.onward(q, j - 1)
    grads.step()
    work(0, 0)
    for q in far:
        scatter.onward(q, sz.seqs - 1)
    for j in range(1, sz.seqs):
        work(0, j)
    grads.step()
    copies = [
        pltpu.make_async_copy(gate_s, dgate_out, keep_sem.at[0]),
        pltpu.make_async_copy(up_s, dup_out, keep_sem.at[1]),
    ]
    for copy in copies:
        copy.start()
    gain_total = None
    for j in range(sz.seqs):
        span = slice(j * sz.block, (j + 1) * sz.block)
        rows = mixed[span, :]
        grad, gain_here = norm_back(scatter.total(j), rows, rms_factor(rows), gains[1:2, :])
        grad_mixed[span, :] = cot[span, :].astype(jnp.float32) + grad
        gain_total = gain_here if gain_total is None else gain_total + gain_here
    gain_grad[...] = gain_total
    while grads.left():
        grads.step()
    for way in range(sz.n_context):
        grads.hop(1, way, 0).wait_recv()
        for i, (src, dst) in enumerate(
            ((grads.result(0, way), down_sum), (grads.held[1].at[way, 0], gate_part))
        ):
            copies.append(
                pltpu.make_async_copy(src, dst.at[way], keep_sem.at[2 + 2 * way + i])
            )
            copies[-1].start()
    scatter.finish()
    grads.finish()
    for copy in copies:
        copy.wait()


def ffn_back_tasks(n_dp):
    return [(0, 0), (0, 1), (1, 0)] + [(0, s) for s in range(2, n_dp)]


def run_ffn_back(sz, n_dp, cot, mixed, gains, rows, gate, up, wg, wu, down, normed, hidden):
    f32, bf16, shape = jnp.float32, jnp.bfloat16, jax.ShapeDtypeStruct
    dma = pltpu.SemaphoreType.DMA
    depth = sz.width // (n_dp * sz.n_context)
    return pl.pallas_call(
        partial(ffn_back_kernel, sz, n_dp),
        out_shape=[
            shape((sz.rows, sz.width), f32),
            shape((1, sz.width), f32),
            shape((sz.seq_len, sz.ff), bf16),
            shape((sz.seq_len, sz.ff), bf16),
            shape((sz.n_context, depth, sz.ff), bf16),
            shape((sz.n_context, depth, sz.ff), bf16),
        ],
        in_specs=[full_spec()] * 3 + [any_spec()] * 9,
        out_specs=[full_spec()] * 2 + [any_spec()] * 4,
        scratch_shapes=[
            pltpu.VMEM((sz.seq_len, sz.width), bf16),
            pltpu.VMEM((sz.seq_len, sz.ff), bf16),
            pltpu.VMEM((sz.seq_len, sz.ff), bf16),
            pltpu.VMEM(wg.shape, bf16),
            pltpu.VMEM(wu.shape, bf16),
            pltpu.VMEM((sz.ff, sz.width), bf16),
            dma((5,)),
            dma((down.shape[0],)),
            dma((2 + 2 * sz.n_context,)),
        ]
        + Scatter.scratch(sz)
        + GradRing.scratch(sz, n_dp, ffn_back_tasks(n_dp), [sz.ff, sz.ff], [True, False]),
        compiler_params=pltpu.CompilerParams(
            collective_id=6, has_side_effects=True, vmem_limit_bytes=VMEM_BYTES
        ),
        cost_estimate=pl.CostEstimate(
            flops=8 * sz.seq_len * sz.width * sz.ff, bytes_accessed=40 << 20, transcendentals=0
        ),
        name="ffn_back",
    )(
        cot, mixed, gains, rows, gate, up, wg, wu, down,
        slot_columns(sz, n_dp, rows), slot_columns(sz, n_dp, normed), hidden,
    )


def attn_back_kernel(sz, n_dp, *refs):
    (grad_mixed, gains, cos_t, sin_t, begin, gain_b, adapted_hbm, state_hbm) = refs[:8]
    (q_hbm, k_hbm, v_hbm, lse_hbm, out_hbm, qkv_hbm) = refs[8:14]
    (x_hbm, dgate_hbm, dup_hbm, down_sum, gate_part) = refs[14:19]
    (grad_low, down_grad, gate_grad, state_out, rows_out, proj_out, up_part) = refs[19:26]
    (rows_s, q_s, k_s, v_s, lse_s, do_s, dk_s, dv_s, proj_s, wout, wqkv) = refs[26:37]
    (load, load_out, keep_sem, swap_out, swap_in, swap_sem, late) = refs[37:44]
    gather_refs, scatter_refs = refs[44:46], refs[46:54]
    ring_refs, deliver_refs = refs[54:66], refs[66:]
    place = Place(sz)
    ring = Ring(place, n_dp)
    grads = GradRing(
        sz, place, ring, attn_back_tasks(n_dp), [x_hbm, x_hbm], [dgate_hbm, dup_hbm], ring_refs,
        given=gate_part,
    )
    deliver = Deliver(sz, place, deliver_refs)
    grads.start()
    split = wqkv.shape[0]
    pairs = (
        (q_hbm, q_s), (k_hbm, k_s), (v_hbm, v_s), (lse_hbm, lse_s),
        (qkv_hbm.at[pl.ds(split, split)], wqkv),
    )
    loads = [
        pltpu.make_async_copy(src, dst, load.at[i]) for i, (src, dst) in enumerate(pairs)
    ]
    out_loads = column_loads(out_hbm, wout, load_out)
    for copy in out_loads + loads:
        copy.start()
    targets = deliver.greet()
    other = other_group(place)
    place.enter([ring.device(1), ring.device(n_dp - 1), other], targets)
    gather = Gather(place, rows_s, *gather_refs)
    scatter = Scatter(place, *scatter_refs)
    for j in range(sz.seqs):
        span = slice(j * sz.block, (j + 1) * sz.block)
        rows_s[gather.own(j), :] = grad_mixed[span, :].astype(jnp.bfloat16)
        gather.start(j)
    grads.step()
    deliver.start(0, [down_sum.at[way] for way in range(sz.n_context)])
    give_rows = pl.ds(pl.multiple_of((1 - place.group) * sz.block, sz.block), sz.block)
    keep_rows = pl.ds(pl.multiple_of(place.group * sz.block, sz.block), sz.block)
    swap = pltpu.make_async_remote_copy(
        src_ref=swap_out,
        dst_ref=swap_in,
        send_sem=swap_sem.at[0],
        recv_sem=swap_sem.at[1],
        device_id=other,
        device_id_type=MESH,
    )
    state_load = pltpu.make_async_copy(
        state_hbm.at[give_rows], scatter.part.at[pl.ds(0, sz.block)], late.at[0]
    )
    state_keep = pltpu.make_async_copy(
        state_hbm.at[keep_rows], state_out.at[place.group], late.at[1]
    )
    state_load.start()
    state_keep.start()
    state_load.wait()
    swap_out[...] = scatter.part[: sz.block, :].astype(jnp.bfloat16)
    swap.start()
    for copy in out_loads:
        copy.wait()
    d = sz.head_dim

    def heads_grad(q, j):
        rows = place.tile(q, j)
        dhead = nt_dot(rows_s[rows, :], wout[...]).astype(jnp.bfloat16)
        for h in range(sz.heads):
            do_s[h, rows, :] = dhead[:, h * d : (h + 1) * d]

    far = range(1, sz.half)
    for j in range(sz.seqs):
        gather.wait_near(j)
        heads_grad(0, j)
    for copy in loads:
        copy.wait()
    for j in range(sz.seqs):
        if j == sz.seqs - 1:
            grads.step()
            grads.step()
        for q in far:
            gather.forward(q, j)
        for q in far:
            gather.wait_far(sz.half - q, j)
            heads_grad(q, j)
    rows_copy = pltpu.make_async_copy(rows_s, rows_out, keep_sem.at[0])
    rows_copy.start()
    gather.finish()
    rows_copy.wait()
    upper = rows_s.at[pl.ds(0, split), pl.ds(0, wqkv.shape[1])]
    upper_load = pltpu.make_async_copy(qkv_hbm.at[pl.ds(0, split)], upper, late.at[2])
    upper_load.start()

    tiles = sz.n_tensor
    scale = 1.0 / math.sqrt(d)

    def head(h, carry):
        for i in reversed(range(tiles)):
            rows = slice(i * sz.tile, (i + 1) * sz.tile)
            length = (i + 1) * sz.tile
            keys, values = k_s[h, 0:length, :], v_s[h, 0:length, :]
            query, grad = q_s[h, rows, :], do_s[h, rows, :]
            start = begin[:, rows]
            key_at = lax.broadcasted_iota(jnp.int32, (length, sz.tile), 0)
            query_at = i * sz.tile + lax.broadcasted_iota(jnp.int32, (1, sz.tile), 1)
            allowed = (key_at >= start) & (key_at <= query_at)
            scores = nt_dot(keys, query)
            scores = jnp.where(allowed, scores * (LOG2E * scale), masked_score)
            probs = jnp.exp2(scores - lse_s[h, :, rows])
            dprobs = nt_dot(values, grad)
            inner = jnp.sum(probs * dprobs, axis=0, keepdims=True)
            dscores = (probs * (dprobs - inner)).astype(jnp.bfloat16)
            dv = nn_dot(probs.astype(jnp.bfloat16), grad)
            dk = nn_dot(dscores, query)
            if i == tiles - 1:
                dv_s[...] = dv
                dk_s[...] = dk
            else:
                dv_s[0:length, :] += dv
                dk_s[0:length, :] += dk
            dq = jnp.transpose(tn_dot(keys, dscores)) * scale
            cos_here, sin_here = cos_t[rows, :], sin_t[rows, :]
            proj_s[rows, pl.ds(pl.multiple_of(h * 3 * d, d), d)] = turn(
                dq, cos_here, -sin_here
            ).astype(jnp.bfloat16)
        dk = turn(dk_s[...] * scale, cos_t[...], -sin_t[...])
        proj_s[:, pl.ds(pl.multiple_of(h * 3 * d + d, d), d)] = dk.astype(jnp.bfloat16)
        proj_s[:, pl.ds(pl.multiple_of(h * 3 * d + 2 * d, d), d)] = dv_s[...].astype(jnp.bfloat16)
        return carry

    lax.fori_loop(0, sz.heads, head, 0)
    copies = [pltpu.make_async_copy(proj_s, proj_out, keep_sem.at[1])]
    copies[0].start()
    upper_load.wait()
    while grads.left() > 1:
        grads.step()
    deliver.start(1, [grads.result(0, way) for way in range(sz.n_context)])

    def give(q, j):
        proj = proj_s[place.tile(q, j), :]
        scatter.part[:, :split] = nt_dot(proj, upper[...])
        scatter.part[:, split:] = nt_dot(proj, wqkv[...])
        scatter.give(q, j)

    for j in range(sz.seqs):
        for q in far:
            give(q, j)
        if j:
            for q in far:
                scatter.onward(q, j - 1)
    give(0, 0)
    for q in far:
        scatter.onward(q, sz.seqs - 1)
    for j in range(1, sz.seqs):
        give(0, j)
    adapted = scatter.part
    adapted_load = pltpu.make_async_copy(adapted_hbm, adapted, late.at[3])
    adapted_load.start()
    grads.step()
    swap.wait()
    state_keep.wait()
    adapted_load.wait()
    state_out[1 - place.group] = swap_in[...].astype(jnp.float32)
    down_grad[...] = deliver.total(0)
    gain_total = None
    for j in range(sz.seqs):
        span = slice(j * sz.block, (j + 1) * sz.block)
        rows = adapted[span, :]
        grad, gain_here = norm_back(scatter.total(j), rows, rms_factor(rows), gains[0:1, :])
        grad_low[span, :] = (grad_mixed[span, :] + grad).astype(jnp.bfloat16)
        gain_total = gain_here if gain_total is None else gain_total + gain_here
    extra = grad_low.shape[0] - sz.rows
    at_row = lax.broadcasted_iota(jnp.int32, (extra, sz.width), 0)
    shares = jnp.where(at_row == 0, gain_total, jnp.where(at_row == 1, gain_b[...], 0.0))
    grad_low[sz.rows :, :] = shares.astype(jnp.bfloat16)
    for way in range(sz.n_context):
        grads.hop(1, way, 1).wait_recv()
        copies.append(
            pltpu.make_async_copy(
                grads.held[1].at[way, 1], up_part.at[way], keep_sem.at[2 + way]
            )
        )
        copies[-1].start()
    gate_grad[...] = deliver.total(1)
    scatter.finish()
    grads.finish()
    deliver.finish()
    for copy in copies:
        copy.wait()


def attn_back_tasks(n_dp):
    return [(0, 1), (0, 2), (1, 0)] + [(0, s) for s in range(3, n_dp)] + [(1, 1)]


def run_attn_back(
    sz, n_dp, grad_mixed, adapted, gains, cos_t, sin_t, begin, gain_b, state, q, k, v, lse, out,
    qkv, x, dgate, dup, down_sum, gate_part,
):
    f32, bf16, shape = jnp.float32, jnp.bfloat16, jax.ShapeDtypeStruct
    dma = pltpu.SemaphoreType.DMA
    heads_shape = (sz.heads, sz.seq_len, sz.head_dim)
    return pl.pallas_call(
        partial(attn_back_kernel, sz, n_dp),
        out_shape=[
            shape((sz.rows + 16, sz.width), bf16),
            shape(down_sum.shape[1:], f32),
            shape(gate_part.shape[1:], f32),
            shape((sz.seqs, sz.block, sz.width), f32),
            shape((sz.seq_len, sz.width), bf16),
            shape((sz.seq_len, qkv.shape[1]), bf16),
            shape(gate_part.shape, bf16),
        ],
        in_specs=[full_spec()] * 6 + [any_spec()] * 13,
        out_specs=[full_spec()] * 4 + [any_spec()] * 3,
        scratch_shapes=[
            pltpu.VMEM((sz.seq_len, sz.width), bf16),
            pltpu.VMEM(heads_shape, bf16),
            pltpu.VMEM(heads_shape, bf16),
            pltpu.VMEM(heads_shape, bf16),
            pltpu.VMEM((sz.heads, 1, sz.seq_len), f32),
            pltpu.VMEM(heads_shape, bf16),
            pltpu.VMEM((sz.seq_len, sz.head_dim), f32),
            pltpu.VMEM((sz.seq_len, sz.head_dim), f32),
            pltpu.VMEM((sz.seq_len, qkv.shape[1]), bf16),
            pltpu.VMEM((sz.heads * sz.head_dim, sz.width), bf16),
            pltpu.VMEM((sz.width // 2, qkv.shape[1]), bf16),
            dma((5,)),
            dma((out.shape[0],)),
            dma((2 + sz.n_context,)),
            pltpu.VMEM((sz.block, sz.width), bf16),
            pltpu.VMEM((sz.block, sz.width), bf16),
            dma((2,)),
            dma((4,)),
        ]
        + Gather.scratch(sz)
        + Scatter.scratch(sz)
        + GradRing.scratch(sz, n_dp, attn_back_tasks(n_dp), [sz.ff, sz.ff])
        + Deliver.scratch(sz, n_dp, [sz.ff, sz.ff]),
        compiler_params=pltpu.CompilerParams(
            collective_id=7, has_side_effects=True, vmem_limit_bytes=VMEM_BYTES
        ),
        cost_estimate=pl.CostEstimate(
            flops=4 * sz.seq_len * sz.width * qkv.shape[1], bytes_accessed=30 << 20, transcendentals=0
        ),
        name="attn_back",
    )(
        grad_mixed, gains, cos_t, sin_t, begin, gain_b, adapted, state, q, k, v, lse, out, qkv,
        slot_columns(sz, n_dp, x), dgate, dup, down_sum, gate_part,
    )


class PlaneRows:
    @staticmethod
    def scratch(n_dp):
        dma = pltpu.SemaphoreType.DMA
        return [dma((n_dp - 1,)), dma((n_dp - 1,)), dma((n_dp,)), dma((n_dp,))]

    def __init__(self, place, ring, own, landed, refs):
        self.place, self.ring, self.own, self.landed = place, ring, own, landed
        self.send, self.recv, self.near_send, self.near_recv = refs
        self.ahead = 1 - 2 * place.ctx

    def slot(self, offset, ctx):
        return self.landed.at[self.ring.index(offset) * self.place.sz.n_context + ctx]

    def source(self, s):
        return self.own if s == 0 else self.slot(-self.ahead * s, self.place.ctx)

    def hop(self, s):
        return pltpu.make_async_remote_copy(
            src_ref=self.source(s),
            dst_ref=self.slot(-self.ahead * s, self.place.ctx),
            send_sem=self.send.at[s],
            recv_sem=self.recv.at[s],
            device_id=self.ring.device(self.ahead),
            device_id_type=MESH,
        )

    def near(self, s):
        return pltpu.make_async_remote_copy(
            src_ref=self.source(s),
            dst_ref=self.slot(-self.ahead * s, self.place.ctx),
            send_sem=self.near_send.at[s],
            recv_sem=self.near_recv.at[s],
            device_id=self.place.sibling(),
            device_id_type=MESH,
        )

    def start(self):
        self.hop(0).start()
        self.near(0).start()

    def step(self, s):
        ref = self.slot(-self.ahead * (s + 1), self.place.ctx)
        pltpu.make_async_remote_copy(
            src_ref=ref,
            dst_ref=ref,
            send_sem=self.send.at[s],
            recv_sem=self.recv.at[s],
            device_id=self.place.sibling(),
            device_id_type=MESH,
        ).wait_recv()
        if s + 1 < self.ring.count - 1:
            self.hop(s + 1).start()
        self.near(s + 1).start()

    def wait_near(self, s):
        ref = self.slot(self.ahead * s, 1 - self.place.ctx)
        pltpu.make_async_remote_copy(
            src_ref=ref,
            dst_ref=ref,
            send_sem=self.near_send.at[s],
            recv_sem=self.near_recv.at[s],
            device_id=self.place.sibling(),
            device_id_type=MESH,
        ).wait_recv()

    def finish(self):
        for s in range(self.ring.count):
            if s < self.ring.count - 1:
                self.hop(s).wait_send()
            self.near(s).wait_send()


class LineSum:
    @staticmethod
    def scratch(sz, parts, chunk):
        dma, bf16 = pltpu.SemaphoreType.DMA, jnp.bfloat16
        far = pltpu.VMEM((max(sz.half - 1, 1), parts, chunk, sz.width), bf16)
        one = pltpu.VMEM((parts, chunk, sz.width), bf16)
        kinds = 2 * sz.half - 1
        return [far, far, one, one, one, far, dma((kinds, parts)), dma((kinds, parts))]

    def __init__(self, place, total, parts, refs):
        self.place, self.total, self.parts = place, total, parts
        (self.out, self.got, self.sum, self.cross, self.done, self.back, self.send, self.recv) = refs
        self.chunk = self.sum.shape[1]

    def rows(self, part, k):
        first = (part * self.parts + k) * self.chunk
        return pl.ds(pl.multiple_of(first, self.chunk), self.chunk)

    def copy(self, src, dst, kind, k, device):
        return pltpu.make_async_remote_copy(
            src_ref=src,
            dst_ref=dst,
            send_sem=self.send.at[kind, k],
            recv_sem=self.recv.at[kind, k],
            device_id=device,
            device_id_type=MESH,
        )

    def spread(self, q, k):
        place = self.place
        device = place.device(place.ahead(q), place.ctx)
        return self.copy(self.out.at[q - 1, k], self.got.at[q - 1, k], q, k, device)

    def swap(self, k):
        return self.copy(self.sum.at[k], self.cross.at[k], 0, k, other_group(self.place))

    def collect(self, q, k):
        place = self.place
        device = place.device(place.ahead(q), place.ctx)
        return self.copy(
            self.done.at[k], self.back.at[q - 1, k], place.sz.half - 1 + q, k, device
        )

    def start(self, k):
        for q in range(1, self.place.sz.half):
            rows = self.rows(self.place.ahead(q), k)
            self.out[q - 1, k] = self.total[rows, :].astype(jnp.bfloat16)
            self.spread(q, k).start()

    def cross_over(self, k):
        value = self.total[self.rows(self.place.part, k), :]
        for q in range(1, self.place.sz.half):
            self.spread(q, k).wait_recv()
            value = value + self.got[q - 1, k].astype(jnp.float32)
        self.sum[k] = value.astype(jnp.bfloat16)
        self.swap(k).start()

    def share(self, k):
        self.swap(k).wait_recv()
        value = self.sum[k].astype(jnp.float32) + self.cross[k].astype(jnp.float32)
        self.done[k] = value.astype(jnp.bfloat16)
        for q in range(1, self.place.sz.half):
            self.collect(q, k).start()
        self.total[self.rows(self.place.part, k), :] = self.done[k].astype(jnp.float32)

    def complete(self, k):
        for q in range(1, self.place.sz.half):
            self.collect(q, k).wait_recv()
            rows = self.rows(self.place.behind(q), k)
            self.total[rows, :] = self.back[q - 1, k].astype(jnp.float32)

    def finish(self):
        for k in range(self.parts):
            self.swap(k).wait_send()
            for q in range(1, self.place.sz.half):
                self.spread(q, k).wait_send()
                self.collect(q, k).wait_send()


SUM_PARTS = 2


def grads_kernel(sz, n_dp, count, *refs):
    n_in = 4 + 2 * count
    low, joined, adapter, up_part = refs[:4]
    xs, ys = refs[4 : 4 + count], refs[4 + count : n_in]
    outs = refs[n_in : n_in + count]
    embed_grad, adapter_out, gains_out, landed = refs[n_in + count : n_in + 4 + count]
    refs = refs[n_in + 4 + count :]

    def take(n):
        nonlocal refs
        head, refs = refs[:n], refs[n:]
        return head

    ring_refs, deliver_refs = take(3 * count + 6), take(count + 3)
    plane_refs, sum_refs = take(4), take(8)
    adapter_grad, d_s, j_s, weight_s, rows_s, swap_in = refs[:6]
    d_sem, j_sem, weight_sem, swap_sem, out_sem = refs[6:]
    place = Place(sz)
    ring = Ring(place, n_dp)
    grads = GradRing(
        sz, place, ring, grads_tasks(n_dp, count), xs, ys, ring_refs, given=up_part
    )
    deliver = Deliver(sz, place, deliver_refs)
    plane = PlaneRows(place, ring, low, landed, plane_refs)
    line = LineSum(place, adapter_grad, SUM_PARTS, sum_refs)
    other = other_group(place)
    grads.start()
    weight_load = [
        pltpu.make_async_copy(
            adapter.at[adapter.shape[0] // 2 + b, pl.ds(0, weight_s.shape[0])], weight_s, weight_sem
        )
        for b in range(adapter.shape[0] // 2)
    ]
    weight_load[0].start()
    place.enter([ring.device(1), ring.device(n_dp - 1), other], deliver.greet())
    plane.start()
    give_rows = pl.ds(pl.multiple_of((1 - place.group) * sz.block, sz.block), sz.block)
    keep_rows = pl.ds(pl.multiple_of(place.group * sz.block, sz.block), sz.block)
    swap = pltpu.make_async_remote_copy(
        src_ref=low.at[give_rows],
        dst_ref=swap_in,
        send_sem=swap_sem.at[0],
        recv_sem=swap_sem.at[1],
        device_id=other,
        device_id_type=MESH,
    )
    swap.start()

    def ring_step():
        if grads.left():
            w, complete = grads.step()
            if complete:
                deliver.start(w, [grads.result(w, way) for way in range(sz.n_context)])

    depth = joined.shape[2]

    def batch(ctx):
        copies = []
        for d in range(n_dp):
            at = d * sz.n_context + ctx
            rows = pl.ds(d * sz.rows, sz.rows)
            copies.append(
                pltpu.make_async_copy(landed.at[at, pl.ds(0, sz.rows)], d_s.at[rows], d_sem.at[d, 0])
            )
            copies.append(pltpu.make_async_copy(joined.at[at], j_s.at[rows], j_sem.at[d]))
            copies.append(
                pltpu.make_async_copy(
                    landed.at[at, pl.ds(sz.rows, 16)],
                    d_s.at[pl.ds(n_dp * sz.rows + 16 * d, 16)],
                    d_sem.at[d, 1],
                )
            )
        return copies

    def product(ctx, first):
        copies = batch(ctx)
        for copy in copies:
            copy.start()
        for copy in copies:
            copy.wait()
        chunk = sz.width // 4
        for n in range(4):
            cols = slice(n * chunk, (n + 1) * chunk)
            value = tn_dot(j_s[...], d_s[: n_dp * sz.rows, cols])
            tail = d_s[n_dp * sz.rows : n_dp * sz.rows + 16, cols].astype(jnp.float32)
            for d in range(1, n_dp):
                at = n_dp * sz.rows + 16 * d
                tail = tail + d_s[at : at + 16, cols].astype(jnp.float32)
            if first:
                adapter_grad[:depth, cols] = value
                adapter_grad[depth : depth + 16, cols] = tail
            else:
                adapter_grad[:depth, cols] += value
                adapter_grad[depth : depth + 16, cols] += tail

    own = pltpu.make_async_copy(low, landed.at[place.dp * sz.n_context + place.ctx], d_sem.at[0, 0])
    own.start()
    rest = adapter_grad.shape[0] - depth - 16
    if rest:
        adapter_grad[depth + 16 :, :] = jnp.zeros((rest, sz.width), jnp.float32)
    for s in range(n_dp - 1):
        ring_step()
        plane.step(s)
    own.wait()
    product(place.ctx, True)
    for s in range(n_dp):
        plane.wait_near(s)
    product(1 - place.ctx, False)
    for k in range(SUM_PARTS):
        line.start(k)
    ring_step()
    ring_step()
    swap.wait()
    rows_s[place.group] = low[keep_rows, :]
    rows_s[1 - place.group] = swap_in[...]
    rows = rows_s[...].reshape(sz.rows, sz.width)
    ring_step()
    for k in range(SUM_PARTS):
        line.cross_over(k)
    ring_step()
    for b, copy in enumerate(weight_load):
        copy.wait()
        part = nt_dot(rows, weight_s[...]).reshape(sz.seqs, sz.block, weight_s.shape[0])
        embed_grad[:, :, b * weight_s.shape[0] : (b + 1) * weight_s.shape[0]] = part
        if b + 1 < len(weight_load):
            weight_load[b + 1].start()
    ring_step()
    for k in range(SUM_PARTS):
        line.share(k)
        ring_step()
    while grads.left():
        ring_step()
    for k in range(SUM_PARTS):
        line.complete(k)
    saves = [
        pltpu.make_async_copy(adapter_grad.at[pl.ds(0, depth)], adapter_out, out_sem.at[0]),
        pltpu.make_async_copy(adapter_grad.at[pl.ds(depth, 16)], gains_out, out_sem.at[1]),
    ]
    for copy in saves:
        copy.start()
    for w in range(count):
        outs[w][...] = deliver.total(w)
    for copy in saves:
        copy.wait()
    grads.finish()
    deliver.finish()
    plane.finish()
    line.finish()


def grads_tasks(n_dp, count):
    others = [(w + 1, s) for w, s in GradRing.all_tasks(n_dp, count - 1)]
    return [(0, s) for s in range(2, n_dp)] + others


def run_grads(sz, n_dp, low, joined, adapter, up_part, xs, ys):
    count, bf16, f32, dma = len(xs), jnp.bfloat16, jnp.float32, pltpu.SemaphoreType.DMA
    shape = jax.ShapeDtypeStruct
    depth = sz.width // (n_dp * sz.n_context)
    wide = [y.shape[1] for y in ys]
    slots, columns = joined.shape[0], joined.shape[2]
    unit = 16 * sz.half * SUM_PARTS
    total_rows = -(-(columns + 16) // unit) * unit
    return pl.pallas_call(
        partial(grads_kernel, sz, n_dp, count),
        out_shape=[shape((depth, n), f32) for n in wide]
        + [
            shape((sz.seqs, sz.block, sz.width), f32),
            shape((columns, sz.width), f32),
            shape((16, sz.width), f32),
            shape((slots,) + low.shape, bf16),
        ],
        in_specs=[full_spec()] + [any_spec()] * (3 + 2 * count),
        out_specs=[full_spec()] * (1 + count) + [any_spec()] * 3,
        scratch_shapes=GradRing.scratch(sz, n_dp, grads_tasks(n_dp, count), wide)
        + Deliver.scratch(sz, n_dp, wide)
        + PlaneRows.scratch(n_dp)
        + LineSum.scratch(sz, SUM_PARTS, total_rows // (sz.half * SUM_PARTS))
        + [
            pltpu.VMEM((total_rows, sz.width), f32),
            pltpu.VMEM((n_dp * (sz.rows + 16), sz.width), bf16),
            pltpu.VMEM((n_dp * sz.rows, columns), bf16),
            pltpu.VMEM((columns, sz.width), bf16),
            pltpu.VMEM((sz.seqs, sz.block, sz.width), bf16),
            pltpu.VMEM((sz.block, sz.width), bf16),
            dma((n_dp, 2)),
            dma((n_dp,)),
            dma,
            dma((2,)),
            dma((2,)),
        ],
        compiler_params=pltpu.CompilerParams(
            collective_id=8, has_side_effects=True, vmem_limit_bytes=VMEM_BYTES
        ),
        cost_estimate=pl.CostEstimate(
            flops=2 * sz.seq_len * sz.width * sum(wide), bytes_accessed=60 << 20, transcendentals=0
        ),
        name="grads",
    )(low, joined, adapter, up_part, *[slot_columns(sz, n_dp, x) for x in xs], *ys)


def shards(
    embedded,
    initial_state,
    cotangent,
    doc_ids,
    recurrences,
    adapter_weight,
    norm_gains,
    qkv_weight,
    output_head_weight,
    gate_up_weight,
    down_weight,
):
    n_dp = lax.axis_size("dp")
    n_tensor = lax.axis_size("tensor")
    n_context = lax.axis_size("context")
    dp_index = lax.axis_index("dp")
    t_index = lax.axis_index("tensor")
    ctx_index = lax.axis_index("context")
    seq_count, block_rows, model_width = embedded.shape
    seq_len = doc_ids.shape[1]
    half = n_tensor // seq_count
    group = t_index // half
    part = t_index % half
    heads_here = qkv_weight.shape[1]
    head_dim = qkv_weight.shape[2] // 3
    ff_here = down_weight.shape[0]
    def side_by_side(blocks):
        count, depth, columns = blocks.shape
        return blocks.transpose(1, 0, 2).reshape(depth, count * columns)

    def role_grad(grad, axis):
        piece = lax.psum_scatter(
            grad.astype(jnp.bfloat16), "dp", scatter_dimension=axis, tiled=True
        )
        low, high = jnp.split(piece, 2, axis=axis)
        give = [jnp.where(group == 0, low, high), jnp.where(group == 0, high, low)]
        back = [
            lax.ppermute(g, ("tensor", "context"), [(b, a) for a, b in perm])
            for g, perm in zip(give, role_perms)
        ]
        return back[0].astype(jnp.float32) + back[1].astype(jnp.float32)

    def gather_rows(rows):
        full = lax.all_gather(
            rows, ("tensor", "context"), axis=0, tiled=True, axis_index_groups=groups
        )
        split = full.reshape(half, n_context, seq_count, block_rows, model_width)
        return split.transpose(2, 0, 1, 3, 4).reshape(seq_len, model_width)

    sz = Sizes(
        n_tensor,
        n_context,
        seq_count,
        half,
        block_rows,
        n_context * block_rows,
        seq_count * block_rows,
        seq_len,
        model_width,
        heads_here,
        head_dim,
        ff_here,
    )
    adapter_block = adapter_weight.shape[0]
    gain_columns = norm_gains.shape[1]
    unit = 16 * half
    padded = -(-(adapter_block + 2) // unit) * unit
    adapter_rows = jnp.concatenate(
        [
            adapter_weight,
            jnp.pad(
                norm_gains,
                ((0, padded - adapter_block - 2), (0, model_width - gain_columns)),
            ),
        ],
        axis=0,
    )
    (
        adapter_all,
        out_blocks,
        qkv_use,
        gate_use,
        up_use,
        down_blocks,
        embed_rows,
        cot_rows,
        grad_ffn,
        embed_part,
        current,
    ) = run_weights(
        sz,
        n_dp,
        adapter_rows,
        adapter_block,
        [
            output_head_weight.reshape(heads_here * head_dim, -1),
            qkv_weight.reshape(qkv_weight.shape[0], -1),
            gate_up_weight[:, 0],
            gate_up_weight[:, 1],
            down_weight,
        ],
        [embedded, initial_state, cotangent],
    )
    qkv_use = qkv_use.reshape(model_width, -1)
    gate_use = gate_use.reshape(model_width, -1)
    up_use = up_use.reshape(model_width, -1)
    gains_full = (
        adapter_all[:, adapter_block : adapter_block + 2, :gain_columns]
        .transpose(1, 0, 2)
        .reshape(2, model_width)
    )
    if out_blocks.shape[2] % 128:
        out_blocks = side_by_side(out_blocks)[None]
        down_blocks = side_by_side(down_blocks)[None]
    gains_f = gains_full.astype(jnp.float32)

    cos_full, sin_full = rope_tables(seq_len, head_dim)
    own_seq = dp_index * seq_count + group
    docs = lax.dynamic_index_in_dim(doc_ids, own_seq, 0, keepdims=False)
    begin = jnp.sum((docs[None, :] < docs[:, None]).astype(jnp.int32), axis=1)[None, :]
    steps_own = lax.dynamic_index_in_dim(recurrences, own_seq, 0, keepdims=False) - BACK
    for step_index in range(MAXR - BACK):
        active = jnp.broadcast_to((step_index < steps_own).astype(jnp.float32), (1, model_width))
        current = run_round(
            sz, current, active, gains_f, cos_full, sin_full, begin, embed_part,
            adapter_all, qkv_use, out_blocks, gate_use, up_use, down_blocks,
        )
    detached = current
    (mixed_rows, adapted, feature_rows, query_hm, key_hm, value_hm, head_flat, lse, joined) = run_attn(
        sz, n_dp, True, detached, embed_part, gains_f, cos_full, sin_full, begin,
        adapter_all, qkv_use, out_blocks, embed_rows,
    )
    (current, ffn_input, gate_pre, up_pre, hidden) = run_ffn(
        sz, True, mixed_rows, detached, gains_f[:1], gains_f, gate_use, up_use, down_blocks
    )
    grad_mixed, gain_b, grad_gate, grad_up, down_sum, gate_part = run_ffn_back(
        sz, n_dp, cot_rows, mixed_rows, gains_f, grad_ffn, gate_pre, up_pre,
        gate_use, up_use, down_blocks, ffn_input, hidden,
    )
    grad_low, down_t, gate_s, state_out, grad_rows, grad_proj, up_part = run_attn_back(
        sz, n_dp, grad_mixed, adapted, gains_f, cos_full, sin_full, begin, gain_b, current,
        query_hm, key_hm, value_hm, lse, out_blocks, qkv_use, ffn_input, grad_gate, grad_up, down_sum,
        gate_part,
    )
    up_s, qkv_s, out_t, embed_out, adapter_s, gains_rows, _ = run_grads(
        sz,
        n_dp,
        grad_low,
        joined,
        adapter_all,
        up_part,
        [ffn_input, feature_rows, grad_rows],
        [grad_up, grad_proj, head_flat],
    )
    place_at = (dp_index * n_context + ctx_index) * gain_columns
    gains_s = lax.dynamic_slice_in_dim(gains_rows[:2], place_at, gain_columns, 1)
    down_s = down_t.T
    out_s = out_t.T.reshape(heads_here, head_dim, -1)
    qkv_s = qkv_s.reshape(-1, heads_here, 3 * head_dim)
    gate_up_s = jnp.stack([gate_s, up_s], axis=1)
    return (state_out, embed_out, adapter_s, gains_s, qkv_s, out_s, gate_up_s, down_s)


def solution(mesh):
    placed = (
        P("dp", ("tensor", "context"), None),
        P("dp", ("tensor", "context"), None),
        P("dp", ("tensor", "context"), None),
        P(),
        P(),
        P(("dp", "context"), None),
        P(None, ("dp", "context")),
        P(("dp", "context"), "tensor", None),
        P("tensor", None, ("dp", "context")),
        P(("dp", "context"), None, "tensor"),
        P("tensor", ("dp", "context")),
    )
    return jax.shard_map(
        shards,
        mesh=mesh,
        in_specs=placed,
        out_specs=(
            P("dp", ("tensor", "context"), None),
            P("dp", ("tensor", "context"), None),
            P(("dp", "context"), None),
            P(None, ("dp", "context")),
            P(("dp", "context"), "tensor", None),
            P("tensor", None, ("dp", "context")),
            P(("dp", "context"), None, "tensor"),
            P("tensor", ("dp", "context")),
        ),
        check_vma=False,
    )
```

```python
from functools import partial
import math
from typing import NamedTuple

import jax
import jax.numpy as jnp
import numpy as np
from jax import lax
from jax.experimental import pallas as pl
from jax.experimental.pallas import tpu as pltpu
from jax.sharding import PartitionSpec as P

BACK = 1
MAXR = 4


rope_base = 50000.0
norm_eps = 1e-06
masked_score = -1e30


def rope_tables(seq_len, head_dim):
    freq_index = np.arange(head_dim // 2, dtype=np.float32)
    inv_freq = 1.0 / np.float32(rope_base) ** (np.float32(2.0) * freq_index / head_dim)
    angles = np.arange(seq_len, dtype=np.float32)[:, None] * inv_freq.astype(np.float32)[None, :]
    cos_t, sin_t = np.cos(angles), np.sin(angles)
    return (
        jnp.asarray(np.concatenate([cos_t, cos_t], axis=1), jnp.float32),
        jnp.asarray(np.concatenate([-sin_t, sin_t], axis=1), jnp.float32),
    )


MESH = pl.DeviceIdType.MESH
LOG2E = 1.4426950408889634
VMEM_BYTES = 62 << 20


class Sizes(NamedTuple):
    n_tensor: int
    n_context: int
    seqs: int
    half: int
    block: int
    tile: int
    rows: int
    seq_len: int
    width: int
    heads: int
    head_dim: int
    ff: int


def full_spec():
    return pl.BlockSpec(memory_space=pltpu.VMEM)


def any_spec():
    return pl.BlockSpec(memory_space=pl.ANY)


def nt_dot(a, b):
    return lax.dot_general(a, b, (((1,), (1,)), ((), ())), preferred_element_type=jnp.float32)


def tn_dot(a, b):
    return lax.dot_general(a, b, (((0,), (0,)), ((), ())), preferred_element_type=jnp.float32)


def nn_dot(a, b):
    return jnp.dot(a, b, preferred_element_type=jnp.float32)


class Place:
    def __init__(self, sz):
        t = lax.axis_index("tensor")
        self.sz = sz
        self.dp = lax.axis_index("dp")
        self.ctx = lax.axis_index("context")
        self.group = t // sz.half
        self.part = lax.rem(t, sz.half)

    def device(self, part, ctx):
        return (self.dp, self.group * self.sz.half + part, ctx)

    def ahead(self, q):
        return lax.rem(self.part + q, self.sz.half)

    def behind(self, q):
        return lax.rem(self.part + (self.sz.half - q), self.sz.half)

    def sibling(self):
        return self.device(self.part, 1 - self.ctx)

    def block(self, part, ctx, j):
        sz = self.sz
        first = ((part + j * sz.half) * sz.n_context + ctx) * sz.block
        return pl.ds(pl.multiple_of(first, sz.block), sz.block)

    def tile(self, q, j):
        sz = self.sz
        first = (self.ahead(q) + j * sz.half) * sz.tile
        return pl.ds(pl.multiple_of(first, sz.tile), sz.tile)

    def enter(self, others=(), more=0):
        barrier = pltpu.get_barrier_semaphore()
        for device in others:
            pl.semaphore_signal(barrier, inc=1, device_id=device, device_id_type=MESH)
        pl.semaphore_signal(
            barrier, inc=1, device_id=self.sibling(), device_id_type=MESH
        )
        for q in range(1, self.sz.half):
            pl.semaphore_signal(
                barrier,
                inc=1,
                device_id=self.device(self.ahead(q), self.ctx),
                device_id_type=MESH,
            )
        pl.semaphore_wait(barrier, self.sz.half + len(others) + more)


class Gather:
    @staticmethod
    def scratch(sz):
        kinds = 2 * sz.half - 1
        return [
            pltpu.SemaphoreType.DMA((kinds, sz.seqs)),
            pltpu.SemaphoreType.DMA((kinds, sz.seqs)),
        ]

    def __init__(self, place, ref, send, recv):
        self.place, self.ref, self.send, self.recv = place, ref, send, recv

    def copy(self, kind, j, rows):
        place, half = self.place, self.place.sz.half
        if 0 < kind < half:
            target = place.device(place.ahead(kind), place.ctx)
        else:
            target = place.sibling()
        return pltpu.make_async_remote_copy(
            src_ref=self.ref.at[rows],
            dst_ref=self.ref.at[rows],
            send_sem=self.send.at[kind, j],
            recv_sem=self.recv.at[kind, j],
            device_id=target,
            device_id_type=MESH,
        )

    def own(self, j):
        return self.place.block(self.place.part, self.place.ctx, j)

    def start(self, j):
        for q in range(1, self.place.sz.half):
            self.copy(q, j, self.own(j)).start()
        self.copy(0, j, self.own(j)).start()

    def wait_near(self, j):
        place = self.place
        self.copy(0, j, place.block(place.part, 1 - place.ctx, j)).wait_recv()

    def forward(self, q, j):
        place = self.place
        rows = place.block(place.behind(q), place.ctx, j)
        self.copy(q, j, rows).wait_recv()
        self.copy(place.sz.half - 1 + q, j, rows).start()

    def wait_far(self, q, j):
        place = self.place
        rows = place.block(place.behind(q), 1 - place.ctx, j)
        self.copy(place.sz.half - 1 + q, j, rows).wait_recv()

    def passed_on(self, j):
        place, half = self.place, self.place.sz.half
        for q in range(1, half):
            rows = place.block(place.behind(q), place.ctx, j)
            self.copy(half - 1 + q, j, rows).wait_send()

    def finish(self, forwards=True):
        for j in range(self.place.sz.seqs):
            for kind in range(self.place.sz.half):
                self.copy(kind, j, self.own(j)).wait_send()
            if forwards:
                self.passed_on(j)


class Scatter:
    @staticmethod
    def scratch(sz):
        kinds = 2 * sz.half - 1
        near = (sz.half, sz.seqs, sz.block, sz.width)
        far = (max(sz.half - 1, 1), sz.seqs, sz.block, sz.width)
        return [
            pltpu.VMEM((sz.tile, sz.width), jnp.float32),
            pltpu.VMEM(near, jnp.bfloat16),
            pltpu.VMEM(near, jnp.bfloat16),
            pltpu.VMEM(near, jnp.bfloat16),
            pltpu.VMEM(far, jnp.bfloat16),
            pltpu.VMEM(far, jnp.bfloat16),
            pltpu.SemaphoreType.DMA((kinds, sz.seqs)),
            pltpu.SemaphoreType.DMA((kinds, sz.seqs)),
        ]

    def __init__(self, place, part, mine, near_out, near_in, far_out, far_in, send, recv):
        self.place, self.part, self.mine = place, part, mine
        self.near_out, self.near_in = near_out, near_in
        self.far_out, self.far_in = far_out, far_in
        self.send, self.recv = send, recv

    def near(self, q, j):
        return pltpu.make_async_remote_copy(
            src_ref=self.near_out.at[q, j],
            dst_ref=self.near_in.at[q, j],
            send_sem=self.send.at[q, j],
            recv_sem=self.recv.at[q, j],
            device_id=self.place.sibling(),
            device_id_type=MESH,
        )

    def far(self, q, j):
        place = self.place
        return pltpu.make_async_remote_copy(
            src_ref=self.far_out.at[q - 1, j],
            dst_ref=self.far_in.at[q - 1, j],
            send_sem=self.send.at[place.sz.half - 1 + q, j],
            recv_sem=self.recv.at[place.sz.half - 1 + q, j],
            device_id=place.device(place.ahead(q), place.ctx),
            device_id_type=MESH,
        )

    def give(self, q, j):
        sz, ctx = self.place.sz, self.place.ctx
        mine = pl.ds(pl.multiple_of(ctx * sz.block, sz.block), sz.block)
        other = pl.ds(pl.multiple_of((1 - ctx) * sz.block, sz.block), sz.block)
        self.near_out[q, j] = self.part[other, :].astype(jnp.bfloat16)
        self.near(q, j).start()
        self.mine[q, j] = self.part[mine, :].astype(jnp.bfloat16)

    def onward(self, q, j):
        self.near(q, j).wait_recv()
        self.far_out[q - 1, j] = (
            self.mine[q, j].astype(jnp.float32) + self.near_in[q, j].astype(jnp.float32)
        ).astype(jnp.bfloat16)
        self.far(q, j).start()

    def total(self, j):
        self.near(0, j).wait_recv()
        total = self.mine[0, j].astype(jnp.float32) + self.near_in[0, j].astype(jnp.float32)
        for q in range(1, self.place.sz.half):
            self.far(q, j).wait_recv()
            total = total + self.far_in[q - 1, j].astype(jnp.float32)
        return total

    def finish(self):
        half = self.place.sz.half
        for j in range(self.place.sz.seqs):
            for q in range(half):
                self.near(q, j).wait_send()
            for q in range(1, half):
                self.far(q, j).wait_send()


def column_loads(blocks_ref, vmem_ref, sem):
    count, _, columns = blocks_ref.shape
    return [
        pltpu.make_async_copy(
            blocks_ref.at[b], vmem_ref.at[:, pl.ds(b * columns, columns)], sem.at[b]
        )
        for b in range(count)
    ]


def adapter_loads(blocks_ref, vmem_ref, sem):
    count, tops = sem.shape
    depth, columns = vmem_ref.shape[0] // tops, vmem_ref.shape[1] // count
    return [
        [
            pltpu.make_async_copy(
                blocks_ref.at[b, pl.ds(0, depth), pl.ds(n * columns, columns)],
                vmem_ref.at[pl.ds(b * depth, depth), pl.ds(n * columns, columns)],
                sem.at[n, b],
            )
            for b in range(tops)
        ]
        for n in range(count)
    ]


def rms_factor(rows):
    return lax.rsqrt(jnp.mean(rows * rows, axis=-1, keepdims=True) + norm_eps)


def turn(x, cos_t, sin_t):
    return x * cos_t + pltpu.roll(x, x.shape[-1] // 2, 1) * sin_t


def attn_kernel(sz, n_dp, keep, *refs):
    (latent, embed, gains, cos_t, sin_t, begin, adapter_hbm, qkv_hbm, out_hbm) = refs[:9]
    refs = refs[9:]
    if keep:
        embed_hbm, refs = refs[0], refs[1:]
    mixed = refs[0]
    refs = refs[1:]
    if keep:
        adapted_out, rows_out, q_out, k_out, v_out, head_out, lse_out, joined_out = refs[:8]
        refs = refs[8:]
    (wa, wqkv, wout, adapted, rows_s, q_s, k_s, v_s, head_s, lse_s) = refs[:10]
    load_a, load_qkv, load_out, keep_sem = refs[10:14]
    gather_refs = refs[14:16]
    scatter_refs = refs[16:24]
    if keep:
        joined_s, load_embed, x_send, x_recv = refs[24:]

    place = Place(sz)
    a_loads = adapter_loads(adapter_hbm, wa, load_a)
    qkv_load = pltpu.make_async_copy(qkv_hbm, wqkv, load_qkv)
    out_loads = column_loads(out_hbm, wout, load_out)
    for group in a_loads:
        for copy in group:
            copy.start()
    qkv_load.start()
    for copy in out_loads:
        copy.start()
    others = []
    if keep:
        ring = Ring(place, n_dp)
        t = lax.axis_index("tensor")
        embed_load = pltpu.make_async_copy(
            embed_hbm, joined_s.at[:, pl.ds(sz.width, sz.width)], load_embed
        )
        embed_load.start()
        plane = [(o, c) for o in range(n_dp) for c in range(2) if (o, c) != (0, 0)]

        def member(o, c):
            return (ring.index(o), t, place.ctx if c == 0 else 1 - place.ctx)

        def columns_to(o, c):
            to = member(o, c)
            depth = joined_out.shape[2]
            first = pl.multiple_of((to[0] * sz.n_context + to[2]) * depth, depth)
            return pltpu.make_async_remote_copy(
                src_ref=joined_s.at[:, pl.ds(first, depth)],
                dst_ref=joined_out.at[place.dp * sz.n_context + place.ctx],
                send_sem=x_send.at[o, c],
                recv_sem=x_recv.at[o, c],
                device_id=to,
                device_id_type=MESH,
            )

        def columns_from(o, c):
            ref = joined_out.at[
                ring.index(-o) * sz.n_context + (place.ctx if c == 0 else 1 - place.ctx)
            ]
            return pltpu.make_async_remote_copy(
                src_ref=ref,
                dst_ref=ref,
                send_sem=x_send.at[o, c],
                recv_sem=x_recv.at[o, c],
                device_id=place.sibling(),
                device_id_type=MESH,
            )

        others = [member(o, c) for o, c in plane if o]
    place.enter(others)
    gather = Gather(place, rows_s, *gather_refs)
    scatter = Scatter(place, *scatter_refs)

    low = latent[...].astype(jnp.bfloat16)
    columns = sz.width // len(a_loads)
    square = None
    for n, group in enumerate(a_loads):
        for copy in group:
            copy.wait()
        cols = pl.ds(n * columns, columns)
        chunk = nn_dot(low, wa[:, cols]) + embed[:, cols]
        adapted[:, cols] = chunk
        here = jnp.sum(chunk * chunk, axis=-1, keepdims=True)
        square = here if square is None else square + here
    factor = lax.rsqrt(square / sz.width + norm_eps)
    for j in range(sz.seqs):
        span = slice(j * sz.block, (j + 1) * sz.block)
        normed = (adapted[span, :] * factor[span]) * gains[0:1, :]
        rows_s[gather.own(j), :] = normed.astype(jnp.bfloat16)
        gather.start(j)

    qkv_load.wait()
    pair = min(2, sz.heads)
    d = sz.head_dim

    def project(q, j):
        rows = place.tile(q, j)
        x = rows_s[rows, :]
        cos_here, sin_here = cos_t[rows, :], sin_t[rows, :]
        for h0 in range(0, sz.heads, pair):
            proj = nn_dot(x, wqkv[:, 3 * d * h0 : 3 * d * (h0 + pair)])
            for h in range(pair):
                at = 3 * d * h
                q_s[h0 + h, rows, :] = turn(proj[:, at : at + d], cos_here, sin_here).astype(
                    jnp.bfloat16
                )
                k_s[h0 + h, rows, :] = turn(
                    proj[:, at + d : at + 2 * d], cos_here, sin_here
                ).astype(jnp.bfloat16)
                v_s[h0 + h, rows, :] = proj[:, at + 2 * d : at + 3 * d].astype(jnp.bfloat16)

    def attend(q, j):
        rows = place.tile(q, j)
        first = (place.ahead(q) + j * sz.half) * sz.tile
        length = (j + 1) * sz.half * sz.tile
        start = begin[:, pl.ds(pl.multiple_of(first, sz.tile), sz.tile)]
        key_at = lax.broadcasted_iota(jnp.int32, (length, sz.tile), 0)
        query_at = first + lax.broadcasted_iota(jnp.int32, (1, sz.tile), 1)
        allowed = (key_at >= start) & (key_at <= query_at)

        def head(h, carry):
            scores = nt_dot(k_s[h, 0:length, :], q_s[h, rows, :])
            scores = jnp.where(allowed, scores * (LOG2E / math.sqrt(d)), masked_score)
            top = jnp.max(scores, axis=0, keepdims=True)
            weight = jnp.exp2(scores - top)
            total = jnp.sum(weight, axis=0, keepdims=True)
            mixed_t = tn_dot(v_s[h, 0:length, :], weight.astype(jnp.bfloat16))
            result = jnp.transpose(mixed_t / total)
            head_s[rows, pl.ds(pl.multiple_of(h * d, d), d)] = result.astype(jnp.bfloat16)
            if keep:
                lse_s[h, :, rows] = top + jnp.log2(total)
            return carry

        lax.fori_loop(0, sz.heads, head, 0)

    def give(q, j):
        rows = place.tile(q, j)
        scatter.part[...] = nn_dot(head_s[rows, :], wout[...])
        scatter.give(q, j)

    copies = []

    def save(src, dst):
        copy = pltpu.make_async_copy(src, dst, keep_sem.at[len(copies)])
        copy.start()
        copies.append(copy)

    if keep:
        save(adapted, adapted_out)
        joined_s[:, : sz.width] = low
        embed_load.wait()
        for o, c in plane:
            columns_to(o, c).start()
        mine = place.dp * sz.n_context + place.ctx
        depth = joined_out.shape[2]
        save(
            joined_s.at[:, pl.ds(pl.multiple_of(mine * depth, depth), depth)], joined_out.at[mine]
        )
    far = range(1, sz.half)
    for j in range(sz.seqs):
        gather.wait_near(j)
        project(0, j)
    for copy in out_loads:
        copy.wait()
    for j in range(sz.seqs):
        for q in far:
            gather.forward(q, j)
        for q in far:
            gather.wait_far(sz.half - q, j)
            project(q, j)
        for q in far:
            attend(q, j)
            give(q, j)
        attend(0, j)
        for q in far:
            scatter.onward(q, j)
        give(0, j)
    if keep:
        for src, dst in ((rows_s, rows_out), (q_s, q_out), (k_s, k_out), (v_s, v_out)):
            save(src, dst)
        save(head_s, head_out)
        save(lse_s, lse_out)
    gather.finish()
    for j in range(sz.seqs):
        span = slice(j * sz.block, (j + 1) * sz.block)
        mixed[span, :] = adapted[span, :] + scatter.total(j)
    scatter.finish()
    if keep:
        for o, c in plane:
            columns_from(o, c).wait_recv()
            columns_to(o, c).wait_send()
    for copy in copies:
        copy.wait()


def run_attn(
    sz, n_dp, keep, latent, embed_part, gains, cos_t, sin_t, begin, adapter, qkv, out, *embed
):
    f32, bf16 = jnp.float32, jnp.bfloat16
    heads_shape = (sz.heads, sz.seq_len, sz.head_dim)
    shape = jax.ShapeDtypeStruct
    outs = [shape((sz.rows, sz.width), f32)]
    if keep:
        outs += [
            shape((sz.rows, sz.width), f32),
            shape((sz.seq_len, sz.width), bf16),
            shape(heads_shape, bf16),
            shape(heads_shape, bf16),
            shape(heads_shape, bf16),
            shape((sz.seq_len, sz.heads * sz.head_dim), bf16),
            shape((sz.heads, 1, sz.seq_len), f32),
            shape((adapter.shape[0], sz.rows, 2 * sz.width // adapter.shape[0]), bf16),
        ]
    scratch = [
        pltpu.VMEM((sz.width, sz.width), bf16),
        pltpu.VMEM(qkv.shape, bf16),
        pltpu.VMEM((sz.heads * sz.head_dim, sz.width), bf16),
        pltpu.VMEM((sz.rows, sz.width), f32),
        pltpu.VMEM((sz.seq_len, sz.width), bf16),
        pltpu.VMEM(heads_shape, bf16),
        pltpu.VMEM(heads_shape, bf16),
        pltpu.VMEM(heads_shape, bf16),
        pltpu.VMEM((sz.seq_len, sz.heads * sz.head_dim), bf16),
        pltpu.VMEM((sz.heads, 1, sz.seq_len), f32),
        pltpu.SemaphoreType.DMA((4, adapter.shape[0] // 2)),
        pltpu.SemaphoreType.DMA,
        pltpu.SemaphoreType.DMA((out.shape[0],)),
        pltpu.SemaphoreType.DMA((8,)),
    ]
    scratch += Gather.scratch(sz) + Scatter.scratch(sz)
    if keep:
        scratch += [
            pltpu.VMEM((sz.rows, 2 * sz.width), bf16),
            pltpu.SemaphoreType.DMA,
            pltpu.SemaphoreType.DMA((n_dp, 2)),
            pltpu.SemaphoreType.DMA((n_dp, 2)),
        ]
    flops = 2 * sz.rows * sz.width * sz.width + 2 * sz.seq_len * sz.width * qkv.shape[1]
    return pl.pallas_call(
        partial(attn_kernel, sz, n_dp, keep),
        out_shape=outs,
        in_specs=[full_spec()] * 6 + [any_spec()] * (3 + len(embed)),
        out_specs=[full_spec()] + [any_spec()] * (len(outs) - 1),
        scratch_shapes=scratch,
        compiler_params=pltpu.CompilerParams(
            collective_id=2 if keep else 1, has_side_effects=True, vmem_limit_bytes=VMEM_BYTES
        ),
        cost_estimate=pl.CostEstimate(
            flops=flops, bytes_accessed=20 << 20, transcendentals=0
        ),
        name="attn_keep" if keep else "attn_round",
    )(latent, embed_part, gains, cos_t, sin_t, begin, adapter, qkv, out, *embed)


def ffn_kernel(sz, keep, *refs):
    (mixed, latent, active, gains, gate_hbm, up_hbm, down_hbm, result) = refs[:8]
    refs = refs[8:]
    if keep:
        rows_out, gate_out, up_out, hidden_out = refs[:4]
        refs = refs[4:]
    wg, wu, wd, rows_s = refs[:4]
    refs = refs[4:]
    if keep:
        gate_s, up_s, hidden_s = refs[:3]
        refs = refs[3:]
    load_gu, load_down, keep_sem = refs[:3]
    gather_refs = refs[3:5]
    scatter_refs = refs[5:]

    place = Place(sz)
    gate_load = pltpu.make_async_copy(gate_hbm, wg, load_gu.at[0])
    up_load = pltpu.make_async_copy(up_hbm, wu, load_gu.at[1])
    down_loads = column_loads(down_hbm, wd, load_down)
    gate_load.start()
    up_load.start()
    for copy in down_loads:
        copy.start()
    place.enter()
    gather = Gather(place, rows_s, *gather_refs)
    scatter = Scatter(place, *scatter_refs)
    for j in range(sz.seqs):
        span = slice(j * sz.block, (j + 1) * sz.block)
        rows = mixed[span, :]
        normed = (rows * rms_factor(rows)) * gains[1:2, :]
        rows_s[gather.own(j), :] = normed.astype(jnp.bfloat16)
        gather.start(j)
    gate_load.wait()
    up_load.wait()
    for copy in down_loads:
        copy.wait()

    copies = []

    def save(src, dst):
        copy = pltpu.make_async_copy(src, dst, keep_sem.at[len(copies)])
        copy.start()
        copies.append(copy)

    def work(q, j):
        rows = place.tile(q, j)
        x = rows_s[rows, :]
        gate = nn_dot(x, wg[...])
        up = nn_dot(x, wu[...])
        hidden = (gate / (1.0 + jnp.exp(-gate)) * up).astype(jnp.bfloat16)
        if keep:
            gate_s[rows, :] = gate.astype(jnp.bfloat16)
            up_s[rows, :] = up.astype(jnp.bfloat16)
            hidden_s[rows, :] = hidden
        scatter.part[...] = nn_dot(hidden, wd[...])
        scatter.give(q, j)

    far = range(1, sz.half)
    for j in range(sz.seqs):
        gather.wait_near(j)
        work(0, j)
    for j in range(sz.seqs):
        for q in far:
            gather.forward(q, j)
        for q in far:
            gather.wait_far(sz.half - q, j)
            work(q, j)
        for q in far:
            scatter.onward(q, j)
    if keep:
        save(rows_s, rows_out)
        save(gate_s, gate_out)
        save(up_s, up_out)
        save(hidden_s, hidden_out)
    gather.finish()
    for j in range(sz.seqs):
        span = slice(j * sz.block, (j + 1) * sz.block)
        total = mixed[span, :] + scatter.total(j)
        if not keep:
            total = jnp.where(active[...] > 0, total, latent[span, :])
        result[span, :] = total
    scatter.finish()
    for copy in copies:
        copy.wait()


def run_ffn(sz, keep, mixed, latent, active, gains, gate, up, down):
    f32, bf16 = jnp.float32, jnp.bfloat16
    shape = jax.ShapeDtypeStruct
    outs = [shape((sz.rows, sz.width), f32)]
    if keep:
        outs += [
            shape((sz.seq_len, sz.width), bf16),
            shape((sz.seq_len, sz.ff), bf16),
            shape((sz.seq_len, sz.ff), bf16),
            shape((sz.seq_len, sz.ff), bf16),
        ]
    scratch = [
        pltpu.VMEM(gate.shape, bf16),
        pltpu.VMEM(up.shape, bf16),
        pltpu.VMEM((sz.ff, sz.width), bf16),
        pltpu.VMEM((sz.seq_len, sz.width), bf16),
    ]
    if keep:
        scratch += [pltpu.VMEM((sz.seq_len, sz.ff), bf16)] * 3
    scratch += [
        pltpu.SemaphoreType.DMA((2,)),
        pltpu.SemaphoreType.DMA((down.shape[0],)),
        pltpu.SemaphoreType.DMA((4,)),
    ]
    scratch += Gather.scratch(sz) + Scatter.scratch(sz)
    return pl.pallas_call(
        partial(ffn_kernel, sz, keep),
        out_shape=outs,
        in_specs=[full_spec()] * 4 + [any_spec()] * 3,
        out_specs=[full_spec()] + [any_spec()] * (len(outs) - 1),
        scratch_shapes=scratch,
        compiler_params=pltpu.CompilerParams(
            collective_id=4 if keep else 3, has_side_effects=True, vmem_limit_bytes=VMEM_BYTES
        ),
        cost_estimate=pl.CostEstimate(
            flops=6 * sz.seq_len * sz.width * sz.ff, bytes_accessed=20 << 20, transcendentals=0
        ),
        name="ffn_keep" if keep else "ffn_round",
    )(mixed, latent, active, gains, gate, up, down)


def rounds_kernel(sz, count, *refs):
    (active, gains, cos_t, sin_t, begin) = refs[:5]
    (latent_hbm, embed_hbm, adapter_hbm, qkv_hbm, out_hbm, gate_hbm, up_hbm, down_hbm) = refs[5:13]
    result = refs[13]
    (wide, narrow, wg, wu, wd, embed, mixed, rows_s, q_s, k_s, v_s, head_s) = refs[14:26]
    load_rows, load_a, load_qkv, load_out, load_gu, load_down = refs[26:32]
    gather_refs, again_refs, scatter_refs = refs[32:34], refs[34:36], refs[36:44]
    columns = sz.width // 4
    depth_out = sz.heads * sz.head_dim

    place = Place(sz)
    row_loads = [
        pltpu.make_async_copy(latent_hbm, result, load_rows.at[0]),
        pltpu.make_async_copy(embed_hbm, embed, load_rows.at[1]),
    ]

    def adapter_columns(n):
        return wide.at[:, pl.ds(n * columns, columns)] if n < 3 else narrow

    tops = load_a.shape[1]
    depth = sz.width // tops
    a_loads = [
        [
            pltpu.make_async_copy(
                adapter_hbm.at[b, pl.ds(0, depth), pl.ds(n * columns, columns)],
                adapter_columns(n).at[pl.ds(b * depth, depth)],
                load_a.at[n, b],
            )
            for b in range(tops)
        ]
        for n in range(4)
    ]
    wqkv = wide.at[:, pl.ds(0, qkv_hbm.shape[1])]
    qkv_load = pltpu.make_async_copy(qkv_hbm, wqkv, load_qkv)
    out_loads = []
    for b in range(out_hbm.shape[0]):
        size = min(out_hbm.shape[2], columns)
        for at in range(0, out_hbm.shape[2], size):
            n, to = divmod(b * out_hbm.shape[2] + at, columns)
            out_loads.append(
                pltpu.make_async_copy(
                    out_hbm.at[b, :, pl.ds(at, size)],
                    narrow.at[pl.ds(n * depth_out, depth_out), pl.ds(to, size)],
                    load_out.at[len(out_loads)],
                )
            )
    ffn_loads = [
        pltpu.make_async_copy(gate_hbm, wg, load_gu.at[0]),
        pltpu.make_async_copy(up_hbm, wu, load_gu.at[1]),
    ] + column_loads(down_hbm, wd, load_down)

    def start_adapter():
        for group in a_loads:
            for copy in group:
                copy.start()

    def start_heads():
        qkv_load.start()
        for copy in out_loads:
            copy.start()

    for copy in row_loads:
        copy.start()
    start_adapter()
    place.enter()
    gather = Gather(place, rows_s, *gather_refs)
    again = Gather(place, rows_s, *again_refs)
    scatter = Scatter(place, *scatter_refs)
    for copy in row_loads:
        copy.wait()

    def spans(j):
        return slice(j * sz.block, (j + 1) * sz.block)

    def open_block(j):
        low = result[spans(j), :].astype(jnp.bfloat16)
        square = None
        for n, group in enumerate(a_loads):
            if j == 0:
                for copy in group:
                    copy.wait()
            cols = slice(n * columns, (n + 1) * columns)
            chunk = nn_dot(low, adapter_columns(n)[...]) + embed[spans(j), cols]
            mixed[spans(j), cols] = chunk
            here = jnp.sum(chunk * chunk, axis=-1, keepdims=True)
            square = here if square is None else square + here
        factor = lax.rsqrt(square / sz.width + norm_eps)
        normed = (mixed[spans(j), :] * factor) * gains[0:1, :]
        rows_s[gather.own(j), :] = normed.astype(jnp.bfloat16)
        gather.start(j)

    for j in range(sz.seqs):
        open_block(j)
    start_heads()
    for copy in ffn_loads:
        copy.start()
    pair = min(2, sz.heads)
    d = sz.head_dim

    def project(q, j):
        rows = place.tile(q, j)
        x = rows_s[rows, :]
        cos_here, sin_here = cos_t[rows, :], sin_t[rows, :]
        for h0 in range(0, sz.heads, pair):
            proj = nn_dot(x, wqkv[:, 3 * d * h0 : 3 * d * (h0 + pair)])
            for h in range(pair):
                at = 3 * d * h
                q_s[h0 + h, rows, :] = turn(proj[:, at : at + d], cos_here, sin_here).astype(
                    jnp.bfloat16
                )
                k_s[h0 + h, rows, :] = turn(
                    proj[:, at + d : at + 2 * d], cos_here, sin_here
                ).astype(jnp.bfloat16)
                v_s[h0 + h, rows, :] = proj[:, at + 2 * d : at + 3 * d].astype(jnp.bfloat16)

    def attend(q, j):
        rows = place.tile(q, j)
        first = (place.ahead(q) + j * sz.half) * sz.tile
        length = (j + 1) * sz.half * sz.tile
        start = begin[:, pl.ds(pl.multiple_of(first, sz.tile), sz.tile)]
        key_at = lax.broadcasted_iota(jnp.int32, (length, sz.tile), 0)
        query_at = first + lax.broadcasted_iota(jnp.int32, (1, sz.tile), 1)
        allowed = (key_at >= start) & (key_at <= query_at)

        def head(h, carry):
            scores = nt_dot(k_s[h, 0:length, :], q_s[h, rows, :])
            scores = jnp.where(allowed, scores * (LOG2E / math.sqrt(d)), masked_score)
            top = jnp.max(scores, axis=0, keepdims=True)
            weight = jnp.exp2(scores - top)
            total = jnp.sum(weight, axis=0, keepdims=True)
            mixed_t = tn_dot(v_s[h, 0:length, :], weight.astype(jnp.bfloat16))
            result = jnp.transpose(mixed_t / total)
            head_s[rows, pl.ds(pl.multiple_of(h * d, d), d)] = result.astype(jnp.bfloat16)
            return carry

        lax.fori_loop(0, sz.heads, head, 0)

    def give(q, j):
        rows = place.tile(q, j)
        for n in range(4):
            scatter.part[:, n * columns : (n + 1) * columns] = nn_dot(
                head_s[rows, :], narrow[n * depth_out : (n + 1) * depth_out, :]
            )
        scatter.give(q, j)

    def work(q, j):
        x = rows_s[place.tile(q, j), :]
        gate = nn_dot(x, wg[...])
        up = nn_dot(x, wu[...])
        hidden = (gate / (1.0 + jnp.exp(-gate)) * up).astype(jnp.bfloat16)
        scatter.part[...] = nn_dot(hidden, wd[...])
        scatter.give(q, j)

    far = range(1, sz.half)

    def one_round(r, carry):
        more = r + 1 < count
        qkv_load.wait()
        for j in range(sz.seqs):
            gather.wait_near(j)
            project(0, j)
        for copy in out_loads:
            copy.wait()
        for j in range(sz.seqs):
            for q in far:
                gather.forward(q, j)
            for q in far:
                gather.wait_far(sz.half - q, j)
                project(q, j)
            for q in far:
                attend(q, j)
                give(q, j)
            attend(0, j)
            gather.passed_on(j)
            for q in far:
                scatter.onward(q, j)
            give(0, j)
        gather.finish(forwards=False)
        pl.when(more)(start_adapter)
        for j in range(sz.seqs):
            rows = mixed[spans(j), :] + scatter.total(j)
            mixed[spans(j), :] = rows
            normed = (rows * rms_factor(rows)) * gains[1:2, :]
            rows_s[again.own(j), :] = normed.astype(jnp.bfloat16)
            again.start(j)
        scatter.finish()

        def first_loads():
            for copy in ffn_loads:
                copy.wait()

        pl.when(r == 0)(first_loads)
        for j in range(sz.seqs):
            again.wait_near(j)
            work(0, j)
        for j in range(sz.seqs):
            for q in far:
                again.forward(q, j)
            for q in far:
                again.wait_far(sz.half - q, j)
                work(q, j)
            again.passed_on(j)
            for q in far:
                scatter.onward(q, j)
        again.finish(forwards=False)
        on = active[pl.ds(r, 1), :] > 0
        for j in range(sz.seqs):
            total = mixed[spans(j), :] + scatter.total(j)
            result[spans(j), :] = jnp.where(on, total, result[spans(j), :])
            pl.when(more)(lambda j=j: open_block(j))
        pl.when(more)(start_heads)
        scatter.finish()
        return carry

    lax.fori_loop(0, count, one_round, 0)


def run_rounds(sz, latent, active, gains, cos_t, sin_t, begin, embed, adapter, qkv, out, gate, up, down):
    f32, bf16, dma = jnp.float32, jnp.bfloat16, pltpu.SemaphoreType.DMA
    heads_shape = (sz.heads, sz.seq_len, sz.head_dim)
    return pl.pallas_call(
        partial(rounds_kernel, sz, active.shape[0]),
        out_shape=jax.ShapeDtypeStruct((sz.rows, sz.width), f32),
        in_specs=[full_spec()] * 5 + [any_spec()] * 8,
        out_specs=full_spec(),
        scratch_shapes=[
            pltpu.VMEM((sz.width, max(3 * sz.width // 4, qkv.shape[1])), bf16),
            pltpu.VMEM((sz.width, sz.width // 4), bf16),
            pltpu.VMEM(gate.shape, bf16),
            pltpu.VMEM(up.shape, bf16),
            pltpu.VMEM((sz.ff, sz.width), bf16),
            pltpu.VMEM((sz.rows, sz.width), f32),
            pltpu.VMEM((sz.rows, sz.width), f32),
            pltpu.VMEM((sz.seq_len, sz.width), bf16),
            pltpu.VMEM(heads_shape, bf16),
            pltpu.VMEM(heads_shape, bf16),
            pltpu.VMEM(heads_shape, bf16),
            pltpu.VMEM((sz.seq_len, sz.heads * sz.head_dim), bf16),
            dma((2,)),
            dma((4, adapter.shape[0] // 2)),
            dma,
            dma((max(4, out.shape[0]),)),
            dma((2,)),
            dma((down.shape[0],)),
        ]
        + Gather.scratch(sz)
        + Gather.scratch(sz)
        + Scatter.scratch(sz),
        compiler_params=pltpu.CompilerParams(
            collective_id=1, has_side_effects=True, vmem_limit_bytes=VMEM_BYTES
        ),
        cost_estimate=pl.CostEstimate(
            flops=24 * sz.seq_len * sz.width * sz.ff, bytes_accessed=80 << 20, transcendentals=0
        ),
        name="rounds",
    )(active, gains, cos_t, sin_t, begin, latent, embed, adapter, qkv, out, gate, up, down)


def other_group(place):
    return (place.dp, (1 - place.group) * place.sz.half + place.part, place.ctx)


class Ring:
    def __init__(self, place, n_dp):
        self.place, self.count = place, n_dp
        self.at = self.swap(place.dp)

    def swap(self, i):
        if self.count != 4:
            return i
        x, y = lax.rem(i, 2), i // 2
        return 2 * y + x + y - 2 * x * y

    def index(self, offset):
        return self.swap(lax.rem(self.at + offset + 2 * self.count, self.count))

    def device(self, offset):
        return (self.index(offset), lax.axis_index("tensor"), self.place.ctx)


def weights_kernel(sz, n_dp, *refs):
    count = 5
    adapter_in, blocks_in = refs[0], refs[1 : 1 + count]
    rows_in, refs = refs[1 + count : 4 + count], refs[4 + count :]
    adapter_out, blocks_out = refs[0], refs[1 : 1 + count]
    embed_out, cot_out, cot_all, embed_part, state_out = refs[1 + count : 6 + count]
    refs = refs[6 + count :]
    (move_send, move_recv, ring_send, ring_recv, a_send, a_recv, x_send, x_recv, own_sem) = refs[:9]
    embed_s, state_s, weight_s, swap_send, swap_recv, keep_sem, weight_sem = refs[9:16]
    gather_refs = refs[16:]
    place = Place(sz)
    ring = Ring(place, n_dp)
    t = lax.axis_index("tensor")
    ctx, part, half, n_c = place.ctx, place.part, sz.half, sz.n_context
    role = part * n_c + ctx
    at_home = role == t
    steps = n_dp - 1
    sub = adapter_in.shape[0] // half
    ahead = 1 - 2 * ctx

    def holder(g):
        return (place.dp, g * half + t // n_c, lax.rem(t, n_c))

    barrier = pltpu.get_barrier_semaphore()

    def greet(device):
        pl.semaphore_signal(barrier, inc=1, device_id=device, device_id_type=MESH)

    greet(ring.device(1))
    greet(ring.device(n_dp - 1))
    greet(place.sibling())
    for q in range(1, half):
        greet(place.device(place.ahead(q), ctx))
    for c in range(n_c):
        pl.when(jnp.logical_not(at_home & (ctx == c)))(
            lambda c=c: greet((place.dp, role, c))
        )
    other = other_group(place)
    greet(other)
    waits = 3 + half + sz.seqs - jnp.where(at_home, 1, 0)
    pl.semaphore_wait(barrier, waits)

    own_at = pl.ds(pl.multiple_of(place.group * sz.block, sz.block), sz.block)
    other_at = pl.ds(pl.multiple_of((1 - place.group) * sz.block, sz.block), sz.block)
    rows_to = (embed_s, state_s, cot_out)

    def swap(i):
        return pltpu.make_async_remote_copy(
            src_ref=rows_in[i].at[1 - place.group],
            dst_ref=rows_to[i].at[own_at],
            send_sem=swap_send.at[i],
            recv_sem=swap_recv.at[i],
            device_id=other,
            device_id_type=MESH,
        )

    def swapped(i):
        ref = rows_to[i].at[other_at]
        return pltpu.make_async_remote_copy(
            src_ref=ref,
            dst_ref=ref,
            send_sem=swap_send.at[i],
            recv_sem=swap_recv.at[i],
            device_id=other,
            device_id_type=MESH,
        )

    def keep(i):
        return pltpu.make_async_copy(
            rows_in[i].at[place.group], rows_to[i].at[own_at], keep_sem.at[i]
        )

    for i in range(3):
        keep(i).start()
    gather = Gather(place, cot_all, *gather_refs)

    def own_rows_of(j):
        return pltpu.make_async_copy(
            cot_out.at[pl.ds(j * sz.block, sz.block)], cot_all.at[gather.own(j)], keep_sem.at[3 + j]
        )

    def move(w, g):
        slot = place.dp * n_c + ctx
        return pltpu.make_async_remote_copy(
            src_ref=blocks_in[w],
            dst_ref=blocks_out[w].at[slot],
            send_sem=move_send.at[w, g],
            recv_sem=move_recv.at[w, ctx],
            device_id=holder(g),
            device_id_type=MESH,
        )

    def stay(w):
        return pltpu.make_async_copy(
            blocks_in[w], blocks_out[w].at[place.dp * n_c + ctx], own_sem.at[w]
        )

    def moved(w, c):
        slot = place.dp * n_c + c
        arrival = pltpu.make_async_remote_copy(
            src_ref=blocks_in[w],
            dst_ref=blocks_out[w].at[slot],
            send_sem=move_send.at[w, 0],
            recv_sem=move_recv.at[w, c],
            device_id=place.sibling(),
            device_id_type=MESH,
        )
        here = at_home & (ctx == c)
        pl.when(here)(lambda: stay(w).wait())
        pl.when(jnp.logical_not(here))(lambda: arrival.wait_recv())

    def adapter_rows(offset, c, p):
        return adapter_out.at[
            ring.index(offset) * n_c + c, pl.ds(pl.multiple_of(p * sub, sub), sub)
        ]

    own_rows = adapter_in.at[pl.ds(pl.multiple_of(part * sub, sub), sub)]

    def around(s):
        rows = adapter_rows(-ahead * s, ctx, part)
        return pltpu.make_async_remote_copy(
            src_ref=own_rows if s == 0 else rows,
            dst_ref=rows,
            send_sem=a_send.at[s],
            recv_sem=a_recv.at[s],
            device_id=ring.device(ahead),
            device_id_type=MESH,
        )

    def across(kind, s):
        offset = -ahead * s
        if kind < half:
            dst = adapter_rows(offset, ctx, part)
            src = own_rows if s == 0 else dst
        else:
            src = dst = adapter_rows(offset, ctx, place.behind(kind - half + 1))
        target = place.device(place.ahead(kind), ctx) if 0 < kind < half else place.sibling()
        return pltpu.make_async_remote_copy(
            src_ref=src,
            dst_ref=dst,
            send_sem=x_send.at[kind, s],
            recv_sem=x_recv.at[kind, s],
            device_id=target,
            device_id_type=MESH,
        )

    def crossed(kind, s):
        if kind == 0:
            rows = adapter_rows(ahead * s, 1 - ctx, part)
        elif kind < half:
            rows = adapter_rows(-ahead * s, ctx, place.behind(kind))
        else:
            rows = adapter_rows(ahead * s, 1 - ctx, place.behind(kind - half + 1))
        return pltpu.make_async_remote_copy(
            src_ref=rows,
            dst_ref=rows,
            send_sem=x_send.at[kind, s],
            recv_sem=x_recv.at[kind, s],
            device_id=place.sibling(),
            device_id_type=MESH,
        )

    def hop(w, way, s):
        offset = -s if way == 0 else s
        rows = blocks_out[w].at[ring.index(offset) * n_c + way]
        return pltpu.make_async_remote_copy(
            src_ref=rows,
            dst_ref=rows,
            send_sem=ring_send.at[w, way, s],
            recv_sem=ring_recv.at[w, way, s],
            device_id=ring.device(1 if way == 0 else n_dp - 1),
            device_id_type=MESH,
        )

    def hopped(w, way, s):
        offset = -(s + 1) if way == 0 else s + 1
        rows = blocks_out[w].at[ring.index(offset) * n_c + way]
        return pltpu.make_async_remote_copy(
            src_ref=rows,
            dst_ref=rows,
            send_sem=ring_send.at[w, way, s],
            recv_sem=ring_recv.at[w, way, s],
            device_id=ring.device(1),
            device_id_type=MESH,
        )

    around(0).start()
    own = pltpu.make_async_copy(own_rows, adapter_rows(0, ctx, part), own_sem.at[count])
    own.start()

    def start_move(w):
        for g in range(sz.seqs):
            here = at_home & (place.group == g)
            pl.when(jnp.logical_not(here))(lambda w=w, g=g: move(w, g).start())
        pl.when(at_home)(lambda w=w: stay(w).start())

    start_move(0)
    start_move(1)
    across(0, 0).start()
    swaps = []

    def across_z():
        if swaps:
            s = swaps.pop(0)
            for q in range(1, half):
                across(q, s).start()

    swaps.append(0)

    def adapter_step(s):
        if s < steps:
            arrival = pltpu.make_async_remote_copy(
                src_ref=own_rows,
                dst_ref=adapter_rows(-ahead * (s + 1), ctx, part),
                send_sem=a_send.at[s],
                recv_sem=a_recv.at[s],
                device_id=ring.device(1),
                device_id_type=MESH,
            )
            arrival.wait_recv()
            if s + 1 < steps:
                around(s + 1).start()
            across(0, s + 1).start()
            swaps.append(s + 1)

    def adapter_pass(s):
        for q in range(1, half):
            crossed(q, s).wait_recv()
            across(half - 1 + q, s).start()

    embed_save = pltpu.make_async_copy(embed_s, embed_out, keep_sem.at[3 + sz.seqs])
    todo = []
    for k in range(count + steps):
        for s in range(min(k, steps - 1), -1, -1):
            w = k - s
            if w < count:
                todo.append((w, s))
    done = 0
    for w, s in todo:
        for way in range(n_c):
            if s == 0:
                moved(w, way)
            else:
                hopped(w, way, s - 1).wait_recv()
            hop(w, way, s).start()
        if s == 0 and w + 2 < count:
            start_move(w + 2)
        if s == 0 and w >= 1:
            across_z()
        if s == 0 and w == count - 2:
            for i in range(3):
                swap(i).start()
        if done < steps:
            adapter_step(done)
        if s == min(1, steps - 1) and w == count - 1:
            for i in range(3):
                keep(i).wait()
                swapped(i).wait_recv()
            for j in range(sz.seqs):
                own_rows_of(j).start()
            embed_save.start()
            for j in range(sz.seqs):
                own_rows_of(j).wait()
                gather.start(j)
            state_out[...] = state_s[...].astype(jnp.float32)
        done += 1
    for s in range(done, steps):
        adapter_step(s)
    while swaps:
        across_z()
    for s in range(n_dp):
        adapter_pass(s)
    for j in range(sz.seqs):
        gather.wait_near(j)
        for q in range(1, half):
            gather.forward(q, j)
    for s in range(n_dp):
        crossed(0, s).wait_recv()
        for q in range(1, half):
            crossed(half - 1 + q, s).wait_recv()
    own.wait()
    slots, depth = adapter_out.shape[0], weight_s.shape[1]
    loads = [
        pltpu.make_async_copy(
            adapter_out.at[slots // 2 + b, pl.ds(0, depth)], weight_s.at[b % 2], weight_sem.at[b % 2]
        )
        for b in range(slots // 2)
    ]
    loads[0].start()
    for b, copy in enumerate(loads):
        if b + 1 < len(loads):
            loads[b + 1].start()
        copy.wait()
        part_here = nn_dot(embed_s[:, b * depth : (b + 1) * depth], weight_s[b % 2])
        if b:
            embed_part[...] += part_here
        else:
            embed_part[...] = part_here
    for w in range(count):
        for way in range(n_c):
            hopped(w, way, steps - 1).wait_recv()
    for j in range(sz.seqs):
        for q in range(1, half):
            gather.wait_far(q, j)
    gather.finish()
    embed_save.wait()
    for i in range(3):
        swap(i).wait_send()
    for w in range(count):
        for g in range(sz.seqs):
            here = at_home & (place.group == g)
            pl.when(jnp.logical_not(here))(lambda w=w, g=g: move(w, g).wait_send())
        for way in range(n_c):
            for s in range(steps):
                hop(w, way, s).wait_send()
    for s in range(steps):
        around(s).wait_send()
    for s in range(n_dp):
        for kind in range(2 * half - 1):
            across(kind, s).wait_send()


def run_weights(sz, n_dp, adapter, adapter_block, blocks, rows):
    bf16, f32 = jnp.bfloat16, jnp.float32
    slots = n_dp * sz.n_context
    outs = [jax.ShapeDtypeStruct((slots,) + a.shape, bf16) for a in [adapter] + blocks]
    outs += [
        jax.ShapeDtypeStruct((sz.rows, sz.width), bf16),
        jax.ShapeDtypeStruct((sz.rows, sz.width), bf16),
        jax.ShapeDtypeStruct((sz.seq_len, sz.width), bf16),
        jax.ShapeDtypeStruct((sz.rows, sz.width), f32),
        jax.ShapeDtypeStruct((sz.rows, sz.width), f32),
    ]
    count, steps, dma = len(blocks), n_dp - 1, pltpu.SemaphoreType.DMA
    kinds = 2 * sz.half - 1
    return pl.pallas_call(
        partial(weights_kernel, sz, n_dp),
        out_shape=outs,
        in_specs=[any_spec()] * (4 + count),
        out_specs=[any_spec()] * (4 + count) + [full_spec()] * 2,
        scratch_shapes=[
            dma((count, sz.seqs)),
            dma((count, sz.n_context)),
            dma((count, sz.n_context, steps)),
            dma((count, sz.n_context, steps)),
            dma((steps,)),
            dma((steps,)),
            dma((kinds, n_dp)),
            dma((kinds, n_dp)),
            dma((count + 1,)),
            pltpu.VMEM((sz.rows, sz.width), bf16),
            pltpu.VMEM((sz.rows, sz.width), bf16),
            pltpu.VMEM((2, adapter_block, sz.width), bf16),
            dma((3,)),
            dma((3,)),
            dma((4 + sz.seqs,)),
            dma((2,)),
        ]
        + Gather.scratch(sz),
        compiler_params=pltpu.CompilerParams(
            collective_id=5, has_side_effects=True, vmem_limit_bytes=VMEM_BYTES
        ),
        name="weights",
    )(adapter, *blocks, *rows)


def norm_back(grad, rows, factor, gain):
    unit = rows * factor
    weighted = grad * gain
    inner = jnp.mean(weighted * unit, axis=-1, keepdims=True)
    return factor * (weighted - unit * inner), jnp.sum(grad * unit, axis=0, keepdims=True)


class GradRing:
    @staticmethod
    def scratch(sz, n_dp, tasks, wide, own_rows=None):
        slots, ways, dma = n_dp * sz.n_context, sz.n_context, pltpu.SemaphoreType.DMA
        depth, bf16, count, last = sz.width // slots, jnp.bfloat16, len(wide), n_dp - 1
        own_rows = [True] * count if own_rows is None else own_rows
        hops = [[s for w, s in tasks if w == i] for i in range(count)]
        return (
            [pltpu.VMEM((sz.seq_len, n), bf16) for n, own in zip(wide, own_rows) if own]
            + [pltpu.VMEM((ways, depth, n) if 0 in h else (ways, 16, 128), bf16) for n, h in zip(wide, hops)]
            + [pltpu.VMEM((ways, min(max(h) + 1, last), depth, n), bf16) for n, h in zip(wide, hops)]
            + [
                pltpu.VMEM((2, ways, sz.seq_len, depth), bf16),
                dma((count,)),
                dma((2, ways)),
                dma((count, ways, last)),
                dma((count, ways, last)),
                dma((ways,)),
            ]
        )

    @staticmethod
    def size(wide, own_rows=None):
        return 2 * len(wide) + (len(wide) if own_rows is None else sum(own_rows)) + 6

    @staticmethod
    def all_tasks(n_dp, count):
        return [
            (k - s, s)
            for k in range(count + n_dp)
            for s in range(min(k, n_dp - 1), -1, -1)
            if k - s < count
        ]

    def __init__(self, sz, place, ring, tasks, xs, ys, refs, rows=None, given=None):
        count, refs = len(xs), list(refs)
        self.sz, self.place, self.ring, self.xs, self.count = sz, place, ring, xs, count
        self.tasks = tasks
        self.ys = [refs.pop(0) if ys[w] is not None else rows[w] for w in range(count)]
        self.first, self.held = refs[:count], refs[count : 2 * count]
        self.x_s, self.load_y, self.load_x, self.send, self.recv, load_given = refs[2 * count :]
        self.y_loads = [
            pltpu.make_async_copy(ys[w], self.ys[w], self.load_y.at[w])
            for w in range(count)
            if ys[w] is not None
        ]
        self.unread = {w: self.y_loads[i] for i, w in enumerate(
            w for w in range(count) if ys[w] is not None
        )}
        self.given = []
        if given is not None:
            self.given = [
                pltpu.make_async_copy(
                    given.at[way], self.held[0].at[way, tasks[0][1] - 1], load_given.at[way]
                )
                for way in range(sz.n_context)
            ]
        self.done = 0

    def start(self):
        for copy in self.y_loads + self.given:
            copy.start()
        for way in range(self.sz.n_context):
            self.x_load(0, way).start()

    def slot(self, way, s):
        return self.ring.index(-(s + 1) if way == 0 else s + 1) * self.sz.n_context + way

    def x_load(self, k, way):
        w, s = self.tasks[k]
        depth = self.x_s.shape[3]
        if self.xs[w].shape[0] == 1:
            at = pl.multiple_of(self.slot(way, s) * depth, depth)
            src = self.xs[w].at[0, :, pl.ds(at, depth)]
        else:
            src = self.xs[w].at[self.slot(way, s)]
        return pltpu.make_async_copy(src, self.x_s.at[k % 2, way], self.load_x.at[k % 2, way])

    def source(self, w, way, s):
        return self.first[w].at[way] if s == 0 else self.held[w].at[way, s - 1]

    def hop(self, w, way, s):
        return pltpu.make_async_remote_copy(
            src_ref=self.source(w, way, s),
            dst_ref=self.held[w].at[way, s],
            send_sem=self.send.at[w, way, s],
            recv_sem=self.recv.at[w, way, s],
            device_id=self.ring.device(1 if way == 0 else self.ring.count - 1),
            device_id_type=MESH,
        )

    def result(self, w, way):
        return self.source(w, way, self.ring.count - 1)

    def step(self):
        k = self.done
        self.done += 1
        w, s = self.tasks[k]
        ways = range(self.sz.n_context)
        if k + 1 < len(self.tasks):
            for way in ways:
                self.x_load(k + 1, way).start()
        if w in self.unread:
            self.unread.pop(w).wait()
        for way in ways:
            self.x_load(k, way).wait()
            value = tn_dot(self.x_s[k % 2, way], self.ys[w][...])
            if k == 0 and self.given:
                self.given[way].wait()
            elif s:
                self.hop(w, way, s - 1).wait_recv()
            if s:
                value = value + self.held[w][way, s - 1].astype(jnp.float32)
            ref = self.source(w, way, s)
            ref[...] = value.astype(jnp.bfloat16)
            if s < self.ring.count - 1:
                self.hop(w, way, s).start()
        return w, s == self.ring.count - 1

    def left(self):
        return len(self.tasks) - self.done

    def finish(self):
        for w, s in self.tasks:
            if s < self.ring.count - 1:
                for way in range(self.sz.n_context):
                    self.hop(w, way, s).wait_send()


class Deliver:
    @staticmethod
    def scratch(sz, n_dp, wide):
        depth, count, dma = sz.width // (n_dp * sz.n_context), len(wide), pltpu.SemaphoreType.DMA
        return [pltpu.VMEM((sz.seqs, depth, n), jnp.bfloat16) for n in wide] + [
            dma((count, sz.n_context)),
            dma((count, sz.seqs)),
            dma((count,)),
        ]

    def __init__(self, sz, place, refs):
        self.sz, self.place = sz, place
        self.landed = refs[:-3]
        self.send, self.recv, self.own = refs[-3:]
        self.count = len(self.landed)
        self.t = lax.axis_index("tensor")
        self.role = place.part * sz.n_context + place.ctx
        self.at_home = self.role == self.t
        self.sources = [None] * self.count

    def greet(self):
        sz, place = self.sz, self.place
        barrier = pltpu.get_barrier_semaphore()
        for g in range(sz.seqs):
            holder = (place.dp, g * sz.half + self.t // sz.n_context, lax.rem(self.t, sz.n_context))
            pl.when(jnp.logical_not(self.at_home & (place.group == g)))(
                lambda holder=holder: pl.semaphore_signal(
                    barrier, inc=1, device_id=holder, device_id_type=MESH
                )
            )
        return sz.n_context - jnp.where(self.at_home, 1, 0)

    def remote(self, w, way):
        return pltpu.make_async_remote_copy(
            src_ref=self.sources[w][way],
            dst_ref=self.landed[w].at[self.place.group],
            send_sem=self.send.at[w, way],
            recv_sem=self.recv.at[w, self.place.group],
            device_id=(self.place.dp, self.role, way),
            device_id_type=MESH,
        )

    def local(self, w, way):
        return pltpu.make_async_copy(
            self.sources[w][way], self.landed[w].at[self.place.group], self.own.at[w]
        )

    def start(self, w, sources):
        self.sources[w] = sources
        for way in range(self.sz.n_context):
            here = self.at_home & (self.place.ctx == way)
            pl.when(here)(lambda way=way: self.local(w, way).start())
            pl.when(jnp.logical_not(here))(lambda way=way: self.remote(w, way).start())

    def total(self, w):
        place = self.place
        for g in range(self.sz.seqs):
            ref = self.landed[w].at[g]
            arrival = pltpu.make_async_remote_copy(
                src_ref=ref,
                dst_ref=ref,
                send_sem=self.send.at[w, 0],
                recv_sem=self.recv.at[w, g],
                device_id=(place.dp, self.t, 1 - place.ctx),
                device_id_type=MESH,
            )
            here = self.at_home & (place.group == g)
            pl.when(here)(lambda: self.local(w, 0).wait())
            pl.when(jnp.logical_not(here))(lambda arrival=arrival: arrival.wait_recv())
        total = self.landed[w][0].astype(jnp.float32)
        for g in range(1, self.sz.seqs):
            total = total + self.landed[w][g].astype(jnp.float32)
        return total

    def finish(self):
        for w in range(self.count):
            for way in range(self.sz.n_context):
                here = self.at_home & (self.place.ctx == way)
                pl.when(jnp.logical_not(here))(lambda w=w, way=way: self.remote(w, way).wait_send())


def slot_columns(sz, n_dp, x):
    slots = n_dp * sz.n_context
    depth = sz.width // slots
    if depth % 128:
        return x.reshape(sz.seq_len, slots, depth).transpose(1, 0, 2)
    return x[None]


def ffn_back_kernel(sz, n_dp, *refs):
    (cot, mixed, gains) = refs[:3]
    (rows_hbm, gate_hbm, up_hbm, wg_hbm, wu_hbm, down_hbm) = refs[3:9]
    (x_hbm, normed_hbm, hidden_hbm) = refs[9:12]
    (grad_mixed, gain_grad, dgate_out, dup_out, down_sum, gate_part) = refs[12:18]
    (rows_s, gate_s, up_s, wg, wu, wd, load, load_down, keep_sem) = refs[18:27]
    scatter_refs, ring_refs = refs[27:35], refs[35:]
    place = Place(sz)
    ring = Ring(place, n_dp)
    grads = GradRing(
        sz, place, ring, ffn_back_tasks(n_dp), [x_hbm, normed_hbm], [hidden_hbm, None], ring_refs,
        rows=[None, gate_s],
    )
    grads.start()
    pairs = ((rows_hbm, rows_s), (gate_hbm, gate_s), (up_hbm, up_s), (wg_hbm, wg), (wu_hbm, wu))
    loads = [
        pltpu.make_async_copy(src, dst, load.at[i]) for i, (src, dst) in enumerate(pairs)
    ]
    down_loads = column_loads(down_hbm, wd, load_down)
    place.enter([ring.device(1), ring.device(n_dp - 1)])
    scatter = Scatter(place, *scatter_refs)
    for copy in [loads[0]] + down_loads + loads[1:]:
        copy.start()
    grads.step()
    for copy in [loads[0]] + down_loads + loads[1:]:
        copy.wait()

    def work(q, j):
        rows = place.tile(q, j)
        dh = nt_dot(rows_s[rows, :], wd[...])
        gate = gate_s[rows, :].astype(jnp.float32)
        up = up_s[rows, :].astype(jnp.float32)
        sig = 1.0 / (1.0 + jnp.exp(-gate))
        dgate = (dh * up * sig * (1.0 + gate * (1.0 - sig))).astype(jnp.bfloat16)
        dup = (dh * gate * sig).astype(jnp.bfloat16)
        gate_s[rows, :] = dgate
        up_s[rows, :] = dup
        scatter.part[...] = nt_dot(dgate, wg[...]) + nt_dot(dup, wu[...])
        scatter.give(q, j)

    far = range(1, sz.half)
    for j in range(sz.seqs):
        for q in far:
            work(q, j)
        if j:
            for q in far:
                scatter.onward(q, j - 1)
    grads.step()
    work(0, 0)
    for q in far:
        scatter.onward(q, sz.seqs - 1)
    for j in range(1, sz.seqs):
        work(0, j)
    grads.step()
    copies = [
        pltpu.make_async_copy(gate_s, dgate_out, keep_sem.at[0]),
        pltpu.make_async_copy(up_s, dup_out, keep_sem.at[1]),
    ]
    for copy in copies:
        copy.start()
    gain_total = None
    for j in range(sz.seqs):
        span = slice(j * sz.block, (j + 1) * sz.block)
        rows = mixed[span, :]
        grad, gain_here = norm_back(scatter.total(j), rows, rms_factor(rows), gains[1:2, :])
        grad_mixed[span, :] = cot[span, :].astype(jnp.float32) + grad
        gain_total = gain_here if gain_total is None else gain_total + gain_here
    gain_grad[...] = gain_total
    while grads.left():
        grads.step()
    for way in range(sz.n_context):
        grads.hop(1, way, 0).wait_recv()
        for i, (src, dst) in enumerate(
            ((grads.result(0, way), down_sum), (grads.held[1].at[way, 0], gate_part))
        ):
            copies.append(
                pltpu.make_async_copy(src, dst.at[way], keep_sem.at[2 + 2 * way + i])
            )
            copies[-1].start()
    scatter.finish()
    grads.finish()
    for copy in copies:
        copy.wait()


def ffn_back_tasks(n_dp):
    return [(0, 0), (0, 1), (1, 0)] + [(0, s) for s in range(2, n_dp)]


def run_ffn_back(sz, n_dp, cot, mixed, gains, rows, gate, up, wg, wu, down, normed, hidden):
    f32, bf16, shape = jnp.float32, jnp.bfloat16, jax.ShapeDtypeStruct
    dma = pltpu.SemaphoreType.DMA
    depth = sz.width // (n_dp * sz.n_context)
    return pl.pallas_call(
        partial(ffn_back_kernel, sz, n_dp),
        out_shape=[
            shape((sz.rows, sz.width), f32),
            shape((1, sz.width), f32),
            shape((sz.seq_len, sz.ff), bf16),
            shape((sz.seq_len, sz.ff), bf16),
            shape((sz.n_context, depth, sz.ff), bf16),
            shape((sz.n_context, depth, sz.ff), bf16),
        ],
        in_specs=[full_spec()] * 3 + [any_spec()] * 9,
        out_specs=[full_spec()] * 2 + [any_spec()] * 4,
        scratch_shapes=[
            pltpu.VMEM((sz.seq_len, sz.width), bf16),
            pltpu.VMEM((sz.seq_len, sz.ff), bf16),
            pltpu.VMEM((sz.seq_len, sz.ff), bf16),
            pltpu.VMEM(wg.shape, bf16),
            pltpu.VMEM(wu.shape, bf16),
            pltpu.VMEM((sz.ff, sz.width), bf16),
            dma((5,)),
            dma((down.shape[0],)),
            dma((2 + 2 * sz.n_context,)),
        ]
        + Scatter.scratch(sz)
        + GradRing.scratch(sz, n_dp, ffn_back_tasks(n_dp), [sz.ff, sz.ff], [True, False]),
        compiler_params=pltpu.CompilerParams(
            collective_id=6, has_side_effects=True, vmem_limit_bytes=VMEM_BYTES
        ),
        cost_estimate=pl.CostEstimate(
            flops=8 * sz.seq_len * sz.width * sz.ff, bytes_accessed=40 << 20, transcendentals=0
        ),
        name="ffn_back",
    )(
        cot, mixed, gains, rows, gate, up, wg, wu, down,
        slot_columns(sz, n_dp, rows), slot_columns(sz, n_dp, normed), hidden,
    )


def attn_back_kernel(sz, n_dp, *refs):
    (grad_mixed, gains, cos_t, sin_t, begin, gain_b, adapted_hbm, state_hbm) = refs[:8]
    (q_hbm, k_hbm, v_hbm, lse_hbm, out_hbm, qkv_hbm) = refs[8:14]
    (x_hbm, dgate_hbm, dup_hbm, down_sum, gate_part) = refs[14:19]
    (grad_low, down_grad, gate_grad, state_out, rows_out, proj_out, up_part) = refs[19:26]
    (rows_s, q_s, k_s, v_s, lse_s, do_s, dk_s, dv_s, proj_s, wout, wqkv) = refs[26:37]
    (load, load_out, keep_sem, swap_out, swap_in, swap_sem, late) = refs[37:44]
    gather_refs, scatter_refs = refs[44:46], refs[46:54]
    ring_refs, deliver_refs = refs[54:66], refs[66:]
    place = Place(sz)
    ring = Ring(place, n_dp)
    grads = GradRing(
        sz, place, ring, attn_back_tasks(n_dp), [x_hbm, x_hbm], [dgate_hbm, dup_hbm], ring_refs,
        given=gate_part,
    )
    deliver = Deliver(sz, place, deliver_refs)
    grads.start()
    split = wqkv.shape[0]
    pairs = (
        (q_hbm, q_s), (k_hbm, k_s), (v_hbm, v_s), (lse_hbm, lse_s),
        (qkv_hbm.at[pl.ds(split, split)], wqkv),
    )
    loads = [
        pltpu.make_async_copy(src, dst, load.at[i]) for i, (src, dst) in enumerate(pairs)
    ]
    out_loads = column_loads(out_hbm, wout, load_out)
    for copy in out_loads + loads:
        copy.start()
    targets = deliver.greet()
    other = other_group(place)
    place.enter([ring.device(1), ring.device(n_dp - 1), other], targets)
    gather = Gather(place, rows_s, *gather_refs)
    scatter = Scatter(place, *scatter_refs)
    for j in range(sz.seqs):
        span = slice(j * sz.block, (j + 1) * sz.block)
        rows_s[gather.own(j), :] = grad_mixed[span, :].astype(jnp.bfloat16)
        gather.start(j)
    grads.step()
    deliver.start(0, [down_sum.at[way] for way in range(sz.n_context)])
    give_rows = pl.ds(pl.multiple_of((1 - place.group) * sz.block, sz.block), sz.block)
    keep_rows = pl.ds(pl.multiple_of(place.group * sz.block, sz.block), sz.block)
    swap = pltpu.make_async_remote_copy(
        src_ref=swap_out,
        dst_ref=swap_in,
        send_sem=swap_sem.at[0],
        recv_sem=swap_sem.at[1],
        device_id=other,
        device_id_type=MESH,
    )
    state_load = pltpu.make_async_copy(
        state_hbm.at[give_rows], scatter.part.at[pl.ds(0, sz.block)], late.at[0]
    )
    state_keep = pltpu.make_async_copy(
        state_hbm.at[keep_rows], state_out.at[place.group], late.at[1]
    )
    state_load.start()
    state_keep.start()
    state_load.wait()
    swap_out[...] = scatter.part[: sz.block, :].astype(jnp.bfloat16)
    swap.start()
    for copy in out_loads:
        copy.wait()
    d = sz.head_dim

    def heads_grad(q, j):
        rows = place.tile(q, j)
        dhead = nt_dot(rows_s[rows, :], wout[...]).astype(jnp.bfloat16)
        for h in range(sz.heads):
            do_s[h, rows, :] = dhead[:, h * d : (h + 1) * d]

    far = range(1, sz.half)
    for j in range(sz.seqs):
        gather.wait_near(j)
        heads_grad(0, j)
    for copy in loads:
        copy.wait()
    for j in range(sz.seqs):
        if j == sz.seqs - 1:
            grads.step()
            grads.step()
        for q in far:
            gather.forward(q, j)
        for q in far:
            gather.wait_far(sz.half - q, j)
            heads_grad(q, j)
    rows_copy = pltpu.make_async_copy(rows_s, rows_out, keep_sem.at[0])
    rows_copy.start()
    gather.finish()
    rows_copy.wait()
    upper = rows_s.at[pl.ds(0, split), pl.ds(0, wqkv.shape[1])]
    upper_load = pltpu.make_async_copy(qkv_hbm.at[pl.ds(0, split)], upper, late.at[2])
    upper_load.start()

    tiles = sz.n_tensor
    scale = 1.0 / math.sqrt(d)

    def head(h, carry):
        for i in reversed(range(tiles)):
            rows = slice(i * sz.tile, (i + 1) * sz.tile)
            length = (i + 1) * sz.tile
            keys, values = k_s[h, 0:length, :], v_s[h, 0:length, :]
            query, grad = q_s[h, rows, :], do_s[h, rows, :]
            start = begin[:, rows]
            key_at = lax.broadcasted_iota(jnp.int32, (length, sz.tile), 0)
            query_at = i * sz.tile + lax.broadcasted_iota(jnp.int32, (1, sz.tile), 1)
            allowed = (key_at >= start) & (key_at <= query_at)
            scores = nt_dot(keys, query)
            scores = jnp.where(allowed, scores * (LOG2E * scale), masked_score)
            probs = jnp.exp2(scores - lse_s[h, :, rows])
            dprobs = nt_dot(values, grad)
            inner = jnp.sum(probs * dprobs, axis=0, keepdims=True)
            dscores = (probs * (dprobs - inner)).astype(jnp.bfloat16)
            dv = nn_dot(probs.astype(jnp.bfloat16), grad)
            dk = nn_dot(dscores, query)
            if i == tiles - 1:
                dv_s[...] = dv
                dk_s[...] = dk
            else:
                dv_s[0:length, :] += dv
                dk_s[0:length, :] += dk
            dq = jnp.transpose(tn_dot(keys, dscores)) * scale
            cos_here, sin_here = cos_t[rows, :], sin_t[rows, :]
            proj_s[rows, pl.ds(pl.multiple_of(h * 3 * d, d), d)] = turn(
                dq, cos_here, -sin_here
            ).astype(jnp.bfloat16)
        dk = turn(dk_s[...] * scale, cos_t[...], -sin_t[...])
        proj_s[:, pl.ds(pl.multiple_of(h * 3 * d + d, d), d)] = dk.astype(jnp.bfloat16)
        proj_s[:, pl.ds(pl.multiple_of(h * 3 * d + 2 * d, d), d)] = dv_s[...].astype(jnp.bfloat16)
        return carry

    lax.fori_loop(0, sz.heads // 2, head, 0)
    while grads.left() > 1:
        grads.step()
    deliver.start(1, [grads.result(0, way) for way in range(sz.n_context)])
    lax.fori_loop(sz.heads // 2, sz.heads, head, 0)
    copies = [pltpu.make_async_copy(proj_s, proj_out, keep_sem.at[1])]
    copies[0].start()
    upper_load.wait()

    def give(q, j):
        proj = proj_s[place.tile(q, j), :]
        scatter.part[:, :split] = nt_dot(proj, upper[...])
        scatter.part[:, split:] = nt_dot(proj, wqkv[...])
        scatter.give(q, j)

    for j in range(sz.seqs):
        for q in far:
            give(q, j)
        if j:
            for q in far:
                scatter.onward(q, j - 1)
    give(0, 0)
    for q in far:
        scatter.onward(q, sz.seqs - 1)
    for j in range(1, sz.seqs):
        give(0, j)
    adapted = scatter.part
    adapted_load = pltpu.make_async_copy(adapted_hbm, adapted, late.at[3])
    adapted_load.start()
    grads.step()
    swap.wait()
    state_keep.wait()
    adapted_load.wait()
    state_out[1 - place.group] = swap_in[...].astype(jnp.float32)
    down_grad[...] = deliver.total(0)
    gain_total = None
    for j in range(sz.seqs):
        span = slice(j * sz.block, (j + 1) * sz.block)
        rows = adapted[span, :]
        grad, gain_here = norm_back(scatter.total(j), rows, rms_factor(rows), gains[0:1, :])
        grad_low[span, :] = (grad_mixed[span, :] + grad).astype(jnp.bfloat16)
        gain_total = gain_here if gain_total is None else gain_total + gain_here
    extra = grad_low.shape[0] - sz.rows
    at_row = lax.broadcasted_iota(jnp.int32, (extra, sz.width), 0)
    shares = jnp.where(at_row == 0, gain_total, jnp.where(at_row == 1, gain_b[...], 0.0))
    grad_low[sz.rows :, :] = shares.astype(jnp.bfloat16)
    for way in range(sz.n_context):
        grads.hop(1, way, 1).wait_recv()
        copies.append(
            pltpu.make_async_copy(
                grads.held[1].at[way, 1], up_part.at[way], keep_sem.at[2 + way]
            )
        )
        copies[-1].start()
    gate_grad[...] = deliver.total(1)
    scatter.finish()
    grads.finish()
    deliver.finish()
    for copy in copies:
        copy.wait()


def attn_back_tasks(n_dp):
    return [(0, 1), (0, 2), (1, 0)] + [(0, s) for s in range(3, n_dp)] + [(1, 1)]


def run_attn_back(
    sz, n_dp, grad_mixed, adapted, gains, cos_t, sin_t, begin, gain_b, state, q, k, v, lse, out,
    qkv, x, dgate, dup, down_sum, gate_part,
):
    f32, bf16, shape = jnp.float32, jnp.bfloat16, jax.ShapeDtypeStruct
    dma = pltpu.SemaphoreType.DMA
    heads_shape = (sz.heads, sz.seq_len, sz.head_dim)
    return pl.pallas_call(
        partial(attn_back_kernel, sz, n_dp),
        out_shape=[
            shape((sz.rows + 16, sz.width), bf16),
            shape(down_sum.shape[1:], f32),
            shape(gate_part.shape[1:], f32),
            shape((sz.seqs, sz.block, sz.width), f32),
            shape((sz.seq_len, sz.width), bf16),
            shape((sz.seq_len, qkv.shape[1]), bf16),
            shape(gate_part.shape, bf16),
        ],
        in_specs=[full_spec()] * 6 + [any_spec()] * 13,
        out_specs=[full_spec()] * 4 + [any_spec()] * 3,
        scratch_shapes=[
            pltpu.VMEM((sz.seq_len, sz.width), bf16),
            pltpu.VMEM(heads_shape, bf16),
            pltpu.VMEM(heads_shape, bf16),
            pltpu.VMEM(heads_shape, bf16),
            pltpu.VMEM((sz.heads, 1, sz.seq_len), f32),
            pltpu.VMEM(heads_shape, bf16),
            pltpu.VMEM((sz.seq_len, sz.head_dim), f32),
            pltpu.VMEM((sz.seq_len, sz.head_dim), f32),
            pltpu.VMEM((sz.seq_len, qkv.shape[1]), bf16),
            pltpu.VMEM((sz.heads * sz.head_dim, sz.width), bf16),
            pltpu.VMEM((sz.width // 2, qkv.shape[1]), bf16),
            dma((5,)),
            dma((out.shape[0],)),
            dma((2 + sz.n_context,)),
            pltpu.VMEM((sz.block, sz.width), bf16),
            pltpu.VMEM((sz.block, sz.width), bf16),
            dma((2,)),
            dma((4,)),
        ]
        + Gather.scratch(sz)
        + Scatter.scratch(sz)
        + GradRing.scratch(sz, n_dp, attn_back_tasks(n_dp), [sz.ff, sz.ff])
        + Deliver.scratch(sz, n_dp, [sz.ff, sz.ff]),
        compiler_params=pltpu.CompilerParams(
            collective_id=7, has_side_effects=True, vmem_limit_bytes=VMEM_BYTES
        ),
        cost_estimate=pl.CostEstimate(
            flops=4 * sz.seq_len * sz.width * qkv.shape[1], bytes_accessed=30 << 20, transcendentals=0
        ),
        name="attn_back",
    )(
        grad_mixed, gains, cos_t, sin_t, begin, gain_b, adapted, state, q, k, v, lse, out, qkv,
        slot_columns(sz, n_dp, x), dgate, dup, down_sum, gate_part,
    )


class PlaneRows:
    @staticmethod
    def scratch(n_dp):
        dma = pltpu.SemaphoreType.DMA
        return [dma((n_dp - 1,)), dma((n_dp - 1,)), dma((n_dp,)), dma((n_dp,))]

    def __init__(self, place, ring, own, landed, refs):
        self.place, self.ring, self.own, self.landed = place, ring, own, landed
        self.send, self.recv, self.near_send, self.near_recv = refs
        self.ahead = 1 - 2 * place.ctx

    def slot(self, offset, ctx):
        return self.landed.at[self.ring.index(offset) * self.place.sz.n_context + ctx]

    def source(self, s):
        return self.own if s == 0 else self.slot(-self.ahead * s, self.place.ctx)

    def hop(self, s):
        return pltpu.make_async_remote_copy(
            src_ref=self.source(s),
            dst_ref=self.slot(-self.ahead * s, self.place.ctx),
            send_sem=self.send.at[s],
            recv_sem=self.recv.at[s],
            device_id=self.ring.device(self.ahead),
            device_id_type=MESH,
        )

    def near(self, s):
        return pltpu.make_async_remote_copy(
            src_ref=self.source(s),
            dst_ref=self.slot(-self.ahead * s, self.place.ctx),
            send_sem=self.near_send.at[s],
            recv_sem=self.near_recv.at[s],
            device_id=self.place.sibling(),
            device_id_type=MESH,
        )

    def start(self):
        self.hop(0).start()
        self.near(0).start()

    def step(self, s):
        ref = self.slot(-self.ahead * (s + 1), self.place.ctx)
        pltpu.make_async_remote_copy(
            src_ref=ref,
            dst_ref=ref,
            send_sem=self.send.at[s],
            recv_sem=self.recv.at[s],
            device_id=self.place.sibling(),
            device_id_type=MESH,
        ).wait_recv()
        if s + 1 < self.ring.count - 1:
            self.hop(s + 1).start()
        self.near(s + 1).start()

    def wait_near(self, s):
        ref = self.slot(self.ahead * s, 1 - self.place.ctx)
        pltpu.make_async_remote_copy(
            src_ref=ref,
            dst_ref=ref,
            send_sem=self.near_send.at[s],
            recv_sem=self.near_recv.at[s],
            device_id=self.place.sibling(),
            device_id_type=MESH,
        ).wait_recv()

    def finish(self):
        for s in range(self.ring.count):
            if s < self.ring.count - 1:
                self.hop(s).wait_send()
            self.near(s).wait_send()


class LineSum:
    @staticmethod
    def scratch(sz, parts, chunk):
        dma, bf16 = pltpu.SemaphoreType.DMA, jnp.bfloat16
        far = pltpu.VMEM((max(sz.half - 1, 1), parts, chunk, sz.width), bf16)
        one = pltpu.VMEM((parts, chunk, sz.width), bf16)
        kinds = 2 * sz.half - 1
        return [far, far, one, one, one, far, dma((kinds, parts)), dma((kinds, parts))]

    def __init__(self, place, total, parts, refs):
        self.place, self.total, self.parts = place, total, parts
        (self.out, self.got, self.sum, self.cross, self.done, self.back, self.send, self.recv) = refs
        self.chunk = self.sum.shape[1]

    def rows(self, part, k):
        first = (part * self.parts + k) * self.chunk
        return pl.ds(pl.multiple_of(first, self.chunk), self.chunk)

    def copy(self, src, dst, kind, k, device):
        return pltpu.make_async_remote_copy(
            src_ref=src,
            dst_ref=dst,
            send_sem=self.send.at[kind, k],
            recv_sem=self.recv.at[kind, k],
            device_id=device,
            device_id_type=MESH,
        )

    def spread(self, q, k):
        place = self.place
        device = place.device(place.ahead(q), place.ctx)
        return self.copy(self.out.at[q - 1, k], self.got.at[q - 1, k], q, k, device)

    def swap(self, k):
        return self.copy(self.sum.at[k], self.cross.at[k], 0, k, other_group(self.place))

    def collect(self, q, k):
        place = self.place
        device = place.device(place.ahead(q), place.ctx)
        return self.copy(
            self.done.at[k], self.back.at[q - 1, k], place.sz.half - 1 + q, k, device
        )

    def start(self, k):
        for q in range(1, self.place.sz.half):
            rows = self.rows(self.place.ahead(q), k)
            self.out[q - 1, k] = self.total[rows, :].astype(jnp.bfloat16)
            self.spread(q, k).start()

    def cross_over(self, k):
        value = self.total[self.rows(self.place.part, k), :]
        for q in range(1, self.place.sz.half):
            self.spread(q, k).wait_recv()
            value = value + self.got[q - 1, k].astype(jnp.float32)
        self.sum[k] = value.astype(jnp.bfloat16)
        self.swap(k).start()

    def share(self, k):
        self.swap(k).wait_recv()
        value = self.sum[k].astype(jnp.float32) + self.cross[k].astype(jnp.float32)
        self.done[k] = value.astype(jnp.bfloat16)
        for q in range(1, self.place.sz.half):
            self.collect(q, k).start()
        self.total[self.rows(self.place.part, k), :] = self.done[k].astype(jnp.float32)

    def complete(self, k):
        for q in range(1, self.place.sz.half):
            self.collect(q, k).wait_recv()
            rows = self.rows(self.place.behind(q), k)
            self.total[rows, :] = self.back[q - 1, k].astype(jnp.float32)

    def finish(self):
        for k in range(self.parts):
            self.swap(k).wait_send()
            for q in range(1, self.place.sz.half):
                self.spread(q, k).wait_send()
                self.collect(q, k).wait_send()


SUM_PARTS = 2


def grads_kernel(sz, n_dp, count, *refs):
    n_in = 4 + 2 * count
    low, joined, adapter, up_part = refs[:4]
    xs, ys = refs[4 : 4 + count], refs[4 + count : n_in]
    outs = refs[n_in : n_in + count]
    embed_grad, adapter_out, gains_out, landed = refs[n_in + count : n_in + 4 + count]
    refs = refs[n_in + 4 + count :]

    def take(n):
        nonlocal refs
        head, refs = refs[:n], refs[n:]
        return head

    ring_refs, deliver_refs = take(3 * count + 6), take(count + 3)
    plane_refs, sum_refs = take(4), take(8)
    adapter_grad, d_s, j_s, weight_s, rows_s, swap_in = refs[:6]
    d_sem, j_sem, weight_sem, swap_sem, out_sem = refs[6:]
    place = Place(sz)
    ring = Ring(place, n_dp)
    grads = GradRing(
        sz, place, ring, grads_tasks(n_dp, count), xs, ys, ring_refs, given=up_part
    )
    deliver = Deliver(sz, place, deliver_refs)
    plane = PlaneRows(place, ring, low, landed, plane_refs)
    line = LineSum(place, adapter_grad, SUM_PARTS, sum_refs)
    other = other_group(place)
    grads.start()
    weight_load = [
        pltpu.make_async_copy(
            adapter.at[adapter.shape[0] // 2 + b, pl.ds(0, weight_s.shape[0])], weight_s, weight_sem
        )
        for b in range(adapter.shape[0] // 2)
    ]
    weight_load[0].start()
    place.enter([ring.device(1), ring.device(n_dp - 1), other], deliver.greet())
    plane.start()
    give_rows = pl.ds(pl.multiple_of((1 - place.group) * sz.block, sz.block), sz.block)
    keep_rows = pl.ds(pl.multiple_of(place.group * sz.block, sz.block), sz.block)
    swap = pltpu.make_async_remote_copy(
        src_ref=low.at[give_rows],
        dst_ref=swap_in,
        send_sem=swap_sem.at[0],
        recv_sem=swap_sem.at[1],
        device_id=other,
        device_id_type=MESH,
    )
    swap.start()

    def ring_step():
        if grads.left():
            w, complete = grads.step()
            if complete:
                deliver.start(w, [grads.result(w, way) for way in range(sz.n_context)])

    depth = joined.shape[2]

    def batch(ctx):
        copies = []
        for d in range(n_dp):
            at = d * sz.n_context + ctx
            rows = pl.ds(d * sz.rows, sz.rows)
            copies.append(
                pltpu.make_async_copy(landed.at[at, pl.ds(0, sz.rows)], d_s.at[rows], d_sem.at[d, 0])
            )
            copies.append(pltpu.make_async_copy(joined.at[at], j_s.at[rows], j_sem.at[d]))
            copies.append(
                pltpu.make_async_copy(
                    landed.at[at, pl.ds(sz.rows, 16)],
                    d_s.at[pl.ds(n_dp * sz.rows + 16 * d, 16)],
                    d_sem.at[d, 1],
                )
            )
        return copies

    def product(ctx, first):
        copies = batch(ctx)
        for copy in copies:
            copy.start()
        for copy in copies:
            copy.wait()
        chunk = sz.width // 4
        for n in range(4):
            cols = slice(n * chunk, (n + 1) * chunk)
            value = tn_dot(j_s[...], d_s[: n_dp * sz.rows, cols])
            tail = d_s[n_dp * sz.rows : n_dp * sz.rows + 16, cols].astype(jnp.float32)
            for d in range(1, n_dp):
                at = n_dp * sz.rows + 16 * d
                tail = tail + d_s[at : at + 16, cols].astype(jnp.float32)
            if first:
                adapter_grad[:depth, cols] = value
                adapter_grad[depth : depth + 16, cols] = tail
            else:
                adapter_grad[:depth, cols] += value
                adapter_grad[depth : depth + 16, cols] += tail

    own = pltpu.make_async_copy(low, landed.at[place.dp * sz.n_context + place.ctx], d_sem.at[0, 0])
    own.start()
    rest = adapter_grad.shape[0] - depth - 16
    if rest:
        adapter_grad[depth + 16 :, :] = jnp.zeros((rest, sz.width), jnp.float32)
    for s in range(n_dp - 1):
        ring_step()
        plane.step(s)
    own.wait()
    product(place.ctx, True)
    for s in range(n_dp):
        plane.wait_near(s)
    product(1 - place.ctx, False)
    for k in range(SUM_PARTS):
        line.start(k)
    ring_step()
    ring_step()
    swap.wait()
    rows_s[place.group] = low[keep_rows, :]
    rows_s[1 - place.group] = swap_in[...]
    rows = rows_s[...].reshape(sz.rows, sz.width)
    ring_step()
    for k in range(SUM_PARTS):
        line.cross_over(k)
    ring_step()
    for b, copy in enumerate(weight_load):
        copy.wait()
        part = nt_dot(rows, weight_s[...]).reshape(sz.seqs, sz.block, weight_s.shape[0])
        embed_grad[:, :, b * weight_s.shape[0] : (b + 1) * weight_s.shape[0]] = part
        if b + 1 < len(weight_load):
            weight_load[b + 1].start()
    ring_step()
    for k in range(SUM_PARTS):
        line.share(k)
        ring_step()
    while grads.left():
        ring_step()
    for k in range(SUM_PARTS):
        line.complete(k)
    saves = [
        pltpu.make_async_copy(adapter_grad.at[pl.ds(0, depth)], adapter_out, out_sem.at[0]),
        pltpu.make_async_copy(adapter_grad.at[pl.ds(depth, 16)], gains_out, out_sem.at[1]),
    ]
    for copy in saves:
        copy.start()
    for w in range(count):
        outs[w][...] = deliver.total(w)
    for copy in saves:
        copy.wait()
    grads.finish()
    deliver.finish()
    plane.finish()
    line.finish()


def grads_tasks(n_dp, count):
    others = [(w + 1, s) for w, s in GradRing.all_tasks(n_dp, count - 1)]
    return [(0, s) for s in range(2, n_dp)] + others


def run_grads(sz, n_dp, low, joined, adapter, up_part, xs, ys):
    count, bf16, f32, dma = len(xs), jnp.bfloat16, jnp.float32, pltpu.SemaphoreType.DMA
    shape = jax.ShapeDtypeStruct
    depth = sz.width // (n_dp * sz.n_context)
    wide = [y.shape[1] for y in ys]
    slots, columns = joined.shape[0], joined.shape[2]
    unit = 16 * sz.half * SUM_PARTS
    total_rows = -(-(columns + 16) // unit) * unit
    return pl.pallas_call(
        partial(grads_kernel, sz, n_dp, count),
        out_shape=[shape((depth, n), f32) for n in wide]
        + [
            shape((sz.seqs, sz.block, sz.width), f32),
            shape((columns, sz.width), f32),
            shape((16, sz.width), f32),
            shape((slots,) + low.shape, bf16),
        ],
        in_specs=[full_spec()] + [any_spec()] * (3 + 2 * count),
        out_specs=[full_spec()] * (1 + count) + [any_spec()] * 3,
        scratch_shapes=GradRing.scratch(sz, n_dp, grads_tasks(n_dp, count), wide)
        + Deliver.scratch(sz, n_dp, wide)
        + PlaneRows.scratch(n_dp)
        + LineSum.scratch(sz, SUM_PARTS, total_rows // (sz.half * SUM_PARTS))
        + [
            pltpu.VMEM((total_rows, sz.width), f32),
            pltpu.VMEM((n_dp * (sz.rows + 16), sz.width), bf16),
            pltpu.VMEM((n_dp * sz.rows, columns), bf16),
            pltpu.VMEM((columns, sz.width), bf16),
            pltpu.VMEM((sz.seqs, sz.block, sz.width), bf16),
            pltpu.VMEM((sz.block, sz.width), bf16),
            dma((n_dp, 2)),
            dma((n_dp,)),
            dma,
            dma((2,)),
            dma((2,)),
        ],
        compiler_params=pltpu.CompilerParams(
            collective_id=8, has_side_effects=True, vmem_limit_bytes=VMEM_BYTES
        ),
        cost_estimate=pl.CostEstimate(
            flops=2 * sz.seq_len * sz.width * sum(wide), bytes_accessed=60 << 20, transcendentals=0
        ),
        name="grads",
    )(low, joined, adapter, up_part, *[slot_columns(sz, n_dp, x) for x in xs], *ys)


def shards(
    embedded,
    initial_state,
    cotangent,
    doc_ids,
    recurrences,
    adapter_weight,
    norm_gains,
    qkv_weight,
    output_head_weight,
    gate_up_weight,
    down_weight,
):
    n_dp = lax.axis_size("dp")
    n_tensor = lax.axis_size("tensor")
    n_context = lax.axis_size("context")
    dp_index = lax.axis_index("dp")
    t_index = lax.axis_index("tensor")
    ctx_index = lax.axis_index("context")
    seq_count, block_rows, model_width = embedded.shape
    seq_len = doc_ids.shape[1]
    half = n_tensor // seq_count
    group = t_index // half
    part = t_index % half
    heads_here = qkv_weight.shape[1]
    head_dim = qkv_weight.shape[2] // 3
    ff_here = down_weight.shape[0]
    def side_by_side(blocks):
        count, depth, columns = blocks.shape
        return blocks.transpose(1, 0, 2).reshape(depth, count * columns)

    def role_grad(grad, axis):
        piece = lax.psum_scatter(
            grad.astype(jnp.bfloat16), "dp", scatter_dimension=axis, tiled=True
        )
        low, high = jnp.split(piece, 2, axis=axis)
        give = [jnp.where(group == 0, low, high), jnp.where(group == 0, high, low)]
        back = [
            lax.ppermute(g, ("tensor", "context"), [(b, a) for a, b in perm])
            for g, perm in zip(give, role_perms)
        ]
        return back[0].astype(jnp.float32) + back[1].astype(jnp.float32)

    def gather_rows(rows):
        full = lax.all_gather(
            rows, ("tensor", "context"), axis=0, tiled=True, axis_index_groups=groups
        )
        split = full.reshape(half, n_context, seq_count, block_rows, model_width)
        return split.transpose(2, 0, 1, 3, 4).reshape(seq_len, model_width)

    sz = Sizes(
        n_tensor,
        n_context,
        seq_count,
        half,
        block_rows,
        n_context * block_rows,
        seq_count * block_rows,
        seq_len,
        model_width,
        heads_here,
        head_dim,
        ff_here,
    )
    adapter_block = adapter_weight.shape[0]
    gain_columns = norm_gains.shape[1]
    unit = 16 * half
    padded = -(-(adapter_block + 2) // unit) * unit
    adapter_rows = jnp.concatenate(
        [
            adapter_weight,
            jnp.pad(
                norm_gains,
                ((0, padded - adapter_block - 2), (0, model_width - gain_columns)),
            ),
        ],
        axis=0,
    )
    (
        adapter_all,
        out_blocks,
        qkv_use,
        gate_use,
        up_use,
        down_blocks,
        embed_rows,
        cot_rows,
        grad_ffn,
        embed_part,
        current,
    ) = run_weights(
        sz,
        n_dp,
        adapter_rows,
        adapter_block,
        [
            output_head_weight.reshape(heads_here * head_dim, -1),
            qkv_weight.reshape(qkv_weight.shape[0], -1),
            gate_up_weight[:, 0],
            gate_up_weight[:, 1],
            down_weight,
        ],
        [embedded, initial_state, cotangent],
    )
    qkv_use = qkv_use.reshape(model_width, -1)
    gate_use = gate_use.reshape(model_width, -1)
    up_use = up_use.reshape(model_width, -1)
    gains_full = (
        adapter_all[:, adapter_block : adapter_block + 2, :gain_columns]
        .transpose(1, 0, 2)
        .reshape(2, model_width)
    )
    if out_blocks.shape[2] % 128:
        out_blocks = side_by_side(out_blocks)[None]
        down_blocks = side_by_side(down_blocks)[None]
    gains_f = gains_full.astype(jnp.float32)

    cos_full, sin_full = rope_tables(seq_len, head_dim)
    own_seq = dp_index * seq_count + group
    docs = lax.dynamic_index_in_dim(doc_ids, own_seq, 0, keepdims=False)
    begin = jnp.sum((docs[None, :] < docs[:, None]).astype(jnp.int32), axis=1)[None, :]
    steps_own = lax.dynamic_index_in_dim(recurrences, own_seq, 0, keepdims=False) - BACK
    active = jnp.arange(MAXR - BACK, dtype=jnp.int32)[:, None] < steps_own
    detached = run_rounds(
        sz,
        current,
        jnp.broadcast_to(active.astype(jnp.float32), (MAXR - BACK, model_width)),
        gains_f, cos_full, sin_full, begin, embed_part,
        adapter_all, qkv_use, out_blocks, gate_use, up_use, down_blocks,
    )
    (mixed_rows, adapted, feature_rows, query_hm, key_hm, value_hm, head_flat, lse, joined) = run_attn(
        sz, n_dp, True, detached, embed_part, gains_f, cos_full, sin_full, begin,
        adapter_all, qkv_use, out_blocks, embed_rows,
    )
    (current, ffn_input, gate_pre, up_pre, hidden) = run_ffn(
        sz, True, mixed_rows, detached, gains_f[:1], gains_f, gate_use, up_use, down_blocks
    )
    grad_mixed, gain_b, grad_gate, grad_up, down_sum, gate_part = run_ffn_back(
        sz, n_dp, cot_rows, mixed_rows, gains_f, grad_ffn, gate_pre, up_pre,
        gate_use, up_use, down_blocks, ffn_input, hidden,
    )
    grad_low, down_t, gate_s, state_out, grad_rows, grad_proj, up_part = run_attn_back(
        sz, n_dp, grad_mixed, adapted, gains_f, cos_full, sin_full, begin, gain_b, current,
        query_hm, key_hm, value_hm, lse, out_blocks, qkv_use, ffn_input, grad_gate, grad_up, down_sum,
        gate_part,
    )
    up_s, qkv_s, out_t, embed_out, adapter_s, gains_rows, _ = run_grads(
        sz,
        n_dp,
        grad_low,
        joined,
        adapter_all,
        up_part,
        [ffn_input, feature_rows, grad_rows],
        [grad_up, grad_proj, head_flat],
    )
    place_at = (dp_index * n_context + ctx_index) * gain_columns
    gains_s = lax.dynamic_slice_in_dim(gains_rows[:2], place_at, gain_columns, 1)
    down_s = down_t.T
    out_s = out_t.T.reshape(heads_here, head_dim, -1)
    qkv_s = qkv_s.reshape(-1, heads_here, 3 * head_dim)
    gate_up_s = jnp.stack([gate_s, up_s], axis=1)
    return (state_out, embed_out, adapter_s, gains_s, qkv_s, out_s, gate_up_s, down_s)


def solution(mesh):
    placed = (
        P("dp", ("tensor", "context"), None),
        P("dp", ("tensor", "context"), None),
        P("dp", ("tensor", "context"), None),
        P(),
        P(),
        P(("dp", "context"), None),
        P(None, ("dp", "context")),
        P(("dp", "context"), "tensor", None),
        P("tensor", None, ("dp", "context")),
        P(("dp", "context"), None, "tensor"),
        P("tensor", ("dp", "context")),
    )
    return jax.shard_map(
        shards,
        mesh=mesh,
        in_specs=placed,
        out_specs=(
            P("dp", ("tensor", "context"), None),
            P("dp", ("tensor", "context"), None),
            P(("dp", "context"), None),
            P(None, ("dp", "context")),
            P(("dp", "context"), "tensor", None),
            P("tensor", None, ("dp", "context")),
            P(("dp", "context"), None, "tensor"),
            P("tensor", ("dp", "context")),
        ),
        check_vma=False,
    )
```

```python
from functools import partial
import math
from typing import NamedTuple

import jax
import jax.numpy as jnp
import numpy as np
from jax import lax
from jax.experimental import pallas as pl
from jax.experimental.pallas import tpu as pltpu
from jax.sharding import PartitionSpec as P

BACK = 1
MAXR = 4


rope_base = 50000.0
norm_eps = 1e-06
masked_score = -1e30


def rope_tables(seq_len, head_dim):
    freq_index = np.arange(head_dim // 2, dtype=np.float32)
    inv_freq = 1.0 / np.float32(rope_base) ** (np.float32(2.0) * freq_index / head_dim)
    angles = np.arange(seq_len, dtype=np.float32)[:, None] * inv_freq.astype(np.float32)[None, :]
    cos_t, sin_t = np.cos(angles), np.sin(angles)
    return (
        jnp.asarray(np.concatenate([cos_t, cos_t], axis=1), jnp.float32),
        jnp.asarray(np.concatenate([-sin_t, sin_t], axis=1), jnp.float32),
    )


MESH = pl.DeviceIdType.MESH
LOG2E = 1.4426950408889634
VMEM_BYTES = 62 << 20


class Sizes(NamedTuple):
    n_tensor: int
    n_context: int
    seqs: int
    half: int
    block: int
    tile: int
    rows: int
    seq_len: int
    width: int
    heads: int
    head_dim: int
    ff: int


def full_spec():
    return pl.BlockSpec(memory_space=pltpu.VMEM)


def any_spec():
    return pl.BlockSpec(memory_space=pl.ANY)


def nt_dot(a, b):
    return lax.dot_general(a, b, (((1,), (1,)), ((), ())), preferred_element_type=jnp.float32)


def tn_dot(a, b):
    return lax.dot_general(a, b, (((0,), (0,)), ((), ())), preferred_element_type=jnp.float32)


def nn_dot(a, b):
    return jnp.dot(a, b, preferred_element_type=jnp.float32)


class Place:
    def __init__(self, sz):
        t = lax.axis_index("tensor")
        self.sz = sz
        self.dp = lax.axis_index("dp")
        self.ctx = lax.axis_index("context")
        self.group = t // sz.half
        self.part = lax.rem(t, sz.half)

    def device(self, part, ctx):
        return (self.dp, self.group * self.sz.half + part, ctx)

    def ahead(self, q):
        return lax.rem(self.part + q, self.sz.half)

    def behind(self, q):
        return lax.rem(self.part + (self.sz.half - q), self.sz.half)

    def sibling(self):
        return self.device(self.part, 1 - self.ctx)

    def block(self, part, ctx, j):
        sz = self.sz
        first = ((part + j * sz.half) * sz.n_context + ctx) * sz.block
        return pl.ds(pl.multiple_of(first, sz.block), sz.block)

    def tile(self, q, j):
        sz = self.sz
        first = (self.ahead(q) + j * sz.half) * sz.tile
        return pl.ds(pl.multiple_of(first, sz.tile), sz.tile)

    def enter(self, others=(), more=0):
        barrier = pltpu.get_barrier_semaphore()
        for device in others:
            pl.semaphore_signal(barrier, inc=1, device_id=device, device_id_type=MESH)
        pl.semaphore_signal(
            barrier, inc=1, device_id=self.sibling(), device_id_type=MESH
        )
        for q in range(1, self.sz.half):
            pl.semaphore_signal(
                barrier,
                inc=1,
                device_id=self.device(self.ahead(q), self.ctx),
                device_id_type=MESH,
            )
        pl.semaphore_wait(barrier, self.sz.half + len(others) + more)


class Gather:
    @staticmethod
    def scratch(sz):
        kinds = 2 * sz.half - 1
        return [
            pltpu.SemaphoreType.DMA((kinds, sz.seqs)),
            pltpu.SemaphoreType.DMA((kinds, sz.seqs)),
        ]

    def __init__(self, place, ref, send, recv):
        self.place, self.ref, self.send, self.recv = place, ref, send, recv

    def copy(self, kind, j, rows):
        place, half = self.place, self.place.sz.half
        if 0 < kind < half:
            target = place.device(place.ahead(kind), place.ctx)
        else:
            target = place.sibling()
        return pltpu.make_async_remote_copy(
            src_ref=self.ref.at[rows],
            dst_ref=self.ref.at[rows],
            send_sem=self.send.at[kind, j],
            recv_sem=self.recv.at[kind, j],
            device_id=target,
            device_id_type=MESH,
        )

    def own(self, j):
        return self.place.block(self.place.part, self.place.ctx, j)

    def start(self, j):
        for q in range(1, self.place.sz.half):
            self.copy(q, j, self.own(j)).start()
        self.copy(0, j, self.own(j)).start()

    def wait_near(self, j):
        place = self.place
        self.copy(0, j, place.block(place.part, 1 - place.ctx, j)).wait_recv()

    def forward(self, q, j):
        place = self.place
        rows = place.block(place.behind(q), place.ctx, j)
        self.copy(q, j, rows).wait_recv()
        self.copy(place.sz.half - 1 + q, j, rows).start()

    def wait_far(self, q, j):
        place = self.place
        rows = place.block(place.behind(q), 1 - place.ctx, j)
        self.copy(place.sz.half - 1 + q, j, rows).wait_recv()

    def passed_on(self, j):
        place, half = self.place, self.place.sz.half
        for q in range(1, half):
            rows = place.block(place.behind(q), place.ctx, j)
            self.copy(half - 1 + q, j, rows).wait_send()

    def finish(self, forwards=True):
        for j in range(self.place.sz.seqs):
            for kind in range(self.place.sz.half):
                self.copy(kind, j, self.own(j)).wait_send()
            if forwards:
                self.passed_on(j)


class Scatter:
    @staticmethod
    def scratch(sz):
        kinds = 2 * sz.half - 1
        near = (sz.half, sz.seqs, sz.block, sz.width)
        far = (max(sz.half - 1, 1), sz.seqs, sz.block, sz.width)
        return [
            pltpu.VMEM((sz.tile, sz.width), jnp.float32),
            pltpu.VMEM(near, jnp.bfloat16),
            pltpu.VMEM(near, jnp.bfloat16),
            pltpu.VMEM(near, jnp.bfloat16),
            pltpu.VMEM(far, jnp.bfloat16),
            pltpu.VMEM(far, jnp.bfloat16),
            pltpu.SemaphoreType.DMA((kinds, sz.seqs)),
            pltpu.SemaphoreType.DMA((kinds, sz.seqs)),
        ]

    def __init__(self, place, part, mine, near_out, near_in, far_out, far_in, send, recv):
        self.place, self.part, self.mine = place, part, mine
        self.near_out, self.near_in = near_out, near_in
        self.far_out, self.far_in = far_out, far_in
        self.send, self.recv = send, recv

    def near(self, q, j):
        return pltpu.make_async_remote_copy(
            src_ref=self.near_out.at[q, j],
            dst_ref=self.near_in.at[q, j],
            send_sem=self.send.at[q, j],
            recv_sem=self.recv.at[q, j],
            device_id=self.place.sibling(),
            device_id_type=MESH,
        )

    def far(self, q, j):
        place = self.place
        return pltpu.make_async_remote_copy(
            src_ref=self.far_out.at[q - 1, j],
            dst_ref=self.far_in.at[q - 1, j],
            send_sem=self.send.at[place.sz.half - 1 + q, j],
            recv_sem=self.recv.at[place.sz.half - 1 + q, j],
            device_id=place.device(place.ahead(q), place.ctx),
            device_id_type=MESH,
        )

    def give(self, q, j):
        sz, ctx = self.place.sz, self.place.ctx
        mine = pl.ds(pl.multiple_of(ctx * sz.block, sz.block), sz.block)
        other = pl.ds(pl.multiple_of((1 - ctx) * sz.block, sz.block), sz.block)
        self.near_out[q, j] = self.part[other, :].astype(jnp.bfloat16)
        self.near(q, j).start()
        self.mine[q, j] = self.part[mine, :].astype(jnp.bfloat16)

    def onward(self, q, j):
        self.near(q, j).wait_recv()
        self.far_out[q - 1, j] = (
            self.mine[q, j].astype(jnp.float32) + self.near_in[q, j].astype(jnp.float32)
        ).astype(jnp.bfloat16)
        self.far(q, j).start()

    def total(self, j):
        self.near(0, j).wait_recv()
        total = self.mine[0, j].astype(jnp.float32) + self.near_in[0, j].astype(jnp.float32)
        for q in range(1, self.place.sz.half):
            self.far(q, j).wait_recv()
            total = total + self.far_in[q - 1, j].astype(jnp.float32)
        return total

    def finish(self):
        half = self.place.sz.half
        for j in range(self.place.sz.seqs):
            for q in range(half):
                self.near(q, j).wait_send()
            for q in range(1, half):
                self.far(q, j).wait_send()


def column_loads(blocks_ref, vmem_ref, sem):
    count, _, columns = blocks_ref.shape
    return [
        pltpu.make_async_copy(
            blocks_ref.at[b], vmem_ref.at[:, pl.ds(b * columns, columns)], sem.at[b]
        )
        for b in range(count)
    ]


def adapter_loads(blocks_ref, vmem_ref, sem):
    count, tops = sem.shape
    depth, columns = vmem_ref.shape[0] // tops, vmem_ref.shape[1] // count
    return [
        [
            pltpu.make_async_copy(
                blocks_ref.at[b, pl.ds(0, depth), pl.ds(n * columns, columns)],
                vmem_ref.at[pl.ds(b * depth, depth), pl.ds(n * columns, columns)],
                sem.at[n, b],
            )
            for b in range(tops)
        ]
        for n in range(count)
    ]


def rms_factor(rows):
    return lax.rsqrt(jnp.mean(rows * rows, axis=-1, keepdims=True) + norm_eps)


def turn(x, cos_t, sin_t):
    return x * cos_t + pltpu.roll(x, x.shape[-1] // 2, 1) * sin_t


def attn_kernel(sz, n_dp, keep, *refs):
    (latent, embed, gains, cos_t, sin_t, begin, adapter_hbm, qkv_hbm, out_hbm) = refs[:9]
    refs = refs[9:]
    extra_in, refs = refs[0], refs[1:]
    mixed = refs[0]
    refs = refs[1:]
    if keep:
        adapted_out, rows_out, q_out, k_out, v_out, head_out, lse_out, joined_out = refs[:8]
        refs = refs[8:]
    else:
        blocks_out, refs = refs[0], refs[1:]
    (wa, wqkv, wout, adapted, rows_s, q_s, k_s, v_s, head_s, lse_s) = refs[:10]
    load_a, load_qkv, load_out, keep_sem = refs[10:14]
    gather_refs = refs[14:16]
    scatter_refs = refs[16:24]
    if keep:
        joined_s, load_embed, x_send, x_recv = refs[24:]
    else:
        hop_send, hop_recv, own_sem = refs[24:]

    place = Place(sz)
    a_loads = adapter_loads(adapter_hbm, wa, load_a)
    qkv_load = pltpu.make_async_copy(qkv_hbm, wqkv, load_qkv)
    out_loads = column_loads(out_hbm, wout, load_out)
    for group in a_loads:
        for copy in group:
            copy.start()
    qkv_load.start()
    for copy in out_loads:
        copy.start()
    ring = Ring(place, n_dp)
    if not keep:
        others = [ring.device(1), ring.device(n_dp - 1)]
        ways = range(sz.n_context)

        def hop(way, s):
            offset = -s if way == 0 else s
            slot = blocks_out.at[ring.index(offset) * sz.n_context + way]
            return pltpu.make_async_remote_copy(
                src_ref=extra_in.at[way] if s == 0 else slot,
                dst_ref=slot,
                send_sem=hop_send.at[way, s],
                recv_sem=hop_recv.at[way, s],
                device_id=ring.device(1 if way == 0 else n_dp - 1),
                device_id_type=MESH,
            )

        def hopped(way, s):
            offset = -(s + 1) if way == 0 else s + 1
            slot = blocks_out.at[ring.index(offset) * sz.n_context + way]
            return pltpu.make_async_remote_copy(
                src_ref=slot,
                dst_ref=slot,
                send_sem=hop_send.at[way, s],
                recv_sem=hop_recv.at[way, s],
                device_id=ring.device(1),
                device_id_type=MESH,
            )

        own_blocks = [
            pltpu.make_async_copy(
                extra_in.at[way], blocks_out.at[place.dp * sz.n_context + way], own_sem.at[way]
            )
            for way in ways
        ]
        hops = list(range(n_dp - 1))

        def next_hop():
            if hops:
                s = hops.pop(0)
                for way in ways:
                    if s:
                        hopped(way, s - 1).wait_recv()
                    hop(way, s).start()

    if keep:
        t = lax.axis_index("tensor")
        embed_load = pltpu.make_async_copy(
            extra_in, joined_s.at[:, pl.ds(sz.width, sz.width)], load_embed
        )
        embed_load.start()
        plane = [(o, c) for o in range(n_dp) for c in range(2) if (o, c) != (0, 0)]

        def member(o, c):
            return (ring.index(o), t, place.ctx if c == 0 else 1 - place.ctx)

        def columns_to(o, c):
            to = member(o, c)
            depth = joined_out.shape[2]
            first = pl.multiple_of((to[0] * sz.n_context + to[2]) * depth, depth)
            return pltpu.make_async_remote_copy(
                src_ref=joined_s.at[:, pl.ds(first, depth)],
                dst_ref=joined_out.at[place.dp * sz.n_context + place.ctx],
                send_sem=x_send.at[o, c],
                recv_sem=x_recv.at[o, c],
                device_id=to,
                device_id_type=MESH,
            )

        def columns_from(o, c):
            ref = joined_out.at[
                ring.index(-o) * sz.n_context + (place.ctx if c == 0 else 1 - place.ctx)
            ]
            return pltpu.make_async_remote_copy(
                src_ref=ref,
                dst_ref=ref,
                send_sem=x_send.at[o, c],
                recv_sem=x_recv.at[o, c],
                device_id=place.sibling(),
                device_id_type=MESH,
            )

        others = [member(o, c) for o, c in plane if o]
    place.enter(others)
    if not keep:
        next_hop()
        for copy in own_blocks:
            copy.start()
    gather = Gather(place, rows_s, *gather_refs)
    scatter = Scatter(place, *scatter_refs)

    low = latent[...].astype(jnp.bfloat16)
    columns = sz.width // len(a_loads)
    square = None
    for n, group in enumerate(a_loads):
        for copy in group:
            copy.wait()
        cols = pl.ds(n * columns, columns)
        chunk = nn_dot(low, wa[:, cols]) + embed[:, cols]
        adapted[:, cols] = chunk
        here = jnp.sum(chunk * chunk, axis=-1, keepdims=True)
        square = here if square is None else square + here
    factor = lax.rsqrt(square / sz.width + norm_eps)
    for j in range(sz.seqs):
        span = slice(j * sz.block, (j + 1) * sz.block)
        normed = (adapted[span, :] * factor[span]) * gains[0:1, :]
        rows_s[gather.own(j), :] = normed.astype(jnp.bfloat16)
        gather.start(j)

    qkv_load.wait()
    pair = min(2, sz.heads)
    d = sz.head_dim

    def project(q, j):
        rows = place.tile(q, j)
        x = rows_s[rows, :]
        cos_here, sin_here = cos_t[rows, :], sin_t[rows, :]
        for h0 in range(0, sz.heads, pair):
            proj = nn_dot(x, wqkv[:, 3 * d * h0 : 3 * d * (h0 + pair)])
            for h in range(pair):
                at = 3 * d * h
                q_s[h0 + h, rows, :] = turn(proj[:, at : at + d], cos_here, sin_here).astype(
                    jnp.bfloat16
                )
                k_s[h0 + h, rows, :] = turn(
                    proj[:, at + d : at + 2 * d], cos_here, sin_here
                ).astype(jnp.bfloat16)
                v_s[h0 + h, rows, :] = proj[:, at + 2 * d : at + 3 * d].astype(jnp.bfloat16)

    def attend(q, j):
        rows = place.tile(q, j)
        first = (place.ahead(q) + j * sz.half) * sz.tile
        length = (j + 1) * sz.half * sz.tile
        start = begin[:, pl.ds(pl.multiple_of(first, sz.tile), sz.tile)]
        key_at = lax.broadcasted_iota(jnp.int32, (length, sz.tile), 0)
        query_at = first + lax.broadcasted_iota(jnp.int32, (1, sz.tile), 1)
        allowed = (key_at >= start) & (key_at <= query_at)

        def head(h, carry):
            scores = nt_dot(k_s[h, 0:length, :], q_s[h, rows, :])
            scores = jnp.where(allowed, scores * (LOG2E / math.sqrt(d)), masked_score)
            top = jnp.max(scores, axis=0, keepdims=True)
            weight = jnp.exp2(scores - top)
            total = jnp.sum(weight, axis=0, keepdims=True)
            mixed_t = tn_dot(v_s[h, 0:length, :], weight.astype(jnp.bfloat16))
            result = jnp.transpose(mixed_t / total)
            head_s[rows, pl.ds(pl.multiple_of(h * d, d), d)] = result.astype(jnp.bfloat16)
            if keep:
                lse_s[h, :, rows] = top + jnp.log2(total)
            return carry

        lax.fori_loop(0, sz.heads, head, 0)

    def give(q, j):
        rows = place.tile(q, j)
        scatter.part[...] = nn_dot(head_s[rows, :], wout[...])
        scatter.give(q, j)

    copies = []

    def save(src, dst):
        copy = pltpu.make_async_copy(src, dst, keep_sem.at[len(copies)])
        copy.start()
        copies.append(copy)

    if keep:
        save(adapted, adapted_out)
        joined_s[:, : sz.width] = low
        embed_load.wait()
        for o, c in plane:
            columns_to(o, c).start()
        mine = place.dp * sz.n_context + place.ctx
        depth = joined_out.shape[2]
        save(
            joined_s.at[:, pl.ds(pl.multiple_of(mine * depth, depth), depth)], joined_out.at[mine]
        )
    far = range(1, sz.half)
    for j in range(sz.seqs):
        gather.wait_near(j)
        project(0, j)
    for copy in out_loads:
        copy.wait()
    for j in range(sz.seqs):
        for q in far:
            gather.forward(q, j)
        for q in far:
            gather.wait_far(sz.half - q, j)
            project(q, j)
        for q in far:
            attend(q, j)
            give(q, j)
        if not keep:
            next_hop()
        attend(0, j)
        for q in far:
            scatter.onward(q, j)
        give(0, j)
    if keep:
        for src, dst in ((rows_s, rows_out), (q_s, q_out), (k_s, k_out), (v_s, v_out)):
            save(src, dst)
        save(head_s, head_out)
        save(lse_s, lse_out)
    gather.finish()
    for j in range(sz.seqs):
        span = slice(j * sz.block, (j + 1) * sz.block)
        mixed[span, :] = adapted[span, :] + scatter.total(j)
    scatter.finish()
    if keep:
        for o, c in plane:
            columns_from(o, c).wait_recv()
            columns_to(o, c).wait_send()
    else:
        while hops:
            next_hop()
        for way in ways:
            hopped(way, n_dp - 2).wait_recv()
            own_blocks[way].wait()
            for s in range(n_dp - 1):
                hop(way, s).wait_send()
    for copy in copies:
        copy.wait()


def run_attn(
    sz, n_dp, keep, latent, embed_part, gains, cos_t, sin_t, begin, adapter, qkv, out, extra
):
    f32, bf16 = jnp.float32, jnp.bfloat16
    heads_shape = (sz.heads, sz.seq_len, sz.head_dim)
    shape = jax.ShapeDtypeStruct
    outs = [shape((sz.rows, sz.width), f32)]
    if keep:
        outs += [
            shape((sz.rows, sz.width), f32),
            shape((sz.seq_len, sz.width), bf16),
            shape(heads_shape, bf16),
            shape(heads_shape, bf16),
            shape(heads_shape, bf16),
            shape((sz.seq_len, sz.heads * sz.head_dim), bf16),
            shape((sz.heads, 1, sz.seq_len), f32),
            shape((adapter.shape[0], sz.rows, 2 * sz.width // adapter.shape[0]), bf16),
        ]
    else:
        outs.append(shape((n_dp * sz.n_context,) + extra.shape[1:], bf16))
    scratch = [
        pltpu.VMEM((sz.width, sz.width), bf16),
        pltpu.VMEM(qkv.shape, bf16),
        pltpu.VMEM((sz.heads * sz.head_dim, sz.width), bf16),
        pltpu.VMEM((sz.rows, sz.width), f32),
        pltpu.VMEM((sz.seq_len, sz.width), bf16),
        pltpu.VMEM(heads_shape, bf16),
        pltpu.VMEM(heads_shape, bf16),
        pltpu.VMEM(heads_shape, bf16),
        pltpu.VMEM((sz.seq_len, sz.heads * sz.head_dim), bf16),
        pltpu.VMEM((sz.heads, 1, sz.seq_len), f32),
        pltpu.SemaphoreType.DMA((4, adapter.shape[0] // 2)),
        pltpu.SemaphoreType.DMA,
        pltpu.SemaphoreType.DMA((out.shape[0],)),
        pltpu.SemaphoreType.DMA((8,)),
    ]
    scratch += Gather.scratch(sz) + Scatter.scratch(sz)
    if keep:
        scratch += [
            pltpu.VMEM((sz.rows, 2 * sz.width), bf16),
            pltpu.SemaphoreType.DMA,
            pltpu.SemaphoreType.DMA((n_dp, 2)),
            pltpu.SemaphoreType.DMA((n_dp, 2)),
        ]
    else:
        scratch += [
            pltpu.SemaphoreType.DMA((sz.n_context, n_dp - 1)),
            pltpu.SemaphoreType.DMA((sz.n_context, n_dp - 1)),
            pltpu.SemaphoreType.DMA((sz.n_context,)),
        ]
    flops = 2 * sz.rows * sz.width * sz.width + 2 * sz.seq_len * sz.width * qkv.shape[1]
    return pl.pallas_call(
        partial(attn_kernel, sz, n_dp, keep),
        out_shape=outs,
        in_specs=[full_spec()] * 6 + [any_spec()] * 4,
        out_specs=[full_spec()] + [any_spec()] * (len(outs) - 1),
        scratch_shapes=scratch,
        compiler_params=pltpu.CompilerParams(
            collective_id=2 if keep else 9, has_side_effects=True, vmem_limit_bytes=VMEM_BYTES
        ),
        cost_estimate=pl.CostEstimate(
            flops=flops, bytes_accessed=20 << 20, transcendentals=0
        ),
        name="attn_keep" if keep else "attn_round",
    )(latent, embed_part, gains, cos_t, sin_t, begin, adapter, qkv, out, extra)


def ffn_kernel(sz, keep, *refs):
    (mixed, latent, active, gains, gate_hbm, up_hbm, down_hbm, result) = refs[:8]
    refs = refs[8:]
    if keep:
        rows_out, gate_out, up_out, hidden_out = refs[:4]
        refs = refs[4:]
    wg, wu, wd, rows_s = refs[:4]
    refs = refs[4:]
    if keep:
        gate_s, up_s, hidden_s = refs[:3]
        refs = refs[3:]
    load_gu, load_down, keep_sem = refs[:3]
    gather_refs = refs[3:5]
    scatter_refs = refs[5:]

    place = Place(sz)
    gate_load = pltpu.make_async_copy(gate_hbm, wg, load_gu.at[0])
    up_load = pltpu.make_async_copy(up_hbm, wu, load_gu.at[1])
    down_loads = column_loads(down_hbm, wd, load_down)
    gate_load.start()
    up_load.start()
    for copy in down_loads:
        copy.start()
    place.enter()
    gather = Gather(place, rows_s, *gather_refs)
    scatter = Scatter(place, *scatter_refs)
    for j in range(sz.seqs):
        span = slice(j * sz.block, (j + 1) * sz.block)
        rows = mixed[span, :]
        normed = (rows * rms_factor(rows)) * gains[1:2, :]
        rows_s[gather.own(j), :] = normed.astype(jnp.bfloat16)
        gather.start(j)
    gate_load.wait()
    up_load.wait()
    for copy in down_loads:
        copy.wait()

    copies = []

    def save(src, dst):
        copy = pltpu.make_async_copy(src, dst, keep_sem.at[len(copies)])
        copy.start()
        copies.append(copy)

    def work(q, j):
        rows = place.tile(q, j)
        x = rows_s[rows, :]
        gate = nn_dot(x, wg[...])
        up = nn_dot(x, wu[...])
        hidden = (gate / (1.0 + jnp.exp(-gate)) * up).astype(jnp.bfloat16)
        if keep:
            gate_s[rows, :] = gate.astype(jnp.bfloat16)
            up_s[rows, :] = up.astype(jnp.bfloat16)
            hidden_s[rows, :] = hidden
        scatter.part[...] = nn_dot(hidden, wd[...])
        scatter.give(q, j)

    far = range(1, sz.half)
    for j in range(sz.seqs):
        gather.wait_near(j)
        work(0, j)
    for j in range(sz.seqs):
        for q in far:
            gather.forward(q, j)
        for q in far:
            gather.wait_far(sz.half - q, j)
            work(q, j)
        for q in far:
            scatter.onward(q, j)
    if keep:
        save(rows_s, rows_out)
        save(gate_s, gate_out)
        save(up_s, up_out)
        save(hidden_s, hidden_out)
    gather.finish()
    for j in range(sz.seqs):
        span = slice(j * sz.block, (j + 1) * sz.block)
        total = mixed[span, :] + scatter.total(j)
        if not keep:
            total = jnp.where(active[...] > 0, total, latent[span, :])
        result[span, :] = total
    scatter.finish()
    for copy in copies:
        copy.wait()


def run_ffn(sz, keep, mixed, latent, active, gains, gate, up, down):
    f32, bf16 = jnp.float32, jnp.bfloat16
    shape = jax.ShapeDtypeStruct
    outs = [shape((sz.rows, sz.width), f32)]
    if keep:
        outs += [
            shape((sz.seq_len, sz.width), bf16),
            shape((sz.seq_len, sz.ff), bf16),
            shape((sz.seq_len, sz.ff), bf16),
            shape((sz.seq_len, sz.ff), bf16),
        ]
    scratch = [
        pltpu.VMEM(gate.shape, bf16),
        pltpu.VMEM(up.shape, bf16),
        pltpu.VMEM((sz.ff, sz.width), bf16),
        pltpu.VMEM((sz.seq_len, sz.width), bf16),
    ]
    if keep:
        scratch += [pltpu.VMEM((sz.seq_len, sz.ff), bf16)] * 3
    scratch += [
        pltpu.SemaphoreType.DMA((2,)),
        pltpu.SemaphoreType.DMA((down.shape[0],)),
        pltpu.SemaphoreType.DMA((4,)),
    ]
    scratch += Gather.scratch(sz) + Scatter.scratch(sz)
    return pl.pallas_call(
        partial(ffn_kernel, sz, keep),
        out_shape=outs,
        in_specs=[full_spec()] * 4 + [any_spec()] * 3,
        out_specs=[full_spec()] + [any_spec()] * (len(outs) - 1),
        scratch_shapes=scratch,
        compiler_params=pltpu.CompilerParams(
            collective_id=4 if keep else 3, has_side_effects=True, vmem_limit_bytes=VMEM_BYTES
        ),
        cost_estimate=pl.CostEstimate(
            flops=6 * sz.seq_len * sz.width * sz.ff, bytes_accessed=20 << 20, transcendentals=0
        ),
        name="ffn_keep" if keep else "ffn_round",
    )(mixed, latent, active, gains, gate, up, down)


def rounds_kernel(sz, count, *refs):
    (active, gains, cos_t, sin_t, begin) = refs[:5]
    (latent_hbm, embed_hbm, adapter_hbm, qkv_hbm, out_hbm, gate_hbm, up_hbm, down_hbm) = refs[5:13]
    result = refs[13]
    (wide, narrow, wg, wu, wd, embed, mixed, rows_s, q_s, k_s, v_s, head_s) = refs[14:26]
    load_rows, load_a, load_qkv, load_out, load_gu, load_down = refs[26:32]
    gather_refs, again_refs, scatter_refs = refs[32:34], refs[34:36], refs[36:44]
    columns = sz.width // 4
    depth_out = sz.heads * sz.head_dim

    place = Place(sz)
    row_loads = [
        pltpu.make_async_copy(latent_hbm, result, load_rows.at[0]),
        pltpu.make_async_copy(embed_hbm, embed, load_rows.at[1]),
    ]

    def adapter_columns(n):
        return wide.at[:, pl.ds(n * columns, columns)] if n < 3 else narrow

    tops = load_a.shape[1]
    depth = sz.width // tops
    a_loads = [
        [
            pltpu.make_async_copy(
                adapter_hbm.at[b, pl.ds(0, depth), pl.ds(n * columns, columns)],
                adapter_columns(n).at[pl.ds(b * depth, depth)],
                load_a.at[n, b],
            )
            for b in range(tops)
        ]
        for n in range(4)
    ]
    wqkv = wide.at[:, pl.ds(0, qkv_hbm.shape[1])]
    qkv_load = pltpu.make_async_copy(qkv_hbm, wqkv, load_qkv)
    out_loads = []
    for b in range(out_hbm.shape[0]):
        size = min(out_hbm.shape[2], columns)
        for at in range(0, out_hbm.shape[2], size):
            n, to = divmod(b * out_hbm.shape[2] + at, columns)
            out_loads.append(
                pltpu.make_async_copy(
                    out_hbm.at[b, :, pl.ds(at, size)],
                    narrow.at[pl.ds(n * depth_out, depth_out), pl.ds(to, size)],
                    load_out.at[len(out_loads)],
                )
            )
    ffn_loads = [
        pltpu.make_async_copy(gate_hbm, wg, load_gu.at[0]),
        pltpu.make_async_copy(up_hbm, wu, load_gu.at[1]),
    ] + column_loads(down_hbm, wd, load_down)

    def start_adapter():
        for group in a_loads:
            for copy in group:
                copy.start()

    def start_heads():
        qkv_load.start()
        for copy in out_loads:
            copy.start()

    for copy in row_loads:
        copy.start()
    start_adapter()
    place.enter()
    gather = Gather(place, rows_s, *gather_refs)
    again = Gather(place, rows_s, *again_refs)
    scatter = Scatter(place, *scatter_refs)
    for copy in row_loads:
        copy.wait()

    def spans(j):
        return slice(j * sz.block, (j + 1) * sz.block)

    def open_block(j):
        low = result[spans(j), :].astype(jnp.bfloat16)
        square = None
        for n, group in enumerate(a_loads):
            if j == 0:
                for copy in group:
                    copy.wait()
            cols = slice(n * columns, (n + 1) * columns)
            chunk = nn_dot(low, adapter_columns(n)[...]) + embed[spans(j), cols]
            mixed[spans(j), cols] = chunk
            here = jnp.sum(chunk * chunk, axis=-1, keepdims=True)
            square = here if square is None else square + here
        factor = lax.rsqrt(square / sz.width + norm_eps)
        normed = (mixed[spans(j), :] * factor) * gains[0:1, :]
        rows_s[gather.own(j), :] = normed.astype(jnp.bfloat16)
        gather.start(j)

    for j in range(sz.seqs):
        open_block(j)
    start_heads()
    for copy in ffn_loads:
        copy.start()
    pair = min(2, sz.heads)
    d = sz.head_dim

    def project(q, j):
        rows = place.tile(q, j)
        x = rows_s[rows, :]
        cos_here, sin_here = cos_t[rows, :], sin_t[rows, :]
        for h0 in range(0, sz.heads, pair):
            proj = nn_dot(x, wqkv[:, 3 * d * h0 : 3 * d * (h0 + pair)])
            for h in range(pair):
                at = 3 * d * h
                q_s[h0 + h, rows, :] = turn(proj[:, at : at + d], cos_here, sin_here).astype(
                    jnp.bfloat16
                )
                k_s[h0 + h, rows, :] = turn(
                    proj[:, at + d : at + 2 * d], cos_here, sin_here
                ).astype(jnp.bfloat16)
                v_s[h0 + h, rows, :] = proj[:, at + 2 * d : at + 3 * d].astype(jnp.bfloat16)

    def attend(q, j):
        rows = place.tile(q, j)
        first = (place.ahead(q) + j * sz.half) * sz.tile
        length = (j + 1) * sz.half * sz.tile
        start = begin[:, pl.ds(pl.multiple_of(first, sz.tile), sz.tile)]
        key_at = lax.broadcasted_iota(jnp.int32, (length, sz.tile), 0)
        query_at = first + lax.broadcasted_iota(jnp.int32, (1, sz.tile), 1)
        allowed = (key_at >= start) & (key_at <= query_at)

        def head(h, carry):
            scores = nt_dot(k_s[h, 0:length, :], q_s[h, rows, :])
            scores = jnp.where(allowed, scores * (LOG2E / math.sqrt(d)), masked_score)
            top = jnp.max(scores, axis=0, keepdims=True)
            weight = jnp.exp2(scores - top)
            total = jnp.sum(weight, axis=0, keepdims=True)
            mixed_t = tn_dot(v_s[h, 0:length, :], weight.astype(jnp.bfloat16))
            result = jnp.transpose(mixed_t / total)
            head_s[rows, pl.ds(pl.multiple_of(h * d, d), d)] = result.astype(jnp.bfloat16)
            return carry

        lax.fori_loop(0, sz.heads, head, 0)

    def give(q, j):
        rows = place.tile(q, j)
        for n in range(4):
            scatter.part[:, n * columns : (n + 1) * columns] = nn_dot(
                head_s[rows, :], narrow[n * depth_out : (n + 1) * depth_out, :]
            )
        scatter.give(q, j)

    def work(q, j):
        x = rows_s[place.tile(q, j), :]
        gate = nn_dot(x, wg[...])
        up = nn_dot(x, wu[...])
        hidden = (gate / (1.0 + jnp.exp(-gate)) * up).astype(jnp.bfloat16)
        scatter.part[...] = nn_dot(hidden, wd[...])
        scatter.give(q, j)

    far = range(1, sz.half)

    def one_round(r, carry):
        more = r + 1 < count
        qkv_load.wait()
        for j in range(sz.seqs):
            gather.wait_near(j)
            project(0, j)
        for copy in out_loads:
            copy.wait()
        for j in range(sz.seqs):
            for q in far:
                gather.forward(q, j)
            for q in far:
                gather.wait_far(sz.half - q, j)
                project(q, j)
            for q in far:
                attend(q, j)
                give(q, j)
            attend(0, j)
            gather.passed_on(j)
            for q in far:
                scatter.onward(q, j)
            give(0, j)
        gather.finish(forwards=False)
        pl.when(more)(start_adapter)
        for j in range(sz.seqs):
            rows = mixed[spans(j), :] + scatter.total(j)
            mixed[spans(j), :] = rows
            normed = (rows * rms_factor(rows)) * gains[1:2, :]
            rows_s[again.own(j), :] = normed.astype(jnp.bfloat16)
            again.start(j)
        scatter.finish()

        def first_loads():
            for copy in ffn_loads:
                copy.wait()

        pl.when(r == 0)(first_loads)
        for j in range(sz.seqs):
            again.wait_near(j)
            work(0, j)
        for j in range(sz.seqs):
            for q in far:
                again.forward(q, j)
            for q in far:
                again.wait_far(sz.half - q, j)
                work(q, j)
            again.passed_on(j)
            for q in far:
                scatter.onward(q, j)
        again.finish(forwards=False)
        on = active[pl.ds(r, 1), :] > 0
        for j in range(sz.seqs):
            total = mixed[spans(j), :] + scatter.total(j)
            result[spans(j), :] = jnp.where(on, total, result[spans(j), :])
            pl.when(more)(lambda j=j: open_block(j))
        pl.when(more)(start_heads)
        scatter.finish()
        return carry

    lax.fori_loop(0, count, one_round, 0)


def run_rounds(sz, latent, active, gains, cos_t, sin_t, begin, embed, adapter, qkv, out, gate, up, down):
    f32, bf16, dma = jnp.float32, jnp.bfloat16, pltpu.SemaphoreType.DMA
    heads_shape = (sz.heads, sz.seq_len, sz.head_dim)
    return pl.pallas_call(
        partial(rounds_kernel, sz, active.shape[0]),
        out_shape=jax.ShapeDtypeStruct((sz.rows, sz.width), f32),
        in_specs=[full_spec()] * 5 + [any_spec()] * 8,
        out_specs=full_spec(),
        scratch_shapes=[
            pltpu.VMEM((sz.width, max(3 * sz.width // 4, qkv.shape[1])), bf16),
            pltpu.VMEM((sz.width, sz.width // 4), bf16),
            pltpu.VMEM(gate.shape, bf16),
            pltpu.VMEM(up.shape, bf16),
            pltpu.VMEM((sz.ff, sz.width), bf16),
            pltpu.VMEM((sz.rows, sz.width), f32),
            pltpu.VMEM((sz.rows, sz.width), f32),
            pltpu.VMEM((sz.seq_len, sz.width), bf16),
            pltpu.VMEM(heads_shape, bf16),
            pltpu.VMEM(heads_shape, bf16),
            pltpu.VMEM(heads_shape, bf16),
            pltpu.VMEM((sz.seq_len, sz.heads * sz.head_dim), bf16),
            dma((2,)),
            dma((4, adapter.shape[0] // 2)),
            dma,
            dma((max(4, out.shape[0]),)),
            dma((2,)),
            dma((down.shape[0],)),
        ]
        + Gather.scratch(sz)
        + Gather.scratch(sz)
        + Scatter.scratch(sz),
        compiler_params=pltpu.CompilerParams(
            collective_id=1, has_side_effects=True, vmem_limit_bytes=VMEM_BYTES
        ),
        cost_estimate=pl.CostEstimate(
            flops=24 * sz.seq_len * sz.width * sz.ff, bytes_accessed=80 << 20, transcendentals=0
        ),
        name="rounds",
    )(active, gains, cos_t, sin_t, begin, latent, embed, adapter, qkv, out, gate, up, down)


def other_group(place):
    return (place.dp, (1 - place.group) * place.sz.half + place.part, place.ctx)


class Ring:
    def __init__(self, place, n_dp):
        self.place, self.count = place, n_dp
        self.at = self.swap(place.dp)

    def swap(self, i):
        if self.count != 4:
            return i
        x, y = lax.rem(i, 2), i // 2
        return 2 * y + x + y - 2 * x * y

    def index(self, offset):
        return self.swap(lax.rem(self.at + offset + 2 * self.count, self.count))

    def device(self, offset):
        return (self.index(offset), lax.axis_index("tensor"), self.place.ctx)


def weights_kernel(sz, n_dp, *refs):
    count = 5
    adapter_in, blocks_in = refs[0], refs[1 : 1 + count]
    rows_in, refs = refs[1 + count : 4 + count], refs[4 + count :]
    adapter_out, blocks_out = refs[0], refs[1 : 1 + count]
    embed_out, cot_out, cot_all, embed_part, state_out = refs[1 + count : 6 + count]
    refs = refs[6 + count :]
    (move_send, move_recv, ring_send, ring_recv, a_send, a_recv, x_send, x_recv, own_sem) = refs[:9]
    embed_s, state_s, weight_s, swap_send, swap_recv, keep_sem, weight_sem = refs[9:16]
    gather_refs = refs[16:]
    place = Place(sz)
    ring = Ring(place, n_dp)
    t = lax.axis_index("tensor")
    ctx, part, half, n_c = place.ctx, place.part, sz.half, sz.n_context
    role = part * n_c + ctx
    at_home = role == t
    steps = n_dp - 1
    sub = adapter_in.shape[0] // half
    ahead = 1 - 2 * ctx

    def holder(g):
        return (place.dp, g * half + t // n_c, lax.rem(t, n_c))

    barrier = pltpu.get_barrier_semaphore()

    def greet(device):
        pl.semaphore_signal(barrier, inc=1, device_id=device, device_id_type=MESH)

    greet(ring.device(1))
    greet(ring.device(n_dp - 1))
    greet(place.sibling())
    for q in range(1, half):
        greet(place.device(place.ahead(q), ctx))
    for c in range(n_c):
        pl.when(jnp.logical_not(at_home & (ctx == c)))(
            lambda c=c: greet((place.dp, role, c))
        )
    other = other_group(place)
    greet(other)
    waits = 3 + half + sz.seqs - jnp.where(at_home, 1, 0)
    pl.semaphore_wait(barrier, waits)

    own_at = pl.ds(pl.multiple_of(place.group * sz.block, sz.block), sz.block)
    other_at = pl.ds(pl.multiple_of((1 - place.group) * sz.block, sz.block), sz.block)
    rows_to = (embed_s, state_s, cot_out)

    def swap(i):
        return pltpu.make_async_remote_copy(
            src_ref=rows_in[i].at[1 - place.group],
            dst_ref=rows_to[i].at[own_at],
            send_sem=swap_send.at[i],
            recv_sem=swap_recv.at[i],
            device_id=other,
            device_id_type=MESH,
        )

    def swapped(i):
        ref = rows_to[i].at[other_at]
        return pltpu.make_async_remote_copy(
            src_ref=ref,
            dst_ref=ref,
            send_sem=swap_send.at[i],
            recv_sem=swap_recv.at[i],
            device_id=other,
            device_id_type=MESH,
        )

    def keep(i):
        return pltpu.make_async_copy(
            rows_in[i].at[place.group], rows_to[i].at[own_at], keep_sem.at[i]
        )

    for i in range(3):
        keep(i).start()
    gather = Gather(place, cot_all, *gather_refs)

    def own_rows_of(j):
        return pltpu.make_async_copy(
            cot_out.at[pl.ds(j * sz.block, sz.block)], cot_all.at[gather.own(j)], keep_sem.at[3 + j]
        )

    rings = count - 1

    def landing(w, c):
        return c if w == rings else place.dp * n_c + c

    def move(w, g):
        slot = landing(w, ctx)
        return pltpu.make_async_remote_copy(
            src_ref=blocks_in[w],
            dst_ref=blocks_out[w].at[slot],
            send_sem=move_send.at[w, g],
            recv_sem=move_recv.at[w, ctx],
            device_id=holder(g),
            device_id_type=MESH,
        )

    def stay(w):
        return pltpu.make_async_copy(
            blocks_in[w], blocks_out[w].at[landing(w, ctx)], own_sem.at[w]
        )

    def moved(w, c):
        slot = landing(w, c)
        arrival = pltpu.make_async_remote_copy(
            src_ref=blocks_in[w],
            dst_ref=blocks_out[w].at[slot],
            send_sem=move_send.at[w, 0],
            recv_sem=move_recv.at[w, c],
            device_id=place.sibling(),
            device_id_type=MESH,
        )
        here = at_home & (ctx == c)
        pl.when(here)(lambda: stay(w).wait())
        pl.when(jnp.logical_not(here))(lambda: arrival.wait_recv())

    def adapter_rows(offset, c, p):
        return adapter_out.at[
            ring.index(offset) * n_c + c, pl.ds(pl.multiple_of(p * sub, sub), sub)
        ]

    own_rows = adapter_in.at[pl.ds(pl.multiple_of(part * sub, sub), sub)]

    def around(s):
        rows = adapter_rows(-ahead * s, ctx, part)
        return pltpu.make_async_remote_copy(
            src_ref=own_rows if s == 0 else rows,
            dst_ref=rows,
            send_sem=a_send.at[s],
            recv_sem=a_recv.at[s],
            device_id=ring.device(ahead),
            device_id_type=MESH,
        )

    def across(kind, s):
        offset = -ahead * s
        if kind < half:
            dst = adapter_rows(offset, ctx, part)
            src = own_rows if s == 0 else dst
        else:
            src = dst = adapter_rows(offset, ctx, place.behind(kind - half + 1))
        target = place.device(place.ahead(kind), ctx) if 0 < kind < half else place.sibling()
        return pltpu.make_async_remote_copy(
            src_ref=src,
            dst_ref=dst,
            send_sem=x_send.at[kind, s],
            recv_sem=x_recv.at[kind, s],
            device_id=target,
            device_id_type=MESH,
        )

    def crossed(kind, s):
        if kind == 0:
            rows = adapter_rows(ahead * s, 1 - ctx, part)
        elif kind < half:
            rows = adapter_rows(-ahead * s, ctx, place.behind(kind))
        else:
            rows = adapter_rows(ahead * s, 1 - ctx, place.behind(kind - half + 1))
        return pltpu.make_async_remote_copy(
            src_ref=rows,
            dst_ref=rows,
            send_sem=x_send.at[kind, s],
            recv_sem=x_recv.at[kind, s],
            device_id=place.sibling(),
            device_id_type=MESH,
        )

    def hop(w, way, s):
        offset = -s if way == 0 else s
        rows = blocks_out[w].at[ring.index(offset) * n_c + way]
        return pltpu.make_async_remote_copy(
            src_ref=rows,
            dst_ref=rows,
            send_sem=ring_send.at[w, way, s],
            recv_sem=ring_recv.at[w, way, s],
            device_id=ring.device(1 if way == 0 else n_dp - 1),
            device_id_type=MESH,
        )

    def hopped(w, way, s):
        offset = -(s + 1) if way == 0 else s + 1
        rows = blocks_out[w].at[ring.index(offset) * n_c + way]
        return pltpu.make_async_remote_copy(
            src_ref=rows,
            dst_ref=rows,
            send_sem=ring_send.at[w, way, s],
            recv_sem=ring_recv.at[w, way, s],
            device_id=ring.device(1),
            device_id_type=MESH,
        )

    around(0).start()
    own = pltpu.make_async_copy(own_rows, adapter_rows(0, ctx, part), own_sem.at[count])
    own.start()

    def start_move(w):
        for g in range(sz.seqs):
            here = at_home & (place.group == g)
            pl.when(jnp.logical_not(here))(lambda w=w, g=g: move(w, g).start())
        pl.when(at_home)(lambda w=w: stay(w).start())

    start_move(0)
    start_move(1)
    across(0, 0).start()
    swaps = []

    def across_z():
        if swaps:
            s = swaps.pop(0)
            for q in range(1, half):
                across(q, s).start()

    swaps.append(0)

    def adapter_step(s):
        if s < steps:
            arrival = pltpu.make_async_remote_copy(
                src_ref=own_rows,
                dst_ref=adapter_rows(-ahead * (s + 1), ctx, part),
                send_sem=a_send.at[s],
                recv_sem=a_recv.at[s],
                device_id=ring.device(1),
                device_id_type=MESH,
            )
            arrival.wait_recv()
            if s + 1 < steps:
                around(s + 1).start()
            across(0, s + 1).start()
            swaps.append(s + 1)

    def adapter_pass(s):
        for q in range(1, half):
            crossed(q, s).wait_recv()
            across(half - 1 + q, s).start()

    embed_save = pltpu.make_async_copy(embed_s, embed_out, keep_sem.at[3 + sz.seqs])
    todo = []
    for k in range(rings + steps):
        for s in range(min(k, steps - 1), -1, -1):
            w = k - s
            if w < rings:
                todo.append((w, s))
    done = 0
    for w, s in todo:
        for way in range(n_c):
            if s == 0:
                moved(w, way)
            else:
                hopped(w, way, s - 1).wait_recv()
            hop(w, way, s).start()
        if s == 0 and w + 2 < count:
            start_move(w + 2)
        if s == 0 and w >= 1:
            across_z()
        if s == 0 and w == rings - 1:
            for i in range(3):
                swap(i).start()
        if done < steps:
            adapter_step(done)
        if s == min(2, steps - 1) and w == rings - 1:
            for i in range(3):
                keep(i).wait()
                swapped(i).wait_recv()
            for j in range(sz.seqs):
                own_rows_of(j).start()
            embed_save.start()
            for j in range(sz.seqs):
                own_rows_of(j).wait()
                gather.start(j)
            state_out[...] = state_s[...].astype(jnp.float32)
        done += 1
    for s in range(done, steps):
        adapter_step(s)
    while swaps:
        across_z()
    for s in range(n_dp):
        adapter_pass(s)
    for j in range(sz.seqs):
        gather.wait_near(j)
        for q in range(1, half):
            gather.forward(q, j)
    for s in range(n_dp):
        crossed(0, s).wait_recv()
        for q in range(1, half):
            crossed(half - 1 + q, s).wait_recv()
    own.wait()
    slots, depth = adapter_out.shape[0], weight_s.shape[1]
    loads = [
        pltpu.make_async_copy(
            adapter_out.at[slots // 2 + b, pl.ds(0, depth)], weight_s.at[b % 2], weight_sem.at[b % 2]
        )
        for b in range(slots // 2)
    ]
    loads[0].start()
    for b, copy in enumerate(loads):
        if b + 1 < len(loads):
            loads[b + 1].start()
        copy.wait()
        part_here = nn_dot(embed_s[:, b * depth : (b + 1) * depth], weight_s[b % 2])
        if b:
            embed_part[...] += part_here
        else:
            embed_part[...] = part_here
    for way in range(n_c):
        for w in range(rings):
            hopped(w, way, steps - 1).wait_recv()
        moved(rings, way)
    for j in range(sz.seqs):
        for q in range(1, half):
            gather.wait_far(q, j)
    gather.finish()
    embed_save.wait()
    for i in range(3):
        swap(i).wait_send()
    for w in range(count):
        for g in range(sz.seqs):
            here = at_home & (place.group == g)
            pl.when(jnp.logical_not(here))(lambda w=w, g=g: move(w, g).wait_send())
        for way in range(n_c if w < rings else 0):
            for s in range(steps):
                hop(w, way, s).wait_send()
    for s in range(steps):
        around(s).wait_send()
    for s in range(n_dp):
        for kind in range(2 * half - 1):
            across(kind, s).wait_send()


def run_weights(sz, n_dp, adapter, adapter_block, blocks, rows):
    bf16, f32 = jnp.bfloat16, jnp.float32
    slots = n_dp * sz.n_context
    outs = [jax.ShapeDtypeStruct((slots,) + a.shape, bf16) for a in [adapter] + blocks[:-1]]
    outs.append(jax.ShapeDtypeStruct((sz.n_context,) + blocks[-1].shape, bf16))
    outs += [
        jax.ShapeDtypeStruct((sz.rows, sz.width), bf16),
        jax.ShapeDtypeStruct((sz.rows, sz.width), bf16),
        jax.ShapeDtypeStruct((sz.seq_len, sz.width), bf16),
        jax.ShapeDtypeStruct((sz.rows, sz.width), f32),
        jax.ShapeDtypeStruct((sz.rows, sz.width), f32),
    ]
    count, steps, dma = len(blocks), n_dp - 1, pltpu.SemaphoreType.DMA
    kinds = 2 * sz.half - 1
    return pl.pallas_call(
        partial(weights_kernel, sz, n_dp),
        out_shape=outs,
        in_specs=[any_spec()] * (4 + count),
        out_specs=[any_spec()] * (4 + count) + [full_spec()] * 2,
        scratch_shapes=[
            dma((count, sz.seqs)),
            dma((count, sz.n_context)),
            dma((count, sz.n_context, steps)),
            dma((count, sz.n_context, steps)),
            dma((steps,)),
            dma((steps,)),
            dma((kinds, n_dp)),
            dma((kinds, n_dp)),
            dma((count + 1,)),
            pltpu.VMEM((sz.rows, sz.width), bf16),
            pltpu.VMEM((sz.rows, sz.width), bf16),
            pltpu.VMEM((2, adapter_block, sz.width), bf16),
            dma((3,)),
            dma((3,)),
            dma((4 + sz.seqs,)),
            dma((2,)),
        ]
        + Gather.scratch(sz),
        compiler_params=pltpu.CompilerParams(
            collective_id=5, has_side_effects=True, vmem_limit_bytes=VMEM_BYTES
        ),
        name="weights",
    )(adapter, *blocks, *rows)


def norm_back(grad, rows, factor, gain):
    unit = rows * factor
    weighted = grad * gain
    inner = jnp.mean(weighted * unit, axis=-1, keepdims=True)
    return factor * (weighted - unit * inner), jnp.sum(grad * unit, axis=0, keepdims=True)


class GradRing:
    @staticmethod
    def scratch(sz, n_dp, tasks, wide, own_rows=None):
        slots, ways, dma = n_dp * sz.n_context, sz.n_context, pltpu.SemaphoreType.DMA
        depth, bf16, count, last = sz.width // slots, jnp.bfloat16, len(wide), n_dp - 1
        own_rows = [True] * count if own_rows is None else own_rows
        hops = [[s for w, s in tasks if w == i] for i in range(count)]
        return (
            [pltpu.VMEM((sz.seq_len, n), bf16) for n, own in zip(wide, own_rows) if own]
            + [pltpu.VMEM((ways, depth, n) if 0 in h else (ways, 16, 128), bf16) for n, h in zip(wide, hops)]
            + [pltpu.VMEM((ways, min(max(h) + 1, last), depth, n), bf16) for n, h in zip(wide, hops)]
            + [
                pltpu.VMEM((2, ways, sz.seq_len, depth), bf16),
                dma((count,)),
                dma((2, ways)),
                dma((count, ways, last)),
                dma((count, ways, last)),
                dma((ways,)),
            ]
        )

    @staticmethod
    def size(wide, own_rows=None):
        return 2 * len(wide) + (len(wide) if own_rows is None else sum(own_rows)) + 6

    @staticmethod
    def all_tasks(n_dp, count):
        return [
            (k - s, s)
            for k in range(count + n_dp)
            for s in range(min(k, n_dp - 1), -1, -1)
            if k - s < count
        ]

    def __init__(self, sz, place, ring, tasks, xs, ys, refs, rows=None, given=None):
        count, refs = len(xs), list(refs)
        self.sz, self.place, self.ring, self.xs, self.count = sz, place, ring, xs, count
        self.tasks = tasks
        self.ys = [refs.pop(0) if ys[w] is not None else rows[w] for w in range(count)]
        self.first, self.held = refs[:count], refs[count : 2 * count]
        self.x_s, self.load_y, self.load_x, self.send, self.recv, load_given = refs[2 * count :]
        self.y_loads = [
            pltpu.make_async_copy(ys[w], self.ys[w], self.load_y.at[w])
            for w in range(count)
            if ys[w] is not None
        ]
        self.unread = {w: self.y_loads[i] for i, w in enumerate(
            w for w in range(count) if ys[w] is not None
        )}
        self.given = []
        if given is not None:
            self.given = [
                pltpu.make_async_copy(
                    given.at[way], self.held[0].at[way, tasks[0][1] - 1], load_given.at[way]
                )
                for way in range(sz.n_context)
            ]
        self.done = 0

    def start(self):
        for copy in self.y_loads + self.given:
            copy.start()
        for way in range(self.sz.n_context):
            self.x_load(0, way).start()

    def slot(self, way, s):
        return self.ring.index(-(s + 1) if way == 0 else s + 1) * self.sz.n_context + way

    def x_load(self, k, way):
        w, s = self.tasks[k]
        depth = self.x_s.shape[3]
        if self.xs[w].shape[0] == 1:
            at = pl.multiple_of(self.slot(way, s) * depth, depth)
            src = self.xs[w].at[0, :, pl.ds(at, depth)]
        else:
            src = self.xs[w].at[self.slot(way, s)]
        return pltpu.make_async_copy(src, self.x_s.at[k % 2, way], self.load_x.at[k % 2, way])

    def source(self, w, way, s):
        return self.first[w].at[way] if s == 0 else self.held[w].at[way, s - 1]

    def hop(self, w, way, s):
        return pltpu.make_async_remote_copy(
            src_ref=self.source(w, way, s),
            dst_ref=self.held[w].at[way, s],
            send_sem=self.send.at[w, way, s],
            recv_sem=self.recv.at[w, way, s],
            device_id=self.ring.device(1 if way == 0 else self.ring.count - 1),
            device_id_type=MESH,
        )

    def result(self, w, way):
        return self.source(w, way, self.ring.count - 1)

    def step(self):
        k = self.done
        self.done += 1
        w, s = self.tasks[k]
        ways = range(self.sz.n_context)
        if k + 1 < len(self.tasks):
            for way in ways:
                self.x_load(k + 1, way).start()
        if w in self.unread:
            self.unread.pop(w).wait()
        for way in ways:
            self.x_load(k, way).wait()
            value = tn_dot(self.x_s[k % 2, way], self.ys[w][...])
            if k == 0 and self.given:
                self.given[way].wait()
            elif s:
                self.hop(w, way, s - 1).wait_recv()
            if s:
                value = value + self.held[w][way, s - 1].astype(jnp.float32)
            ref = self.source(w, way, s)
            ref[...] = value.astype(jnp.bfloat16)
            if s < self.ring.count - 1:
                self.hop(w, way, s).start()
        return w, s == self.ring.count - 1

    def left(self):
        return len(self.tasks) - self.done

    def finish(self):
        for w, s in self.tasks:
            if s < self.ring.count - 1:
                for way in range(self.sz.n_context):
                    self.hop(w, way, s).wait_send()


class Deliver:
    @staticmethod
    def scratch(sz, n_dp, wide):
        depth, count, dma = sz.width // (n_dp * sz.n_context), len(wide), pltpu.SemaphoreType.DMA
        return [pltpu.VMEM((sz.seqs, depth, n), jnp.bfloat16) for n in wide] + [
            dma((count, sz.n_context)),
            dma((count, sz.seqs)),
            dma((count,)),
        ]

    def __init__(self, sz, place, refs):
        self.sz, self.place = sz, place
        self.landed = refs[:-3]
        self.send, self.recv, self.own = refs[-3:]
        self.count = len(self.landed)
        self.t = lax.axis_index("tensor")
        self.role = place.part * sz.n_context + place.ctx
        self.at_home = self.role == self.t
        self.sources = [None] * self.count

    def greet(self):
        sz, place = self.sz, self.place
        barrier = pltpu.get_barrier_semaphore()
        for g in range(sz.seqs):
            holder = (place.dp, g * sz.half + self.t // sz.n_context, lax.rem(self.t, sz.n_context))
            pl.when(jnp.logical_not(self.at_home & (place.group == g)))(
                lambda holder=holder: pl.semaphore_signal(
                    barrier, inc=1, device_id=holder, device_id_type=MESH
                )
            )
        return sz.n_context - jnp.where(self.at_home, 1, 0)

    def remote(self, w, way):
        return pltpu.make_async_remote_copy(
            src_ref=self.sources[w][way],
            dst_ref=self.landed[w].at[self.place.group],
            send_sem=self.send.at[w, way],
            recv_sem=self.recv.at[w, self.place.group],
            device_id=(self.place.dp, self.role, way),
            device_id_type=MESH,
        )

    def local(self, w, way):
        return pltpu.make_async_copy(
            self.sources[w][way], self.landed[w].at[self.place.group], self.own.at[w]
        )

    def start(self, w, sources):
        self.sources[w] = sources
        for way in range(self.sz.n_context):
            here = self.at_home & (self.place.ctx == way)
            pl.when(here)(lambda way=way: self.local(w, way).start())
            pl.when(jnp.logical_not(here))(lambda way=way: self.remote(w, way).start())

    def total(self, w):
        place = self.place
        for g in range(self.sz.seqs):
            ref = self.landed[w].at[g]
            arrival = pltpu.make_async_remote_copy(
                src_ref=ref,
                dst_ref=ref,
                send_sem=self.send.at[w, 0],
                recv_sem=self.recv.at[w, g],
                device_id=(place.dp, self.t, 1 - place.ctx),
                device_id_type=MESH,
            )
            here = self.at_home & (place.group == g)
            pl.when(here)(lambda: self.local(w, 0).wait())
            pl.when(jnp.logical_not(here))(lambda arrival=arrival: arrival.wait_recv())
        total = self.landed[w][0].astype(jnp.float32)
        for g in range(1, self.sz.seqs):
            total = total + self.landed[w][g].astype(jnp.float32)
        return total

    def finish(self):
        for w in range(self.count):
            for way in range(self.sz.n_context):
                here = self.at_home & (self.place.ctx == way)
                pl.when(jnp.logical_not(here))(lambda w=w, way=way: self.remote(w, way).wait_send())


def slot_columns(sz, n_dp, x):
    slots = n_dp * sz.n_context
    depth = sz.width // slots
    if depth % 128:
        return x.reshape(sz.seq_len, slots, depth).transpose(1, 0, 2)
    return x[None]


def ffn_back_kernel(sz, n_dp, *refs):
    (cot, mixed, gains) = refs[:3]
    (rows_hbm, gate_hbm, up_hbm, wg_hbm, wu_hbm, down_hbm) = refs[3:9]
    (x_hbm, normed_hbm, hidden_hbm) = refs[9:12]
    (grad_mixed, gain_grad, dgate_out, dup_out, down_sum, gate_part) = refs[12:18]
    (rows_s, gate_s, up_s, wg, wu, wd, load, load_down, keep_sem) = refs[18:27]
    scatter_refs, ring_refs = refs[27:35], refs[35:]
    place = Place(sz)
    ring = Ring(place, n_dp)
    grads = GradRing(
        sz, place, ring, ffn_back_tasks(n_dp), [x_hbm, normed_hbm], [hidden_hbm, None], ring_refs,
        rows=[None, gate_s],
    )
    grads.start()
    pairs = ((rows_hbm, rows_s), (gate_hbm, gate_s), (up_hbm, up_s), (wg_hbm, wg), (wu_hbm, wu))
    loads = [
        pltpu.make_async_copy(src, dst, load.at[i]) for i, (src, dst) in enumerate(pairs)
    ]
    down_loads = column_loads(down_hbm, wd, load_down)
    place.enter([ring.device(1), ring.device(n_dp - 1)])
    scatter = Scatter(place, *scatter_refs)
    for copy in [loads[0]] + down_loads + loads[1:]:
        copy.start()
    grads.step()
    for copy in [loads[0]] + down_loads + loads[1:]:
        copy.wait()

    def work(q, j):
        rows = place.tile(q, j)
        dh = nt_dot(rows_s[rows, :], wd[...])
        gate = gate_s[rows, :].astype(jnp.float32)
        up = up_s[rows, :].astype(jnp.float32)
        sig = 1.0 / (1.0 + jnp.exp(-gate))
        dgate = (dh * up * sig * (1.0 + gate * (1.0 - sig))).astype(jnp.bfloat16)
        dup = (dh * gate * sig).astype(jnp.bfloat16)
        gate_s[rows, :] = dgate
        up_s[rows, :] = dup
        scatter.part[...] = nt_dot(dgate, wg[...]) + nt_dot(dup, wu[...])
        scatter.give(q, j)

    far = range(1, sz.half)
    for j in range(sz.seqs):
        for q in far:
            work(q, j)
        if j:
            for q in far:
                scatter.onward(q, j - 1)
    grads.step()
    work(0, 0)
    for q in far:
        scatter.onward(q, sz.seqs - 1)
    for j in range(1, sz.seqs):
        work(0, j)
    grads.step()
    copies = [
        pltpu.make_async_copy(gate_s, dgate_out, keep_sem.at[0]),
        pltpu.make_async_copy(up_s, dup_out, keep_sem.at[1]),
    ]
    for copy in copies:
        copy.start()
    gain_total = None
    for j in range(sz.seqs):
        span = slice(j * sz.block, (j + 1) * sz.block)
        rows = mixed[span, :]
        grad, gain_here = norm_back(scatter.total(j), rows, rms_factor(rows), gains[1:2, :])
        grad_mixed[span, :] = cot[span, :].astype(jnp.float32) + grad
        gain_total = gain_here if gain_total is None else gain_total + gain_here
    gain_grad[...] = gain_total
    while grads.left():
        grads.step()
    for way in range(sz.n_context):
        grads.hop(1, way, 0).wait_recv()
        for i, (src, dst) in enumerate(
            ((grads.result(0, way), down_sum), (grads.held[1].at[way, 0], gate_part))
        ):
            copies.append(
                pltpu.make_async_copy(src, dst.at[way], keep_sem.at[2 + 2 * way + i])
            )
            copies[-1].start()
    scatter.finish()
    grads.finish()
    for copy in copies:
        copy.wait()


def ffn_back_tasks(n_dp):
    return [(0, 0), (0, 1), (1, 0)] + [(0, s) for s in range(2, n_dp)]


def run_ffn_back(sz, n_dp, cot, mixed, gains, rows, gate, up, wg, wu, down, normed, hidden):
    f32, bf16, shape = jnp.float32, jnp.bfloat16, jax.ShapeDtypeStruct
    dma = pltpu.SemaphoreType.DMA
    depth = sz.width // (n_dp * sz.n_context)
    return pl.pallas_call(
        partial(ffn_back_kernel, sz, n_dp),
        out_shape=[
            shape((sz.rows, sz.width), f32),
            shape((1, sz.width), f32),
            shape((sz.seq_len, sz.ff), bf16),
            shape((sz.seq_len, sz.ff), bf16),
            shape((sz.n_context, depth, sz.ff), bf16),
            shape((sz.n_context, depth, sz.ff), bf16),
        ],
        in_specs=[full_spec()] * 3 + [any_spec()] * 9,
        out_specs=[full_spec()] * 2 + [any_spec()] * 4,
        scratch_shapes=[
            pltpu.VMEM((sz.seq_len, sz.width), bf16),
            pltpu.VMEM((sz.seq_len, sz.ff), bf16),
            pltpu.VMEM((sz.seq_len, sz.ff), bf16),
            pltpu.VMEM(wg.shape, bf16),
            pltpu.VMEM(wu.shape, bf16),
            pltpu.VMEM((sz.ff, sz.width), bf16),
            dma((5,)),
            dma((down.shape[0],)),
            dma((2 + 2 * sz.n_context,)),
        ]
        + Scatter.scratch(sz)
        + GradRing.scratch(sz, n_dp, ffn_back_tasks(n_dp), [sz.ff, sz.ff], [True, False]),
        compiler_params=pltpu.CompilerParams(
            collective_id=6, has_side_effects=True, vmem_limit_bytes=VMEM_BYTES
        ),
        cost_estimate=pl.CostEstimate(
            flops=8 * sz.seq_len * sz.width * sz.ff, bytes_accessed=40 << 20, transcendentals=0
        ),
        name="ffn_back",
    )(
        cot, mixed, gains, rows, gate, up, wg, wu, down,
        slot_columns(sz, n_dp, rows), slot_columns(sz, n_dp, normed), hidden,
    )


def attn_back_kernel(sz, n_dp, *refs):
    (grad_mixed, gains, cos_t, sin_t, begin, gain_b, adapted_hbm, state_hbm) = refs[:8]
    (q_hbm, k_hbm, v_hbm, lse_hbm, out_hbm, qkv_hbm) = refs[8:14]
    (x_hbm, dgate_hbm, dup_hbm, down_sum, gate_part) = refs[14:19]
    (grad_low, down_grad, gate_grad, state_out, rows_out, proj_out, up_part) = refs[19:26]
    (rows_s, q_s, k_s, v_s, lse_s, do_s, dk_s, dv_s, proj_s, wout, wqkv) = refs[26:37]
    (load, load_out, keep_sem, swap_out, swap_in, swap_sem, late) = refs[37:44]
    gather_refs, scatter_refs = refs[44:46], refs[46:54]
    ring_refs, deliver_refs = refs[54:66], refs[66:]
    place = Place(sz)
    ring = Ring(place, n_dp)
    grads = GradRing(
        sz, place, ring, attn_back_tasks(n_dp), [x_hbm, x_hbm], [dgate_hbm, dup_hbm], ring_refs,
        given=gate_part,
    )
    deliver = Deliver(sz, place, deliver_refs)
    grads.start()
    split = wqkv.shape[0]
    pairs = (
        (q_hbm, q_s), (k_hbm, k_s), (v_hbm, v_s), (lse_hbm, lse_s),
        (qkv_hbm.at[pl.ds(split, split)], wqkv),
    )
    loads = [
        pltpu.make_async_copy(src, dst, load.at[i]) for i, (src, dst) in enumerate(pairs)
    ]
    out_loads = column_loads(out_hbm, wout, load_out)
    for copy in out_loads + loads:
        copy.start()
    targets = deliver.greet()
    other = other_group(place)
    place.enter([ring.device(1), ring.device(n_dp - 1), other], targets)
    gather = Gather(place, rows_s, *gather_refs)
    scatter = Scatter(place, *scatter_refs)
    for j in range(sz.seqs):
        span = slice(j * sz.block, (j + 1) * sz.block)
        rows_s[gather.own(j), :] = grad_mixed[span, :].astype(jnp.bfloat16)
        gather.start(j)
    grads.step()
    deliver.start(0, [down_sum.at[way] for way in range(sz.n_context)])
    give_rows = pl.ds(pl.multiple_of((1 - place.group) * sz.block, sz.block), sz.block)
    keep_rows = pl.ds(pl.multiple_of(place.group * sz.block, sz.block), sz.block)
    swap = pltpu.make_async_remote_copy(
        src_ref=swap_out,
        dst_ref=swap_in,
        send_sem=swap_sem.at[0],
        recv_sem=swap_sem.at[1],
        device_id=other,
        device_id_type=MESH,
    )
    state_load = pltpu.make_async_copy(
        state_hbm.at[give_rows], scatter.part.at[pl.ds(0, sz.block)], late.at[0]
    )
    state_keep = pltpu.make_async_copy(
        state_hbm.at[keep_rows], state_out.at[place.group], late.at[1]
    )
    state_load.start()
    state_keep.start()
    state_load.wait()
    swap_out[...] = scatter.part[: sz.block, :].astype(jnp.bfloat16)
    swap.start()
    for copy in out_loads:
        copy.wait()
    d = sz.head_dim

    def heads_grad(q, j):
        rows = place.tile(q, j)
        dhead = nt_dot(rows_s[rows, :], wout[...]).astype(jnp.bfloat16)
        for h in range(sz.heads):
            do_s[h, rows, :] = dhead[:, h * d : (h + 1) * d]

    far = range(1, sz.half)
    for j in range(sz.seqs):
        gather.wait_near(j)
        heads_grad(0, j)
    for copy in loads:
        copy.wait()
    for j in range(sz.seqs):
        if j == sz.seqs - 1:
            grads.step()
            grads.step()
        for q in far:
            gather.forward(q, j)
        for q in far:
            gather.wait_far(sz.half - q, j)
            heads_grad(q, j)
    rows_copy = pltpu.make_async_copy(rows_s, rows_out, keep_sem.at[0])
    rows_copy.start()
    gather.finish()
    rows_copy.wait()
    upper = rows_s.at[pl.ds(0, split), pl.ds(0, wqkv.shape[1])]
    upper_load = pltpu.make_async_copy(qkv_hbm.at[pl.ds(0, split)], upper, late.at[2])
    upper_load.start()

    tiles = sz.n_tensor
    scale = 1.0 / math.sqrt(d)

    def head(h, carry):
        for i in reversed(range(tiles)):
            rows = slice(i * sz.tile, (i + 1) * sz.tile)
            length = (i + 1) * sz.tile
            keys, values = k_s[h, 0:length, :], v_s[h, 0:length, :]
            query, grad = q_s[h, rows, :], do_s[h, rows, :]
            start = begin[:, rows]
            key_at = lax.broadcasted_iota(jnp.int32, (length, sz.tile), 0)
            query_at = i * sz.tile + lax.broadcasted_iota(jnp.int32, (1, sz.tile), 1)
            allowed = (key_at >= start) & (key_at <= query_at)
            scores = nt_dot(keys, query)
            scores = jnp.where(allowed, scores * (LOG2E * scale), masked_score)
            probs = jnp.exp2(scores - lse_s[h, :, rows])
            dprobs = nt_dot(values, grad)
            inner = jnp.sum(probs * dprobs, axis=0, keepdims=True)
            dscores = (probs * (dprobs - inner)).astype(jnp.bfloat16)
            dv = nn_dot(probs.astype(jnp.bfloat16), grad)
            dk = nn_dot(dscores, query)
            if i == tiles - 1:
                dv_s[...] = dv
                dk_s[...] = dk
            else:
                dv_s[0:length, :] += dv
                dk_s[0:length, :] += dk
            dq = jnp.transpose(tn_dot(keys, dscores)) * scale
            cos_here, sin_here = cos_t[rows, :], sin_t[rows, :]
            proj_s[rows, pl.ds(pl.multiple_of(h * 3 * d, d), d)] = turn(
                dq, cos_here, -sin_here
            ).astype(jnp.bfloat16)
        dk = turn(dk_s[...] * scale, cos_t[...], -sin_t[...])
        proj_s[:, pl.ds(pl.multiple_of(h * 3 * d + d, d), d)] = dk.astype(jnp.bfloat16)
        proj_s[:, pl.ds(pl.multiple_of(h * 3 * d + 2 * d, d), d)] = dv_s[...].astype(jnp.bfloat16)
        return carry

    lax.fori_loop(0, sz.heads // 2, head, 0)
    while grads.left() > 1:
        grads.step()
    deliver.start(1, [grads.result(0, way) for way in range(sz.n_context)])
    lax.fori_loop(sz.heads // 2, sz.heads, head, 0)
    copies = [pltpu.make_async_copy(proj_s, proj_out, keep_sem.at[1])]
    copies[0].start()
    upper_load.wait()

    def give(q, j):
        proj = proj_s[place.tile(q, j), :]
        scatter.part[:, :split] = nt_dot(proj, upper[...])
        scatter.part[:, split:] = nt_dot(proj, wqkv[...])
        scatter.give(q, j)

    for j in range(sz.seqs):
        for q in far:
            give(q, j)
        if j:
            for q in far:
                scatter.onward(q, j - 1)
    give(0, 0)
    for q in far:
        scatter.onward(q, sz.seqs - 1)
    for j in range(1, sz.seqs):
        give(0, j)
    adapted = scatter.part
    adapted_load = pltpu.make_async_copy(adapted_hbm, adapted, late.at[3])
    adapted_load.start()
    grads.step()
    swap.wait()
    state_keep.wait()
    adapted_load.wait()
    state_out[1 - place.group] = swap_in[...].astype(jnp.float32)
    down_grad[...] = deliver.total(0)
    gain_total = None
    for j in range(sz.seqs):
        span = slice(j * sz.block, (j + 1) * sz.block)
        rows = adapted[span, :]
        grad, gain_here = norm_back(scatter.total(j), rows, rms_factor(rows), gains[0:1, :])
        grad_low[span, :] = (grad_mixed[span, :] + grad).astype(jnp.bfloat16)
        gain_total = gain_here if gain_total is None else gain_total + gain_here
    extra = grad_low.shape[0] - sz.rows
    at_row = lax.broadcasted_iota(jnp.int32, (extra, sz.width), 0)
    shares = jnp.where(at_row == 0, gain_total, jnp.where(at_row == 1, gain_b[...], 0.0))
    grad_low[sz.rows :, :] = shares.astype(jnp.bfloat16)
    for way in range(sz.n_context):
        grads.hop(1, way, 1).wait_recv()
        copies.append(
            pltpu.make_async_copy(
                grads.held[1].at[way, 1], up_part.at[way], keep_sem.at[2 + way]
            )
        )
        copies[-1].start()
    gate_grad[...] = deliver.total(1)
    scatter.finish()
    grads.finish()
    deliver.finish()
    for copy in copies:
        copy.wait()


def attn_back_tasks(n_dp):
    return [(0, 1), (0, 2), (1, 0)] + [(0, s) for s in range(3, n_dp)] + [(1, 1)]


def run_attn_back(
    sz, n_dp, grad_mixed, adapted, gains, cos_t, sin_t, begin, gain_b, state, q, k, v, lse, out,
    qkv, x, dgate, dup, down_sum, gate_part,
):
    f32, bf16, shape = jnp.float32, jnp.bfloat16, jax.ShapeDtypeStruct
    dma = pltpu.SemaphoreType.DMA
    heads_shape = (sz.heads, sz.seq_len, sz.head_dim)
    return pl.pallas_call(
        partial(attn_back_kernel, sz, n_dp),
        out_shape=[
            shape((sz.rows + 16, sz.width), bf16),
            shape(down_sum.shape[1:], f32),
            shape(gate_part.shape[1:], f32),
            shape((sz.seqs, sz.block, sz.width), f32),
            shape((sz.seq_len, sz.width), bf16),
            shape((sz.seq_len, qkv.shape[1]), bf16),
            shape(gate_part.shape, bf16),
        ],
        in_specs=[full_spec()] * 6 + [any_spec()] * 13,
        out_specs=[full_spec()] * 4 + [any_spec()] * 3,
        scratch_shapes=[
            pltpu.VMEM((sz.seq_len, sz.width), bf16),
            pltpu.VMEM(heads_shape, bf16),
            pltpu.VMEM(heads_shape, bf16),
            pltpu.VMEM(heads_shape, bf16),
            pltpu.VMEM((sz.heads, 1, sz.seq_len), f32),
            pltpu.VMEM(heads_shape, bf16),
            pltpu.VMEM((sz.seq_len, sz.head_dim), f32),
            pltpu.VMEM((sz.seq_len, sz.head_dim), f32),
            pltpu.VMEM((sz.seq_len, qkv.shape[1]), bf16),
            pltpu.VMEM((sz.heads * sz.head_dim, sz.width), bf16),
            pltpu.VMEM((sz.width // 2, qkv.shape[1]), bf16),
            dma((5,)),
            dma((out.shape[0],)),
            dma((2 + sz.n_context,)),
            pltpu.VMEM((sz.block, sz.width), bf16),
            pltpu.VMEM((sz.block, sz.width), bf16),
            dma((2,)),
            dma((4,)),
        ]
        + Gather.scratch(sz)
        + Scatter.scratch(sz)
        + GradRing.scratch(sz, n_dp, attn_back_tasks(n_dp), [sz.ff, sz.ff])
        + Deliver.scratch(sz, n_dp, [sz.ff, sz.ff]),
        compiler_params=pltpu.CompilerParams(
            collective_id=7, has_side_effects=True, vmem_limit_bytes=VMEM_BYTES
        ),
        cost_estimate=pl.CostEstimate(
            flops=4 * sz.seq_len * sz.width * qkv.shape[1], bytes_accessed=30 << 20, transcendentals=0
        ),
        name="attn_back",
    )(
        grad_mixed, gains, cos_t, sin_t, begin, gain_b, adapted, state, q, k, v, lse, out, qkv,
        slot_columns(sz, n_dp, x), dgate, dup, down_sum, gate_part,
    )


class PlaneRows:
    @staticmethod
    def scratch(n_dp):
        dma = pltpu.SemaphoreType.DMA
        return [dma((n_dp - 1,)), dma((n_dp - 1,)), dma((n_dp,)), dma((n_dp,))]

    def __init__(self, place, ring, own, landed, refs):
        self.place, self.ring, self.own, self.landed = place, ring, own, landed
        self.send, self.recv, self.near_send, self.near_recv = refs
        self.ahead = 1 - 2 * place.ctx

    def slot(self, offset, ctx):
        return self.landed.at[self.ring.index(offset) * self.place.sz.n_context + ctx]

    def source(self, s):
        return self.own if s == 0 else self.slot(-self.ahead * s, self.place.ctx)

    def hop(self, s):
        return pltpu.make_async_remote_copy(
            src_ref=self.source(s),
            dst_ref=self.slot(-self.ahead * s, self.place.ctx),
            send_sem=self.send.at[s],
            recv_sem=self.recv.at[s],
            device_id=self.ring.device(self.ahead),
            device_id_type=MESH,
        )

    def near(self, s):
        return pltpu.make_async_remote_copy(
            src_ref=self.source(s),
            dst_ref=self.slot(-self.ahead * s, self.place.ctx),
            send_sem=self.near_send.at[s],
            recv_sem=self.near_recv.at[s],
            device_id=self.place.sibling(),
            device_id_type=MESH,
        )

    def start(self):
        self.hop(0).start()
        self.near(0).start()

    def step(self, s):
        ref = self.slot(-self.ahead * (s + 1), self.place.ctx)
        pltpu.make_async_remote_copy(
            src_ref=ref,
            dst_ref=ref,
            send_sem=self.send.at[s],
            recv_sem=self.recv.at[s],
            device_id=self.place.sibling(),
            device_id_type=MESH,
        ).wait_recv()
        if s + 1 < self.ring.count - 1:
            self.hop(s + 1).start()
        self.near(s + 1).start()

    def wait_near(self, s):
        ref = self.slot(self.ahead * s, 1 - self.place.ctx)
        pltpu.make_async_remote_copy(
            src_ref=ref,
            dst_ref=ref,
            send_sem=self.near_send.at[s],
            recv_sem=self.near_recv.at[s],
            device_id=self.place.sibling(),
            device_id_type=MESH,
        ).wait_recv()

    def finish(self):
        for s in range(self.ring.count):
            if s < self.ring.count - 1:
                self.hop(s).wait_send()
            self.near(s).wait_send()


class LineSum:
    @staticmethod
    def scratch(sz, parts, chunk):
        dma, bf16 = pltpu.SemaphoreType.DMA, jnp.bfloat16
        far = pltpu.VMEM((max(sz.half - 1, 1), parts, chunk, sz.width), bf16)
        one = pltpu.VMEM((parts, chunk, sz.width), bf16)
        kinds = 2 * sz.half - 1
        return [far, far, one, one, one, far, dma((kinds, parts)), dma((kinds, parts))]

    def __init__(self, place, total, parts, refs):
        self.place, self.total, self.parts = place, total, parts
        (self.out, self.got, self.sum, self.cross, self.done, self.back, self.send, self.recv) = refs
        self.chunk = self.sum.shape[1]

    def rows(self, part, k):
        first = (part * self.parts + k) * self.chunk
        return pl.ds(pl.multiple_of(first, self.chunk), self.chunk)

    def copy(self, src, dst, kind, k, device):
        return pltpu.make_async_remote_copy(
            src_ref=src,
            dst_ref=dst,
            send_sem=self.send.at[kind, k],
            recv_sem=self.recv.at[kind, k],
            device_id=device,
            device_id_type=MESH,
        )

    def spread(self, q, k):
        place = self.place
        device = place.device(place.ahead(q), place.ctx)
        return self.copy(self.out.at[q - 1, k], self.got.at[q - 1, k], q, k, device)

    def swap(self, k):
        return self.copy(self.sum.at[k], self.cross.at[k], 0, k, other_group(self.place))

    def collect(self, q, k):
        place = self.place
        device = place.device(place.ahead(q), place.ctx)
        return self.copy(
            self.done.at[k], self.back.at[q - 1, k], place.sz.half - 1 + q, k, device
        )

    def start(self, k):
        for q in range(1, self.place.sz.half):
            rows = self.rows(self.place.ahead(q), k)
            self.out[q - 1, k] = self.total[rows, :].astype(jnp.bfloat16)
            self.spread(q, k).start()

    def cross_over(self, k):
        value = self.total[self.rows(self.place.part, k), :]
        for q in range(1, self.place.sz.half):
            self.spread(q, k).wait_recv()
            value = value + self.got[q - 1, k].astype(jnp.float32)
        self.sum[k] = value.astype(jnp.bfloat16)
        self.swap(k).start()

    def share(self, k):
        self.swap(k).wait_recv()
        value = self.sum[k].astype(jnp.float32) + self.cross[k].astype(jnp.float32)
        self.done[k] = value.astype(jnp.bfloat16)
        for q in range(1, self.place.sz.half):
            self.collect(q, k).start()
        self.total[self.rows(self.place.part, k), :] = self.done[k].astype(jnp.float32)

    def complete(self, k):
        for q in range(1, self.place.sz.half):
            self.collect(q, k).wait_recv()
            rows = self.rows(self.place.behind(q), k)
            self.total[rows, :] = self.back[q - 1, k].astype(jnp.float32)

    def finish(self):
        for k in range(self.parts):
            self.swap(k).wait_send()
            for q in range(1, self.place.sz.half):
                self.spread(q, k).wait_send()
                self.collect(q, k).wait_send()


SUM_PARTS = 2


def grads_kernel(sz, n_dp, count, *refs):
    n_in = 4 + 2 * count
    low, joined, adapter, up_part = refs[:4]
    xs, ys = refs[4 : 4 + count], refs[4 + count : n_in]
    outs = refs[n_in : n_in + count]
    embed_grad, adapter_out, gains_out, landed = refs[n_in + count : n_in + 4 + count]
    refs = refs[n_in + 4 + count :]

    def take(n):
        nonlocal refs
        head, refs = refs[:n], refs[n:]
        return head

    ring_refs, deliver_refs = take(3 * count + 6), take(count + 3)
    plane_refs, sum_refs = take(4), take(8)
    adapter_grad, d_s, j_s, weight_s, rows_s, swap_in = refs[:6]
    d_sem, j_sem, weight_sem, swap_sem, out_sem = refs[6:]
    place = Place(sz)
    ring = Ring(place, n_dp)
    grads = GradRing(
        sz, place, ring, grads_tasks(n_dp, count), xs, ys, ring_refs, given=up_part
    )
    deliver = Deliver(sz, place, deliver_refs)
    plane = PlaneRows(place, ring, low, landed, plane_refs)
    line = LineSum(place, adapter_grad, SUM_PARTS, sum_refs)
    other = other_group(place)
    grads.start()
    weight_load = [
        pltpu.make_async_copy(
            adapter.at[adapter.shape[0] // 2 + b, pl.ds(0, weight_s.shape[0])], weight_s, weight_sem
        )
        for b in range(adapter.shape[0] // 2)
    ]
    weight_load[0].start()
    place.enter([ring.device(1), ring.device(n_dp - 1), other], deliver.greet())
    plane.start()
    give_rows = pl.ds(pl.multiple_of((1 - place.group) * sz.block, sz.block), sz.block)
    keep_rows = pl.ds(pl.multiple_of(place.group * sz.block, sz.block), sz.block)
    swap = pltpu.make_async_remote_copy(
        src_ref=low.at[give_rows],
        dst_ref=swap_in,
        send_sem=swap_sem.at[0],
        recv_sem=swap_sem.at[1],
        device_id=other,
        device_id_type=MESH,
    )
    swap.start()

    def ring_step():
        if grads.left():
            w, complete = grads.step()
            if complete:
                deliver.start(w, [grads.result(w, way) for way in range(sz.n_context)])

    depth = joined.shape[2]

    def batch(ctx):
        copies = []
        for d in range(n_dp):
            at = d * sz.n_context + ctx
            rows = pl.ds(d * sz.rows, sz.rows)
            copies.append(
                pltpu.make_async_copy(landed.at[at, pl.ds(0, sz.rows)], d_s.at[rows], d_sem.at[d, 0])
            )
            copies.append(pltpu.make_async_copy(joined.at[at], j_s.at[rows], j_sem.at[d]))
            copies.append(
                pltpu.make_async_copy(
                    landed.at[at, pl.ds(sz.rows, 16)],
                    d_s.at[pl.ds(n_dp * sz.rows + 16 * d, 16)],
                    d_sem.at[d, 1],
                )
            )
        return copies

    def product(ctx, first):
        copies = batch(ctx)
        for copy in copies:
            copy.start()
        for copy in copies:
            copy.wait()
        chunk = sz.width // 4
        for n in range(4):
            cols = slice(n * chunk, (n + 1) * chunk)
            value = tn_dot(j_s[...], d_s[: n_dp * sz.rows, cols])
            tail = d_s[n_dp * sz.rows : n_dp * sz.rows + 16, cols].astype(jnp.float32)
            for d in range(1, n_dp):
                at = n_dp * sz.rows + 16 * d
                tail = tail + d_s[at : at + 16, cols].astype(jnp.float32)
            if first:
                adapter_grad[:depth, cols] = value
                adapter_grad[depth : depth + 16, cols] = tail
            else:
                adapter_grad[:depth, cols] += value
                adapter_grad[depth : depth + 16, cols] += tail

    own = pltpu.make_async_copy(low, landed.at[place.dp * sz.n_context + place.ctx], d_sem.at[0, 0])
    own.start()
    rest = adapter_grad.shape[0] - depth - 16
    if rest:
        adapter_grad[depth + 16 :, :] = jnp.zeros((rest, sz.width), jnp.float32)
    for s in range(n_dp - 1):
        ring_step()
        plane.step(s)
    own.wait()
    product(place.ctx, True)
    for s in range(n_dp):
        plane.wait_near(s)
    product(1 - place.ctx, False)
    for k in range(SUM_PARTS):
        line.start(k)
    ring_step()
    ring_step()
    swap.wait()
    rows_s[place.group] = low[keep_rows, :]
    rows_s[1 - place.group] = swap_in[...]
    rows = rows_s[...].reshape(sz.rows, sz.width)
    ring_step()
    for k in range(SUM_PARTS):
        line.cross_over(k)
    ring_step()
    for b, copy in enumerate(weight_load):
        copy.wait()
        part = nt_dot(rows, weight_s[...]).reshape(sz.seqs, sz.block, weight_s.shape[0])
        embed_grad[:, :, b * weight_s.shape[0] : (b + 1) * weight_s.shape[0]] = part
        if b + 1 < len(weight_load):
            weight_load[b + 1].start()
    ring_step()
    for k in range(SUM_PARTS):
        line.share(k)
        ring_step()
    while grads.left():
        ring_step()
    for k in range(SUM_PARTS):
        line.complete(k)
    saves = [
        pltpu.make_async_copy(adapter_grad.at[pl.ds(0, depth)], adapter_out, out_sem.at[0]),
        pltpu.make_async_copy(adapter_grad.at[pl.ds(depth, 16)], gains_out, out_sem.at[1]),
    ]
    for copy in saves:
        copy.start()
    for w in range(count):
        outs[w][...] = deliver.total(w)
    for copy in saves:
        copy.wait()
    grads.finish()
    deliver.finish()
    plane.finish()
    line.finish()


def grads_tasks(n_dp, count):
    others = [(w + 1, s) for w, s in GradRing.all_tasks(n_dp, count - 1)]
    return [(0, s) for s in range(2, n_dp)] + others


def run_grads(sz, n_dp, low, joined, adapter, up_part, xs, ys):
    count, bf16, f32, dma = len(xs), jnp.bfloat16, jnp.float32, pltpu.SemaphoreType.DMA
    shape = jax.ShapeDtypeStruct
    depth = sz.width // (n_dp * sz.n_context)
    wide = [y.shape[1] for y in ys]
    slots, columns = joined.shape[0], joined.shape[2]
    unit = 16 * sz.half * SUM_PARTS
    total_rows = -(-(columns + 16) // unit) * unit
    return pl.pallas_call(
        partial(grads_kernel, sz, n_dp, count),
        out_shape=[shape((depth, n), f32) for n in wide]
        + [
            shape((sz.seqs, sz.block, sz.width), f32),
            shape((columns, sz.width), f32),
            shape((16, sz.width), f32),
            shape((slots,) + low.shape, bf16),
        ],
        in_specs=[full_spec()] + [any_spec()] * (3 + 2 * count),
        out_specs=[full_spec()] * (1 + count) + [any_spec()] * 3,
        scratch_shapes=GradRing.scratch(sz, n_dp, grads_tasks(n_dp, count), wide)
        + Deliver.scratch(sz, n_dp, wide)
        + PlaneRows.scratch(n_dp)
        + LineSum.scratch(sz, SUM_PARTS, total_rows // (sz.half * SUM_PARTS))
        + [
            pltpu.VMEM((total_rows, sz.width), f32),
            pltpu.VMEM((n_dp * (sz.rows + 16), sz.width), bf16),
            pltpu.VMEM((n_dp * sz.rows, columns), bf16),
            pltpu.VMEM((columns, sz.width), bf16),
            pltpu.VMEM((sz.seqs, sz.block, sz.width), bf16),
            pltpu.VMEM((sz.block, sz.width), bf16),
            dma((n_dp, 2)),
            dma((n_dp,)),
            dma,
            dma((2,)),
            dma((2,)),
        ],
        compiler_params=pltpu.CompilerParams(
            collective_id=8, has_side_effects=True, vmem_limit_bytes=VMEM_BYTES
        ),
        cost_estimate=pl.CostEstimate(
            flops=2 * sz.seq_len * sz.width * sum(wide), bytes_accessed=60 << 20, transcendentals=0
        ),
        name="grads",
    )(low, joined, adapter, up_part, *[slot_columns(sz, n_dp, x) for x in xs], *ys)


def shards(
    embedded,
    initial_state,
    cotangent,
    doc_ids,
    recurrences,
    adapter_weight,
    norm_gains,
    qkv_weight,
    output_head_weight,
    gate_up_weight,
    down_weight,
):
    n_dp = lax.axis_size("dp")
    n_tensor = lax.axis_size("tensor")
    n_context = lax.axis_size("context")
    dp_index = lax.axis_index("dp")
    t_index = lax.axis_index("tensor")
    ctx_index = lax.axis_index("context")
    seq_count, block_rows, model_width = embedded.shape
    seq_len = doc_ids.shape[1]
    half = n_tensor // seq_count
    group = t_index // half
    part = t_index % half
    heads_here = qkv_weight.shape[1]
    head_dim = qkv_weight.shape[2] // 3
    ff_here = down_weight.shape[0]
    def side_by_side(blocks):
        count, depth, columns = blocks.shape
        return blocks.transpose(1, 0, 2).reshape(depth, count * columns)

    def role_grad(grad, axis):
        piece = lax.psum_scatter(
            grad.astype(jnp.bfloat16), "dp", scatter_dimension=axis, tiled=True
        )
        low, high = jnp.split(piece, 2, axis=axis)
        give = [jnp.where(group == 0, low, high), jnp.where(group == 0, high, low)]
        back = [
            lax.ppermute(g, ("tensor", "context"), [(b, a) for a, b in perm])
            for g, perm in zip(give, role_perms)
        ]
        return back[0].astype(jnp.float32) + back[1].astype(jnp.float32)

    def gather_rows(rows):
        full = lax.all_gather(
            rows, ("tensor", "context"), axis=0, tiled=True, axis_index_groups=groups
        )
        split = full.reshape(half, n_context, seq_count, block_rows, model_width)
        return split.transpose(2, 0, 1, 3, 4).reshape(seq_len, model_width)

    sz = Sizes(
        n_tensor,
        n_context,
        seq_count,
        half,
        block_rows,
        n_context * block_rows,
        seq_count * block_rows,
        seq_len,
        model_width,
        heads_here,
        head_dim,
        ff_here,
    )
    adapter_block = adapter_weight.shape[0]
    gain_columns = norm_gains.shape[1]
    unit = 16 * half
    padded = -(-(adapter_block + 2) // unit) * unit
    adapter_rows = jnp.concatenate(
        [
            adapter_weight,
            jnp.pad(
                norm_gains,
                ((0, padded - adapter_block - 2), (0, model_width - gain_columns)),
            ),
        ],
        axis=0,
    )
    (
        adapter_all,
        out_blocks,
        qkv_use,
        gate_use,
        up_use,
        down_pair,
        embed_rows,
        cot_rows,
        grad_ffn,
        embed_part,
        current,
    ) = run_weights(
        sz,
        n_dp,
        adapter_rows,
        adapter_block,
        [
            output_head_weight.reshape(heads_here * head_dim, -1),
            qkv_weight.reshape(qkv_weight.shape[0], -1),
            gate_up_weight[:, 0],
            gate_up_weight[:, 1],
            down_weight,
        ],
        [embedded, initial_state, cotangent],
    )
    qkv_use = qkv_use.reshape(model_width, -1)
    gate_use = gate_use.reshape(model_width, -1)
    up_use = up_use.reshape(model_width, -1)
    gains_full = (
        adapter_all[:, adapter_block : adapter_block + 2, :gain_columns]
        .transpose(1, 0, 2)
        .reshape(2, model_width)
    )
    if out_blocks.shape[2] % 128:
        out_blocks = side_by_side(out_blocks)[None]
    gains_f = gains_full.astype(jnp.float32)

    cos_full, sin_full = rope_tables(seq_len, head_dim)
    own_seq = dp_index * seq_count + group
    docs = lax.dynamic_index_in_dim(doc_ids, own_seq, 0, keepdims=False)
    begin = jnp.sum((docs[None, :] < docs[:, None]).astype(jnp.int32), axis=1)[None, :]
    steps_own = lax.dynamic_index_in_dim(recurrences, own_seq, 0, keepdims=False) - BACK
    active = jnp.arange(MAXR - BACK, dtype=jnp.int32)[:, None] < steps_own
    active = jnp.broadcast_to(active.astype(jnp.float32), (MAXR - BACK, model_width))
    mixed, down_blocks = run_attn(
        sz, n_dp, False, current, embed_part, gains_f, cos_full, sin_full, begin,
        adapter_all, qkv_use, out_blocks, down_pair,
    )
    if down_blocks.shape[2] % 128:
        down_blocks = side_by_side(down_blocks)[None]
    (current,) = run_ffn(
        sz, False, mixed, current, active[:1], gains_f, gate_use, up_use, down_blocks
    )
    detached = run_rounds(
        sz, current, active[1:], gains_f, cos_full, sin_full, begin, embed_part,
        adapter_all, qkv_use, out_blocks, gate_use, up_use, down_blocks,
    )
    (mixed_rows, adapted, feature_rows, query_hm, key_hm, value_hm, head_flat, lse, joined) = run_attn(
        sz, n_dp, True, detached, embed_part, gains_f, cos_full, sin_full, begin,
        adapter_all, qkv_use, out_blocks, embed_rows,
    )
    (current, ffn_input, gate_pre, up_pre, hidden) = run_ffn(
        sz, True, mixed_rows, detached, gains_f[:1], gains_f, gate_use, up_use, down_blocks
    )
    grad_mixed, gain_b, grad_gate, grad_up, down_sum, gate_part = run_ffn_back(
        sz, n_dp, cot_rows, mixed_rows, gains_f, grad_ffn, gate_pre, up_pre,
        gate_use, up_use, down_blocks, ffn_input, hidden,
    )
    grad_low, down_t, gate_s, state_out, grad_rows, grad_proj, up_part = run_attn_back(
        sz, n_dp, grad_mixed, adapted, gains_f, cos_full, sin_full, begin, gain_b, current,
        query_hm, key_hm, value_hm, lse, out_blocks, qkv_use, ffn_input, grad_gate, grad_up, down_sum,
        gate_part,
    )
    up_s, qkv_s, out_t, embed_out, adapter_s, gains_rows, _ = run_grads(
        sz,
        n_dp,
        grad_low,
        joined,
        adapter_all,
        up_part,
        [ffn_input, feature_rows, grad_rows],
        [grad_up, grad_proj, head_flat],
    )
    place_at = (dp_index * n_context + ctx_index) * gain_columns
    gains_s = lax.dynamic_slice_in_dim(gains_rows[:2], place_at, gain_columns, 1)
    down_s = down_t.T
    out_s = out_t.T.reshape(heads_here, head_dim, -1)
    qkv_s = qkv_s.reshape(-1, heads_here, 3 * head_dim)
    gate_up_s = jnp.stack([gate_s, up_s], axis=1)
    return (state_out, embed_out, adapter_s, gains_s, qkv_s, out_s, gate_up_s, down_s)


def solution(mesh):
    placed = (
        P("dp", ("tensor", "context"), None),
        P("dp", ("tensor", "context"), None),
        P("dp", ("tensor", "context"), None),
        P(),
        P(),
        P(("dp", "context"), None),
        P(None, ("dp", "context")),
        P(("dp", "context"), "tensor", None),
        P("tensor", None, ("dp", "context")),
        P(("dp", "context"), None, "tensor"),
        P("tensor", ("dp", "context")),
    )
    return jax.shard_map(
        shards,
        mesh=mesh,
        in_specs=placed,
        out_specs=(
            P("dp", ("tensor", "context"), None),
            P("dp", ("tensor", "context"), None),
            P(("dp", "context"), None),
            P(None, ("dp", "context")),
            P(("dp", "context"), "tensor", None),
            P("tensor", None, ("dp", "context")),
            P(("dp", "context"), None, "tensor"),
            P("tensor", ("dp", "context")),
        ),
        check_vma=False,
    )
```

```python
from functools import partial
import math
from typing import NamedTuple

import jax
import jax.numpy as jnp
import numpy as np
from jax import lax
from jax.experimental import pallas as pl
from jax.experimental.pallas import tpu as pltpu
from jax.sharding import PartitionSpec as P

BACK = 1
MAXR = 4


rope_base = 50000.0
norm_eps = 1e-06
masked_score = -1e30


def rope_tables(seq_len, head_dim):
    freq_index = np.arange(head_dim // 2, dtype=np.float32)
    inv_freq = 1.0 / np.float32(rope_base) ** (np.float32(2.0) * freq_index / head_dim)
    angles = np.arange(seq_len, dtype=np.float32)[:, None] * inv_freq.astype(np.float32)[None, :]
    cos_t, sin_t = np.cos(angles), np.sin(angles)
    return (
        jnp.asarray(np.concatenate([cos_t, cos_t], axis=1), jnp.float32),
        jnp.asarray(np.concatenate([-sin_t, sin_t], axis=1), jnp.float32),
    )


MESH = pl.DeviceIdType.MESH
LOG2E = 1.4426950408889634
VMEM_BYTES = 62 << 20


class Sizes(NamedTuple):
    n_tensor: int
    n_context: int
    seqs: int
    half: int
    block: int
    tile: int
    rows: int
    seq_len: int
    width: int
    heads: int
    head_dim: int
    ff: int


def full_spec():
    return pl.BlockSpec(memory_space=pltpu.VMEM)


def any_spec():
    return pl.BlockSpec(memory_space=pl.ANY)


def nt_dot(a, b):
    return lax.dot_general(a, b, (((1,), (1,)), ((), ())), preferred_element_type=jnp.float32)


def tn_dot(a, b):
    return lax.dot_general(a, b, (((0,), (0,)), ((), ())), preferred_element_type=jnp.float32)


def nn_dot(a, b):
    return jnp.dot(a, b, preferred_element_type=jnp.float32)


class Place:
    def __init__(self, sz):
        t = lax.axis_index("tensor")
        self.sz = sz
        self.dp = lax.axis_index("dp")
        self.ctx = lax.axis_index("context")
        self.group = t // sz.half
        self.part = lax.rem(t, sz.half)

    def device(self, part, ctx):
        return (self.dp, self.group * self.sz.half + part, ctx)

    def ahead(self, q):
        return lax.rem(self.part + q, self.sz.half)

    def behind(self, q):
        return lax.rem(self.part + (self.sz.half - q), self.sz.half)

    def sibling(self):
        return self.device(self.part, 1 - self.ctx)

    def block(self, part, ctx, j):
        sz = self.sz
        first = ((part + j * sz.half) * sz.n_context + ctx) * sz.block
        return pl.ds(pl.multiple_of(first, sz.block), sz.block)

    def tile(self, q, j):
        sz = self.sz
        first = (self.ahead(q) + j * sz.half) * sz.tile
        return pl.ds(pl.multiple_of(first, sz.tile), sz.tile)

    def enter(self, others=(), more=0):
        barrier = pltpu.get_barrier_semaphore()
        for device in others:
            pl.semaphore_signal(barrier, inc=1, device_id=device, device_id_type=MESH)
        pl.semaphore_signal(
            barrier, inc=1, device_id=self.sibling(), device_id_type=MESH
        )
        for q in range(1, self.sz.half):
            pl.semaphore_signal(
                barrier,
                inc=1,
                device_id=self.device(self.ahead(q), self.ctx),
                device_id_type=MESH,
            )
        pl.semaphore_wait(barrier, self.sz.half + len(others) + more)


class Gather:
    @staticmethod
    def scratch(sz):
        kinds = 2 * sz.half - 1
        return [
            pltpu.SemaphoreType.DMA((kinds, sz.seqs)),
            pltpu.SemaphoreType.DMA((kinds, sz.seqs)),
        ]

    def __init__(self, place, ref, send, recv):
        self.place, self.ref, self.send, self.recv = place, ref, send, recv

    def copy(self, kind, j, rows):
        place, half = self.place, self.place.sz.half
        if 0 < kind < half:
            target = place.device(place.ahead(kind), place.ctx)
        else:
            target = place.sibling()
        return pltpu.make_async_remote_copy(
            src_ref=self.ref.at[rows],
            dst_ref=self.ref.at[rows],
            send_sem=self.send.at[kind, j],
            recv_sem=self.recv.at[kind, j],
            device_id=target,
            device_id_type=MESH,
        )

    def own(self, j):
        return self.place.block(self.place.part, self.place.ctx, j)

    def start(self, j):
        for q in range(1, self.place.sz.half):
            self.copy(q, j, self.own(j)).start()
        self.copy(0, j, self.own(j)).start()

    def wait_near(self, j):
        place = self.place
        self.copy(0, j, place.block(place.part, 1 - place.ctx, j)).wait_recv()

    def forward(self, q, j):
        place = self.place
        rows = place.block(place.behind(q), place.ctx, j)
        self.copy(q, j, rows).wait_recv()
        self.copy(place.sz.half - 1 + q, j, rows).start()

    def wait_far(self, q, j):
        place = self.place
        rows = place.block(place.behind(q), 1 - place.ctx, j)
        self.copy(place.sz.half - 1 + q, j, rows).wait_recv()

    def passed_on(self, j):
        place, half = self.place, self.place.sz.half
        for q in range(1, half):
            rows = place.block(place.behind(q), place.ctx, j)
            self.copy(half - 1 + q, j, rows).wait_send()

    def finish(self, forwards=True):
        for j in range(self.place.sz.seqs):
            for kind in range(self.place.sz.half):
                self.copy(kind, j, self.own(j)).wait_send()
            if forwards:
                self.passed_on(j)


class Scatter:
    @staticmethod
    def scratch(sz):
        kinds = 2 * sz.half - 1
        near = (sz.half, sz.seqs, sz.block, sz.width)
        far = (max(sz.half - 1, 1), sz.seqs, sz.block, sz.width)
        return [
            pltpu.VMEM((sz.tile, sz.width), jnp.float32),
            pltpu.VMEM(near, jnp.bfloat16),
            pltpu.VMEM(near, jnp.bfloat16),
            pltpu.VMEM(near, jnp.bfloat16),
            pltpu.VMEM(far, jnp.bfloat16),
            pltpu.VMEM(far, jnp.bfloat16),
            pltpu.SemaphoreType.DMA((kinds, sz.seqs)),
            pltpu.SemaphoreType.DMA((kinds, sz.seqs)),
        ]

    def __init__(self, place, part, mine, near_out, near_in, far_out, far_in, send, recv):
        self.place, self.part, self.mine = place, part, mine
        self.near_out, self.near_in = near_out, near_in
        self.far_out, self.far_in = far_out, far_in
        self.send, self.recv = send, recv

    def near(self, q, j):
        return pltpu.make_async_remote_copy(
            src_ref=self.near_out.at[q, j],
            dst_ref=self.near_in.at[q, j],
            send_sem=self.send.at[q, j],
            recv_sem=self.recv.at[q, j],
            device_id=self.place.sibling(),
            device_id_type=MESH,
        )

    def far(self, q, j):
        place = self.place
        return pltpu.make_async_remote_copy(
            src_ref=self.far_out.at[q - 1, j],
            dst_ref=self.far_in.at[q - 1, j],
            send_sem=self.send.at[place.sz.half - 1 + q, j],
            recv_sem=self.recv.at[place.sz.half - 1 + q, j],
            device_id=place.device(place.ahead(q), place.ctx),
            device_id_type=MESH,
        )

    def give(self, q, j):
        sz, ctx = self.place.sz, self.place.ctx
        mine = pl.ds(pl.multiple_of(ctx * sz.block, sz.block), sz.block)
        other = pl.ds(pl.multiple_of((1 - ctx) * sz.block, sz.block), sz.block)
        self.near_out[q, j] = self.part[other, :].astype(jnp.bfloat16)
        self.near(q, j).start()
        self.mine[q, j] = self.part[mine, :].astype(jnp.bfloat16)

    def onward(self, q, j):
        self.near(q, j).wait_recv()
        self.far_out[q - 1, j] = (
            self.mine[q, j].astype(jnp.float32) + self.near_in[q, j].astype(jnp.float32)
        ).astype(jnp.bfloat16)
        self.far(q, j).start()

    def total(self, j):
        self.near(0, j).wait_recv()
        total = self.mine[0, j].astype(jnp.float32) + self.near_in[0, j].astype(jnp.float32)
        for q in range(1, self.place.sz.half):
            self.far(q, j).wait_recv()
            total = total + self.far_in[q - 1, j].astype(jnp.float32)
        return total

    def finish(self):
        half = self.place.sz.half
        for j in range(self.place.sz.seqs):
            for q in range(half):
                self.near(q, j).wait_send()
            for q in range(1, half):
                self.far(q, j).wait_send()


def column_loads(blocks_ref, vmem_ref, sem):
    count, _, columns = blocks_ref.shape
    return [
        pltpu.make_async_copy(
            blocks_ref.at[b], vmem_ref.at[:, pl.ds(b * columns, columns)], sem.at[b]
        )
        for b in range(count)
    ]


def adapter_loads(blocks_ref, vmem_ref, sem):
    count, tops = sem.shape
    depth, columns = vmem_ref.shape[0] // tops, vmem_ref.shape[1] // count
    return [
        [
            pltpu.make_async_copy(
                blocks_ref.at[b, pl.ds(0, depth), pl.ds(n * columns, columns)],
                vmem_ref.at[pl.ds(b * depth, depth), pl.ds(n * columns, columns)],
                sem.at[n, b],
            )
            for b in range(tops)
        ]
        for n in range(count)
    ]


def rms_factor(rows):
    return lax.rsqrt(jnp.mean(rows * rows, axis=-1, keepdims=True) + norm_eps)


def turn(x, cos_t, sin_t):
    return x * cos_t + pltpu.roll(x, x.shape[-1] // 2, 1) * sin_t


def attn_kernel(sz, n_dp, keep, *refs):
    (latent, embed, gains, cos_t, sin_t, begin, adapter_hbm, qkv_hbm, out_hbm) = refs[:9]
    refs = refs[9:]
    extra_in, refs = refs[0], refs[1:]
    mixed = refs[0]
    refs = refs[1:]
    if keep:
        adapted_out, rows_out, q_out, k_out, v_out, head_out, lse_out, joined_out = refs[:8]
        refs = refs[8:]
    else:
        blocks_out, refs = refs[0], refs[1:]
    (wa, wqkv, wout, adapted, rows_s, q_s, k_s, v_s, head_s, lse_s) = refs[:10]
    load_a, load_qkv, load_out, keep_sem = refs[10:14]
    gather_refs = refs[14:16]
    scatter_refs = refs[16:24]
    if keep:
        joined_s, load_embed, x_send, x_recv = refs[24:]
    else:
        hop_send, hop_recv, own_sem = refs[24:]

    place = Place(sz)
    a_loads = adapter_loads(adapter_hbm, wa, load_a)
    qkv_load = pltpu.make_async_copy(qkv_hbm, wqkv, load_qkv)
    out_loads = column_loads(out_hbm, wout, load_out)
    for group in a_loads:
        for copy in group:
            copy.start()
    qkv_load.start()
    for copy in out_loads:
        copy.start()
    ring = Ring(place, n_dp)
    if not keep:
        others = [ring.device(1), ring.device(n_dp - 1)]
        ways = range(sz.n_context)

        def hop(way, s):
            offset = -s if way == 0 else s
            slot = blocks_out.at[ring.index(offset) * sz.n_context + way]
            return pltpu.make_async_remote_copy(
                src_ref=extra_in.at[way] if s == 0 else slot,
                dst_ref=slot,
                send_sem=hop_send.at[way, s],
                recv_sem=hop_recv.at[way, s],
                device_id=ring.device(1 if way == 0 else n_dp - 1),
                device_id_type=MESH,
            )

        def hopped(way, s):
            offset = -(s + 1) if way == 0 else s + 1
            slot = blocks_out.at[ring.index(offset) * sz.n_context + way]
            return pltpu.make_async_remote_copy(
                src_ref=slot,
                dst_ref=slot,
                send_sem=hop_send.at[way, s],
                recv_sem=hop_recv.at[way, s],
                device_id=ring.device(1),
                device_id_type=MESH,
            )

        own_blocks = [
            pltpu.make_async_copy(
                extra_in.at[way], blocks_out.at[place.dp * sz.n_context + way], own_sem.at[way]
            )
            for way in ways
        ]
        hops = list(range(n_dp - 1))

        def next_hop():
            if hops:
                s = hops.pop(0)
                for way in ways:
                    if s:
                        hopped(way, s - 1).wait_recv()
                    hop(way, s).start()

    if keep:
        t = lax.axis_index("tensor")
        embed_load = pltpu.make_async_copy(
            extra_in, joined_s.at[:, pl.ds(sz.width, sz.width)], load_embed
        )
        embed_load.start()
        plane = [(o, c) for o in range(n_dp) for c in range(2) if (o, c) != (0, 0)]

        def member(o, c):
            return (ring.index(o), t, place.ctx if c == 0 else 1 - place.ctx)

        def columns_to(o, c):
            to = member(o, c)
            depth = joined_out.shape[2]
            first = pl.multiple_of((to[0] * sz.n_context + to[2]) * depth, depth)
            return pltpu.make_async_remote_copy(
                src_ref=joined_s.at[:, pl.ds(first, depth)],
                dst_ref=joined_out.at[place.dp * sz.n_context + place.ctx],
                send_sem=x_send.at[o, c],
                recv_sem=x_recv.at[o, c],
                device_id=to,
                device_id_type=MESH,
            )

        def columns_from(o, c):
            ref = joined_out.at[
                ring.index(-o) * sz.n_context + (place.ctx if c == 0 else 1 - place.ctx)
            ]
            return pltpu.make_async_remote_copy(
                src_ref=ref,
                dst_ref=ref,
                send_sem=x_send.at[o, c],
                recv_sem=x_recv.at[o, c],
                device_id=place.sibling(),
                device_id_type=MESH,
            )

        others = [member(o, c) for o, c in plane if o]
    place.enter(others)
    if not keep:
        next_hop()
        for copy in own_blocks:
            copy.start()
    gather = Gather(place, rows_s, *gather_refs)
    scatter = Scatter(place, *scatter_refs)

    low = latent[...].astype(jnp.bfloat16)
    columns = sz.width // len(a_loads)
    square = None
    for n, group in enumerate(a_loads):
        for copy in group:
            copy.wait()
        cols = pl.ds(n * columns, columns)
        chunk = nn_dot(low, wa[:, cols]) + embed[:, cols]
        adapted[:, cols] = chunk
        here = jnp.sum(chunk * chunk, axis=-1, keepdims=True)
        square = here if square is None else square + here
    factor = lax.rsqrt(square / sz.width + norm_eps)
    for j in range(sz.seqs):
        span = slice(j * sz.block, (j + 1) * sz.block)
        normed = (adapted[span, :] * factor[span]) * gains[0:1, :]
        rows_s[gather.own(j), :] = normed.astype(jnp.bfloat16)
        gather.start(j)

    qkv_load.wait()
    pair = min(2, sz.heads)
    d = sz.head_dim

    def project(q, j):
        rows = place.tile(q, j)
        x = rows_s[rows, :]
        cos_here, sin_here = cos_t[rows, :], sin_t[rows, :]
        for h0 in range(0, sz.heads, pair):
            proj = nn_dot(x, wqkv[:, 3 * d * h0 : 3 * d * (h0 + pair)])
            for h in range(pair):
                at = 3 * d * h
                q_s[h0 + h, rows, :] = turn(proj[:, at : at + d], cos_here, sin_here).astype(
                    jnp.bfloat16
                )
                k_s[h0 + h, rows, :] = turn(
                    proj[:, at + d : at + 2 * d], cos_here, sin_here
                ).astype(jnp.bfloat16)
                v_s[h0 + h, rows, :] = proj[:, at + 2 * d : at + 3 * d].astype(jnp.bfloat16)

    def attend(q, j):
        rows = place.tile(q, j)
        first = (place.ahead(q) + j * sz.half) * sz.tile
        length = (j + 1) * sz.half * sz.tile
        start = begin[:, pl.ds(pl.multiple_of(first, sz.tile), sz.tile)]
        key_at = lax.broadcasted_iota(jnp.int32, (length, sz.tile), 0)
        query_at = first + lax.broadcasted_iota(jnp.int32, (1, sz.tile), 1)
        allowed = (key_at >= start) & (key_at <= query_at)

        def head(h, carry):
            scores = nt_dot(k_s[h, 0:length, :], q_s[h, rows, :])
            scores = jnp.where(allowed, scores * (LOG2E / math.sqrt(d)), masked_score)
            top = jnp.max(scores, axis=0, keepdims=True)
            weight = jnp.exp2(scores - top)
            total = jnp.sum(weight, axis=0, keepdims=True)
            mixed_t = tn_dot(v_s[h, 0:length, :], weight.astype(jnp.bfloat16))
            result = jnp.transpose(mixed_t / total)
            head_s[rows, pl.ds(pl.multiple_of(h * d, d), d)] = result.astype(jnp.bfloat16)
            if keep:
                lse_s[h, :, rows] = top + jnp.log2(total)
            return carry

        lax.fori_loop(0, sz.heads, head, 0)

    def give(q, j):
        rows = place.tile(q, j)
        scatter.part[...] = nn_dot(head_s[rows, :], wout[...])
        scatter.give(q, j)

    copies = []

    def save(src, dst):
        copy = pltpu.make_async_copy(src, dst, keep_sem.at[len(copies)])
        copy.start()
        copies.append(copy)

    if keep:
        save(adapted, adapted_out)
        joined_s[:, : sz.width] = low
        embed_load.wait()
        for o, c in plane:
            columns_to(o, c).start()
        mine = place.dp * sz.n_context + place.ctx
        depth = joined_out.shape[2]
        save(
            joined_s.at[:, pl.ds(pl.multiple_of(mine * depth, depth), depth)], joined_out.at[mine]
        )
    far = range(1, sz.half)
    for j in range(sz.seqs):
        gather.wait_near(j)
        project(0, j)
    for copy in out_loads:
        copy.wait()
    for j in range(sz.seqs):
        for q in far:
            gather.forward(q, j)
        for q in far:
            gather.wait_far(sz.half - q, j)
            project(q, j)
        for q in far:
            attend(q, j)
            give(q, j)
        if not keep:
            next_hop()
        attend(0, j)
        for q in far:
            scatter.onward(q, j)
        give(0, j)
    if keep:
        for src, dst in ((rows_s, rows_out), (q_s, q_out), (k_s, k_out), (v_s, v_out)):
            save(src, dst)
        save(head_s, head_out)
        save(lse_s, lse_out)
    gather.finish()
    for j in range(sz.seqs):
        span = slice(j * sz.block, (j + 1) * sz.block)
        mixed[span, :] = adapted[span, :] + scatter.total(j)
    scatter.finish()
    if keep:
        for o, c in plane:
            columns_from(o, c).wait_recv()
            columns_to(o, c).wait_send()
    else:
        while hops:
            next_hop()
        for way in ways:
            hopped(way, n_dp - 2).wait_recv()
            own_blocks[way].wait()
            for s in range(n_dp - 1):
                hop(way, s).wait_send()
    for copy in copies:
        copy.wait()


def run_attn(
    sz, n_dp, keep, latent, embed_part, gains, cos_t, sin_t, begin, adapter, qkv, out, extra
):
    f32, bf16 = jnp.float32, jnp.bfloat16
    heads_shape = (sz.heads, sz.seq_len, sz.head_dim)
    shape = jax.ShapeDtypeStruct
    outs = [shape((sz.rows, sz.width), f32)]
    if keep:
        outs += [
            shape((sz.rows, sz.width), f32),
            shape((sz.seq_len, sz.width), bf16),
            shape(heads_shape, bf16),
            shape(heads_shape, bf16),
            shape(heads_shape, bf16),
            shape((sz.seq_len, sz.heads * sz.head_dim), bf16),
            shape((sz.heads, 1, sz.seq_len), f32),
            shape((adapter.shape[0], sz.rows, 2 * sz.width // adapter.shape[0]), bf16),
        ]
    else:
        outs.append(shape((n_dp * sz.n_context,) + extra.shape[1:], bf16))
    scratch = [
        pltpu.VMEM((sz.width, sz.width), bf16),
        pltpu.VMEM(qkv.shape, bf16),
        pltpu.VMEM((sz.heads * sz.head_dim, sz.width), bf16),
        pltpu.VMEM((sz.rows, sz.width), f32),
        pltpu.VMEM((sz.seq_len, sz.width), bf16),
        pltpu.VMEM(heads_shape, bf16),
        pltpu.VMEM(heads_shape, bf16),
        pltpu.VMEM(heads_shape, bf16),
        pltpu.VMEM((sz.seq_len, sz.heads * sz.head_dim), bf16),
        pltpu.VMEM((sz.heads, 1, sz.seq_len), f32),
        pltpu.SemaphoreType.DMA((4, adapter.shape[0] // 2)),
        pltpu.SemaphoreType.DMA,
        pltpu.SemaphoreType.DMA((out.shape[0],)),
        pltpu.SemaphoreType.DMA((8,)),
    ]
    scratch += Gather.scratch(sz) + Scatter.scratch(sz)
    if keep:
        scratch += [
            pltpu.VMEM((sz.rows, 2 * sz.width), bf16),
            pltpu.SemaphoreType.DMA,
            pltpu.SemaphoreType.DMA((n_dp, 2)),
            pltpu.SemaphoreType.DMA((n_dp, 2)),
        ]
    else:
        scratch += [
            pltpu.SemaphoreType.DMA((sz.n_context, n_dp - 1)),
            pltpu.SemaphoreType.DMA((sz.n_context, n_dp - 1)),
            pltpu.SemaphoreType.DMA((sz.n_context,)),
        ]
    flops = 2 * sz.rows * sz.width * sz.width + 2 * sz.seq_len * sz.width * qkv.shape[1]
    return pl.pallas_call(
        partial(attn_kernel, sz, n_dp, keep),
        out_shape=outs,
        in_specs=[full_spec()] * 6 + [any_spec()] * 4,
        out_specs=[full_spec()] + [any_spec()] * (len(outs) - 1),
        scratch_shapes=scratch,
        compiler_params=pltpu.CompilerParams(
            collective_id=2 if keep else 9, has_side_effects=True, vmem_limit_bytes=VMEM_BYTES
        ),
        cost_estimate=pl.CostEstimate(
            flops=flops, bytes_accessed=20 << 20, transcendentals=0
        ),
        name="attn_keep" if keep else "attn_round",
    )(latent, embed_part, gains, cos_t, sin_t, begin, adapter, qkv, out, extra)


def ffn_kernel(sz, keep, *refs):
    (mixed, latent, active, gains, gate_hbm, up_hbm, down_hbm, result) = refs[:8]
    refs = refs[8:]
    if keep:
        rows_out, gate_out, up_out, hidden_out = refs[:4]
        refs = refs[4:]
    wg, wu, wd, rows_s = refs[:4]
    refs = refs[4:]
    if keep:
        gate_s, up_s, hidden_s = refs[:3]
        refs = refs[3:]
    load_gu, load_down, keep_sem = refs[:3]
    gather_refs = refs[3:5]
    scatter_refs = refs[5:]

    place = Place(sz)
    gate_load = pltpu.make_async_copy(gate_hbm, wg, load_gu.at[0])
    up_load = pltpu.make_async_copy(up_hbm, wu, load_gu.at[1])
    down_loads = column_loads(down_hbm, wd, load_down)
    gate_load.start()
    up_load.start()
    for copy in down_loads:
        copy.start()
    place.enter()
    gather = Gather(place, rows_s, *gather_refs)
    scatter = Scatter(place, *scatter_refs)
    for j in range(sz.seqs):
        span = slice(j * sz.block, (j + 1) * sz.block)
        rows = mixed[span, :]
        normed = (rows * rms_factor(rows)) * gains[1:2, :]
        rows_s[gather.own(j), :] = normed.astype(jnp.bfloat16)
        gather.start(j)
    gate_load.wait()
    up_load.wait()
    for copy in down_loads:
        copy.wait()

    copies = []

    def save(src, dst):
        copy = pltpu.make_async_copy(src, dst, keep_sem.at[len(copies)])
        copy.start()
        copies.append(copy)

    def work(q, j):
        rows = place.tile(q, j)
        x = rows_s[rows, :]
        gate = nn_dot(x, wg[...])
        up = nn_dot(x, wu[...])
        hidden = (gate / (1.0 + jnp.exp(-gate)) * up).astype(jnp.bfloat16)
        if keep:
            gate_s[rows, :] = gate.astype(jnp.bfloat16)
            up_s[rows, :] = up.astype(jnp.bfloat16)
            hidden_s[rows, :] = hidden
        scatter.part[...] = nn_dot(hidden, wd[...])
        scatter.give(q, j)

    far = range(1, sz.half)
    for j in range(sz.seqs):
        gather.wait_near(j)
        work(0, j)
    for j in range(sz.seqs):
        for q in far:
            gather.forward(q, j)
        for q in far:
            gather.wait_far(sz.half - q, j)
            work(q, j)
        for q in far:
            scatter.onward(q, j)
    if keep:
        save(rows_s, rows_out)
        save(gate_s, gate_out)
        save(up_s, up_out)
        save(hidden_s, hidden_out)
    gather.finish()
    for j in range(sz.seqs):
        span = slice(j * sz.block, (j + 1) * sz.block)
        total = mixed[span, :] + scatter.total(j)
        if not keep:
            total = jnp.where(active[...] > 0, total, latent[span, :])
        result[span, :] = total
    scatter.finish()
    for copy in copies:
        copy.wait()


def run_ffn(sz, keep, mixed, latent, active, gains, gate, up, down):
    f32, bf16 = jnp.float32, jnp.bfloat16
    shape = jax.ShapeDtypeStruct
    outs = [shape((sz.rows, sz.width), f32)]
    if keep:
        outs += [
            shape((sz.seq_len, sz.width), bf16),
            shape((sz.seq_len, sz.ff), bf16),
            shape((sz.seq_len, sz.ff), bf16),
            shape((sz.seq_len, sz.ff), bf16),
        ]
    scratch = [
        pltpu.VMEM(gate.shape, bf16),
        pltpu.VMEM(up.shape, bf16),
        pltpu.VMEM((sz.ff, sz.width), bf16),
        pltpu.VMEM((sz.seq_len, sz.width), bf16),
    ]
    if keep:
        scratch += [pltpu.VMEM((sz.seq_len, sz.ff), bf16)] * 3
    scratch += [
        pltpu.SemaphoreType.DMA((2,)),
        pltpu.SemaphoreType.DMA((down.shape[0],)),
        pltpu.SemaphoreType.DMA((4,)),
    ]
    scratch += Gather.scratch(sz) + Scatter.scratch(sz)
    return pl.pallas_call(
        partial(ffn_kernel, sz, keep),
        out_shape=outs,
        in_specs=[full_spec()] * 4 + [any_spec()] * 3,
        out_specs=[full_spec()] + [any_spec()] * (len(outs) - 1),
        scratch_shapes=scratch,
        compiler_params=pltpu.CompilerParams(
            collective_id=4 if keep else 3, has_side_effects=True, vmem_limit_bytes=VMEM_BYTES
        ),
        cost_estimate=pl.CostEstimate(
            flops=6 * sz.seq_len * sz.width * sz.ff, bytes_accessed=20 << 20, transcendentals=0
        ),
        name="ffn_keep" if keep else "ffn_round",
    )(mixed, latent, active, gains, gate, up, down)


def rounds_kernel(sz, count, *refs):
    (active, gains, cos_t, sin_t, begin) = refs[:5]
    (latent_hbm, embed_hbm, adapter_hbm, qkv_hbm, out_hbm, gate_hbm, up_hbm, down_hbm) = refs[5:13]
    result = refs[13]
    (wide, narrow, wg, wu, wd, embed, mixed, rows_s, q_s, k_s, v_s, head_s) = refs[14:26]
    load_rows, load_a, load_qkv, load_out, load_gu, load_down = refs[26:32]
    gather_refs, again_refs, scatter_refs = refs[32:34], refs[34:36], refs[36:44]
    columns = sz.width // 4
    depth_out = sz.heads * sz.head_dim

    place = Place(sz)
    row_loads = [
        pltpu.make_async_copy(latent_hbm, result, load_rows.at[0]),
        pltpu.make_async_copy(embed_hbm, embed, load_rows.at[1]),
    ]

    def adapter_columns(n):
        return wide.at[:, pl.ds(n * columns, columns)] if n < 3 else narrow

    tops = load_a.shape[1]
    depth = sz.width // tops
    a_loads = [
        [
            pltpu.make_async_copy(
                adapter_hbm.at[b, pl.ds(0, depth), pl.ds(n * columns, columns)],
                adapter_columns(n).at[pl.ds(b * depth, depth)],
                load_a.at[n, b],
            )
            for b in range(tops)
        ]
        for n in range(4)
    ]
    wqkv = wide.at[:, pl.ds(0, qkv_hbm.shape[1])]
    qkv_load = pltpu.make_async_copy(qkv_hbm, wqkv, load_qkv)
    out_loads = []
    for b in range(out_hbm.shape[0]):
        size = min(out_hbm.shape[2], columns)
        for at in range(0, out_hbm.shape[2], size):
            n, to = divmod(b * out_hbm.shape[2] + at, columns)
            out_loads.append(
                pltpu.make_async_copy(
                    out_hbm.at[b, :, pl.ds(at, size)],
                    narrow.at[pl.ds(n * depth_out, depth_out), pl.ds(to, size)],
                    load_out.at[len(out_loads)],
                )
            )
    ffn_loads = [
        pltpu.make_async_copy(gate_hbm, wg, load_gu.at[0]),
        pltpu.make_async_copy(up_hbm, wu, load_gu.at[1]),
    ] + column_loads(down_hbm, wd, load_down)

    def start_adapter():
        for group in a_loads:
            for copy in group:
                copy.start()

    def start_heads():
        qkv_load.start()
        for copy in out_loads:
            copy.start()

    for copy in row_loads:
        copy.start()
    start_adapter()
    place.enter()
    gather = Gather(place, rows_s, *gather_refs)
    again = Gather(place, rows_s, *again_refs)
    scatter = Scatter(place, *scatter_refs)
    for copy in row_loads:
        copy.wait()

    def spans(j):
        return slice(j * sz.block, (j + 1) * sz.block)

    def open_block(j):
        low = result[spans(j), :].astype(jnp.bfloat16)
        square = None
        for n, group in enumerate(a_loads):
            if j == 0:
                for copy in group:
                    copy.wait()
            cols = slice(n * columns, (n + 1) * columns)
            chunk = nn_dot(low, adapter_columns(n)[...]) + embed[spans(j), cols]
            mixed[spans(j), cols] = chunk
            here = jnp.sum(chunk * chunk, axis=-1, keepdims=True)
            square = here if square is None else square + here
        factor = lax.rsqrt(square / sz.width + norm_eps)
        normed = (mixed[spans(j), :] * factor) * gains[0:1, :]
        rows_s[gather.own(j), :] = normed.astype(jnp.bfloat16)
        gather.start(j)

    for j in range(sz.seqs):
        open_block(j)
    start_heads()
    for copy in ffn_loads:
        copy.start()
    pair = min(2, sz.heads)
    d = sz.head_dim

    def project(q, j):
        rows = place.tile(q, j)
        x = rows_s[rows, :]
        cos_here, sin_here = cos_t[rows, :], sin_t[rows, :]
        for h0 in range(0, sz.heads, pair):
            proj = nn_dot(x, wqkv[:, 3 * d * h0 : 3 * d * (h0 + pair)])
            for h in range(pair):
                at = 3 * d * h
                q_s[h0 + h, rows, :] = turn(proj[:, at : at + d], cos_here, sin_here).astype(
                    jnp.bfloat16
                )
                k_s[h0 + h, rows, :] = turn(
                    proj[:, at + d : at + 2 * d], cos_here, sin_here
                ).astype(jnp.bfloat16)
                v_s[h0 + h, rows, :] = proj[:, at + 2 * d : at + 3 * d].astype(jnp.bfloat16)

    def attend(q, j):
        rows = place.tile(q, j)
        first = (place.ahead(q) + j * sz.half) * sz.tile
        length = (j + 1) * sz.half * sz.tile
        start = begin[:, pl.ds(pl.multiple_of(first, sz.tile), sz.tile)]
        key_at = lax.broadcasted_iota(jnp.int32, (length, sz.tile), 0)
        query_at = first + lax.broadcasted_iota(jnp.int32, (1, sz.tile), 1)
        allowed = (key_at >= start) & (key_at <= query_at)

        def head(h, carry):
            scores = nt_dot(k_s[h, 0:length, :], q_s[h, rows, :])
            scores = jnp.where(allowed, scores * (LOG2E / math.sqrt(d)), masked_score)
            top = jnp.max(scores, axis=0, keepdims=True)
            weight = jnp.exp2(scores - top)
            total = jnp.sum(weight, axis=0, keepdims=True)
            mixed_t = tn_dot(v_s[h, 0:length, :], weight.astype(jnp.bfloat16))
            result = jnp.transpose(mixed_t / total)
            head_s[rows, pl.ds(pl.multiple_of(h * d, d), d)] = result.astype(jnp.bfloat16)
            return carry

        lax.fori_loop(0, sz.heads, head, 0)

    def give(q, j):
        rows = place.tile(q, j)
        for n in range(4):
            scatter.part[:, n * columns : (n + 1) * columns] = nn_dot(
                head_s[rows, :], narrow[n * depth_out : (n + 1) * depth_out, :]
            )
        scatter.give(q, j)

    def work(q, j):
        x = rows_s[place.tile(q, j), :]
        gate = nn_dot(x, wg[...])
        up = nn_dot(x, wu[...])
        hidden = (gate / (1.0 + jnp.exp(-gate)) * up).astype(jnp.bfloat16)
        scatter.part[...] = nn_dot(hidden, wd[...])
        scatter.give(q, j)

    far = range(1, sz.half)

    def one_round(r, carry):
        more = r + 1 < count
        qkv_load.wait()
        for j in range(sz.seqs):
            gather.wait_near(j)
            project(0, j)
        for copy in out_loads:
            copy.wait()
        for j in range(sz.seqs):
            for q in far:
                gather.forward(q, j)
            for q in far:
                gather.wait_far(sz.half - q, j)
                project(q, j)
            for q in far:
                attend(q, j)
                give(q, j)
            attend(0, j)
            gather.passed_on(j)
            for q in far:
                scatter.onward(q, j)
            give(0, j)
        gather.finish(forwards=False)
        pl.when(more)(start_adapter)
        for j in range(sz.seqs):
            rows = mixed[spans(j), :] + scatter.total(j)
            mixed[spans(j), :] = rows
            normed = (rows * rms_factor(rows)) * gains[1:2, :]
            rows_s[again.own(j), :] = normed.astype(jnp.bfloat16)
            again.start(j)
        scatter.finish()

        def first_loads():
            for copy in ffn_loads:
                copy.wait()

        pl.when(r == 0)(first_loads)
        for j in range(sz.seqs):
            again.wait_near(j)
            work(0, j)
        for j in range(sz.seqs):
            for q in far:
                again.forward(q, j)
            for q in far:
                again.wait_far(sz.half - q, j)
                work(q, j)
            again.passed_on(j)
            for q in far:
                scatter.onward(q, j)
        again.finish(forwards=False)
        on = active[pl.ds(r, 1), :] > 0
        for j in range(sz.seqs):
            total = mixed[spans(j), :] + scatter.total(j)
            result[spans(j), :] = jnp.where(on, total, result[spans(j), :])
            pl.when(more)(lambda j=j: open_block(j))
        pl.when(more)(start_heads)
        scatter.finish()
        return carry

    lax.fori_loop(0, count, one_round, 0)


def run_rounds(sz, latent, active, gains, cos_t, sin_t, begin, embed, adapter, qkv, out, gate, up, down):
    f32, bf16, dma = jnp.float32, jnp.bfloat16, pltpu.SemaphoreType.DMA
    heads_shape = (sz.heads, sz.seq_len, sz.head_dim)
    return pl.pallas_call(
        partial(rounds_kernel, sz, active.shape[0]),
        out_shape=jax.ShapeDtypeStruct((sz.rows, sz.width), f32),
        in_specs=[full_spec()] * 5 + [any_spec()] * 8,
        out_specs=full_spec(),
        scratch_shapes=[
            pltpu.VMEM((sz.width, max(3 * sz.width // 4, qkv.shape[1])), bf16),
            pltpu.VMEM((sz.width, sz.width // 4), bf16),
            pltpu.VMEM(gate.shape, bf16),
            pltpu.VMEM(up.shape, bf16),
            pltpu.VMEM((sz.ff, sz.width), bf16),
            pltpu.VMEM((sz.rows, sz.width), f32),
            pltpu.VMEM((sz.rows, sz.width), f32),
            pltpu.VMEM((sz.seq_len, sz.width), bf16),
            pltpu.VMEM(heads_shape, bf16),
            pltpu.VMEM(heads_shape, bf16),
            pltpu.VMEM(heads_shape, bf16),
            pltpu.VMEM((sz.seq_len, sz.heads * sz.head_dim), bf16),
            dma((2,)),
            dma((4, adapter.shape[0] // 2)),
            dma,
            dma((max(4, out.shape[0]),)),
            dma((2,)),
            dma((down.shape[0],)),
        ]
        + Gather.scratch(sz)
        + Gather.scratch(sz)
        + Scatter.scratch(sz),
        compiler_params=pltpu.CompilerParams(
            collective_id=1, has_side_effects=True, vmem_limit_bytes=VMEM_BYTES
        ),
        cost_estimate=pl.CostEstimate(
            flops=24 * sz.seq_len * sz.width * sz.ff, bytes_accessed=80 << 20, transcendentals=0
        ),
        name="rounds",
    )(active, gains, cos_t, sin_t, begin, latent, embed, adapter, qkv, out, gate, up, down)


def other_group(place):
    return (place.dp, (1 - place.group) * place.sz.half + place.part, place.ctx)


class Ring:
    def __init__(self, place, n_dp):
        self.place, self.count = place, n_dp
        self.at = self.swap(place.dp)

    def swap(self, i):
        if self.count != 4:
            return i
        x, y = lax.rem(i, 2), i // 2
        return 2 * y + x + y - 2 * x * y

    def index(self, offset):
        return self.swap(lax.rem(self.at + offset + 2 * self.count, self.count))

    def device(self, offset):
        return (self.index(offset), lax.axis_index("tensor"), self.place.ctx)


def weights_kernel(sz, n_dp, *refs):
    count = 5
    adapter_in, blocks_in = refs[0], refs[1 : 1 + count]
    rows_in, refs = refs[1 + count : 4 + count], refs[4 + count :]
    adapter_out, blocks_out = refs[0], refs[1 : 1 + count]
    embed_out, cot_out, cot_all, embed_part, state_out = refs[1 + count : 6 + count]
    refs = refs[6 + count :]
    (move_send, move_recv, ring_send, ring_recv, a_send, a_recv, x_send, x_recv, own_sem) = refs[:9]
    embed_s, state_s, weight_s, swap_send, swap_recv, keep_sem, weight_sem = refs[9:16]
    gather_refs = refs[16:]
    place = Place(sz)
    ring = Ring(place, n_dp)
    t = lax.axis_index("tensor")
    ctx, part, half, n_c = place.ctx, place.part, sz.half, sz.n_context
    role = part * n_c + ctx
    at_home = role == t
    steps = n_dp - 1
    ahead = 1 - 2 * ctx

    def holder(g):
        return (place.dp, g * half + t // n_c, lax.rem(t, n_c))

    barrier = pltpu.get_barrier_semaphore()

    def greet(device):
        pl.semaphore_signal(barrier, inc=1, device_id=device, device_id_type=MESH)

    greet(ring.device(1))
    greet(ring.device(n_dp - 1))
    greet(place.sibling())
    for q in range(1, half):
        greet(place.device(place.ahead(q), ctx))
    for c in range(n_c):
        pl.when(jnp.logical_not(at_home & (ctx == c)))(
            lambda c=c: greet((place.dp, role, c))
        )
    other = other_group(place)
    greet(other)
    waits = 3 + half + sz.seqs - jnp.where(at_home, 1, 0)
    pl.semaphore_wait(barrier, waits)

    own_at = pl.ds(pl.multiple_of(place.group * sz.block, sz.block), sz.block)
    other_at = pl.ds(pl.multiple_of((1 - place.group) * sz.block, sz.block), sz.block)
    rows_to = (embed_s, state_s, cot_out)

    def swap(i):
        return pltpu.make_async_remote_copy(
            src_ref=rows_in[i].at[1 - place.group],
            dst_ref=rows_to[i].at[own_at],
            send_sem=swap_send.at[i],
            recv_sem=swap_recv.at[i],
            device_id=other,
            device_id_type=MESH,
        )

    def swapped(i):
        ref = rows_to[i].at[other_at]
        return pltpu.make_async_remote_copy(
            src_ref=ref,
            dst_ref=ref,
            send_sem=swap_send.at[i],
            recv_sem=swap_recv.at[i],
            device_id=other,
            device_id_type=MESH,
        )

    def keep(i):
        return pltpu.make_async_copy(
            rows_in[i].at[place.group], rows_to[i].at[own_at], keep_sem.at[i]
        )

    for i in range(3):
        keep(i).start()
    gather = Gather(place, cot_all, *gather_refs)

    def own_rows_of(j):
        return pltpu.make_async_copy(
            cot_out.at[pl.ds(j * sz.block, sz.block)], cot_all.at[gather.own(j)], keep_sem.at[3 + j]
        )

    rings = count - 1

    def landing(w, c):
        return c if w == rings else place.dp * n_c + c

    def move(w, g):
        slot = landing(w, ctx)
        return pltpu.make_async_remote_copy(
            src_ref=blocks_in[w],
            dst_ref=blocks_out[w].at[slot],
            send_sem=move_send.at[w, g],
            recv_sem=move_recv.at[w, ctx],
            device_id=holder(g),
            device_id_type=MESH,
        )

    def stay(w):
        return pltpu.make_async_copy(
            blocks_in[w], blocks_out[w].at[landing(w, ctx)], own_sem.at[w]
        )

    def moved(w, c):
        slot = landing(w, c)
        arrival = pltpu.make_async_remote_copy(
            src_ref=blocks_in[w],
            dst_ref=blocks_out[w].at[slot],
            send_sem=move_send.at[w, 0],
            recv_sem=move_recv.at[w, c],
            device_id=place.sibling(),
            device_id_type=MESH,
        )
        here = at_home & (ctx == c)
        pl.when(here)(lambda: stay(w).wait())
        pl.when(jnp.logical_not(here))(lambda: arrival.wait_recv())

    def adapter_rows(offset, c):
        return adapter_out.at[ring.index(offset) * n_c + c]

    def around(s):
        rows = adapter_rows(-ahead * s, ctx)
        return pltpu.make_async_remote_copy(
            src_ref=adapter_in if s == 0 else rows,
            dst_ref=rows,
            send_sem=a_send.at[s],
            recv_sem=a_recv.at[s],
            device_id=ring.device(ahead),
            device_id_type=MESH,
        )

    def across(s):
        rows = adapter_rows(-ahead * s, ctx)
        return pltpu.make_async_remote_copy(
            src_ref=adapter_in if s == 0 else rows,
            dst_ref=rows,
            send_sem=x_send.at[s],
            recv_sem=x_recv.at[s],
            device_id=place.sibling(),
            device_id_type=MESH,
        )

    def crossed(s):
        rows = adapter_rows(ahead * s, 1 - ctx)
        return pltpu.make_async_remote_copy(
            src_ref=rows,
            dst_ref=rows,
            send_sem=x_send.at[s],
            recv_sem=x_recv.at[s],
            device_id=place.sibling(),
            device_id_type=MESH,
        )

    def hop(w, way, s):
        offset = -s if way == 0 else s
        rows = blocks_out[w].at[ring.index(offset) * n_c + way]
        return pltpu.make_async_remote_copy(
            src_ref=rows,
            dst_ref=rows,
            send_sem=ring_send.at[w, way, s],
            recv_sem=ring_recv.at[w, way, s],
            device_id=ring.device(1 if way == 0 else n_dp - 1),
            device_id_type=MESH,
        )

    def hopped(w, way, s):
        offset = -(s + 1) if way == 0 else s + 1
        rows = blocks_out[w].at[ring.index(offset) * n_c + way]
        return pltpu.make_async_remote_copy(
            src_ref=rows,
            dst_ref=rows,
            send_sem=ring_send.at[w, way, s],
            recv_sem=ring_recv.at[w, way, s],
            device_id=ring.device(1),
            device_id_type=MESH,
        )

    around(0).start()
    own = pltpu.make_async_copy(adapter_in, adapter_rows(0, ctx), own_sem.at[count])
    own.start()

    def start_move(w):
        for g in range(sz.seqs):
            here = at_home & (place.group == g)
            pl.when(jnp.logical_not(here))(lambda w=w, g=g: move(w, g).start())
        pl.when(at_home)(lambda w=w: stay(w).start())

    start_move(0)
    start_move(1)
    across(0).start()

    def adapter_step(s):
        rows = adapter_rows(-ahead * (s + 1), ctx)
        arrival = pltpu.make_async_remote_copy(
            src_ref=rows,
            dst_ref=rows,
            send_sem=a_send.at[s],
            recv_sem=a_recv.at[s],
            device_id=ring.device(1),
            device_id_type=MESH,
        )
        arrival.wait_recv()
        if s + 1 < steps:
            around(s + 1).start()
        across(s + 1).start()

    embed_save = pltpu.make_async_copy(embed_s, embed_out, keep_sem.at[3 + sz.seqs])
    todo = []
    for k in range(rings + steps):
        for s in range(min(k, steps - 1), -1, -1):
            w = k - s
            if w < rings:
                todo.append((w, s))
    done = 0
    for w, s in todo:
        for way in range(n_c):
            if s == 0:
                moved(w, way)
            else:
                hopped(w, way, s - 1).wait_recv()
            hop(w, way, s).start()
        if s == 0 and w + 2 < rings:
            start_move(w + 2)
        if s == 0 and w == rings - 2:
            for i in range(3):
                swap(i).start()
        if s == 0 and w == rings - 1:
            start_move(rings)
        if done < steps:
            adapter_step(done)
        if s == min(1, steps - 1) and w == rings - 1:
            for i in range(3):
                keep(i).wait()
                swapped(i).wait_recv()
            for j in range(sz.seqs):
                own_rows_of(j).start()
            embed_save.start()
            for j in range(sz.seqs):
                own_rows_of(j).wait()
                gather.start(j)
            state_out[...] = state_s[...].astype(jnp.float32)
        done += 1
    for s in range(done, steps):
        adapter_step(s)
    for j in range(sz.seqs):
        gather.wait_near(j)
        for q in range(1, half):
            gather.forward(q, j)
    for s in range(n_dp):
        crossed(s).wait_recv()
    own.wait()
    slots, depth = adapter_out.shape[0], weight_s.shape[1]
    loads = [
        pltpu.make_async_copy(
            adapter_out.at[slots // 2 + b, pl.ds(0, depth)], weight_s.at[b % 2], weight_sem.at[b % 2]
        )
        for b in range(slots // 2)
    ]
    loads[0].start()
    for b, copy in enumerate(loads):
        if b + 1 < len(loads):
            loads[b + 1].start()
        copy.wait()
        part_here = nn_dot(embed_s[:, b * depth : (b + 1) * depth], weight_s[b % 2])
        if b:
            embed_part[...] += part_here
        else:
            embed_part[...] = part_here
    for way in range(n_c):
        for w in range(rings):
            hopped(w, way, steps - 1).wait_recv()
        moved(rings, way)
    for j in range(sz.seqs):
        for q in range(1, half):
            gather.wait_far(q, j)
    gather.finish()
    embed_save.wait()
    for i in range(3):
        swap(i).wait_send()
    for w in range(count):
        for g in range(sz.seqs):
            here = at_home & (place.group == g)
            pl.when(jnp.logical_not(here))(lambda w=w, g=g: move(w, g).wait_send())
        for way in range(n_c if w < rings else 0):
            for s in range(steps):
                hop(w, way, s).wait_send()
    for s in range(steps):
        around(s).wait_send()
    for s in range(n_dp):
        across(s).wait_send()


def run_weights(sz, n_dp, adapter, adapter_block, blocks, rows):
    bf16, f32 = jnp.bfloat16, jnp.float32
    slots = n_dp * sz.n_context
    outs = [jax.ShapeDtypeStruct((slots,) + a.shape, bf16) for a in [adapter] + blocks[:-1]]
    outs.append(jax.ShapeDtypeStruct((sz.n_context,) + blocks[-1].shape, bf16))
    outs += [
        jax.ShapeDtypeStruct((sz.rows, sz.width), bf16),
        jax.ShapeDtypeStruct((sz.rows, sz.width), bf16),
        jax.ShapeDtypeStruct((sz.seq_len, sz.width), bf16),
        jax.ShapeDtypeStruct((sz.rows, sz.width), f32),
        jax.ShapeDtypeStruct((sz.rows, sz.width), f32),
    ]
    count, steps, dma = len(blocks), n_dp - 1, pltpu.SemaphoreType.DMA
    return pl.pallas_call(
        partial(weights_kernel, sz, n_dp),
        out_shape=outs,
        in_specs=[any_spec()] * (4 + count),
        out_specs=[any_spec()] * (4 + count) + [full_spec()] * 2,
        scratch_shapes=[
            dma((count, sz.seqs)),
            dma((count, sz.n_context)),
            dma((count, sz.n_context, steps)),
            dma((count, sz.n_context, steps)),
            dma((steps,)),
            dma((steps,)),
            dma((n_dp,)),
            dma((n_dp,)),
            dma((count + 1,)),
            pltpu.VMEM((sz.rows, sz.width), bf16),
            pltpu.VMEM((sz.rows, sz.width), bf16),
            pltpu.VMEM((2, adapter_block, sz.width), bf16),
            dma((3,)),
            dma((3,)),
            dma((4 + sz.seqs,)),
            dma((2,)),
        ]
        + Gather.scratch(sz),
        compiler_params=pltpu.CompilerParams(
            collective_id=5, has_side_effects=True, vmem_limit_bytes=VMEM_BYTES
        ),
        name="weights",
    )(adapter, *blocks, *rows)


def norm_back(grad, rows, factor, gain):
    unit = rows * factor
    weighted = grad * gain
    inner = jnp.mean(weighted * unit, axis=-1, keepdims=True)
    return factor * (weighted - unit * inner), jnp.sum(grad * unit, axis=0, keepdims=True)


class GradRing:
    @staticmethod
    def scratch(sz, n_dp, tasks, wide, own_rows=None):
        slots, ways, dma = n_dp * sz.n_context, sz.n_context, pltpu.SemaphoreType.DMA
        depth, bf16, count, last = sz.width // slots, jnp.bfloat16, len(wide), n_dp - 1
        own_rows = [True] * count if own_rows is None else own_rows
        hops = [[s for w, s in tasks if w == i] for i in range(count)]
        return (
            [pltpu.VMEM((sz.seq_len, n), bf16) for n, own in zip(wide, own_rows) if own]
            + [pltpu.VMEM((ways, depth, n) if 0 in h else (ways, 16, 128), bf16) for n, h in zip(wide, hops)]
            + [pltpu.VMEM((ways, min(max(h) + 1, last), depth, n), bf16) for n, h in zip(wide, hops)]
            + [
                pltpu.VMEM((2, ways, sz.seq_len, depth), bf16),
                dma((count,)),
                dma((2, ways)),
                dma((count, ways, last)),
                dma((count, ways, last)),
                dma((ways,)),
            ]
        )

    @staticmethod
    def size(wide, own_rows=None):
        return 2 * len(wide) + (len(wide) if own_rows is None else sum(own_rows)) + 6

    @staticmethod
    def all_tasks(n_dp, count):
        return [
            (k - s, s)
            for k in range(count + n_dp)
            for s in range(min(k, n_dp - 1), -1, -1)
            if k - s < count
        ]

    def __init__(self, sz, place, ring, tasks, xs, ys, refs, rows=None, given=None):
        count, refs = len(xs), list(refs)
        self.sz, self.place, self.ring, self.xs, self.count = sz, place, ring, xs, count
        self.tasks = tasks
        self.ys = [refs.pop(0) if ys[w] is not None else rows[w] for w in range(count)]
        self.first, self.held = refs[:count], refs[count : 2 * count]
        self.x_s, self.load_y, self.load_x, self.send, self.recv, load_given = refs[2 * count :]
        self.y_loads = [
            pltpu.make_async_copy(ys[w], self.ys[w], self.load_y.at[w])
            for w in range(count)
            if ys[w] is not None
        ]
        self.unread = {w: self.y_loads[i] for i, w in enumerate(
            w for w in range(count) if ys[w] is not None
        )}
        self.given = []
        if given is not None:
            self.given = [
                pltpu.make_async_copy(
                    given.at[way], self.held[0].at[way, tasks[0][1] - 1], load_given.at[way]
                )
                for way in range(sz.n_context)
            ]
        self.done = 0

    def start(self):
        for copy in self.y_loads + self.given:
            copy.start()
        for way in range(self.sz.n_context):
            self.x_load(0, way).start()

    def slot(self, way, s):
        return self.ring.index(-(s + 1) if way == 0 else s + 1) * self.sz.n_context + way

    def x_load(self, k, way):
        w, s = self.tasks[k]
        depth = self.x_s.shape[3]
        if self.xs[w].shape[0] == 1:
            at = pl.multiple_of(self.slot(way, s) * depth, depth)
            src = self.xs[w].at[0, :, pl.ds(at, depth)]
        else:
            src = self.xs[w].at[self.slot(way, s)]
        return pltpu.make_async_copy(src, self.x_s.at[k % 2, way], self.load_x.at[k % 2, way])

    def source(self, w, way, s):
        return self.first[w].at[way] if s == 0 else self.held[w].at[way, s - 1]

    def hop(self, w, way, s):
        return pltpu.make_async_remote_copy(
            src_ref=self.source(w, way, s),
            dst_ref=self.held[w].at[way, s],
            send_sem=self.send.at[w, way, s],
            recv_sem=self.recv.at[w, way, s],
            device_id=self.ring.device(1 if way == 0 else self.ring.count - 1),
            device_id_type=MESH,
        )

    def result(self, w, way):
        return self.source(w, way, self.ring.count - 1)

    def step(self):
        k = self.done
        self.done += 1
        w, s = self.tasks[k]
        ways = range(self.sz.n_context)
        if k + 1 < len(self.tasks):
            for way in ways:
                self.x_load(k + 1, way).start()
        if w in self.unread:
            self.unread.pop(w).wait()
        for way in ways:
            self.x_load(k, way).wait()
            value = tn_dot(self.x_s[k % 2, way], self.ys[w][...])
            if k == 0 and self.given:
                self.given[way].wait()
            elif s:
                self.hop(w, way, s - 1).wait_recv()
            if s:
                value = value + self.held[w][way, s - 1].astype(jnp.float32)
            ref = self.source(w, way, s)
            ref[...] = value.astype(jnp.bfloat16)
            if s < self.ring.count - 1:
                self.hop(w, way, s).start()
        return w, s == self.ring.count - 1

    def left(self):
        return len(self.tasks) - self.done

    def finish(self):
        for w, s in self.tasks:
            if s < self.ring.count - 1:
                for way in range(self.sz.n_context):
                    self.hop(w, way, s).wait_send()


class Deliver:
    @staticmethod
    def scratch(sz, n_dp, wide):
        depth, count, dma = sz.width // (n_dp * sz.n_context), len(wide), pltpu.SemaphoreType.DMA
        return [pltpu.VMEM((sz.seqs, depth, n), jnp.bfloat16) for n in wide] + [
            dma((count, sz.n_context)),
            dma((count, sz.seqs)),
            dma((count,)),
        ]

    def __init__(self, sz, place, refs):
        self.sz, self.place = sz, place
        self.landed = refs[:-3]
        self.send, self.recv, self.own = refs[-3:]
        self.count = len(self.landed)
        self.t = lax.axis_index("tensor")
        self.role = place.part * sz.n_context + place.ctx
        self.at_home = self.role == self.t
        self.sources = [None] * self.count

    def greet(self):
        sz, place = self.sz, self.place
        barrier = pltpu.get_barrier_semaphore()
        for g in range(sz.seqs):
            holder = (place.dp, g * sz.half + self.t // sz.n_context, lax.rem(self.t, sz.n_context))
            pl.when(jnp.logical_not(self.at_home & (place.group == g)))(
                lambda holder=holder: pl.semaphore_signal(
                    barrier, inc=1, device_id=holder, device_id_type=MESH
                )
            )
        return sz.n_context - jnp.where(self.at_home, 1, 0)

    def remote(self, w, way):
        return pltpu.make_async_remote_copy(
            src_ref=self.sources[w][way],
            dst_ref=self.landed[w].at[self.place.group],
            send_sem=self.send.at[w, way],
            recv_sem=self.recv.at[w, self.place.group],
            device_id=(self.place.dp, self.role, way),
            device_id_type=MESH,
        )

    def local(self, w, way):
        return pltpu.make_async_copy(
            self.sources[w][way], self.landed[w].at[self.place.group], self.own.at[w]
        )

    def start(self, w, sources):
        self.sources[w] = sources
        for way in range(self.sz.n_context):
            here = self.at_home & (self.place.ctx == way)
            pl.when(here)(lambda way=way: self.local(w, way).start())
            pl.when(jnp.logical_not(here))(lambda way=way: self.remote(w, way).start())

    def total(self, w):
        place = self.place
        for g in range(self.sz.seqs):
            ref = self.landed[w].at[g]
            arrival = pltpu.make_async_remote_copy(
                src_ref=ref,
                dst_ref=ref,
                send_sem=self.send.at[w, 0],
                recv_sem=self.recv.at[w, g],
                device_id=(place.dp, self.t, 1 - place.ctx),
                device_id_type=MESH,
            )
            here = self.at_home & (place.group == g)
            pl.when(here)(lambda: self.local(w, 0).wait())
            pl.when(jnp.logical_not(here))(lambda arrival=arrival: arrival.wait_recv())
        total = self.landed[w][0].astype(jnp.float32)
        for g in range(1, self.sz.seqs):
            total = total + self.landed[w][g].astype(jnp.float32)
        return total

    def finish(self):
        for w in range(self.count):
            for way in range(self.sz.n_context):
                here = self.at_home & (self.place.ctx == way)
                pl.when(jnp.logical_not(here))(lambda w=w, way=way: self.remote(w, way).wait_send())


def slot_columns(sz, n_dp, x):
    slots = n_dp * sz.n_context
    depth = sz.width // slots
    if depth % 128:
        return x.reshape(sz.seq_len, slots, depth).transpose(1, 0, 2)
    return x[None]


def ffn_back_kernel(sz, n_dp, *refs):
    (cot, mixed, gains) = refs[:3]
    (rows_hbm, gate_hbm, up_hbm, wg_hbm, wu_hbm, down_hbm) = refs[3:9]
    (x_hbm, normed_hbm, hidden_hbm) = refs[9:12]
    (grad_mixed, gain_grad, dgate_out, dup_out, down_sum, gate_part) = refs[12:18]
    (rows_s, gate_s, up_s, wg, wu, wd, load, load_down, keep_sem) = refs[18:27]
    scatter_refs, ring_refs = refs[27:35], refs[35:]
    place = Place(sz)
    ring = Ring(place, n_dp)
    grads = GradRing(
        sz, place, ring, ffn_back_tasks(n_dp), [x_hbm, normed_hbm], [hidden_hbm, None], ring_refs,
        rows=[None, gate_s],
    )
    grads.start()
    pairs = ((rows_hbm, rows_s), (gate_hbm, gate_s), (up_hbm, up_s), (wg_hbm, wg), (wu_hbm, wu))
    loads = [
        pltpu.make_async_copy(src, dst, load.at[i]) for i, (src, dst) in enumerate(pairs)
    ]
    down_loads = column_loads(down_hbm, wd, load_down)
    place.enter([ring.device(1), ring.device(n_dp - 1)])
    scatter = Scatter(place, *scatter_refs)
    for copy in [loads[0]] + down_loads + loads[1:]:
        copy.start()
    grads.step()
    for copy in [loads[0]] + down_loads + loads[1:]:
        copy.wait()

    def work(q, j):
        rows = place.tile(q, j)
        dh = nt_dot(rows_s[rows, :], wd[...])
        gate = gate_s[rows, :].astype(jnp.float32)
        up = up_s[rows, :].astype(jnp.float32)
        sig = 1.0 / (1.0 + jnp.exp(-gate))
        dgate = (dh * up * sig * (1.0 + gate * (1.0 - sig))).astype(jnp.bfloat16)
        dup = (dh * gate * sig).astype(jnp.bfloat16)
        gate_s[rows, :] = dgate
        up_s[rows, :] = dup
        scatter.part[...] = nt_dot(dgate, wg[...]) + nt_dot(dup, wu[...])
        scatter.give(q, j)

    far = range(1, sz.half)
    for j in range(sz.seqs):
        for q in far:
            work(q, j)
        if j:
            for q in far:
                scatter.onward(q, j - 1)
    grads.step()
    work(0, 0)
    for q in far:
        scatter.onward(q, sz.seqs - 1)
    for j in range(1, sz.seqs):
        work(0, j)
    grads.step()
    copies = [
        pltpu.make_async_copy(gate_s, dgate_out, keep_sem.at[0]),
        pltpu.make_async_copy(up_s, dup_out, keep_sem.at[1]),
    ]
    for copy in copies:
        copy.start()
    gain_total = None
    for j in range(sz.seqs):
        span = slice(j * sz.block, (j + 1) * sz.block)
        rows = mixed[span, :]
        grad, gain_here = norm_back(scatter.total(j), rows, rms_factor(rows), gains[1:2, :])
        grad_mixed[span, :] = cot[span, :].astype(jnp.float32) + grad
        gain_total = gain_here if gain_total is None else gain_total + gain_here
    gain_grad[...] = gain_total
    while grads.left():
        grads.step()
    for way in range(sz.n_context):
        grads.hop(1, way, 0).wait_recv()
        for i, (src, dst) in enumerate(
            ((grads.result(0, way), down_sum), (grads.held[1].at[way, 0], gate_part))
        ):
            copies.append(
                pltpu.make_async_copy(src, dst.at[way], keep_sem.at[2 + 2 * way + i])
            )
            copies[-1].start()
    scatter.finish()
    grads.finish()
    for copy in copies:
        copy.wait()


def ffn_back_tasks(n_dp):
    return [(0, 0), (0, 1), (1, 0)] + [(0, s) for s in range(2, n_dp)]


def run_ffn_back(sz, n_dp, cot, mixed, gains, rows, gate, up, wg, wu, down, normed, hidden):
    f32, bf16, shape = jnp.float32, jnp.bfloat16, jax.ShapeDtypeStruct
    dma = pltpu.SemaphoreType.DMA
    depth = sz.width // (n_dp * sz.n_context)
    return pl.pallas_call(
        partial(ffn_back_kernel, sz, n_dp),
        out_shape=[
            shape((sz.rows, sz.width), f32),
            shape((1, sz.width), f32),
            shape((sz.seq_len, sz.ff), bf16),
            shape((sz.seq_len, sz.ff), bf16),
            shape((sz.n_context, depth, sz.ff), bf16),
            shape((sz.n_context, depth, sz.ff), bf16),
        ],
        in_specs=[full_spec()] * 3 + [any_spec()] * 9,
        out_specs=[full_spec()] * 2 + [any_spec()] * 4,
        scratch_shapes=[
            pltpu.VMEM((sz.seq_len, sz.width), bf16),
            pltpu.VMEM((sz.seq_len, sz.ff), bf16),
            pltpu.VMEM((sz.seq_len, sz.ff), bf16),
            pltpu.VMEM(wg.shape, bf16),
            pltpu.VMEM(wu.shape, bf16),
            pltpu.VMEM((sz.ff, sz.width), bf16),
            dma((5,)),
            dma((down.shape[0],)),
            dma((2 + 2 * sz.n_context,)),
        ]
        + Scatter.scratch(sz)
        + GradRing.scratch(sz, n_dp, ffn_back_tasks(n_dp), [sz.ff, sz.ff], [True, False]),
        compiler_params=pltpu.CompilerParams(
            collective_id=6, has_side_effects=True, vmem_limit_bytes=VMEM_BYTES
        ),
        cost_estimate=pl.CostEstimate(
            flops=8 * sz.seq_len * sz.width * sz.ff, bytes_accessed=40 << 20, transcendentals=0
        ),
        name="ffn_back",
    )(
        cot, mixed, gains, rows, gate, up, wg, wu, down,
        slot_columns(sz, n_dp, rows), slot_columns(sz, n_dp, normed), hidden,
    )


def attn_back_kernel(sz, n_dp, *refs):
    (grad_mixed, gains, cos_t, sin_t, begin, gain_b, adapted_hbm, state_hbm) = refs[:8]
    (q_hbm, k_hbm, v_hbm, lse_hbm, out_hbm, qkv_hbm) = refs[8:14]
    (x_hbm, dgate_hbm, dup_hbm, down_sum, gate_part) = refs[14:19]
    (grad_low, down_grad, gate_grad, state_out, rows_out, proj_out, up_part) = refs[19:26]
    (rows_s, q_s, k_s, v_s, lse_s, do_s, dk_s, dv_s, proj_s, wout, wqkv) = refs[26:37]
    (load, load_out, keep_sem, swap_out, swap_in, swap_sem, late) = refs[37:44]
    gather_refs, scatter_refs = refs[44:46], refs[46:54]
    ring_refs, deliver_refs = refs[54:66], refs[66:]
    place = Place(sz)
    ring = Ring(place, n_dp)
    grads = GradRing(
        sz, place, ring, attn_back_tasks(n_dp), [x_hbm, x_hbm], [dgate_hbm, dup_hbm], ring_refs,
        given=gate_part,
    )
    deliver = Deliver(sz, place, deliver_refs)
    grads.start()
    split = wqkv.shape[0]
    pairs = (
        (q_hbm, q_s), (k_hbm, k_s), (v_hbm, v_s), (lse_hbm, lse_s),
        (qkv_hbm.at[pl.ds(split, split)], wqkv),
    )
    loads = [
        pltpu.make_async_copy(src, dst, load.at[i]) for i, (src, dst) in enumerate(pairs)
    ]
    out_loads = column_loads(out_hbm, wout, load_out)
    for copy in out_loads + loads:
        copy.start()
    targets = deliver.greet()
    other = other_group(place)
    place.enter([ring.device(1), ring.device(n_dp - 1), other], targets)
    gather = Gather(place, rows_s, *gather_refs)
    scatter = Scatter(place, *scatter_refs)
    for j in range(sz.seqs):
        span = slice(j * sz.block, (j + 1) * sz.block)
        rows_s[gather.own(j), :] = grad_mixed[span, :].astype(jnp.bfloat16)
        gather.start(j)
    grads.step()
    deliver.start(0, [down_sum.at[way] for way in range(sz.n_context)])
    give_rows = pl.ds(pl.multiple_of((1 - place.group) * sz.block, sz.block), sz.block)
    keep_rows = pl.ds(pl.multiple_of(place.group * sz.block, sz.block), sz.block)
    swap = pltpu.make_async_remote_copy(
        src_ref=swap_out,
        dst_ref=swap_in,
        send_sem=swap_sem.at[0],
        recv_sem=swap_sem.at[1],
        device_id=other,
        device_id_type=MESH,
    )
    state_load = pltpu.make_async_copy(
        state_hbm.at[give_rows], scatter.part.at[pl.ds(0, sz.block)], late.at[0]
    )
    state_keep = pltpu.make_async_copy(
        state_hbm.at[keep_rows], state_out.at[place.group], late.at[1]
    )
    state_load.start()
    state_keep.start()
    state_load.wait()
    swap_out[...] = scatter.part[: sz.block, :].astype(jnp.bfloat16)
    swap.start()
    for copy in out_loads:
        copy.wait()
    d = sz.head_dim

    def heads_grad(q, j):
        rows = place.tile(q, j)
        dhead = nt_dot(rows_s[rows, :], wout[...]).astype(jnp.bfloat16)
        for h in range(sz.heads):
            do_s[h, rows, :] = dhead[:, h * d : (h + 1) * d]

    far = range(1, sz.half)
    for j in range(sz.seqs):
        gather.wait_near(j)
        heads_grad(0, j)
    for copy in loads:
        copy.wait()
    for j in range(sz.seqs):
        if j == sz.seqs - 1:
            grads.step()
            grads.step()
        for q in far:
            gather.forward(q, j)
        for q in far:
            gather.wait_far(sz.half - q, j)
            heads_grad(q, j)
    rows_copy = pltpu.make_async_copy(rows_s, rows_out, keep_sem.at[0])
    rows_copy.start()
    gather.finish()
    rows_copy.wait()
    upper = rows_s.at[pl.ds(0, split), pl.ds(0, wqkv.shape[1])]
    upper_load = pltpu.make_async_copy(qkv_hbm.at[pl.ds(0, split)], upper, late.at[2])
    upper_load.start()

    tiles = sz.n_tensor
    scale = 1.0 / math.sqrt(d)

    def head(h, carry):
        for i in reversed(range(tiles)):
            rows = slice(i * sz.tile, (i + 1) * sz.tile)
            length = (i + 1) * sz.tile
            keys, values = k_s[h, 0:length, :], v_s[h, 0:length, :]
            query, grad = q_s[h, rows, :], do_s[h, rows, :]
            start = begin[:, rows]
            key_at = lax.broadcasted_iota(jnp.int32, (length, sz.tile), 0)
            query_at = i * sz.tile + lax.broadcasted_iota(jnp.int32, (1, sz.tile), 1)
            allowed = (key_at >= start) & (key_at <= query_at)
            scores = nt_dot(keys, query)
            scores = jnp.where(allowed, scores * (LOG2E * scale), masked_score)
            probs = jnp.exp2(scores - lse_s[h, :, rows])
            dprobs = nt_dot(values, grad)
            inner = jnp.sum(probs * dprobs, axis=0, keepdims=True)
            dscores = (probs * (dprobs - inner)).astype(jnp.bfloat16)
            dv = nn_dot(probs.astype(jnp.bfloat16), grad)
            dk = nn_dot(dscores, query)
            if i == tiles - 1:
                dv_s[...] = dv
                dk_s[...] = dk
            else:
                dv_s[0:length, :] += dv
                dk_s[0:length, :] += dk
            dq = jnp.transpose(tn_dot(keys, dscores)) * scale
            cos_here, sin_here = cos_t[rows, :], sin_t[rows, :]
            proj_s[rows, pl.ds(pl.multiple_of(h * 3 * d, d), d)] = turn(
                dq, cos_here, -sin_here
            ).astype(jnp.bfloat16)
        dk = turn(dk_s[...] * scale, cos_t[...], -sin_t[...])
        proj_s[:, pl.ds(pl.multiple_of(h * 3 * d + d, d), d)] = dk.astype(jnp.bfloat16)
        proj_s[:, pl.ds(pl.multiple_of(h * 3 * d + 2 * d, d), d)] = dv_s[...].astype(jnp.bfloat16)
        return carry

    lax.fori_loop(0, sz.heads // 2, head, 0)
    while grads.left() > 1:
        grads.step()
    deliver.start(1, [grads.result(0, way) for way in range(sz.n_context)])
    lax.fori_loop(sz.heads // 2, sz.heads, head, 0)
    copies = [pltpu.make_async_copy(proj_s, proj_out, keep_sem.at[1])]
    copies[0].start()
    upper_load.wait()

    def give(q, j):
        proj = proj_s[place.tile(q, j), :]
        scatter.part[:, :split] = nt_dot(proj, upper[...])
        scatter.part[:, split:] = nt_dot(proj, wqkv[...])
        scatter.give(q, j)

    for j in range(sz.seqs):
        for q in far:
            give(q, j)
        if j:
            for q in far:
                scatter.onward(q, j - 1)
    give(0, 0)
    for q in far:
        scatter.onward(q, sz.seqs - 1)
    for j in range(1, sz.seqs):
        give(0, j)
    adapted = scatter.part
    adapted_load = pltpu.make_async_copy(adapted_hbm, adapted, late.at[3])
    adapted_load.start()
    grads.step()
    swap.wait()
    state_keep.wait()
    adapted_load.wait()
    state_out[1 - place.group] = swap_in[...].astype(jnp.float32)
    down_grad[...] = deliver.total(0)
    gain_total = None
    for j in range(sz.seqs):
        span = slice(j * sz.block, (j + 1) * sz.block)
        rows = adapted[span, :]
        grad, gain_here = norm_back(scatter.total(j), rows, rms_factor(rows), gains[0:1, :])
        grad_low[span, :] = (grad_mixed[span, :] + grad).astype(jnp.bfloat16)
        gain_total = gain_here if gain_total is None else gain_total + gain_here
    extra = grad_low.shape[0] - sz.rows
    at_row = lax.broadcasted_iota(jnp.int32, (extra, sz.width), 0)
    shares = jnp.where(at_row == 0, gain_total, jnp.where(at_row == 1, gain_b[...], 0.0))
    grad_low[sz.rows :, :] = shares.astype(jnp.bfloat16)
    for way in range(sz.n_context):
        grads.hop(1, way, 1).wait_recv()
        copies.append(
            pltpu.make_async_copy(
                grads.held[1].at[way, 1], up_part.at[way], keep_sem.at[2 + way]
            )
        )
        copies[-1].start()
    gate_grad[...] = deliver.total(1)
    scatter.finish()
    grads.finish()
    deliver.finish()
    for copy in copies:
        copy.wait()


def attn_back_tasks(n_dp):
    return [(0, 1), (0, 2), (1, 0)] + [(0, s) for s in range(3, n_dp)] + [(1, 1)]


def run_attn_back(
    sz, n_dp, grad_mixed, adapted, gains, cos_t, sin_t, begin, gain_b, state, q, k, v, lse, out,
    qkv, x, dgate, dup, down_sum, gate_part,
):
    f32, bf16, shape = jnp.float32, jnp.bfloat16, jax.ShapeDtypeStruct
    dma = pltpu.SemaphoreType.DMA
    heads_shape = (sz.heads, sz.seq_len, sz.head_dim)
    return pl.pallas_call(
        partial(attn_back_kernel, sz, n_dp),
        out_shape=[
            shape((sz.rows + 16, sz.width), bf16),
            shape(down_sum.shape[1:], f32),
            shape(gate_part.shape[1:], f32),
            shape((sz.seqs, sz.block, sz.width), f32),
            shape((sz.seq_len, sz.width), bf16),
            shape((sz.seq_len, qkv.shape[1]), bf16),
            shape(gate_part.shape, bf16),
        ],
        in_specs=[full_spec()] * 6 + [any_spec()] * 13,
        out_specs=[full_spec()] * 4 + [any_spec()] * 3,
        scratch_shapes=[
            pltpu.VMEM((sz.seq_len, sz.width), bf16),
            pltpu.VMEM(heads_shape, bf16),
            pltpu.VMEM(heads_shape, bf16),
            pltpu.VMEM(heads_shape, bf16),
            pltpu.VMEM((sz.heads, 1, sz.seq_len), f32),
            pltpu.VMEM(heads_shape, bf16),
            pltpu.VMEM((sz.seq_len, sz.head_dim), f32),
            pltpu.VMEM((sz.seq_len, sz.head_dim), f32),
            pltpu.VMEM((sz.seq_len, qkv.shape[1]), bf16),
            pltpu.VMEM((sz.heads * sz.head_dim, sz.width), bf16),
            pltpu.VMEM((sz.width // 2, qkv.shape[1]), bf16),
            dma((5,)),
            dma((out.shape[0],)),
            dma((2 + sz.n_context,)),
            pltpu.VMEM((sz.block, sz.width), bf16),
            pltpu.VMEM((sz.block, sz.width), bf16),
            dma((2,)),
            dma((4,)),
        ]
        + Gather.scratch(sz)
        + Scatter.scratch(sz)
        + GradRing.scratch(sz, n_dp, attn_back_tasks(n_dp), [sz.ff, sz.ff])
        + Deliver.scratch(sz, n_dp, [sz.ff, sz.ff]),
        compiler_params=pltpu.CompilerParams(
            collective_id=7, has_side_effects=True, vmem_limit_bytes=VMEM_BYTES
        ),
        cost_estimate=pl.CostEstimate(
            flops=4 * sz.seq_len * sz.width * qkv.shape[1], bytes_accessed=30 << 20, transcendentals=0
        ),
        name="attn_back",
    )(
        grad_mixed, gains, cos_t, sin_t, begin, gain_b, adapted, state, q, k, v, lse, out, qkv,
        slot_columns(sz, n_dp, x), dgate, dup, down_sum, gate_part,
    )


class PlaneRows:
    @staticmethod
    def scratch(n_dp):
        dma = pltpu.SemaphoreType.DMA
        return [dma((n_dp - 1,)), dma((n_dp - 1,)), dma((n_dp,)), dma((n_dp,))]

    def __init__(self, place, ring, own, landed, refs):
        self.place, self.ring, self.own, self.landed = place, ring, own, landed
        self.send, self.recv, self.near_send, self.near_recv = refs
        self.ahead = 1 - 2 * place.ctx

    def slot(self, offset, ctx):
        return self.landed.at[self.ring.index(offset) * self.place.sz.n_context + ctx]

    def source(self, s):
        return self.own if s == 0 else self.slot(-self.ahead * s, self.place.ctx)

    def hop(self, s):
        return pltpu.make_async_remote_copy(
            src_ref=self.source(s),
            dst_ref=self.slot(-self.ahead * s, self.place.ctx),
            send_sem=self.send.at[s],
            recv_sem=self.recv.at[s],
            device_id=self.ring.device(self.ahead),
            device_id_type=MESH,
        )

    def near(self, s):
        return pltpu.make_async_remote_copy(
            src_ref=self.source(s),
            dst_ref=self.slot(-self.ahead * s, self.place.ctx),
            send_sem=self.near_send.at[s],
            recv_sem=self.near_recv.at[s],
            device_id=self.place.sibling(),
            device_id_type=MESH,
        )

    def start(self):
        self.hop(0).start()
        self.near(0).start()

    def step(self, s):
        ref = self.slot(-self.ahead * (s + 1), self.place.ctx)
        pltpu.make_async_remote_copy(
            src_ref=ref,
            dst_ref=ref,
            send_sem=self.send.at[s],
            recv_sem=self.recv.at[s],
            device_id=self.place.sibling(),
            device_id_type=MESH,
        ).wait_recv()
        if s + 1 < self.ring.count - 1:
            self.hop(s + 1).start()
        self.near(s + 1).start()

    def wait_near(self, s):
        ref = self.slot(self.ahead * s, 1 - self.place.ctx)
        pltpu.make_async_remote_copy(
            src_ref=ref,
            dst_ref=ref,
            send_sem=self.near_send.at[s],
            recv_sem=self.near_recv.at[s],
            device_id=self.place.sibling(),
            device_id_type=MESH,
        ).wait_recv()

    def finish(self):
        for s in range(self.ring.count):
            if s < self.ring.count - 1:
                self.hop(s).wait_send()
            self.near(s).wait_send()


class LineSum:
    @staticmethod
    def scratch(sz, parts, chunk):
        dma, bf16 = pltpu.SemaphoreType.DMA, jnp.bfloat16
        far = pltpu.VMEM((max(sz.half - 1, 1), parts, chunk, sz.width), bf16)
        one = pltpu.VMEM((parts, chunk, sz.width), bf16)
        kinds = 2 * sz.half - 1
        return [far, far, one, one, one, far, dma((kinds, parts)), dma((kinds, parts))]

    def __init__(self, place, total, parts, refs):
        self.place, self.total, self.parts = place, total, parts
        (self.out, self.got, self.sum, self.cross, self.done, self.back, self.send, self.recv) = refs
        self.chunk = self.sum.shape[1]

    def rows(self, part, k):
        first = (part * self.parts + k) * self.chunk
        return pl.ds(pl.multiple_of(first, self.chunk), self.chunk)

    def copy(self, src, dst, kind, k, device):
        return pltpu.make_async_remote_copy(
            src_ref=src,
            dst_ref=dst,
            send_sem=self.send.at[kind, k],
            recv_sem=self.recv.at[kind, k],
            device_id=device,
            device_id_type=MESH,
        )

    def spread(self, q, k):
        place = self.place
        device = place.device(place.ahead(q), place.ctx)
        return self.copy(self.out.at[q - 1, k], self.got.at[q - 1, k], q, k, device)

    def swap(self, k):
        return self.copy(self.sum.at[k], self.cross.at[k], 0, k, other_group(self.place))

    def collect(self, q, k):
        place = self.place
        device = place.device(place.ahead(q), place.ctx)
        return self.copy(
            self.done.at[k], self.back.at[q - 1, k], place.sz.half - 1 + q, k, device
        )

    def start(self, k):
        for q in range(1, self.place.sz.half):
            rows = self.rows(self.place.ahead(q), k)
            self.out[q - 1, k] = self.total[rows, :].astype(jnp.bfloat16)
            self.spread(q, k).start()

    def cross_over(self, k):
        value = self.total[self.rows(self.place.part, k), :]
        for q in range(1, self.place.sz.half):
            self.spread(q, k).wait_recv()
            value = value + self.got[q - 1, k].astype(jnp.float32)
        self.sum[k] = value.astype(jnp.bfloat16)
        self.swap(k).start()

    def share(self, k):
        self.swap(k).wait_recv()
        value = self.sum[k].astype(jnp.float32) + self.cross[k].astype(jnp.float32)
        self.done[k] = value.astype(jnp.bfloat16)
        for q in range(1, self.place.sz.half):
            self.collect(q, k).start()
        self.total[self.rows(self.place.part, k), :] = self.done[k].astype(jnp.float32)

    def complete(self, k):
        for q in range(1, self.place.sz.half):
            self.collect(q, k).wait_recv()
            rows = self.rows(self.place.behind(q), k)
            self.total[rows, :] = self.back[q - 1, k].astype(jnp.float32)

    def finish(self):
        for k in range(self.parts):
            self.swap(k).wait_send()
            for q in range(1, self.place.sz.half):
                self.spread(q, k).wait_send()
                self.collect(q, k).wait_send()


SUM_PARTS = 2


def grads_kernel(sz, n_dp, count, *refs):
    n_in = 4 + 2 * count
    low, joined, adapter, up_part = refs[:4]
    xs, ys = refs[4 : 4 + count], refs[4 + count : n_in]
    outs = refs[n_in : n_in + count]
    embed_grad, adapter_out, gains_out, landed = refs[n_in + count : n_in + 4 + count]
    refs = refs[n_in + 4 + count :]

    def take(n):
        nonlocal refs
        head, refs = refs[:n], refs[n:]
        return head

    ring_refs, deliver_refs = take(3 * count + 6), take(count + 3)
    plane_refs, sum_refs = take(4), take(8)
    adapter_grad, d_s, j_s, weight_s, rows_s, swap_in = refs[:6]
    d_sem, j_sem, weight_sem, swap_sem, out_sem = refs[6:]
    place = Place(sz)
    ring = Ring(place, n_dp)
    grads = GradRing(
        sz, place, ring, grads_tasks(n_dp, count), xs, ys, ring_refs, given=up_part
    )
    deliver = Deliver(sz, place, deliver_refs)
    plane = PlaneRows(place, ring, low, landed, plane_refs)
    line = LineSum(place, adapter_grad, SUM_PARTS, sum_refs)
    other = other_group(place)
    grads.start()
    weight_load = [
        pltpu.make_async_copy(
            adapter.at[adapter.shape[0] // 2 + b, pl.ds(0, weight_s.shape[0])], weight_s, weight_sem
        )
        for b in range(adapter.shape[0] // 2)
    ]
    weight_load[0].start()
    place.enter([ring.device(1), ring.device(n_dp - 1), other], deliver.greet())
    plane.start()
    give_rows = pl.ds(pl.multiple_of((1 - place.group) * sz.block, sz.block), sz.block)
    keep_rows = pl.ds(pl.multiple_of(place.group * sz.block, sz.block), sz.block)
    swap = pltpu.make_async_remote_copy(
        src_ref=low.at[give_rows],
        dst_ref=swap_in,
        send_sem=swap_sem.at[0],
        recv_sem=swap_sem.at[1],
        device_id=other,
        device_id_type=MESH,
    )
    swap.start()

    def ring_step():
        if grads.left():
            w, complete = grads.step()
            if complete:
                deliver.start(w, [grads.result(w, way) for way in range(sz.n_context)])

    depth = joined.shape[2]

    def batch(ctx):
        copies = []
        for d in range(n_dp):
            at = d * sz.n_context + ctx
            rows = pl.ds(d * sz.rows, sz.rows)
            copies.append(
                pltpu.make_async_copy(landed.at[at, pl.ds(0, sz.rows)], d_s.at[rows], d_sem.at[d, 0])
            )
            copies.append(pltpu.make_async_copy(joined.at[at], j_s.at[rows], j_sem.at[d]))
            copies.append(
                pltpu.make_async_copy(
                    landed.at[at, pl.ds(sz.rows, 16)],
                    d_s.at[pl.ds(n_dp * sz.rows + 16 * d, 16)],
                    d_sem.at[d, 1],
                )
            )
        return copies

    def product(ctx, first):
        copies = batch(ctx)
        for copy in copies:
            copy.start()
        for copy in copies:
            copy.wait()
        chunk = sz.width // 4
        for n in range(4):
            cols = slice(n * chunk, (n + 1) * chunk)
            value = tn_dot(j_s[...], d_s[: n_dp * sz.rows, cols])
            tail = d_s[n_dp * sz.rows : n_dp * sz.rows + 16, cols].astype(jnp.float32)
            for d in range(1, n_dp):
                at = n_dp * sz.rows + 16 * d
                tail = tail + d_s[at : at + 16, cols].astype(jnp.float32)
            if first:
                adapter_grad[:depth, cols] = value
                adapter_grad[depth : depth + 16, cols] = tail
            else:
                adapter_grad[:depth, cols] += value
                adapter_grad[depth : depth + 16, cols] += tail

    own = pltpu.make_async_copy(low, landed.at[place.dp * sz.n_context + place.ctx], d_sem.at[0, 0])
    own.start()
    rest = adapter_grad.shape[0] - depth - 16
    if rest:
        adapter_grad[depth + 16 :, :] = jnp.zeros((rest, sz.width), jnp.float32)
    for s in range(n_dp - 1):
        ring_step()
        plane.step(s)
    own.wait()
    product(place.ctx, True)
    for s in range(n_dp):
        plane.wait_near(s)
    product(1 - place.ctx, False)
    for k in range(SUM_PARTS):
        line.start(k)
    ring_step()
    ring_step()
    swap.wait()
    rows_s[place.group] = low[keep_rows, :]
    rows_s[1 - place.group] = swap_in[...]
    rows = rows_s[...].reshape(sz.rows, sz.width)
    ring_step()
    for k in range(SUM_PARTS):
        line.cross_over(k)
    ring_step()
    for b, copy in enumerate(weight_load):
        copy.wait()
        part = nt_dot(rows, weight_s[...]).reshape(sz.seqs, sz.block, weight_s.shape[0])
        embed_grad[:, :, b * weight_s.shape[0] : (b + 1) * weight_s.shape[0]] = part
        if b + 1 < len(weight_load):
            weight_load[b + 1].start()
    ring_step()
    for k in range(SUM_PARTS):
        line.share(k)
        ring_step()
    while grads.left():
        ring_step()
    for k in range(SUM_PARTS):
        line.complete(k)
    saves = [
        pltpu.make_async_copy(adapter_grad.at[pl.ds(0, depth)], adapter_out, out_sem.at[0]),
        pltpu.make_async_copy(adapter_grad.at[pl.ds(depth, 16)], gains_out, out_sem.at[1]),
    ]
    for copy in saves:
        copy.start()
    for w in range(count):
        outs[w][...] = deliver.total(w)
    for copy in saves:
        copy.wait()
    grads.finish()
    deliver.finish()
    plane.finish()
    line.finish()


def grads_tasks(n_dp, count):
    others = [(w + 1, s) for w, s in GradRing.all_tasks(n_dp, count - 1)]
    return [(0, s) for s in range(2, n_dp)] + others


def run_grads(sz, n_dp, low, joined, adapter, up_part, xs, ys):
    count, bf16, f32, dma = len(xs), jnp.bfloat16, jnp.float32, pltpu.SemaphoreType.DMA
    shape = jax.ShapeDtypeStruct
    depth = sz.width // (n_dp * sz.n_context)
    wide = [y.shape[1] for y in ys]
    slots, columns = joined.shape[0], joined.shape[2]
    unit = 16 * sz.half * SUM_PARTS
    total_rows = -(-(columns + 16) // unit) * unit
    return pl.pallas_call(
        partial(grads_kernel, sz, n_dp, count),
        out_shape=[shape((depth, n), f32) for n in wide]
        + [
            shape((sz.seqs, sz.block, sz.width), f32),
            shape((columns, sz.width), f32),
            shape((16, sz.width), f32),
            shape((slots,) + low.shape, bf16),
        ],
        in_specs=[full_spec()] + [any_spec()] * (3 + 2 * count),
        out_specs=[full_spec()] * (1 + count) + [any_spec()] * 3,
        scratch_shapes=GradRing.scratch(sz, n_dp, grads_tasks(n_dp, count), wide)
        + Deliver.scratch(sz, n_dp, wide)
        + PlaneRows.scratch(n_dp)
        + LineSum.scratch(sz, SUM_PARTS, total_rows // (sz.half * SUM_PARTS))
        + [
            pltpu.VMEM((total_rows, sz.width), f32),
            pltpu.VMEM((n_dp * (sz.rows + 16), sz.width), bf16),
            pltpu.VMEM((n_dp * sz.rows, columns), bf16),
            pltpu.VMEM((columns, sz.width), bf16),
            pltpu.VMEM((sz.seqs, sz.block, sz.width), bf16),
            pltpu.VMEM((sz.block, sz.width), bf16),
            dma((n_dp, 2)),
            dma((n_dp,)),
            dma,
            dma((2,)),
            dma((2,)),
        ],
        compiler_params=pltpu.CompilerParams(
            collective_id=8, has_side_effects=True, vmem_limit_bytes=VMEM_BYTES
        ),
        cost_estimate=pl.CostEstimate(
            flops=2 * sz.seq_len * sz.width * sum(wide), bytes_accessed=60 << 20, transcendentals=0
        ),
        name="grads",
    )(low, joined, adapter, up_part, *[slot_columns(sz, n_dp, x) for x in xs], *ys)


def shards(
    embedded,
    initial_state,
    cotangent,
    doc_ids,
    recurrences,
    adapter_weight,
    norm_gains,
    qkv_weight,
    output_head_weight,
    gate_up_weight,
    down_weight,
):
    n_dp = lax.axis_size("dp")
    n_tensor = lax.axis_size("tensor")
    n_context = lax.axis_size("context")
    dp_index = lax.axis_index("dp")
    t_index = lax.axis_index("tensor")
    ctx_index = lax.axis_index("context")
    seq_count, block_rows, model_width = embedded.shape
    seq_len = doc_ids.shape[1]
    half = n_tensor // seq_count
    group = t_index // half
    part = t_index % half
    heads_here = qkv_weight.shape[1]
    head_dim = qkv_weight.shape[2] // 3
    ff_here = down_weight.shape[0]
    def side_by_side(blocks):
        count, depth, columns = blocks.shape
        return blocks.transpose(1, 0, 2).reshape(depth, count * columns)

    def role_grad(grad, axis):
        piece = lax.psum_scatter(
            grad.astype(jnp.bfloat16), "dp", scatter_dimension=axis, tiled=True
        )
        low, high = jnp.split(piece, 2, axis=axis)
        give = [jnp.where(group == 0, low, high), jnp.where(group == 0, high, low)]
        back = [
            lax.ppermute(g, ("tensor", "context"), [(b, a) for a, b in perm])
            for g, perm in zip(give, role_perms)
        ]
        return back[0].astype(jnp.float32) + back[1].astype(jnp.float32)

    def gather_rows(rows):
        full = lax.all_gather(
            rows, ("tensor", "context"), axis=0, tiled=True, axis_index_groups=groups
        )
        split = full.reshape(half, n_context, seq_count, block_rows, model_width)
        return split.transpose(2, 0, 1, 3, 4).reshape(seq_len, model_width)

    sz = Sizes(
        n_tensor,
        n_context,
        seq_count,
        half,
        block_rows,
        n_context * block_rows,
        seq_count * block_rows,
        seq_len,
        model_width,
        heads_here,
        head_dim,
        ff_here,
    )
    adapter_block = adapter_weight.shape[0]
    gain_columns = norm_gains.shape[1]
    unit = 16 * half
    padded = -(-(adapter_block + 2) // unit) * unit
    adapter_rows = jnp.concatenate(
        [
            adapter_weight,
            jnp.pad(
                norm_gains,
                ((0, padded - adapter_block - 2), (0, model_width - gain_columns)),
            ),
        ],
        axis=0,
    )
    (
        adapter_all,
        out_blocks,
        qkv_use,
        gate_use,
        up_use,
        down_pair,
        embed_rows,
        cot_rows,
        grad_ffn,
        embed_part,
        current,
    ) = run_weights(
        sz,
        n_dp,
        adapter_rows,
        adapter_block,
        [
            output_head_weight.reshape(heads_here * head_dim, -1),
            qkv_weight.reshape(qkv_weight.shape[0], -1),
            gate_up_weight[:, 0],
            gate_up_weight[:, 1],
            down_weight,
        ],
        [embedded, initial_state, cotangent],
    )
    qkv_use = qkv_use.reshape(model_width, -1)
    gate_use = gate_use.reshape(model_width, -1)
    up_use = up_use.reshape(model_width, -1)
    gains_full = (
        adapter_all[:, adapter_block : adapter_block + 2, :gain_columns]
        .transpose(1, 0, 2)
        .reshape(2, model_width)
    )
    if out_blocks.shape[2] % 128:
        out_blocks = side_by_side(out_blocks)[None]
    gains_f = gains_full.astype(jnp.float32)

    cos_full, sin_full = rope_tables(seq_len, head_dim)
    own_seq = dp_index * seq_count + group
    docs = lax.dynamic_index_in_dim(doc_ids, own_seq, 0, keepdims=False)
    begin = jnp.sum((docs[None, :] < docs[:, None]).astype(jnp.int32), axis=1)[None, :]
    steps_own = lax.dynamic_index_in_dim(recurrences, own_seq, 0, keepdims=False) - BACK
    active = jnp.arange(MAXR - BACK, dtype=jnp.int32)[:, None] < steps_own
    active = jnp.broadcast_to(active.astype(jnp.float32), (MAXR - BACK, model_width))
    mixed, down_blocks = run_attn(
        sz, n_dp, False, current, embed_part, gains_f, cos_full, sin_full, begin,
        adapter_all, qkv_use, out_blocks, down_pair,
    )
    if down_blocks.shape[2] % 128:
        down_blocks = side_by_side(down_blocks)[None]
    (current,) = run_ffn(
        sz, False, mixed, current, active[:1], gains_f, gate_use, up_use, down_blocks
    )
    detached = run_rounds(
        sz, current, active[1:], gains_f, cos_full, sin_full, begin, embed_part,
        adapter_all, qkv_use, out_blocks, gate_use, up_use, down_blocks,
    )
    (mixed_rows, adapted, feature_rows, query_hm, key_hm, value_hm, head_flat, lse, joined) = run_attn(
        sz, n_dp, True, detached, embed_part, gains_f, cos_full, sin_full, begin,
        adapter_all, qkv_use, out_blocks, embed_rows,
    )
    (current, ffn_input, gate_pre, up_pre, hidden) = run_ffn(
        sz, True, mixed_rows, detached, gains_f[:1], gains_f, gate_use, up_use, down_blocks
    )
    grad_mixed, gain_b, grad_gate, grad_up, down_sum, gate_part = run_ffn_back(
        sz, n_dp, cot_rows, mixed_rows, gains_f, grad_ffn, gate_pre, up_pre,
        gate_use, up_use, down_blocks, ffn_input, hidden,
    )
    grad_low, down_t, gate_s, state_out, grad_rows, grad_proj, up_part = run_attn_back(
        sz, n_dp, grad_mixed, adapted, gains_f, cos_full, sin_full, begin, gain_b, current,
        query_hm, key_hm, value_hm, lse, out_blocks, qkv_use, ffn_input, grad_gate, grad_up, down_sum,
        gate_part,
    )
    up_s, qkv_s, out_t, embed_out, adapter_s, gains_rows, _ = run_grads(
        sz,
        n_dp,
        grad_low,
        joined,
        adapter_all,
        up_part,
        [ffn_input, feature_rows, grad_rows],
        [grad_up, grad_proj, head_flat],
    )
    place_at = (dp_index * n_context + ctx_index) * gain_columns
    gains_s = lax.dynamic_slice_in_dim(gains_rows[:2], place_at, gain_columns, 1)
    down_s = down_t.T
    out_s = out_t.T.reshape(heads_here, head_dim, -1)
    qkv_s = qkv_s.reshape(-1, heads_here, 3 * head_dim)
    gate_up_s = jnp.stack([gate_s, up_s], axis=1)
    return (state_out, embed_out, adapter_s, gains_s, qkv_s, out_s, gate_up_s, down_s)


def solution(mesh):
    placed = (
        P("dp", ("tensor", "context"), None),
        P("dp", ("tensor", "context"), None),
        P("dp", ("tensor", "context"), None),
        P(),
        P(),
        P(("dp", "context"), None),
        P(None, ("dp", "context")),
        P(("dp", "context"), "tensor", None),
        P("tensor", None, ("dp", "context")),
        P(("dp", "context"), None, "tensor"),
        P("tensor", ("dp", "context")),
    )
    return jax.shard_map(
        shards,
        mesh=mesh,
        in_specs=placed,
        out_specs=(
            P("dp", ("tensor", "context"), None),
            P("dp", ("tensor", "context"), None),
            P(("dp", "context"), None),
            P(None, ("dp", "context")),
            P(("dp", "context"), "tensor", None),
            P("tensor", None, ("dp", "context")),
            P(("dp", "context"), None, "tensor"),
            P("tensor", ("dp", "context")),
        ),
        check_vma=False,
    )
```

```python
from functools import partial
import math
from typing import NamedTuple

import jax
import jax.numpy as jnp
import numpy as np
from jax import lax
from jax.experimental import pallas as pl
from jax.experimental.pallas import tpu as pltpu
from jax.sharding import PartitionSpec as P

BACK = 1
MAXR = 4


rope_base = 50000.0
norm_eps = 1e-06
masked_score = -1e30


def rope_tables(seq_len, head_dim):
    freq_index = np.arange(head_dim // 2, dtype=np.float32)
    inv_freq = 1.0 / np.float32(rope_base) ** (np.float32(2.0) * freq_index / head_dim)
    angles = np.arange(seq_len, dtype=np.float32)[:, None] * inv_freq.astype(np.float32)[None, :]
    cos_t, sin_t = np.cos(angles), np.sin(angles)
    return (
        jnp.asarray(np.concatenate([cos_t, cos_t], axis=1), jnp.float32),
        jnp.asarray(np.concatenate([-sin_t, sin_t], axis=1), jnp.float32),
    )


MESH = pl.DeviceIdType.MESH
LOG2E = 1.4426950408889634
VMEM_BYTES = 62 << 20


class Sizes(NamedTuple):
    n_tensor: int
    n_context: int
    seqs: int
    half: int
    block: int
    tile: int
    rows: int
    seq_len: int
    width: int
    heads: int
    head_dim: int
    ff: int


def full_spec():
    return pl.BlockSpec(memory_space=pltpu.VMEM)


def any_spec():
    return pl.BlockSpec(memory_space=pl.ANY)


def nt_dot(a, b):
    return lax.dot_general(a, b, (((1,), (1,)), ((), ())), preferred_element_type=jnp.float32)


def tn_dot(a, b):
    return lax.dot_general(a, b, (((0,), (0,)), ((), ())), preferred_element_type=jnp.float32)


def nn_dot(a, b):
    return jnp.dot(a, b, preferred_element_type=jnp.float32)


class Place:
    def __init__(self, sz):
        t = lax.axis_index("tensor")
        self.sz = sz
        self.dp = lax.axis_index("dp")
        self.ctx = lax.axis_index("context")
        self.group = t // sz.half
        self.part = lax.rem(t, sz.half)

    def device(self, part, ctx):
        return (self.dp, self.group * self.sz.half + part, ctx)

    def ahead(self, q):
        return lax.rem(self.part + q, self.sz.half)

    def behind(self, q):
        return lax.rem(self.part + (self.sz.half - q), self.sz.half)

    def sibling(self):
        return self.device(self.part, 1 - self.ctx)

    def block(self, part, ctx, j):
        sz = self.sz
        first = ((part + j * sz.half) * sz.n_context + ctx) * sz.block
        return pl.ds(pl.multiple_of(first, sz.block), sz.block)

    def tile(self, q, j):
        sz = self.sz
        first = (self.ahead(q) + j * sz.half) * sz.tile
        return pl.ds(pl.multiple_of(first, sz.tile), sz.tile)

    def enter(self, others=(), more=0):
        barrier = pltpu.get_barrier_semaphore()
        for device in others:
            pl.semaphore_signal(barrier, inc=1, device_id=device, device_id_type=MESH)
        pl.semaphore_signal(
            barrier, inc=1, device_id=self.sibling(), device_id_type=MESH
        )
        for q in range(1, self.sz.half):
            pl.semaphore_signal(
                barrier,
                inc=1,
                device_id=self.device(self.ahead(q), self.ctx),
                device_id_type=MESH,
            )
        pl.semaphore_wait(barrier, self.sz.half + len(others) + more)


class Gather:
    @staticmethod
    def scratch(sz):
        kinds = 2 * sz.half - 1
        return [
            pltpu.SemaphoreType.DMA((kinds, sz.seqs)),
            pltpu.SemaphoreType.DMA((kinds, sz.seqs)),
        ]

    def __init__(self, place, ref, send, recv):
        self.place, self.ref, self.send, self.recv = place, ref, send, recv

    def copy(self, kind, j, rows):
        place, half = self.place, self.place.sz.half
        if 0 < kind < half:
            target = place.device(place.ahead(kind), place.ctx)
        else:
            target = place.sibling()
        return pltpu.make_async_remote_copy(
            src_ref=self.ref.at[rows],
            dst_ref=self.ref.at[rows],
            send_sem=self.send.at[kind, j],
            recv_sem=self.recv.at[kind, j],
            device_id=target,
            device_id_type=MESH,
        )

    def own(self, j):
        return self.place.block(self.place.part, self.place.ctx, j)

    def start(self, j):
        for q in range(1, self.place.sz.half):
            self.copy(q, j, self.own(j)).start()
        self.copy(0, j, self.own(j)).start()

    def wait_near(self, j):
        place = self.place
        self.copy(0, j, place.block(place.part, 1 - place.ctx, j)).wait_recv()

    def forward(self, q, j):
        place = self.place
        rows = place.block(place.behind(q), place.ctx, j)
        self.copy(q, j, rows).wait_recv()
        self.copy(place.sz.half - 1 + q, j, rows).start()

    def wait_far(self, q, j):
        place = self.place
        rows = place.block(place.behind(q), 1 - place.ctx, j)
        self.copy(place.sz.half - 1 + q, j, rows).wait_recv()

    def passed_on(self, j):
        place, half = self.place, self.place.sz.half
        for q in range(1, half):
            rows = place.block(place.behind(q), place.ctx, j)
            self.copy(half - 1 + q, j, rows).wait_send()

    def finish(self, forwards=True):
        for j in range(self.place.sz.seqs):
            for kind in range(self.place.sz.half):
                self.copy(kind, j, self.own(j)).wait_send()
            if forwards:
                self.passed_on(j)


class Scatter:
    @staticmethod
    def scratch(sz):
        kinds = 2 * sz.half - 1
        near = (sz.half, sz.seqs, sz.block, sz.width)
        far = (max(sz.half - 1, 1), sz.seqs, sz.block, sz.width)
        return [
            pltpu.VMEM((sz.tile, sz.width), jnp.float32),
            pltpu.VMEM(near, jnp.bfloat16),
            pltpu.VMEM(near, jnp.bfloat16),
            pltpu.VMEM(near, jnp.bfloat16),
            pltpu.VMEM(far, jnp.bfloat16),
            pltpu.VMEM(far, jnp.bfloat16),
            pltpu.SemaphoreType.DMA((kinds, sz.seqs)),
            pltpu.SemaphoreType.DMA((kinds, sz.seqs)),
        ]

    def __init__(self, place, part, mine, near_out, near_in, far_out, far_in, send, recv):
        self.place, self.part, self.mine = place, part, mine
        self.near_out, self.near_in = near_out, near_in
        self.far_out, self.far_in = far_out, far_in
        self.send, self.recv = send, recv

    def near(self, q, j):
        return pltpu.make_async_remote_copy(
            src_ref=self.near_out.at[q, j],
            dst_ref=self.near_in.at[q, j],
            send_sem=self.send.at[q, j],
            recv_sem=self.recv.at[q, j],
            device_id=self.place.sibling(),
            device_id_type=MESH,
        )

    def far(self, q, j):
        place = self.place
        return pltpu.make_async_remote_copy(
            src_ref=self.far_out.at[q - 1, j],
            dst_ref=self.far_in.at[q - 1, j],
            send_sem=self.send.at[place.sz.half - 1 + q, j],
            recv_sem=self.recv.at[place.sz.half - 1 + q, j],
            device_id=place.device(place.ahead(q), place.ctx),
            device_id_type=MESH,
        )

    def give(self, q, j):
        sz, ctx = self.place.sz, self.place.ctx
        mine = pl.ds(pl.multiple_of(ctx * sz.block, sz.block), sz.block)
        other = pl.ds(pl.multiple_of((1 - ctx) * sz.block, sz.block), sz.block)
        self.near_out[q, j] = self.part[other, :].astype(jnp.bfloat16)
        self.near(q, j).start()
        self.mine[q, j] = self.part[mine, :].astype(jnp.bfloat16)

    def onward(self, q, j):
        self.near(q, j).wait_recv()
        self.far_out[q - 1, j] = (
            self.mine[q, j].astype(jnp.float32) + self.near_in[q, j].astype(jnp.float32)
        ).astype(jnp.bfloat16)
        self.far(q, j).start()

    def total(self, j):
        self.near(0, j).wait_recv()
        total = self.mine[0, j].astype(jnp.float32) + self.near_in[0, j].astype(jnp.float32)
        for q in range(1, self.place.sz.half):
            self.far(q, j).wait_recv()
            total = total + self.far_in[q - 1, j].astype(jnp.float32)
        return total

    def finish(self):
        half = self.place.sz.half
        for j in range(self.place.sz.seqs):
            for q in range(half):
                self.near(q, j).wait_send()
            for q in range(1, half):
                self.far(q, j).wait_send()


def column_loads(blocks_ref, vmem_ref, sem):
    count, _, columns = blocks_ref.shape
    return [
        pltpu.make_async_copy(
            blocks_ref.at[b], vmem_ref.at[:, pl.ds(b * columns, columns)], sem.at[b]
        )
        for b in range(count)
    ]


def adapter_loads(blocks_ref, vmem_ref, sem):
    count, tops = sem.shape
    depth, columns = vmem_ref.shape[0] // tops, vmem_ref.shape[1] // count
    return [
        [
            pltpu.make_async_copy(
                blocks_ref.at[b, pl.ds(0, depth), pl.ds(n * columns, columns)],
                vmem_ref.at[pl.ds(b * depth, depth), pl.ds(n * columns, columns)],
                sem.at[n, b],
            )
            for b in range(tops)
        ]
        for n in range(count)
    ]


def rms_factor(rows):
    return lax.rsqrt(jnp.mean(rows * rows, axis=-1, keepdims=True) + norm_eps)


def turn(x, cos_t, sin_t):
    return x * cos_t + pltpu.roll(x, x.shape[-1] // 2, 1) * sin_t


def attn_kernel(sz, n_dp, keep, *refs):
    (latent, embed, gains, cos_t, sin_t, begin, adapter_hbm, qkv_hbm, out_hbm) = refs[:9]
    refs = refs[9:]
    if keep:
        embed_hbm, refs = refs[0], refs[1:]
    mixed = refs[0]
    refs = refs[1:]
    if keep:
        adapted_out, rows_out, q_out, k_out, v_out, head_out, lse_out, joined_out = refs[:8]
        refs = refs[8:]
    (wa, wqkv, wout, adapted, rows_s, q_s, k_s, v_s, head_s, lse_s) = refs[:10]
    load_a, load_qkv, load_out, keep_sem = refs[10:14]
    gather_refs = refs[14:16]
    scatter_refs = refs[16:24]
    if keep:
        joined_s, load_embed, x_send, x_recv = refs[24:]

    place = Place(sz)
    a_loads = adapter_loads(adapter_hbm, wa, load_a)
    qkv_load = pltpu.make_async_copy(qkv_hbm, wqkv, load_qkv)
    out_loads = column_loads(out_hbm, wout, load_out)
    for group in a_loads:
        for copy in group:
            copy.start()
    qkv_load.start()
    for copy in out_loads:
        copy.start()
    others = []
    if keep:
        ring = Ring(place, n_dp)
        t = lax.axis_index("tensor")
        embed_load = pltpu.make_async_copy(
            embed_hbm, joined_s.at[:, pl.ds(sz.width, sz.width)], load_embed
        )
        embed_load.start()
        plane = [(o, c) for o in range(n_dp) for c in range(2) if (o, c) != (0, 0)]

        def member(o, c):
            return (ring.index(o), t, place.ctx if c == 0 else 1 - place.ctx)

        def columns_to(o, c):
            to = member(o, c)
            depth = joined_out.shape[2]
            first = pl.multiple_of((to[0] * sz.n_context + to[2]) * depth, depth)
            return pltpu.make_async_remote_copy(
                src_ref=joined_s.at[:, pl.ds(first, depth)],
                dst_ref=joined_out.at[place.dp * sz.n_context + place.ctx],
                send_sem=x_send.at[o, c],
                recv_sem=x_recv.at[o, c],
                device_id=to,
                device_id_type=MESH,
            )

        def columns_from(o, c):
            ref = joined_out.at[
                ring.index(-o) * sz.n_context + (place.ctx if c == 0 else 1 - place.ctx)
            ]
            return pltpu.make_async_remote_copy(
                src_ref=ref,
                dst_ref=ref,
                send_sem=x_send.at[o, c],
                recv_sem=x_recv.at[o, c],
                device_id=place.sibling(),
                device_id_type=MESH,
            )

        others = [member(o, c) for o, c in plane if o]
    place.enter(others)
    gather = Gather(place, rows_s, *gather_refs)
    scatter = Scatter(place, *scatter_refs)

    low = latent[...].astype(jnp.bfloat16)
    columns = sz.width // len(a_loads)
    square = None
    for n, group in enumerate(a_loads):
        for copy in group:
            copy.wait()
        cols = pl.ds(n * columns, columns)
        chunk = nn_dot(low, wa[:, cols]) + embed[:, cols]
        adapted[:, cols] = chunk
        here = jnp.sum(chunk * chunk, axis=-1, keepdims=True)
        square = here if square is None else square + here
    factor = lax.rsqrt(square / sz.width + norm_eps)
    for j in range(sz.seqs):
        span = slice(j * sz.block, (j + 1) * sz.block)
        normed = (adapted[span, :] * factor[span]) * gains[0:1, :]
        rows_s[gather.own(j), :] = normed.astype(jnp.bfloat16)
        gather.start(j)

    qkv_load.wait()
    pair = min(2, sz.heads)
    d = sz.head_dim

    def project(q, j):
        rows = place.tile(q, j)
        x = rows_s[rows, :]
        cos_here, sin_here = cos_t[rows, :], sin_t[rows, :]
        for h0 in range(0, sz.heads, pair):
            proj = nn_dot(x, wqkv[:, 3 * d * h0 : 3 * d * (h0 + pair)])
            for h in range(pair):
                at = 3 * d * h
                q_s[h0 + h, rows, :] = turn(proj[:, at : at + d], cos_here, sin_here).astype(
                    jnp.bfloat16
                )
                k_s[h0 + h, rows, :] = turn(
                    proj[:, at + d : at + 2 * d], cos_here, sin_here
                ).astype(jnp.bfloat16)
                v_s[h0 + h, rows, :] = proj[:, at + 2 * d : at + 3 * d].astype(jnp.bfloat16)

    def attend(q, j):
        rows = place.tile(q, j)
        first = (place.ahead(q) + j * sz.half) * sz.tile
        length = (j + 1) * sz.half * sz.tile
        start = begin[:, pl.ds(pl.multiple_of(first, sz.tile), sz.tile)]
        key_at = lax.broadcasted_iota(jnp.int32, (length, sz.tile), 0)
        query_at = first + lax.broadcasted_iota(jnp.int32, (1, sz.tile), 1)
        allowed = (key_at >= start) & (key_at <= query_at)

        def head(h, carry):
            scores = nt_dot(k_s[h, 0:length, :], q_s[h, rows, :])
            scores = jnp.where(allowed, scores * (LOG2E / math.sqrt(d)), masked_score)
            top = jnp.max(scores, axis=0, keepdims=True)
            weight = jnp.exp2(scores - top)
            total = jnp.sum(weight, axis=0, keepdims=True)
            mixed_t = tn_dot(v_s[h, 0:length, :], weight.astype(jnp.bfloat16))
            result = jnp.transpose(mixed_t / total)
            head_s[rows, pl.ds(pl.multiple_of(h * d, d), d)] = result.astype(jnp.bfloat16)
            if keep:
                lse_s[h, :, rows] = top + jnp.log2(total)
            return carry

        lax.fori_loop(0, sz.heads, head, 0)

    def give(q, j):
        rows = place.tile(q, j)
        scatter.part[...] = nn_dot(head_s[rows, :], wout[...])
        scatter.give(q, j)

    copies = []

    def save(src, dst):
        copy = pltpu.make_async_copy(src, dst, keep_sem.at[len(copies)])
        copy.start()
        copies.append(copy)

    if keep:
        save(adapted, adapted_out)
        joined_s[:, : sz.width] = low
        embed_load.wait()
        for o, c in plane:
            columns_to(o, c).start()
        mine = place.dp * sz.n_context + place.ctx
        depth = joined_out.shape[2]
        save(
            joined_s.at[:, pl.ds(pl.multiple_of(mine * depth, depth), depth)], joined_out.at[mine]
        )
    far = range(1, sz.half)
    for j in range(sz.seqs):
        gather.wait_near(j)
        project(0, j)
    for copy in out_loads:
        copy.wait()
    for j in range(sz.seqs):
        for q in far:
            gather.forward(q, j)
        for q in far:
            gather.wait_far(sz.half - q, j)
            project(q, j)
        for q in far:
            attend(q, j)
            give(q, j)
        attend(0, j)
        for q in far:
            scatter.onward(q, j)
        give(0, j)
    if keep:
        for src, dst in ((rows_s, rows_out), (q_s, q_out), (k_s, k_out), (v_s, v_out)):
            save(src, dst)
        save(head_s, head_out)
        save(lse_s, lse_out)
    gather.finish()
    for j in range(sz.seqs):
        span = slice(j * sz.block, (j + 1) * sz.block)
        mixed[span, :] = adapted[span, :] + scatter.total(j)
    scatter.finish()
    if keep:
        for o, c in plane:
            columns_from(o, c).wait_recv()
            columns_to(o, c).wait_send()
    for copy in copies:
        copy.wait()


def run_attn(
    sz, n_dp, keep, latent, embed_part, gains, cos_t, sin_t, begin, adapter, qkv, out, *embed
):
    f32, bf16 = jnp.float32, jnp.bfloat16
    heads_shape = (sz.heads, sz.seq_len, sz.head_dim)
    shape = jax.ShapeDtypeStruct
    outs = [shape((sz.rows, sz.width), f32)]
    if keep:
        outs += [
            shape((sz.rows, sz.width), f32),
            shape((sz.seq_len, sz.width), bf16),
            shape(heads_shape, bf16),
            shape(heads_shape, bf16),
            shape(heads_shape, bf16),
            shape((sz.seq_len, sz.heads * sz.head_dim), bf16),
            shape((sz.heads, 1, sz.seq_len), f32),
            shape((adapter.shape[0], sz.rows, 2 * sz.width // adapter.shape[0]), bf16),
        ]
    scratch = [
        pltpu.VMEM((sz.width, sz.width), bf16),
        pltpu.VMEM(qkv.shape, bf16),
        pltpu.VMEM((sz.heads * sz.head_dim, sz.width), bf16),
        pltpu.VMEM((sz.rows, sz.width), f32),
        pltpu.VMEM((sz.seq_len, sz.width), bf16),
        pltpu.VMEM(heads_shape, bf16),
        pltpu.VMEM(heads_shape, bf16),
        pltpu.VMEM(heads_shape, bf16),
        pltpu.VMEM((sz.seq_len, sz.heads * sz.head_dim), bf16),
        pltpu.VMEM((sz.heads, 1, sz.seq_len), f32),
        pltpu.SemaphoreType.DMA((4, adapter.shape[0] // 2)),
        pltpu.SemaphoreType.DMA,
        pltpu.SemaphoreType.DMA((out.shape[0],)),
        pltpu.SemaphoreType.DMA((8,)),
    ]
    scratch += Gather.scratch(sz) + Scatter.scratch(sz)
    if keep:
        scratch += [
            pltpu.VMEM((sz.rows, 2 * sz.width), bf16),
            pltpu.SemaphoreType.DMA,
            pltpu.SemaphoreType.DMA((n_dp, 2)),
            pltpu.SemaphoreType.DMA((n_dp, 2)),
        ]
    flops = 2 * sz.rows * sz.width * sz.width + 2 * sz.seq_len * sz.width * qkv.shape[1]
    return pl.pallas_call(
        partial(attn_kernel, sz, n_dp, keep),
        out_shape=outs,
        in_specs=[full_spec()] * 6 + [any_spec()] * (3 + len(embed)),
        out_specs=[full_spec()] + [any_spec()] * (len(outs) - 1),
        scratch_shapes=scratch,
        compiler_params=pltpu.CompilerParams(
            collective_id=2 if keep else 1, has_side_effects=True, vmem_limit_bytes=VMEM_BYTES
        ),
        cost_estimate=pl.CostEstimate(
            flops=flops, bytes_accessed=20 << 20, transcendentals=0
        ),
        name="attn_keep" if keep else "attn_round",
    )(latent, embed_part, gains, cos_t, sin_t, begin, adapter, qkv, out, *embed)


def ffn_kernel(sz, keep, *refs):
    (mixed, latent, active, gains, gate_hbm, up_hbm, down_hbm, result) = refs[:8]
    refs = refs[8:]
    if keep:
        rows_out, gate_out, up_out, hidden_out = refs[:4]
        refs = refs[4:]
    wg, wu, wd, rows_s = refs[:4]
    refs = refs[4:]
    if keep:
        gate_s, up_s, hidden_s = refs[:3]
        refs = refs[3:]
    load_gu, load_down, keep_sem = refs[:3]
    gather_refs = refs[3:5]
    scatter_refs = refs[5:]

    place = Place(sz)
    gate_load = pltpu.make_async_copy(gate_hbm, wg, load_gu.at[0])
    up_load = pltpu.make_async_copy(up_hbm, wu, load_gu.at[1])
    down_loads = column_loads(down_hbm, wd, load_down)
    gate_load.start()
    up_load.start()
    for copy in down_loads:
        copy.start()
    place.enter()
    gather = Gather(place, rows_s, *gather_refs)
    scatter = Scatter(place, *scatter_refs)
    for j in range(sz.seqs):
        span = slice(j * sz.block, (j + 1) * sz.block)
        rows = mixed[span, :]
        normed = (rows * rms_factor(rows)) * gains[1:2, :]
        rows_s[gather.own(j), :] = normed.astype(jnp.bfloat16)
        gather.start(j)
    gate_load.wait()
    up_load.wait()
    for copy in down_loads:
        copy.wait()

    copies = []

    def save(src, dst):
        copy = pltpu.make_async_copy(src, dst, keep_sem.at[len(copies)])
        copy.start()
        copies.append(copy)

    def work(q, j):
        rows = place.tile(q, j)
        x = rows_s[rows, :]
        gate = nn_dot(x, wg[...])
        up = nn_dot(x, wu[...])
        hidden = (gate / (1.0 + jnp.exp(-gate)) * up).astype(jnp.bfloat16)
        if keep:
            gate_s[rows, :] = gate.astype(jnp.bfloat16)
            up_s[rows, :] = up.astype(jnp.bfloat16)
            hidden_s[rows, :] = hidden
        scatter.part[...] = nn_dot(hidden, wd[...])
        scatter.give(q, j)

    far = range(1, sz.half)
    for j in range(sz.seqs):
        gather.wait_near(j)
        work(0, j)
    for j in range(sz.seqs):
        for q in far:
            gather.forward(q, j)
        for q in far:
            gather.wait_far(sz.half - q, j)
            work(q, j)
        for q in far:
            scatter.onward(q, j)
    if keep:
        save(rows_s, rows_out)
        save(gate_s, gate_out)
        save(up_s, up_out)
        save(hidden_s, hidden_out)
    gather.finish()
    for j in range(sz.seqs):
        span = slice(j * sz.block, (j + 1) * sz.block)
        total = mixed[span, :] + scatter.total(j)
        if not keep:
            total = jnp.where(active[...] > 0, total, latent[span, :])
        result[span, :] = total
    scatter.finish()
    for copy in copies:
        copy.wait()


def run_ffn(sz, keep, mixed, latent, active, gains, gate, up, down):
    f32, bf16 = jnp.float32, jnp.bfloat16
    shape = jax.ShapeDtypeStruct
    outs = [shape((sz.rows, sz.width), f32)]
    if keep:
        outs += [
            shape((sz.seq_len, sz.width), bf16),
            shape((sz.seq_len, sz.ff), bf16),
            shape((sz.seq_len, sz.ff), bf16),
            shape((sz.seq_len, sz.ff), bf16),
        ]
    scratch = [
        pltpu.VMEM(gate.shape, bf16),
        pltpu.VMEM(up.shape, bf16),
        pltpu.VMEM((sz.ff, sz.width), bf16),
        pltpu.VMEM((sz.seq_len, sz.width), bf16),
    ]
    if keep:
        scratch += [pltpu.VMEM((sz.seq_len, sz.ff), bf16)] * 3
    scratch += [
        pltpu.SemaphoreType.DMA((2,)),
        pltpu.SemaphoreType.DMA((down.shape[0],)),
        pltpu.SemaphoreType.DMA((4,)),
    ]
    scratch += Gather.scratch(sz) + Scatter.scratch(sz)
    return pl.pallas_call(
        partial(ffn_kernel, sz, keep),
        out_shape=outs,
        in_specs=[full_spec()] * 4 + [any_spec()] * 3,
        out_specs=[full_spec()] + [any_spec()] * (len(outs) - 1),
        scratch_shapes=scratch,
        compiler_params=pltpu.CompilerParams(
            collective_id=4 if keep else 3, has_side_effects=True, vmem_limit_bytes=VMEM_BYTES
        ),
        cost_estimate=pl.CostEstimate(
            flops=6 * sz.seq_len * sz.width * sz.ff, bytes_accessed=20 << 20, transcendentals=0
        ),
        name="ffn_keep" if keep else "ffn_round",
    )(mixed, latent, active, gains, gate, up, down)


def rounds_kernel(sz, count, *refs):
    (active, gains, cos_t, sin_t, begin) = refs[:5]
    (latent_hbm, embed_hbm, adapter_hbm, qkv_hbm, out_hbm, gate_hbm, up_hbm, down_hbm) = refs[5:13]
    result = refs[13]
    (wide, narrow, wg, wu, wd, embed, mixed, rows_s, q_s, k_s, v_s, head_s) = refs[14:26]
    load_rows, load_a, load_qkv, load_out, load_gu, load_down = refs[26:32]
    gather_refs, again_refs, scatter_refs = refs[32:34], refs[34:36], refs[36:44]
    columns = sz.width // 4
    depth_out = sz.heads * sz.head_dim

    place = Place(sz)
    row_loads = [
        pltpu.make_async_copy(latent_hbm, result, load_rows.at[0]),
        pltpu.make_async_copy(embed_hbm, embed, load_rows.at[1]),
    ]

    def adapter_columns(n):
        return wide.at[:, pl.ds(n * columns, columns)] if n < 3 else narrow

    tops = load_a.shape[1]
    depth = sz.width // tops
    a_loads = [
        [
            pltpu.make_async_copy(
                adapter_hbm.at[b, pl.ds(0, depth), pl.ds(n * columns, columns)],
                adapter_columns(n).at[pl.ds(b * depth, depth)],
                load_a.at[n, b],
            )
            for b in range(tops)
        ]
        for n in range(4)
    ]
    wqkv = wide.at[:, pl.ds(0, qkv_hbm.shape[1])]
    qkv_load = pltpu.make_async_copy(qkv_hbm, wqkv, load_qkv)
    out_loads = []
    for b in range(out_hbm.shape[0]):
        size = min(out_hbm.shape[2], columns)
        for at in range(0, out_hbm.shape[2], size):
            n, to = divmod(b * out_hbm.shape[2] + at, columns)
            out_loads.append(
                pltpu.make_async_copy(
                    out_hbm.at[b, :, pl.ds(at, size)],
                    narrow.at[pl.ds(n * depth_out, depth_out), pl.ds(to, size)],
                    load_out.at[len(out_loads)],
                )
            )
    ffn_loads = [
        pltpu.make_async_copy(gate_hbm, wg, load_gu.at[0]),
        pltpu.make_async_copy(up_hbm, wu, load_gu.at[1]),
    ] + column_loads(down_hbm, wd, load_down)

    def start_adapter():
        for group in a_loads:
            for copy in group:
                copy.start()

    def start_heads():
        qkv_load.start()
        for copy in out_loads:
            copy.start()

    for copy in row_loads:
        copy.start()
    start_adapter()
    place.enter()
    gather = Gather(place, rows_s, *gather_refs)
    again = Gather(place, rows_s, *again_refs)
    scatter = Scatter(place, *scatter_refs)
    for copy in row_loads:
        copy.wait()

    def spans(j):
        return slice(j * sz.block, (j + 1) * sz.block)

    def open_block(j):
        low = result[spans(j), :].astype(jnp.bfloat16)
        square = None
        for n, group in enumerate(a_loads):
            if j == 0:
                for copy in group:
                    copy.wait()
            cols = slice(n * columns, (n + 1) * columns)
            chunk = nn_dot(low, adapter_columns(n)[...]) + embed[spans(j), cols]
            mixed[spans(j), cols] = chunk
            here = jnp.sum(chunk * chunk, axis=-1, keepdims=True)
            square = here if square is None else square + here
        factor = lax.rsqrt(square / sz.width + norm_eps)
        normed = (mixed[spans(j), :] * factor) * gains[0:1, :]
        rows_s[gather.own(j), :] = normed.astype(jnp.bfloat16)
        gather.start(j)

    for j in range(sz.seqs):
        open_block(j)
    start_heads()
    for copy in ffn_loads:
        copy.start()
    pair = min(2, sz.heads)
    d = sz.head_dim

    def project(q, j):
        rows = place.tile(q, j)
        x = rows_s[rows, :]
        cos_here, sin_here = cos_t[rows, :], sin_t[rows, :]
        for h0 in range(0, sz.heads, pair):
            proj = nn_dot(x, wqkv[:, 3 * d * h0 : 3 * d * (h0 + pair)])
            for h in range(pair):
                at = 3 * d * h
                q_s[h0 + h, rows, :] = turn(proj[:, at : at + d], cos_here, sin_here).astype(
                    jnp.bfloat16
                )
                k_s[h0 + h, rows, :] = turn(
                    proj[:, at + d : at + 2 * d], cos_here, sin_here
                ).astype(jnp.bfloat16)
                v_s[h0 + h, rows, :] = proj[:, at + 2 * d : at + 3 * d].astype(jnp.bfloat16)

    def attend(q, j):
        rows = place.tile(q, j)
        first = (place.ahead(q) + j * sz.half) * sz.tile
        length = (j + 1) * sz.half * sz.tile
        start = begin[:, pl.ds(pl.multiple_of(first, sz.tile), sz.tile)]
        key_at = lax.broadcasted_iota(jnp.int32, (length, sz.tile), 0)
        query_at = first + lax.broadcasted_iota(jnp.int32, (1, sz.tile), 1)
        allowed = (key_at >= start) & (key_at <= query_at)

        def head(h, carry):
            scores = nt_dot(k_s[h, 0:length, :], q_s[h, rows, :])
            scores = jnp.where(allowed, scores * (LOG2E / math.sqrt(d)), masked_score)
            top = jnp.max(scores, axis=0, keepdims=True)
            weight = jnp.exp2(scores - top)
            total = jnp.sum(weight, axis=0, keepdims=True)
            mixed_t = tn_dot(v_s[h, 0:length, :], weight.astype(jnp.bfloat16))
            result = jnp.transpose(mixed_t / total)
            head_s[rows, pl.ds(pl.multiple_of(h * d, d), d)] = result.astype(jnp.bfloat16)
            return carry

        lax.fori_loop(0, sz.heads, head, 0)

    def give(q, j):
        rows = place.tile(q, j)
        for n in range(4):
            scatter.part[:, n * columns : (n + 1) * columns] = nn_dot(
                head_s[rows, :], narrow[n * depth_out : (n + 1) * depth_out, :]
            )
        scatter.give(q, j)

    def work(q, j):
        x = rows_s[place.tile(q, j), :]
        gate = nn_dot(x, wg[...])
        up = nn_dot(x, wu[...])
        hidden = (gate / (1.0 + jnp.exp(-gate)) * up).astype(jnp.bfloat16)
        scatter.part[...] = nn_dot(hidden, wd[...])
        scatter.give(q, j)

    far = range(1, sz.half)

    def one_round(r, carry):
        more = r + 1 < count
        qkv_load.wait()
        for j in range(sz.seqs):
            gather.wait_near(j)
            project(0, j)
        for copy in out_loads:
            copy.wait()
        for j in range(sz.seqs):
            for q in far:
                gather.forward(q, j)
            for q in far:
                gather.wait_far(sz.half - q, j)
                project(q, j)
            for q in far:
                attend(q, j)
                give(q, j)
            attend(0, j)
            gather.passed_on(j)
            for q in far:
                scatter.onward(q, j)
            give(0, j)
        gather.finish(forwards=False)
        pl.when(more)(start_adapter)
        for j in range(sz.seqs):
            rows = mixed[spans(j), :] + scatter.total(j)
            mixed[spans(j), :] = rows
            normed = (rows * rms_factor(rows)) * gains[1:2, :]
            rows_s[again.own(j), :] = normed.astype(jnp.bfloat16)
            again.start(j)
        scatter.finish()

        def first_loads():
            for copy in ffn_loads:
                copy.wait()

        pl.when(r == 0)(first_loads)
        for j in range(sz.seqs):
            again.wait_near(j)
            work(0, j)
        for j in range(sz.seqs):
            for q in far:
                again.forward(q, j)
            for q in far:
                again.wait_far(sz.half - q, j)
                work(q, j)
            again.passed_on(j)
            for q in far:
                scatter.onward(q, j)
        again.finish(forwards=False)
        on = active[pl.ds(r, 1), :] > 0
        for j in range(sz.seqs):
            total = mixed[spans(j), :] + scatter.total(j)
            result[spans(j), :] = jnp.where(on, total, result[spans(j), :])
            pl.when(more)(lambda j=j: open_block(j))
        pl.when(more)(start_heads)
        scatter.finish()
        return carry

    lax.fori_loop(0, count, one_round, 0)


def run_rounds(sz, latent, active, gains, cos_t, sin_t, begin, embed, adapter, qkv, out, gate, up, down):
    f32, bf16, dma = jnp.float32, jnp.bfloat16, pltpu.SemaphoreType.DMA
    heads_shape = (sz.heads, sz.seq_len, sz.head_dim)
    return pl.pallas_call(
        partial(rounds_kernel, sz, active.shape[0]),
        out_shape=jax.ShapeDtypeStruct((sz.rows, sz.width), f32),
        in_specs=[full_spec()] * 5 + [any_spec()] * 8,
        out_specs=full_spec(),
        scratch_shapes=[
            pltpu.VMEM((sz.width, max(3 * sz.width // 4, qkv.shape[1])), bf16),
            pltpu.VMEM((sz.width, sz.width // 4), bf16),
            pltpu.VMEM(gate.shape, bf16),
            pltpu.VMEM(up.shape, bf16),
            pltpu.VMEM((sz.ff, sz.width), bf16),
            pltpu.VMEM((sz.rows, sz.width), f32),
            pltpu.VMEM((sz.rows, sz.width), f32),
            pltpu.VMEM((sz.seq_len, sz.width), bf16),
            pltpu.VMEM(heads_shape, bf16),
            pltpu.VMEM(heads_shape, bf16),
            pltpu.VMEM(heads_shape, bf16),
            pltpu.VMEM((sz.seq_len, sz.heads * sz.head_dim), bf16),
            dma((2,)),
            dma((4, adapter.shape[0] // 2)),
            dma,
            dma((max(4, out.shape[0]),)),
            dma((2,)),
            dma((down.shape[0],)),
        ]
        + Gather.scratch(sz)
        + Gather.scratch(sz)
        + Scatter.scratch(sz),
        compiler_params=pltpu.CompilerParams(
            collective_id=1, has_side_effects=True, vmem_limit_bytes=VMEM_BYTES
        ),
        cost_estimate=pl.CostEstimate(
            flops=24 * sz.seq_len * sz.width * sz.ff, bytes_accessed=80 << 20, transcendentals=0
        ),
        name="rounds",
    )(active, gains, cos_t, sin_t, begin, latent, embed, adapter, qkv, out, gate, up, down)


def other_group(place):
    return (place.dp, (1 - place.group) * place.sz.half + place.part, place.ctx)


class Ring:
    def __init__(self, place, n_dp):
        self.place, self.count = place, n_dp
        self.at = self.swap(place.dp)

    def swap(self, i):
        if self.count != 4:
            return i
        x, y = lax.rem(i, 2), i // 2
        return 2 * y + x + y - 2 * x * y

    def index(self, offset):
        return self.swap(lax.rem(self.at + offset + 2 * self.count, self.count))

    def device(self, offset):
        return (self.index(offset), lax.axis_index("tensor"), self.place.ctx)


def weights_kernel(sz, n_dp, *refs):
    count = 5
    adapter_in, blocks_in = refs[0], refs[1 : 1 + count]
    rows_in, refs = refs[1 + count : 4 + count], refs[4 + count :]
    adapter_out, blocks_out = refs[0], refs[1 : 1 + count]
    embed_out, cot_out, cot_all, embed_part, state_out = refs[1 + count : 6 + count]
    refs = refs[6 + count :]
    (move_send, move_recv, ring_send, ring_recv, a_send, a_recv, x_send, x_recv, own_sem) = refs[:9]
    embed_s, state_s, weight_s, swap_send, swap_recv, keep_sem, weight_sem = refs[9:16]
    gather_refs = refs[16:]
    place = Place(sz)
    ring = Ring(place, n_dp)
    t = lax.axis_index("tensor")
    ctx, part, half, n_c = place.ctx, place.part, sz.half, sz.n_context
    role = part * n_c + ctx
    at_home = role == t
    steps = n_dp - 1
    sub = adapter_in.shape[0] // half
    ahead = 1 - 2 * ctx

    def holder(g):
        return (place.dp, g * half + t // n_c, lax.rem(t, n_c))

    barrier = pltpu.get_barrier_semaphore()

    def greet(device):
        pl.semaphore_signal(barrier, inc=1, device_id=device, device_id_type=MESH)

    greet(ring.device(1))
    greet(ring.device(n_dp - 1))
    greet(place.sibling())
    for q in range(1, half):
        greet(place.device(place.ahead(q), ctx))
    for c in range(n_c):
        pl.when(jnp.logical_not(at_home & (ctx == c)))(
            lambda c=c: greet((place.dp, role, c))
        )
    other = other_group(place)
    greet(other)
    waits = 3 + half + sz.seqs - jnp.where(at_home, 1, 0)
    pl.semaphore_wait(barrier, waits)

    own_at = pl.ds(pl.multiple_of(place.group * sz.block, sz.block), sz.block)
    other_at = pl.ds(pl.multiple_of((1 - place.group) * sz.block, sz.block), sz.block)
    rows_to = (embed_s, state_s, cot_out)

    def swap(i):
        return pltpu.make_async_remote_copy(
            src_ref=rows_in[i].at[1 - place.group],
            dst_ref=rows_to[i].at[own_at],
            send_sem=swap_send.at[i],
            recv_sem=swap_recv.at[i],
            device_id=other,
            device_id_type=MESH,
        )

    def swapped(i):
        ref = rows_to[i].at[other_at]
        return pltpu.make_async_remote_copy(
            src_ref=ref,
            dst_ref=ref,
            send_sem=swap_send.at[i],
            recv_sem=swap_recv.at[i],
            device_id=other,
            device_id_type=MESH,
        )

    def keep(i):
        return pltpu.make_async_copy(
            rows_in[i].at[place.group], rows_to[i].at[own_at], keep_sem.at[i]
        )

    for i in range(3):
        keep(i).start()
    gather = Gather(place, cot_all, *gather_refs)

    def own_rows_of(j):
        return pltpu.make_async_copy(
            cot_out.at[pl.ds(j * sz.block, sz.block)], cot_all.at[gather.own(j)], keep_sem.at[3 + j]
        )

    def move(w, g):
        slot = place.dp * n_c + ctx
        return pltpu.make_async_remote_copy(
            src_ref=blocks_in[w],
            dst_ref=blocks_out[w].at[slot],
            send_sem=move_send.at[w, g],
            recv_sem=move_recv.at[w, ctx],
            device_id=holder(g),
            device_id_type=MESH,
        )

    def stay(w):
        return pltpu.make_async_copy(
            blocks_in[w], blocks_out[w].at[place.dp * n_c + ctx], own_sem.at[w]
        )

    def moved(w, c):
        slot = place.dp * n_c + c
        arrival = pltpu.make_async_remote_copy(
            src_ref=blocks_in[w],
            dst_ref=blocks_out[w].at[slot],
            send_sem=move_send.at[w, 0],
            recv_sem=move_recv.at[w, c],
            device_id=place.sibling(),
            device_id_type=MESH,
        )
        here = at_home & (ctx == c)
        pl.when(here)(lambda: stay(w).wait())
        pl.when(jnp.logical_not(here))(lambda: arrival.wait_recv())

    def adapter_rows(offset, c, p):
        return adapter_out.at[
            ring.index(offset) * n_c + c, pl.ds(pl.multiple_of(p * sub, sub), sub)
        ]

    own_rows = adapter_in.at[pl.ds(pl.multiple_of(part * sub, sub), sub)]

    def around(s):
        rows = adapter_rows(-ahead * s, ctx, part)
        return pltpu.make_async_remote_copy(
            src_ref=own_rows if s == 0 else rows,
            dst_ref=rows,
            send_sem=a_send.at[s],
            recv_sem=a_recv.at[s],
            device_id=ring.device(ahead),
            device_id_type=MESH,
        )

    def across(kind, s):
        offset = -ahead * s
        if kind < half:
            dst = adapter_rows(offset, ctx, part)
            src = own_rows if s == 0 else dst
        else:
            src = dst = adapter_rows(offset, ctx, place.behind(kind - half + 1))
        target = place.device(place.ahead(kind), ctx) if 0 < kind < half else place.sibling()
        return pltpu.make_async_remote_copy(
            src_ref=src,
            dst_ref=dst,
            send_sem=x_send.at[kind, s],
            recv_sem=x_recv.at[kind, s],
            device_id=target,
            device_id_type=MESH,
        )

    def crossed(kind, s):
        if kind == 0:
            rows = adapter_rows(ahead * s, 1 - ctx, part)
        elif kind < half:
            rows = adapter_rows(-ahead * s, ctx, place.behind(kind))
        else:
            rows = adapter_rows(ahead * s, 1 - ctx, place.behind(kind - half + 1))
        return pltpu.make_async_remote_copy(
            src_ref=rows,
            dst_ref=rows,
            send_sem=x_send.at[kind, s],
            recv_sem=x_recv.at[kind, s],
            device_id=place.sibling(),
            device_id_type=MESH,
        )

    def hop(w, way, s):
        offset = -s if way == 0 else s
        rows = blocks_out[w].at[ring.index(offset) * n_c + way]
        return pltpu.make_async_remote_copy(
            src_ref=rows,
            dst_ref=rows,
            send_sem=ring_send.at[w, way, s],
            recv_sem=ring_recv.at[w, way, s],
            device_id=ring.device(1 if way == 0 else n_dp - 1),
            device_id_type=MESH,
        )

    def hopped(w, way, s):
        offset = -(s + 1) if way == 0 else s + 1
        rows = blocks_out[w].at[ring.index(offset) * n_c + way]
        return pltpu.make_async_remote_copy(
            src_ref=rows,
            dst_ref=rows,
            send_sem=ring_send.at[w, way, s],
            recv_sem=ring_recv.at[w, way, s],
            device_id=ring.device(1),
            device_id_type=MESH,
        )

    around(0).start()
    own = pltpu.make_async_copy(own_rows, adapter_rows(0, ctx, part), own_sem.at[count])
    own.start()

    def start_move(w):
        for g in range(sz.seqs):
            here = at_home & (place.group == g)
            pl.when(jnp.logical_not(here))(lambda w=w, g=g: move(w, g).start())
        pl.when(at_home)(lambda w=w: stay(w).start())

    for w in range(count):
        start_move(w)
    across(0, 0).start()
    swaps = []

    def across_z():
        if swaps:
            s = swaps.pop(0)
            for q in range(1, half):
                across(q, s).start()

    swaps.append(0)

    def adapter_step(s):
        if s < steps:
            arrival = pltpu.make_async_remote_copy(
                src_ref=own_rows,
                dst_ref=adapter_rows(-ahead * (s + 1), ctx, part),
                send_sem=a_send.at[s],
                recv_sem=a_recv.at[s],
                device_id=ring.device(1),
                device_id_type=MESH,
            )
            arrival.wait_recv()
            if s + 1 < steps:
                around(s + 1).start()
            across(0, s + 1).start()
            swaps.append(s + 1)

    def adapter_pass(s):
        for q in range(1, half):
            crossed(q, s).wait_recv()
            across(half - 1 + q, s).start()

    embed_save = pltpu.make_async_copy(embed_s, embed_out, keep_sem.at[3 + sz.seqs])
    todo = []
    for k in range(count + steps):
        for s in range(min(k, steps - 1), -1, -1):
            w = k - s
            if w < count:
                todo.append((w, s))
    done = 0
    for w, s in todo:
        for way in range(n_c):
            if s == 0:
                moved(w, way)
            else:
                hopped(w, way, s - 1).wait_recv()
            hop(w, way, s).start()
        if s == 0 and w >= 1:
            across_z()
        if s == 0 and w == count - 2:
            for i in range(3):
                swap(i).start()
        if done < steps:
            adapter_step(done)
        if s == min(1, steps - 1) and w == count - 1:
            for i in range(3):
                keep(i).wait()
                swapped(i).wait_recv()
            for j in range(sz.seqs):
                own_rows_of(j).start()
            embed_save.start()
            for j in range(sz.seqs):
                own_rows_of(j).wait()
                gather.start(j)
            state_out[...] = state_s[...].astype(jnp.float32)
        done += 1
    for s in range(done, steps):
        adapter_step(s)
    while swaps:
        across_z()
    for s in range(n_dp):
        adapter_pass(s)
    for j in range(sz.seqs):
        gather.wait_near(j)
        for q in range(1, half):
            gather.forward(q, j)
    for s in range(n_dp):
        crossed(0, s).wait_recv()
        for q in range(1, half):
            crossed(half - 1 + q, s).wait_recv()
    own.wait()
    slots, depth = adapter_out.shape[0], weight_s.shape[1]
    loads = [
        pltpu.make_async_copy(
            adapter_out.at[slots // 2 + b, pl.ds(0, depth)], weight_s.at[b % 2], weight_sem.at[b % 2]
        )
        for b in range(slots // 2)
    ]
    loads[0].start()
    for b, copy in enumerate(loads):
        if b + 1 < len(loads):
            loads[b + 1].start()
        copy.wait()
        part_here = nn_dot(embed_s[:, b * depth : (b + 1) * depth], weight_s[b % 2])
        if b:
            embed_part[...] += part_here
        else:
            embed_part[...] = part_here
    for w in range(count):
        for way in range(n_c):
            hopped(w, way, steps - 1).wait_recv()
    for j in range(sz.seqs):
        for q in range(1, half):
            gather.wait_far(q, j)
    gather.finish()
    embed_save.wait()
    for i in range(3):
        swap(i).wait_send()
    for w in range(count):
        for g in range(sz.seqs):
            here = at_home & (place.group == g)
            pl.when(jnp.logical_not(here))(lambda w=w, g=g: move(w, g).wait_send())
        for way in range(n_c):
            for s in range(steps):
                hop(w, way, s).wait_send()
    for s in range(steps):
        around(s).wait_send()
    for s in range(n_dp):
        for kind in range(2 * half - 1):
            across(kind, s).wait_send()


def run_weights(sz, n_dp, adapter, adapter_block, blocks, rows):
    bf16, f32 = jnp.bfloat16, jnp.float32
    slots = n_dp * sz.n_context
    outs = [jax.ShapeDtypeStruct((slots,) + a.shape, bf16) for a in [adapter] + blocks]
    outs += [
        jax.ShapeDtypeStruct((sz.rows, sz.width), bf16),
        jax.ShapeDtypeStruct((sz.rows, sz.width), bf16),
        jax.ShapeDtypeStruct((sz.seq_len, sz.width), bf16),
        jax.ShapeDtypeStruct((sz.rows, sz.width), f32),
        jax.ShapeDtypeStruct((sz.rows, sz.width), f32),
    ]
    count, steps, dma = len(blocks), n_dp - 1, pltpu.SemaphoreType.DMA
    kinds = 2 * sz.half - 1
    return pl.pallas_call(
        partial(weights_kernel, sz, n_dp),
        out_shape=outs,
        in_specs=[any_spec()] * (4 + count),
        out_specs=[any_spec()] * (4 + count) + [full_spec()] * 2,
        scratch_shapes=[
            dma((count, sz.seqs)),
            dma((count, sz.n_context)),
            dma((count, sz.n_context, steps)),
            dma((count, sz.n_context, steps)),
            dma((steps,)),
            dma((steps,)),
            dma((kinds, n_dp)),
            dma((kinds, n_dp)),
            dma((count + 1,)),
            pltpu.VMEM((sz.rows, sz.width), bf16),
            pltpu.VMEM((sz.rows, sz.width), bf16),
            pltpu.VMEM((2, adapter_block, sz.width), bf16),
            dma((3,)),
            dma((3,)),
            dma((4 + sz.seqs,)),
            dma((2,)),
        ]
        + Gather.scratch(sz),
        compiler_params=pltpu.CompilerParams(
            collective_id=5, has_side_effects=True, vmem_limit_bytes=VMEM_BYTES
        ),
        name="weights",
    )(adapter, *blocks, *rows)


def norm_back(grad, rows, factor, gain):
    unit = rows * factor
    weighted = grad * gain
    inner = jnp.mean(weighted * unit, axis=-1, keepdims=True)
    return factor * (weighted - unit * inner), jnp.sum(grad * unit, axis=0, keepdims=True)


class GradRing:
    @staticmethod
    def scratch(sz, n_dp, tasks, wide, own_rows=None):
        slots, ways, dma = n_dp * sz.n_context, sz.n_context, pltpu.SemaphoreType.DMA
        depth, bf16, count, last = sz.width // slots, jnp.bfloat16, len(wide), n_dp - 1
        own_rows = [True] * count if own_rows is None else own_rows
        hops = [[s for w, s in tasks if w == i] for i in range(count)]
        return (
            [pltpu.VMEM((sz.seq_len, n), bf16) for n, own in zip(wide, own_rows) if own]
            + [pltpu.VMEM((ways, depth, n) if 0 in h else (ways, 16, 128), bf16) for n, h in zip(wide, hops)]
            + [pltpu.VMEM((ways, min(max(h) + 1, last), depth, n), bf16) for n, h in zip(wide, hops)]
            + [
                pltpu.VMEM((2, ways, sz.seq_len, depth), bf16),
                dma((count,)),
                dma((2, ways)),
                dma((count, ways, last)),
                dma((count, ways, last)),
                dma((ways,)),
            ]
        )

    @staticmethod
    def size(wide, own_rows=None):
        return 2 * len(wide) + (len(wide) if own_rows is None else sum(own_rows)) + 6

    @staticmethod
    def all_tasks(n_dp, count):
        return [
            (k - s, s)
            for k in range(count + n_dp)
            for s in range(min(k, n_dp - 1), -1, -1)
            if k - s < count
        ]

    def __init__(self, sz, place, ring, tasks, xs, ys, refs, rows=None, given=None):
        count, refs = len(xs), list(refs)
        self.sz, self.place, self.ring, self.xs, self.count = sz, place, ring, xs, count
        self.tasks = tasks
        self.ys = [refs.pop(0) if ys[w] is not None else rows[w] for w in range(count)]
        self.first, self.held = refs[:count], refs[count : 2 * count]
        self.x_s, self.load_y, self.load_x, self.send, self.recv, load_given = refs[2 * count :]
        self.y_loads = [
            pltpu.make_async_copy(ys[w], self.ys[w], self.load_y.at[w])
            for w in range(count)
            if ys[w] is not None
        ]
        self.unread = {w: self.y_loads[i] for i, w in enumerate(
            w for w in range(count) if ys[w] is not None
        )}
        self.given = []
        if given is not None:
            self.given = [
                pltpu.make_async_copy(
                    given.at[way], self.held[0].at[way, tasks[0][1] - 1], load_given.at[way]
                )
                for way in range(sz.n_context)
            ]
        self.done = 0

    def start(self):
        for copy in self.y_loads + self.given:
            copy.start()
        for way in range(self.sz.n_context):
            self.x_load(0, way).start()

    def slot(self, way, s):
        return self.ring.index(-(s + 1) if way == 0 else s + 1) * self.sz.n_context + way

    def x_load(self, k, way):
        w, s = self.tasks[k]
        depth = self.x_s.shape[3]
        if self.xs[w].shape[0] == 1:
            at = pl.multiple_of(self.slot(way, s) * depth, depth)
            src = self.xs[w].at[0, :, pl.ds(at, depth)]
        else:
            src = self.xs[w].at[self.slot(way, s)]
        return pltpu.make_async_copy(src, self.x_s.at[k % 2, way], self.load_x.at[k % 2, way])

    def source(self, w, way, s):
        return self.first[w].at[way] if s == 0 else self.held[w].at[way, s - 1]

    def hop(self, w, way, s):
        return pltpu.make_async_remote_copy(
            src_ref=self.source(w, way, s),
            dst_ref=self.held[w].at[way, s],
            send_sem=self.send.at[w, way, s],
            recv_sem=self.recv.at[w, way, s],
            device_id=self.ring.device(1 if way == 0 else self.ring.count - 1),
            device_id_type=MESH,
        )

    def result(self, w, way):
        return self.source(w, way, self.ring.count - 1)

    def step(self):
        k = self.done
        self.done += 1
        w, s = self.tasks[k]
        ways = range(self.sz.n_context)
        if k + 1 < len(self.tasks):
            for way in ways:
                self.x_load(k + 1, way).start()
        if w in self.unread:
            self.unread.pop(w).wait()
        for way in ways:
            self.x_load(k, way).wait()
            value = tn_dot(self.x_s[k % 2, way], self.ys[w][...])
            if k == 0 and self.given:
                self.given[way].wait()
            elif s:
                self.hop(w, way, s - 1).wait_recv()
            if s:
                value = value + self.held[w][way, s - 1].astype(jnp.float32)
            ref = self.source(w, way, s)
            ref[...] = value.astype(jnp.bfloat16)
            if s < self.ring.count - 1:
                self.hop(w, way, s).start()
        return w, s == self.ring.count - 1

    def left(self):
        return len(self.tasks) - self.done

    def finish(self):
        for w, s in self.tasks:
            if s < self.ring.count - 1:
                for way in range(self.sz.n_context):
                    self.hop(w, way, s).wait_send()


class Deliver:
    @staticmethod
    def scratch(sz, n_dp, wide):
        depth, count, dma = sz.width // (n_dp * sz.n_context), len(wide), pltpu.SemaphoreType.DMA
        return [pltpu.VMEM((sz.seqs, depth, n), jnp.bfloat16) for n in wide] + [
            dma((count, sz.n_context)),
            dma((count, sz.seqs)),
            dma((count,)),
        ]

    def __init__(self, sz, place, refs):
        self.sz, self.place = sz, place
        self.landed = refs[:-3]
        self.send, self.recv, self.own = refs[-3:]
        self.count = len(self.landed)
        self.t = lax.axis_index("tensor")
        self.role = place.part * sz.n_context + place.ctx
        self.at_home = self.role == self.t
        self.sources = [None] * self.count

    def greet(self):
        sz, place = self.sz, self.place
        barrier = pltpu.get_barrier_semaphore()
        for g in range(sz.seqs):
            holder = (place.dp, g * sz.half + self.t // sz.n_context, lax.rem(self.t, sz.n_context))
            pl.when(jnp.logical_not(self.at_home & (place.group == g)))(
                lambda holder=holder: pl.semaphore_signal(
                    barrier, inc=1, device_id=holder, device_id_type=MESH
                )
            )
        return sz.n_context - jnp.where(self.at_home, 1, 0)

    def remote(self, w, way):
        return pltpu.make_async_remote_copy(
            src_ref=self.sources[w][way],
            dst_ref=self.landed[w].at[self.place.group],
            send_sem=self.send.at[w, way],
            recv_sem=self.recv.at[w, self.place.group],
            device_id=(self.place.dp, self.role, way),
            device_id_type=MESH,
        )

    def local(self, w, way):
        return pltpu.make_async_copy(
            self.sources[w][way], self.landed[w].at[self.place.group], self.own.at[w]
        )

    def start(self, w, sources):
        self.sources[w] = sources
        for way in range(self.sz.n_context):
            here = self.at_home & (self.place.ctx == way)
            pl.when(here)(lambda way=way: self.local(w, way).start())
            pl.when(jnp.logical_not(here))(lambda way=way: self.remote(w, way).start())

    def total(self, w):
        place = self.place
        for g in range(self.sz.seqs):
            ref = self.landed[w].at[g]
            arrival = pltpu.make_async_remote_copy(
                src_ref=ref,
                dst_ref=ref,
                send_sem=self.send.at[w, 0],
                recv_sem=self.recv.at[w, g],
                device_id=(place.dp, self.t, 1 - place.ctx),
                device_id_type=MESH,
            )
            here = self.at_home & (place.group == g)
            pl.when(here)(lambda: self.local(w, 0).wait())
            pl.when(jnp.logical_not(here))(lambda arrival=arrival: arrival.wait_recv())
        total = self.landed[w][0].astype(jnp.float32)
        for g in range(1, self.sz.seqs):
            total = total + self.landed[w][g].astype(jnp.float32)
        return total

    def finish(self):
        for w in range(self.count):
            for way in range(self.sz.n_context):
                here = self.at_home & (self.place.ctx == way)
                pl.when(jnp.logical_not(here))(lambda w=w, way=way: self.remote(w, way).wait_send())


def slot_columns(sz, n_dp, x):
    slots = n_dp * sz.n_context
    depth = sz.width // slots
    if depth % 128:
        return x.reshape(sz.seq_len, slots, depth).transpose(1, 0, 2)
    return x[None]


def ffn_back_kernel(sz, n_dp, *refs):
    (cot, mixed, gains) = refs[:3]
    (rows_hbm, gate_hbm, up_hbm, wg_hbm, wu_hbm, down_hbm) = refs[3:9]
    (x_hbm, normed_hbm, hidden_hbm) = refs[9:12]
    (grad_mixed, gain_grad, dgate_out, dup_out, down_sum, gate_part) = refs[12:18]
    (rows_s, gate_s, up_s, wg, wu, wd, load, load_down, keep_sem) = refs[18:27]
    scatter_refs, ring_refs = refs[27:35], refs[35:]
    place = Place(sz)
    ring = Ring(place, n_dp)
    grads = GradRing(
        sz, place, ring, ffn_back_tasks(n_dp), [x_hbm, normed_hbm], [hidden_hbm, None], ring_refs,
        rows=[None, gate_s],
    )
    grads.start()
    pairs = ((rows_hbm, rows_s), (gate_hbm, gate_s), (up_hbm, up_s), (wg_hbm, wg), (wu_hbm, wu))
    loads = [
        pltpu.make_async_copy(src, dst, load.at[i]) for i, (src, dst) in enumerate(pairs)
    ]
    down_loads = column_loads(down_hbm, wd, load_down)
    place.enter([ring.device(1), ring.device(n_dp - 1)])
    scatter = Scatter(place, *scatter_refs)
    for copy in [loads[0]] + down_loads + loads[1:]:
        copy.start()
    grads.step()
    for copy in [loads[0]] + down_loads + loads[1:]:
        copy.wait()

    def work(q, j):
        rows = place.tile(q, j)
        dh = nt_dot(rows_s[rows, :], wd[...])
        gate = gate_s[rows, :].astype(jnp.float32)
        up = up_s[rows, :].astype(jnp.float32)
        sig = 1.0 / (1.0 + jnp.exp(-gate))
        dgate = (dh * up * sig * (1.0 + gate * (1.0 - sig))).astype(jnp.bfloat16)
        dup = (dh * gate * sig).astype(jnp.bfloat16)
        gate_s[rows, :] = dgate
        up_s[rows, :] = dup
        scatter.part[...] = nt_dot(dgate, wg[...]) + nt_dot(dup, wu[...])
        scatter.give(q, j)

    far = range(1, sz.half)
    for j in range(sz.seqs):
        for q in far:
            work(q, j)
        if j:
            for q in far:
                scatter.onward(q, j - 1)
    grads.step()
    work(0, 0)
    for q in far:
        scatter.onward(q, sz.seqs - 1)
    for j in range(1, sz.seqs):
        work(0, j)
    grads.step()
    copies = [
        pltpu.make_async_copy(gate_s, dgate_out, keep_sem.at[0]),
        pltpu.make_async_copy(up_s, dup_out, keep_sem.at[1]),
    ]
    for copy in copies:
        copy.start()
    gain_total = None
    for j in range(sz.seqs):
        span = slice(j * sz.block, (j + 1) * sz.block)
        rows = mixed[span, :]
        grad, gain_here = norm_back(scatter.total(j), rows, rms_factor(rows), gains[1:2, :])
        grad_mixed[span, :] = cot[span, :].astype(jnp.float32) + grad
        gain_total = gain_here if gain_total is None else gain_total + gain_here
    gain_grad[...] = gain_total
    while grads.left():
        grads.step()
    for way in range(sz.n_context):
        grads.hop(1, way, 0).wait_recv()
        for i, (src, dst) in enumerate(
            ((grads.result(0, way), down_sum), (grads.held[1].at[way, 0], gate_part))
        ):
            copies.append(
                pltpu.make_async_copy(src, dst.at[way], keep_sem.at[2 + 2 * way + i])
            )
            copies[-1].start()
    scatter.finish()
    grads.finish()
    for copy in copies:
        copy.wait()


def ffn_back_tasks(n_dp):
    return [(0, 0), (0, 1), (1, 0)] + [(0, s) for s in range(2, n_dp)]


def run_ffn_back(sz, n_dp, cot, mixed, gains, rows, gate, up, wg, wu, down, normed, hidden):
    f32, bf16, shape = jnp.float32, jnp.bfloat16, jax.ShapeDtypeStruct
    dma = pltpu.SemaphoreType.DMA
    depth = sz.width // (n_dp * sz.n_context)
    return pl.pallas_call(
        partial(ffn_back_kernel, sz, n_dp),
        out_shape=[
            shape((sz.rows, sz.width), f32),
            shape((1, sz.width), f32),
            shape((sz.seq_len, sz.ff), bf16),
            shape((sz.seq_len, sz.ff), bf16),
            shape((sz.n_context, depth, sz.ff), bf16),
            shape((sz.n_context, depth, sz.ff), bf16),
        ],
        in_specs=[full_spec()] * 3 + [any_spec()] * 9,
        out_specs=[full_spec()] * 2 + [any_spec()] * 4,
        scratch_shapes=[
            pltpu.VMEM((sz.seq_len, sz.width), bf16),
            pltpu.VMEM((sz.seq_len, sz.ff), bf16),
            pltpu.VMEM((sz.seq_len, sz.ff), bf16),
            pltpu.VMEM(wg.shape, bf16),
            pltpu.VMEM(wu.shape, bf16),
            pltpu.VMEM((sz.ff, sz.width), bf16),
            dma((5,)),
            dma((down.shape[0],)),
            dma((2 + 2 * sz.n_context,)),
        ]
        + Scatter.scratch(sz)
        + GradRing.scratch(sz, n_dp, ffn_back_tasks(n_dp), [sz.ff, sz.ff], [True, False]),
        compiler_params=pltpu.CompilerParams(
            collective_id=6, has_side_effects=True, vmem_limit_bytes=VMEM_BYTES
        ),
        cost_estimate=pl.CostEstimate(
            flops=8 * sz.seq_len * sz.width * sz.ff, bytes_accessed=40 << 20, transcendentals=0
        ),
        name="ffn_back",
    )(
        cot, mixed, gains, rows, gate, up, wg, wu, down,
        slot_columns(sz, n_dp, rows), slot_columns(sz, n_dp, normed), hidden,
    )


def attn_back_kernel(sz, n_dp, *refs):
    (grad_mixed, gains, cos_t, sin_t, begin, gain_b, adapted_hbm, state_hbm) = refs[:8]
    (q_hbm, k_hbm, v_hbm, lse_hbm, out_hbm, qkv_hbm) = refs[8:14]
    (x_hbm, dgate_hbm, dup_hbm, down_sum, gate_part) = refs[14:19]
    (grad_low, down_grad, gate_grad, state_out, rows_out, proj_out, up_part) = refs[19:26]
    (rows_s, q_s, k_s, v_s, lse_s, do_s, dk_s, dv_s, proj_s, wout, wqkv) = refs[26:37]
    (load, load_out, keep_sem, swap_out, swap_in, swap_sem, late) = refs[37:44]
    gather_refs, scatter_refs = refs[44:46], refs[46:54]
    ring_refs, deliver_refs = refs[54:66], refs[66:]
    place = Place(sz)
    ring = Ring(place, n_dp)
    grads = GradRing(
        sz, place, ring, attn_back_tasks(n_dp), [x_hbm, x_hbm], [dgate_hbm, dup_hbm], ring_refs,
        given=gate_part,
    )
    deliver = Deliver(sz, place, deliver_refs)
    grads.start()
    split = wqkv.shape[0]
    pairs = (
        (q_hbm, q_s), (k_hbm, k_s), (v_hbm, v_s), (lse_hbm, lse_s),
        (qkv_hbm.at[pl.ds(split, split)], wqkv),
    )
    loads = [
        pltpu.make_async_copy(src, dst, load.at[i]) for i, (src, dst) in enumerate(pairs)
    ]
    out_loads = column_loads(out_hbm, wout, load_out)
    for copy in out_loads + loads:
        copy.start()
    targets = deliver.greet()
    other = other_group(place)
    place.enter([ring.device(1), ring.device(n_dp - 1), other], targets)
    gather = Gather(place, rows_s, *gather_refs)
    scatter = Scatter(place, *scatter_refs)
    for j in range(sz.seqs):
        span = slice(j * sz.block, (j + 1) * sz.block)
        rows_s[gather.own(j), :] = grad_mixed[span, :].astype(jnp.bfloat16)
        gather.start(j)
    grads.step()
    deliver.start(0, [down_sum.at[way] for way in range(sz.n_context)])
    give_rows = pl.ds(pl.multiple_of((1 - place.group) * sz.block, sz.block), sz.block)
    keep_rows = pl.ds(pl.multiple_of(place.group * sz.block, sz.block), sz.block)
    swap = pltpu.make_async_remote_copy(
        src_ref=swap_out,
        dst_ref=swap_in,
        send_sem=swap_sem.at[0],
        recv_sem=swap_sem.at[1],
        device_id=other,
        device_id_type=MESH,
    )
    state_load = pltpu.make_async_copy(
        state_hbm.at[give_rows], scatter.part.at[pl.ds(0, sz.block)], late.at[0]
    )
    state_keep = pltpu.make_async_copy(
        state_hbm.at[keep_rows], state_out.at[place.group], late.at[1]
    )
    state_load.start()
    state_keep.start()
    state_load.wait()
    swap_out[...] = scatter.part[: sz.block, :].astype(jnp.bfloat16)
    swap.start()
    for copy in out_loads:
        copy.wait()
    d = sz.head_dim

    def heads_grad(q, j):
        rows = place.tile(q, j)
        dhead = nt_dot(rows_s[rows, :], wout[...]).astype(jnp.bfloat16)
        for h in range(sz.heads):
            do_s[h, rows, :] = dhead[:, h * d : (h + 1) * d]

    far = range(1, sz.half)
    for j in range(sz.seqs):
        gather.wait_near(j)
        heads_grad(0, j)
    for copy in loads:
        copy.wait()
    for j in range(sz.seqs):
        if j == sz.seqs - 1:
            grads.step()
            grads.step()
        for q in far:
            gather.forward(q, j)
        for q in far:
            gather.wait_far(sz.half - q, j)
            heads_grad(q, j)
    rows_copy = pltpu.make_async_copy(rows_s, rows_out, keep_sem.at[0])
    rows_copy.start()
    gather.finish()
    rows_copy.wait()
    upper = rows_s.at[pl.ds(0, split), pl.ds(0, wqkv.shape[1])]
    upper_load = pltpu.make_async_copy(qkv_hbm.at[pl.ds(0, split)], upper, late.at[2])
    upper_load.start()

    tiles = sz.n_tensor
    scale = 1.0 / math.sqrt(d)

    def head(h, carry):
        for i in reversed(range(tiles)):
            rows = slice(i * sz.tile, (i + 1) * sz.tile)
            length = (i + 1) * sz.tile
            keys, values = k_s[h, 0:length, :], v_s[h, 0:length, :]
            query, grad = q_s[h, rows, :], do_s[h, rows, :]
            start = begin[:, rows]
            key_at = lax.broadcasted_iota(jnp.int32, (length, sz.tile), 0)
            query_at = i * sz.tile + lax.broadcasted_iota(jnp.int32, (1, sz.tile), 1)
            allowed = (key_at >= start) & (key_at <= query_at)
            scores = nt_dot(keys, query)
            scores = jnp.where(allowed, scores * (LOG2E * scale), masked_score)
            probs = jnp.exp2(scores - lse_s[h, :, rows])
            dprobs = nt_dot(values, grad)
            inner = jnp.sum(probs * dprobs, axis=0, keepdims=True)
            dscores = (probs * (dprobs - inner)).astype(jnp.bfloat16)
            dv = nn_dot(probs.astype(jnp.bfloat16), grad)
            dk = nn_dot(dscores, query)
            if i == tiles - 1:
                dv_s[...] = dv
                dk_s[...] = dk
            else:
                dv_s[0:length, :] += dv
                dk_s[0:length, :] += dk
            dq = jnp.transpose(tn_dot(keys, dscores)) * scale
            cos_here, sin_here = cos_t[rows, :], sin_t[rows, :]
            proj_s[rows, pl.ds(pl.multiple_of(h * 3 * d, d), d)] = turn(
                dq, cos_here, -sin_here
            ).astype(jnp.bfloat16)
        dk = turn(dk_s[...] * scale, cos_t[...], -sin_t[...])
        proj_s[:, pl.ds(pl.multiple_of(h * 3 * d + d, d), d)] = dk.astype(jnp.bfloat16)
        proj_s[:, pl.ds(pl.multiple_of(h * 3 * d + 2 * d, d), d)] = dv_s[...].astype(jnp.bfloat16)
        return carry

    lax.fori_loop(0, sz.heads // 2, head, 0)
    while grads.left() > 1:
        grads.step()
    deliver.start(1, [grads.result(0, way) for way in range(sz.n_context)])
    lax.fori_loop(sz.heads // 2, sz.heads, head, 0)
    copies = [pltpu.make_async_copy(proj_s, proj_out, keep_sem.at[1])]
    copies[0].start()
    upper_load.wait()

    def give(q, j):
        proj = proj_s[place.tile(q, j), :]
        scatter.part[:, :split] = nt_dot(proj, upper[...])
        scatter.part[:, split:] = nt_dot(proj, wqkv[...])
        scatter.give(q, j)

    for j in range(sz.seqs):
        for q in far:
            give(q, j)
        if j:
            for q in far:
                scatter.onward(q, j - 1)
    give(0, 0)
    for q in far:
        scatter.onward(q, sz.seqs - 1)
    for j in range(1, sz.seqs):
        give(0, j)
    adapted = scatter.part
    adapted_load = pltpu.make_async_copy(adapted_hbm, adapted, late.at[3])
    adapted_load.start()
    grads.step()
    swap.wait()
    state_keep.wait()
    adapted_load.wait()
    state_out[1 - place.group] = swap_in[...].astype(jnp.float32)
    down_grad[...] = jnp.transpose(deliver.total(0))
    gain_total = None
    for j in range(sz.seqs):
        span = slice(j * sz.block, (j + 1) * sz.block)
        rows = adapted[span, :]
        grad, gain_here = norm_back(scatter.total(j), rows, rms_factor(rows), gains[0:1, :])
        grad_low[span, :] = (grad_mixed[span, :] + grad).astype(jnp.bfloat16)
        gain_total = gain_here if gain_total is None else gain_total + gain_here
    extra = grad_low.shape[0] - sz.rows
    at_row = lax.broadcasted_iota(jnp.int32, (extra, sz.width), 0)
    shares = jnp.where(at_row == 0, gain_total, jnp.where(at_row == 1, gain_b[...], 0.0))
    grad_low[sz.rows :, :] = shares.astype(jnp.bfloat16)
    for way in range(sz.n_context):
        grads.hop(1, way, 1).wait_recv()
        copies.append(
            pltpu.make_async_copy(
                grads.held[1].at[way, 1], up_part.at[way], keep_sem.at[2 + way]
            )
        )
        copies[-1].start()
    gate_grad[...] = deliver.total(1)
    scatter.finish()
    grads.finish()
    deliver.finish()
    for copy in copies:
        copy.wait()


def attn_back_tasks(n_dp):
    return [(0, 1), (0, 2), (1, 0)] + [(0, s) for s in range(3, n_dp)] + [(1, 1)]


def run_attn_back(
    sz, n_dp, grad_mixed, adapted, gains, cos_t, sin_t, begin, gain_b, state, q, k, v, lse, out,
    qkv, x, dgate, dup, down_sum, gate_part,
):
    f32, bf16, shape = jnp.float32, jnp.bfloat16, jax.ShapeDtypeStruct
    dma = pltpu.SemaphoreType.DMA
    heads_shape = (sz.heads, sz.seq_len, sz.head_dim)
    return pl.pallas_call(
        partial(attn_back_kernel, sz, n_dp),
        out_shape=[
            shape((sz.rows + 16, sz.width), bf16),
            shape(down_sum.shape[:0:-1], f32),
            shape(gate_part.shape[1:], f32),
            shape((sz.seqs, sz.block, sz.width), f32),
            shape((sz.seq_len, sz.width), bf16),
            shape((sz.seq_len, qkv.shape[1]), bf16),
            shape(gate_part.shape, bf16),
        ],
        in_specs=[full_spec()] * 6 + [any_spec()] * 13,
        out_specs=[full_spec()] * 4 + [any_spec()] * 3,
        scratch_shapes=[
            pltpu.VMEM((sz.seq_len, sz.width), bf16),
            pltpu.VMEM(heads_shape, bf16),
            pltpu.VMEM(heads_shape, bf16),
            pltpu.VMEM(heads_shape, bf16),
            pltpu.VMEM((sz.heads, 1, sz.seq_len), f32),
            pltpu.VMEM(heads_shape, bf16),
            pltpu.VMEM((sz.seq_len, sz.head_dim), f32),
            pltpu.VMEM((sz.seq_len, sz.head_dim), f32),
            pltpu.VMEM((sz.seq_len, qkv.shape[1]), bf16),
            pltpu.VMEM((sz.heads * sz.head_dim, sz.width), bf16),
            pltpu.VMEM((sz.width // 2, qkv.shape[1]), bf16),
            dma((5,)),
            dma((out.shape[0],)),
            dma((2 + sz.n_context,)),
            pltpu.VMEM((sz.block, sz.width), bf16),
            pltpu.VMEM((sz.block, sz.width), bf16),
            dma((2,)),
            dma((4,)),
        ]
        + Gather.scratch(sz)
        + Scatter.scratch(sz)
        + GradRing.scratch(sz, n_dp, attn_back_tasks(n_dp), [sz.ff, sz.ff])
        + Deliver.scratch(sz, n_dp, [sz.ff, sz.ff]),
        compiler_params=pltpu.CompilerParams(
            collective_id=7, has_side_effects=True, vmem_limit_bytes=VMEM_BYTES
        ),
        cost_estimate=pl.CostEstimate(
            flops=4 * sz.seq_len * sz.width * qkv.shape[1], bytes_accessed=30 << 20, transcendentals=0
        ),
        name="attn_back",
    )(
        grad_mixed, gains, cos_t, sin_t, begin, gain_b, adapted, state, q, k, v, lse, out, qkv,
        slot_columns(sz, n_dp, x), dgate, dup, down_sum, gate_part,
    )


class PlaneRows:
    @staticmethod
    def scratch(n_dp):
        dma = pltpu.SemaphoreType.DMA
        return [dma((n_dp - 1,)), dma((n_dp - 1,)), dma((n_dp,)), dma((n_dp,))]

    def __init__(self, place, ring, own, landed, refs):
        self.place, self.ring, self.own, self.landed = place, ring, own, landed
        self.send, self.recv, self.near_send, self.near_recv = refs
        self.ahead = 1 - 2 * place.ctx

    def slot(self, offset, ctx):
        return self.landed.at[self.ring.index(offset) * self.place.sz.n_context + ctx]

    def source(self, s):
        return self.own if s == 0 else self.slot(-self.ahead * s, self.place.ctx)

    def hop(self, s):
        return pltpu.make_async_remote_copy(
            src_ref=self.source(s),
            dst_ref=self.slot(-self.ahead * s, self.place.ctx),
            send_sem=self.send.at[s],
            recv_sem=self.recv.at[s],
            device_id=self.ring.device(self.ahead),
            device_id_type=MESH,
        )

    def near(self, s):
        return pltpu.make_async_remote_copy(
            src_ref=self.source(s),
            dst_ref=self.slot(-self.ahead * s, self.place.ctx),
            send_sem=self.near_send.at[s],
            recv_sem=self.near_recv.at[s],
            device_id=self.place.sibling(),
            device_id_type=MESH,
        )

    def start(self):
        self.hop(0).start()
        self.near(0).start()

    def step(self, s):
        ref = self.slot(-self.ahead * (s + 1), self.place.ctx)
        pltpu.make_async_remote_copy(
            src_ref=ref,
            dst_ref=ref,
            send_sem=self.send.at[s],
            recv_sem=self.recv.at[s],
            device_id=self.place.sibling(),
            device_id_type=MESH,
        ).wait_recv()
        if s + 1 < self.ring.count - 1:
            self.hop(s + 1).start()
        self.near(s + 1).start()

    def wait_near(self, s):
        ref = self.slot(self.ahead * s, 1 - self.place.ctx)
        pltpu.make_async_remote_copy(
            src_ref=ref,
            dst_ref=ref,
            send_sem=self.near_send.at[s],
            recv_sem=self.near_recv.at[s],
            device_id=self.place.sibling(),
            device_id_type=MESH,
        ).wait_recv()

    def finish(self):
        for s in range(self.ring.count):
            if s < self.ring.count - 1:
                self.hop(s).wait_send()
            self.near(s).wait_send()


class LineSum:
    @staticmethod
    def scratch(sz, parts, chunk):
        dma, bf16 = pltpu.SemaphoreType.DMA, jnp.bfloat16
        far = pltpu.VMEM((max(sz.half - 1, 1), parts, chunk, sz.width), bf16)
        one = pltpu.VMEM((parts, chunk, sz.width), bf16)
        kinds = 2 * sz.half - 1
        return [far, far, one, one, one, far, dma((kinds, parts)), dma((kinds, parts))]

    def __init__(self, place, total, parts, refs):
        self.place, self.total, self.parts = place, total, parts
        (self.out, self.got, self.sum, self.cross, self.done, self.back, self.send, self.recv) = refs
        self.chunk = self.sum.shape[1]

    def rows(self, part, k):
        first = (part * self.parts + k) * self.chunk
        return pl.ds(pl.multiple_of(first, self.chunk), self.chunk)

    def copy(self, src, dst, kind, k, device):
        return pltpu.make_async_remote_copy(
            src_ref=src,
            dst_ref=dst,
            send_sem=self.send.at[kind, k],
            recv_sem=self.recv.at[kind, k],
            device_id=device,
            device_id_type=MESH,
        )

    def spread(self, q, k):
        place = self.place
        device = place.device(place.ahead(q), place.ctx)
        return self.copy(self.out.at[q - 1, k], self.got.at[q - 1, k], q, k, device)

    def swap(self, k):
        return self.copy(self.sum.at[k], self.cross.at[k], 0, k, other_group(self.place))

    def collect(self, q, k):
        place = self.place
        device = place.device(place.ahead(q), place.ctx)
        return self.copy(
            self.done.at[k], self.back.at[q - 1, k], place.sz.half - 1 + q, k, device
        )

    def start(self, k):
        for q in range(1, self.place.sz.half):
            rows = self.rows(self.place.ahead(q), k)
            self.out[q - 1, k] = self.total[rows, :].astype(jnp.bfloat16)
            self.spread(q, k).start()

    def cross_over(self, k):
        value = self.total[self.rows(self.place.part, k), :]
        for q in range(1, self.place.sz.half):
            self.spread(q, k).wait_recv()
            value = value + self.got[q - 1, k].astype(jnp.float32)
        self.sum[k] = value.astype(jnp.bfloat16)
        self.swap(k).start()

    def share(self, k):
        self.swap(k).wait_recv()
        value = self.sum[k].astype(jnp.float32) + self.cross[k].astype(jnp.float32)
        self.done[k] = value.astype(jnp.bfloat16)
        for q in range(1, self.place.sz.half):
            self.collect(q, k).start()
        self.total[self.rows(self.place.part, k), :] = self.done[k].astype(jnp.float32)

    def complete(self, k):
        for q in range(1, self.place.sz.half):
            self.collect(q, k).wait_recv()
            rows = self.rows(self.place.behind(q), k)
            self.total[rows, :] = self.back[q - 1, k].astype(jnp.float32)

    def finish(self):
        for k in range(self.parts):
            self.swap(k).wait_send()
            for q in range(1, self.place.sz.half):
                self.spread(q, k).wait_send()
                self.collect(q, k).wait_send()


SUM_PARTS = 2


def grads_kernel(sz, n_dp, count, *refs):
    n_in = 4 + 2 * count
    low, joined, adapter, up_part = refs[:4]
    gate_grad, refs = refs[4], refs[:4] + refs[5:]
    xs, ys = refs[4 : 4 + count], refs[4 + count : n_in]
    outs = refs[n_in : n_in + count]
    embed_grad, adapter_out, gains_out, landed = refs[n_in + count : n_in + 4 + count]
    refs = refs[n_in + 4 + count :]

    def take(n):
        nonlocal refs
        head, refs = refs[:n], refs[n:]
        return head

    ring_refs, deliver_refs = take(3 * count + 6), take(count + 3)
    plane_refs, sum_refs = take(4), take(8)
    adapter_grad, d_s, j_s, weight_s, rows_s, swap_in = refs[:6]
    d_sem, j_sem, weight_sem, swap_sem, out_sem = refs[6:]
    place = Place(sz)
    ring = Ring(place, n_dp)
    grads = GradRing(
        sz, place, ring, grads_tasks(n_dp, count), xs, ys, ring_refs, given=up_part
    )
    deliver = Deliver(sz, place, deliver_refs)
    plane = PlaneRows(place, ring, low, landed, plane_refs)
    line = LineSum(place, adapter_grad, SUM_PARTS, sum_refs)
    other = other_group(place)
    grads.start()
    weight_load = [
        pltpu.make_async_copy(
            adapter.at[adapter.shape[0] // 2 + b, pl.ds(0, weight_s.shape[0])], weight_s, weight_sem
        )
        for b in range(adapter.shape[0] // 2)
    ]
    weight_load[0].start()
    place.enter([ring.device(1), ring.device(n_dp - 1), other], deliver.greet())
    plane.start()
    give_rows = pl.ds(pl.multiple_of((1 - place.group) * sz.block, sz.block), sz.block)
    keep_rows = pl.ds(pl.multiple_of(place.group * sz.block, sz.block), sz.block)
    swap = pltpu.make_async_remote_copy(
        src_ref=low.at[give_rows],
        dst_ref=swap_in,
        send_sem=swap_sem.at[0],
        recv_sem=swap_sem.at[1],
        device_id=other,
        device_id_type=MESH,
    )
    swap.start()

    def ring_step():
        if grads.left():
            w, complete = grads.step()
            if complete:
                deliver.start(w, [grads.result(w, way) for way in range(sz.n_context)])

    depth = joined.shape[2]

    def batch(ctx):
        copies = []
        for d in range(n_dp):
            at = d * sz.n_context + ctx
            rows = pl.ds(d * sz.rows, sz.rows)
            copies.append(
                pltpu.make_async_copy(landed.at[at, pl.ds(0, sz.rows)], d_s.at[rows], d_sem.at[d, 0])
            )
            copies.append(pltpu.make_async_copy(joined.at[at], j_s.at[rows], j_sem.at[d]))
            copies.append(
                pltpu.make_async_copy(
                    landed.at[at, pl.ds(sz.rows, 16)],
                    d_s.at[pl.ds(n_dp * sz.rows + 16 * d, 16)],
                    d_sem.at[d, 1],
                )
            )
        return copies

    def product(ctx, first):
        copies = batch(ctx)
        for copy in copies:
            copy.start()
        for copy in copies:
            copy.wait()
        chunk = sz.width // 4
        for n in range(4):
            cols = slice(n * chunk, (n + 1) * chunk)
            value = tn_dot(j_s[...], d_s[: n_dp * sz.rows, cols])
            tail = d_s[n_dp * sz.rows : n_dp * sz.rows + 16, cols].astype(jnp.float32)
            for d in range(1, n_dp):
                at = n_dp * sz.rows + 16 * d
                tail = tail + d_s[at : at + 16, cols].astype(jnp.float32)
            if first:
                adapter_grad[:depth, cols] = value
                adapter_grad[depth : depth + 16, cols] = tail
            else:
                adapter_grad[:depth, cols] += value
                adapter_grad[depth : depth + 16, cols] += tail

    own = pltpu.make_async_copy(low, landed.at[place.dp * sz.n_context + place.ctx], d_sem.at[0, 0])
    own.start()
    rest = adapter_grad.shape[0] - depth - 16
    if rest:
        adapter_grad[depth + 16 :, :] = jnp.zeros((rest, sz.width), jnp.float32)
    for s in range(n_dp - 1):
        ring_step()
        plane.step(s)
    own.wait()
    product(place.ctx, True)
    for s in range(n_dp):
        plane.wait_near(s)
    product(1 - place.ctx, False)
    for k in range(SUM_PARTS):
        line.start(k)
    ring_step()
    ring_step()
    swap.wait()
    rows_s[place.group] = low[keep_rows, :]
    rows_s[1 - place.group] = swap_in[...]
    rows = rows_s[...].reshape(sz.rows, sz.width)
    ring_step()
    for k in range(SUM_PARTS):
        line.cross_over(k)
    ring_step()
    for b, copy in enumerate(weight_load):
        copy.wait()
        part = nt_dot(rows, weight_s[...]).reshape(sz.seqs, sz.block, weight_s.shape[0])
        embed_grad[:, :, b * weight_s.shape[0] : (b + 1) * weight_s.shape[0]] = part
        if b + 1 < len(weight_load):
            weight_load[b + 1].start()
    ring_step()
    for k in range(SUM_PARTS):
        line.share(k)
        ring_step()
    while grads.left():
        ring_step()
    for k in range(SUM_PARTS):
        line.complete(k)
    saves = [
        pltpu.make_async_copy(gate_grad, outs[0].at[0], out_sem.at[2]),
        pltpu.make_async_copy(adapter_grad.at[pl.ds(0, depth)], adapter_out, out_sem.at[0]),
        pltpu.make_async_copy(adapter_grad.at[pl.ds(depth, 16)], gains_out, out_sem.at[1]),
    ]
    for copy in saves:
        copy.start()
    outs[0][1] = deliver.total(0)
    outs[1][...] = deliver.total(1)
    outs[2][...] = jnp.transpose(deliver.total(2))
    for copy in saves:
        copy.wait()
    grads.finish()
    deliver.finish()
    plane.finish()
    line.finish()


def grads_tasks(n_dp, count):
    others = [(w + 1, s) for w, s in GradRing.all_tasks(n_dp, count - 1)]
    return [(0, s) for s in range(2, n_dp)] + others


def run_grads(sz, n_dp, low, joined, adapter, up_part, gate_grad, xs, ys):
    count, bf16, f32, dma = len(xs), jnp.bfloat16, jnp.float32, pltpu.SemaphoreType.DMA
    shape = jax.ShapeDtypeStruct
    depth = sz.width // (n_dp * sz.n_context)
    wide = [y.shape[1] for y in ys]
    slots, columns = joined.shape[0], joined.shape[2]
    unit = 16 * sz.half * SUM_PARTS
    total_rows = -(-(columns + 16) // unit) * unit
    return pl.pallas_call(
        partial(grads_kernel, sz, n_dp, count),
        out_shape=[
            shape((2, depth, wide[0]), f32),
            shape((depth, wide[1]), f32),
            shape((wide[2], depth), f32),
        ]
        + [
            shape((sz.seqs, sz.block, sz.width), f32),
            shape((columns, sz.width), f32),
            shape((16, sz.width), f32),
            shape((slots,) + low.shape, bf16),
        ],
        in_specs=[full_spec()] + [any_spec()] * (4 + 2 * count),
        out_specs=[full_spec()] * (1 + count) + [any_spec()] * 3,
        scratch_shapes=GradRing.scratch(sz, n_dp, grads_tasks(n_dp, count), wide)
        + Deliver.scratch(sz, n_dp, wide)
        + PlaneRows.scratch(n_dp)
        + LineSum.scratch(sz, SUM_PARTS, total_rows // (sz.half * SUM_PARTS))
        + [
            pltpu.VMEM((total_rows, sz.width), f32),
            pltpu.VMEM((n_dp * (sz.rows + 16), sz.width), bf16),
            pltpu.VMEM((n_dp * sz.rows, columns), bf16),
            pltpu.VMEM((columns, sz.width), bf16),
            pltpu.VMEM((sz.seqs, sz.block, sz.width), bf16),
            pltpu.VMEM((sz.block, sz.width), bf16),
            dma((n_dp, 2)),
            dma((n_dp,)),
            dma,
            dma((2,)),
            dma((3,)),
        ],
        compiler_params=pltpu.CompilerParams(
            collective_id=8, has_side_effects=True, vmem_limit_bytes=VMEM_BYTES
        ),
        cost_estimate=pl.CostEstimate(
            flops=2 * sz.seq_len * sz.width * sum(wide), bytes_accessed=60 << 20, transcendentals=0
        ),
        name="grads",
    )(low, joined, adapter, up_part, gate_grad, *[slot_columns(sz, n_dp, x) for x in xs], *ys)


def shards(
    embedded,
    initial_state,
    cotangent,
    doc_ids,
    recurrences,
    adapter_weight,
    norm_gains,
    qkv_weight,
    output_head_weight,
    gate_up_weight,
    down_weight,
):
    n_dp = lax.axis_size("dp")
    n_tensor = lax.axis_size("tensor")
    n_context = lax.axis_size("context")
    dp_index = lax.axis_index("dp")
    t_index = lax.axis_index("tensor")
    ctx_index = lax.axis_index("context")
    seq_count, block_rows, model_width = embedded.shape
    seq_len = doc_ids.shape[1]
    half = n_tensor // seq_count
    group = t_index // half
    part = t_index % half
    heads_here = qkv_weight.shape[1]
    head_dim = qkv_weight.shape[2] // 3
    ff_here = down_weight.shape[0]
    def side_by_side(blocks):
        count, depth, columns = blocks.shape
        return blocks.transpose(1, 0, 2).reshape(depth, count * columns)

    def role_grad(grad, axis):
        piece = lax.psum_scatter(
            grad.astype(jnp.bfloat16), "dp", scatter_dimension=axis, tiled=True
        )
        low, high = jnp.split(piece, 2, axis=axis)
        give = [jnp.where(group == 0, low, high), jnp.where(group == 0, high, low)]
        back = [
            lax.ppermute(g, ("tensor", "context"), [(b, a) for a, b in perm])
            for g, perm in zip(give, role_perms)
        ]
        return back[0].astype(jnp.float32) + back[1].astype(jnp.float32)

    def gather_rows(rows):
        full = lax.all_gather(
            rows, ("tensor", "context"), axis=0, tiled=True, axis_index_groups=groups
        )
        split = full.reshape(half, n_context, seq_count, block_rows, model_width)
        return split.transpose(2, 0, 1, 3, 4).reshape(seq_len, model_width)

    sz = Sizes(
        n_tensor,
        n_context,
        seq_count,
        half,
        block_rows,
        n_context * block_rows,
        seq_count * block_rows,
        seq_len,
        model_width,
        heads_here,
        head_dim,
        ff_here,
    )
    adapter_block = adapter_weight.shape[0]
    gain_columns = norm_gains.shape[1]
    unit = 16 * half
    padded = -(-(adapter_block + 2) // unit) * unit
    adapter_rows = jnp.concatenate(
        [
            adapter_weight,
            jnp.pad(
                norm_gains,
                ((0, padded - adapter_block - 2), (0, model_width - gain_columns)),
            ),
        ],
        axis=0,
    )
    (
        adapter_all,
        out_blocks,
        qkv_use,
        gate_use,
        up_use,
        down_blocks,
        embed_rows,
        cot_rows,
        grad_ffn,
        embed_part,
        current,
    ) = run_weights(
        sz,
        n_dp,
        adapter_rows,
        adapter_block,
        [
            output_head_weight.reshape(heads_here * head_dim, -1),
            qkv_weight.reshape(qkv_weight.shape[0], -1),
            gate_up_weight[:, 0],
            gate_up_weight[:, 1],
            down_weight,
        ],
        [embedded, initial_state, cotangent],
    )
    qkv_use = qkv_use.reshape(model_width, -1)
    gate_use = gate_use.reshape(model_width, -1)
    up_use = up_use.reshape(model_width, -1)
    gains_full = (
        adapter_all[:, adapter_block : adapter_block + 2, :gain_columns]
        .transpose(1, 0, 2)
        .reshape(2, model_width)
    )
    if out_blocks.shape[2] % 128:
        out_blocks = side_by_side(out_blocks)[None]
        down_blocks = side_by_side(down_blocks)[None]
    gains_f = gains_full.astype(jnp.float32)

    cos_full, sin_full = rope_tables(seq_len, head_dim)
    own_seq = dp_index * seq_count + group
    docs = lax.dynamic_index_in_dim(doc_ids, own_seq, 0, keepdims=False)
    begin = jnp.sum((docs[None, :] < docs[:, None]).astype(jnp.int32), axis=1)[None, :]
    steps_own = lax.dynamic_index_in_dim(recurrences, own_seq, 0, keepdims=False) - BACK
    active = jnp.arange(MAXR - BACK, dtype=jnp.int32)[:, None] < steps_own
    detached = run_rounds(
        sz,
        current,
        jnp.broadcast_to(active.astype(jnp.float32), (MAXR - BACK, model_width)),
        gains_f, cos_full, sin_full, begin, embed_part,
        adapter_all, qkv_use, out_blocks, gate_use, up_use, down_blocks,
    )
    (mixed_rows, adapted, feature_rows, query_hm, key_hm, value_hm, head_flat, lse, joined) = run_attn(
        sz, n_dp, True, detached, embed_part, gains_f, cos_full, sin_full, begin,
        adapter_all, qkv_use, out_blocks, embed_rows,
    )
    (current, ffn_input, gate_pre, up_pre, hidden) = run_ffn(
        sz, True, mixed_rows, detached, gains_f[:1], gains_f, gate_use, up_use, down_blocks
    )
    grad_mixed, gain_b, grad_gate, grad_up, down_sum, gate_part = run_ffn_back(
        sz, n_dp, cot_rows, mixed_rows, gains_f, grad_ffn, gate_pre, up_pre,
        gate_use, up_use, down_blocks, ffn_input, hidden,
    )
    grad_low, down_s, gate_s, state_out, grad_rows, grad_proj, up_part = run_attn_back(
        sz, n_dp, grad_mixed, adapted, gains_f, cos_full, sin_full, begin, gain_b, current,
        query_hm, key_hm, value_hm, lse, out_blocks, qkv_use, ffn_input, grad_gate, grad_up, down_sum,
        gate_part,
    )
    pair_s, qkv_s, out_s, embed_out, adapter_s, gains_rows, _ = run_grads(
        sz,
        n_dp,
        grad_low,
        joined,
        adapter_all,
        up_part,
        gate_s,
        [ffn_input, feature_rows, grad_rows],
        [grad_up, grad_proj, head_flat],
    )
    place_at = (dp_index * n_context + ctx_index) * gain_columns
    gains_s = lax.dynamic_slice_in_dim(gains_rows[:2], place_at, gain_columns, 1)
    out_s = out_s.reshape(heads_here, head_dim, -1)
    qkv_s = qkv_s.reshape(-1, heads_here, 3 * head_dim)
    gate_up_s = pair_s.transpose(1, 0, 2)
    return (state_out, embed_out, adapter_s, gains_s, qkv_s, out_s, gate_up_s, down_s)


def solution(mesh):
    placed = (
        P("dp", ("tensor", "context"), None),
        P("dp", ("tensor", "context"), None),
        P("dp", ("tensor", "context"), None),
        P(),
        P(),
        P(("dp", "context"), None),
        P(None, ("dp", "context")),
        P(("dp", "context"), "tensor", None),
        P("tensor", None, ("dp", "context")),
        P(("dp", "context"), None, "tensor"),
        P("tensor", ("dp", "context")),
    )
    return jax.shard_map(
        shards,
        mesh=mesh,
        in_specs=placed,
        out_specs=(
            P("dp", ("tensor", "context"), None),
            P("dp", ("tensor", "context"), None),
            P(("dp", "context"), None),
            P(None, ("dp", "context")),
            P(("dp", "context"), "tensor", None),
            P("tensor", None, ("dp", "context")),
            P(("dp", "context"), None, "tensor"),
            P("tensor", ("dp", "context")),
        ),
        check_vma=False,
    )
```

```python
from functools import partial
import math
from typing import NamedTuple

import jax
import jax.numpy as jnp
import numpy as np
from jax import lax
from jax.experimental import pallas as pl
from jax.experimental.pallas import tpu as pltpu
from jax.sharding import PartitionSpec as P

BACK = 1
MAXR = 4


rope_base = 50000.0
norm_eps = 1e-06
masked_score = -1e30


def rope_tables(seq_len, head_dim):
    freq_index = np.arange(head_dim // 2, dtype=np.float32)
    inv_freq = 1.0 / np.float32(rope_base) ** (np.float32(2.0) * freq_index / head_dim)
    angles = np.arange(seq_len, dtype=np.float32)[:, None] * inv_freq.astype(np.float32)[None, :]
    cos_t, sin_t = np.cos(angles), np.sin(angles)
    return (
        jnp.asarray(np.concatenate([cos_t, cos_t], axis=1), jnp.float32),
        jnp.asarray(np.concatenate([-sin_t, sin_t], axis=1), jnp.float32),
    )


MESH = pl.DeviceIdType.MESH
LOG2E = 1.4426950408889634
VMEM_BYTES = 62 << 20


class Sizes(NamedTuple):
    n_tensor: int
    n_context: int
    seqs: int
    half: int
    block: int
    tile: int
    rows: int
    seq_len: int
    width: int
    heads: int
    head_dim: int
    ff: int


def full_spec():
    return pl.BlockSpec(memory_space=pltpu.VMEM)


def any_spec():
    return pl.BlockSpec(memory_space=pl.ANY)


def nt_dot(a, b):
    return lax.dot_general(a, b, (((1,), (1,)), ((), ())), preferred_element_type=jnp.float32)


def tn_dot(a, b):
    return lax.dot_general(a, b, (((0,), (0,)), ((), ())), preferred_element_type=jnp.float32)


def nn_dot(a, b):
    return jnp.dot(a, b, preferred_element_type=jnp.float32)


class Place:
    def __init__(self, sz):
        t = lax.axis_index("tensor")
        self.sz = sz
        self.dp = lax.axis_index("dp")
        self.ctx = lax.axis_index("context")
        self.group = t // sz.half
        self.part = lax.rem(t, sz.half)

    def device(self, part, ctx):
        return (self.dp, self.group * self.sz.half + part, ctx)

    def ahead(self, q):
        return lax.rem(self.part + q, self.sz.half)

    def behind(self, q):
        return lax.rem(self.part + (self.sz.half - q), self.sz.half)

    def sibling(self):
        return self.device(self.part, 1 - self.ctx)

    def block(self, part, ctx, j):
        sz = self.sz
        first = ((part + j * sz.half) * sz.n_context + ctx) * sz.block
        return pl.ds(pl.multiple_of(first, sz.block), sz.block)

    def tile(self, q, j):
        sz = self.sz
        first = (self.ahead(q) + j * sz.half) * sz.tile
        return pl.ds(pl.multiple_of(first, sz.tile), sz.tile)

    def enter(self, others=(), more=0):
        barrier = pltpu.get_barrier_semaphore()
        for device in others:
            pl.semaphore_signal(barrier, inc=1, device_id=device, device_id_type=MESH)
        pl.semaphore_signal(
            barrier, inc=1, device_id=self.sibling(), device_id_type=MESH
        )
        for q in range(1, self.sz.half):
            pl.semaphore_signal(
                barrier,
                inc=1,
                device_id=self.device(self.ahead(q), self.ctx),
                device_id_type=MESH,
            )
        pl.semaphore_wait(barrier, self.sz.half + len(others) + more)


class Gather:
    @staticmethod
    def scratch(sz):
        kinds = 2 * sz.half - 1
        return [
            pltpu.SemaphoreType.DMA((kinds, sz.seqs)),
            pltpu.SemaphoreType.DMA((kinds, sz.seqs)),
        ]

    def __init__(self, place, ref, send, recv):
        self.place, self.ref, self.send, self.recv = place, ref, send, recv

    def copy(self, kind, j, rows):
        place, half = self.place, self.place.sz.half
        if 0 < kind < half:
            target = place.device(place.ahead(kind), place.ctx)
        else:
            target = place.sibling()
        return pltpu.make_async_remote_copy(
            src_ref=self.ref.at[rows],
            dst_ref=self.ref.at[rows],
            send_sem=self.send.at[kind, j],
            recv_sem=self.recv.at[kind, j],
            device_id=target,
            device_id_type=MESH,
        )

    def own(self, j):
        return self.place.block(self.place.part, self.place.ctx, j)

    def start(self, j):
        for q in range(1, self.place.sz.half):
            self.copy(q, j, self.own(j)).start()
        self.copy(0, j, self.own(j)).start()

    def wait_near(self, j):
        place = self.place
        self.copy(0, j, place.block(place.part, 1 - place.ctx, j)).wait_recv()

    def forward(self, q, j):
        place = self.place
        rows = place.block(place.behind(q), place.ctx, j)
        self.copy(q, j, rows).wait_recv()
        self.copy(place.sz.half - 1 + q, j, rows).start()

    def wait_far(self, q, j):
        place = self.place
        rows = place.block(place.behind(q), 1 - place.ctx, j)
        self.copy(place.sz.half - 1 + q, j, rows).wait_recv()

    def passed_on(self, j):
        place, half = self.place, self.place.sz.half
        for q in range(1, half):
            rows = place.block(place.behind(q), place.ctx, j)
            self.copy(half - 1 + q, j, rows).wait_send()

    def finish(self, forwards=True):
        for j in range(self.place.sz.seqs):
            for kind in range(self.place.sz.half):
                self.copy(kind, j, self.own(j)).wait_send()
            if forwards:
                self.passed_on(j)


class Scatter:
    @staticmethod
    def scratch(sz):
        kinds = 2 * sz.half - 1
        near = (sz.half, sz.seqs, sz.block, sz.width)
        far = (max(sz.half - 1, 1), sz.seqs, sz.block, sz.width)
        return [
            pltpu.VMEM((sz.tile, sz.width), jnp.float32),
            pltpu.VMEM(near, jnp.bfloat16),
            pltpu.VMEM(near, jnp.bfloat16),
            pltpu.VMEM(near, jnp.bfloat16),
            pltpu.VMEM(far, jnp.bfloat16),
            pltpu.VMEM(far, jnp.bfloat16),
            pltpu.SemaphoreType.DMA((kinds, sz.seqs)),
            pltpu.SemaphoreType.DMA((kinds, sz.seqs)),
        ]

    def __init__(self, place, part, mine, near_out, near_in, far_out, far_in, send, recv):
        self.place, self.part, self.mine = place, part, mine
        self.near_out, self.near_in = near_out, near_in
        self.far_out, self.far_in = far_out, far_in
        self.send, self.recv = send, recv

    def near(self, q, j):
        return pltpu.make_async_remote_copy(
            src_ref=self.near_out.at[q, j],
            dst_ref=self.near_in.at[q, j],
            send_sem=self.send.at[q, j],
            recv_sem=self.recv.at[q, j],
            device_id=self.place.sibling(),
            device_id_type=MESH,
        )

    def far(self, q, j):
        place = self.place
        return pltpu.make_async_remote_copy(
            src_ref=self.far_out.at[q - 1, j],
            dst_ref=self.far_in.at[q - 1, j],
            send_sem=self.send.at[place.sz.half - 1 + q, j],
            recv_sem=self.recv.at[place.sz.half - 1 + q, j],
            device_id=place.device(place.ahead(q), place.ctx),
            device_id_type=MESH,
        )

    def give(self, q, j):
        sz, ctx = self.place.sz, self.place.ctx
        mine = pl.ds(pl.multiple_of(ctx * sz.block, sz.block), sz.block)
        other = pl.ds(pl.multiple_of((1 - ctx) * sz.block, sz.block), sz.block)
        self.near_out[q, j] = self.part[other, :].astype(jnp.bfloat16)
        self.near(q, j).start()
        self.mine[q, j] = self.part[mine, :].astype(jnp.bfloat16)

    def onward(self, q, j):
        self.near(q, j).wait_recv()
        self.far_out[q - 1, j] = (
            self.mine[q, j].astype(jnp.float32) + self.near_in[q, j].astype(jnp.float32)
        ).astype(jnp.bfloat16)
        self.far(q, j).start()

    def total(self, j):
        self.near(0, j).wait_recv()
        total = self.mine[0, j].astype(jnp.float32) + self.near_in[0, j].astype(jnp.float32)
        for q in range(1, self.place.sz.half):
            self.far(q, j).wait_recv()
            total = total + self.far_in[q - 1, j].astype(jnp.float32)
        return total

    def finish(self):
        half = self.place.sz.half
        for j in range(self.place.sz.seqs):
            for q in range(half):
                self.near(q, j).wait_send()
            for q in range(1, half):
                self.far(q, j).wait_send()


def column_loads(blocks_ref, vmem_ref, sem):
    count, _, columns = blocks_ref.shape
    return [
        pltpu.make_async_copy(
            blocks_ref.at[b], vmem_ref.at[:, pl.ds(b * columns, columns)], sem.at[b]
        )
        for b in range(count)
    ]


def adapter_loads(blocks_ref, vmem_ref, sem):
    count, tops = sem.shape
    depth, columns = vmem_ref.shape[0] // tops, vmem_ref.shape[1] // count
    return [
        [
            pltpu.make_async_copy(
                blocks_ref.at[b, pl.ds(0, depth), pl.ds(n * columns, columns)],
                vmem_ref.at[pl.ds(b * depth, depth), pl.ds(n * columns, columns)],
                sem.at[n, b],
            )
            for b in range(tops)
        ]
        for n in range(count)
    ]


def rms_factor(rows):
    return lax.rsqrt(jnp.mean(rows * rows, axis=-1, keepdims=True) + norm_eps)


def turn(x, cos_t, sin_t):
    return x * cos_t + pltpu.roll(x, x.shape[-1] // 2, 1) * sin_t


def attn_kernel(sz, n_dp, keep, *refs):
    (latent, embed, gains, cos_t, sin_t, begin, adapter_hbm, qkv_hbm, out_hbm) = refs[:9]
    refs = refs[9:]
    if keep:
        embed_hbm, refs = refs[0], refs[1:]
    mixed = refs[0]
    refs = refs[1:]
    if keep:
        adapted_out, rows_out, q_out, k_out, v_out, head_out, lse_out, joined_out = refs[:8]
        refs = refs[8:]
    (wa, wqkv, wout, adapted, rows_s, q_s, k_s, v_s, head_s, lse_s) = refs[:10]
    load_a, load_qkv, load_out, keep_sem = refs[10:14]
    gather_refs = refs[14:16]
    scatter_refs = refs[16:24]
    if keep:
        joined_s, load_embed, x_send, x_recv = refs[24:]

    place = Place(sz)
    a_loads = adapter_loads(adapter_hbm, wa, load_a)
    qkv_load = pltpu.make_async_copy(qkv_hbm, wqkv, load_qkv)
    out_loads = column_loads(out_hbm, wout, load_out)
    for group in a_loads:
        for copy in group:
            copy.start()
    qkv_load.start()
    for copy in out_loads:
        copy.start()
    others = []
    if keep:
        ring = Ring(place, n_dp)
        t = lax.axis_index("tensor")
        embed_load = pltpu.make_async_copy(
            embed_hbm, joined_s.at[:, pl.ds(sz.width, sz.width)], load_embed
        )
        embed_load.start()
        plane = [(o, c) for o in range(n_dp) for c in range(2) if (o, c) != (0, 0)]

        def member(o, c):
            return (ring.index(o), t, place.ctx if c == 0 else 1 - place.ctx)

        def columns_to(o, c):
            to = member(o, c)
            depth = joined_out.shape[2]
            first = pl.multiple_of((to[0] * sz.n_context + to[2]) * depth, depth)
            return pltpu.make_async_remote_copy(
                src_ref=joined_s.at[:, pl.ds(first, depth)],
                dst_ref=joined_out.at[place.dp * sz.n_context + place.ctx],
                send_sem=x_send.at[o, c],
                recv_sem=x_recv.at[o, c],
                device_id=to,
                device_id_type=MESH,
            )

        def columns_from(o, c):
            ref = joined_out.at[
                ring.index(-o) * sz.n_context + (place.ctx if c == 0 else 1 - place.ctx)
            ]
            return pltpu.make_async_remote_copy(
                src_ref=ref,
                dst_ref=ref,
                send_sem=x_send.at[o, c],
                recv_sem=x_recv.at[o, c],
                device_id=place.sibling(),
                device_id_type=MESH,
            )

        others = [member(o, c) for o, c in plane if o]
    place.enter(others)
    gather = Gather(place, rows_s, *gather_refs)
    scatter = Scatter(place, *scatter_refs)

    low = latent[...].astype(jnp.bfloat16)
    columns = sz.width // len(a_loads)
    square = None
    for n, group in enumerate(a_loads):
        for copy in group:
            copy.wait()
        cols = pl.ds(n * columns, columns)
        chunk = nn_dot(low, wa[:, cols]) + embed[:, cols]
        adapted[:, cols] = chunk
        here = jnp.sum(chunk * chunk, axis=-1, keepdims=True)
        square = here if square is None else square + here
    factor = lax.rsqrt(square / sz.width + norm_eps)
    for j in range(sz.seqs):
        span = slice(j * sz.block, (j + 1) * sz.block)
        normed = (adapted[span, :] * factor[span]) * gains[0:1, :]
        rows_s[gather.own(j), :] = normed.astype(jnp.bfloat16)
        gather.start(j)

    qkv_load.wait()
    pair = min(2, sz.heads)
    d = sz.head_dim

    def project(q, j):
        rows = place.tile(q, j)
        x = rows_s[rows, :]
        cos_here, sin_here = cos_t[rows, :], sin_t[rows, :]
        for h0 in range(0, sz.heads, pair):
            proj = nn_dot(x, wqkv[:, 3 * d * h0 : 3 * d * (h0 + pair)])
            for h in range(pair):
                at = 3 * d * h
                q_s[h0 + h, rows, :] = turn(proj[:, at : at + d], cos_here, sin_here).astype(
                    jnp.bfloat16
                )
                k_s[h0 + h, rows, :] = turn(
                    proj[:, at + d : at + 2 * d], cos_here, sin_here
                ).astype(jnp.bfloat16)
                v_s[h0 + h, rows, :] = proj[:, at + 2 * d : at + 3 * d].astype(jnp.bfloat16)

    def attend(q, j):
        rows = place.tile(q, j)
        first = (place.ahead(q) + j * sz.half) * sz.tile
        length = (j + 1) * sz.half * sz.tile
        start = begin[:, pl.ds(pl.multiple_of(first, sz.tile), sz.tile)]
        key_at = lax.broadcasted_iota(jnp.int32, (length, sz.tile), 0)
        query_at = first + lax.broadcasted_iota(jnp.int32, (1, sz.tile), 1)
        allowed = (key_at >= start) & (key_at <= query_at)

        def head(h, carry):
            scores = nt_dot(k_s[h, 0:length, :], q_s[h, rows, :])
            scores = jnp.where(allowed, scores * (LOG2E / math.sqrt(d)), masked_score)
            top = jnp.max(scores, axis=0, keepdims=True)
            weight = jnp.exp2(scores - top)
            total = jnp.sum(weight, axis=0, keepdims=True)
            mixed_t = tn_dot(v_s[h, 0:length, :], weight.astype(jnp.bfloat16))
            result = jnp.transpose(mixed_t / total)
            head_s[rows, pl.ds(pl.multiple_of(h * d, d), d)] = result.astype(jnp.bfloat16)
            if keep:
                lse_s[h, :, rows] = top + jnp.log2(total)
            return carry

        lax.fori_loop(0, sz.heads, head, 0)

    def give(q, j):
        rows = place.tile(q, j)
        scatter.part[...] = nn_dot(head_s[rows, :], wout[...])
        scatter.give(q, j)

    copies = []

    def save(src, dst):
        copy = pltpu.make_async_copy(src, dst, keep_sem.at[len(copies)])
        copy.start()
        copies.append(copy)

    if keep:
        save(adapted, adapted_out)
        joined_s[:, : sz.width] = low
        embed_load.wait()
        for o, c in plane:
            columns_to(o, c).start()
        mine = place.dp * sz.n_context + place.ctx
        depth = joined_out.shape[2]
        save(
            joined_s.at[:, pl.ds(pl.multiple_of(mine * depth, depth), depth)], joined_out.at[mine]
        )
    far = range(1, sz.half)
    for j in range(sz.seqs):
        gather.wait_near(j)
        project(0, j)
    for copy in out_loads:
        copy.wait()
    for j in range(sz.seqs):
        for q in far:
            gather.forward(q, j)
        for q in far:
            gather.wait_far(sz.half - q, j)
            project(q, j)
        for q in far:
            attend(q, j)
            give(q, j)
        attend(0, j)
        for q in far:
            scatter.onward(q, j)
        give(0, j)
    if keep:
        for src, dst in ((rows_s, rows_out), (q_s, q_out), (k_s, k_out), (v_s, v_out)):
            save(src, dst)
        save(head_s, head_out)
        save(lse_s, lse_out)
    gather.finish()
    for j in range(sz.seqs):
        span = slice(j * sz.block, (j + 1) * sz.block)
        mixed[span, :] = adapted[span, :] + scatter.total(j)
    scatter.finish()
    if keep:
        for o, c in plane:
            columns_from(o, c).wait_recv()
            columns_to(o, c).wait_send()
    for copy in copies:
        copy.wait()


def run_attn(
    sz, n_dp, keep, latent, embed_part, gains, cos_t, sin_t, begin, adapter, qkv, out, *embed
):
    f32, bf16 = jnp.float32, jnp.bfloat16
    heads_shape = (sz.heads, sz.seq_len, sz.head_dim)
    shape = jax.ShapeDtypeStruct
    outs = [shape((sz.rows, sz.width), f32)]
    if keep:
        outs += [
            shape((sz.rows, sz.width), f32),
            shape((sz.seq_len, sz.width), bf16),
            shape(heads_shape, bf16),
            shape(heads_shape, bf16),
            shape(heads_shape, bf16),
            shape((sz.seq_len, sz.heads * sz.head_dim), bf16),
            shape((sz.heads, 1, sz.seq_len), f32),
            shape((adapter.shape[0], sz.rows, 2 * sz.width // adapter.shape[0]), bf16),
        ]
    scratch = [
        pltpu.VMEM((sz.width, sz.width), bf16),
        pltpu.VMEM(qkv.shape, bf16),
        pltpu.VMEM((sz.heads * sz.head_dim, sz.width), bf16),
        pltpu.VMEM((sz.rows, sz.width), f32),
        pltpu.VMEM((sz.seq_len, sz.width), bf16),
        pltpu.VMEM(heads_shape, bf16),
        pltpu.VMEM(heads_shape, bf16),
        pltpu.VMEM(heads_shape, bf16),
        pltpu.VMEM((sz.seq_len, sz.heads * sz.head_dim), bf16),
        pltpu.VMEM((sz.heads, 1, sz.seq_len), f32),
        pltpu.SemaphoreType.DMA((4, adapter.shape[0] // 2)),
        pltpu.SemaphoreType.DMA,
        pltpu.SemaphoreType.DMA((out.shape[0],)),
        pltpu.SemaphoreType.DMA((8,)),
    ]
    scratch += Gather.scratch(sz) + Scatter.scratch(sz)
    if keep:
        scratch += [
            pltpu.VMEM((sz.rows, 2 * sz.width), bf16),
            pltpu.SemaphoreType.DMA,
            pltpu.SemaphoreType.DMA((n_dp, 2)),
            pltpu.SemaphoreType.DMA((n_dp, 2)),
        ]
    flops = 2 * sz.rows * sz.width * sz.width + 2 * sz.seq_len * sz.width * qkv.shape[1]
    return pl.pallas_call(
        partial(attn_kernel, sz, n_dp, keep),
        out_shape=outs,
        in_specs=[full_spec()] * 6 + [any_spec()] * (3 + len(embed)),
        out_specs=[full_spec()] + [any_spec()] * (len(outs) - 1),
        scratch_shapes=scratch,
        compiler_params=pltpu.CompilerParams(
            collective_id=2 if keep else 1, has_side_effects=True, vmem_limit_bytes=VMEM_BYTES
        ),
        cost_estimate=pl.CostEstimate(
            flops=flops, bytes_accessed=20 << 20, transcendentals=0
        ),
        name="attn_keep" if keep else "attn_round",
    )(latent, embed_part, gains, cos_t, sin_t, begin, adapter, qkv, out, *embed)


def ffn_kernel(sz, keep, *refs):
    (mixed, latent, active, gains, gate_hbm, up_hbm, down_hbm, result) = refs[:8]
    refs = refs[8:]
    if keep:
        rows_out, gate_out, up_out, hidden_out = refs[:4]
        refs = refs[4:]
    wg, wu, wd, rows_s = refs[:4]
    refs = refs[4:]
    if keep:
        gate_s, up_s, hidden_s = refs[:3]
        refs = refs[3:]
    load_gu, load_down, keep_sem = refs[:3]
    gather_refs = refs[3:5]
    scatter_refs = refs[5:]

    place = Place(sz)
    gate_load = pltpu.make_async_copy(gate_hbm, wg, load_gu.at[0])
    up_load = pltpu.make_async_copy(up_hbm, wu, load_gu.at[1])
    down_loads = column_loads(down_hbm, wd, load_down)
    gate_load.start()
    up_load.start()
    for copy in down_loads:
        copy.start()
    place.enter()
    gather = Gather(place, rows_s, *gather_refs)
    scatter = Scatter(place, *scatter_refs)
    for j in range(sz.seqs):
        span = slice(j * sz.block, (j + 1) * sz.block)
        rows = mixed[span, :]
        normed = (rows * rms_factor(rows)) * gains[1:2, :]
        rows_s[gather.own(j), :] = normed.astype(jnp.bfloat16)
        gather.start(j)
    gate_load.wait()
    up_load.wait()
    for copy in down_loads:
        copy.wait()

    copies = []

    def save(src, dst):
        copy = pltpu.make_async_copy(src, dst, keep_sem.at[len(copies)])
        copy.start()
        copies.append(copy)

    def work(q, j):
        rows = place.tile(q, j)
        x = rows_s[rows, :]
        gate = nn_dot(x, wg[...])
        up = nn_dot(x, wu[...])
        hidden = (gate / (1.0 + jnp.exp(-gate)) * up).astype(jnp.bfloat16)
        if keep:
            gate_s[rows, :] = gate.astype(jnp.bfloat16)
            up_s[rows, :] = up.astype(jnp.bfloat16)
            hidden_s[rows, :] = hidden
        scatter.part[...] = nn_dot(hidden, wd[...])
        scatter.give(q, j)

    far = range(1, sz.half)
    for j in range(sz.seqs):
        gather.wait_near(j)
        work(0, j)
    for j in range(sz.seqs):
        for q in far:
            gather.forward(q, j)
        for q in far:
            gather.wait_far(sz.half - q, j)
            work(q, j)
        for q in far:
            scatter.onward(q, j)
    if keep:
        save(rows_s, rows_out)
        save(gate_s, gate_out)
        save(up_s, up_out)
        save(hidden_s, hidden_out)
    gather.finish()
    for j in range(sz.seqs):
        span = slice(j * sz.block, (j + 1) * sz.block)
        total = mixed[span, :] + scatter.total(j)
        if not keep:
            total = jnp.where(active[...] > 0, total, latent[span, :])
        result[span, :] = total
    scatter.finish()
    for copy in copies:
        copy.wait()


def run_ffn(sz, keep, mixed, latent, active, gains, gate, up, down):
    f32, bf16 = jnp.float32, jnp.bfloat16
    shape = jax.ShapeDtypeStruct
    outs = [shape((sz.rows, sz.width), f32)]
    if keep:
        outs += [
            shape((sz.seq_len, sz.width), bf16),
            shape((sz.seq_len, sz.ff), bf16),
            shape((sz.seq_len, sz.ff), bf16),
            shape((sz.seq_len, sz.ff), bf16),
        ]
    scratch = [
        pltpu.VMEM(gate.shape, bf16),
        pltpu.VMEM(up.shape, bf16),
        pltpu.VMEM((sz.ff, sz.width), bf16),
        pltpu.VMEM((sz.seq_len, sz.width), bf16),
    ]
    if keep:
        scratch += [pltpu.VMEM((sz.seq_len, sz.ff), bf16)] * 3
    scratch += [
        pltpu.SemaphoreType.DMA((2,)),
        pltpu.SemaphoreType.DMA((down.shape[0],)),
        pltpu.SemaphoreType.DMA((4,)),
    ]
    scratch += Gather.scratch(sz) + Scatter.scratch(sz)
    return pl.pallas_call(
        partial(ffn_kernel, sz, keep),
        out_shape=outs,
        in_specs=[full_spec()] * 4 + [any_spec()] * 3,
        out_specs=[full_spec()] + [any_spec()] * (len(outs) - 1),
        scratch_shapes=scratch,
        compiler_params=pltpu.CompilerParams(
            collective_id=4 if keep else 3, has_side_effects=True, vmem_limit_bytes=VMEM_BYTES
        ),
        cost_estimate=pl.CostEstimate(
            flops=6 * sz.seq_len * sz.width * sz.ff, bytes_accessed=20 << 20, transcendentals=0
        ),
        name="ffn_keep" if keep else "ffn_round",
    )(mixed, latent, active, gains, gate, up, down)


def rounds_kernel(sz, count, *refs):
    (active, gains, cos_t, sin_t, begin) = refs[:5]
    (latent_hbm, embed_hbm, adapter_hbm, qkv_hbm, out_hbm, gate_hbm, up_hbm, down_hbm) = refs[5:13]
    result = refs[13]
    (wide, narrow, wg, wu, wd, embed, mixed, rows_s, q_s, k_s, v_s, head_s) = refs[14:26]
    load_rows, load_a, load_qkv, load_out, load_gu, load_down = refs[26:32]
    gather_refs, again_refs, scatter_refs = refs[32:34], refs[34:36], refs[36:44]
    columns = sz.width // 4
    depth_out = sz.heads * sz.head_dim

    place = Place(sz)
    row_loads = [
        pltpu.make_async_copy(latent_hbm, result, load_rows.at[0]),
        pltpu.make_async_copy(embed_hbm, embed, load_rows.at[1]),
    ]

    def adapter_columns(n):
        return wide.at[:, pl.ds(n * columns, columns)] if n < 3 else narrow

    tops = load_a.shape[1]
    depth = sz.width // tops
    a_loads = [
        [
            pltpu.make_async_copy(
                adapter_hbm.at[b, pl.ds(0, depth), pl.ds(n * columns, columns)],
                adapter_columns(n).at[pl.ds(b * depth, depth)],
                load_a.at[n, b],
            )
            for b in range(tops)
        ]
        for n in range(4)
    ]
    wqkv = wide.at[:, pl.ds(0, qkv_hbm.shape[1])]
    qkv_load = pltpu.make_async_copy(qkv_hbm, wqkv, load_qkv)
    out_loads = []
    for b in range(out_hbm.shape[0]):
        size = min(out_hbm.shape[2], columns)
        for at in range(0, out_hbm.shape[2], size):
            n, to = divmod(b * out_hbm.shape[2] + at, columns)
            out_loads.append(
                pltpu.make_async_copy(
                    out_hbm.at[b, :, pl.ds(at, size)],
                    narrow.at[pl.ds(n * depth_out, depth_out), pl.ds(to, size)],
                    load_out.at[len(out_loads)],
                )
            )
    ffn_loads = [
        pltpu.make_async_copy(gate_hbm, wg, load_gu.at[0]),
        pltpu.make_async_copy(up_hbm, wu, load_gu.at[1]),
    ] + column_loads(down_hbm, wd, load_down)

    def start_adapter():
        for group in a_loads:
            for copy in group:
                copy.start()

    def start_heads():
        qkv_load.start()
        for copy in out_loads:
            copy.start()

    for copy in row_loads:
        copy.start()
    start_adapter()
    place.enter()
    gather = Gather(place, rows_s, *gather_refs)
    again = Gather(place, rows_s, *again_refs)
    scatter = Scatter(place, *scatter_refs)
    for copy in row_loads:
        copy.wait()

    def spans(j):
        return slice(j * sz.block, (j + 1) * sz.block)

    def open_block(j):
        low = result[spans(j), :].astype(jnp.bfloat16)
        square = None
        for n, group in enumerate(a_loads):
            if j == 0:
                for copy in group:
                    copy.wait()
            cols = slice(n * columns, (n + 1) * columns)
            chunk = nn_dot(low, adapter_columns(n)[...]) + embed[spans(j), cols]
            mixed[spans(j), cols] = chunk
            here = jnp.sum(chunk * chunk, axis=-1, keepdims=True)
            square = here if square is None else square + here
        factor = lax.rsqrt(square / sz.width + norm_eps)
        normed = (mixed[spans(j), :] * factor) * gains[0:1, :]
        rows_s[gather.own(j), :] = normed.astype(jnp.bfloat16)
        gather.start(j)

    for j in range(sz.seqs):
        open_block(j)
    start_heads()
    for copy in ffn_loads:
        copy.start()
    pair = min(2, sz.heads)
    d = sz.head_dim

    def project(q, j):
        rows = place.tile(q, j)
        x = rows_s[rows, :]
        cos_here, sin_here = cos_t[rows, :], sin_t[rows, :]
        for h0 in range(0, sz.heads, pair):
            proj = nn_dot(x, wqkv[:, 3 * d * h0 : 3 * d * (h0 + pair)])
            for h in range(pair):
                at = 3 * d * h
                q_s[h0 + h, rows, :] = turn(proj[:, at : at + d], cos_here, sin_here).astype(
                    jnp.bfloat16
                )
                k_s[h0 + h, rows, :] = turn(
                    proj[:, at + d : at + 2 * d], cos_here, sin_here
                ).astype(jnp.bfloat16)
                v_s[h0 + h, rows, :] = proj[:, at + 2 * d : at + 3 * d].astype(jnp.bfloat16)

    def attend(q, j):
        rows = place.tile(q, j)
        first = (place.ahead(q) + j * sz.half) * sz.tile
        length = (j + 1) * sz.half * sz.tile
        start = begin[:, pl.ds(pl.multiple_of(first, sz.tile), sz.tile)]
        key_at = lax.broadcasted_iota(jnp.int32, (length, sz.tile), 0)
        query_at = first + lax.broadcasted_iota(jnp.int32, (1, sz.tile), 1)
        allowed = (key_at >= start) & (key_at <= query_at)

        def head(h, carry):
            scores = nt_dot(k_s[h, 0:length, :], q_s[h, rows, :])
            scores = jnp.where(allowed, scores * (LOG2E / math.sqrt(d)), masked_score)
            top = jnp.max(scores, axis=0, keepdims=True)
            weight = jnp.exp2(scores - top)
            total = jnp.sum(weight, axis=0, keepdims=True)
            mixed_t = tn_dot(v_s[h, 0:length, :], weight.astype(jnp.bfloat16))
            result = jnp.transpose(mixed_t / total)
            head_s[rows, pl.ds(pl.multiple_of(h * d, d), d)] = result.astype(jnp.bfloat16)
            return carry

        lax.fori_loop(0, sz.heads, head, 0)

    def give(q, j):
        rows = place.tile(q, j)
        for n in range(4):
            scatter.part[:, n * columns : (n + 1) * columns] = nn_dot(
                head_s[rows, :], narrow[n * depth_out : (n + 1) * depth_out, :]
            )
        scatter.give(q, j)

    def work(q, j):
        x = rows_s[place.tile(q, j), :]
        gate = nn_dot(x, wg[...])
        up = nn_dot(x, wu[...])
        hidden = (gate / (1.0 + jnp.exp(-gate)) * up).astype(jnp.bfloat16)
        scatter.part[...] = nn_dot(hidden, wd[...])
        scatter.give(q, j)

    far = range(1, sz.half)

    def one_round(r, carry):
        more = r + 1 < count
        qkv_load.wait()
        for j in range(sz.seqs):
            gather.wait_near(j)
            project(0, j)
        for copy in out_loads:
            copy.wait()
        for j in range(sz.seqs):
            for q in far:
                gather.forward(q, j)
            for q in far:
                gather.wait_far(sz.half - q, j)
                project(q, j)
            for q in far:
                attend(q, j)
                give(q, j)
            attend(0, j)
            gather.passed_on(j)
            for q in far:
                scatter.onward(q, j)
            give(0, j)
        gather.finish(forwards=False)
        pl.when(more)(start_adapter)
        for j in range(sz.seqs):
            rows = mixed[spans(j), :] + scatter.total(j)
            mixed[spans(j), :] = rows
            normed = (rows * rms_factor(rows)) * gains[1:2, :]
            rows_s[again.own(j), :] = normed.astype(jnp.bfloat16)
            again.start(j)
        scatter.finish()

        def first_loads():
            for copy in ffn_loads:
                copy.wait()

        pl.when(r == 0)(first_loads)
        for j in range(sz.seqs):
            again.wait_near(j)
            work(0, j)
        for j in range(sz.seqs):
            for q in far:
                again.forward(q, j)
            for q in far:
                again.wait_far(sz.half - q, j)
                work(q, j)
            again.passed_on(j)
            for q in far:
                scatter.onward(q, j)
        again.finish(forwards=False)
        on = active[pl.ds(r, 1), :] > 0
        for j in range(sz.seqs):
            total = mixed[spans(j), :] + scatter.total(j)
            result[spans(j), :] = jnp.where(on, total, result[spans(j), :])
            pl.when(more)(lambda j=j: open_block(j))
        pl.when(more)(start_heads)
        scatter.finish()
        return carry

    lax.fori_loop(0, count, one_round, 0)


def run_rounds(sz, latent, active, gains, cos_t, sin_t, begin, embed, adapter, qkv, out, gate, up, down):
    f32, bf16, dma = jnp.float32, jnp.bfloat16, pltpu.SemaphoreType.DMA
    heads_shape = (sz.heads, sz.seq_len, sz.head_dim)
    return pl.pallas_call(
        partial(rounds_kernel, sz, active.shape[0]),
        out_shape=jax.ShapeDtypeStruct((sz.rows, sz.width), f32),
        in_specs=[full_spec()] * 5 + [any_spec()] * 8,
        out_specs=full_spec(),
        scratch_shapes=[
            pltpu.VMEM((sz.width, max(3 * sz.width // 4, qkv.shape[1])), bf16),
            pltpu.VMEM((sz.width, sz.width // 4), bf16),
            pltpu.VMEM(gate.shape, bf16),
            pltpu.VMEM(up.shape, bf16),
            pltpu.VMEM((sz.ff, sz.width), bf16),
            pltpu.VMEM((sz.rows, sz.width), f32),
            pltpu.VMEM((sz.rows, sz.width), f32),
            pltpu.VMEM((sz.seq_len, sz.width), bf16),
            pltpu.VMEM(heads_shape, bf16),
            pltpu.VMEM(heads_shape, bf16),
            pltpu.VMEM(heads_shape, bf16),
            pltpu.VMEM((sz.seq_len, sz.heads * sz.head_dim), bf16),
            dma((2,)),
            dma((4, adapter.shape[0] // 2)),
            dma,
            dma((max(4, out.shape[0]),)),
            dma((2,)),
            dma((down.shape[0],)),
        ]
        + Gather.scratch(sz)
        + Gather.scratch(sz)
        + Scatter.scratch(sz),
        compiler_params=pltpu.CompilerParams(
            collective_id=1, has_side_effects=True, vmem_limit_bytes=VMEM_BYTES
        ),
        cost_estimate=pl.CostEstimate(
            flops=24 * sz.seq_len * sz.width * sz.ff, bytes_accessed=80 << 20, transcendentals=0
        ),
        name="rounds",
    )(active, gains, cos_t, sin_t, begin, latent, embed, adapter, qkv, out, gate, up, down)


def other_group(place):
    return (place.dp, (1 - place.group) * place.sz.half + place.part, place.ctx)


class Ring:
    def __init__(self, place, n_dp):
        self.place, self.count = place, n_dp
        self.at = self.swap(place.dp)

    def swap(self, i):
        if self.count != 4:
            return i
        x, y = lax.rem(i, 2), i // 2
        return 2 * y + x + y - 2 * x * y

    def index(self, offset):
        return self.swap(lax.rem(self.at + offset + 2 * self.count, self.count))

    def device(self, offset):
        return (self.index(offset), lax.axis_index("tensor"), self.place.ctx)


def weights_kernel(sz, n_dp, *refs):
    count = 5
    adapter_in, blocks_in = refs[0], refs[1 : 1 + count]
    rows_in, refs = refs[1 + count : 4 + count], refs[4 + count :]
    adapter_out, blocks_out = refs[0], refs[1 : 1 + count]
    embed_out, cot_out, cot_all, embed_part, state_out = refs[1 + count : 6 + count]
    refs = refs[6 + count :]
    (move_send, move_recv, ring_send, ring_recv, a_send, a_recv, x_send, x_recv, own_sem) = refs[:9]
    embed_s, state_s, weight_s, swap_send, swap_recv, keep_sem, weight_sem = refs[9:16]
    gather_refs = refs[16:]
    place = Place(sz)
    ring = Ring(place, n_dp)
    t = lax.axis_index("tensor")
    ctx, part, half, n_c = place.ctx, place.part, sz.half, sz.n_context
    role = part * n_c + ctx
    at_home = role == t
    steps = n_dp - 1
    sub = adapter_in.shape[0] // half
    ahead = 1 - 2 * ctx

    def holder(g):
        return (place.dp, g * half + t // n_c, lax.rem(t, n_c))

    barrier = pltpu.get_barrier_semaphore()

    def greet(device):
        pl.semaphore_signal(barrier, inc=1, device_id=device, device_id_type=MESH)

    greet(ring.device(1))
    greet(ring.device(n_dp - 1))
    greet(place.sibling())
    for q in range(1, half):
        greet(place.device(place.ahead(q), ctx))
    for c in range(n_c):
        pl.when(jnp.logical_not(at_home & (ctx == c)))(
            lambda c=c: greet((place.dp, role, c))
        )
    other = other_group(place)
    greet(other)
    waits = 3 + half + sz.seqs - jnp.where(at_home, 1, 0)
    pl.semaphore_wait(barrier, waits)

    own_at = pl.ds(pl.multiple_of(place.group * sz.block, sz.block), sz.block)
    other_at = pl.ds(pl.multiple_of((1 - place.group) * sz.block, sz.block), sz.block)
    rows_to = (embed_s, state_s, cot_out)

    def swap(i):
        return pltpu.make_async_remote_copy(
            src_ref=rows_in[i].at[1 - place.group],
            dst_ref=rows_to[i].at[own_at],
            send_sem=swap_send.at[i],
            recv_sem=swap_recv.at[i],
            device_id=other,
            device_id_type=MESH,
        )

    def swapped(i):
        ref = rows_to[i].at[other_at]
        return pltpu.make_async_remote_copy(
            src_ref=ref,
            dst_ref=ref,
            send_sem=swap_send.at[i],
            recv_sem=swap_recv.at[i],
            device_id=other,
            device_id_type=MESH,
        )

    def keep(i):
        return pltpu.make_async_copy(
            rows_in[i].at[place.group], rows_to[i].at[own_at], keep_sem.at[i]
        )

    for i in range(3):
        keep(i).start()
    gather = Gather(place, cot_all, *gather_refs)

    def own_rows_of(j):
        return pltpu.make_async_copy(
            cot_out.at[pl.ds(j * sz.block, sz.block)], cot_all.at[gather.own(j)], keep_sem.at[3 + j]
        )

    def move(w, g):
        slot = place.dp * n_c + ctx
        return pltpu.make_async_remote_copy(
            src_ref=blocks_in[w],
            dst_ref=blocks_out[w].at[slot],
            send_sem=move_send.at[w, g],
            recv_sem=move_recv.at[w, ctx],
            device_id=holder(g),
            device_id_type=MESH,
        )

    def stay(w):
        return pltpu.make_async_copy(
            blocks_in[w], blocks_out[w].at[place.dp * n_c + ctx], own_sem.at[w]
        )

    def moved(w, c):
        slot = place.dp * n_c + c
        arrival = pltpu.make_async_remote_copy(
            src_ref=blocks_in[w],
            dst_ref=blocks_out[w].at[slot],
            send_sem=move_send.at[w, 0],
            recv_sem=move_recv.at[w, c],
            device_id=place.sibling(),
            device_id_type=MESH,
        )
        here = at_home & (ctx == c)
        pl.when(here)(lambda: stay(w).wait())
        pl.when(jnp.logical_not(here))(lambda: arrival.wait_recv())

    def adapter_rows(offset, c, p):
        return adapter_out.at[
            ring.index(offset) * n_c + c, pl.ds(pl.multiple_of(p * sub, sub), sub)
        ]

    own_rows = adapter_in.at[pl.ds(pl.multiple_of(part * sub, sub), sub)]

    def around(s):
        rows = adapter_rows(-ahead * s, ctx, part)
        return pltpu.make_async_remote_copy(
            src_ref=own_rows if s == 0 else rows,
            dst_ref=rows,
            send_sem=a_send.at[s],
            recv_sem=a_recv.at[s],
            device_id=ring.device(ahead),
            device_id_type=MESH,
        )

    def across(kind, s):
        offset = -ahead * s
        if kind < half:
            dst = adapter_rows(offset, ctx, part)
            src = own_rows if s == 0 else dst
        else:
            src = dst = adapter_rows(offset, ctx, place.behind(kind - half + 1))
        target = place.device(place.ahead(kind), ctx) if 0 < kind < half else place.sibling()
        return pltpu.make_async_remote_copy(
            src_ref=src,
            dst_ref=dst,
            send_sem=x_send.at[kind, s],
            recv_sem=x_recv.at[kind, s],
            device_id=target,
            device_id_type=MESH,
        )

    def crossed(kind, s):
        if kind == 0:
            rows = adapter_rows(ahead * s, 1 - ctx, part)
        elif kind < half:
            rows = adapter_rows(-ahead * s, ctx, place.behind(kind))
        else:
            rows = adapter_rows(ahead * s, 1 - ctx, place.behind(kind - half + 1))
        return pltpu.make_async_remote_copy(
            src_ref=rows,
            dst_ref=rows,
            send_sem=x_send.at[kind, s],
            recv_sem=x_recv.at[kind, s],
            device_id=place.sibling(),
            device_id_type=MESH,
        )

    def hop(w, way, s):
        offset = -s if way == 0 else s
        rows = blocks_out[w].at[ring.index(offset) * n_c + way]
        return pltpu.make_async_remote_copy(
            src_ref=rows,
            dst_ref=rows,
            send_sem=ring_send.at[w, way, s],
            recv_sem=ring_recv.at[w, way, s],
            device_id=ring.device(1 if way == 0 else n_dp - 1),
            device_id_type=MESH,
        )

    def hopped(w, way, s):
        offset = -(s + 1) if way == 0 else s + 1
        rows = blocks_out[w].at[ring.index(offset) * n_c + way]
        return pltpu.make_async_remote_copy(
            src_ref=rows,
            dst_ref=rows,
            send_sem=ring_send.at[w, way, s],
            recv_sem=ring_recv.at[w, way, s],
            device_id=ring.device(1),
            device_id_type=MESH,
        )

    around(0).start()
    own = pltpu.make_async_copy(own_rows, adapter_rows(0, ctx, part), own_sem.at[count])
    own.start()

    def start_move(w):
        for g in range(sz.seqs):
            here = at_home & (place.group == g)
            pl.when(jnp.logical_not(here))(lambda w=w, g=g: move(w, g).start())
        pl.when(at_home)(lambda w=w: stay(w).start())

    for w in range(count):
        start_move(w)
    across(0, 0).start()
    swaps = []

    def across_z():
        if swaps:
            s = swaps.pop(0)
            for q in range(1, half):
                across(q, s).start()

    swaps.append(0)

    def adapter_step(s):
        if s < steps:
            arrival = pltpu.make_async_remote_copy(
                src_ref=own_rows,
                dst_ref=adapter_rows(-ahead * (s + 1), ctx, part),
                send_sem=a_send.at[s],
                recv_sem=a_recv.at[s],
                device_id=ring.device(1),
                device_id_type=MESH,
            )
            arrival.wait_recv()
            if s + 1 < steps:
                around(s + 1).start()
            across(0, s + 1).start()
            swaps.append(s + 1)

    def adapter_pass(s):
        for q in range(1, half):
            crossed(q, s).wait_recv()
            across(half - 1 + q, s).start()

    embed_save = pltpu.make_async_copy(embed_s, embed_out, keep_sem.at[3 + sz.seqs])
    todo = []
    for k in range(count + steps):
        for s in range(min(k, steps - 1), -1, -1):
            w = k - s
            if w < count:
                todo.append((w, s))
    done = 0
    for w, s in todo:
        for way in range(n_c):
            if s == 0:
                moved(w, way)
            else:
                hopped(w, way, s - 1).wait_recv()
            hop(w, way, s).start()
        if s == 0 and w >= 1:
            across_z()
        if s == 0 and w == count - 2:
            for i in range(3):
                swap(i).start()
        if done < steps:
            adapter_step(done)
        if s == min(1, steps - 1) and w == count - 1:
            for i in range(3):
                keep(i).wait()
                swapped(i).wait_recv()
            for j in range(sz.seqs):
                own_rows_of(j).start()
            embed_save.start()
            for j in range(sz.seqs):
                own_rows_of(j).wait()
                gather.start(j)
            state_out[...] = state_s[...].astype(jnp.float32)
        done += 1
    for s in range(done, steps):
        adapter_step(s)
    while swaps:
        across_z()
    for s in range(n_dp):
        adapter_pass(s)
    for j in range(sz.seqs):
        gather.wait_near(j)
        for q in range(1, half):
            gather.forward(q, j)
    for s in range(n_dp):
        crossed(0, s).wait_recv()
        for q in range(1, half):
            crossed(half - 1 + q, s).wait_recv()
    own.wait()
    slots, depth = adapter_out.shape[0], weight_s.shape[1]
    loads = [
        pltpu.make_async_copy(
            adapter_out.at[slots // 2 + b, pl.ds(0, depth)], weight_s.at[b % 2], weight_sem.at[b % 2]
        )
        for b in range(slots // 2)
    ]
    loads[0].start()
    for b, copy in enumerate(loads):
        if b + 1 < len(loads):
            loads[b + 1].start()
        copy.wait()
        part_here = nn_dot(embed_s[:, b * depth : (b + 1) * depth], weight_s[b % 2])
        if b:
            embed_part[...] += part_here
        else:
            embed_part[...] = part_here
    for w in range(count):
        for way in range(n_c):
            hopped(w, way, steps - 1).wait_recv()
    for j in range(sz.seqs):
        for q in range(1, half):
            gather.wait_far(q, j)
    gather.finish()
    embed_save.wait()
    for i in range(3):
        swap(i).wait_send()
    for w in range(count):
        for g in range(sz.seqs):
            here = at_home & (place.group == g)
            pl.when(jnp.logical_not(here))(lambda w=w, g=g: move(w, g).wait_send())
        for way in range(n_c):
            for s in range(steps):
                hop(w, way, s).wait_send()
    for s in range(steps):
        around(s).wait_send()
    for s in range(n_dp):
        for kind in range(2 * half - 1):
            across(kind, s).wait_send()


def run_weights(sz, n_dp, adapter, adapter_block, blocks, rows):
    bf16, f32 = jnp.bfloat16, jnp.float32
    slots = n_dp * sz.n_context
    outs = [jax.ShapeDtypeStruct((slots,) + a.shape, bf16) for a in [adapter] + blocks]
    outs += [
        jax.ShapeDtypeStruct((sz.rows, sz.width), bf16),
        jax.ShapeDtypeStruct((sz.rows, sz.width), bf16),
        jax.ShapeDtypeStruct((sz.seq_len, sz.width), bf16),
        jax.ShapeDtypeStruct((sz.rows, sz.width), f32),
        jax.ShapeDtypeStruct((sz.rows, sz.width), f32),
    ]
    count, steps, dma = len(blocks), n_dp - 1, pltpu.SemaphoreType.DMA
    kinds = 2 * sz.half - 1
    return pl.pallas_call(
        partial(weights_kernel, sz, n_dp),
        out_shape=outs,
        in_specs=[any_spec()] * (4 + count),
        out_specs=[any_spec()] * (4 + count) + [full_spec()] * 2,
        scratch_shapes=[
            dma((count, sz.seqs)),
            dma((count, sz.n_context)),
            dma((count, sz.n_context, steps)),
            dma((count, sz.n_context, steps)),
            dma((steps,)),
            dma((steps,)),
            dma((kinds, n_dp)),
            dma((kinds, n_dp)),
            dma((count + 1,)),
            pltpu.VMEM((sz.rows, sz.width), bf16),
            pltpu.VMEM((sz.rows, sz.width), bf16),
            pltpu.VMEM((2, adapter_block, sz.width), bf16),
            dma((3,)),
            dma((3,)),
            dma((4 + sz.seqs,)),
            dma((2,)),
        ]
        + Gather.scratch(sz),
        compiler_params=pltpu.CompilerParams(
            collective_id=5, has_side_effects=True, vmem_limit_bytes=VMEM_BYTES
        ),
        name="weights",
    )(adapter, *blocks, *rows)


def norm_back(grad, rows, factor, gain):
    unit = rows * factor
    weighted = grad * gain
    inner = jnp.mean(weighted * unit, axis=-1, keepdims=True)
    return factor * (weighted - unit * inner), jnp.sum(grad * unit, axis=0, keepdims=True)


class GradRing:
    @staticmethod
    def scratch(sz, n_dp, tasks, wide, own_rows=None):
        slots, ways, dma = n_dp * sz.n_context, sz.n_context, pltpu.SemaphoreType.DMA
        depth, bf16, count, last = sz.width // slots, jnp.bfloat16, len(wide), n_dp - 1
        own_rows = [True] * count if own_rows is None else own_rows
        hops = [[s for w, s in tasks if w == i] for i in range(count)]
        return (
            [pltpu.VMEM((sz.seq_len, n), bf16) for n, own in zip(wide, own_rows) if own]
            + [pltpu.VMEM((ways, depth, n) if 0 in h else (ways, 16, 128), bf16) for n, h in zip(wide, hops)]
            + [pltpu.VMEM((ways, min(max(h) + 1, last), depth, n), bf16) for n, h in zip(wide, hops)]
            + [
                pltpu.VMEM((2, ways, sz.seq_len, depth), bf16),
                dma((count,)),
                dma((2, ways)),
                dma((count, ways, last)),
                dma((count, ways, last)),
                dma((ways,)),
            ]
        )

    @staticmethod
    def size(wide, own_rows=None):
        return 2 * len(wide) + (len(wide) if own_rows is None else sum(own_rows)) + 6

    @staticmethod
    def all_tasks(n_dp, count):
        return [
            (k - s, s)
            for k in range(count + n_dp)
            for s in range(min(k, n_dp - 1), -1, -1)
            if k - s < count
        ]

    def __init__(self, sz, place, ring, tasks, xs, ys, refs, rows=None, given=None):
        count, refs = len(xs), list(refs)
        self.sz, self.place, self.ring, self.xs, self.count = sz, place, ring, xs, count
        self.tasks = tasks
        self.ys = [refs.pop(0) if ys[w] is not None else rows[w] for w in range(count)]
        self.first, self.held = refs[:count], refs[count : 2 * count]
        self.x_s, self.load_y, self.load_x, self.send, self.recv, load_given = refs[2 * count :]
        self.y_loads = [
            pltpu.make_async_copy(ys[w], self.ys[w], self.load_y.at[w])
            for w in range(count)
            if ys[w] is not None
        ]
        self.unread = {w: self.y_loads[i] for i, w in enumerate(
            w for w in range(count) if ys[w] is not None
        )}
        self.given = []
        if given is not None:
            self.given = [
                pltpu.make_async_copy(
                    given.at[way], self.held[0].at[way, tasks[0][1] - 1], load_given.at[way]
                )
                for way in range(sz.n_context)
            ]
        self.done = 0

    def start(self):
        for copy in self.y_loads + self.given:
            copy.start()
        for way in range(self.sz.n_context):
            self.x_load(0, way).start()

    def slot(self, way, s):
        return self.ring.index(-(s + 1) if way == 0 else s + 1) * self.sz.n_context + way

    def x_load(self, k, way):
        w, s = self.tasks[k]
        depth = self.x_s.shape[3]
        if self.xs[w].shape[0] == 1:
            at = pl.multiple_of(self.slot(way, s) * depth, depth)
            src = self.xs[w].at[0, :, pl.ds(at, depth)]
        else:
            src = self.xs[w].at[self.slot(way, s)]
        return pltpu.make_async_copy(src, self.x_s.at[k % 2, way], self.load_x.at[k % 2, way])

    def source(self, w, way, s):
        return self.first[w].at[way] if s == 0 else self.held[w].at[way, s - 1]

    def hop(self, w, way, s):
        return pltpu.make_async_remote_copy(
            src_ref=self.source(w, way, s),
            dst_ref=self.held[w].at[way, s],
            send_sem=self.send.at[w, way, s],
            recv_sem=self.recv.at[w, way, s],
            device_id=self.ring.device(1 if way == 0 else self.ring.count - 1),
            device_id_type=MESH,
        )

    def result(self, w, way):
        return self.source(w, way, self.ring.count - 1)

    def step(self):
        k = self.done
        self.done += 1
        w, s = self.tasks[k]
        ways = range(self.sz.n_context)
        if k + 1 < len(self.tasks):
            for way in ways:
                self.x_load(k + 1, way).start()
        if w in self.unread:
            self.unread.pop(w).wait()
        for way in ways:
            self.x_load(k, way).wait()
            value = tn_dot(self.x_s[k % 2, way], self.ys[w][...])
            if k == 0 and self.given:
                self.given[way].wait()
            elif s:
                self.hop(w, way, s - 1).wait_recv()
            if s:
                value = value + self.held[w][way, s - 1].astype(jnp.float32)
            ref = self.source(w, way, s)
            ref[...] = value.astype(jnp.bfloat16)
            if s < self.ring.count - 1:
                self.hop(w, way, s).start()
        return w, s == self.ring.count - 1

    def left(self):
        return len(self.tasks) - self.done

    def finish(self):
        for w, s in self.tasks:
            if s < self.ring.count - 1:
                for way in range(self.sz.n_context):
                    self.hop(w, way, s).wait_send()


class Deliver:
    @staticmethod
    def scratch(sz, n_dp, wide):
        depth, count, dma = sz.width // (n_dp * sz.n_context), len(wide), pltpu.SemaphoreType.DMA
        return [pltpu.VMEM((sz.seqs, depth, n), jnp.bfloat16) for n in wide] + [
            dma((count, sz.n_context)),
            dma((count, sz.seqs)),
            dma((count,)),
        ]

    def __init__(self, sz, place, refs):
        self.sz, self.place = sz, place
        self.landed = refs[:-3]
        self.send, self.recv, self.own = refs[-3:]
        self.count = len(self.landed)
        self.t = lax.axis_index("tensor")
        self.role = place.part * sz.n_context + place.ctx
        self.at_home = self.role == self.t
        self.sources = [None] * self.count

    def greet(self):
        sz, place = self.sz, self.place
        barrier = pltpu.get_barrier_semaphore()
        for g in range(sz.seqs):
            holder = (place.dp, g * sz.half + self.t // sz.n_context, lax.rem(self.t, sz.n_context))
            pl.when(jnp.logical_not(self.at_home & (place.group == g)))(
                lambda holder=holder: pl.semaphore_signal(
                    barrier, inc=1, device_id=holder, device_id_type=MESH
                )
            )
        return sz.n_context - jnp.where(self.at_home, 1, 0)

    def remote(self, w, way):
        return pltpu.make_async_remote_copy(
            src_ref=self.sources[w][way],
            dst_ref=self.landed[w].at[self.place.group],
            send_sem=self.send.at[w, way],
            recv_sem=self.recv.at[w, self.place.group],
            device_id=(self.place.dp, self.role, way),
            device_id_type=MESH,
        )

    def local(self, w, way):
        return pltpu.make_async_copy(
            self.sources[w][way], self.landed[w].at[self.place.group], self.own.at[w]
        )

    def start(self, w, sources):
        self.sources[w] = sources
        for way in range(self.sz.n_context):
            here = self.at_home & (self.place.ctx == way)
            pl.when(here)(lambda way=way: self.local(w, way).start())
            pl.when(jnp.logical_not(here))(lambda way=way: self.remote(w, way).start())

    def total(self, w):
        place = self.place
        for g in range(self.sz.seqs):
            ref = self.landed[w].at[g]
            arrival = pltpu.make_async_remote_copy(
                src_ref=ref,
                dst_ref=ref,
                send_sem=self.send.at[w, 0],
                recv_sem=self.recv.at[w, g],
                device_id=(place.dp, self.t, 1 - place.ctx),
                device_id_type=MESH,
            )
            here = self.at_home & (place.group == g)
            pl.when(here)(lambda: self.local(w, 0).wait())
            pl.when(jnp.logical_not(here))(lambda arrival=arrival: arrival.wait_recv())
        total = self.landed[w][0].astype(jnp.float32)
        for g in range(1, self.sz.seqs):
            total = total + self.landed[w][g].astype(jnp.float32)
        return total

    def finish(self):
        for w in range(self.count):
            for way in range(self.sz.n_context):
                here = self.at_home & (self.place.ctx == way)
                pl.when(jnp.logical_not(here))(lambda w=w, way=way: self.remote(w, way).wait_send())


def slot_columns(sz, n_dp, x):
    slots = n_dp * sz.n_context
    depth = sz.width // slots
    if depth % 128:
        return x.reshape(sz.seq_len, slots, depth).transpose(1, 0, 2)
    return x[None]


def ffn_back_kernel(sz, n_dp, *refs):
    (cot, mixed, gains) = refs[:3]
    (rows_hbm, gate_hbm, up_hbm, wg_hbm, wu_hbm, down_hbm) = refs[3:9]
    (x_hbm, normed_hbm, hidden_hbm) = refs[9:12]
    (grad_mixed, gain_grad, dgate_out, dup_out, down_sum, gate_part) = refs[12:18]
    (rows_s, gate_s, up_s, wg, wu, wd, load, load_down, keep_sem) = refs[18:27]
    scatter_refs, ring_refs = refs[27:35], refs[35:]
    place = Place(sz)
    ring = Ring(place, n_dp)
    grads = GradRing(
        sz, place, ring, ffn_back_tasks(n_dp), [x_hbm, normed_hbm], [hidden_hbm, None], ring_refs,
        rows=[None, gate_s],
    )
    grads.start()
    pairs = ((rows_hbm, rows_s), (gate_hbm, gate_s), (up_hbm, up_s), (wg_hbm, wg), (wu_hbm, wu))
    loads = [
        pltpu.make_async_copy(src, dst, load.at[i]) for i, (src, dst) in enumerate(pairs)
    ]
    down_loads = column_loads(down_hbm, wd, load_down)
    place.enter([ring.device(1), ring.device(n_dp - 1)])
    scatter = Scatter(place, *scatter_refs)
    for copy in [loads[0]] + down_loads + loads[1:]:
        copy.start()
    grads.step()
    for copy in [loads[0]] + down_loads + loads[1:]:
        copy.wait()

    def work(q, j):
        rows = place.tile(q, j)
        dh = nt_dot(rows_s[rows, :], wd[...])
        gate = gate_s[rows, :].astype(jnp.float32)
        up = up_s[rows, :].astype(jnp.float32)
        sig = 1.0 / (1.0 + jnp.exp(-gate))
        dgate = (dh * up * sig * (1.0 + gate * (1.0 - sig))).astype(jnp.bfloat16)
        dup = (dh * gate * sig).astype(jnp.bfloat16)
        gate_s[rows, :] = dgate
        up_s[rows, :] = dup
        scatter.part[...] = nt_dot(dgate, wg[...]) + nt_dot(dup, wu[...])
        scatter.give(q, j)

    far = range(1, sz.half)
    for j in range(sz.seqs):
        for q in far:
            work(q, j)
        if j:
            for q in far:
                scatter.onward(q, j - 1)
    grads.step()
    work(0, 0)
    for q in far:
        scatter.onward(q, sz.seqs - 1)
    for j in range(1, sz.seqs):
        work(0, j)
    grads.step()
    copies = [
        pltpu.make_async_copy(gate_s, dgate_out, keep_sem.at[0]),
        pltpu.make_async_copy(up_s, dup_out, keep_sem.at[1]),
    ]
    for copy in copies:
        copy.start()
    gain_total = None
    for j in range(sz.seqs):
        span = slice(j * sz.block, (j + 1) * sz.block)
        rows = mixed[span, :]
        grad, gain_here = norm_back(scatter.total(j), rows, rms_factor(rows), gains[1:2, :])
        grad_mixed[span, :] = cot[span, :].astype(jnp.float32) + grad
        gain_total = gain_here if gain_total is None else gain_total + gain_here
    gain_grad[...] = gain_total
    while grads.left():
        grads.step()
    for way in range(sz.n_context):
        grads.hop(1, way, 0).wait_recv()
        for i, (src, dst) in enumerate(
            ((grads.result(0, way), down_sum), (grads.held[1].at[way, 0], gate_part))
        ):
            copies.append(
                pltpu.make_async_copy(src, dst.at[way], keep_sem.at[2 + 2 * way + i])
            )
            copies[-1].start()
    scatter.finish()
    grads.finish()
    for copy in copies:
        copy.wait()


def ffn_back_tasks(n_dp):
    return [(0, 0), (0, 1), (1, 0)] + [(0, s) for s in range(2, n_dp)]


def run_ffn_back(sz, n_dp, cot, mixed, gains, rows, gate, up, wg, wu, down, normed, hidden):
    f32, bf16, shape = jnp.float32, jnp.bfloat16, jax.ShapeDtypeStruct
    dma = pltpu.SemaphoreType.DMA
    depth = sz.width // (n_dp * sz.n_context)
    return pl.pallas_call(
        partial(ffn_back_kernel, sz, n_dp),
        out_shape=[
            shape((sz.rows, sz.width), f32),
            shape((1, sz.width), f32),
            shape((sz.seq_len, sz.ff), bf16),
            shape((sz.seq_len, sz.ff), bf16),
            shape((sz.n_context, depth, sz.ff), bf16),
            shape((sz.n_context, depth, sz.ff), bf16),
        ],
        in_specs=[full_spec()] * 3 + [any_spec()] * 9,
        out_specs=[full_spec()] * 2 + [any_spec()] * 4,
        scratch_shapes=[
            pltpu.VMEM((sz.seq_len, sz.width), bf16),
            pltpu.VMEM((sz.seq_len, sz.ff), bf16),
            pltpu.VMEM((sz.seq_len, sz.ff), bf16),
            pltpu.VMEM(wg.shape, bf16),
            pltpu.VMEM(wu.shape, bf16),
            pltpu.VMEM((sz.ff, sz.width), bf16),
            dma((5,)),
            dma((down.shape[0],)),
            dma((2 + 2 * sz.n_context,)),
        ]
        + Scatter.scratch(sz)
        + GradRing.scratch(sz, n_dp, ffn_back_tasks(n_dp), [sz.ff, sz.ff], [True, False]),
        compiler_params=pltpu.CompilerParams(
            collective_id=6, has_side_effects=True, vmem_limit_bytes=VMEM_BYTES
        ),
        cost_estimate=pl.CostEstimate(
            flops=8 * sz.seq_len * sz.width * sz.ff, bytes_accessed=40 << 20, transcendentals=0
        ),
        name="ffn_back",
    )(
        cot, mixed, gains, rows, gate, up, wg, wu, down,
        slot_columns(sz, n_dp, rows), slot_columns(sz, n_dp, normed), hidden,
    )


def attn_back_kernel(sz, n_dp, *refs):
    (grad_mixed, gains, cos_t, sin_t, begin, gain_b, adapted_hbm, state_hbm) = refs[:8]
    (q_hbm, k_hbm, v_hbm, lse_hbm, out_hbm, qkv_hbm) = refs[8:14]
    (x_hbm, dgate_hbm, dup_hbm, down_sum, gate_part) = refs[14:19]
    (grad_low, down_grad, gate_grad, state_out, rows_out, proj_out, up_part) = refs[19:26]
    (rows_s, q_s, k_s, v_s, lse_s, do_s, dk_s, dv_s, proj_s, wout, wqkv) = refs[26:37]
    (load, load_out, keep_sem, swap_out, swap_in, swap_sem, late) = refs[37:44]
    gather_refs, scatter_refs = refs[44:46], refs[46:54]
    ring_refs, deliver_refs = refs[54:66], refs[66:]
    place = Place(sz)
    ring = Ring(place, n_dp)
    grads = GradRing(
        sz, place, ring, attn_back_tasks(n_dp), [x_hbm, x_hbm], [dgate_hbm, dup_hbm], ring_refs,
        given=gate_part,
    )
    deliver = Deliver(sz, place, deliver_refs)
    grads.start()
    split = wqkv.shape[0]
    pairs = (
        (q_hbm, q_s), (k_hbm, k_s), (v_hbm, v_s), (lse_hbm, lse_s),
        (qkv_hbm.at[pl.ds(split, split)], wqkv),
    )
    loads = [
        pltpu.make_async_copy(src, dst, load.at[i]) for i, (src, dst) in enumerate(pairs)
    ]
    out_loads = column_loads(out_hbm, wout, load_out)
    for copy in out_loads + loads:
        copy.start()
    targets = deliver.greet()
    other = other_group(place)
    place.enter([ring.device(1), ring.device(n_dp - 1), other], targets)
    gather = Gather(place, rows_s, *gather_refs)
    scatter = Scatter(place, *scatter_refs)
    for j in range(sz.seqs):
        span = slice(j * sz.block, (j + 1) * sz.block)
        rows_s[gather.own(j), :] = grad_mixed[span, :].astype(jnp.bfloat16)
        gather.start(j)
    grads.step()
    deliver.start(0, [down_sum.at[way] for way in range(sz.n_context)])
    give_rows = pl.ds(pl.multiple_of((1 - place.group) * sz.block, sz.block), sz.block)
    keep_rows = pl.ds(pl.multiple_of(place.group * sz.block, sz.block), sz.block)
    swap = pltpu.make_async_remote_copy(
        src_ref=swap_out,
        dst_ref=swap_in,
        send_sem=swap_sem.at[0],
        recv_sem=swap_sem.at[1],
        device_id=other,
        device_id_type=MESH,
    )
    state_load = pltpu.make_async_copy(
        state_hbm.at[give_rows], scatter.part.at[pl.ds(0, sz.block)], late.at[0]
    )
    state_keep = pltpu.make_async_copy(
        state_hbm.at[keep_rows], state_out.at[place.group], late.at[1]
    )
    state_load.start()
    state_keep.start()
    state_load.wait()
    swap_out[...] = scatter.part[: sz.block, :].astype(jnp.bfloat16)
    swap.start()
    for copy in out_loads:
        copy.wait()
    d = sz.head_dim

    def heads_grad(q, j):
        rows = place.tile(q, j)
        dhead = nt_dot(rows_s[rows, :], wout[...]).astype(jnp.bfloat16)
        for h in range(sz.heads):
            do_s[h, rows, :] = dhead[:, h * d : (h + 1) * d]

    far = range(1, sz.half)
    for j in range(sz.seqs):
        gather.wait_near(j)
        heads_grad(0, j)
    for copy in loads:
        copy.wait()
    for j in range(sz.seqs):
        if j == sz.seqs - 1:
            grads.step()
            grads.step()
        for q in far:
            gather.forward(q, j)
        for q in far:
            gather.wait_far(sz.half - q, j)
            heads_grad(q, j)
    rows_copy = pltpu.make_async_copy(rows_s, rows_out, keep_sem.at[0])
    rows_copy.start()
    gather.finish()
    rows_copy.wait()
    upper = rows_s.at[pl.ds(0, split), pl.ds(0, wqkv.shape[1])]
    upper_load = pltpu.make_async_copy(qkv_hbm.at[pl.ds(0, split)], upper, late.at[2])
    upper_load.start()

    tiles = sz.n_tensor
    scale = 1.0 / math.sqrt(d)

    def head(h, carry):
        for i in reversed(range(tiles)):
            rows = slice(i * sz.tile, (i + 1) * sz.tile)
            length = (i + 1) * sz.tile
            keys, values = k_s[h, 0:length, :], v_s[h, 0:length, :]
            query, grad = q_s[h, rows, :], do_s[h, rows, :]
            start = begin[:, rows]
            key_at = lax.broadcasted_iota(jnp.int32, (length, sz.tile), 0)
            query_at = i * sz.tile + lax.broadcasted_iota(jnp.int32, (1, sz.tile), 1)
            allowed = (key_at >= start) & (key_at <= query_at)
            scores = nt_dot(keys, query)
            scores = jnp.where(allowed, scores * (LOG2E * scale), masked_score)
            probs = jnp.exp2(scores - lse_s[h, :, rows])
            dprobs = nt_dot(values, grad)
            inner = jnp.sum(probs * dprobs, axis=0, keepdims=True)
            dscores = (probs * (dprobs - inner)).astype(jnp.bfloat16)
            dv = nn_dot(probs.astype(jnp.bfloat16), grad)
            dk = nn_dot(dscores, query)
            if i == tiles - 1:
                dv_s[...] = dv
                dk_s[...] = dk
            else:
                dv_s[0:length, :] += dv
                dk_s[0:length, :] += dk
            dq = jnp.transpose(tn_dot(keys, dscores)) * scale
            cos_here, sin_here = cos_t[rows, :], sin_t[rows, :]
            proj_s[rows, pl.ds(pl.multiple_of(h * 3 * d, d), d)] = turn(
                dq, cos_here, -sin_here
            ).astype(jnp.bfloat16)
        dk = turn(dk_s[...] * scale, cos_t[...], -sin_t[...])
        proj_s[:, pl.ds(pl.multiple_of(h * 3 * d + d, d), d)] = dk.astype(jnp.bfloat16)
        proj_s[:, pl.ds(pl.multiple_of(h * 3 * d + 2 * d, d), d)] = dv_s[...].astype(jnp.bfloat16)
        return carry

    lax.fori_loop(0, sz.heads // 2, head, 0)
    while grads.left() > 1:
        grads.step()
    deliver.start(1, [grads.result(0, way) for way in range(sz.n_context)])
    lax.fori_loop(sz.heads // 2, sz.heads, head, 0)
    copies = [pltpu.make_async_copy(proj_s, proj_out, keep_sem.at[1])]
    copies[0].start()
    upper_load.wait()

    def give(q, j):
        proj = proj_s[place.tile(q, j), :]
        scatter.part[:, :split] = nt_dot(proj, upper[...])
        scatter.part[:, split:] = nt_dot(proj, wqkv[...])
        scatter.give(q, j)

    for j in range(sz.seqs):
        for q in far:
            give(q, j)
        if j:
            for q in far:
                scatter.onward(q, j - 1)
    give(0, 0)
    for q in far:
        scatter.onward(q, sz.seqs - 1)
    for j in range(1, sz.seqs):
        give(0, j)
    adapted = scatter.part
    adapted_load = pltpu.make_async_copy(adapted_hbm, adapted, late.at[3])
    adapted_load.start()
    grads.step()
    swap.wait()
    state_keep.wait()
    adapted_load.wait()
    state_out[1 - place.group] = swap_in[...].astype(jnp.float32)
    down_grad[...] = jnp.transpose(deliver.total(0))
    gain_total = None
    for j in range(sz.seqs):
        span = slice(j * sz.block, (j + 1) * sz.block)
        rows = adapted[span, :]
        grad, gain_here = norm_back(scatter.total(j), rows, rms_factor(rows), gains[0:1, :])
        grad_low[span, :] = (grad_mixed[span, :] + grad).astype(jnp.bfloat16)
        gain_total = gain_here if gain_total is None else gain_total + gain_here
    extra = grad_low.shape[0] - sz.rows
    at_row = lax.broadcasted_iota(jnp.int32, (extra, sz.width), 0)
    shares = jnp.where(at_row == 0, gain_total, jnp.where(at_row == 1, gain_b[...], 0.0))
    grad_low[sz.rows :, :] = shares.astype(jnp.bfloat16)
    for way in range(sz.n_context):
        grads.hop(1, way, 1).wait_recv()
        copies.append(
            pltpu.make_async_copy(
                grads.held[1].at[way, 1], up_part.at[way], keep_sem.at[2 + way]
            )
        )
        copies[-1].start()
    gate_grad[...] = deliver.total(1)
    scatter.finish()
    grads.finish()
    deliver.finish()
    for copy in copies:
        copy.wait()


def attn_back_tasks(n_dp):
    return [(0, 1), (0, 2), (1, 0)] + [(0, s) for s in range(3, n_dp)] + [(1, 1)]


def run_attn_back(
    sz, n_dp, grad_mixed, adapted, gains, cos_t, sin_t, begin, gain_b, state, q, k, v, lse, out,
    qkv, x, dgate, dup, down_sum, gate_part,
):
    f32, bf16, shape = jnp.float32, jnp.bfloat16, jax.ShapeDtypeStruct
    dma = pltpu.SemaphoreType.DMA
    heads_shape = (sz.heads, sz.seq_len, sz.head_dim)
    return pl.pallas_call(
        partial(attn_back_kernel, sz, n_dp),
        out_shape=[
            shape((sz.rows + 16, sz.width), bf16),
            shape(down_sum.shape[:0:-1], f32),
            shape(gate_part.shape[1:], f32),
            shape((sz.seqs, sz.block, sz.width), f32),
            shape((sz.seq_len, sz.width), bf16),
            shape((sz.seq_len, qkv.shape[1]), bf16),
            shape(gate_part.shape, bf16),
        ],
        in_specs=[full_spec()] * 6 + [any_spec()] * 13,
        out_specs=[full_spec()] * 4 + [any_spec()] * 3,
        scratch_shapes=[
            pltpu.VMEM((sz.seq_len, sz.width), bf16),
            pltpu.VMEM(heads_shape, bf16),
            pltpu.VMEM(heads_shape, bf16),
            pltpu.VMEM(heads_shape, bf16),
            pltpu.VMEM((sz.heads, 1, sz.seq_len), f32),
            pltpu.VMEM(heads_shape, bf16),
            pltpu.VMEM((sz.seq_len, sz.head_dim), f32),
            pltpu.VMEM((sz.seq_len, sz.head_dim), f32),
            pltpu.VMEM((sz.seq_len, qkv.shape[1]), bf16),
            pltpu.VMEM((sz.heads * sz.head_dim, sz.width), bf16),
            pltpu.VMEM((sz.width // 2, qkv.shape[1]), bf16),
            dma((5,)),
            dma((out.shape[0],)),
            dma((2 + sz.n_context,)),
            pltpu.VMEM((sz.block, sz.width), bf16),
            pltpu.VMEM((sz.block, sz.width), bf16),
            dma((2,)),
            dma((4,)),
        ]
        + Gather.scratch(sz)
        + Scatter.scratch(sz)
        + GradRing.scratch(sz, n_dp, attn_back_tasks(n_dp), [sz.ff, sz.ff])
        + Deliver.scratch(sz, n_dp, [sz.ff, sz.ff]),
        compiler_params=pltpu.CompilerParams(
            collective_id=7, has_side_effects=True, vmem_limit_bytes=VMEM_BYTES
        ),
        cost_estimate=pl.CostEstimate(
            flops=4 * sz.seq_len * sz.width * qkv.shape[1], bytes_accessed=30 << 20, transcendentals=0
        ),
        name="attn_back",
    )(
        grad_mixed, gains, cos_t, sin_t, begin, gain_b, adapted, state, q, k, v, lse, out, qkv,
        slot_columns(sz, n_dp, x), dgate, dup, down_sum, gate_part,
    )


class PlaneRows:
    @staticmethod
    def scratch(n_dp):
        dma = pltpu.SemaphoreType.DMA
        return [dma((n_dp - 1,)), dma((n_dp - 1,)), dma((n_dp,)), dma((n_dp,))]

    def __init__(self, place, ring, own, landed, refs):
        self.place, self.ring, self.own, self.landed = place, ring, own, landed
        self.send, self.recv, self.near_send, self.near_recv = refs
        self.ahead = 1 - 2 * place.ctx

    def slot(self, offset, ctx):
        return self.landed.at[self.ring.index(offset) * self.place.sz.n_context + ctx]

    def source(self, s):
        return self.own if s == 0 else self.slot(-self.ahead * s, self.place.ctx)

    def hop(self, s):
        return pltpu.make_async_remote_copy(
            src_ref=self.source(s),
            dst_ref=self.slot(-self.ahead * s, self.place.ctx),
            send_sem=self.send.at[s],
            recv_sem=self.recv.at[s],
            device_id=self.ring.device(self.ahead),
            device_id_type=MESH,
        )

    def near(self, s):
        return pltpu.make_async_remote_copy(
            src_ref=self.source(s),
            dst_ref=self.slot(-self.ahead * s, self.place.ctx),
            send_sem=self.near_send.at[s],
            recv_sem=self.near_recv.at[s],
            device_id=self.place.sibling(),
            device_id_type=MESH,
        )

    def start(self):
        self.hop(0).start()
        self.near(0).start()

    def step(self, s):
        ref = self.slot(-self.ahead * (s + 1), self.place.ctx)
        pltpu.make_async_remote_copy(
            src_ref=ref,
            dst_ref=ref,
            send_sem=self.send.at[s],
            recv_sem=self.recv.at[s],
            device_id=self.place.sibling(),
            device_id_type=MESH,
        ).wait_recv()
        if s + 1 < self.ring.count - 1:
            self.hop(s + 1).start()
        self.near(s + 1).start()

    def wait_near(self, s):
        ref = self.slot(self.ahead * s, 1 - self.place.ctx)
        pltpu.make_async_remote_copy(
            src_ref=ref,
            dst_ref=ref,
            send_sem=self.near_send.at[s],
            recv_sem=self.near_recv.at[s],
            device_id=self.place.sibling(),
            device_id_type=MESH,
        ).wait_recv()

    def finish(self):
        for s in range(self.ring.count):
            if s < self.ring.count - 1:
                self.hop(s).wait_send()
            self.near(s).wait_send()


class LineSum:
    @staticmethod
    def scratch(sz, parts, chunk):
        dma, bf16 = pltpu.SemaphoreType.DMA, jnp.bfloat16
        far = pltpu.VMEM((max(sz.half - 1, 1), parts, chunk, sz.width), bf16)
        one = pltpu.VMEM((parts, chunk, sz.width), bf16)
        kinds = 2 * sz.half - 1
        return [far, far, one, one, one, far, dma((kinds, parts)), dma((kinds, parts))]

    def __init__(self, place, total, parts, refs):
        self.place, self.total, self.parts = place, total, parts
        (self.out, self.got, self.sum, self.cross, self.done, self.back, self.send, self.recv) = refs
        self.chunk = self.sum.shape[1]

    def rows(self, part, k):
        first = (part * self.parts + k) * self.chunk
        return pl.ds(pl.multiple_of(first, self.chunk), self.chunk)

    def copy(self, src, dst, kind, k, device):
        return pltpu.make_async_remote_copy(
            src_ref=src,
            dst_ref=dst,
            send_sem=self.send.at[kind, k],
            recv_sem=self.recv.at[kind, k],
            device_id=device,
            device_id_type=MESH,
        )

    def spread(self, q, k):
        place = self.place
        device = place.device(place.ahead(q), place.ctx)
        return self.copy(self.out.at[q - 1, k], self.got.at[q - 1, k], q, k, device)

    def swap(self, k):
        return self.copy(self.sum.at[k], self.cross.at[k], 0, k, other_group(self.place))

    def collect(self, q, k):
        place = self.place
        device = place.device(place.ahead(q), place.ctx)
        return self.copy(
            self.done.at[k], self.back.at[q - 1, k], place.sz.half - 1 + q, k, device
        )

    def start(self, k):
        for q in range(1, self.place.sz.half):
            rows = self.rows(self.place.ahead(q), k)
            self.out[q - 1, k] = self.total[rows, :].astype(jnp.bfloat16)
            self.spread(q, k).start()

    def cross_over(self, k):
        value = self.total[self.rows(self.place.part, k), :]
        for q in range(1, self.place.sz.half):
            self.spread(q, k).wait_recv()
            value = value + self.got[q - 1, k].astype(jnp.float32)
        self.sum[k] = value.astype(jnp.bfloat16)
        self.swap(k).start()

    def share(self, k):
        self.swap(k).wait_recv()
        value = self.sum[k].astype(jnp.float32) + self.cross[k].astype(jnp.float32)
        self.done[k] = value.astype(jnp.bfloat16)
        for q in range(1, self.place.sz.half):
            self.collect(q, k).start()
        self.total[self.rows(self.place.part, k), :] = self.done[k].astype(jnp.float32)

    def complete(self, k):
        for q in range(1, self.place.sz.half):
            self.collect(q, k).wait_recv()
            rows = self.rows(self.place.behind(q), k)
            self.total[rows, :] = self.back[q - 1, k].astype(jnp.float32)

    def finish(self):
        for k in range(self.parts):
            self.swap(k).wait_send()
            for q in range(1, self.place.sz.half):
                self.spread(q, k).wait_send()
                self.collect(q, k).wait_send()


SUM_PARTS = 3


def grads_kernel(sz, n_dp, count, *refs):
    n_in = 4 + 2 * count
    low, joined, adapter, up_part = refs[:4]
    gate_grad, refs = refs[4], refs[:4] + refs[5:]
    xs, ys = refs[4 : 4 + count], refs[4 + count : n_in]
    outs = refs[n_in : n_in + count]
    embed_grad, adapter_out, gains_out, landed = refs[n_in + count : n_in + 4 + count]
    refs = refs[n_in + 4 + count :]

    def take(n):
        nonlocal refs
        head, refs = refs[:n], refs[n:]
        return head

    ring_refs, deliver_refs = take(3 * count + 6), take(count + 3)
    plane_refs, sum_refs = take(4), take(8)
    adapter_grad, d_s, j_s, weight_s, rows_s, swap_in = refs[:6]
    d_sem, j_sem, weight_sem, swap_sem, out_sem = refs[6:]
    place = Place(sz)
    ring = Ring(place, n_dp)
    grads = GradRing(
        sz, place, ring, grads_tasks(n_dp, count), xs, ys, ring_refs, given=up_part
    )
    deliver = Deliver(sz, place, deliver_refs)
    plane = PlaneRows(place, ring, low, landed, plane_refs)
    line = LineSum(place, adapter_grad, SUM_PARTS, sum_refs)
    other = other_group(place)
    grads.start()
    weight_load = [
        pltpu.make_async_copy(
            adapter.at[adapter.shape[0] // 2 + b, pl.ds(0, weight_s.shape[0])], weight_s, weight_sem
        )
        for b in range(adapter.shape[0] // 2)
    ]
    weight_load[0].start()
    place.enter([ring.device(1), ring.device(n_dp - 1), other], deliver.greet())
    plane.start()
    give_rows = pl.ds(pl.multiple_of((1 - place.group) * sz.block, sz.block), sz.block)
    keep_rows = pl.ds(pl.multiple_of(place.group * sz.block, sz.block), sz.block)
    swap = pltpu.make_async_remote_copy(
        src_ref=low.at[give_rows],
        dst_ref=swap_in,
        send_sem=swap_sem.at[0],
        recv_sem=swap_sem.at[1],
        device_id=other,
        device_id_type=MESH,
    )
    swap.start()

    def ring_step():
        if grads.left():
            w, complete = grads.step()
            if complete:
                deliver.start(w, [grads.result(w, way) for way in range(sz.n_context)])

    depth = joined.shape[2]

    def batch(ctx):
        copies = []
        for d in range(n_dp):
            at = d * sz.n_context + ctx
            rows = pl.ds(d * sz.rows, sz.rows)
            copies.append(
                pltpu.make_async_copy(landed.at[at, pl.ds(0, sz.rows)], d_s.at[rows], d_sem.at[d, 0])
            )
            copies.append(pltpu.make_async_copy(joined.at[at], j_s.at[rows], j_sem.at[d]))
            copies.append(
                pltpu.make_async_copy(
                    landed.at[at, pl.ds(sz.rows, 16)],
                    d_s.at[pl.ds(n_dp * sz.rows + 16 * d, 16)],
                    d_sem.at[d, 1],
                )
            )
        return copies

    def product(ctx, first):
        copies = batch(ctx)
        for copy in copies:
            copy.start()
        for copy in copies:
            copy.wait()
        chunk = sz.width // 4
        for n in range(4):
            cols = slice(n * chunk, (n + 1) * chunk)
            value = tn_dot(j_s[...], d_s[: n_dp * sz.rows, cols])
            tail = d_s[n_dp * sz.rows : n_dp * sz.rows + 16, cols].astype(jnp.float32)
            for d in range(1, n_dp):
                at = n_dp * sz.rows + 16 * d
                tail = tail + d_s[at : at + 16, cols].astype(jnp.float32)
            if first:
                adapter_grad[:depth, cols] = value
                adapter_grad[depth : depth + 16, cols] = tail
            else:
                adapter_grad[:depth, cols] += value
                adapter_grad[depth : depth + 16, cols] += tail

    own = pltpu.make_async_copy(low, landed.at[place.dp * sz.n_context + place.ctx], d_sem.at[0, 0])
    own.start()
    rest = adapter_grad.shape[0] - depth - 16
    if rest:
        adapter_grad[depth + 16 :, :] = jnp.zeros((rest, sz.width), jnp.float32)
    for s in range(n_dp - 1):
        ring_step()
        plane.step(s)
    own.wait()
    product(place.ctx, True)
    for s in range(n_dp):
        plane.wait_near(s)
    product(1 - place.ctx, False)
    for k in range(SUM_PARTS):
        line.start(k)
    ring_step()
    ring_step()
    swap.wait()
    rows_s[place.group] = low[keep_rows, :]
    rows_s[1 - place.group] = swap_in[...]
    rows = rows_s[...].reshape(sz.rows, sz.width)
    ring_step()
    for k in range(SUM_PARTS):
        line.cross_over(k)
    ring_step()
    for b, copy in enumerate(weight_load):
        copy.wait()
        part = nt_dot(rows, weight_s[...]).reshape(sz.seqs, sz.block, weight_s.shape[0])
        embed_grad[:, :, b * weight_s.shape[0] : (b + 1) * weight_s.shape[0]] = part
        if b + 1 < len(weight_load):
            weight_load[b + 1].start()
    ring_step()
    for k in range(SUM_PARTS):
        line.share(k)
        ring_step()
    while grads.left():
        ring_step()
    for k in range(SUM_PARTS):
        line.complete(k)
    saves = [
        pltpu.make_async_copy(gate_grad, outs[0].at[0], out_sem.at[2]),
        pltpu.make_async_copy(adapter_grad.at[pl.ds(0, depth)], adapter_out, out_sem.at[0]),
        pltpu.make_async_copy(adapter_grad.at[pl.ds(depth, 16)], gains_out, out_sem.at[1]),
    ]
    for copy in saves:
        copy.start()
    outs[0][1] = deliver.total(0)
    outs[1][...] = deliver.total(1)
    outs[2][...] = jnp.transpose(deliver.total(2))
    for copy in saves:
        copy.wait()
    grads.finish()
    deliver.finish()
    plane.finish()
    line.finish()


def grads_tasks(n_dp, count):
    others = [(w + 1, s) for w, s in GradRing.all_tasks(n_dp, count - 1)]
    return [(0, s) for s in range(2, n_dp)] + others


def run_grads(sz, n_dp, low, joined, adapter, up_part, gate_grad, xs, ys):
    count, bf16, f32, dma = len(xs), jnp.bfloat16, jnp.float32, pltpu.SemaphoreType.DMA
    shape = jax.ShapeDtypeStruct
    depth = sz.width // (n_dp * sz.n_context)
    wide = [y.shape[1] for y in ys]
    slots, columns = joined.shape[0], joined.shape[2]
    unit = 16 * sz.half * SUM_PARTS
    total_rows = -(-(columns + 16) // unit) * unit
    return pl.pallas_call(
        partial(grads_kernel, sz, n_dp, count),
        out_shape=[
            shape((2, depth, wide[0]), f32),
            shape((depth, wide[1]), f32),
            shape((wide[2], depth), f32),
        ]
        + [
            shape((sz.seqs, sz.block, sz.width), f32),
            shape((columns, sz.width), f32),
            shape((16, sz.width), f32),
            shape((slots,) + low.shape, bf16),
        ],
        in_specs=[full_spec()] + [any_spec()] * (4 + 2 * count),
        out_specs=[full_spec()] * (1 + count) + [any_spec()] * 3,
        scratch_shapes=GradRing.scratch(sz, n_dp, grads_tasks(n_dp, count), wide)
        + Deliver.scratch(sz, n_dp, wide)
        + PlaneRows.scratch(n_dp)
        + LineSum.scratch(sz, SUM_PARTS, total_rows // (sz.half * SUM_PARTS))
        + [
            pltpu.VMEM((total_rows, sz.width), f32),
            pltpu.VMEM((n_dp * (sz.rows + 16), sz.width), bf16),
            pltpu.VMEM((n_dp * sz.rows, columns), bf16),
            pltpu.VMEM((columns, sz.width), bf16),
            pltpu.VMEM((sz.seqs, sz.block, sz.width), bf16),
            pltpu.VMEM((sz.block, sz.width), bf16),
            dma((n_dp, 2)),
            dma((n_dp,)),
            dma,
            dma((2,)),
            dma((3,)),
        ],
        compiler_params=pltpu.CompilerParams(
            collective_id=8, has_side_effects=True, vmem_limit_bytes=VMEM_BYTES
        ),
        cost_estimate=pl.CostEstimate(
            flops=2 * sz.seq_len * sz.width * sum(wide), bytes_accessed=60 << 20, transcendentals=0
        ),
        name="grads",
    )(low, joined, adapter, up_part, gate_grad, *[slot_columns(sz, n_dp, x) for x in xs], *ys)


def shards(
    embedded,
    initial_state,
    cotangent,
    doc_ids,
    recurrences,
    adapter_weight,
    norm_gains,
    qkv_weight,
    output_head_weight,
    gate_up_weight,
    down_weight,
):
    n_dp = lax.axis_size("dp")
    n_tensor = lax.axis_size("tensor")
    n_context = lax.axis_size("context")
    dp_index = lax.axis_index("dp")
    t_index = lax.axis_index("tensor")
    ctx_index = lax.axis_index("context")
    seq_count, block_rows, model_width = embedded.shape
    seq_len = doc_ids.shape[1]
    half = n_tensor // seq_count
    group = t_index // half
    part = t_index % half
    heads_here = qkv_weight.shape[1]
    head_dim = qkv_weight.shape[2] // 3
    ff_here = down_weight.shape[0]
    def side_by_side(blocks):
        count, depth, columns = blocks.shape
        return blocks.transpose(1, 0, 2).reshape(depth, count * columns)

    def role_grad(grad, axis):
        piece = lax.psum_scatter(
            grad.astype(jnp.bfloat16), "dp", scatter_dimension=axis, tiled=True
        )
        low, high = jnp.split(piece, 2, axis=axis)
        give = [jnp.where(group == 0, low, high), jnp.where(group == 0, high, low)]
        back = [
            lax.ppermute(g, ("tensor", "context"), [(b, a) for a, b in perm])
            for g, perm in zip(give, role_perms)
        ]
        return back[0].astype(jnp.float32) + back[1].astype(jnp.float32)

    def gather_rows(rows):
        full = lax.all_gather(
            rows, ("tensor", "context"), axis=0, tiled=True, axis_index_groups=groups
        )
        split = full.reshape(half, n_context, seq_count, block_rows, model_width)
        return split.transpose(2, 0, 1, 3, 4).reshape(seq_len, model_width)

    sz = Sizes(
        n_tensor,
        n_context,
        seq_count,
        half,
        block_rows,
        n_context * block_rows,
        seq_count * block_rows,
        seq_len,
        model_width,
        heads_here,
        head_dim,
        ff_here,
    )
    adapter_block = adapter_weight.shape[0]
    gain_columns = norm_gains.shape[1]
    unit = 16 * half
    padded = -(-(adapter_block + 2) // unit) * unit
    adapter_rows = jnp.concatenate(
        [
            adapter_weight,
            jnp.pad(
                norm_gains,
                ((0, padded - adapter_block - 2), (0, model_width - gain_columns)),
            ),
        ],
        axis=0,
    )
    (
        adapter_all,
        out_blocks,
        qkv_use,
        gate_use,
        up_use,
        down_blocks,
        embed_rows,
        cot_rows,
        grad_ffn,
        embed_part,
        current,
    ) = run_weights(
        sz,
        n_dp,
        adapter_rows,
        adapter_block,
        [
            output_head_weight.reshape(heads_here * head_dim, -1),
            qkv_weight.reshape(qkv_weight.shape[0], -1),
            gate_up_weight[:, 0],
            gate_up_weight[:, 1],
            down_weight,
        ],
        [embedded, initial_state, cotangent],
    )
    qkv_use = qkv_use.reshape(model_width, -1)
    gate_use = gate_use.reshape(model_width, -1)
    up_use = up_use.reshape(model_width, -1)
    gains_full = (
        adapter_all[:, adapter_block : adapter_block + 2, :gain_columns]
        .transpose(1, 0, 2)
        .reshape(2, model_width)
    )
    if out_blocks.shape[2] % 128:
        out_blocks = side_by_side(out_blocks)[None]
        down_blocks = side_by_side(down_blocks)[None]
    gains_f = gains_full.astype(jnp.float32)

    cos_full, sin_full = rope_tables(seq_len, head_dim)
    own_seq = dp_index * seq_count + group
    docs = lax.dynamic_index_in_dim(doc_ids, own_seq, 0, keepdims=False)
    begin = jnp.sum((docs[None, :] < docs[:, None]).astype(jnp.int32), axis=1)[None, :]
    steps_own = lax.dynamic_index_in_dim(recurrences, own_seq, 0, keepdims=False) - BACK
    active = jnp.arange(MAXR - BACK, dtype=jnp.int32)[:, None] < steps_own
    detached = run_rounds(
        sz,
        current,
        jnp.broadcast_to(active.astype(jnp.float32), (MAXR - BACK, model_width)),
        gains_f, cos_full, sin_full, begin, embed_part,
        adapter_all, qkv_use, out_blocks, gate_use, up_use, down_blocks,
    )
    (mixed_rows, adapted, feature_rows, query_hm, key_hm, value_hm, head_flat, lse, joined) = run_attn(
        sz, n_dp, True, detached, embed_part, gains_f, cos_full, sin_full, begin,
        adapter_all, qkv_use, out_blocks, embed_rows,
    )
    (current, ffn_input, gate_pre, up_pre, hidden) = run_ffn(
        sz, True, mixed_rows, detached, gains_f[:1], gains_f, gate_use, up_use, down_blocks
    )
    grad_mixed, gain_b, grad_gate, grad_up, down_sum, gate_part = run_ffn_back(
        sz, n_dp, cot_rows, mixed_rows, gains_f, grad_ffn, gate_pre, up_pre,
        gate_use, up_use, down_blocks, ffn_input, hidden,
    )
    grad_low, down_s, gate_s, state_out, grad_rows, grad_proj, up_part = run_attn_back(
        sz, n_dp, grad_mixed, adapted, gains_f, cos_full, sin_full, begin, gain_b, current,
        query_hm, key_hm, value_hm, lse, out_blocks, qkv_use, ffn_input, grad_gate, grad_up, down_sum,
        gate_part,
    )
    pair_s, qkv_s, out_s, embed_out, adapter_s, gains_rows, _ = run_grads(
        sz,
        n_dp,
        grad_low,
        joined,
        adapter_all,
        up_part,
        gate_s,
        [ffn_input, feature_rows, grad_rows],
        [grad_up, grad_proj, head_flat],
    )
    place_at = (dp_index * n_context + ctx_index) * gain_columns
    gains_s = lax.dynamic_slice_in_dim(gains_rows[:2], place_at, gain_columns, 1)
    out_s = out_s.reshape(heads_here, head_dim, -1)
    qkv_s = qkv_s.reshape(-1, heads_here, 3 * head_dim)
    gate_up_s = pair_s.transpose(1, 0, 2)
    return (state_out, embed_out, adapter_s, gains_s, qkv_s, out_s, gate_up_s, down_s)


def solution(mesh):
    placed = (
        P("dp", ("tensor", "context"), None),
        P("dp", ("tensor", "context"), None),
        P("dp", ("tensor", "context"), None),
        P(),
        P(),
        P(("dp", "context"), None),
        P(None, ("dp", "context")),
        P(("dp", "context"), "tensor", None),
        P("tensor", None, ("dp", "context")),
        P(("dp", "context"), None, "tensor"),
        P("tensor", ("dp", "context")),
    )
    return jax.shard_map(
        shards,
        mesh=mesh,
        in_specs=placed,
        out_specs=(
            P("dp", ("tensor", "context"), None),
            P("dp", ("tensor", "context"), None),
            P(("dp", "context"), None),
            P(None, ("dp", "context")),
            P(("dp", "context"), "tensor", None),
            P("tensor", None, ("dp", "context")),
            P(("dp", "context"), None, "tensor"),
            P("tensor", ("dp", "context")),
        ),
        check_vma=False,
    )
```
